32 devices in a mesh: tok: 8 (over y, x, core), rep: 4 (over z).
Axes of the slice: x: 2, y: 2, z: 4, core: 2. Of those that a mesh axis runs over, the one named last changes fastest.
Arguments:
- tokens: bfloat16 [32768, 768], P(('rep', 'tok')), may hold values from -6 to 6
- cotangent: bfloat16 [32768, 768], P(('rep', 'tok')), may hold values from -6 to 6
- cluster_order: int32 [32768], P(('rep', 'tok')), may hold values from 0 to 4095, as said below
- block_owner: int32 [96, 1], replicated, may hold values from 0 to 7; in each aligned block of 96 rows (0 to 95, 96 to 191, ...) at most 13 rows name the same one
- master_slots: float32 [104, 96, 768], P('tok'), may hold values from -0.3125 to 0.3125
- moment_one: float32 [104, 96, 768], P('tok'), as said below
- moment_two: float32 [104, 96, 768], P('tok'), as said below
- vector_master: float32 [9216], P('tok'), may hold values from -3 to 3
- vector_moment_one: float32 [9216], P('tok'), as said below
- vector_moment_two: float32 [9216], P('tok'), as said below
Outputs:
- output: bfloat16 [32768, 768], P(('rep', 'tok'))
- input_grad: bfloat16 [32768, 768], P(('rep', 'tok'))
- weight_grads: float32 [104, 96, 768], P('tok')
- moment_one_new: float32 [104, 96, 768], P('tok')
- moment_two_new: float32 [104, 96, 768], P('tok')
- master_new: float32 [104, 96, 768], P('tok')
- weight_low_new: bfloat16 [104, 96, 768], P('tok')
- vector_grads: float32 [9216], P('tok')
- vector_moment_one_new: float32 [9216], P('tok')
- vector_moment_two_new: float32 [9216], P('tok')
- vector_master_new: float32 [9216], P('tok')
- vector_low_new: bfloat16 [9216], P('tok')
- row_entropy: bfloat16 [32768], P(('rep', 'tok'))
- occupancy: int32 [8, 8], replicated
The draws below stay inside these ranges and needn't reach their ends.
Inputs may be any that keep to these rules, and one draw needn't show every extreme that they name: Within each sequence the 4096 values are a permutation. For the rows of one device, the number of rows whose (sequence number * 32 + cluster_order // 128) modulo 8 equals a given residue is at most 192, and equals 192 for some residue on every device. `block_owner`: each index owns at most 13 blocks, some index owns exactly 13, and every index owns at least one. `moment_one`: of both signs. `moment_two`: Positive. `vector_moment_one`: of both signs. `vector_moment_two`: Positive.
All inputs are finite; a program needn't handle non-finite values.
Results may differ from the reference program's by a relative error of at most 0.02.
Values may be sent and summed in bfloat16 or wider, within the bound.
A program may use at most 256 MiB of HBM per device.

```python
import math
import jax
import jax.numpy as jnp
import numpy as np
from jax import lax

D = 768
HEADS = 12
HD = 64
FF = 3072
TOK_DEV = 1024
SD = 4
CL = 128
NBLK = 96
STEP = 10
LEN = 4096
CPS = 32
TOKENS = 32768
WROWS = 9216
BLK = 96
SLOTS = 13
OWNED = 104
SMALL = 9216
N_TOK = 8


def grad_size():
    return 0.3 * math.sqrt(TOKENS)


def first_moment(key, array_shape):
    normal_draw = jax.random.normal(key, array_shape, jnp.float32)
    return jnp.clip(normal_draw, -4.0, 4.0) * (0.1 / 0.9) * grad_size()


def second_moment(key, array_shape):
    factor = jnp.exp(jax.random.uniform(key, array_shape, jnp.float32, 0.0, math.log(4.0)))
    return factor * (0.001 / 0.999) * grad_size() * grad_size()


def draw_moment_one(key, part):
    key = jax.random.fold_in(key, 3)
    return first_moment(key, (OWNED, BLK, D))


def draw_moment_two(key, part):
    key = jax.random.fold_in(key, 4)
    return second_moment(key, (OWNED, BLK, D))


def draw_vector_moment_one(key, part):
    key = jax.random.fold_in(key, 5)
    return first_moment(key, (SMALL,))


def draw_vector_moment_two(key, part):
    key = jax.random.fold_in(key, 6)
    return second_moment(key, (SMALL,))


def sequence_order(seq_key):
    sign_key, row_key = jax.random.split(seq_key)
    sign_flags = jnp.where(jax.random.permutation(sign_key, SD) < SD // 2, 1, -1).astype(jnp.int32)
    parity = jnp.where(jnp.arange(CPS, dtype=jnp.int32) % 2 == 0, 1, -1).astype(jnp.int32)
    counts = CL // SD + CL // (2 * SD) * sign_flags[:, None] * parity[None, :]
    bounds = jnp.cumsum(counts, axis=0)
    places = jnp.arange(LEN, dtype=jnp.int32)
    source = jnp.sum((bounds[:, places // CL] <= (places % CL)[None, :]).astype(jnp.int32), axis=0)
    ranked = jnp.argsort(source * LEN + places, stable=True).astype(jnp.int32)
    grouped = ranked.reshape(SD, TOK_DEV)
    shuffles = jax.vmap(lambda row_seed: jax.random.permutation(row_seed, TOK_DEV))(jax.random.split(row_key, SD))
    return jnp.take_along_axis(grouped, shuffles.astype(jnp.int32), axis=1).reshape(LEN).astype(jnp.int32)


def draw_cluster_order(key, part):
    key = jax.random.fold_in(key, 7)
    seq_keys = jax.random.split(key, TOKENS // LEN)
    return jax.vmap(sequence_order)(seq_keys).reshape(TOKENS)


def steps_of(stream_key, shape, cuts, low, largest):
    level = 1.0
    for axis_at, shards_of in cuts:
        steps = jax.random.uniform(jax.random.fold_in(jax.random.fold_in(stream_key, 6), axis_at), (shards_of,), jnp.float32, low / len(cuts), largest / len(cuts))
        level = level * jnp.repeat(jnp.exp(steps), shape[axis_at] // shards_of).reshape((-1,) + (1,) * (len(shape) - 1 - axis_at))
    return level


def deal_out(key, own, number, rows, amount, top, limit, skew):
    ranking = jax.random.permutation(key, amount)
    crowded, ordinary = portions_of(amount, rows * top, limit, skew, True), portions_of(amount, rows * top, limit, skew, False)
    places = jnp.arange(amount)

    def named(sizes, turn):
        used = int((sizes > 0).sum())
        fixed = max(1, used // 4)
        passed = fixed + (places - fixed + turn * (used - fixed)) % max(1, amount - fixed)
        return jnp.zeros((amount,), jnp.int32).at[ranking[jnp.where(places < fixed, places, passed)]].set(jnp.asarray(sizes, jnp.int32))

    sizes = jnp.where(number % 4 == 0, named(crowded, number // 4), named(ordinary, number - number // 4 - 1))
    mixed = jax.random.permutation(jax.random.fold_in(own, 3), amount)
    donor, sink = mixed[0:amount // 2 * 2:2], mixed[1:amount // 2 * 2:2]
    margin = jnp.minimum(sizes[donor] - 1, limit - sizes[sink]) // 2
    margin = jnp.where((donor == ranking[0]) | (sink == ranking[0]) | (sizes[sink] == 0), 0, jnp.maximum(margin, 0))
    passed = jax.random.randint(jax.random.fold_in(own, 4), (amount // 2,), 0, 1 << 20) % (margin + 1)
    sizes = sizes.at[donor].add(-passed).at[sink].add(passed)
    members = jnp.searchsorted(jnp.cumsum(sizes), jnp.arange(rows * top), side="right").astype(jnp.int32)
    table = members.reshape(top, rows).T
    table = table[jax.random.permutation(jax.random.fold_in(own, 1), rows)]
    turn = jax.random.randint(jax.random.fold_in(own, 2), (rows, 1), 0, top)
    return jnp.take_along_axis(table, (jnp.arange(top)[None, :] + turn) % top, axis=1)


def portions_of(number_of, total, limit, skew, full):
    portions = [(1 << 20) // math.isqrt(standing ** skew) + 1 for standing in range(1, number_of + 1)]
    largest = limit if full else min(limit, max(-(-total // number_of), total * portions[0] // sum(portions)))
    least = 1 if total - largest >= number_of - 1 else 0
    given, rest = [largest] + [least] * (number_of - 1), total - largest - least * (number_of - 1)
    while rest > 0:
        candidates = [i for i in range(1, number_of) if given[i] < largest] or [i for i in range(1, number_of) if given[i] < limit]
        mass, remaining = sum([portions[i] for i in candidates]), rest
        for i in candidates:
            extra = min(limit - given[i], max(1, remaining * portions[i] // mass), rest)
            given[i] = given[i] + extra
            rest = rest - extra
    return np.array(given)


def gaussian(key, extent, scale, bound, cuts=(), kind=jnp.bfloat16):
    drawn = scale * jax.random.normal(key, extent, jnp.float32)
    if cuts:
        drawn = drawn * steps_of(key, extent, cuts, -0.22, 0.18)
    return jnp.clip(drawn, -bound, bound).astype(kind)


def setup_inputs(seed: int = 0) -> dict:
    splits = jax.random.split(jax.random.key(seed), 11)
    tokens = gaussian(splits[0], (TOKENS, D), 1.0, 6.0, ((0, 32),))
    cotangent = gaussian(splits[1], (TOKENS, D), 1.0, 6.0, ((0, 32),))
    cluster_order = draw_cluster_order(jax.random.fold_in(splits[10], 71), 0)
    block_owner_keys = jax.random.split(jax.random.fold_in(splits[3], 1), NBLK // NBLK)
    block_owner_turns = jax.random.permutation(jax.random.fold_in(splits[3], 3), NBLK // NBLK)
    block_owner = jax.vmap(lambda own, number: deal_out(jax.random.fold_in(splits[3], 2), own, number, NBLK, N_TOK, 1, SLOTS, 1))(block_owner_keys, block_owner_turns).reshape((NBLK, 1))
    master_slots = gaussian(splits[4], (OWNED, BLK, D), (D // 2) ** -0.5, 0.3125, ((0, 8),), jnp.float32)
    moment_one = draw_moment_one(jax.random.fold_in(splits[10], 71), 0)
    moment_two = draw_moment_two(jax.random.fold_in(splits[10], 71), 0)
    vector_master = gaussian(splits[7], (SMALL,), 0.7, 3.0, ((0, 8),), jnp.float32)
    vector_moment_one = draw_vector_moment_one(jax.random.fold_in(splits[10], 71), 0)
    vector_moment_two = draw_vector_moment_two(jax.random.fold_in(splits[10], 71), 0)
    return dict(tokens=tokens, cotangent=cotangent, cluster_order=cluster_order, block_owner=block_owner, master_slots=master_slots, moment_one=moment_one, moment_two=moment_two, vector_master=vector_master, vector_moment_one=vector_moment_one, vector_moment_two=vector_moment_two)


@jax.custom_vjp
def low(v):
    return lax.optimization_barrier(v.astype(jnp.bfloat16)).astype(jnp.float32)

@jax.custom_vjp
def low_back(v):
    return v

def low_keep(v):
    return (low(v), None)

def low_pass(kept, grad):
    return (grad,)

def back_keep(v):
    return (v, None)

def back_low(kept, grad):
    return (low(grad),)
low.defvjp(low_keep, low_pass)
low_back.defvjp(back_keep, back_low)
exact_mode = lax.Precision.HIGHEST
norm_epsilon = 1e-06
beta_first = 0.9
beta_second = 0.999
adam_epsilon = 1e-08
weight_decay = 0.01
rate_matrix = 0.02
rate_vector = 0.2

def product(matrix_a, matrix_b):
    return jnp.dot(matrix_a, matrix_b, precision=exact_mode)

def layer_norm(values, gain_vec, shift_vec):
    centred = values - lax.optimization_barrier(jnp.mean(values, axis=-1, keepdims=True))
    variance = lax.optimization_barrier(jnp.mean(centred * centred, axis=-1, keepdims=True))
    return centred * lax.rsqrt(variance + norm_epsilon) * gain_vec + shift_vec

def slot_positions(block_owner, slot_count):
    owners = block_owner[:, 0]
    blocks = owners.shape[0]
    shared = owners[:, None] == owners[None, :]
    before = jnp.arange(blocks, dtype=jnp.int32)[None, :] < jnp.arange(blocks, dtype=jnp.int32)[:, None]
    earlier = lax.optimization_barrier(jnp.sum((shared & before).astype(jnp.int32), axis=1))
    return (owners * slot_count + earlier).astype(jnp.int32)

def split_matrices(stacked):
    w_query = stacked[0:D]
    w_key = stacked[D:2 * D]
    w_value = stacked[2 * D:3 * D]
    w_out = stacked[3 * D:4 * D]
    w_up = stacked[4 * D:4 * D + FF]
    w_down = stacked[4 * D + FF:4 * D + 2 * FF]
    return (w_query, w_key, w_value, w_out, w_up, w_down)

def split_vectors(vectors):
    pieces = [vectors[index_one * D:(index_one + 1) * D] for index_one in range(8)]
    return tuple(pieces) + (vectors[8 * D:8 * D + FF],)

def adam_update(grad_now, weight_old, first_old, second_old, rate_step):
    first_new = beta_first * first_old + (1.0 - beta_first) * grad_now
    second_new = beta_second * second_old + (1.0 - beta_second) * grad_now * grad_now
    first_hat = first_new / (1.0 - beta_first ** STEP)
    second_hat = second_new / (1.0 - beta_second ** STEP)
    weight_new = weight_old - rate_step * (first_hat / (jnp.sqrt(second_hat) + adam_epsilon) + weight_decay * weight_old)
    return (first_new, second_new, weight_new)

def sequence_layer(params, x_seq, order_seq):
    w_query, w_key, w_value, w_out, w_up, w_down = split_matrices(params[0])
    b_query, b_value, b_out, b_down, gain_one, shift_one, gain_two, shift_two, b_up = split_vectors(params[1])
    places = jnp.arange(LEN, dtype=jnp.int32)
    inverse = jnp.zeros((LEN,), jnp.int32).at[order_seq].set(places)
    x_clus = low_back(x_seq[inverse])
    query_rows = low(low_back(product(x_clus, w_query) + b_query))
    key_rows = low(low_back(product(x_clus, w_key)))
    value_rows = low(low_back(product(x_clus, w_value) + b_value))
    head_shape = (LEN // CL, CL, HEADS, HD)
    scores = low_back(jnp.einsum('nqhd,nkhd->nhqk', query_rows.reshape(head_shape), key_rows.reshape(head_shape), precision=exact_mode) / math.sqrt(HD))
    attention = jax.nn.softmax(scores, axis=-1)
    log_attention = jax.nn.log_softmax(scores, axis=-1)
    entropy = -lax.optimization_barrier(jnp.sum(attention * log_attention, axis=-1))
    entropy = lax.optimization_barrier(jnp.mean(entropy, axis=1)).reshape(LEN)
    head_out = jnp.einsum('nhqk,nkhd->nqhd', low(attention), value_rows.reshape(head_shape), precision=exact_mode).reshape(LEN, D)
    head_out = low(low_back(head_out))
    attended = head_out[order_seq]
    resid_one = x_seq + low_back(product(attended, w_out) + b_out)
    hidden = layer_norm(resid_one, gain_one, shift_one)
    upper_rows = low_back(product(low(hidden), w_up.T) + b_up)
    act_rows = low(jax.nn.gelu(upper_rows, approximate=False))
    branch = low_back(product(act_rows, w_down) + b_down)
    return (layer_norm(hidden + branch, gain_two, shift_two), entropy[order_seq])

def reference(tokens, cotangent, cluster_order, block_owner, master_slots, moment_one, moment_two, vector_master, vector_moment_one, vector_moment_two):
    positions = slot_positions(block_owner, SLOTS)
    weight_low = master_slots.astype(jnp.bfloat16).astype(jnp.float32)
    stacked = weight_low[positions].reshape(WROWS, D)
    vectors = vector_master.astype(jnp.bfloat16).astype(jnp.float32)
    seq_count = TOKENS // LEN
    order_seqs = cluster_order.reshape(seq_count, LEN)

    def forward(params, inputs):

        def one_sequence(packed):
            return sequence_layer(params, packed[0], packed[1])
        outputs, entropy = lax.map(jax.checkpoint(one_sequence), (inputs.reshape(seq_count, LEN, D), order_seqs))
        return (outputs.reshape(TOKENS, D), entropy.reshape(TOKENS))
    output, pull_back, entropy = jax.vjp(forward, (stacked, vectors), tokens.astype(jnp.float32), has_aux=True)
    param_grads, input_grad = pull_back(cotangent.astype(jnp.float32))
    grad_slots = jnp.zeros((OWNED, BLK, D), jnp.float32).at[positions].set(param_grads[0].reshape(NBLK, BLK, D))
    first_new, second_new, master_new = adam_update(grad_slots, master_slots, moment_one, moment_two, rate_matrix)
    vec_first, vec_second, vec_new = adam_update(param_grads[1], vector_master, vector_moment_one, vector_moment_two, rate_vector)
    rows = jnp.arange(TOKENS, dtype=jnp.int32)
    tok_place = rows // TOK_DEV % N_TOK
    cluster = tok_place // SD * CPS + cluster_order // CL
    target = cluster % N_TOK
    occupancy = jax.ops.segment_sum(jnp.ones((TOKENS,), jnp.int32), (tok_place * N_TOK + target).astype(jnp.int32), num_segments=N_TOK * N_TOK).reshape(N_TOK, N_TOK).astype(jnp.int32)
    return (output.astype(jnp.bfloat16), input_grad.astype(jnp.bfloat16), grad_slots, first_new, second_new, master_new, master_new.astype(jnp.bfloat16), param_grads[1], vec_first, vec_second, vec_new, vec_new.astype(jnp.bfloat16), entropy.astype(jnp.bfloat16), occupancy)
```

```python
import functools
import math

import jax
import jax.numpy as jnp
from jax import lax
from jax.experimental import pallas as pl
from jax.experimental.pallas import tpu as pltpu
from jax.sharding import PartitionSpec as P

D = 768
HEADS = 12
HD = 64
FF = 3072
SD = 4
CL = 128
NBLK = 96
STEP = 10
CPS = 32
WROWS = 9216
BLK = 96
ROWS = 1024
PAIRS = HEADS // 2
PW = 2 * HD
TM = 256
META = 16
FC = 768

norm_epsilon = 1e-06
beta_first = 0.9
beta_second = 0.999
adam_epsilon = 1e-08
weight_decay = 0.01
rate_matrix = 0.02
rate_vector = 0.2

BF = jnp.bfloat16
F32 = jnp.float32
I32 = jnp.int32

VMEM = pl.BlockSpec(memory_space=pltpu.VMEM)
SMEM = pl.BlockSpec(memory_space=pltpu.SMEM)
ANY = pl.BlockSpec(memory_space=pl.ANY)

NN = (((1,), (0,)), ((), ()))
NT = (((1,), (1,)), ((), ()))
TN = (((0,), (0,)), ((), ()))


def mm(a, b, dims=NN):
    return lax.dot_general(a, b, dims, preferred_element_type=F32)


def slot_positions(block_owner, slot_count):
    owners = block_owner[:, 0]
    blocks = owners.shape[0]
    shared = owners[:, None] == owners[None, :]
    before = (
        jnp.arange(blocks, dtype=jnp.int32)[None, :] < jnp.arange(blocks, dtype=jnp.int32)[:, None]
    )
    earlier = jnp.sum((shared & before).astype(jnp.int32), axis=1)
    return owners * slot_count + earlier


def adam_update(grad_now, weight_old, first_old, second_old, rate_step):
    first_new = beta_first * first_old + (1.0 - beta_first) * grad_now
    second_new = beta_second * second_old + (1.0 - beta_second) * grad_now * grad_now
    first_hat = first_new / (1.0 - beta_first**STEP)
    second_hat = second_new / (1.0 - beta_second**STEP)
    weight_new = weight_old - rate_step * (
        first_hat / (jnp.sqrt(second_hat) + adam_epsilon) + weight_decay * weight_old
    )
    return (first_new, second_new, weight_new)


def route_slots(order, seat, cap):
    cluster = order // CL
    rel = lax.rem(cluster, SD) ^ seat
    place = (cluster // SD) * CL + lax.rem(order, CL) + 1
    chosen = lax.broadcasted_iota(I32, (8, ROWS), 0) == rel
    chosen_low = jnp.where(chosen, 1.0, 0.0).astype(BF)
    before = lax.broadcasted_iota(I32, (ROWS, ROWS), 0) < lax.broadcasted_iota(I32, (ROWS, ROWS), 1)
    before_low = jnp.where(before, 1.0, 0.0).astype(BF)
    running = mm(chosen_low, before_low)
    rank = jnp.sum(jnp.where(chosen, running, 0.0), axis=0, keepdims=True).astype(I32)
    return rel * cap + rank, place


def slot_matrix(slots, at, cap):
    rows = lax.broadcasted_iota(I32, (cap, ROWS), 0) + at * cap
    return jnp.where(rows == slots, 1.0, 0.0).astype(BF)


def send_kernel(cap, tokens, cotangent, order, send_x, send_c, meta):
    seat = lax.rem(lax.axis_index("tok"), SD)
    slots, place = route_slots(order[...], seat, cap)
    digits = jnp.concatenate([place // CL, lax.rem(place, CL)] + [place * 0] * 6, axis=0).astype(F32).astype(BF)
    for at in range(SD):
        picked = slot_matrix(slots, at, cap)
        send_x[at] = mm(picked, tokens[...]).astype(BF)
        send_c[at] = mm(picked, cotangent[...]).astype(BF)
        coded = mm(digits, picked, NT)
        line = jnp.concatenate([coded[0:1], coded[1:2]], axis=1)
        meta[at] = jnp.broadcast_to(line, (META, D)).astype(BF)


def return_kernel(cap, order, back, back_meta, out, entropy):
    seat = lax.rem(lax.axis_index("tok"), SD)
    slots, _ = route_slots(order[...], seat, cap)
    picked = jnp.concatenate([slot_matrix(slots, at, cap) for at in range(SD)], axis=0)
    rows = back[...].reshape(SD * cap, D)
    out[...] = mm(picked, rows, TN).astype(BF)
    if entropy is not None:
        line = jnp.concatenate([back_meta[at, 0:8, 0:cap] for at in range(SD)], axis=1)
        entropy[...] = mm(line, picked).astype(BF)


def swap_blocks(blocks):
    n = lax.axis_size("tok")
    parts = [blocks[0]]
    for k in range(1, SD):
        parts.append(lax.ppermute(blocks[k], "tok", [(i, i ^ k) for i in range(n)]))
    return jnp.stack(parts)


V_BQ, V_BV, V_BO, V_BD, V_G1, V_C1, V_G2, V_C2 = range(8)


def erf_parts(v):
    z = jnp.abs(v) * (1.0 / math.sqrt(2.0))
    t = 1.0 / (1.0 + 0.3275911 * z)
    e = jnp.exp(-z * z)
    poly = 0.5 * 1.061405429
    for c in (-1.453152027, 1.421413741, -0.284496736, 0.254829592):
        poly = poly * t + 0.5 * c
    tail = poly * t * e
    return jnp.where(v >= 0.0, 1.0 - tail, tail), e


def lane_sum(x):
    return jnp.sum(x, axis=1, keepdims=True)


def layer_kernel(
    cap,
    pos,
    slots,
    vecs,
    b_u,
    recv_x,
    recv_c,
    meta,
    ret_out,
    ret_meta,
    ret_ing,
    grads,
    gvec,
    g_bu,
    w,
    place,
    xbuf,
    x_c,
    heads,
    act,
    d_up,
    d_q,
    d_k,
    d_v,
    d_proj,
    hid,
    d_br,
    out_c,
    ing_c,
    ent,
    q_t,
    k_t,
    v_t,
    p_t,
    gp_t,
    dh_t,
    n1_t,
    hid_t,
    stage,
    w_sem,
    x_sem,
    g_sem,
):
    inv = 1.0 / math.sqrt(HD)

    def w_copy(b):
        return pltpu.make_async_copy(slots.at[pos[b]], w.at[pl.ds(b * BLK, BLK)], w_sem)

    def start_w(b, c):
        w_copy(b).start()
        return c

    def wait_w(b, c):
        w_copy(b).wait()
        return c

    cx = pltpu.make_async_copy(recv_x, xbuf, x_sem)
    cx.start()
    lax.fori_loop(0, NBLK, start_w, 0)
    gvec[...] = jnp.zeros_like(gvec)
    g_bu[...] = jnp.zeros_like(g_bu)

    for k in range(SD):
        hi = meta[k, 0:8, 0:cap].astype(F32)[0:1]
        lo = meta[k, 0:8, cap : 2 * cap].astype(F32)[0:1]
        at = (hi * CL + lo).astype(I32)
        rows = lax.broadcasted_iota(I32, (ROWS, cap), 0) + 1
        place[:, k * cap : (k + 1) * cap] = jnp.where(rows == at, 1.0, 0.0).astype(BF)
    def seat_rows(to):
        def body(t, c):
            rows = pl.ds(pl.multiple_of(t * TM, TM), TM)
            to[rows, :] = mm(place[rows, :], xbuf[...].reshape(SD * cap, D)).astype(BF)
            return c

        lax.fori_loop(0, ROWS // TM, body, 0)

    cx.wait()
    seat_rows(x_c)
    cc = pltpu.make_async_copy(recv_c, xbuf, x_sem)
    cc.start()
    cc.wait()
    seat_rows(d_br)
    lax.fori_loop(0, NBLK, wait_w, 0)

    wq, wk, wv, wo = (w.at[pl.ds(i * D, D)] for i in range(4))
    wu = w.at[pl.ds(4 * D, FF)]
    wd = w.at[pl.ds(4 * D + FF, FF)]

    lane = lax.broadcasted_iota(I32, (1, PW), 1)
    m0 = jnp.where(lane < HD, 1.0, 0.0).astype(BF)
    m1 = jnp.where(lane < HD, 0.0, 1.0).astype(BF)
    first_half = lax.broadcasted_iota(I32, (CL, PW), 1) < HD
    eye = lax.broadcasted_iota(I32, (CL, CL), 0) == lax.broadcasted_iota(I32, (CL, CL), 1)

    def vec(i):
        return vecs[i : i + 1, :]

    def add_vec(i, value):
        gvec[i : i + 1, :] += jnp.sum(value, axis=0, keepdims=True)

    def tile(t, carry):
        r0 = pl.multiple_of(t * TM, TM)
        rows = pl.ds(r0, TM)
        x = x_c[rows, :]
        q_t[...] = ((mm(x, wq[...]) + vec(V_BQ)).astype(BF).astype(F32) * inv).astype(BF)
        k_t[...] = mm(x, wk[...]).astype(BF)
        v_t[...] = (mm(x, wv[...]) + vec(V_BV)).astype(BF)

        def attend(c, z):
            cr = pl.ds(pl.multiple_of(c * CL, CL), CL)
            total = jnp.zeros((CL, 1), F32)
            for p in range(PAIRS):
                ps = slice(p * PW, (p + 1) * PW)
                kp, vp = k_t[cr, ps], v_t[cr, ps]
                s = mm(q_t[cr, ps], jnp.concatenate([kp * m0, kp * m1], axis=0), NT)
                halves = []
                for h in range(2):
                    sh = s[:, h * CL : (h + 1) * CL]
                    sh = sh - jnp.max(sh, axis=1, keepdims=True)
                    e = jnp.exp(sh)
                    tot = lane_sum(e)
                    r = 1.0 / tot
                    total += jnp.log(tot) - lane_sum(e * sh) * r
                    halves.append((e * r).astype(BF))
                weights = jnp.concatenate(halves, axis=1)
                p_t[c, p] = weights
                o = mm(weights, jnp.concatenate([vp * m0, vp * m1], axis=0))
                heads[pl.ds(pl.multiple_of(r0 + c * CL, CL), CL), ps] = o.astype(BF)
            line = jnp.sum(jnp.where(eye, total * (1.0 / HEADS), 0.0), axis=0, keepdims=True)
            ent[:, pl.ds(pl.multiple_of(r0 + c * CL, CL), CL)] = jnp.broadcast_to(line, (8, CL))
            return z

        lax.fori_loop(0, TM // CL, attend, 0)

        r1 = x.astype(F32) + mm(heads[rows, :], wo[...]) + vec(V_BO)
        c1 = r1 - lane_sum(r1) * (1.0 / D)
        rs1 = lax.rsqrt(lane_sum(c1 * c1) * (1.0 / D) + norm_epsilon)
        n1 = c1 * rs1
        hidden = n1 * vec(V_G1) + vec(V_C1)
        hid[rows, :] = hidden.astype(BF)
        n1_t[...] = n1
        hid_t[...] = hidden

        def widen(f, z):
            fs = pl.ds(pl.multiple_of(f * FC, FC), FC)
            up = mm(hid[rows, :], wu[fs, :], NT) + b_u[:, fs]
            phi, e = erf_parts(up)
            act[rows, fs] = (up * phi).astype(BF)
            gp_t[:, fs] = (phi + up * (e * (1.0 / math.sqrt(2.0 * math.pi)))).astype(BF)
            return z

        lax.fori_loop(0, FF // FC, widen, 0)
        r2 = hid_t[...] + mm(act[rows, :], wd[...]) + vec(V_BD)
        c2 = r2 - lane_sum(r2) * (1.0 / D)
        rs2 = lax.rsqrt(lane_sum(c2 * c2) * (1.0 / D) + norm_epsilon)
        n2 = c2 * rs2
        out_c[rows, :] = (n2 * vec(V_G2) + vec(V_C2)).astype(BF)

        e2 = d_br[rows, :].astype(F32)
        add_vec(V_G2, e2 * n2)
        add_vec(V_C2, e2)
        eg = e2 * vec(V_G2)
        d_r2 = rs2 * (eg - lane_sum(eg) * (1.0 / D) - n2 * (lane_sum(eg * n2) * (1.0 / D)))
        d_br[rows, :] = d_r2.astype(BF)
        add_vec(V_BD, d_br[rows, :].astype(F32))
        hid_t[...] = d_r2

        def widen_back(f, z):
            fs = pl.ds(pl.multiple_of(f * FC, FC), FC)
            du = (mm(d_br[rows, :], wd[fs, :], NT) * gp_t[:, fs].astype(F32)).astype(BF)
            d_up[rows, fs] = du
            g_bu[:, fs] += jnp.sum(du.astype(F32), axis=0, keepdims=True)
            return z

        lax.fori_loop(0, FF // FC, widen_back, 0)
        n1 = n1_t[...]
        d_h = hid_t[...] + mm(d_up[rows, :], wu[...])
        add_vec(V_G1, d_h * n1)
        add_vec(V_C1, d_h)
        eg = d_h * vec(V_G1)
        d_r1 = rs1 * (eg - lane_sum(eg) * (1.0 / D) - n1 * (lane_sum(eg * n1) * (1.0 / D)))
        d_proj[rows, :] = d_r1.astype(BF)
        hid_t[...] = d_r1
        add_vec(V_BO, d_proj[rows, :].astype(F32))
        dh_t[...] = mm(d_proj[rows, :], wo[...], NT).astype(BF)

        def attend_back(c, z):
            cr = pl.ds(pl.multiple_of(c * CL, CL), CL)
            gr = pl.ds(pl.multiple_of(r0 + c * CL, CL), CL)
            for p in range(PAIRS):
                ps = slice(p * PW, (p + 1) * PW)
                qp, kp, vp, dh = q_t[cr, ps], k_t[cr, ps], v_t[cr, ps], dh_t[cr, ps]
                weights = p_t[c, p]
                d_w = mm(dh, jnp.concatenate([vp * m0, vp * m1], axis=0), NT)
                halves = []
                for h in range(2):
                    wh = weights[:, h * CL : (h + 1) * CL].astype(F32)
                    dwh = d_w[:, h * CL : (h + 1) * CL]
                    halves.append((wh * (dwh - lane_sum(dwh * wh))).astype(BF))
                d_s = jnp.concatenate(halves, axis=1)
                d_q[gr, ps] = (mm(d_s, jnp.concatenate([kp * m0, kp * m1], axis=0)) * inv).astype(BF)
                dk = mm(d_s, qp, TN)
                d_k[gr, ps] = jnp.where(first_half, dk[0:CL], dk[CL:]).astype(BF)
                dv = mm(weights, dh, TN)
                d_v[gr, ps] = jnp.where(first_half, dv[0:CL], dv[CL:]).astype(BF)
            return z

        lax.fori_loop(0, TM // CL, attend_back, 0)
        dq, dk, dv = d_q[rows, :], d_k[rows, :], d_v[rows, :]
        add_vec(V_BQ, dq.astype(F32))
        add_vec(V_BV, dv.astype(F32))
        d_x = mm(dq, wq[...], NT) + mm(dk, wk[...], NT) + mm(dv, wv[...], NT)
        ing_c[rows, :] = (hid_t[...] + d_x.astype(BF).astype(F32)).astype(BF)
        return carry

    lax.fori_loop(0, ROWS // TM, tile, 0)

    def back_rows(source, to):
        for k in range(SD):
            xbuf[k] = mm(place[:, k * cap : (k + 1) * cap], source[...], TN).astype(BF)
        return pltpu.make_async_copy(xbuf, to, x_sem)

    for k in range(SD):
        line = mm(ent[...].astype(BF), place[:, k * cap : (k + 1) * cap])
        ret_meta[k] = jnp.concatenate([line, line], axis=1)[0:1].astype(BF) * jnp.ones((META, 1), BF)
    back_out = back_rows(out_c, ret_out)
    back_out.start()

    WC = 4 * BLK

    def g_copy(chunk, j, at):
        return pltpu.make_async_copy(
            stage.at[at, pl.ds(j * BLK, BLK)], grads.at[pos[chunk * 4 + j]], g_sem.at[at]
        )

    def put(chunk, left, right):
        at = lax.rem(chunk, 2)

        @pl.when(chunk >= 2)
        def _():
            for j in range(4):
                g_copy(chunk - 2, j, at).wait()

        stage[at] = mm(left, right, TN).astype(BF)
        for j in range(4):
            g_copy(chunk, j, at).start()

    def wide(left, right, first):
        def body(j, c):
            put(first + j, left[:, pl.ds(pl.multiple_of(j * WC, WC), WC)], right[...])
            return c

        lax.fori_loop(0, left.shape[1] // WC, body, 0)

    first = 0
    for left, right in ((x_c, d_q), (x_c, d_k), (x_c, d_v), (heads, d_proj), (d_up, hid), (act, d_br)):
        wide(left, right, first)
        first += left.shape[1] // WC
    back_out.wait()
    back_ing = back_rows(ing_c, ret_ing)
    back_ing.start()
    back_ing.wait()
    last = WROWS // WC
    last = WROWS // WC
    for ch in (last - 2, last - 1):
        for j in range(4):
            g_copy(ch, j, ch % 2).wait()


def local(
    tokens,
    cotangent,
    cluster_order,
    block_owner,
    master_slots,
    moment_one,
    moment_two,
    vector_master,
    vector_moment_one,
    vector_moment_two,
):
    tok_count = lax.axis_size("tok")
    tok_index = lax.axis_index("tok")
    slot_count = master_slots.shape[0]
    cap = tok_count // SD * (max(1, CPS // tok_count) * 3 * CL // (2 * SD))
    total_slots = tok_count * slot_count
    positions = slot_positions(block_owner, slot_count)
    order = cluster_order.reshape(1, ROWS)

    slots_low = lax.all_gather(master_slots.astype(BF), "tok", axis=0, tiled=True)
    vector_low = lax.all_gather(vector_master.astype(BF), "tok", axis=0, tiled=True)

    cluster = tok_index // SD * CPS + cluster_order // CL
    target = cluster % tok_count
    chosen = target[None, :] == jnp.arange(tok_count, dtype=jnp.int32)[:, None]
    sent_counts = jnp.sum(chosen.astype(F32), axis=1)
    own_row = (jnp.arange(tok_count, dtype=jnp.int32) == tok_index).astype(F32)
    occupancy = lax.psum(own_row[:, None] * sent_counts[None, :], ("tok", "rep")).astype(jnp.int32)

    block = jax.ShapeDtypeStruct((SD, cap, D), BF)
    meta_shape = jax.ShapeDtypeStruct((SD, META, D), BF)
    send_x, send_c, meta = pl.pallas_call(
        functools.partial(send_kernel, cap),
        out_shape=(block, block, meta_shape),
        in_specs=[VMEM] * 3,
        out_specs=(VMEM,) * 3,
        compiler_params=pltpu.CompilerParams(vmem_limit_bytes=40 << 20),
        name="send_rows",
    )(tokens, cotangent, order)
    recv_x, recv_c, recv_meta = swap_blocks(send_x), swap_blocks(send_c), swap_blocks(meta)

    vectors = vector_low.astype(F32)
    ret_out, ret_meta, ret_ing, grads, gvec, g_bu = pl.pallas_call(
        functools.partial(layer_kernel, cap),
        out_shape=(
            block,
            meta_shape,
            block,
            jax.ShapeDtypeStruct((total_slots, BLK, D), BF),
            jax.ShapeDtypeStruct((8, D), F32),
            jax.ShapeDtypeStruct((1, FF), F32),
        ),
        in_specs=[SMEM, ANY, VMEM, VMEM, ANY, ANY, VMEM],
        out_specs=(ANY, VMEM, ANY, ANY, VMEM, VMEM),
        scratch_shapes=[
            pltpu.VMEM((WROWS, D), BF),
            pltpu.VMEM((ROWS, SD * cap), BF),
            pltpu.VMEM((SD, cap, D), BF),
            pltpu.VMEM((ROWS, D), BF),
            pltpu.VMEM((ROWS, D), BF),
            pltpu.VMEM((ROWS, FF), BF),
            pltpu.VMEM((ROWS, FF), BF),
            pltpu.VMEM((ROWS, D), BF),
            pltpu.VMEM((ROWS, D), BF),
            pltpu.VMEM((ROWS, D), BF),
            pltpu.VMEM((ROWS, D), BF),
            pltpu.VMEM((ROWS, D), BF),
            pltpu.VMEM((ROWS, D), BF),
            pltpu.VMEM((ROWS, D), BF),
            pltpu.VMEM((ROWS, D), BF),
            pltpu.VMEM((8, ROWS), F32),
            pltpu.VMEM((TM, D), BF),
            pltpu.VMEM((TM, D), BF),
            pltpu.VMEM((TM, D), BF),
            pltpu.VMEM((TM // CL, PAIRS, CL, 2 * CL), BF),
            pltpu.VMEM((TM, FF), BF),
            pltpu.VMEM((TM, D), BF),
            pltpu.VMEM((TM, D), F32),
            pltpu.VMEM((TM, D), F32),
            pltpu.VMEM((2, 4 * BLK, D), BF),
            pltpu.SemaphoreType.DMA,
            pltpu.SemaphoreType.DMA,
            pltpu.SemaphoreType.DMA((2,)),
        ],
        compiler_params=pltpu.CompilerParams(vmem_limit_bytes=63 << 20),
        name="layer",
    )(positions, slots_low, vectors[: 8 * D].reshape(8, D), vectors[8 * D :].reshape(1, FF), recv_x, recv_c, recv_meta)

    back_out, back_meta, back_ing = swap_blocks(ret_out), swap_blocks(ret_meta), swap_blocks(ret_ing)
    row_block = jax.ShapeDtypeStruct((ROWS, D), BF)
    output, entropy = pl.pallas_call(
        functools.partial(return_kernel, cap),
        out_shape=(row_block, jax.ShapeDtypeStruct((8, ROWS), BF)),
        in_specs=[VMEM] * 3,
        out_specs=(VMEM,) * 2,
        compiler_params=pltpu.CompilerParams(vmem_limit_bytes=40 << 20),
        name="return_output",
    )(order, back_out, back_meta)
    input_grad = pl.pallas_call(
        lambda o, b, r: return_kernel(cap, o, b, None, r, None),
        out_shape=row_block,
        in_specs=[VMEM] * 2,
        out_specs=VMEM,
        compiler_params=pltpu.CompilerParams(vmem_limit_bytes=40 << 20),
        name="return_grad",
    )(order, back_ing)

    used = jnp.any(
        positions[None, :] == (tok_index * slot_count + jnp.arange(slot_count, dtype=I32))[:, None], axis=1
    )
    owned_grad = lax.psum_scatter(grads, "tok", scatter_dimension=0, tiled=True)
    owned_grad = lax.psum(owned_grad, "rep").astype(F32)
    owned_grad = jnp.where(used[:, None, None], owned_grad, 0.0)
    grad_vector = jnp.concatenate([gvec.reshape(-1), g_bu.reshape(-1)])
    vec_owned = lax.psum_scatter(grad_vector, "tok", scatter_dimension=0, tiled=True)
    vec_owned = lax.psum(vec_owned, "rep")
    first_new, second_new, master_new = adam_update(
        owned_grad, master_slots, moment_one, moment_two, rate_matrix
    )
    vec_first, vec_second, vec_new = adam_update(
        vec_owned, vector_master, vector_moment_one, vector_moment_two, rate_vector
    )
    return (
        output,
        input_grad,
        owned_grad,
        first_new,
        second_new,
        master_new,
        master_new.astype(BF),
        vec_owned,
        vec_first,
        vec_second,
        vec_new,
        vec_new.astype(BF),
        entropy[0],
        occupancy,
    )


def solution(mesh):
    placed = (
        P(("rep", "tok"), None),
        P(("rep", "tok"), None),
        P(("rep", "tok")),
        P(),
        P("tok", None, None),
        P("tok", None, None),
        P("tok", None, None),
        P("tok"),
        P("tok"),
        P("tok"),
    )
    return jax.shard_map(
        local,
        mesh=mesh,
        in_specs=placed,
        out_specs=(
            P(("rep", "tok"), None),
            P(("rep", "tok"), None),
            P("tok", None, None),
            P("tok", None, None),
            P("tok", None, None),
            P("tok", None, None),
            P("tok", None, None),
            P("tok"),
            P("tok"),
            P("tok"),
            P("tok"),
            P("tok"),
            P(("rep", "tok")),
            P(),
        ),
        check_vma=False,
    )
```

```python
import functools
import math

import jax
import jax.numpy as jnp
from jax import lax
from jax.experimental import pallas as pl
from jax.experimental.pallas import tpu as pltpu
from jax.sharding import PartitionSpec as P

D = 768
HEADS = 12
HD = 64
FF = 3072
SD = 4
CL = 128
NBLK = 96
STEP = 10
CPS = 32
WROWS = 9216
BLK = 96
ROWS = 1024
PAIRS = HEADS // 2
PW = 2 * HD
TM = 256
META = 16
FC = 768

norm_epsilon = 1e-06
beta_first = 0.9
beta_second = 0.999
adam_epsilon = 1e-08
weight_decay = 0.01
rate_matrix = 0.02
rate_vector = 0.2

BF = jnp.bfloat16
F32 = jnp.float32
I32 = jnp.int32

VMEM = pl.BlockSpec(memory_space=pltpu.VMEM)
SMEM = pl.BlockSpec(memory_space=pltpu.SMEM)
ANY = pl.BlockSpec(memory_space=pl.ANY)

NN = (((1,), (0,)), ((), ()))
NT = (((1,), (1,)), ((), ()))
TN = (((0,), (0,)), ((), ()))


def mm(a, b, dims=NN):
    return lax.dot_general(a, b, dims, preferred_element_type=F32)


def slot_positions(block_owner, slot_count):
    owners = block_owner[:, 0]
    blocks = owners.shape[0]
    shared = owners[:, None] == owners[None, :]
    before = (
        jnp.arange(blocks, dtype=jnp.int32)[None, :] < jnp.arange(blocks, dtype=jnp.int32)[:, None]
    )
    earlier = jnp.sum((shared & before).astype(jnp.int32), axis=1)
    return owners * slot_count + earlier


def adam_update(grad_now, weight_old, first_old, second_old, rate_step):
    first_new = beta_first * first_old + (1.0 - beta_first) * grad_now
    second_new = beta_second * second_old + (1.0 - beta_second) * grad_now * grad_now
    first_hat = first_new / (1.0 - beta_first**STEP)
    second_hat = second_new / (1.0 - beta_second**STEP)
    weight_new = weight_old - rate_step * (
        first_hat / (jnp.sqrt(second_hat) + adam_epsilon) + weight_decay * weight_old
    )
    return (first_new, second_new, weight_new)


def route_slots(order, seat, cap):
    cluster = order // CL
    rel = lax.rem(cluster, SD) ^ seat
    place = (cluster // SD) * CL + lax.rem(order, CL) + 1
    chosen = lax.broadcasted_iota(I32, (8, ROWS), 0) == rel
    chosen_low = jnp.where(chosen, 1.0, 0.0).astype(BF)
    before = lax.broadcasted_iota(I32, (ROWS, ROWS), 0) < lax.broadcasted_iota(I32, (ROWS, ROWS), 1)
    before_low = jnp.where(before, 1.0, 0.0).astype(BF)
    running = mm(chosen_low, before_low)
    rank = jnp.sum(jnp.where(chosen, running, 0.0), axis=0, keepdims=True).astype(I32)
    return rel * cap + rank, place


def slot_matrix(slots, at, cap):
    rows = lax.broadcasted_iota(I32, (cap, ROWS), 0) + at * cap
    return jnp.where(rows == slots, 1.0, 0.0).astype(BF)


def send_kernel(cap, tokens, cotangent, order, send_x, send_c, meta):
    seat = lax.rem(lax.axis_index("tok"), SD)
    slots, place = route_slots(order[...], seat, cap)
    digits = jnp.concatenate([place // CL, lax.rem(place, CL)] + [place * 0] * 6, axis=0).astype(F32).astype(BF)
    for at in range(SD):
        picked = slot_matrix(slots, at, cap)
        send_x[at] = mm(picked, tokens[...]).astype(BF)
        send_c[at] = mm(picked, cotangent[...]).astype(BF)
        coded = mm(digits, picked, NT)
        line = jnp.concatenate([coded[0:1], coded[1:2]], axis=1)
        meta[at] = jnp.broadcast_to(line, (META, D)).astype(BF)


def remote(src, dst, send_sem, recv_sem, tok, rep):
    return pltpu.make_async_remote_copy(
        src_ref=src,
        dst_ref=dst,
        send_sem=send_sem,
        recv_sem=recv_sem,
        device_id={"tok": tok, "rep": rep},
        device_id_type=pl.DeviceIdType.MESH,
    )


def loop(n, body):
    def run(i, c):
        body(i)
        return c

    lax.fori_loop(0, n, run, 0)


class Place:
    def __init__(self):
        self.me = me = lax.axis_index("tok")
        self.z = z = lax.axis_index("rep")
        core, x, y = me % 2, (me // 2) % 2, me // 4
        self.twin = me + 1 - 2 * core
        self.xn = me + 2 - 4 * x
        self.yn = me + 4 - 8 * y
        self.dn = self.xn + 4 - 8 * y
        self.side = z % 2
        self.zp = z + 1 - 2 * self.side

    def twin_of(self, tok):
        return tok + 1 - 2 * (tok % 2)

    def greet(self, peers):
        barrier = pltpu.get_barrier_semaphore()
        for tok, rep in peers:
            pl.semaphore_signal(
                barrier, inc=1, device_id={"tok": tok, "rep": rep}, device_id_type=pl.DeviceIdType.MESH
            )
        return lambda: pl.semaphore_wait(barrier, len(peers))


def gather_kernel(
    cap,
    count,
    tokens,
    cotangent,
    order,
    master,
    vector,
    slots,
    recv_x,
    recv_c,
    recv_meta,
    small,
    own,
    send_x,
    send_c,
    meta,
    mine,
    by_z,
    by_tok,
    x_s,
    x_r,
    y_s,
    y_r,
    d_s,
    d_r,
    zx_s,
    zx_r,
    zd_s,
    zd_r,
    p_s,
    p_r,
    row_s,
    row_r,
    z_s,
    z_r,
    t_s,
    t_r,
    local_s,
):
    at = Place()
    me, z, side = at.me, at.z, at.side
    n_tok, n_rep = 8, 4
    peers = [((me + d) % n_tok, z) for d in range(1, n_tok)] + [(me, (z + d) % n_rep) for d in range(1, n_rep)]
    wait_peers = at.greet(peers)
    for s in range(count):
        own[s] = master[s].astype(BF)
    wait_peers()

    half = count // 2

    def slot(owner, s):
        return slots.at[owner * count + s]

    def to_x(s):
        return remote(own.at[s], slot(me, s), x_s.at[s], x_r.at[s], at.xn, z)

    def to_y(s):
        return remote(own.at[s], slot(me, s), y_s.at[s], y_r.at[s], at.yn, z)

    def on_y(s):
        return remote(slot(at.xn, s), slot(at.xn, s), d_s.at[s], d_r.at[s], at.yn, z)

    def x_on_z(s):
        return remote(slot(at.xn, s), slot(at.xn, s), zx_s.at[s], zx_r.at[s], me, at.zp)

    def d_on_z(s):
        return remote(slot(at.dn, s), slot(at.dn, s), zd_s.at[s], zd_r.at[s], me, at.zp)

    owners = (me, at.xn, at.yn, at.dn)

    def to_twin(q, s):
        src = own.at[s] if q == 0 else slot(owners[q], s)
        return remote(src, slot(owners[q], s), p_s.at[q, s], p_r.at[q, s], at.twin, z)

    def near(j):
        return (half + 1) * side + j

    def far(j):
        return (half + 1) * (1 - side) + j

    loop(half, lambda j: to_x(near(j)).start())
    to_x(half).start()
    for s in range(3):
        to_y(s).start()
    loop(count, lambda s: to_twin(0, s).start())
    keep = pltpu.make_async_copy(own, slots.at[pl.ds(me * count, count)], local_s.at[0])
    keep.start()

    seat = me % SD
    slot_of, place = route_slots(order[...], seat, cap)
    digits = jnp.concatenate([place // CL, lax.rem(place, CL)] + [place * 0] * 6, axis=0).astype(F32).astype(BF)
    for k in range(SD):
        picked = slot_matrix(slot_of, k, cap)
        send_x[k] = mm(picked, tokens[...]).astype(BF)
        send_c[k] = mm(picked, cotangent[...]).astype(BF)
        coded = mm(digits, picked, NT)
        line = jnp.concatenate([coded[0:1], coded[1:2]], axis=1)
        meta[k] = jnp.broadcast_to(line, (META, D)).astype(BF)
    seats = (me, at.twin, at.xn, at.twin_of(at.xn))
    rows_of = ((meta, recv_meta), (send_x, recv_x), (send_c, recv_c))

    def row_copy(i, k):
        src, dst = rows_of[i]
        return remote(src.at[k], dst.at[k], row_s.at[i, k], row_r.at[i, k], seats[k], z)

    def row_keep(i):
        src, dst = rows_of[i]
        return pltpu.make_async_copy(src.at[0], dst.at[0], local_s.at[1 + i])

    for i in range(3):
        row_keep(i).start()
        for k in (2, 3, 1):
            row_copy(i, k).start()

    residue = lax.rem(me // SD * CPS + order[...] // CL, n_tok)
    hit = lax.broadcasted_iota(I32, (n_tok, ROWS), 0) == residue
    mine[0:16] = vector[...].astype(BF).astype(F32)
    by_z[0] = jnp.broadcast_to(lane_sum(jnp.where(hit, 1.0, 0.0)), (n_tok, 128))

    def z_copy(d):
        return remote(by_z.at[0], by_z.at[d], z_s.at[d], z_r.at[d], me, (z + d) % n_rep)

    def t_copy(d):
        return remote(mine, by_tok.at[d], t_s.at[d], t_r.at[d], (me + d) % n_tok, z)

    for d in range(1, n_rep):
        z_copy(d).start()
    for d in range(1, n_rep):
        z_copy(d).wait()
    mine[16:24] = by_z[0] + by_z[1] + by_z[2] + by_z[3]
    for d in range(1, n_tok):
        t_copy(d).start()

    def x_here(s):
        to_x_in(s).wait_recv()
        on_y(s).start()
        to_twin(1, s).start()

    def to_x_in(s):
        return remote(own.at[s], slot(at.xn, s), x_s.at[s], x_r.at[s], at.xn, z)

    def y_in(s):
        return remote(own.at[s], slot(at.yn, s), y_s.at[s], y_r.at[s], at.yn, z)

    def d_in(s):
        return remote(own.at[s], slot(at.dn, s), d_s.at[s], d_r.at[s], at.yn, z)

    def first(j):
        x_here(near(j))
        x_on_z(near(j)).start()
        to_y(3 + j).start()

    loop(half, first)
    x_here(half)
    for s in range(3 + half, count):
        to_y(s).start()

    def y_here(s):
        y_in(s).wait_recv()
        to_twin(2, s).start()

    def second(j):
        x_on_z(far(j)).wait_recv()
        to_twin(1, far(j)).start()
        y_here(j)
        d_in(near(j)).wait_recv()
        d_on_z(near(j)).start()
        to_twin(3, near(j)).start()

    loop(half, second)
    d_in(half).wait_recv()
    to_twin(3, half).start()
    loop(count - half, lambda j: y_here(half + j))

    def third(j):
        d_on_z(far(j)).wait_recv()
        to_twin(3, far(j)).start()

    loop(half, third)

    small[0] = mine[...]
    for d in range(1, n_tok):
        t_copy(d).wait()
        small[d] = by_tok[d]
    for i in range(3):
        row_keep(i).wait()
        for k in (2, 3, 1):
            row_copy(i, k).wait()
    keep.wait()

    def sent_half(j):
        to_x(near(j)).wait_send()
        on_y(near(j)).wait_send()
        x_on_z(near(j)).wait_send()
        d_on_z(near(j)).wait_send()

    loop(half, sent_half)
    to_x(half).wait_send()
    on_y(half).wait_send()

    def sent(s):
        to_y(s).wait_send()
        for q in range(4):
            to_twin(q, s).wait()

    loop(count, sent)


def gather_all(cap, tokens, cotangent, order, master, vector):
    count = master.shape[0]
    block = jax.ShapeDtypeStruct((SD, cap, D), BF)
    meta_shape = jax.ShapeDtypeStruct((SD, META, D), BF)
    dma = pltpu.SemaphoreType.DMA
    slots, recv_x, recv_c, recv_meta, small = pl.pallas_call(
        functools.partial(gather_kernel, cap, count),
        out_shape=(
            jax.ShapeDtypeStruct((8 * count, BLK, D), BF),
            block,
            block,
            meta_shape,
            jax.ShapeDtypeStruct((8, 24, 128), F32),
        ),
        in_specs=[VMEM] * 5,
        out_specs=(ANY, ANY, ANY, ANY, VMEM),
        scratch_shapes=[
            pltpu.VMEM((count, BLK, D), BF),
            pltpu.VMEM((SD, cap, D), BF),
            pltpu.VMEM((SD, cap, D), BF),
            pltpu.VMEM((SD, META, D), BF),
            pltpu.VMEM((24, 128), F32),
            pltpu.VMEM((4, 8, 128), F32),
            pltpu.VMEM((8, 24, 128), F32),
        ]
        + [dma((count,))] * 10
        + [dma((4, count))] * 2
        + [dma((3, SD))] * 2
        + [dma((4,))] * 2
        + [dma((8,))] * 2
        + [dma((4,))],
        compiler_params=pltpu.CompilerParams(
            collective_id=0, has_side_effects=True, vmem_limit_bytes=40 << 20
        ),
        name="gather",
    )(tokens, cotangent, order, master, jnp.pad(vector.reshape(9, 128), ((0, 7), (0, 0))))
    me = lax.axis_index("tok")
    from_tok = (me - jnp.arange(8, dtype=I32)) % 8
    by_owner = jnp.take(small, from_tok, axis=0)
    vectors = by_owner[:, 0:9].reshape(-1)
    occupancy = by_owner[:, 16:24, 0].astype(I32)
    return slots, recv_x, recv_c, recv_meta, vectors, occupancy


def return_kernel(cap, order, back, back_meta, out, entropy):
    seat = lax.rem(lax.axis_index("tok"), SD)
    slots, _ = route_slots(order[...], seat, cap)
    picked = jnp.concatenate([slot_matrix(slots, at, cap) for at in range(SD)], axis=0)
    rows = back[...].reshape(SD * cap, D)
    out[...] = mm(picked, rows, TN).astype(BF)
    if entropy is not None:
        line = jnp.concatenate([back_meta[at, 0:8, 0:cap] for at in range(SD)], axis=1)
        entropy[...] = mm(line, picked).astype(BF)


def swap_blocks(blocks):
    n = lax.axis_size("tok")
    parts = [blocks[0]]
    for k in range(1, SD):
        parts.append(lax.ppermute(blocks[k], "tok", [(i, i ^ k) for i in range(n)]))
    return jnp.stack(parts)


V_BQ, V_BV, V_BO, V_BD, V_G1, V_C1, V_G2, V_C2 = range(8)


def erf_parts(v):
    z = jnp.abs(v) * (1.0 / math.sqrt(2.0))
    t = 1.0 / (1.0 + 0.3275911 * z)
    e = jnp.exp(-z * z)
    poly = 0.5 * 1.061405429
    for c in (-1.453152027, 1.421413741, -0.284496736, 0.254829592):
        poly = poly * t + 0.5 * c
    tail = poly * t * e
    return jnp.where(v >= 0.0, 1.0 - tail, tail), e


def lane_sum(x):
    return jnp.sum(x, axis=1, keepdims=True)


def layer_kernel(
    cap,
    pos,
    slots,
    vecs,
    b_u,
    recv_x,
    recv_c,
    meta,
    ret_out,
    ret_meta,
    ret_ing,
    grads,
    gvec,
    g_bu,
    w,
    place,
    xbuf,
    x_c,
    heads,
    act,
    d_up,
    d_q,
    d_k,
    d_v,
    d_proj,
    hid,
    d_br,
    out_c,
    ing_c,
    ent,
    q_t,
    k_t,
    v_t,
    p_t,
    gp_t,
    dh_t,
    n1_t,
    hid_t,
    stage,
    w_sem,
    x_sem,
    g_sem,
):
    inv = 1.0 / math.sqrt(HD)

    def w_copy(b):
        return pltpu.make_async_copy(slots.at[pos[b]], w.at[pl.ds(b * BLK, BLK)], w_sem)

    def start_w(b, c):
        w_copy(b).start()
        return c

    def wait_w(b, c):
        w_copy(b).wait()
        return c

    cx = pltpu.make_async_copy(recv_x, xbuf, x_sem)
    cx.start()
    lax.fori_loop(0, NBLK, start_w, 0)
    gvec[...] = jnp.zeros_like(gvec)
    g_bu[...] = jnp.zeros_like(g_bu)

    for k in range(SD):
        hi = meta[k, 0:8, 0:cap].astype(F32)[0:1]
        lo = meta[k, 0:8, cap : 2 * cap].astype(F32)[0:1]
        at = (hi * CL + lo).astype(I32)
        rows = lax.broadcasted_iota(I32, (ROWS, cap), 0) + 1
        place[:, k * cap : (k + 1) * cap] = jnp.where(rows == at, 1.0, 0.0).astype(BF)
    def seat_rows(to):
        def body(t, c):
            rows = pl.ds(pl.multiple_of(t * TM, TM), TM)
            to[rows, :] = mm(place[rows, :], xbuf[...].reshape(SD * cap, D)).astype(BF)
            return c

        lax.fori_loop(0, ROWS // TM, body, 0)

    cx.wait()
    seat_rows(x_c)
    cc = pltpu.make_async_copy(recv_c, xbuf, x_sem)
    cc.start()
    cc.wait()
    seat_rows(d_br)
    lax.fori_loop(0, NBLK, wait_w, 0)

    wq, wk, wv, wo = (w.at[pl.ds(i * D, D)] for i in range(4))
    wu = w.at[pl.ds(4 * D, FF)]
    wd = w.at[pl.ds(4 * D + FF, FF)]

    lane = lax.broadcasted_iota(I32, (1, PW), 1)
    m0 = jnp.where(lane < HD, 1.0, 0.0).astype(BF)
    m1 = jnp.where(lane < HD, 0.0, 1.0).astype(BF)
    first_half = lax.broadcasted_iota(I32, (CL, PW), 1) < HD
    eye = lax.broadcasted_iota(I32, (CL, CL), 0) == lax.broadcasted_iota(I32, (CL, CL), 1)

    def vec(i):
        return vecs[i : i + 1, :]

    def add_vec(i, value):
        gvec[i : i + 1, :] += jnp.sum(value, axis=0, keepdims=True)

    def tile(t, carry):
        r0 = pl.multiple_of(t * TM, TM)
        rows = pl.ds(r0, TM)
        x = x_c[rows, :]
        q_t[...] = ((mm(x, wq[...]) + vec(V_BQ)).astype(BF).astype(F32) * inv).astype(BF)
        k_t[...] = mm(x, wk[...]).astype(BF)
        v_t[...] = (mm(x, wv[...]) + vec(V_BV)).astype(BF)

        def attend(c, z):
            cr = pl.ds(pl.multiple_of(c * CL, CL), CL)
            total = jnp.zeros((CL, 1), F32)
            for p in range(PAIRS):
                ps = slice(p * PW, (p + 1) * PW)
                kp, vp = k_t[cr, ps], v_t[cr, ps]
                s = mm(q_t[cr, ps], jnp.concatenate([kp * m0, kp * m1], axis=0), NT)
                halves = []
                for h in range(2):
                    sh = s[:, h * CL : (h + 1) * CL]
                    sh = sh - jnp.max(sh, axis=1, keepdims=True)
                    e = jnp.exp(sh)
                    tot = lane_sum(e)
                    r = 1.0 / tot
                    total += jnp.log(tot) - lane_sum(e * sh) * r
                    halves.append((e * r).astype(BF))
                weights = jnp.concatenate(halves, axis=1)
                p_t[c, p] = weights
                o = mm(weights, jnp.concatenate([vp * m0, vp * m1], axis=0))
                heads[pl.ds(pl.multiple_of(r0 + c * CL, CL), CL), ps] = o.astype(BF)
            line = jnp.sum(jnp.where(eye, total * (1.0 / HEADS), 0.0), axis=0, keepdims=True)
            ent[:, pl.ds(pl.multiple_of(r0 + c * CL, CL), CL)] = jnp.broadcast_to(line, (8, CL))
            return z

        lax.fori_loop(0, TM // CL, attend, 0)

        r1 = x.astype(F32) + mm(heads[rows, :], wo[...]) + vec(V_BO)
        c1 = r1 - lane_sum(r1) * (1.0 / D)
        rs1 = lax.rsqrt(lane_sum(c1 * c1) * (1.0 / D) + norm_epsilon)
        n1 = c1 * rs1
        hidden = n1 * vec(V_G1) + vec(V_C1)
        hid[rows, :] = hidden.astype(BF)
        n1_t[...] = n1
        hid_t[...] = hidden

        def widen(f, z):
            fs = pl.ds(pl.multiple_of(f * FC, FC), FC)
            up = mm(hid[rows, :], wu[fs, :], NT) + b_u[:, fs]
            phi, e = erf_parts(up)
            act[rows, fs] = (up * phi).astype(BF)
            gp_t[:, fs] = (phi + up * (e * (1.0 / math.sqrt(2.0 * math.pi)))).astype(BF)
            return z

        lax.fori_loop(0, FF // FC, widen, 0)
        r2 = hid_t[...] + mm(act[rows, :], wd[...]) + vec(V_BD)
        c2 = r2 - lane_sum(r2) * (1.0 / D)
        rs2 = lax.rsqrt(lane_sum(c2 * c2) * (1.0 / D) + norm_epsilon)
        n2 = c2 * rs2
        out_c[rows, :] = (n2 * vec(V_G2) + vec(V_C2)).astype(BF)

        e2 = d_br[rows, :].astype(F32)
        add_vec(V_G2, e2 * n2)
        add_vec(V_C2, e2)
        eg = e2 * vec(V_G2)
        d_r2 = rs2 * (eg - lane_sum(eg) * (1.0 / D) - n2 * (lane_sum(eg * n2) * (1.0 / D)))
        d_br[rows, :] = d_r2.astype(BF)
        add_vec(V_BD, d_br[rows, :].astype(F32))
        hid_t[...] = d_r2

        def widen_back(f, z):
            fs = pl.ds(pl.multiple_of(f * FC, FC), FC)
            du = (mm(d_br[rows, :], wd[fs, :], NT) * gp_t[:, fs].astype(F32)).astype(BF)
            d_up[rows, fs] = du
            g_bu[:, fs] += jnp.sum(du.astype(F32), axis=0, keepdims=True)
            return z

        lax.fori_loop(0, FF // FC, widen_back, 0)
        n1 = n1_t[...]
        d_h = hid_t[...] + mm(d_up[rows, :], wu[...])
        add_vec(V_G1, d_h * n1)
        add_vec(V_C1, d_h)
        eg = d_h * vec(V_G1)
        d_r1 = rs1 * (eg - lane_sum(eg) * (1.0 / D) - n1 * (lane_sum(eg * n1) * (1.0 / D)))
        d_proj[rows, :] = d_r1.astype(BF)
        hid_t[...] = d_r1
        add_vec(V_BO, d_proj[rows, :].astype(F32))
        dh_t[...] = mm(d_proj[rows, :], wo[...], NT).astype(BF)

        def attend_back(c, z):
            cr = pl.ds(pl.multiple_of(c * CL, CL), CL)
            gr = pl.ds(pl.multiple_of(r0 + c * CL, CL), CL)
            for p in range(PAIRS):
                ps = slice(p * PW, (p + 1) * PW)
                qp, kp, vp, dh = q_t[cr, ps], k_t[cr, ps], v_t[cr, ps], dh_t[cr, ps]
                weights = p_t[c, p]
                d_w = mm(dh, jnp.concatenate([vp * m0, vp * m1], axis=0), NT)
                halves = []
                for h in range(2):
                    wh = weights[:, h * CL : (h + 1) * CL].astype(F32)
                    dwh = d_w[:, h * CL : (h + 1) * CL]
                    halves.append((wh * (dwh - lane_sum(dwh * wh))).astype(BF))
                d_s = jnp.concatenate(halves, axis=1)
                d_q[gr, ps] = (mm(d_s, jnp.concatenate([kp * m0, kp * m1], axis=0)) * inv).astype(BF)
                dk = mm(d_s, qp, TN)
                d_k[gr, ps] = jnp.where(first_half, dk[0:CL], dk[CL:]).astype(BF)
                dv = mm(weights, dh, TN)
                d_v[gr, ps] = jnp.where(first_half, dv[0:CL], dv[CL:]).astype(BF)
            return z

        lax.fori_loop(0, TM // CL, attend_back, 0)
        dq, dk, dv = d_q[rows, :], d_k[rows, :], d_v[rows, :]
        add_vec(V_BQ, dq.astype(F32))
        add_vec(V_BV, dv.astype(F32))
        d_x = mm(dq, wq[...], NT) + mm(dk, wk[...], NT) + mm(dv, wv[...], NT)
        ing_c[rows, :] = (hid_t[...] + d_x.astype(BF).astype(F32)).astype(BF)
        return carry

    lax.fori_loop(0, ROWS // TM, tile, 0)

    def back_rows(source, to):
        for k in range(SD):
            xbuf[k] = mm(place[:, k * cap : (k + 1) * cap], source[...], TN).astype(BF)
        return pltpu.make_async_copy(xbuf, to, x_sem)

    for k in range(SD):
        line = mm(ent[...].astype(BF), place[:, k * cap : (k + 1) * cap])
        ret_meta[k] = jnp.concatenate([line, line], axis=1)[0:1].astype(BF) * jnp.ones((META, 1), BF)
    back_out = back_rows(out_c, ret_out)
    back_out.start()

    WC = 4 * BLK

    def g_copy(chunk, j, at):
        return pltpu.make_async_copy(
            stage.at[at, pl.ds(j * BLK, BLK)], grads.at[pos[chunk * 4 + j]], g_sem.at[at]
        )

    def put(chunk, left, right):
        at = lax.rem(chunk, 2)

        @pl.when(chunk >= 2)
        def _():
            for j in range(4):
                g_copy(chunk - 2, j, at).wait()

        stage[at] = mm(left, right, TN).astype(BF)
        for j in range(4):
            g_copy(chunk, j, at).start()

    def wide(left, right, first):
        def body(j, c):
            put(first + j, left[:, pl.ds(pl.multiple_of(j * WC, WC), WC)], right[...])
            return c

        lax.fori_loop(0, left.shape[1] // WC, body, 0)

    first = 0
    for left, right in ((x_c, d_q), (x_c, d_k), (x_c, d_v), (heads, d_proj), (d_up, hid), (act, d_br)):
        wide(left, right, first)
        first += left.shape[1] // WC
    back_out.wait()
    back_ing = back_rows(ing_c, ret_ing)
    back_ing.start()
    back_ing.wait()
    last = WROWS // WC
    last = WROWS // WC
    for ch in (last - 2, last - 1):
        for j in range(4):
            g_copy(ch, j, ch % 2).wait()


def local(
    tokens,
    cotangent,
    cluster_order,
    block_owner,
    master_slots,
    moment_one,
    moment_two,
    vector_master,
    vector_moment_one,
    vector_moment_two,
):
    tok_count = lax.axis_size("tok")
    tok_index = lax.axis_index("tok")
    slot_count = master_slots.shape[0]
    cap = tok_count // SD * (max(1, CPS // tok_count) * 3 * CL // (2 * SD))
    total_slots = tok_count * slot_count
    positions = slot_positions(block_owner, slot_count)
    order = cluster_order.reshape(1, ROWS)

    block = jax.ShapeDtypeStruct((SD, cap, D), BF)
    meta_shape = jax.ShapeDtypeStruct((SD, META, D), BF)
    four_planes = tok_count == 8 and lax.axis_size("rep") == 4
    if four_planes:
        slots_low, recv_x, recv_c, recv_meta, vectors, occupancy = gather_all(
            cap, tokens, cotangent, order, master_slots, vector_master
        )
    else:
        slots_low = lax.all_gather(master_slots.astype(BF), "tok", axis=0, tiled=True)
        vectors = lax.all_gather(vector_master.astype(BF), "tok", axis=0, tiled=True).astype(F32)
        cluster = tok_index // SD * CPS + cluster_order // CL
        target = cluster % tok_count
        chosen = target[None, :] == jnp.arange(tok_count, dtype=jnp.int32)[:, None]
        sent_counts = jnp.sum(chosen.astype(F32), axis=1)
        own_row = (jnp.arange(tok_count, dtype=jnp.int32) == tok_index).astype(F32)
        occupancy = lax.psum(own_row[:, None] * sent_counts[None, :], ("tok", "rep")).astype(jnp.int32)
        send_x, send_c, meta = pl.pallas_call(
            functools.partial(send_kernel, cap),
            out_shape=(block, block, meta_shape),
            in_specs=[VMEM] * 3,
            out_specs=(VMEM,) * 3,
            compiler_params=pltpu.CompilerParams(vmem_limit_bytes=40 << 20),
            name="send_rows",
        )(tokens, cotangent, order)
        recv_x, recv_c, recv_meta = swap_blocks(send_x), swap_blocks(send_c), swap_blocks(meta)

    ret_out, ret_meta, ret_ing, grads, gvec, g_bu = pl.pallas_call(
        functools.partial(layer_kernel, cap),
        out_shape=(
            block,
            meta_shape,
            block,
            jax.ShapeDtypeStruct((total_slots, BLK, D), BF),
            jax.ShapeDtypeStruct((8, D), F32),
            jax.ShapeDtypeStruct((1, FF), F32),
        ),
        in_specs=[SMEM, ANY, VMEM, VMEM, ANY, ANY, VMEM],
        out_specs=(ANY, VMEM, ANY, ANY, VMEM, VMEM),
        scratch_shapes=[
            pltpu.VMEM((WROWS, D), BF),
            pltpu.VMEM((ROWS, SD * cap), BF),
            pltpu.VMEM((SD, cap, D), BF),
            pltpu.VMEM((ROWS, D), BF),
            pltpu.VMEM((ROWS, D), BF),
            pltpu.VMEM((ROWS, FF), BF),
            pltpu.VMEM((ROWS, FF), BF),
            pltpu.VMEM((ROWS, D), BF),
            pltpu.VMEM((ROWS, D), BF),
            pltpu.VMEM((ROWS, D), BF),
            pltpu.VMEM((ROWS, D), BF),
            pltpu.VMEM((ROWS, D), BF),
            pltpu.VMEM((ROWS, D), BF),
            pltpu.VMEM((ROWS, D), BF),
            pltpu.VMEM((ROWS, D), BF),
            pltpu.VMEM((8, ROWS), F32),
            pltpu.VMEM((TM, D), BF),
            pltpu.VMEM((TM, D), BF),
            pltpu.VMEM((TM, D), BF),
            pltpu.VMEM((TM // CL, PAIRS, CL, 2 * CL), BF),
            pltpu.VMEM((TM, FF), BF),
            pltpu.VMEM((TM, D), BF),
            pltpu.VMEM((TM, D), F32),
            pltpu.VMEM((TM, D), F32),
            pltpu.VMEM((2, 4 * BLK, D), BF),
            pltpu.SemaphoreType.DMA,
            pltpu.SemaphoreType.DMA,
            pltpu.SemaphoreType.DMA((2,)),
        ],
        compiler_params=pltpu.CompilerParams(vmem_limit_bytes=63 << 20),
        name="layer",
    )(positions, slots_low, vectors[: 8 * D].reshape(8, D), vectors[8 * D :].reshape(1, FF), recv_x, recv_c, recv_meta)

    back_out, back_meta, back_ing = swap_blocks(ret_out), swap_blocks(ret_meta), swap_blocks(ret_ing)
    row_block = jax.ShapeDtypeStruct((ROWS, D), BF)
    output, entropy = pl.pallas_call(
        functools.partial(return_kernel, cap),
        out_shape=(row_block, jax.ShapeDtypeStruct((8, ROWS), BF)),
        in_specs=[VMEM] * 3,
        out_specs=(VMEM,) * 2,
        compiler_params=pltpu.CompilerParams(vmem_limit_bytes=40 << 20),
        name="return_output",
    )(order, back_out, back_meta)
    input_grad = pl.pallas_call(
        lambda o, b, r: return_kernel(cap, o, b, None, r, None),
        out_shape=row_block,
        in_specs=[VMEM] * 2,
        out_specs=VMEM,
        compiler_params=pltpu.CompilerParams(vmem_limit_bytes=40 << 20),
        name="return_grad",
    )(order, back_ing)

    used = jnp.any(
        positions[None, :] == (tok_index * slot_count + jnp.arange(slot_count, dtype=I32))[:, None], axis=1
    )
    owned_grad = lax.psum_scatter(grads, "tok", scatter_dimension=0, tiled=True)
    owned_grad = lax.psum(owned_grad, "rep").astype(F32)
    owned_grad = jnp.where(used[:, None, None], owned_grad, 0.0)
    grad_vector = jnp.concatenate([gvec.reshape(-1), g_bu.reshape(-1)])
    vec_owned = lax.psum_scatter(grad_vector, "tok", scatter_dimension=0, tiled=True)
    vec_owned = lax.psum(vec_owned, "rep")
    first_new, second_new, master_new = adam_update(
        owned_grad, master_slots, moment_one, moment_two, rate_matrix
    )
    vec_first, vec_second, vec_new = adam_update(
        vec_owned, vector_master, vector_moment_one, vector_moment_two, rate_vector
    )
    return (
        output,
        input_grad,
        owned_grad,
        first_new,
        second_new,
        master_new,
        master_new.astype(BF),
        vec_owned,
        vec_first,
        vec_second,
        vec_new,
        vec_new.astype(BF),
        entropy[0],
        occupancy,
    )


def solution(mesh):
    placed = (
        P(("rep", "tok"), None),
        P(("rep", "tok"), None),
        P(("rep", "tok")),
        P(),
        P("tok", None, None),
        P("tok", None, None),
        P("tok", None, None),
        P("tok"),
        P("tok"),
        P("tok"),
    )
    return jax.shard_map(
        local,
        mesh=mesh,
        in_specs=placed,
        out_specs=(
            P(("rep", "tok"), None),
            P(("rep", "tok"), None),
            P("tok", None, None),
            P("tok", None, None),
            P("tok", None, None),
            P("tok", None, None),
            P("tok", None, None),
            P("tok"),
            P("tok"),
            P("tok"),
            P("tok"),
            P("tok"),
            P(("rep", "tok")),
            P(),
        ),
        check_vma=False,
    )
```

```python
import functools
import math

import jax
import jax.numpy as jnp
from jax import lax
from jax.experimental import pallas as pl
from jax.experimental.pallas import tpu as pltpu
from jax.sharding import PartitionSpec as P

D = 768
HEADS = 12
HD = 64
FF = 3072
SD = 4
CL = 128
NBLK = 96
STEP = 10
CPS = 32
WROWS = 9216
BLK = 96
ROWS = 1024
PAIRS = HEADS // 2
PW = 2 * HD
TM = 256
META = 16
FC = 768

norm_epsilon = 1e-06
beta_first = 0.9
beta_second = 0.999
adam_epsilon = 1e-08
weight_decay = 0.01
rate_matrix = 0.02
rate_vector = 0.2

BF = jnp.bfloat16
F32 = jnp.float32
I32 = jnp.int32

VMEM = pl.BlockSpec(memory_space=pltpu.VMEM)
SMEM = pl.BlockSpec(memory_space=pltpu.SMEM)
ANY = pl.BlockSpec(memory_space=pl.ANY)

NN = (((1,), (0,)), ((), ()))
NT = (((1,), (1,)), ((), ()))
TN = (((0,), (0,)), ((), ()))


def mm(a, b, dims=NN):
    return lax.dot_general(a, b, dims, preferred_element_type=F32)


def slot_positions(block_owner, slot_count):
    owners = block_owner[:, 0]
    blocks = owners.shape[0]
    shared = owners[:, None] == owners[None, :]
    before = (
        jnp.arange(blocks, dtype=jnp.int32)[None, :] < jnp.arange(blocks, dtype=jnp.int32)[:, None]
    )
    earlier = jnp.sum((shared & before).astype(jnp.int32), axis=1)
    return owners * slot_count + earlier


def adam_update(grad_now, weight_old, first_old, second_old, rate_step):
    first_new = beta_first * first_old + (1.0 - beta_first) * grad_now
    second_new = beta_second * second_old + (1.0 - beta_second) * grad_now * grad_now
    first_hat = first_new / (1.0 - beta_first**STEP)
    second_hat = second_new / (1.0 - beta_second**STEP)
    weight_new = weight_old - rate_step * (
        first_hat / (jnp.sqrt(second_hat) + adam_epsilon) + weight_decay * weight_old
    )
    return (first_new, second_new, weight_new)


def route_slots(order, seat, cap):
    cluster = order // CL
    rel = lax.rem(cluster, SD) ^ seat
    place = (cluster // SD) * CL + lax.rem(order, CL) + 1
    chosen = lax.broadcasted_iota(I32, (8, ROWS), 0) == rel
    chosen_low = jnp.where(chosen, 1.0, 0.0).astype(BF)
    before = lax.broadcasted_iota(I32, (ROWS, ROWS), 0) < lax.broadcasted_iota(I32, (ROWS, ROWS), 1)
    before_low = jnp.where(before, 1.0, 0.0).astype(BF)
    running = mm(chosen_low, before_low)
    rank = jnp.sum(jnp.where(chosen, running, 0.0), axis=0, keepdims=True).astype(I32)
    return rel * cap + rank, place


def slot_matrix(slots, at, cap):
    rows = lax.broadcasted_iota(I32, (cap, ROWS), 0) + at * cap
    return jnp.where(rows == slots, 1.0, 0.0).astype(BF)


def send_kernel(cap, tokens, cotangent, order, send_x, send_c, meta):
    seat = lax.rem(lax.axis_index("tok"), SD)
    slots, place = route_slots(order[...], seat, cap)
    digits = jnp.concatenate([place // CL, lax.rem(place, CL)] + [place * 0] * 6, axis=0).astype(F32).astype(BF)
    for at in range(SD):
        picked = slot_matrix(slots, at, cap)
        send_x[at] = mm(picked, tokens[...]).astype(BF)
        send_c[at] = mm(picked, cotangent[...]).astype(BF)
        coded = mm(digits, picked, NT)
        line = jnp.concatenate([coded[0:1], coded[1:2]], axis=1)
        meta[at] = jnp.broadcast_to(line, (META, D)).astype(BF)


def remote(src, dst, send_sem, recv_sem, tok, rep):
    return pltpu.make_async_remote_copy(
        src_ref=src,
        dst_ref=dst,
        send_sem=send_sem,
        recv_sem=recv_sem,
        device_id={"tok": tok, "rep": rep},
        device_id_type=pl.DeviceIdType.MESH,
    )


def loop(n, body):
    def run(i, c):
        body(i)
        return c

    lax.fori_loop(0, n, run, 0)


class Place:
    def __init__(self):
        self.me = me = lax.axis_index("tok")
        self.z = z = lax.axis_index("rep")
        core, x, y = me % 2, (me // 2) % 2, me // 4
        self.twin = me + 1 - 2 * core
        self.xn = me + 2 - 4 * x
        self.yn = me + 4 - 8 * y
        self.dn = self.xn + 4 - 8 * y
        self.side = z % 2
        self.zp = z + 1 - 2 * self.side

    def twin_of(self, tok):
        return tok + 1 - 2 * (tok % 2)

    def greet(self, peers):
        barrier = pltpu.get_barrier_semaphore()
        for tok, rep in peers:
            pl.semaphore_signal(
                barrier, inc=1, device_id={"tok": tok, "rep": rep}, device_id_type=pl.DeviceIdType.MESH
            )
        return lambda: pl.semaphore_wait(barrier, len(peers))


def gather_kernel(
    cap,
    count,
    tokens,
    cotangent,
    order,
    master,
    vector,
    slots,
    recv_x,
    recv_c,
    recv_meta,
    small,
    own,
    send_x,
    send_c,
    meta,
    mine,
    by_z,
    by_tok,
    x_s,
    x_r,
    y_s,
    y_r,
    d_s,
    d_r,
    zx_s,
    zx_r,
    zd_s,
    zd_r,
    p_s,
    p_r,
    row_s,
    row_r,
    z_s,
    z_r,
    t_s,
    t_r,
    local_s,
):
    at = Place()
    me, z, side = at.me, at.z, at.side
    n_tok, n_rep = 8, 4
    peers = [((me + d) % n_tok, z) for d in range(1, n_tok)] + [(me, (z + d) % n_rep) for d in range(1, n_rep)]
    wait_peers = at.greet(peers)
    for s in range(count):
        own[s] = master[s].astype(BF)
    wait_peers()

    half = count // 2

    def slot(owner, s):
        return slots.at[owner * count + s]

    def to_x(s):
        return remote(own.at[s], slot(me, s), x_s.at[s], x_r.at[s], at.xn, z)

    def to_y(s):
        return remote(own.at[s], slot(me, s), y_s.at[s], y_r.at[s], at.yn, z)

    def on_y(s):
        return remote(slot(at.xn, s), slot(at.xn, s), d_s.at[s], d_r.at[s], at.yn, z)

    def x_on_z(s):
        return remote(slot(at.xn, s), slot(at.xn, s), zx_s.at[s], zx_r.at[s], me, at.zp)

    def d_on_z(s):
        return remote(slot(at.dn, s), slot(at.dn, s), zd_s.at[s], zd_r.at[s], me, at.zp)

    owners = (me, at.xn, at.yn, at.dn)

    def to_twin(q, s):
        src = own.at[s] if q == 0 else slot(owners[q], s)
        return remote(src, slot(owners[q], s), p_s.at[q, s], p_r.at[q, s], at.twin, z)

    def near(j):
        return (half + 1) * side + j

    def far(j):
        return (half + 1) * (1 - side) + j

    loop(half, lambda j: to_x(near(j)).start())
    to_x(half).start()
    for s in range(3):
        to_y(s).start()
    loop(count, lambda s: to_twin(0, s).start())
    keep = pltpu.make_async_copy(own, slots.at[pl.ds(me * count, count)], local_s.at[0])
    keep.start()

    seat = me % SD
    slot_of, place = route_slots(order[...], seat, cap)
    digits = jnp.concatenate([place // CL, lax.rem(place, CL)] + [place * 0] * 6, axis=0).astype(F32).astype(BF)
    for k in range(SD):
        picked = slot_matrix(slot_of, k, cap)
        send_x[k] = mm(picked, tokens[...]).astype(BF)
        send_c[k] = mm(picked, cotangent[...]).astype(BF)
        coded = mm(digits, picked, NT)
        line = jnp.concatenate([coded[0:1], coded[1:2]], axis=1)
        meta[k] = jnp.broadcast_to(line, (META, D)).astype(BF)
    seats = (me, at.twin, at.xn, at.twin_of(at.xn))
    rows_of = ((meta, recv_meta), (send_x, recv_x), (send_c, recv_c))

    def row_copy(i, k):
        src, dst = rows_of[i]
        return remote(src.at[k], dst.at[k], row_s.at[i, k], row_r.at[i, k], seats[k], z)

    def row_keep(i):
        src, dst = rows_of[i]
        return pltpu.make_async_copy(src.at[0], dst.at[0], local_s.at[1 + i])

    for i in range(3):
        row_keep(i).start()
        for k in (2, 3, 1):
            row_copy(i, k).start()

    residue = lax.rem(me // SD * CPS + order[...] // CL, n_tok)
    hit = lax.broadcasted_iota(I32, (n_tok, ROWS), 0) == residue
    mine[0:16] = vector[...].astype(BF).astype(F32)
    by_z[0] = jnp.broadcast_to(lane_sum(jnp.where(hit, 1.0, 0.0)), (n_tok, 128))

    def z_copy(d):
        return remote(by_z.at[0], by_z.at[d], z_s.at[d], z_r.at[d], me, (z + d) % n_rep)

    def t_copy(d):
        return remote(mine, by_tok.at[d], t_s.at[d], t_r.at[d], (me + d) % n_tok, z)

    for d in range(1, n_rep):
        z_copy(d).start()
    for d in range(1, n_rep):
        z_copy(d).wait()
    mine[16:24] = by_z[0] + by_z[1] + by_z[2] + by_z[3]
    for d in range(1, n_tok):
        t_copy(d).start()

    def x_here(s):
        to_x_in(s).wait_recv()
        on_y(s).start()
        to_twin(1, s).start()

    def to_x_in(s):
        return remote(own.at[s], slot(at.xn, s), x_s.at[s], x_r.at[s], at.xn, z)

    def y_in(s):
        return remote(own.at[s], slot(at.yn, s), y_s.at[s], y_r.at[s], at.yn, z)

    def d_in(s):
        return remote(own.at[s], slot(at.dn, s), d_s.at[s], d_r.at[s], at.yn, z)

    def first(j):
        x_here(near(j))
        x_on_z(near(j)).start()
        to_y(3 + j).start()

    loop(half, first)
    x_here(half)
    for s in range(3 + half, count):
        to_y(s).start()

    def y_here(s):
        y_in(s).wait_recv()
        to_twin(2, s).start()

    def second(j):
        x_on_z(far(j)).wait_recv()
        to_twin(1, far(j)).start()
        y_here(j)
        d_in(near(j)).wait_recv()
        d_on_z(near(j)).start()
        to_twin(3, near(j)).start()

    loop(half, second)
    d_in(half).wait_recv()
    to_twin(3, half).start()
    loop(count - half, lambda j: y_here(half + j))

    def third(j):
        d_on_z(far(j)).wait_recv()
        to_twin(3, far(j)).start()

    loop(half, third)

    small[0] = mine[...]
    for d in range(1, n_tok):
        t_copy(d).wait()
        small[d] = by_tok[d]
    for i in range(3):
        row_keep(i).wait()
        for k in (2, 3, 1):
            row_copy(i, k).wait()
    keep.wait()

    def sent_half(j):
        to_x(near(j)).wait_send()
        on_y(near(j)).wait_send()
        x_on_z(near(j)).wait_send()
        d_on_z(near(j)).wait_send()

    loop(half, sent_half)
    to_x(half).wait_send()
    on_y(half).wait_send()

    def sent(s):
        to_y(s).wait_send()
        for q in range(4):
            to_twin(q, s).wait()

    loop(count, sent)


def gather_all(cap, tokens, cotangent, order, master, vector):
    count = master.shape[0]
    block = jax.ShapeDtypeStruct((SD, cap, D), BF)
    meta_shape = jax.ShapeDtypeStruct((SD, META, D), BF)
    dma = pltpu.SemaphoreType.DMA
    slots, recv_x, recv_c, recv_meta, small = pl.pallas_call(
        functools.partial(gather_kernel, cap, count),
        out_shape=(
            jax.ShapeDtypeStruct((8 * count, BLK, D), BF),
            block,
            block,
            meta_shape,
            jax.ShapeDtypeStruct((8, 24, 128), F32),
        ),
        in_specs=[VMEM] * 5,
        out_specs=(ANY, ANY, ANY, ANY, VMEM),
        scratch_shapes=[
            pltpu.VMEM((count, BLK, D), BF),
            pltpu.VMEM((SD, cap, D), BF),
            pltpu.VMEM((SD, cap, D), BF),
            pltpu.VMEM((SD, META, D), BF),
            pltpu.VMEM((24, 128), F32),
            pltpu.VMEM((4, 8, 128), F32),
            pltpu.VMEM((8, 24, 128), F32),
        ]
        + [dma((count,))] * 10
        + [dma((4, count))] * 2
        + [dma((3, SD))] * 2
        + [dma((4,))] * 2
        + [dma((8,))] * 2
        + [dma((4,))],
        compiler_params=pltpu.CompilerParams(
            collective_id=0, has_side_effects=True, vmem_limit_bytes=40 << 20
        ),
        name="gather",
    )(tokens, cotangent, order, master, jnp.pad(vector.reshape(9, 128), ((0, 7), (0, 0))))
    me = lax.axis_index("tok")
    from_tok = (me - jnp.arange(8, dtype=I32)) % 8
    by_owner = jnp.take(small, from_tok, axis=0)
    vectors = by_owner[:, 0:9].reshape(-1)
    occupancy = by_owner[:, 16:24, 0].astype(I32)
    return slots, recv_x, recv_c, recv_meta, vectors, occupancy


def return_kernel(cap, with_entropy, order, *refs):
    seat = lax.rem(lax.axis_index("tok"), SD)
    slots, _ = route_slots(order[...], seat, cap)
    picked = jnp.concatenate([slot_matrix(slots, at, cap) for at in range(SD)], axis=0)
    out = refs[2 * SD] if with_entropy else refs[SD]
    rows = jnp.concatenate([refs[at][...] for at in range(SD)], axis=0)
    out[...] = mm(picked, rows, TN).astype(BF)
    if with_entropy:
        line = jnp.concatenate([refs[SD + at][0:8, 0:cap] for at in range(SD)], axis=1)
        refs[2 * SD + 1][...] = mm(line, picked).astype(BF)


def swap_blocks(blocks):
    n = lax.axis_size("tok")
    parts = [blocks[0]]
    for k in range(1, SD):
        parts.append(lax.ppermute(blocks[k], "tok", [(i, i ^ k) for i in range(n)]))
    return parts


def reduce_kernel(
    count,
    split,
    grads,
    vec,
    total,
    vec_out,
    a,
    tw,
    rd,
    rx,
    ry,
    o,
    rz1,
    pz,
    rz2,
    fz,
    vt,
    va,
    vb,
    vc,
    a_l,
    keep_l,
    p_s,
    p_r,
    d_s,
    d_r,
    x_s,
    x_r,
    y_s,
    y_r,
    z1_s,
    z1_r,
    z2_s,
    z2_r,
    z3_s,
    z3_r,
    t_s,
    t_r,
    v_s,
    v_r,
):
    at = Place()
    me, z = at.me, at.z
    n_tok, n_rep = 8, 4
    peers = [((me + d) % n_tok, z) for d in range(1, n_tok)] + [(me, (z + d) % n_rep) for d in range(1, n_rep)]
    wait_peers = at.greet(peers)
    owners = (me, at.xn, at.yn, at.dn)

    def load(q):
        return pltpu.make_async_copy(grads.at[pl.ds(owners[q] * count, count)], a.at[q], a_l.at[q])

    for q in (3, 1, 2, 0):
        load(q).start()
    wait_peers()

    def to_twin(q, s):
        src = grads.at[at.twin_of(owners[q]) * count + s]
        return remote(src, tw.at[q, s], p_s.at[q, s], p_r.at[q, s], at.twin, z)

    def d_y(s):
        return remote(a.at[3, s], rd.at[s], d_s.at[s], d_r.at[s], at.yn, z)

    def d_x(s):
        return remote(a.at[3, s], rd.at[s], d_s.at[s], d_r.at[s], at.xn, z)

    def to_x(s):
        return remote(a.at[1, s], rx.at[s], x_s.at[s], x_r.at[s], at.xn, z)

    def to_y(s):
        return remote(a.at[2, s], ry.at[s], y_s.at[s], y_r.at[s], at.yn, z)

    def z_in(s):
        return remote(o.at[s], rz1.at[s], z1_s.at[s], z1_r.at[s], me, at.zp)

    def z_swap(s):
        return remote(pz.at[s], rz2.at[s], z2_s.at[s], z2_r.at[s], me, n_rep - 1 - z)

    def z_out(s):
        return remote(fz.at[s], fz.at[s], z3_s.at[s], z3_r.at[s], me, at.zp)

    def keep(s):
        return pltpu.make_async_copy(fz.at[s], total.at[s], keep_l.at[s])

    def f32(ref, *index):
        return ref[index].astype(F32)

    loop(count, lambda s: to_twin(3, s).start())

    def others(s):
        for q in (2, 1, 0):
            to_twin(q, s).start()

    loop(count, others)

    def v_tok(d):
        return remote(vec.at[(me + d) % n_tok], vt.at[d], t_s.at[d], t_r.at[d], (me + d) % n_tok, z)

    def v_rep(i, src):
        return remote(src, vb.at[i], v_s.at[i], v_r.at[i], me, at.zp if i == 0 else (z + 2) % n_rep)

    for d in range(1, n_tok):
        v_tok(d).start()

    load(3).wait()

    def join(q, s):
        to_twin(q, s).wait_recv()
        return f32(a, q, s) + f32(tw, q, s)

    def diagonal(s, send):
        a[3, s] = join(3, s).astype(BF)
        send(s).start()

    loop(split, lambda s: diagonal(s, d_y))
    loop(count - split, lambda j: diagonal(split + j, d_x))

    v_sum = vec[me]
    for d in range(1, n_tok):
        v_tok(d).wait()
        v_sum = v_sum + vt[d]
    va[...] = v_sum
    v_rep(0, va).start()

    load(1).wait()
    load(2).wait()

    def plane_y(s):
        a[2, s] = join(2, s).astype(BF)
        to_y(s).start()
        d_y(s).wait_recv()
        a[1, s] = (join(1, s) + f32(rd, s)).astype(BF)
        to_x(s).start()

    def plane_x(s):
        a[1, s] = join(1, s).astype(BF)
        to_x(s).start()
        d_x(s).wait_recv()
        a[2, s] = (join(2, s) + f32(rd, s)).astype(BF)
        to_y(s).start()

    loop(split, plane_y)
    loop(count - split, lambda j: plane_x(split + j))

    v_rep(0, va).wait()
    vc[...] = va[...] + vb[0]
    v_rep(1, vc).start()
    load(0).wait()
    inner = (z == 1) | (z == 2)
    outer = (z == 0) | (z == 3)

    def planes(i):
        @pl.when(i < count)
        def _():
            to_x(i).wait_recv()
            to_y(i).wait_recv()
            o[i] = (join(0, i) + f32(rx, i) + f32(ry, i)).astype(BF)

        @pl.when(outer & (i < count))
        def _():
            z_in(i).start()

        @pl.when(inner & (i >= 1) & (i < count + 1))
        def _():
            s = i - 1
            z_in(s).wait_recv()
            pz[s] = (f32(o, s) + f32(rz1, s)).astype(BF)
            z_swap(s).start()

        @pl.when(inner & (i >= 2) & (i < count + 2))
        def _():
            s = i - 2
            z_swap(s).wait_recv()
            fz[s] = (f32(pz, s) + f32(rz2, s)).astype(BF)
            z_out(s).start()
            keep(s).start()

        @pl.when(outer & (i >= 3))
        def _():
            s = i - 3
            z_out(s).wait_recv()
            keep(s).start()

    loop(count + 3, planes)
    v_rep(1, vc).wait()
    vec_out[...] = vc[...] + vb[1]

    def sent(s):
        for q in range(4):
            to_twin(q, s).wait_send()
        d_y(s).wait_send()
        to_x(s).wait_send()
        to_y(s).wait_send()
        keep(s).wait()

    loop(count, sent)

    @pl.when(outer)
    def _():
        loop(count, lambda s: z_in(s).wait_send())

    @pl.when(inner)
    def _():
        def back(s):
            z_swap(s).wait_send()
            z_out(s).wait_send()

        loop(count, back)


def reduce_all(grads, grad_vector, count):
    dma = pltpu.SemaphoreType.DMA
    part = pltpu.VMEM((count, BLK, D), BF)
    whole = pltpu.VMEM((4, count, BLK, D), BF)
    line = pltpu.VMEM((16, 128), F32)
    shares = jnp.pad(grad_vector.reshape(8, 9, 128), ((0, 0), (0, 7), (0, 0)))
    total, vec = pl.pallas_call(
        functools.partial(reduce_kernel, count, count),
        out_shape=(
            jax.ShapeDtypeStruct((count, BLK, D), BF),
            jax.ShapeDtypeStruct((16, 128), F32),
        ),
        in_specs=[ANY, VMEM],
        out_specs=(ANY, VMEM),
        scratch_shapes=[whole, whole]
        + [part] * 8
        + [pltpu.VMEM((8, 16, 128), F32), line, pltpu.VMEM((2, 16, 128), F32), line]
        + [dma((4,)), dma((count,))]
        + [dma((4, count))] * 2
        + [dma((count,))] * 12
        + [dma((8,))] * 2
        + [dma((2,))] * 2,
        compiler_params=pltpu.CompilerParams(
            collective_id=1, has_side_effects=True, vmem_limit_bytes=48 << 20
        ),
        name="reduce",
    )(grads, shares)
    return total, vec[0:9].reshape(-1)


V_BQ, V_BV, V_BO, V_BD, V_G1, V_C1, V_G2, V_C2 = range(8)


def erf_parts(v):
    z = jnp.abs(v) * (1.0 / math.sqrt(2.0))
    t = 1.0 / (1.0 + 0.3275911 * z)
    e = jnp.exp(-z * z)
    poly = 0.5 * 1.061405429
    for c in (-1.453152027, 1.421413741, -0.284496736, 0.254829592):
        poly = poly * t + 0.5 * c
    tail = poly * t * e
    return jnp.where(v >= 0.0, 1.0 - tail, tail), e


def lane_sum(x):
    return jnp.sum(x, axis=1, keepdims=True)


def layer_kernel(
    cap,
    pos,
    slots,
    vecs,
    b_u,
    recv_x,
    recv_c,
    meta,
    ret_out,
    ret_meta,
    ret_ing,
    grads,
    gvec,
    g_bu,
    w,
    place,
    xbuf,
    x_c,
    heads,
    act,
    d_up,
    d_q,
    d_k,
    d_v,
    d_proj,
    hid,
    d_br,
    out_c,
    ing_c,
    ent,
    q_t,
    k_t,
    v_t,
    p_t,
    gp_t,
    dh_t,
    n1_t,
    hid_t,
    stage,
    w_sem,
    x_sem,
    g_sem,
):
    inv = 1.0 / math.sqrt(HD)

    def w_copy(b):
        return pltpu.make_async_copy(slots.at[pos[b]], w.at[pl.ds(b * BLK, BLK)], w_sem)

    def start_w(b, c):
        w_copy(b).start()
        return c

    def wait_w(b, c):
        w_copy(b).wait()
        return c

    cx = pltpu.make_async_copy(recv_x, xbuf, x_sem)
    cx.start()
    lax.fori_loop(0, NBLK, start_w, 0)
    gvec[...] = jnp.zeros_like(gvec)
    g_bu[...] = jnp.zeros_like(g_bu)

    for k in range(SD):
        hi = meta[k, 0:8, 0:cap].astype(F32)[0:1]
        lo = meta[k, 0:8, cap : 2 * cap].astype(F32)[0:1]
        at = (hi * CL + lo).astype(I32)
        rows = lax.broadcasted_iota(I32, (ROWS, cap), 0) + 1
        place[:, k * cap : (k + 1) * cap] = jnp.where(rows == at, 1.0, 0.0).astype(BF)
    def seat_rows(to):
        def body(t, c):
            rows = pl.ds(pl.multiple_of(t * TM, TM), TM)
            to[rows, :] = mm(place[rows, :], xbuf[...].reshape(SD * cap, D)).astype(BF)
            return c

        lax.fori_loop(0, ROWS // TM, body, 0)

    cx.wait()
    seat_rows(x_c)
    cc = pltpu.make_async_copy(recv_c, xbuf, x_sem)
    cc.start()
    cc.wait()
    seat_rows(d_br)
    lax.fori_loop(0, NBLK, wait_w, 0)

    wq, wk, wv, wo = (w.at[pl.ds(i * D, D)] for i in range(4))
    wu = w.at[pl.ds(4 * D, FF)]
    wd = w.at[pl.ds(4 * D + FF, FF)]

    lane = lax.broadcasted_iota(I32, (1, PW), 1)
    m0 = jnp.where(lane < HD, 1.0, 0.0).astype(BF)
    m1 = jnp.where(lane < HD, 0.0, 1.0).astype(BF)
    first_half = lax.broadcasted_iota(I32, (CL, PW), 1) < HD
    eye = lax.broadcasted_iota(I32, (CL, CL), 0) == lax.broadcasted_iota(I32, (CL, CL), 1)

    def vec(i):
        return vecs[i : i + 1, :]

    def add_vec(i, value):
        gvec[i : i + 1, :] += jnp.sum(value, axis=0, keepdims=True)

    def tile(t, carry):
        r0 = pl.multiple_of(t * TM, TM)
        rows = pl.ds(r0, TM)
        x = x_c[rows, :]
        q_t[...] = ((mm(x, wq[...]) + vec(V_BQ)).astype(BF).astype(F32) * inv).astype(BF)
        k_t[...] = mm(x, wk[...]).astype(BF)
        v_t[...] = (mm(x, wv[...]) + vec(V_BV)).astype(BF)

        def attend(c, z):
            cr = pl.ds(pl.multiple_of(c * CL, CL), CL)
            total = jnp.zeros((CL, 1), F32)
            for p in range(PAIRS):
                ps = slice(p * PW, (p + 1) * PW)
                kp, vp = k_t[cr, ps], v_t[cr, ps]
                s = mm(q_t[cr, ps], jnp.concatenate([kp * m0, kp * m1], axis=0), NT)
                halves = []
                for h in range(2):
                    sh = s[:, h * CL : (h + 1) * CL]
                    sh = sh - jnp.max(sh, axis=1, keepdims=True)
                    e = jnp.exp(sh)
                    tot = lane_sum(e)
                    r = 1.0 / tot
                    total += jnp.log(tot) - lane_sum(e * sh) * r
                    halves.append((e * r).astype(BF))
                weights = jnp.concatenate(halves, axis=1)
                p_t[c, p] = weights
                o = mm(weights, jnp.concatenate([vp * m0, vp * m1], axis=0))
                heads[pl.ds(pl.multiple_of(r0 + c * CL, CL), CL), ps] = o.astype(BF)
            line = jnp.sum(jnp.where(eye, total * (1.0 / HEADS), 0.0), axis=0, keepdims=True)
            ent[:, pl.ds(pl.multiple_of(r0 + c * CL, CL), CL)] = jnp.broadcast_to(line, (8, CL))
            return z

        lax.fori_loop(0, TM // CL, attend, 0)

        r1 = x.astype(F32) + mm(heads[rows, :], wo[...]) + vec(V_BO)
        c1 = r1 - lane_sum(r1) * (1.0 / D)
        rs1 = lax.rsqrt(lane_sum(c1 * c1) * (1.0 / D) + norm_epsilon)
        n1 = c1 * rs1
        hidden = n1 * vec(V_G1) + vec(V_C1)
        hid[rows, :] = hidden.astype(BF)
        n1_t[...] = n1
        hid_t[...] = hidden

        def widen(f, z):
            fs = pl.ds(pl.multiple_of(f * FC, FC), FC)
            up = mm(hid[rows, :], wu[fs, :], NT) + b_u[:, fs]
            phi, e = erf_parts(up)
            act[rows, fs] = (up * phi).astype(BF)
            gp_t[:, fs] = (phi + up * (e * (1.0 / math.sqrt(2.0 * math.pi)))).astype(BF)
            return z

        lax.fori_loop(0, FF // FC, widen, 0)
        r2 = hid_t[...] + mm(act[rows, :], wd[...]) + vec(V_BD)
        c2 = r2 - lane_sum(r2) * (1.0 / D)
        rs2 = lax.rsqrt(lane_sum(c2 * c2) * (1.0 / D) + norm_epsilon)
        n2 = c2 * rs2
        out_c[rows, :] = (n2 * vec(V_G2) + vec(V_C2)).astype(BF)

        e2 = d_br[rows, :].astype(F32)
        add_vec(V_G2, e2 * n2)
        add_vec(V_C2, e2)
        eg = e2 * vec(V_G2)
        d_r2 = rs2 * (eg - lane_sum(eg) * (1.0 / D) - n2 * (lane_sum(eg * n2) * (1.0 / D)))
        d_br[rows, :] = d_r2.astype(BF)
        add_vec(V_BD, d_br[rows, :].astype(F32))
        hid_t[...] = d_r2

        def widen_back(f, z):
            fs = pl.ds(pl.multiple_of(f * FC, FC), FC)
            du = (mm(d_br[rows, :], wd[fs, :], NT) * gp_t[:, fs].astype(F32)).astype(BF)
            d_up[rows, fs] = du
            g_bu[:, fs] += jnp.sum(du.astype(F32), axis=0, keepdims=True)
            return z

        lax.fori_loop(0, FF // FC, widen_back, 0)
        n1 = n1_t[...]
        d_h = hid_t[...] + mm(d_up[rows, :], wu[...])
        add_vec(V_G1, d_h * n1)
        add_vec(V_C1, d_h)
        eg = d_h * vec(V_G1)
        d_r1 = rs1 * (eg - lane_sum(eg) * (1.0 / D) - n1 * (lane_sum(eg * n1) * (1.0 / D)))
        d_proj[rows, :] = d_r1.astype(BF)
        hid_t[...] = d_r1
        add_vec(V_BO, d_proj[rows, :].astype(F32))
        dh_t[...] = mm(d_proj[rows, :], wo[...], NT).astype(BF)

        def attend_back(c, z):
            cr = pl.ds(pl.multiple_of(c * CL, CL), CL)
            gr = pl.ds(pl.multiple_of(r0 + c * CL, CL), CL)
            for p in range(PAIRS):
                ps = slice(p * PW, (p + 1) * PW)
                qp, kp, vp, dh = q_t[cr, ps], k_t[cr, ps], v_t[cr, ps], dh_t[cr, ps]
                weights = p_t[c, p]
                d_w = mm(dh, jnp.concatenate([vp * m0, vp * m1], axis=0), NT)
                halves = []
                for h in range(2):
                    wh = weights[:, h * CL : (h + 1) * CL].astype(F32)
                    dwh = d_w[:, h * CL : (h + 1) * CL]
                    halves.append((wh * (dwh - lane_sum(dwh * wh))).astype(BF))
                d_s = jnp.concatenate(halves, axis=1)
                d_q[gr, ps] = (mm(d_s, jnp.concatenate([kp * m0, kp * m1], axis=0)) * inv).astype(BF)
                dk = mm(d_s, qp, TN)
                d_k[gr, ps] = jnp.where(first_half, dk[0:CL], dk[CL:]).astype(BF)
                dv = mm(weights, dh, TN)
                d_v[gr, ps] = jnp.where(first_half, dv[0:CL], dv[CL:]).astype(BF)
            return z

        lax.fori_loop(0, TM // CL, attend_back, 0)
        dq, dk, dv = d_q[rows, :], d_k[rows, :], d_v[rows, :]
        add_vec(V_BQ, dq.astype(F32))
        add_vec(V_BV, dv.astype(F32))
        d_x = mm(dq, wq[...], NT) + mm(dk, wk[...], NT) + mm(dv, wv[...], NT)
        ing_c[rows, :] = (hid_t[...] + d_x.astype(BF).astype(F32)).astype(BF)
        return carry

    lax.fori_loop(0, ROWS // TM, tile, 0)

    def back_rows(source, to):
        for k in range(SD):
            xbuf[k] = mm(place[:, k * cap : (k + 1) * cap], source[...], TN).astype(BF)
        return pltpu.make_async_copy(xbuf, to, x_sem)

    for k in range(SD):
        line = mm(ent[...].astype(BF), place[:, k * cap : (k + 1) * cap])
        ret_meta[k] = jnp.concatenate([line, line], axis=1)[0:1].astype(BF) * jnp.ones((META, 1), BF)
    back_out = back_rows(out_c, ret_out)
    back_out.start()

    WC = 4 * BLK

    def g_copy(chunk, j, at):
        return pltpu.make_async_copy(
            stage.at[at, pl.ds(j * BLK, BLK)], grads.at[pos[chunk * 4 + j]], g_sem.at[at]
        )

    def put(chunk, left, right):
        at = lax.rem(chunk, 2)

        @pl.when(chunk >= 2)
        def _():
            for j in range(4):
                g_copy(chunk - 2, j, at).wait()

        stage[at] = mm(left, right, TN).astype(BF)
        for j in range(4):
            g_copy(chunk, j, at).start()

    def wide(left, right, first):
        def body(j, c):
            put(first + j, left[:, pl.ds(pl.multiple_of(j * WC, WC), WC)], right[...])
            return c

        lax.fori_loop(0, left.shape[1] // WC, body, 0)

    first = 0
    for left, right in ((x_c, d_q), (x_c, d_k), (x_c, d_v), (heads, d_proj), (d_up, hid), (act, d_br)):
        wide(left, right, first)
        first += left.shape[1] // WC
    back_out.wait()
    back_ing = back_rows(ing_c, ret_ing)
    back_ing.start()
    back_ing.wait()
    last = WROWS // WC
    last = WROWS // WC
    for ch in (last - 2, last - 1):
        for j in range(4):
            g_copy(ch, j, ch % 2).wait()


def local(
    tokens,
    cotangent,
    cluster_order,
    block_owner,
    master_slots,
    moment_one,
    moment_two,
    vector_master,
    vector_moment_one,
    vector_moment_two,
):
    tok_count = lax.axis_size("tok")
    tok_index = lax.axis_index("tok")
    slot_count = master_slots.shape[0]
    cap = tok_count // SD * (max(1, CPS // tok_count) * 3 * CL // (2 * SD))
    total_slots = tok_count * slot_count
    positions = slot_positions(block_owner, slot_count)
    order = cluster_order.reshape(1, ROWS)

    block = jax.ShapeDtypeStruct((SD, cap, D), BF)
    meta_shape = jax.ShapeDtypeStruct((SD, META, D), BF)
    four_planes = tok_count == 8 and lax.axis_size("rep") == 4
    if four_planes:
        slots_low, recv_x, recv_c, recv_meta, vectors, occupancy = gather_all(
            cap, tokens, cotangent, order, master_slots, vector_master
        )
    else:
        slots_low = lax.all_gather(master_slots.astype(BF), "tok", axis=0, tiled=True)
        vectors = lax.all_gather(vector_master.astype(BF), "tok", axis=0, tiled=True).astype(F32)
        cluster = tok_index // SD * CPS + cluster_order // CL
        target = cluster % tok_count
        chosen = target[None, :] == jnp.arange(tok_count, dtype=jnp.int32)[:, None]
        sent_counts = jnp.sum(chosen.astype(F32), axis=1)
        own_row = (jnp.arange(tok_count, dtype=jnp.int32) == tok_index).astype(F32)
        occupancy = lax.psum(own_row[:, None] * sent_counts[None, :], ("tok", "rep")).astype(jnp.int32)
        send_x, send_c, meta = pl.pallas_call(
            functools.partial(send_kernel, cap),
            out_shape=(block, block, meta_shape),
            in_specs=[VMEM] * 3,
            out_specs=(VMEM,) * 3,
            compiler_params=pltpu.CompilerParams(vmem_limit_bytes=40 << 20),
            name="send_rows",
        )(tokens, cotangent, order)
        recv_x, recv_c, recv_meta = (jnp.stack(swap_blocks(b)) for b in (send_x, send_c, meta))

    ret_out, ret_meta, ret_ing, grads, gvec, g_bu = pl.pallas_call(
        functools.partial(layer_kernel, cap),
        out_shape=(
            block,
            meta_shape,
            block,
            jax.ShapeDtypeStruct((total_slots, BLK, D), BF),
            jax.ShapeDtypeStruct((8, D), F32),
            jax.ShapeDtypeStruct((1, FF), F32),
        ),
        in_specs=[SMEM, ANY, VMEM, VMEM, ANY, ANY, VMEM],
        out_specs=(ANY, VMEM, ANY, ANY, VMEM, VMEM),
        scratch_shapes=[
            pltpu.VMEM((WROWS, D), BF),
            pltpu.VMEM((ROWS, SD * cap), BF),
            pltpu.VMEM((SD, cap, D), BF),
            pltpu.VMEM((ROWS, D), BF),
            pltpu.VMEM((ROWS, D), BF),
            pltpu.VMEM((ROWS, FF), BF),
            pltpu.VMEM((ROWS, FF), BF),
            pltpu.VMEM((ROWS, D), BF),
            pltpu.VMEM((ROWS, D), BF),
            pltpu.VMEM((ROWS, D), BF),
            pltpu.VMEM((ROWS, D), BF),
            pltpu.VMEM((ROWS, D), BF),
            pltpu.VMEM((ROWS, D), BF),
            pltpu.VMEM((ROWS, D), BF),
            pltpu.VMEM((ROWS, D), BF),
            pltpu.VMEM((8, ROWS), F32),
            pltpu.VMEM((TM, D), BF),
            pltpu.VMEM((TM, D), BF),
            pltpu.VMEM((TM, D), BF),
            pltpu.VMEM((TM // CL, PAIRS, CL, 2 * CL), BF),
            pltpu.VMEM((TM, FF), BF),
            pltpu.VMEM((TM, D), BF),
            pltpu.VMEM((TM, D), F32),
            pltpu.VMEM((TM, D), F32),
            pltpu.VMEM((2, 4 * BLK, D), BF),
            pltpu.SemaphoreType.DMA,
            pltpu.SemaphoreType.DMA,
            pltpu.SemaphoreType.DMA((2,)),
        ],
        compiler_params=pltpu.CompilerParams(vmem_limit_bytes=63 << 20),
        name="layer",
    )(positions, slots_low, vectors[: 8 * D].reshape(8, D), vectors[8 * D :].reshape(1, FF), recv_x, recv_c, recv_meta)

    back_out, back_meta, back_ing = swap_blocks(ret_out), swap_blocks(ret_meta), swap_blocks(ret_ing)
    row_block = jax.ShapeDtypeStruct((ROWS, D), BF)
    output, entropy = pl.pallas_call(
        functools.partial(return_kernel, cap, True),
        out_shape=(row_block, jax.ShapeDtypeStruct((8, ROWS), BF)),
        in_specs=[VMEM] * (2 * SD + 1),
        out_specs=(VMEM,) * 2,
        compiler_params=pltpu.CompilerParams(vmem_limit_bytes=40 << 20),
        name="return_output",
    )(order, *back_out, *back_meta)
    input_grad = pl.pallas_call(
        functools.partial(return_kernel, cap, False),
        out_shape=row_block,
        in_specs=[VMEM] * (SD + 1),
        out_specs=VMEM,
        compiler_params=pltpu.CompilerParams(vmem_limit_bytes=40 << 20),
        name="return_grad",
    )(order, *back_ing)

    used = jnp.any(
        positions[None, :] == (tok_index * slot_count + jnp.arange(slot_count, dtype=I32))[:, None], axis=1
    )
    grad_vector = jnp.concatenate([gvec.reshape(-1), g_bu.reshape(-1)])
    if four_planes:
        total, vec_owned = reduce_all(grads, grad_vector, slot_count)
    else:
        total = lax.psum(lax.psum_scatter(grads, "tok", scatter_dimension=0, tiled=True), "rep")
        vec_owned = lax.psum(lax.psum_scatter(grad_vector, "tok", scatter_dimension=0, tiled=True), "rep")
    owned_grad = jnp.where(used[:, None, None], total.astype(F32), 0.0)
    first_new, second_new, master_new = adam_update(
        owned_grad, master_slots, moment_one, moment_two, rate_matrix
    )
    vec_first, vec_second, vec_new = adam_update(
        vec_owned, vector_master, vector_moment_one, vector_moment_two, rate_vector
    )
    return (
        output,
        input_grad,
        owned_grad,
        first_new,
        second_new,
        master_new,
        master_new.astype(BF),
        vec_owned,
        vec_first,
        vec_second,
        vec_new,
        vec_new.astype(BF),
        entropy[0],
        occupancy,
    )


def solution(mesh):
    placed = (
        P(("rep", "tok"), None),
        P(("rep", "tok"), None),
        P(("rep", "tok")),
        P(),
        P("tok", None, None),
        P("tok", None, None),
        P("tok", None, None),
        P("tok"),
        P("tok"),
        P("tok"),
    )
    return jax.shard_map(
        local,
        mesh=mesh,
        in_specs=placed,
        out_specs=(
            P(("rep", "tok"), None),
            P(("rep", "tok"), None),
            P("tok", None, None),
            P("tok", None, None),
            P("tok", None, None),
            P("tok", None, None),
            P("tok", None, None),
            P("tok"),
            P("tok"),
            P("tok"),
            P("tok"),
            P("tok"),
            P(("rep", "tok")),
            P(),
        ),
        check_vma=False,
    )
```

```python
import functools
import math

import jax
import jax.numpy as jnp
from jax import lax
from jax.experimental import pallas as pl
from jax.experimental.pallas import tpu as pltpu
from jax.sharding import PartitionSpec as P

D = 768
HEADS = 12
HD = 64
FF = 3072
SD = 4
CL = 128
NBLK = 96
STEP = 10
CPS = 32
WROWS = 9216
BLK = 96
ROWS = 1024
PAIRS = HEADS // 2
PW = 2 * HD
TM = 512
META = 16
VMEM_LIMIT = 63 << 20
FC = 768

norm_epsilon = 1e-06
beta_first = 0.9
beta_second = 0.999
adam_epsilon = 1e-08
weight_decay = 0.01
rate_matrix = 0.02
rate_vector = 0.2

BF = jnp.bfloat16
F32 = jnp.float32
I32 = jnp.int32

VMEM = pl.BlockSpec(memory_space=pltpu.VMEM)
SMEM = pl.BlockSpec(memory_space=pltpu.SMEM)
ANY = pl.BlockSpec(memory_space=pl.ANY)

NN = (((1,), (0,)), ((), ()))
NT = (((1,), (1,)), ((), ()))
TN = (((0,), (0,)), ((), ()))


def mm(a, b, dims=NN):
    return lax.dot_general(a, b, dims, preferred_element_type=F32)


def slot_positions(block_owner, slot_count):
    owners = block_owner[:, 0]
    blocks = owners.shape[0]
    shared = owners[:, None] == owners[None, :]
    before = (
        jnp.arange(blocks, dtype=jnp.int32)[None, :] < jnp.arange(blocks, dtype=jnp.int32)[:, None]
    )
    earlier = jnp.sum((shared & before).astype(jnp.int32), axis=1)
    return owners * slot_count + earlier


def adam_update(grad_now, weight_old, first_old, second_old, rate_step):
    first_new = beta_first * first_old + (1.0 - beta_first) * grad_now
    second_new = beta_second * second_old + (1.0 - beta_second) * grad_now * grad_now
    first_hat = first_new / (1.0 - beta_first**STEP)
    second_hat = second_new / (1.0 - beta_second**STEP)
    weight_new = weight_old - rate_step * (
        first_hat / (jnp.sqrt(second_hat) + adam_epsilon) + weight_decay * weight_old
    )
    return (first_new, second_new, weight_new)


def route_slots(order, seat, cap):
    cluster = order // CL
    rel = lax.rem(cluster, SD) ^ seat
    place = (cluster // SD) * CL + lax.rem(order, CL) + 1
    chosen = lax.broadcasted_iota(I32, (8, ROWS), 0) == rel
    chosen_low = jnp.where(chosen, 1.0, 0.0).astype(BF)
    before = lax.broadcasted_iota(I32, (ROWS, ROWS), 0) < lax.broadcasted_iota(I32, (ROWS, ROWS), 1)
    before_low = jnp.where(before, 1.0, 0.0).astype(BF)
    running = mm(chosen_low, before_low)
    rank = jnp.sum(jnp.where(chosen, running, 0.0), axis=0, keepdims=True).astype(I32)
    return rel * cap + rank, place


def slot_matrix(slots, at, cap):
    rows = lax.broadcasted_iota(I32, (cap, ROWS), 0) + at * cap
    return jnp.where(rows == slots, 1.0, 0.0).astype(BF)


def send_kernel(cap, tokens, cotangent, order, send_x, send_c, meta):
    seat = lax.rem(lax.axis_index("tok"), SD)
    slots, place = route_slots(order[...], seat, cap)
    digits = jnp.concatenate([place // CL, lax.rem(place, CL)] + [place * 0] * 6, axis=0).astype(F32).astype(BF)
    for at in range(SD):
        picked = slot_matrix(slots, at, cap)
        send_x[at] = mm(picked, tokens[...]).astype(BF)
        send_c[at] = mm(picked, cotangent[...]).astype(BF)
        coded = mm(digits, picked, NT)
        line = jnp.concatenate([coded[0:1], coded[1:2]], axis=1)
        meta[at] = jnp.broadcast_to(line, (META, D)).astype(BF)


def remote(src, dst, send_sem, recv_sem, tok, rep):
    return pltpu.make_async_remote_copy(
        src_ref=src,
        dst_ref=dst,
        send_sem=send_sem,
        recv_sem=recv_sem,
        device_id={"tok": tok, "rep": rep},
        device_id_type=pl.DeviceIdType.MESH,
    )


def loop(n, body):
    def run(i, c):
        body(i)
        return c

    lax.fori_loop(0, n, run, 0)


class Place:
    def __init__(self):
        self.me = me = lax.axis_index("tok")
        self.z = z = lax.axis_index("rep")
        core, x, y = me % 2, (me // 2) % 2, me // 4
        self.twin = me + 1 - 2 * core
        self.xn = me + 2 - 4 * x
        self.yn = me + 4 - 8 * y
        self.dn = self.xn + 4 - 8 * y
        self.side = z % 2
        self.zp = z + 1 - 2 * self.side

    def twin_of(self, tok):
        return tok + 1 - 2 * (tok % 2)

    def greet(self, peers):
        barrier = pltpu.get_barrier_semaphore()
        for tok, rep in peers:
            pl.semaphore_signal(
                barrier, inc=1, device_id={"tok": tok, "rep": rep}, device_id_type=pl.DeviceIdType.MESH
            )
        return lambda: pl.semaphore_wait(barrier, len(peers))


def seat_matrix(meta, first, rows, cap):
    hi = jnp.concatenate([meta[k, 0:8, 0:cap] for k in range(SD)], axis=1).astype(F32)[0:1]
    lo = jnp.concatenate([meta[k, 0:8, cap : 2 * cap] for k in range(SD)], axis=1).astype(F32)[0:1]
    at = (hi * CL + lo).astype(I32)
    seats = lax.broadcasted_iota(I32, (rows, SD * cap), 0) + (first + 1)
    return jnp.where(seats == at, 1.0, 0.0).astype(BF)


def seat_part(meta, k, cap):
    hi = meta[k, 0:8, 0:cap].astype(F32)[0:1]
    lo = meta[k, 0:8, cap : 2 * cap].astype(F32)[0:1]
    at = (hi * CL + lo).astype(I32)
    seats = lax.broadcasted_iota(I32, (ROWS, cap), 0) + 1
    return jnp.where(seats == at, 1.0, 0.0).astype(BF)


def seat_rows(meta, blocks, cap, to):
    def body(t):
        r0 = pl.multiple_of(t * 256, 256)
        rows = blocks[...].reshape(SD * cap, D)
        to[pl.ds(r0, 256), :] = mm(seat_matrix(meta, r0, 256, cap), rows).astype(BF)

    loop(ROWS // 256, body)


def seat_kernel(cap, blocks, meta, to):
    seat_rows(meta, blocks, cap, to)


def gather_kernel(
    cap,
    count,
    tokens_h,
    cotangent_h,
    order,
    master_h,
    vector,
    slots,
    x_c,
    cot_c,
    recv_meta,
    vecs,
    b_u,
    occupancy,
    tokens,
    cotangent,
    master,
    own,
    send_x,
    send_c,
    meta,
    recv_x,
    recv_c,
    got_meta,
    mine,
    by_z,
    by_tok,
    x_s,
    x_r,
    y_s,
    y_r,
    d_s,
    d_r,
    zx_s,
    zx_r,
    zd_s,
    zd_r,
    p_s,
    p_r,
    row_s,
    row_r,
    z_s,
    z_r,
    t_s,
    t_r,
    local_s,
):
    at = Place()
    me, z, side = at.me, at.z, at.side
    n_tok, n_rep = 8, 4
    peers = [((me + d) % n_tok, z) for d in range(1, n_tok)] + [(me, (z + d) % n_rep) for d in range(1, n_rep)]
    fetch = [
        pltpu.make_async_copy(src, dst, local_s.at[i])
        for i, (src, dst) in enumerate(((master_h, master), (tokens_h, tokens), (cotangent_h, cotangent)))
    ]
    for copy in fetch:
        copy.start()
    wait_peers = at.greet(peers)
    fetch[0].wait()

    def cast(s):
        own[s] = master[s].astype(BF)

    loop(count, cast)
    wait_peers()

    half = count // 2

    def slot(owner, s):
        return slots.at[owner * count + s]

    def to_x(s):
        return remote(own.at[s], slot(me, s), x_s.at[s], x_r.at[s], at.xn, z)

    def to_y(s):
        return remote(own.at[s], slot(me, s), y_s.at[s], y_r.at[s], at.yn, z)

    def on_y(s):
        return remote(slot(at.xn, s), slot(at.xn, s), d_s.at[s], d_r.at[s], at.yn, z)

    def x_on_z(s):
        return remote(slot(at.xn, s), slot(at.xn, s), zx_s.at[s], zx_r.at[s], me, at.zp)

    def d_on_z(s):
        return remote(slot(at.dn, s), slot(at.dn, s), zd_s.at[s], zd_r.at[s], me, at.zp)

    owners = (me, at.xn, at.yn, at.dn)

    def to_twin(q, s):
        src = own.at[s] if q == 0 else slot(owners[q], s)
        return remote(src, slot(owners[q], s), p_s.at[q, s], p_r.at[q, s], at.twin, z)

    def near(j):
        return (half + 1) * side + j

    def far(j):
        return (half + 1) * (1 - side) + j

    loop(half, lambda j: to_x(near(j)).start())
    to_x(half).start()
    for s in range(3):
        to_y(s).start()
    loop(count, lambda s: to_twin(0, s).start())
    keep = pltpu.make_async_copy(own, slots.at[pl.ds(me * count, count)], local_s.at[3])
    keep.start()
    fetch[1].wait()
    fetch[2].wait()

    seat = me % SD
    slot_of, place = route_slots(order[...], seat, cap)
    digits = jnp.concatenate([place // CL, lax.rem(place, CL)] + [place * 0] * 6, axis=0).astype(F32).astype(BF)
    for k in range(SD):
        picked = slot_matrix(slot_of, k, cap)
        send_x[k] = mm(picked, tokens[...]).astype(BF)
        send_c[k] = mm(picked, cotangent[...]).astype(BF)
        coded = mm(digits, picked, NT)
        line = jnp.concatenate([coded[0:1], coded[1:2]], axis=1)
        meta[k] = jnp.broadcast_to(line, (META, D)).astype(BF)
    seats = (me, at.twin, at.xn, at.twin_of(at.xn))
    rows_of = ((meta, got_meta), (send_x, recv_x), (send_c, recv_c))

    def row_copy(i, k):
        src, dst = rows_of[i]
        return remote(src.at[k], dst.at[k], row_s.at[i, k], row_r.at[i, k], seats[k], z)

    for i in range(3):
        src, dst = rows_of[i]
        for k in (2, 3, 1):
            row_copy(i, k).start()
        dst[0] = src[0]

    residue = lax.rem(me // SD * CPS + order[...] // CL, n_tok)
    hit = lax.broadcasted_iota(I32, (128, ROWS), 0) == residue
    mine[0:16] = vector[...].astype(BF).astype(F32)
    by_z[0] = mm(jnp.ones((8, ROWS), BF), jnp.where(hit, 1.0, 0.0).astype(BF), NT)

    def z_copy(d):
        return remote(by_z.at[0], by_z.at[d], z_s.at[d], z_r.at[d], me, (z + d) % n_rep)

    def t_copy(d):
        return remote(mine, by_tok.at[d], t_s.at[d], t_r.at[d], (me + d) % n_tok, z)

    for d in range(1, n_rep):
        z_copy(d).start()
    for d in range(1, n_rep):
        z_copy(d).wait()
    mine[16:24] = by_z[0] + by_z[1] + by_z[2] + by_z[3]
    for d in range(1, n_tok):
        t_copy(d).start()

    def x_here(s):
        to_x_in(s).wait_recv()
        on_y(s).start()
        to_twin(1, s).start()

    def to_x_in(s):
        return remote(own.at[s], slot(at.xn, s), x_s.at[s], x_r.at[s], at.xn, z)

    def y_in(s):
        return remote(own.at[s], slot(at.yn, s), y_s.at[s], y_r.at[s], at.yn, z)

    def d_in(s):
        return remote(own.at[s], slot(at.dn, s), d_s.at[s], d_r.at[s], at.yn, z)

    def first(j):
        x_here(near(j))
        x_on_z(near(j)).start()
        to_y(3 + j).start()

    loop(half, first)
    x_here(half)
    for s in range(3 + half, count):
        to_y(s).start()

    def y_here(s):
        y_in(s).wait_recv()
        to_twin(2, s).start()

    def second(j):
        x_on_z(far(j)).wait_recv()
        to_twin(1, far(j)).start()
        y_here(j)
        d_in(near(j)).wait_recv()
        d_on_z(near(j)).start()
        to_twin(3, near(j)).start()

    loop(half, second)
    d_in(half).wait_recv()
    to_twin(3, half).start()
    loop(count - half, lambda j: y_here(half + j))
    for i in (0, 1):
        for k in (2, 3, 1):
            row_copy(i, k).wait_recv()
    recv_meta[...] = got_meta[...]
    seat_rows(got_meta, recv_x, cap, x_c)

    def third(j):
        d_on_z(far(j)).wait_recv()
        to_twin(3, far(j)).start()

    loop(half, third)

    by_tok[0] = mine[...]
    for d in range(1, n_tok):
        t_copy(d).wait()
    for owner in range(n_tok):
        share = by_tok[(me + n_tok - owner) % n_tok]
        occupancy[owner : owner + 1, :] = share[16:17, 0:n_tok].astype(I32)
        for i in range(9):
            chunk = owner * 9 + i
            row, lane = chunk // 6, chunk % 6 * 128
            if row < 8:
                vecs[row : row + 1, lane : lane + 128] = share[i : i + 1]
            else:
                lane += (row - 8) * D
                b_u[:, lane : lane + 128] = share[i : i + 1]
    for k in (2, 3, 1):
        row_copy(2, k).wait_recv()
    seat_rows(got_meta, recv_c, cap, cot_c)
    for i in range(3):
        for k in (2, 3, 1):
            row_copy(i, k).wait_send()
    keep.wait()

    def sent_half(j):
        to_x(near(j)).wait_send()
        on_y(near(j)).wait_send()
        x_on_z(near(j)).wait_send()
        d_on_z(near(j)).wait_send()

    loop(half, sent_half)
    to_x(half).wait_send()
    on_y(half).wait_send()

    def sent(s):
        to_y(s).wait_send()
        for q in range(4):
            to_twin(q, s).wait()

    loop(count, sent)


def gather_all(cap, tokens, cotangent, order, master, vector):
    count = master.shape[0]
    rows = jax.ShapeDtypeStruct((ROWS, D), BF)
    dma = pltpu.SemaphoreType.DMA
    block = pltpu.VMEM((SD, cap, D), BF)
    meta = pltpu.VMEM((SD, META, D), BF)
    return pl.pallas_call(
        functools.partial(gather_kernel, cap, count),
        out_shape=(
            jax.ShapeDtypeStruct((8 * count, BLK, D), BF),
            rows,
            rows,
            jax.ShapeDtypeStruct((SD, META, D), BF),
            jax.ShapeDtypeStruct((8, D), F32),
            jax.ShapeDtypeStruct((1, FF), F32),
            jax.ShapeDtypeStruct((8, 8), I32),
        ),
        in_specs=[ANY, ANY, VMEM, ANY, VMEM],
        out_specs=(ANY,) + (VMEM,) * 6,
        scratch_shapes=[
            pltpu.VMEM((ROWS, D), BF),
            pltpu.VMEM((ROWS, D), BF),
            pltpu.VMEM((count, BLK, D), F32),
            pltpu.VMEM((count, BLK, D), BF),
            block,
            block,
            meta,
            block,
            block,
            meta,
            pltpu.VMEM((24, 128), F32),
            pltpu.VMEM((4, 8, 128), F32),
            pltpu.VMEM((8, 24, 128), F32),
        ]
        + [dma((count,))] * 10
        + [dma((4, count))] * 2
        + [dma((3, SD))] * 2
        + [dma((4,))] * 2
        + [dma((8,))] * 2
        + [dma((4,))],
        compiler_params=pltpu.CompilerParams(collective_id=0, has_side_effects=True, vmem_limit_bytes=VMEM_LIMIT),
        name="gather",
    )(tokens, cotangent, order, master, jnp.pad(vector.reshape(9, 128), ((0, 7), (0, 0))))


def return_kernel(cap, order, *refs):
    blocks, (out, ing, entropy) = refs[:SD], refs[SD:]
    seat = lax.rem(lax.axis_index("tok"), SD)
    slots, _ = route_slots(order[...], seat, cap)
    picked = jnp.concatenate([slot_matrix(slots, at, cap) for at in range(SD)], axis=0)
    for to, first in ((out, 0), (ing, cap)):
        rows = jnp.concatenate([block[first : first + cap, :] for block in blocks], axis=0)
        to[...] = mm(picked, rows, TN).astype(BF)
    line = jnp.concatenate([block[2 * cap : 2 * cap + 8, 0:cap] for block in blocks], axis=1)
    entropy[...] = mm(line, picked).astype(BF)


def swap_blocks(blocks):
    n = lax.axis_size("tok")
    parts = [blocks[0]]
    for k in range(1, SD):
        parts.append(lax.ppermute(blocks[k], "tok", [(i, i ^ k) for i in range(n)]))
    return parts


def reduce_kernel(
    count,
    split,
    grads,
    vec,
    total,
    vec_out,
    a,
    tw,
    rd,
    rx,
    ry,
    o,
    rz1,
    pz,
    rz2,
    fz,
    vt,
    va,
    vb,
    vc,
    a_l,
    keep_l,
    p_s,
    p_r,
    d_s,
    d_r,
    x_s,
    x_r,
    y_s,
    y_r,
    z1_s,
    z1_r,
    z2_s,
    z2_r,
    z3_s,
    z3_r,
    t_s,
    t_r,
    v_s,
    v_r,
):
    at = Place()
    me, z = at.me, at.z
    n_tok, n_rep = 8, 4
    peers = [((me + d) % n_tok, z) for d in range(1, n_tok)] + [(me, (z + d) % n_rep) for d in range(1, n_rep)]
    wait_peers = at.greet(peers)
    owners = (me, at.xn, at.yn, at.dn)

    def load(q):
        return pltpu.make_async_copy(grads.at[pl.ds(owners[q] * count, count)], a.at[q], a_l.at[q])

    for q in (3, 1, 2, 0):
        load(q).start()
    wait_peers()

    def to_twin(q, s):
        src = grads.at[at.twin_of(owners[q]) * count + s]
        return remote(src, tw.at[q, s], p_s.at[q, s], p_r.at[q, s], at.twin, z)

    def d_y(s):
        return remote(a.at[3, s], rd.at[s], d_s.at[s], d_r.at[s], at.yn, z)

    def d_x(s):
        return remote(a.at[3, s], rd.at[s], d_s.at[s], d_r.at[s], at.xn, z)

    def to_x(s):
        return remote(a.at[1, s], rx.at[s], x_s.at[s], x_r.at[s], at.xn, z)

    def to_y(s):
        return remote(a.at[2, s], ry.at[s], y_s.at[s], y_r.at[s], at.yn, z)

    def z_in(s):
        return remote(o.at[s], rz1.at[s], z1_s.at[s], z1_r.at[s], me, at.zp)

    def z_swap(s):
        return remote(pz.at[s], rz2.at[s], z2_s.at[s], z2_r.at[s], me, n_rep - 1 - z)

    def z_out(s):
        return remote(fz.at[s], fz.at[s], z3_s.at[s], z3_r.at[s], me, at.zp)

    def keep(s):
        return pltpu.make_async_copy(fz.at[s], total.at[s], keep_l.at[s])

    def f32(ref, *index):
        return ref[index].astype(F32)

    loop(count, lambda s: to_twin(3, s).start())

    def others(s):
        for q in (2, 1, 0):
            to_twin(q, s).start()

    loop(count, others)

    def v_tok(d):
        return remote(vec.at[(me + d) % n_tok], vt.at[d], t_s.at[d], t_r.at[d], (me + d) % n_tok, z)

    def v_rep(i, src):
        return remote(src, vb.at[i], v_s.at[i], v_r.at[i], me, at.zp if i == 0 else (z + 2) % n_rep)

    for d in range(1, n_tok):
        v_tok(d).start()

    load(3).wait()

    def join(q, s):
        to_twin(q, s).wait_recv()
        return f32(a, q, s) + f32(tw, q, s)

    def diagonal(s, send):
        a[3, s] = join(3, s).astype(BF)
        send(s).start()

    loop(split, lambda s: diagonal(s, d_y))
    loop(count - split, lambda j: diagonal(split + j, d_x))

    v_sum = vec[me]
    for d in range(1, n_tok):
        v_tok(d).wait()
        v_sum = v_sum + vt[d]
    va[...] = v_sum
    v_rep(0, va).start()

    load(1).wait()
    load(2).wait()

    def plane_y(s):
        a[2, s] = join(2, s).astype(BF)
        to_y(s).start()
        d_y(s).wait_recv()
        a[1, s] = (join(1, s) + f32(rd, s)).astype(BF)
        to_x(s).start()

    def plane_x(s):
        a[1, s] = join(1, s).astype(BF)
        to_x(s).start()
        d_x(s).wait_recv()
        a[2, s] = (join(2, s) + f32(rd, s)).astype(BF)
        to_y(s).start()

    loop(split, plane_y)
    loop(count - split, lambda j: plane_x(split + j))

    v_rep(0, va).wait()
    vc[...] = va[...] + vb[0]
    v_rep(1, vc).start()
    load(0).wait()
    inner = (z == 1) | (z == 2)
    outer = (z == 0) | (z == 3)

    def planes(i):
        @pl.when(i < count)
        def _():
            to_x(i).wait_recv()
            to_y(i).wait_recv()
            o[i] = (join(0, i) + f32(rx, i) + f32(ry, i)).astype(BF)

        @pl.when(outer & (i < count))
        def _():
            z_in(i).start()

        @pl.when(inner & (i >= 1) & (i < count + 1))
        def _():
            s = i - 1
            z_in(s).wait_recv()
            pz[s] = (f32(o, s) + f32(rz1, s)).astype(BF)
            z_swap(s).start()

        @pl.when(inner & (i >= 2) & (i < count + 2))
        def _():
            s = i - 2
            z_swap(s).wait_recv()
            fz[s] = (f32(pz, s) + f32(rz2, s)).astype(BF)
            z_out(s).start()
            keep(s).start()

        @pl.when(outer & (i >= 3))
        def _():
            s = i - 3
            z_out(s).wait_recv()
            keep(s).start()

    loop(count + 3, planes)
    v_rep(1, vc).wait()
    vec_out[...] = vc[...] + vb[1]

    def sent(s):
        for q in range(4):
            to_twin(q, s).wait_send()
        d_y(s).wait_send()
        to_x(s).wait_send()
        to_y(s).wait_send()
        keep(s).wait()

    loop(count, sent)

    @pl.when(outer)
    def _():
        loop(count, lambda s: z_in(s).wait_send())

    @pl.when(inner)
    def _():
        def back(s):
            z_swap(s).wait_send()
            z_out(s).wait_send()

        loop(count, back)


def reduce_all(grads, shares, count):
    dma = pltpu.SemaphoreType.DMA
    part = pltpu.VMEM((count, BLK, D), BF)
    whole = pltpu.VMEM((4, count, BLK, D), BF)
    line = pltpu.VMEM((16, 128), F32)
    total, vec = pl.pallas_call(
        functools.partial(reduce_kernel, count, count),
        out_shape=(
            jax.ShapeDtypeStruct((count, BLK, D), BF),
            jax.ShapeDtypeStruct((16, 128), F32),
        ),
        in_specs=[ANY, VMEM],
        out_specs=(ANY, VMEM),
        scratch_shapes=[whole, whole]
        + [part] * 8
        + [pltpu.VMEM((8, 16, 128), F32), line, pltpu.VMEM((2, 16, 128), F32), line]
        + [dma((4,)), dma((count,))]
        + [dma((4, count))] * 2
        + [dma((count,))] * 12
        + [dma((8,))] * 2
        + [dma((2,))] * 2,
        compiler_params=pltpu.CompilerParams(
            collective_id=1, has_side_effects=True, vmem_limit_bytes=VMEM_LIMIT
        ),
        name="reduce",
    )(grads, shares)
    return total, vec[0:9].reshape(-1)


V_BQ, V_BV, V_BO, V_BD, V_G1, V_C1, V_G2, V_C2 = range(8)


def erf_parts(v):
    z = jnp.abs(v) * (1.0 / math.sqrt(2.0))
    t = 1.0 / (1.0 + 0.3275911 * z)
    e = jnp.exp(-z * z)
    poly = 0.5 * 1.061405429
    for c in (-1.453152027, 1.421413741, -0.284496736, 0.254829592):
        poly = poly * t + 0.5 * c
    tail = poly * t * e
    return jnp.where(v >= 0.0, 1.0 - tail, tail), e


def lane_sum(x):
    return jnp.sum(x, axis=1, keepdims=True)


def gelu_parts(v):
    phi, e = erf_parts(v)
    return v * phi, phi + v * (e * (1.0 / math.sqrt(2.0 * math.pi)))


def chain_kernel(
    cap,
    pos,
    slots,
    vecs,
    b_u,
    x_h,
    cot_h,
    meta,
    back_0,
    back_1,
    back_2,
    back_3,
    shares,
    heads_h,
    act_h,
    d_up_h,
    d_q_h,
    d_k_h,
    d_v_h,
    d_proj_h,
    hid_h,
    d_br_h,
    w,
    x_c,
    heads,
    act,
    d_up,
    d_q,
    d_k,
    d_v,
    d_proj,
    hid,
    d_br,
    out_c,
    ing_c,
    ent,
    gvec,
    g_bu,
    q_t,
    k_t,
    v_t,
    p_t,
    dh_t,
    n1_t,
    hid_t,
    w_sem,
    x_sem,
    o_sem,
):
    inv = 1.0 / math.sqrt(HD)

    def w_copy(b):
        return pltpu.make_async_copy(slots.at[pos[b]], w.at[pl.ds(b * BLK, BLK)], w_sem)

    get_x = pltpu.make_async_copy(x_h, x_c, x_sem.at[0])
    get_cot = pltpu.make_async_copy(cot_h, d_br, x_sem.at[1])
    get_x.start()
    loop(NBLK, lambda b: w_copy(b).start())
    get_cot.start()
    gvec[...] = jnp.zeros_like(gvec)
    g_bu[...] = jnp.zeros_like(g_bu)
    shares[...] = jnp.zeros_like(shares)
    get_x.wait()
    loop(NBLK, lambda b: w_copy(b).wait())
    get_cot.wait()

    wq, wk, wv, wo = (w.at[pl.ds(i * D, D)] for i in range(4))
    wu = w.at[pl.ds(4 * D, FF)]
    wd = w.at[pl.ds(4 * D + FF, FF)]

    lane = lax.broadcasted_iota(I32, (1, PW), 1)
    m0 = jnp.where(lane < HD, 1.0, 0.0).astype(BF)
    m1 = jnp.where(lane < HD, 0.0, 1.0).astype(BF)
    first_half = lax.broadcasted_iota(I32, (CL, PW), 1) < HD

    def apart(pair):
        return jnp.concatenate([pair * m0, pair * m1], axis=0)

    def vec(i):
        return vecs[i : i + 1, :]

    def add_vec(i, value):
        gvec[i : i + 1, :] += jnp.sum(value, axis=0, keepdims=True)

    saved = (
        (heads, heads_h),
        (act, act_h),
        (d_up, d_up_h),
        (d_q, d_q_h),
        (d_k, d_k_h),
        (d_v, d_v_h),
        (d_proj, d_proj_h),
        (hid, hid_h),
        (d_br, d_br_h),
    )

    def save(t, i):
        rows = pl.ds(pl.multiple_of(t * TM, TM), TM)
        src, dst = saved[i]
        return pltpu.make_async_copy(src.at[rows], dst.at[rows], o_sem.at[i])

    def tile(t):
        r0 = pl.multiple_of(t * TM, TM)
        rows = pl.ds(r0, TM)
        q_t[...] = ((mm(x_c[rows, :], wq[...]) + vec(V_BQ)).astype(BF).astype(F32) * inv).astype(BF)
        k_t[...] = mm(x_c[rows, :], wk[...]).astype(BF)
        v_t[...] = (mm(x_c[rows, :], wv[...]) + vec(V_BV)).astype(BF)

        def attend(c):
            cr = pl.ds(pl.multiple_of(c * CL, CL), CL)
            gr = pl.ds(pl.multiple_of(r0 + c * CL, CL), CL)
            total = jnp.zeros((1, CL), F32)
            for p in range(PAIRS):
                ps = slice(p * PW, (p + 1) * PW)
                scores = mm(apart(k_t[cr, ps]), q_t[cr, ps], NT)
                halves = []
                for h in range(2):
                    sh = scores[h * CL : (h + 1) * CL]
                    sh = sh - jnp.max(sh, axis=0, keepdims=True)
                    e = jnp.exp(sh)
                    tot = jnp.sum(e, axis=0, keepdims=True)
                    r = 1.0 / tot
                    total += jnp.log(tot) - jnp.sum(e * sh, axis=0, keepdims=True) * r
                    halves.append((e * r).astype(BF))
                weights = jnp.concatenate(halves, axis=0)
                p_t[c, p] = weights
                heads[gr, ps] = mm(weights, apart(v_t[cr, ps]), TN).astype(BF)
            ent[:, gr] = jnp.broadcast_to(total * (1.0 / HEADS), (8, CL))

        loop(TM // CL, attend)

        r1 = x_c[rows, :].astype(F32) + mm(heads[rows, :], wo[...]) + vec(V_BO)
        c1 = r1 - lane_sum(r1) * (1.0 / D)
        rs1 = lax.rsqrt(lane_sum(c1 * c1) * (1.0 / D) + norm_epsilon)
        n1 = c1 * rs1
        hidden = n1 * vec(V_G1) + vec(V_C1)
        hid[rows, :] = hidden.astype(BF)
        n1_t[...] = n1
        hid_t[...] = hidden

        def widen(f):
            fs = pl.ds(pl.multiple_of(f * FC, FC), FC)
            g, g_slope = gelu_parts(mm(hid[rows, :], wu[fs, :], NT) + b_u[:, fs])
            act[rows, fs] = g.astype(BF)
            d_up[rows, fs] = g_slope.astype(BF)

        loop(FF // FC, widen)
        r2 = hid_t[...] + mm(act[rows, :], wd[...]) + vec(V_BD)
        c2 = r2 - lane_sum(r2) * (1.0 / D)
        rs2 = lax.rsqrt(lane_sum(c2 * c2) * (1.0 / D) + norm_epsilon)
        n2 = c2 * rs2
        out_c[rows, :] = (n2 * vec(V_G2) + vec(V_C2)).astype(BF)

        e2 = d_br[rows, :].astype(F32)
        add_vec(V_G2, e2 * n2)
        add_vec(V_C2, e2)
        eg = e2 * vec(V_G2)
        d_r2 = rs2 * (eg - lane_sum(eg) * (1.0 / D) - n2 * (lane_sum(eg * n2) * (1.0 / D)))
        d_br[rows, :] = d_r2.astype(BF)
        add_vec(V_BD, d_br[rows, :].astype(F32))
        hid_t[...] = d_r2

        def widen_back(f):
            fs = pl.ds(pl.multiple_of(f * FC, FC), FC)
            du = (mm(d_br[rows, :], wd[fs, :], NT) * d_up[rows, fs].astype(F32)).astype(BF)
            d_up[rows, fs] = du
            g_bu[:, fs] += jnp.sum(du.astype(F32), axis=0, keepdims=True)

        loop(FF // FC, widen_back)
        n1 = n1_t[...]
        d_h = hid_t[...] + mm(d_up[rows, :], wu[...])
        add_vec(V_G1, d_h * n1)
        add_vec(V_C1, d_h)
        eg = d_h * vec(V_G1)
        d_r1 = rs1 * (eg - lane_sum(eg) * (1.0 / D) - n1 * (lane_sum(eg * n1) * (1.0 / D)))
        d_proj[rows, :] = d_r1.astype(BF)
        hid_t[...] = d_r1
        add_vec(V_BO, d_proj[rows, :].astype(F32))
        dh_t[...] = mm(d_proj[rows, :], wo[...], NT).astype(BF)

        def attend_back(c):
            cr = pl.ds(pl.multiple_of(c * CL, CL), CL)
            gr = pl.ds(pl.multiple_of(r0 + c * CL, CL), CL)
            for p in range(PAIRS):
                ps = slice(p * PW, (p + 1) * PW)
                dh = dh_t[cr, ps]
                weights = p_t[c, p]
                d_w = mm(apart(v_t[cr, ps]), dh, NT)
                halves = []
                for h in range(2):
                    wh = weights[h * CL : (h + 1) * CL].astype(F32)
                    dwh = d_w[h * CL : (h + 1) * CL]
                    halves.append((wh * (dwh - jnp.sum(dwh * wh, axis=0, keepdims=True))).astype(BF))
                d_s = jnp.concatenate(halves, axis=0)
                d_q[gr, ps] = (mm(d_s, apart(k_t[cr, ps]), TN) * inv).astype(BF)
                dk = mm(d_s, q_t[cr, ps])
                d_k[gr, ps] = jnp.where(first_half, dk[0:CL], dk[CL:]).astype(BF)
                dv = mm(weights, dh)
                d_v[gr, ps] = jnp.where(first_half, dv[0:CL], dv[CL:]).astype(BF)

        loop(TM // CL, attend_back)
        add_vec(V_BQ, d_q[rows, :].astype(F32))
        add_vec(V_BV, d_v[rows, :].astype(F32))
        d_x = mm(d_q[rows, :], wq[...], NT) + mm(d_k[rows, :], wk[...], NT) + mm(d_v[rows, :], wv[...], NT)
        ing_c[rows, :] = (hid_t[...] + d_x.astype(BF).astype(F32)).astype(BF)
        for i in range(len(saved)):
            save(t, i).start()

    loop(ROWS // TM, tile)

    for k, back in enumerate((back_0, back_1, back_2, back_3)):
        own = seat_part(meta, k, cap)
        back[0:cap, :] = mm(own, out_c[...], TN).astype(BF)
        back[cap : 2 * cap, :] = mm(own, ing_c[...], TN).astype(BF)
        line = mm(ent[...].astype(BF), own)
        back[2 * cap :, :] = jnp.concatenate([line, line], axis=1)[0:1].astype(BF) * jnp.ones((META, 1), BF)

    for chunk in range(72):
        row, lane = chunk // 6, chunk % 6 * 128
        if row < 8:
            part = gvec[row : row + 1, lane : lane + 128]
        else:
            lane += (row - 8) * D
            part = g_bu[:, lane : lane + 128]
        shares[chunk // 9, chunk % 9 : chunk % 9 + 1, :] = part

    def saved_all(t):
        for i in range(len(saved)):
            save(t, i).wait()

    loop(ROWS // TM, saved_all)


def chain(cap, positions, slots, vecs, b_u, x_c, cot_c, meta):
    rows = jax.ShapeDtypeStruct((ROWS, D), BF)
    wide = jax.ShapeDtypeStruct((ROWS, FF), BF)
    back = jax.ShapeDtypeStruct((2 * cap + META, D), BF)
    r_v, w_v, t_v, t_f = (pltpu.VMEM(shape, kind) for shape, kind in (
        ((ROWS, D), BF), ((ROWS, FF), BF), ((TM, D), BF), ((TM, D), F32)
    ))
    return pl.pallas_call(
        functools.partial(chain_kernel, cap),
        out_shape=(back,) * SD + (jax.ShapeDtypeStruct((8, 16, 128), F32), rows, wide, wide) + (rows,) * 6,
        in_specs=[SMEM, ANY, VMEM, VMEM, ANY, ANY, VMEM],
        out_specs=(VMEM,) * (SD + 1) + (ANY,) * 9,
        scratch_shapes=[
            pltpu.VMEM((WROWS, D), BF),
            r_v,
            r_v,
            w_v,
            w_v,
            r_v,
            r_v,
            r_v,
            r_v,
            r_v,
            r_v,
            r_v,
            r_v,
            pltpu.VMEM((8, ROWS), F32),
            pltpu.VMEM((8, D), F32),
            pltpu.VMEM((1, FF), F32),
            t_v,
            t_v,
            t_v,
            pltpu.VMEM((TM // CL, PAIRS, 2 * CL, CL), BF),
            t_v,
            t_f,
            t_f,
            pltpu.SemaphoreType.DMA,
            pltpu.SemaphoreType.DMA((2,)),
            pltpu.SemaphoreType.DMA((9,)),
        ],
        compiler_params=pltpu.CompilerParams(vmem_limit_bytes=VMEM_LIMIT),
        name="layer",
    )(positions, slots, vecs, b_u, x_c, cot_c, meta)


WC = 8 * BLK


def weight_kernel(
    pos,
    x_h,
    heads_h,
    act_h,
    d_up_h,
    d_q_h,
    d_k_h,
    d_v_h,
    d_proj_h,
    hid_h,
    d_br_h,
    grads,
    x_c,
    heads,
    act,
    d_up,
    d_q,
    d_k,
    d_v,
    d_proj,
    hid,
    d_br,
    stage,
    i_sem,
    g_sem,
):
    refs = (
        (x_h, x_c),
        (d_q_h, d_q),
        (d_k_h, d_k),
        (d_v_h, d_v),
        (heads_h, heads),
        (d_proj_h, d_proj),
        (hid_h, hid),
        (d_up_h, d_up),
        (d_br_h, d_br),
        (act_h, act),
    )
    fetch = [pltpu.make_async_copy(src, dst, i_sem.at[i]) for i, (src, dst) in enumerate(refs)]
    for copy in fetch:
        copy.start()

    per = WC // BLK

    def g_copy(chunk, j, at):
        return pltpu.make_async_copy(
            stage.at[at, pl.ds(j * BLK, BLK)], grads.at[pos[chunk * per + j]], g_sem.at[at]
        )

    def put(chunk, left, right):
        at = lax.rem(chunk, 2)

        @pl.when(chunk >= 2)
        def _():
            for j in range(per):
                g_copy(chunk - 2, j, at).wait()

        stage[at] = mm(left, right, TN).astype(BF)
        for j in range(per):
            g_copy(chunk, j, at).start()

    first = 0
    for left, right, needs in (
        (x_c, d_q, (0, 1)),
        (x_c, d_k, (2,)),
        (x_c, d_v, (3,)),
        (heads, d_proj, (4, 5)),
        (d_up, hid, (6, 7)),
        (act, d_br, (8, 9)),
    ):
        for i in needs:
            fetch[i].wait()

        def body(j, left=left, right=right, first=first):
            put(first + j, left[:, pl.ds(pl.multiple_of(j * WC, WC), WC)], right[...])

        loop(left.shape[1] // WC, body)
        first += left.shape[1] // WC
    for chunk in (first - 2, first - 1):
        for j in range(per):
            g_copy(chunk, j, chunk % 2).wait()


def weight_grads_of(total_slots, positions, x_c, saved):
    r_v, w_v = pltpu.VMEM((ROWS, D), BF), pltpu.VMEM((ROWS, FF), BF)
    return pl.pallas_call(
        weight_kernel,
        out_shape=jax.ShapeDtypeStruct((total_slots, BLK, D), BF),
        in_specs=[SMEM] + [ANY] * 10,
        out_specs=ANY,
        scratch_shapes=[r_v, r_v, w_v, w_v]
        + [r_v] * 6
        + [
            pltpu.VMEM((2, WC, D), BF),
            pltpu.SemaphoreType.DMA((10,)),
            pltpu.SemaphoreType.DMA((2,)),
        ],
        compiler_params=pltpu.CompilerParams(vmem_limit_bytes=VMEM_LIMIT),
        cost_estimate=pl.CostEstimate(flops=2 * ROWS * WROWS * D, bytes_accessed=40 << 20, transcendentals=0),
        name="weight_grads",
    )(positions, x_c, *saved)


def local(
    tokens,
    cotangent,
    cluster_order,
    block_owner,
    master_slots,
    moment_one,
    moment_two,
    vector_master,
    vector_moment_one,
    vector_moment_two,
):
    tok_count = lax.axis_size("tok")
    tok_index = lax.axis_index("tok")
    slot_count = master_slots.shape[0]
    cap = tok_count // SD * (max(1, CPS // tok_count) * 3 * CL // (2 * SD))
    total_slots = tok_count * slot_count
    positions = slot_positions(block_owner, slot_count)
    order = cluster_order.reshape(1, ROWS)

    block = jax.ShapeDtypeStruct((SD, cap, D), BF)
    meta_shape = jax.ShapeDtypeStruct((SD, META, D), BF)
    row_block = jax.ShapeDtypeStruct((ROWS, D), BF)
    four_planes = tok_count == 8 and lax.axis_size("rep") == 4
    if four_planes:
        slots_low, x_c, cot_c, recv_meta, vecs, b_u, occupancy = gather_all(
            cap, tokens, cotangent, order, master_slots, vector_master
        )
    else:
        slots_low = lax.all_gather(master_slots.astype(BF), "tok", axis=0, tiled=True)
        vectors = lax.all_gather(vector_master.astype(BF), "tok", axis=0, tiled=True).astype(F32)
        vecs, b_u = vectors[: 8 * D].reshape(8, D), vectors[8 * D :].reshape(1, FF)
        cluster = tok_index // SD * CPS + cluster_order // CL
        target = cluster % tok_count
        chosen = target[None, :] == jnp.arange(tok_count, dtype=jnp.int32)[:, None]
        sent_counts = jnp.sum(chosen.astype(F32), axis=1)
        own_row = (jnp.arange(tok_count, dtype=jnp.int32) == tok_index).astype(F32)
        occupancy = lax.psum(own_row[:, None] * sent_counts[None, :], ("tok", "rep")).astype(jnp.int32)
        send_x, send_c, meta = pl.pallas_call(
            functools.partial(send_kernel, cap),
            out_shape=(block, block, meta_shape),
            in_specs=[VMEM] * 3,
            out_specs=(VMEM,) * 3,
            compiler_params=pltpu.CompilerParams(vmem_limit_bytes=VMEM_LIMIT),
            name="send_rows",
        )(tokens, cotangent, order)
        recv_x, recv_c, recv_meta = (jnp.stack(swap_blocks(b)) for b in (send_x, send_c, meta))
        x_c, cot_c = (
            pl.pallas_call(
                functools.partial(seat_kernel, cap),
                out_shape=row_block,
                in_specs=[VMEM] * 2,
                out_specs=VMEM,
                compiler_params=pltpu.CompilerParams(vmem_limit_bytes=VMEM_LIMIT),
                name="seat_rows",
            )(rows, recv_meta)
            for rows in (recv_x, recv_c)
        )

    *backs, shares, heads, act, d_up, d_q, d_k, d_v, d_proj, hid, d_br = chain(
        cap, positions, slots_low, vecs, b_u, x_c, cot_c, recv_meta
    )
    returned = swap_blocks(backs)
    grads = weight_grads_of(
        total_slots, positions, x_c, (heads, act, d_up, d_q, d_k, d_v, d_proj, hid, d_br)
    )
    if four_planes:
        total, vec_owned = reduce_all(grads, shares, slot_count)
    else:
        total = lax.psum(lax.psum_scatter(grads, "tok", scatter_dimension=0, tiled=True), "rep")
        grad_vector = shares[:, 0:9].reshape(-1)
        vec_owned = lax.psum(lax.psum_scatter(grad_vector, "tok", scatter_dimension=0, tiled=True), "rep")
    output, input_grad, entropy = pl.pallas_call(
        functools.partial(return_kernel, cap),
        out_shape=(row_block, row_block, jax.ShapeDtypeStruct((8, ROWS), BF)),
        in_specs=[VMEM] * (SD + 1),
        out_specs=(VMEM,) * 3,
        compiler_params=pltpu.CompilerParams(vmem_limit_bytes=VMEM_LIMIT),
        name="return_rows",
    )(order, *returned)

    used = jnp.any(
        positions[None, :] == (tok_index * slot_count + jnp.arange(slot_count, dtype=I32))[:, None], axis=1
    )
    owned_grad = jnp.where(used[:, None, None], total.astype(F32), 0.0)
    first_new, second_new, master_new = adam_update(
        owned_grad, master_slots, moment_one, moment_two, rate_matrix
    )
    vec_first, vec_second, vec_new = adam_update(
        vec_owned, vector_master, vector_moment_one, vector_moment_two, rate_vector
    )
    return (
        output,
        input_grad,
        owned_grad,
        first_new,
        second_new,
        master_new,
        master_new.astype(BF),
        vec_owned,
        vec_first,
        vec_second,
        vec_new,
        vec_new.astype(BF),
        entropy[0],
        occupancy,
    )


def solution(mesh):
    placed = (
        P(("rep", "tok"), None),
        P(("rep", "tok"), None),
        P(("rep", "tok")),
        P(),
        P("tok", None, None),
        P("tok", None, None),
        P("tok", None, None),
        P("tok"),
        P("tok"),
        P("tok"),
    )
    return jax.shard_map(
        local,
        mesh=mesh,
        in_specs=placed,
        out_specs=(
            P(("rep", "tok"), None),
            P(("rep", "tok"), None),
            P("tok", None, None),
            P("tok", None, None),
            P("tok", None, None),
            P("tok", None, None),
            P("tok", None, None),
            P("tok"),
            P("tok"),
            P("tok"),
            P("tok"),
            P("tok"),
            P(("rep", "tok")),
            P(),
        ),
        check_vma=False,
    )
```

```python
import functools
import math

import jax
import jax.numpy as jnp
from jax import lax
from jax.experimental import pallas as pl
from jax.experimental.pallas import tpu as pltpu
from jax.sharding import PartitionSpec as P

D = 768
HEADS = 12
HD = 64
FF = 3072
SD = 4
CL = 128
NBLK = 96
STEP = 10
CPS = 32
WROWS = 9216
BLK = 96
ROWS = 1024
PAIRS = HEADS // 2
PW = 2 * HD
TM = 512
META = 16
VMEM_LIMIT = 63 << 20
FC = 768

norm_epsilon = 1e-06
beta_first = 0.9
beta_second = 0.999
adam_epsilon = 1e-08
weight_decay = 0.01
rate_matrix = 0.02
rate_vector = 0.2

BF = jnp.bfloat16
F32 = jnp.float32
I32 = jnp.int32

VMEM = pl.BlockSpec(memory_space=pltpu.VMEM)
SMEM = pl.BlockSpec(memory_space=pltpu.SMEM)
ANY = pl.BlockSpec(memory_space=pl.ANY)

NN = (((1,), (0,)), ((), ()))
NT = (((1,), (1,)), ((), ()))
TN = (((0,), (0,)), ((), ()))


def mm(a, b, dims=NN):
    return lax.dot_general(a, b, dims, preferred_element_type=F32)


def slot_positions(block_owner, slot_count):
    owners = block_owner[:, 0]
    blocks = owners.shape[0]
    shared = owners[:, None] == owners[None, :]
    before = (
        jnp.arange(blocks, dtype=jnp.int32)[None, :] < jnp.arange(blocks, dtype=jnp.int32)[:, None]
    )
    earlier = jnp.sum((shared & before).astype(jnp.int32), axis=1)
    return owners * slot_count + earlier


def adam_update(grad_now, weight_old, first_old, second_old, rate_step):
    first_new = beta_first * first_old + (1.0 - beta_first) * grad_now
    second_new = beta_second * second_old + (1.0 - beta_second) * grad_now * grad_now
    first_hat = first_new / (1.0 - beta_first**STEP)
    second_hat = second_new / (1.0 - beta_second**STEP)
    weight_new = weight_old - rate_step * (
        first_hat / (jnp.sqrt(second_hat) + adam_epsilon) + weight_decay * weight_old
    )
    return (first_new, second_new, weight_new)


def route_slots(order, seat, cap):
    cluster = order // CL
    rel = lax.rem(cluster, SD) ^ seat
    place = (cluster // SD) * CL + lax.rem(order, CL) + 1
    chosen = lax.broadcasted_iota(I32, (8, ROWS), 0) == rel
    chosen_low = jnp.where(chosen, 1.0, 0.0).astype(BF)
    before = lax.broadcasted_iota(I32, (ROWS, ROWS), 0) < lax.broadcasted_iota(I32, (ROWS, ROWS), 1)
    before_low = jnp.where(before, 1.0, 0.0).astype(BF)
    running = mm(chosen_low, before_low)
    rank = jnp.sum(jnp.where(chosen, running, 0.0), axis=0, keepdims=True).astype(I32)
    return rel * cap + rank, place


def slot_matrix(slots, at, cap):
    rows = lax.broadcasted_iota(I32, (cap, ROWS), 0) + at * cap
    return jnp.where(rows == slots, 1.0, 0.0).astype(BF)


def send_kernel(cap, tokens, cotangent, order, send_x, send_c, meta):
    seat = lax.rem(lax.axis_index("tok"), SD)
    slots, place = route_slots(order[...], seat, cap)
    digits = jnp.concatenate([place // CL, lax.rem(place, CL)] + [place * 0] * 6, axis=0).astype(F32).astype(BF)
    for at in range(SD):
        picked = slot_matrix(slots, at, cap)
        send_x[at] = mm(picked, tokens[...]).astype(BF)
        send_c[at] = mm(picked, cotangent[...]).astype(BF)
        coded = mm(digits, picked, NT)
        line = jnp.concatenate([coded[0:1], coded[1:2]], axis=1)
        meta[at] = jnp.broadcast_to(line, (META, D)).astype(BF)


def remote(src, dst, send_sem, recv_sem, tok, rep):
    return pltpu.make_async_remote_copy(
        src_ref=src,
        dst_ref=dst,
        send_sem=send_sem,
        recv_sem=recv_sem,
        device_id={"tok": tok, "rep": rep},
        device_id_type=pl.DeviceIdType.MESH,
    )


def loop(n, body):
    def run(i, c):
        body(i)
        return c

    lax.fori_loop(0, n, run, 0)


class Place:
    def __init__(self):
        self.me = me = lax.axis_index("tok")
        self.z = z = lax.axis_index("rep")
        core, x, y = me % 2, (me // 2) % 2, me // 4
        self.twin = me + 1 - 2 * core
        self.xn = me + 2 - 4 * x
        self.yn = me + 4 - 8 * y
        self.dn = self.xn + 4 - 8 * y
        self.side = z % 2
        self.zp = z + 1 - 2 * self.side

    def twin_of(self, tok):
        return tok + 1 - 2 * (tok % 2)

    def greet(self, peers):
        barrier = pltpu.get_barrier_semaphore()
        for tok, rep in peers:
            pl.semaphore_signal(
                barrier, inc=1, device_id={"tok": tok, "rep": rep}, device_id_type=pl.DeviceIdType.MESH
            )
        return lambda: pl.semaphore_wait(barrier, len(peers))


def seat_matrix(meta, first, rows, cap):
    hi = jnp.concatenate([meta[k, 0:8, 0:cap] for k in range(SD)], axis=1).astype(F32)[0:1]
    lo = jnp.concatenate([meta[k, 0:8, cap : 2 * cap] for k in range(SD)], axis=1).astype(F32)[0:1]
    at = (hi * CL + lo).astype(I32)
    seats = lax.broadcasted_iota(I32, (rows, SD * cap), 0) + (first + 1)
    return jnp.where(seats == at, 1.0, 0.0).astype(BF)


def seat_part(meta, k, cap):
    hi = meta[k, 0:8, 0:cap].astype(F32)[0:1]
    lo = meta[k, 0:8, cap : 2 * cap].astype(F32)[0:1]
    at = (hi * CL + lo).astype(I32)
    seats = lax.broadcasted_iota(I32, (ROWS, cap), 0) + 1
    return jnp.where(seats == at, 1.0, 0.0).astype(BF)


def seat_rows(meta, blocks, cap, to):
    def body(t):
        r0 = pl.multiple_of(t * 256, 256)
        rows = blocks[...].reshape(SD * cap, D)
        to[pl.ds(r0, 256), :] = mm(seat_matrix(meta, r0, 256, cap), rows).astype(BF)

    loop(ROWS // 256, body)


def seat_kernel(cap, blocks, meta, to):
    seat_rows(meta, blocks, cap, to)


def gather_kernel(
    cap,
    count,
    tokens_h,
    cotangent_h,
    order,
    master_h,
    vector,
    owner_of,
    slots,
    x_c,
    cot_c,
    recv_meta,
    vecs,
    b_u,
    occupancy,
    positions,
    tokens,
    cotangent,
    master,
    own,
    send_x,
    send_c,
    meta,
    recv_x,
    recv_c,
    got_meta,
    mine,
    by_z,
    by_tok,
    x_s,
    x_r,
    y_s,
    y_r,
    d_s,
    d_r,
    zx_s,
    zx_r,
    zd_s,
    zd_r,
    p_s,
    p_r,
    row_s,
    row_r,
    z_s,
    z_r,
    t_s,
    t_r,
    local_s,
):
    at = Place()
    me, z, side = at.me, at.z, at.side
    n_tok, n_rep = 8, 4
    peers = [((me + d) % n_tok, z) for d in range(1, n_tok)] + [(me, (z + d) % n_rep) for d in range(1, n_rep)]
    fetch = [
        pltpu.make_async_copy(src, dst, local_s.at[i])
        for i, (src, dst) in enumerate(((master_h, master), (tokens_h, tokens), (cotangent_h, cotangent)))
    ]
    for copy in fetch:
        copy.start()
    wait_peers = at.greet(peers)
    fetch[0].wait()

    def cast(s):
        own[s] = master[s].astype(BF)

    loop(count, cast)
    wait_peers()

    half = count // 2

    def slot(owner, s):
        return slots.at[owner * count + s]

    def to_x(s):
        return remote(own.at[s], slot(me, s), x_s.at[s], x_r.at[s], at.xn, z)

    def to_y(s):
        return remote(own.at[s], slot(me, s), y_s.at[s], y_r.at[s], at.yn, z)

    def on_y(s):
        return remote(slot(at.xn, s), slot(at.xn, s), d_s.at[s], d_r.at[s], at.yn, z)

    def x_on_z(s):
        return remote(slot(at.xn, s), slot(at.xn, s), zx_s.at[s], zx_r.at[s], me, at.zp)

    def d_on_z(s):
        return remote(slot(at.dn, s), slot(at.dn, s), zd_s.at[s], zd_r.at[s], me, at.zp)

    owners = (me, at.xn, at.yn, at.dn)

    def to_twin(q, s):
        src = own.at[s] if q == 0 else slot(owners[q], s)
        return remote(src, slot(owners[q], s), p_s.at[q, s], p_r.at[q, s], at.twin, z)

    def near(j):
        return (half + 1) * side + j

    def far(j):
        return (half + 1) * (1 - side) + j

    loop(half, lambda j: to_x(near(j)).start())
    to_x(half).start()
    for s in range(3):
        to_y(s).start()
    loop(count, lambda s: to_twin(0, s).start())
    keep = pltpu.make_async_copy(own, slots.at[pl.ds(me * count, count)], local_s.at[3])
    keep.start()
    fetch[1].wait()
    fetch[2].wait()

    seat = me % SD
    slot_of, place = route_slots(order[...], seat, cap)
    digits = jnp.concatenate([place // CL, lax.rem(place, CL)] + [place * 0] * 6, axis=0).astype(F32).astype(BF)
    for k in range(SD):
        picked = slot_matrix(slot_of, k, cap)
        send_x[k] = mm(picked, tokens[...]).astype(BF)
        send_c[k] = mm(picked, cotangent[...]).astype(BF)
        coded = mm(digits, picked, NT)
        line = jnp.concatenate([coded[0:1], coded[1:2]], axis=1)
        meta[k] = jnp.broadcast_to(line, (META, D)).astype(BF)
    seats = (me, at.twin, at.xn, at.twin_of(at.xn))
    rows_of = ((meta, got_meta), (send_x, recv_x), (send_c, recv_c))

    def row_copy(i, k):
        src, dst = rows_of[i]
        return remote(src.at[k], dst.at[k], row_s.at[i, k], row_r.at[i, k], seats[k], z)

    for i in range(3):
        src, dst = rows_of[i]
        for k in (2, 3, 1):
            row_copy(i, k).start()
        dst[0] = src[0]

    residue = lax.rem(me // SD * CPS + order[...] // CL, n_tok)
    hit = lax.broadcasted_iota(I32, (128, ROWS), 0) == residue
    for i in range(9):
        mine[i : i + 1] = vector[i * 128 : (i + 1) * 128].reshape(1, 128).astype(BF).astype(F32)
    block_row = lax.broadcasted_iota(I32, (NBLK, NBLK), 0)
    block_col = lax.broadcasted_iota(I32, (NBLK, NBLK), 1)
    by_col = owner_of[...].astype(F32)
    by_row = lane_sum(jnp.where(block_row == block_col, by_col, 0.0))
    earlier = jnp.where((by_row == by_col) & (block_row < block_col), 1.0, 0.0)
    positions[...] = (by_col * count + jnp.sum(earlier, axis=0, keepdims=True)).astype(I32)
    by_z[0] = mm(jnp.ones((8, ROWS), BF), jnp.where(hit, 1.0, 0.0).astype(BF), NT)

    def z_copy(d):
        return remote(by_z.at[0], by_z.at[d], z_s.at[d], z_r.at[d], me, (z + d) % n_rep)

    def t_copy(d):
        return remote(mine, by_tok.at[d], t_s.at[d], t_r.at[d], (me + d) % n_tok, z)

    for d in range(1, n_rep):
        z_copy(d).start()
    for d in range(1, n_rep):
        z_copy(d).wait()
    mine[16:24] = by_z[0] + by_z[1] + by_z[2] + by_z[3]
    for d in range(1, n_tok):
        t_copy(d).start()

    def x_here(s):
        to_x_in(s).wait_recv()
        on_y(s).start()
        to_twin(1, s).start()

    def to_x_in(s):
        return remote(own.at[s], slot(at.xn, s), x_s.at[s], x_r.at[s], at.xn, z)

    def y_in(s):
        return remote(own.at[s], slot(at.yn, s), y_s.at[s], y_r.at[s], at.yn, z)

    def d_in(s):
        return remote(own.at[s], slot(at.dn, s), d_s.at[s], d_r.at[s], at.yn, z)

    def first(j):
        x_here(near(j))
        x_on_z(near(j)).start()
        to_y(3 + j).start()

    loop(half, first)
    x_here(half)
    for s in range(3 + half, count):
        to_y(s).start()

    def y_here(s):
        y_in(s).wait_recv()
        to_twin(2, s).start()

    def second(j):
        x_on_z(far(j)).wait_recv()
        to_twin(1, far(j)).start()
        y_here(j)
        d_in(near(j)).wait_recv()
        d_on_z(near(j)).start()
        to_twin(3, near(j)).start()

    loop(half, second)
    d_in(half).wait_recv()
    to_twin(3, half).start()
    loop(count - half, lambda j: y_here(half + j))
    for i in (0, 1):
        for k in (2, 3, 1):
            row_copy(i, k).wait_recv()
    recv_meta[...] = got_meta[...]
    seat_rows(got_meta, recv_x, cap, x_c)

    def third(j):
        d_on_z(far(j)).wait_recv()
        to_twin(3, far(j)).start()

    loop(half, third)

    by_tok[0] = mine[...]
    for d in range(1, n_tok):
        t_copy(d).wait()
    for owner in range(n_tok):
        share = by_tok[(me + n_tok - owner) % n_tok]
        occupancy[owner : owner + 1, :] = share[16:17, 0:n_tok].astype(I32)
        for i in range(9):
            chunk = owner * 9 + i
            row, lane = chunk // 6, chunk % 6 * 128
            if row < 8:
                vecs[row : row + 1, lane : lane + 128] = share[i : i + 1]
            else:
                lane += (row - 8) * D
                b_u[:, lane : lane + 128] = share[i : i + 1]
    for k in (2, 3, 1):
        row_copy(2, k).wait_recv()
    seat_rows(got_meta, recv_c, cap, cot_c)
    for i in range(3):
        for k in (2, 3, 1):
            row_copy(i, k).wait_send()
    keep.wait()

    def sent_half(j):
        to_x(near(j)).wait_send()
        on_y(near(j)).wait_send()
        x_on_z(near(j)).wait_send()
        d_on_z(near(j)).wait_send()

    loop(half, sent_half)
    to_x(half).wait_send()
    on_y(half).wait_send()

    def sent(s):
        to_y(s).wait_send()
        for q in range(4):
            to_twin(q, s).wait()

    loop(count, sent)


def gather_all(cap, tokens, cotangent, order, master, vector, block_owner):
    count = master.shape[0]
    rows = jax.ShapeDtypeStruct((ROWS, D), BF)
    dma = pltpu.SemaphoreType.DMA
    block = pltpu.VMEM((SD, cap, D), BF)
    meta = pltpu.VMEM((SD, META, D), BF)
    return pl.pallas_call(
        functools.partial(gather_kernel, cap, count),
        out_shape=(
            jax.ShapeDtypeStruct((8 * count, BLK, D), BF),
            rows,
            rows,
            jax.ShapeDtypeStruct((SD, META, D), BF),
            jax.ShapeDtypeStruct((8, D), F32),
            jax.ShapeDtypeStruct((1, FF), F32),
            jax.ShapeDtypeStruct((8, 8), I32),
            jax.ShapeDtypeStruct((1, NBLK), I32),
        ),
        in_specs=[ANY, ANY, VMEM, ANY, VMEM, VMEM],
        out_specs=(ANY,) + (VMEM,) * 7,
        scratch_shapes=[
            pltpu.VMEM((ROWS, D), BF),
            pltpu.VMEM((ROWS, D), BF),
            pltpu.VMEM((count, BLK, D), F32),
            pltpu.VMEM((count, BLK, D), BF),
            block,
            block,
            meta,
            block,
            block,
            meta,
            pltpu.VMEM((24, 128), F32),
            pltpu.VMEM((4, 8, 128), F32),
            pltpu.VMEM((8, 24, 128), F32),
        ]
        + [dma((count,))] * 10
        + [dma((4, count))] * 2
        + [dma((3, SD))] * 2
        + [dma((4,))] * 2
        + [dma((8,))] * 2
        + [dma((4,))],
        compiler_params=pltpu.CompilerParams(collective_id=0, has_side_effects=True, vmem_limit_bytes=VMEM_LIMIT),
        name="gather",
    )(tokens, cotangent, order, master, vector, block_owner.reshape(1, NBLK))


def return_kernel(cap, order, *refs):
    blocks, (out, ing, entropy) = refs[:SD], refs[SD:]
    seat = lax.rem(lax.axis_index("tok"), SD)
    slots, _ = route_slots(order[...], seat, cap)
    picked = jnp.concatenate([slot_matrix(slots, at, cap) for at in range(SD)], axis=0)
    for to, first in ((out, 0), (ing, cap)):
        rows = jnp.concatenate([block[first : first + cap, :] for block in blocks], axis=0)
        to[...] = mm(picked, rows, TN).astype(BF)
    line = jnp.concatenate([block[2 * cap : 2 * cap + 8, 0:cap] for block in blocks], axis=1)
    entropy[...] = mm(line, picked)[0:1].astype(BF)


def swap_blocks(blocks):
    n = lax.axis_size("tok")
    parts = [blocks[0]]
    for k in range(1, SD):
        parts.append(lax.ppermute(blocks[k], "tok", [(i, i ^ k) for i in range(n)]))
    return parts


def reduce_kernel(
    count,
    split,
    grads,
    vec,
    total,
    vec_out,
    a,
    tw,
    rd,
    rx,
    ry,
    o,
    rz1,
    pz,
    rz2,
    fz,
    vt,
    va,
    vb,
    vc,
    a_l,
    keep_l,
    p_s,
    p_r,
    d_s,
    d_r,
    x_s,
    x_r,
    y_s,
    y_r,
    z1_s,
    z1_r,
    z2_s,
    z2_r,
    z3_s,
    z3_r,
    t_s,
    t_r,
    v_s,
    v_r,
):
    at = Place()
    me, z = at.me, at.z
    n_tok, n_rep = 8, 4
    peers = [((me + d) % n_tok, z) for d in range(1, n_tok)] + [(me, (z + d) % n_rep) for d in range(1, n_rep)]
    wait_peers = at.greet(peers)
    owners = (me, at.xn, at.yn, at.dn)

    def load(q):
        return pltpu.make_async_copy(grads.at[pl.ds(owners[q] * count, count)], a.at[q], a_l.at[q])

    for q in (3, 1, 2, 0):
        load(q).start()
    wait_peers()

    def to_twin(q, s):
        src = grads.at[at.twin_of(owners[q]) * count + s]
        return remote(src, tw.at[q, s], p_s.at[q, s], p_r.at[q, s], at.twin, z)

    def d_y(s):
        return remote(a.at[3, s], rd.at[s], d_s.at[s], d_r.at[s], at.yn, z)

    def d_x(s):
        return remote(a.at[3, s], rd.at[s], d_s.at[s], d_r.at[s], at.xn, z)

    def to_x(s):
        return remote(a.at[1, s], rx.at[s], x_s.at[s], x_r.at[s], at.xn, z)

    def to_y(s):
        return remote(a.at[2, s], ry.at[s], y_s.at[s], y_r.at[s], at.yn, z)

    def z_in(s):
        return remote(o.at[s], rz1.at[s], z1_s.at[s], z1_r.at[s], me, at.zp)

    def z_swap(s):
        return remote(pz.at[s], rz2.at[s], z2_s.at[s], z2_r.at[s], me, n_rep - 1 - z)

    def z_out(s):
        return remote(fz.at[s], fz.at[s], z3_s.at[s], z3_r.at[s], me, at.zp)

    def keep(s):
        return pltpu.make_async_copy(fz.at[s], total.at[s], keep_l.at[s])

    def f32(ref, *index):
        return ref[index].astype(F32)

    loop(count, lambda s: to_twin(3, s).start())

    def others(s):
        for q in (2, 1, 0):
            to_twin(q, s).start()

    loop(count, others)

    def v_tok(d):
        return remote(vec.at[(me + d) % n_tok], vt.at[d], t_s.at[d], t_r.at[d], (me + d) % n_tok, z)

    def v_rep(i, src):
        return remote(src, vb.at[i], v_s.at[i], v_r.at[i], me, at.zp if i == 0 else (z + 2) % n_rep)

    for d in range(1, n_tok):
        v_tok(d).start()

    load(3).wait()

    def join(q, s):
        to_twin(q, s).wait_recv()
        return f32(a, q, s) + f32(tw, q, s)

    def diagonal(s, send):
        a[3, s] = join(3, s).astype(BF)
        send(s).start()

    loop(split, lambda s: diagonal(s, d_y))
    loop(count - split, lambda j: diagonal(split + j, d_x))

    v_sum = vec[me]
    for d in range(1, n_tok):
        v_tok(d).wait()
        v_sum = v_sum + vt[d]
    va[...] = v_sum
    v_rep(0, va).start()

    load(1).wait()
    load(2).wait()

    def plane_y(s):
        a[2, s] = join(2, s).astype(BF)
        to_y(s).start()
        d_y(s).wait_recv()
        a[1, s] = (join(1, s) + f32(rd, s)).astype(BF)
        to_x(s).start()

    def plane_x(s):
        a[1, s] = join(1, s).astype(BF)
        to_x(s).start()
        d_x(s).wait_recv()
        a[2, s] = (join(2, s) + f32(rd, s)).astype(BF)
        to_y(s).start()

    loop(count - split, lambda j: plane_x(split + j))
    loop(split, plane_y)

    v_rep(0, va).wait()
    vc[...] = va[...] + vb[0]
    v_rep(1, vc).start()
    load(0).wait()
    inner = (z == 1) | (z == 2)
    outer = (z == 0) | (z == 3)

    def turn(i):
        return (i + split) % count

    def planes(i):
        @pl.when(i < count)
        def _():
            s = turn(i)
            to_x(s).wait_recv()
            to_y(s).wait_recv()
            o[s] = (join(0, s) + f32(rx, s) + f32(ry, s)).astype(BF)

        @pl.when(outer & (i < count))
        def _():
            z_in(turn(i)).start()

        @pl.when(inner & (i >= 1) & (i < count + 1))
        def _():
            s = turn(i - 1)
            z_in(s).wait_recv()
            pz[s] = (f32(o, s) + f32(rz1, s)).astype(BF)
            z_swap(s).start()

        @pl.when(inner & (i >= 2) & (i < count + 2))
        def _():
            s = turn(i - 2)
            z_swap(s).wait_recv()
            fz[s] = (f32(pz, s) + f32(rz2, s)).astype(BF)
            z_out(s).start()
            keep(s).start()

        @pl.when(outer & (i >= 3))
        def _():
            s = turn(i - 3)
            z_out(s).wait_recv()
            keep(s).start()

    loop(count + 3, planes)
    v_rep(1, vc).wait()
    vec_out[...] = vc[...] + vb[1]

    def sent(s):
        for q in range(4):
            to_twin(q, s).wait_send()
        d_y(s).wait_send()
        to_x(s).wait_send()
        to_y(s).wait_send()
        keep(s).wait()

    loop(count, sent)

    @pl.when(outer)
    def _():
        loop(count, lambda s: z_in(s).wait_send())

    @pl.when(inner)
    def _():
        def back(s):
            z_swap(s).wait_send()
            z_out(s).wait_send()

        loop(count, back)


def reduce_all(grads, shares, count):
    dma = pltpu.SemaphoreType.DMA
    part = pltpu.VMEM((count, BLK, D), BF)
    whole = pltpu.VMEM((4, count, BLK, D), BF)
    line = pltpu.VMEM((16, 128), F32)
    total, vec = pl.pallas_call(
        functools.partial(reduce_kernel, count, count - count // 4),
        out_shape=(
            jax.ShapeDtypeStruct((count, BLK, D), BF),
            jax.ShapeDtypeStruct((16, 128), F32),
        ),
        in_specs=[ANY, VMEM],
        out_specs=(ANY, VMEM),
        scratch_shapes=[whole, whole]
        + [part] * 8
        + [pltpu.VMEM((8, 16, 128), F32), line, pltpu.VMEM((2, 16, 128), F32), line]
        + [dma((4,)), dma((count,))]
        + [dma((4, count))] * 2
        + [dma((count,))] * 12
        + [dma((8,))] * 2
        + [dma((2,))] * 2,
        compiler_params=pltpu.CompilerParams(
            collective_id=1, has_side_effects=True, vmem_limit_bytes=VMEM_LIMIT
        ),
        name="reduce",
    )(grads, shares)
    return total, vec[0:9].reshape(-1)


V_BQ, V_BV, V_BO, V_BD, V_G1, V_C1, V_G2, V_C2 = range(8)


def erf_parts(v):
    z = jnp.abs(v) * (1.0 / math.sqrt(2.0))
    t = 1.0 / (1.0 + 0.3275911 * z)
    e = jnp.exp(-z * z)
    poly = 0.5 * 1.061405429
    for c in (-1.453152027, 1.421413741, -0.284496736, 0.254829592):
        poly = poly * t + 0.5 * c
    tail = poly * t * e
    return jnp.where(v >= 0.0, 1.0 - tail, tail), e


def lane_sum(x):
    return jnp.sum(x, axis=1, keepdims=True)


def gelu_parts(v):
    phi, e = erf_parts(v)
    return v * phi, phi + v * (e * (1.0 / math.sqrt(2.0 * math.pi)))


def chain_kernel(
    cap,
    pos,
    slots,
    vecs,
    b_u,
    x_h,
    cot_h,
    meta,
    back_0,
    back_1,
    back_2,
    back_3,
    shares,
    heads_h,
    act_h,
    d_up_h,
    d_q_h,
    d_k_h,
    d_v_h,
    d_proj_h,
    hid_h,
    d_br_h,
    w,
    x_c,
    heads,
    act,
    d_up,
    d_q,
    d_k,
    d_v,
    d_proj,
    hid,
    d_br,
    out_c,
    ing_c,
    ent,
    gvec,
    g_bu,
    q_t,
    k_t,
    v_t,
    p_t,
    dh_t,
    n1_t,
    hid_t,
    w_sem,
    x_sem,
    o_sem,
):
    inv = 1.0 / math.sqrt(HD)

    def w_copy(b):
        return pltpu.make_async_copy(slots.at[pos[b]], w.at[pl.ds(b * BLK, BLK)], w_sem)

    get_x = pltpu.make_async_copy(x_h, x_c, x_sem.at[0])
    get_cot = pltpu.make_async_copy(cot_h, d_br, x_sem.at[1])
    get_x.start()
    loop(NBLK, lambda b: w_copy(b).start())
    get_cot.start()
    gvec[...] = jnp.zeros_like(gvec)
    g_bu[...] = jnp.zeros_like(g_bu)
    shares[...] = jnp.zeros_like(shares)
    get_x.wait()
    loop(NBLK, lambda b: w_copy(b).wait())
    get_cot.wait()

    wq, wk, wv, wo = (w.at[pl.ds(i * D, D)] for i in range(4))
    wu = w.at[pl.ds(4 * D, FF)]
    wd = w.at[pl.ds(4 * D + FF, FF)]

    lane = lax.broadcasted_iota(I32, (1, PW), 1)
    m0 = jnp.where(lane < HD, 1.0, 0.0).astype(BF)
    m1 = jnp.where(lane < HD, 0.0, 1.0).astype(BF)
    first_half = lax.broadcasted_iota(I32, (CL, PW), 1) < HD

    def apart(pair):
        return jnp.concatenate([pair * m0, pair * m1], axis=0)

    def vec(i):
        return vecs[i : i + 1, :]

    def add_vec(i, value):
        gvec[i : i + 1, :] += jnp.sum(value, axis=0, keepdims=True)

    saved = (
        (heads, heads_h),
        (act, act_h),
        (d_up, d_up_h),
        (d_q, d_q_h),
        (d_k, d_k_h),
        (d_v, d_v_h),
        (d_proj, d_proj_h),
        (hid, hid_h),
        (d_br, d_br_h),
    )

    def save(t, i):
        rows = pl.ds(pl.multiple_of(t * TM, TM), TM)
        src, dst = saved[i]
        return pltpu.make_async_copy(src.at[rows], dst.at[rows], o_sem.at[i])

    def tile(t):
        r0 = pl.multiple_of(t * TM, TM)
        rows = pl.ds(r0, TM)
        q_t[...] = ((mm(x_c[rows, :], wq[...]) + vec(V_BQ)).astype(BF).astype(F32) * inv).astype(BF)
        k_t[...] = mm(x_c[rows, :], wk[...]).astype(BF)
        v_t[...] = (mm(x_c[rows, :], wv[...]) + vec(V_BV)).astype(BF)

        def attend(c):
            cr = pl.ds(pl.multiple_of(c * CL, CL), CL)
            gr = pl.ds(pl.multiple_of(r0 + c * CL, CL), CL)
            total = jnp.zeros((1, CL), F32)
            for p in range(PAIRS):
                ps = slice(p * PW, (p + 1) * PW)
                scores = mm(apart(k_t[cr, ps]), q_t[cr, ps], NT)
                halves = []
                for h in range(2):
                    sh = scores[h * CL : (h + 1) * CL]
                    sh = sh - jnp.max(sh, axis=0, keepdims=True)
                    e = jnp.exp(sh)
                    tot = jnp.sum(e, axis=0, keepdims=True)
                    r = 1.0 / tot
                    total += jnp.log(tot) - jnp.sum(e * sh, axis=0, keepdims=True) * r
                    halves.append((e * r).astype(BF))
                weights = jnp.concatenate(halves, axis=0)
                p_t[c, p] = weights
                heads[gr, ps] = mm(weights, apart(v_t[cr, ps]), TN).astype(BF)
            ent[:, gr] = jnp.broadcast_to(total * (1.0 / HEADS), (8, CL))

        loop(TM // CL, attend)

        r1 = x_c[rows, :].astype(F32) + mm(heads[rows, :], wo[...]) + vec(V_BO)
        c1 = r1 - lane_sum(r1) * (1.0 / D)
        rs1 = lax.rsqrt(lane_sum(c1 * c1) * (1.0 / D) + norm_epsilon)
        n1 = c1 * rs1
        hidden = n1 * vec(V_G1) + vec(V_C1)
        hid[rows, :] = hidden.astype(BF)
        n1_t[...] = n1
        hid_t[...] = hidden

        def widen(f):
            fs = pl.ds(pl.multiple_of(f * FC, FC), FC)
            g, g_slope = gelu_parts(mm(hid[rows, :], wu[fs, :], NT) + b_u[:, fs])
            act[rows, fs] = g.astype(BF)
            d_up[rows, fs] = g_slope.astype(BF)

        loop(FF // FC, widen)
        r2 = hid_t[...] + mm(act[rows, :], wd[...]) + vec(V_BD)
        c2 = r2 - lane_sum(r2) * (1.0 / D)
        rs2 = lax.rsqrt(lane_sum(c2 * c2) * (1.0 / D) + norm_epsilon)
        n2 = c2 * rs2
        out_c[rows, :] = (n2 * vec(V_G2) + vec(V_C2)).astype(BF)

        e2 = d_br[rows, :].astype(F32)
        add_vec(V_G2, e2 * n2)
        add_vec(V_C2, e2)
        eg = e2 * vec(V_G2)
        d_r2 = rs2 * (eg - lane_sum(eg) * (1.0 / D) - n2 * (lane_sum(eg * n2) * (1.0 / D)))
        d_br[rows, :] = d_r2.astype(BF)
        add_vec(V_BD, d_br[rows, :].astype(F32))
        hid_t[...] = d_r2

        def widen_back(f):
            fs = pl.ds(pl.multiple_of(f * FC, FC), FC)
            du = (mm(d_br[rows, :], wd[fs, :], NT) * d_up[rows, fs].astype(F32)).astype(BF)
            d_up[rows, fs] = du
            g_bu[:, fs] += jnp.sum(du.astype(F32), axis=0, keepdims=True)

        loop(FF // FC, widen_back)
        n1 = n1_t[...]
        d_h = hid_t[...] + mm(d_up[rows, :], wu[...])
        add_vec(V_G1, d_h * n1)
        add_vec(V_C1, d_h)
        eg = d_h * vec(V_G1)
        d_r1 = rs1 * (eg - lane_sum(eg) * (1.0 / D) - n1 * (lane_sum(eg * n1) * (1.0 / D)))
        d_proj[rows, :] = d_r1.astype(BF)
        hid_t[...] = d_r1
        add_vec(V_BO, d_proj[rows, :].astype(F32))
        dh_t[...] = mm(d_proj[rows, :], wo[...], NT).astype(BF)

        def attend_back(c):
            cr = pl.ds(pl.multiple_of(c * CL, CL), CL)
            gr = pl.ds(pl.multiple_of(r0 + c * CL, CL), CL)
            for p in range(PAIRS):
                ps = slice(p * PW, (p + 1) * PW)
                dh = dh_t[cr, ps]
                weights = p_t[c, p]
                d_w = mm(apart(v_t[cr, ps]), dh, NT)
                halves = []
                for h in range(2):
                    wh = weights[h * CL : (h + 1) * CL].astype(F32)
                    dwh = d_w[h * CL : (h + 1) * CL]
                    halves.append((wh * (dwh - jnp.sum(dwh * wh, axis=0, keepdims=True))).astype(BF))
                d_s = jnp.concatenate(halves, axis=0)
                d_q[gr, ps] = (mm(d_s, apart(k_t[cr, ps]), TN) * inv).astype(BF)
                dk = mm(d_s, q_t[cr, ps])
                d_k[gr, ps] = jnp.where(first_half, dk[0:CL], dk[CL:]).astype(BF)
                dv = mm(weights, dh)
                d_v[gr, ps] = jnp.where(first_half, dv[0:CL], dv[CL:]).astype(BF)

        loop(TM // CL, attend_back)
        add_vec(V_BQ, d_q[rows, :].astype(F32))
        add_vec(V_BV, d_v[rows, :].astype(F32))
        d_x = mm(d_q[rows, :], wq[...], NT) + mm(d_k[rows, :], wk[...], NT) + mm(d_v[rows, :], wv[...], NT)
        ing_c[rows, :] = (hid_t[...] + d_x.astype(BF).astype(F32)).astype(BF)
        for i in range(len(saved)):
            save(t, i).start()

    loop(ROWS // TM, tile)

    for k, back in enumerate((back_0, back_1, back_2, back_3)):
        own = seat_part(meta, k, cap)
        back[0:cap, :] = mm(own, out_c[...], TN).astype(BF)
        back[cap : 2 * cap, :] = mm(own, ing_c[...], TN).astype(BF)
        line = mm(ent[...].astype(BF), own)
        back[2 * cap :, :] = jnp.concatenate([line, line], axis=1)[0:1].astype(BF) * jnp.ones((META, 1), BF)

    for chunk in range(72):
        row, lane = chunk // 6, chunk % 6 * 128
        if row < 8:
            part = gvec[row : row + 1, lane : lane + 128]
        else:
            lane += (row - 8) * D
            part = g_bu[:, lane : lane + 128]
        shares[chunk // 9, chunk % 9 : chunk % 9 + 1, :] = part

    def saved_all(t):
        for i in range(len(saved)):
            save(t, i).wait()

    loop(ROWS // TM, saved_all)


def chain(cap, positions, slots, vecs, b_u, x_c, cot_c, meta):
    rows = jax.ShapeDtypeStruct((ROWS, D), BF)
    wide = jax.ShapeDtypeStruct((ROWS, FF), BF)
    back = jax.ShapeDtypeStruct((2 * cap + META, D), BF)
    r_v, w_v, t_v, t_f = (pltpu.VMEM(shape, kind) for shape, kind in (
        ((ROWS, D), BF), ((ROWS, FF), BF), ((TM, D), BF), ((TM, D), F32)
    ))
    return pl.pallas_call(
        functools.partial(chain_kernel, cap),
        out_shape=(back,) * SD + (jax.ShapeDtypeStruct((8, 16, 128), F32), rows, wide, wide) + (rows,) * 6,
        in_specs=[SMEM, ANY, VMEM, VMEM, ANY, ANY, VMEM],
        out_specs=(VMEM,) * (SD + 1) + (ANY,) * 9,
        scratch_shapes=[
            pltpu.VMEM((WROWS, D), BF),
            r_v,
            r_v,
            w_v,
            w_v,
            r_v,
            r_v,
            r_v,
            r_v,
            r_v,
            r_v,
            r_v,
            r_v,
            pltpu.VMEM((8, ROWS), F32),
            pltpu.VMEM((8, D), F32),
            pltpu.VMEM((1, FF), F32),
            t_v,
            t_v,
            t_v,
            pltpu.VMEM((TM // CL, PAIRS, 2 * CL, CL), BF),
            t_v,
            t_f,
            t_f,
            pltpu.SemaphoreType.DMA,
            pltpu.SemaphoreType.DMA((2,)),
            pltpu.SemaphoreType.DMA((9,)),
        ],
        compiler_params=pltpu.CompilerParams(vmem_limit_bytes=VMEM_LIMIT),
        name="layer",
    )(positions, slots, vecs, b_u, x_c, cot_c, meta)


WC = 8 * BLK


def weight_kernel(
    pos,
    x_h,
    heads_h,
    act_h,
    d_up_h,
    d_q_h,
    d_k_h,
    d_v_h,
    d_proj_h,
    hid_h,
    d_br_h,
    grads,
    x_c,
    heads,
    act,
    d_up,
    d_q,
    d_k,
    d_v,
    d_proj,
    hid,
    d_br,
    stage,
    i_sem,
    g_sem,
):
    refs = (
        (x_h, x_c),
        (d_q_h, d_q),
        (d_k_h, d_k),
        (d_v_h, d_v),
        (heads_h, heads),
        (d_proj_h, d_proj),
        (hid_h, hid),
        (d_up_h, d_up),
        (d_br_h, d_br),
        (act_h, act),
    )
    fetch = [pltpu.make_async_copy(src, dst, i_sem.at[i]) for i, (src, dst) in enumerate(refs)]
    for copy in fetch:
        copy.start()

    per = WC // BLK

    def g_copy(chunk, j, at):
        return pltpu.make_async_copy(
            stage.at[at, pl.ds(j * BLK, BLK)], grads.at[pos[chunk * per + j]], g_sem.at[at]
        )

    def put(chunk, left, right):
        at = lax.rem(chunk, 2)

        @pl.when(chunk >= 2)
        def _():
            for j in range(per):
                g_copy(chunk - 2, j, at).wait()

        stage[at] = mm(left, right, TN).astype(BF)
        for j in range(per):
            g_copy(chunk, j, at).start()

    first = 0
    for left, right, needs in (
        (x_c, d_q, (0, 1)),
        (x_c, d_k, (2,)),
        (x_c, d_v, (3,)),
        (heads, d_proj, (4, 5)),
        (d_up, hid, (6, 7)),
        (act, d_br, (8, 9)),
    ):
        for i in needs:
            fetch[i].wait()

        def body(j, left=left, right=right, first=first):
            put(first + j, left[:, pl.ds(pl.multiple_of(j * WC, WC), WC)], right[...])

        loop(left.shape[1] // WC, body)
        first += left.shape[1] // WC
    for chunk in (first - 2, first - 1):
        for j in range(per):
            g_copy(chunk, j, chunk % 2).wait()


def weight_grads_of(total_slots, positions, x_c, saved):
    r_v, w_v = pltpu.VMEM((ROWS, D), BF), pltpu.VMEM((ROWS, FF), BF)
    return pl.pallas_call(
        weight_kernel,
        out_shape=jax.ShapeDtypeStruct((total_slots, BLK, D), BF),
        in_specs=[SMEM] + [ANY] * 10,
        out_specs=ANY,
        scratch_shapes=[r_v, r_v, w_v, w_v]
        + [r_v] * 6
        + [
            pltpu.VMEM((2, WC, D), BF),
            pltpu.SemaphoreType.DMA((10,)),
            pltpu.SemaphoreType.DMA((2,)),
        ],
        compiler_params=pltpu.CompilerParams(vmem_limit_bytes=VMEM_LIMIT),
        cost_estimate=pl.CostEstimate(flops=2 * ROWS * WROWS * D, bytes_accessed=40 << 20, transcendentals=0),
        name="weight_grads",
    )(positions, x_c, *saved)


def local(
    tokens,
    cotangent,
    cluster_order,
    block_owner,
    master_slots,
    moment_one,
    moment_two,
    vector_master,
    vector_moment_one,
    vector_moment_two,
):
    tok_count = lax.axis_size("tok")
    tok_index = lax.axis_index("tok")
    slot_count = master_slots.shape[0]
    cap = tok_count // SD * (max(1, CPS // tok_count) * 3 * CL // (2 * SD))
    total_slots = tok_count * slot_count
    order = cluster_order.reshape(1, ROWS)

    block = jax.ShapeDtypeStruct((SD, cap, D), BF)
    meta_shape = jax.ShapeDtypeStruct((SD, META, D), BF)
    row_block = jax.ShapeDtypeStruct((ROWS, D), BF)
    four_planes = tok_count == 8 and lax.axis_size("rep") == 4
    if four_planes:
        slots_low, x_c, cot_c, recv_meta, vecs, b_u, occupancy, positions = gather_all(
            cap, tokens, cotangent, order, master_slots, vector_master, block_owner
        )
        positions = positions.reshape(NBLK)
    else:
        positions = slot_positions(block_owner, slot_count)
        slots_low = lax.all_gather(master_slots.astype(BF), "tok", axis=0, tiled=True)
        vectors = lax.all_gather(vector_master.astype(BF), "tok", axis=0, tiled=True).astype(F32)
        vecs, b_u = vectors[: 8 * D].reshape(8, D), vectors[8 * D :].reshape(1, FF)
        cluster = tok_index // SD * CPS + cluster_order // CL
        target = cluster % tok_count
        chosen = target[None, :] == jnp.arange(tok_count, dtype=jnp.int32)[:, None]
        sent_counts = jnp.sum(chosen.astype(F32), axis=1)
        own_row = (jnp.arange(tok_count, dtype=jnp.int32) == tok_index).astype(F32)
        occupancy = lax.psum(own_row[:, None] * sent_counts[None, :], ("tok", "rep")).astype(jnp.int32)
        send_x, send_c, meta = pl.pallas_call(
            functools.partial(send_kernel, cap),
            out_shape=(block, block, meta_shape),
            in_specs=[VMEM] * 3,
            out_specs=(VMEM,) * 3,
            compiler_params=pltpu.CompilerParams(vmem_limit_bytes=VMEM_LIMIT),
            name="send_rows",
        )(tokens, cotangent, order)
        recv_x, recv_c, recv_meta = (jnp.stack(swap_blocks(b)) for b in (send_x, send_c, meta))
        x_c, cot_c = (
            pl.pallas_call(
                functools.partial(seat_kernel, cap),
                out_shape=row_block,
                in_specs=[VMEM] * 2,
                out_specs=VMEM,
                compiler_params=pltpu.CompilerParams(vmem_limit_bytes=VMEM_LIMIT),
                name="seat_rows",
            )(rows, recv_meta)
            for rows in (recv_x, recv_c)
        )

    *backs, shares, heads, act, d_up, d_q, d_k, d_v, d_proj, hid, d_br = chain(
        cap, positions, slots_low, vecs, b_u, x_c, cot_c, recv_meta
    )
    returned = swap_blocks(backs)
    grads = weight_grads_of(
        total_slots, positions, x_c, (heads, act, d_up, d_q, d_k, d_v, d_proj, hid, d_br)
    )
    if four_planes:
        total, vec_owned = reduce_all(grads, shares, slot_count)
    else:
        total = lax.psum(lax.psum_scatter(grads, "tok", scatter_dimension=0, tiled=True), "rep")
        grad_vector = shares[:, 0:9].reshape(-1)
        vec_owned = lax.psum(lax.psum_scatter(grad_vector, "tok", scatter_dimension=0, tiled=True), "rep")
    output, input_grad, entropy = pl.pallas_call(
        functools.partial(return_kernel, cap),
        out_shape=(row_block, row_block, jax.ShapeDtypeStruct((1, ROWS), BF)),
        in_specs=[VMEM] * (SD + 1),
        out_specs=(VMEM,) * 3,
        compiler_params=pltpu.CompilerParams(vmem_limit_bytes=VMEM_LIMIT),
        name="return_rows",
    )(order, *returned)

    used = jnp.any(
        positions[None, :] == (tok_index * slot_count + jnp.arange(slot_count, dtype=I32))[:, None], axis=1
    )
    owned_grad = jnp.where(used[:, None, None], total.astype(F32), 0.0)
    first_new, second_new, master_new = adam_update(
        owned_grad, master_slots, moment_one, moment_two, rate_matrix
    )
    vec_first, vec_second, vec_new = adam_update(
        vec_owned, vector_master, vector_moment_one, vector_moment_two, rate_vector
    )
    return (
        output,
        input_grad,
        owned_grad,
        first_new,
        second_new,
        master_new,
        master_new.astype(BF),
        vec_owned,
        vec_first,
        vec_second,
        vec_new,
        vec_new.astype(BF),
        entropy.reshape(-1),
        occupancy,
    )


def solution(mesh):
    placed = (
        P(("rep", "tok"), None),
        P(("rep", "tok"), None),
        P(("rep", "tok")),
        P(),
        P("tok", None, None),
        P("tok", None, None),
        P("tok", None, None),
        P("tok"),
        P("tok"),
        P("tok"),
    )
    return jax.shard_map(
        local,
        mesh=mesh,
        in_specs=placed,
        out_specs=(
            P(("rep", "tok"), None),
            P(("rep", "tok"), None),
            P("tok", None, None),
            P("tok", None, None),
            P("tok", None, None),
            P("tok", None, None),
            P("tok", None, None),
            P("tok"),
            P("tok"),
            P("tok"),
            P("tok"),
            P("tok"),
            P(("rep", "tok")),
            P(),
        ),
        check_vma=False,
    )
```

```python
import functools
import math

import jax
import jax.numpy as jnp
from jax import lax
from jax.experimental import pallas as pl
from jax.experimental.pallas import tpu as pltpu
from jax.sharding import PartitionSpec as P

D = 768
HEADS = 12
HD = 64
FF = 3072
SD = 4
CL = 128
NBLK = 96
STEP = 10
CPS = 32
WROWS = 9216
BLK = 96
ROWS = 1024
PAIRS = HEADS // 2
PW = 2 * HD
TM = 512
META = 16
VMEM_LIMIT = 63 << 20
FC = 768

norm_epsilon = 1e-06
beta_first = 0.9
beta_second = 0.999
adam_epsilon = 1e-08
weight_decay = 0.01
rate_matrix = 0.02
rate_vector = 0.2

BF = jnp.bfloat16
F32 = jnp.float32
I32 = jnp.int32

VMEM = pl.BlockSpec(memory_space=pltpu.VMEM)
SMEM = pl.BlockSpec(memory_space=pltpu.SMEM)
ANY = pl.BlockSpec(memory_space=pl.ANY)

NN = (((1,), (0,)), ((), ()))
NT = (((1,), (1,)), ((), ()))
TN = (((0,), (0,)), ((), ()))


def mm(a, b, dims=NN):
    return lax.dot_general(a, b, dims, preferred_element_type=F32)


def unit(n):
    same = lax.broadcasted_iota(I32, (n, n), 0) == lax.broadcasted_iota(I32, (n, n), 1)
    return jnp.where(same, 1.0, 0.0).astype(BF)


def turned(a, one):
    return mm(one, a, NT).astype(BF)


def slot_positions(block_owner, slot_count):
    owners = block_owner[:, 0]
    blocks = owners.shape[0]
    shared = owners[:, None] == owners[None, :]
    before = (
        jnp.arange(blocks, dtype=jnp.int32)[None, :] < jnp.arange(blocks, dtype=jnp.int32)[:, None]
    )
    earlier = jnp.sum((shared & before).astype(jnp.int32), axis=1)
    return owners * slot_count + earlier


def adam_update(grad_now, weight_old, first_old, second_old, rate_step):
    first_new = beta_first * first_old + (1.0 - beta_first) * grad_now
    second_new = beta_second * second_old + (1.0 - beta_second) * grad_now * grad_now
    first_hat = first_new / (1.0 - beta_first**STEP)
    second_hat = second_new / (1.0 - beta_second**STEP)
    weight_new = weight_old - rate_step * (
        first_hat / (jnp.sqrt(second_hat) + adam_epsilon) + weight_decay * weight_old
    )
    return (first_new, second_new, weight_new)


def route_slots(order, seat, cap):
    cluster = order // CL
    rel = lax.rem(cluster, SD) ^ seat
    place = (cluster // SD) * CL + lax.rem(order, CL) + 1
    chosen = lax.broadcasted_iota(I32, (8, ROWS), 0) == rel
    chosen_low = jnp.where(chosen, 1.0, 0.0).astype(BF)
    before = lax.broadcasted_iota(I32, (ROWS, ROWS), 0) < lax.broadcasted_iota(I32, (ROWS, ROWS), 1)
    before_low = jnp.where(before, 1.0, 0.0).astype(BF)
    running = mm(chosen_low, before_low)
    rank = jnp.sum(jnp.where(chosen, running, 0.0), axis=0, keepdims=True).astype(I32)
    return rel * cap + rank, place


def slot_matrix(slots, at, cap):
    rows = lax.broadcasted_iota(I32, (cap, ROWS), 0) + at * cap
    return jnp.where(rows == slots, 1.0, 0.0).astype(BF)


def send_kernel(cap, tokens, cotangent, order, send_x, send_c, meta):
    seat = lax.rem(lax.axis_index("tok"), SD)
    slots, place = route_slots(order[...], seat, cap)
    digits = jnp.concatenate([place // CL, lax.rem(place, CL)] + [place * 0] * 6, axis=0).astype(F32).astype(BF)
    for at in range(SD):
        picked = slot_matrix(slots, at, cap)
        send_x[at] = mm(picked, tokens[...]).astype(BF)
        send_c[at] = mm(picked, cotangent[...]).astype(BF)
        coded = mm(digits, picked, NT)
        line = jnp.concatenate([coded[0:1], coded[1:2]], axis=1)
        meta[at] = jnp.broadcast_to(line, (META, D)).astype(BF)


def remote(src, dst, send_sem, recv_sem, tok, rep):
    return pltpu.make_async_remote_copy(
        src_ref=src,
        dst_ref=dst,
        send_sem=send_sem,
        recv_sem=recv_sem,
        device_id={"tok": tok, "rep": rep},
        device_id_type=pl.DeviceIdType.MESH,
    )


def loop(n, body):
    def run(i, c):
        body(i)
        return c

    lax.fori_loop(0, n, run, 0)


class Place:
    def __init__(self):
        self.me = me = lax.axis_index("tok")
        self.z = z = lax.axis_index("rep")
        core, x, y = me % 2, (me // 2) % 2, me // 4
        self.twin = me + 1 - 2 * core
        self.xn = me + 2 - 4 * x
        self.yn = me + 4 - 8 * y
        self.dn = self.xn + 4 - 8 * y
        self.side = z % 2
        self.zp = z + 1 - 2 * self.side

    def twin_of(self, tok):
        return tok + 1 - 2 * (tok % 2)

    def greet(self, peers):
        barrier = pltpu.get_barrier_semaphore()
        for tok, rep in peers:
            pl.semaphore_signal(
                barrier, inc=1, device_id={"tok": tok, "rep": rep}, device_id_type=pl.DeviceIdType.MESH
            )
        return lambda: pl.semaphore_wait(barrier, len(peers))


def seat_matrix(meta, first, rows, cap):
    hi = jnp.concatenate([meta[k, 0:8, 0:cap] for k in range(SD)], axis=1).astype(F32)[0:1]
    lo = jnp.concatenate([meta[k, 0:8, cap : 2 * cap] for k in range(SD)], axis=1).astype(F32)[0:1]
    at = (hi * CL + lo).astype(I32)
    seats = lax.broadcasted_iota(I32, (rows, SD * cap), 0) + (first + 1)
    return jnp.where(seats == at, 1.0, 0.0).astype(BF)


def seat_part(meta, k, cap):
    hi = meta[k, 0:8, 0:cap].astype(F32)[0:1]
    lo = meta[k, 0:8, cap : 2 * cap].astype(F32)[0:1]
    at = (hi * CL + lo).astype(I32)
    seats = lax.broadcasted_iota(I32, (ROWS, cap), 0) + 1
    return jnp.where(seats == at, 1.0, 0.0).astype(BF)


def seat_rows(meta, blocks, cap, to):
    def body(t):
        r0 = pl.multiple_of(t * 256, 256)
        rows = blocks[...].reshape(SD * cap, D)
        to[pl.ds(r0, 256), :] = mm(seat_matrix(meta, r0, 256, cap), rows).astype(BF)

    loop(ROWS // 256, body)


def seat_kernel(cap, blocks, meta, to):
    seat_rows(meta, blocks, cap, to)


def gather_kernel(
    cap,
    count,
    tokens_h,
    cotangent_h,
    order,
    master_h,
    vector,
    owner_of,
    slots,
    x_c,
    cot_c,
    recv_meta,
    vecs,
    b_u,
    occupancy,
    positions,
    tokens,
    cotangent,
    master,
    own,
    send_x,
    send_c,
    meta,
    recv_x,
    recv_c,
    got_meta,
    mine,
    by_z,
    by_tok,
    x_s,
    x_r,
    y_s,
    y_r,
    d_s,
    d_r,
    zx_s,
    zx_r,
    zd_s,
    zd_r,
    p_s,
    p_r,
    row_s,
    row_r,
    z_s,
    z_r,
    t_s,
    t_r,
    local_s,
):
    at = Place()
    me, z, side = at.me, at.z, at.side
    n_tok, n_rep = 8, 4
    peers = [((me + d) % n_tok, z) for d in range(1, n_tok)] + [(me, (z + d) % n_rep) for d in range(1, n_rep)]
    fetch = [
        pltpu.make_async_copy(src, dst, local_s.at[i])
        for i, (src, dst) in enumerate(((master_h, master), (tokens_h, tokens), (cotangent_h, cotangent)))
    ]
    for copy in fetch:
        copy.start()
    wait_peers = at.greet(peers)
    fetch[0].wait()

    def cast(s):
        own[s] = master[s].astype(BF)

    loop(count, cast)
    wait_peers()

    half = count // 2

    def slot(owner, s):
        return slots.at[owner * count + s]

    def to_x(s):
        return remote(own.at[s], slot(me, s), x_s.at[s], x_r.at[s], at.xn, z)

    def to_y(s):
        return remote(own.at[s], slot(me, s), y_s.at[s], y_r.at[s], at.yn, z)

    def on_y(s):
        return remote(slot(at.xn, s), slot(at.xn, s), d_s.at[s], d_r.at[s], at.yn, z)

    def x_on_z(s):
        return remote(slot(at.xn, s), slot(at.xn, s), zx_s.at[s], zx_r.at[s], me, at.zp)

    def d_on_z(s):
        return remote(slot(at.dn, s), slot(at.dn, s), zd_s.at[s], zd_r.at[s], me, at.zp)

    owners = (me, at.xn, at.yn, at.dn)

    def to_twin(q, s):
        src = own.at[s] if q == 0 else slot(owners[q], s)
        return remote(src, slot(owners[q], s), p_s.at[q, s], p_r.at[q, s], at.twin, z)

    def near(j):
        return (half + 1) * side + j

    def far(j):
        return (half + 1) * (1 - side) + j

    loop(half, lambda j: to_x(near(j)).start())
    to_x(half).start()
    for s in range(3):
        to_y(s).start()
    loop(count, lambda s: to_twin(0, s).start())
    keep = pltpu.make_async_copy(own, slots.at[pl.ds(me * count, count)], local_s.at[3])
    keep.start()
    fetch[1].wait()
    fetch[2].wait()

    seat = me % SD
    slot_of, place = route_slots(order[...], seat, cap)
    digits = jnp.concatenate([place // CL, lax.rem(place, CL)] + [place * 0] * 6, axis=0).astype(F32).astype(BF)
    for k in range(SD):
        picked = slot_matrix(slot_of, k, cap)
        send_x[k] = mm(picked, tokens[...]).astype(BF)
        send_c[k] = mm(picked, cotangent[...]).astype(BF)
        coded = mm(digits, picked, NT)
        line = jnp.concatenate([coded[0:1], coded[1:2]], axis=1)
        meta[k] = jnp.broadcast_to(line, (META, D)).astype(BF)
    seats = (me, at.twin, at.xn, at.twin_of(at.xn))
    rows_of = ((meta, got_meta), (send_x, recv_x), (send_c, recv_c))

    def row_copy(i, k):
        src, dst = rows_of[i]
        return remote(src.at[k], dst.at[k], row_s.at[i, k], row_r.at[i, k], seats[k], z)

    for i in range(3):
        src, dst = rows_of[i]
        for k in (2, 3, 1):
            row_copy(i, k).start()
        dst[0] = src[0]

    residue = lax.rem(me // SD * CPS + order[...] // CL, n_tok)
    hit = lax.broadcasted_iota(I32, (128, ROWS), 0) == residue
    for i in range(9):
        mine[i : i + 1] = vector[i * 128 : (i + 1) * 128].reshape(1, 128).astype(BF).astype(F32)
    block_row = lax.broadcasted_iota(I32, (NBLK, NBLK), 0)
    block_col = lax.broadcasted_iota(I32, (NBLK, NBLK), 1)
    by_col = owner_of[...].astype(F32)
    by_row = lane_sum(jnp.where(block_row == block_col, by_col, 0.0))
    earlier = jnp.where((by_row == by_col) & (block_row < block_col), 1.0, 0.0)
    positions[...] = (by_col * count + jnp.sum(earlier, axis=0, keepdims=True)).astype(I32)
    by_z[0] = mm(jnp.ones((8, ROWS), BF), jnp.where(hit, 1.0, 0.0).astype(BF), NT)

    def z_copy(d):
        return remote(by_z.at[0], by_z.at[d], z_s.at[d], z_r.at[d], me, (z + d) % n_rep)

    def t_copy(d):
        return remote(mine, by_tok.at[d], t_s.at[d], t_r.at[d], (me + d) % n_tok, z)

    for d in range(1, n_rep):
        z_copy(d).start()
    for d in range(1, n_rep):
        z_copy(d).wait()
    mine[16:24] = by_z[0] + by_z[1] + by_z[2] + by_z[3]
    for d in range(1, n_tok):
        t_copy(d).start()

    def x_here(s):
        to_x_in(s).wait_recv()
        on_y(s).start()
        to_twin(1, s).start()

    def to_x_in(s):
        return remote(own.at[s], slot(at.xn, s), x_s.at[s], x_r.at[s], at.xn, z)

    def y_in(s):
        return remote(own.at[s], slot(at.yn, s), y_s.at[s], y_r.at[s], at.yn, z)

    def d_in(s):
        return remote(own.at[s], slot(at.dn, s), d_s.at[s], d_r.at[s], at.yn, z)

    def first(j):
        x_here(near(j))
        x_on_z(near(j)).start()
        to_y(3 + j).start()

    loop(half, first)
    x_here(half)
    for s in range(3 + half, count):
        to_y(s).start()

    def y_here(s):
        y_in(s).wait_recv()
        to_twin(2, s).start()

    def second(j):
        x_on_z(far(j)).wait_recv()
        to_twin(1, far(j)).start()
        y_here(j)
        d_in(near(j)).wait_recv()
        d_on_z(near(j)).start()
        to_twin(3, near(j)).start()

    loop(half, second)
    d_in(half).wait_recv()
    to_twin(3, half).start()
    loop(count - half, lambda j: y_here(half + j))
    for i in (0, 1):
        for k in (2, 3, 1):
            row_copy(i, k).wait_recv()
    recv_meta[...] = got_meta[...]
    seat_rows(got_meta, recv_x, cap, x_c)

    def third(j):
        d_on_z(far(j)).wait_recv()
        to_twin(3, far(j)).start()

    loop(half, third)

    by_tok[0] = mine[...]
    for d in range(1, n_tok):
        t_copy(d).wait()
    for owner in range(n_tok):
        share = by_tok[(me + n_tok - owner) % n_tok]
        occupancy[owner : owner + 1, :] = share[16:17, 0:n_tok].astype(I32)
        for i in range(9):
            chunk = owner * 9 + i
            row, lane = chunk // 6, chunk % 6 * 128
            if row < 8:
                vecs[row : row + 1, lane : lane + 128] = share[i : i + 1]
            else:
                lane += (row - 8) * D
                b_u[:, lane : lane + 128] = share[i : i + 1]
    for k in (2, 3, 1):
        row_copy(2, k).wait_recv()
    seat_rows(got_meta, recv_c, cap, cot_c)
    for i in range(3):
        for k in (2, 3, 1):
            row_copy(i, k).wait_send()
    keep.wait()

    def sent_half(j):
        to_x(near(j)).wait_send()
        on_y(near(j)).wait_send()
        x_on_z(near(j)).wait_send()
        d_on_z(near(j)).wait_send()

    loop(half, sent_half)
    to_x(half).wait_send()
    on_y(half).wait_send()

    def sent(s):
        to_y(s).wait_send()
        for q in range(4):
            to_twin(q, s).wait()

    loop(count, sent)


def gather_all(cap, tokens, cotangent, order, master, vector, block_owner):
    count = master.shape[0]
    rows = jax.ShapeDtypeStruct((ROWS, D), BF)
    dma = pltpu.SemaphoreType.DMA
    block = pltpu.VMEM((SD, cap, D), BF)
    meta = pltpu.VMEM((SD, META, D), BF)
    return pl.pallas_call(
        functools.partial(gather_kernel, cap, count),
        out_shape=(
            jax.ShapeDtypeStruct((8 * count, BLK, D), BF),
            rows,
            rows,
            jax.ShapeDtypeStruct((SD, META, D), BF),
            jax.ShapeDtypeStruct((8, D), F32),
            jax.ShapeDtypeStruct((1, FF), F32),
            jax.ShapeDtypeStruct((8, 8), I32),
            jax.ShapeDtypeStruct((1, NBLK), I32),
        ),
        in_specs=[ANY, ANY, VMEM, ANY, VMEM, VMEM],
        out_specs=(ANY,) + (VMEM,) * 7,
        scratch_shapes=[
            pltpu.VMEM((ROWS, D), BF),
            pltpu.VMEM((ROWS, D), BF),
            pltpu.VMEM((count, BLK, D), F32),
            pltpu.VMEM((count, BLK, D), BF),
            block,
            block,
            meta,
            block,
            block,
            meta,
            pltpu.VMEM((24, 128), F32),
            pltpu.VMEM((4, 8, 128), F32),
            pltpu.VMEM((8, 24, 128), F32),
        ]
        + [dma((count,))] * 10
        + [dma((4, count))] * 2
        + [dma((3, SD))] * 2
        + [dma((4,))] * 2
        + [dma((8,))] * 2
        + [dma((4,))],
        compiler_params=pltpu.CompilerParams(collective_id=0, has_side_effects=True, vmem_limit_bytes=VMEM_LIMIT),
        name="gather",
    )(tokens, cotangent, order, master, vector, block_owner.reshape(1, NBLK))


def return_kernel(cap, order, *refs):
    blocks, (out, ing, entropy) = refs[:SD], refs[SD:]
    seat = lax.rem(lax.axis_index("tok"), SD)
    slots, _ = route_slots(order[...], seat, cap)
    picked = jnp.concatenate([slot_matrix(slots, at, cap) for at in range(SD)], axis=0)
    line = jnp.concatenate([block[2 * cap : 2 * cap + 8, 0:cap] for block in blocks], axis=1)
    entropy[...] = mm(line, picked)[0:1].astype(BF)
    digits = jnp.concatenate([slots // CL, lax.rem(slots, CL)] + [slots * 0] * 6, axis=0).astype(F32).astype(BF)
    one = unit(256)
    for t in range(ROWS // 256):
        ts = slice(t * 256, (t + 1) * 256)
        column = mm(one, digits[:, ts], NT)
        mine = (column[:, 0:1] * CL + column[:, 1:2]).astype(I32)
        hit = lax.broadcasted_iota(I32, (256, SD * cap), 1) == mine
        flipped = jnp.where(hit, 1.0, 0.0).astype(BF)
        for to, first in ((out, 0), (ing, cap)):
            rows = jnp.concatenate([block[first : first + cap, :] for block in blocks], axis=0)
            to[ts, :] = mm(flipped, rows).astype(BF)


def swap_blocks(blocks):
    n = lax.axis_size("tok")
    parts = [blocks[0]]
    for k in range(1, SD):
        parts.append(lax.ppermute(blocks[k], "tok", [(i, i ^ k) for i in range(n)]))
    return parts


def reduce_kernel(
    count,
    split,
    grads,
    vec,
    total,
    vec_out,
    a,
    tw,
    rd,
    rx,
    ry,
    o,
    rz1,
    pz,
    rz2,
    fz,
    rzx,
    vt,
    va,
    vb,
    vc,
    a_l,
    keep_l,
    p_s,
    p_r,
    d_s,
    d_r,
    x_s,
    x_r,
    y_s,
    y_r,
    z1_s,
    z1_r,
    z2_s,
    z2_r,
    z3_s,
    z3_r,
    zx_s,
    zx_r,
    t_s,
    t_r,
    v_s,
    v_r,
):
    at = Place()
    me, z = at.me, at.z
    n_tok, n_rep = 8, 4
    peers = [((me + d) % n_tok, z) for d in range(1, n_tok)] + [(me, (z + d) % n_rep) for d in range(1, n_rep)]
    wait_peers = at.greet(peers)
    owners = (me, at.xn, at.yn, at.dn)

    def load(q):
        return pltpu.make_async_copy(grads.at[pl.ds(owners[q] * count, count)], a.at[q], a_l.at[q])

    for q in (3, 1, 2, 0):
        load(q).start()
    wait_peers()

    def to_twin(q, s):
        src = grads.at[at.twin_of(owners[q]) * count + s]
        return remote(src, tw.at[q, s], p_s.at[q, s], p_r.at[q, s], at.twin, z)

    def d_y(s):
        return remote(a.at[3, s], rd.at[s], d_s.at[s], d_r.at[s], at.yn, z)

    def d_x(s):
        return remote(a.at[3, s], rd.at[s], d_s.at[s], d_r.at[s], at.xn, z)

    def to_x(s):
        return remote(a.at[1, s], rx.at[s], x_s.at[s], x_r.at[s], at.xn, z)

    def to_y(s):
        return remote(a.at[2, s], ry.at[s], y_s.at[s], y_r.at[s], at.yn, z)

    def z_in(s):
        return remote(o.at[s], rz1.at[s], z1_s.at[s], z1_r.at[s], me, at.zp)

    def z_swap(s):
        return remote(pz.at[s], rz2.at[s], z2_s.at[s], z2_r.at[s], me, n_rep - 1 - z)

    def z_out(s):
        return remote(fz.at[s], fz.at[s], z3_s.at[s], z3_r.at[s], me, at.zp)

    def keep(s):
        return pltpu.make_async_copy(fz.at[s], total.at[s], keep_l.at[s])

    def f32(ref, *index):
        return ref[index].astype(F32)

    loop(count, lambda s: to_twin(3, s).start())

    def others(s):
        for q in (2, 1, 0):
            to_twin(q, s).start()

    loop(count, others)

    def v_tok(d):
        return remote(vec.at[(me + d) % n_tok], vt.at[d], t_s.at[d], t_r.at[d], (me + d) % n_tok, z)

    def v_rep(i, src):
        return remote(src, vb.at[i], v_s.at[i], v_r.at[i], me, at.zp if i == 0 else (z + 2) % n_rep)

    for d in range(1, n_tok):
        v_tok(d).start()

    load(3).wait()

    def join(q, s):
        to_twin(q, s).wait_recv()
        return f32(a, q, s) + f32(tw, q, s)

    def diagonal(s, send):
        a[3, s] = join(3, s).astype(BF)
        send(s).start()

    loop(split, lambda s: diagonal(s, d_y))
    loop(count - split, lambda j: diagonal(split + j, d_x))

    v_sum = vec[me]
    for d in range(1, n_tok):
        v_tok(d).wait()
        v_sum = v_sum + vt[d]
    va[...] = v_sum
    v_rep(0, va).start()

    load(1).wait()
    load(2).wait()

    half = count // 2
    side = at.side

    def near(j):
        return (half + 1) * side + j

    def far(j):
        return (half + 1) * (1 - side) + j

    def is_far(s):
        return ((side == 0) & (s > half)) | ((side == 1) & (s < half))

    def x_ready(s):
        @pl.when(s < split)
        def _():
            d_y(s).wait_recv()
            a[1, s] = (join(1, s) + f32(rd, s)).astype(BF)

        @pl.when(s >= split)
        def _():
            a[1, s] = join(1, s).astype(BF)

    def y_ready(s):
        @pl.when(s < split)
        def _():
            a[2, s] = join(2, s).astype(BF)

        @pl.when(s >= split)
        def _():
            d_x(s).wait_recv()
            a[2, s] = (join(2, s) + f32(rd, s)).astype(BF)

        to_y(s).start()

    def x_pair(s):
        return remote(a.at[1, s], rzx.at[s], zx_s.at[s], zx_r.at[s], me, at.zp)

    def far_x(j):
        x_ready(far(j))
        x_pair(far(j)).start()
        y_ready(j)

    loop(half, far_x)

    def near_x(j):
        s = near(j)
        x_ready(s)
        x_pair(s).wait_recv()
        a[1, s] = (f32(a, 1, s) + f32(rzx, s)).astype(BF)
        to_x(s).start()
        y_ready(half + j)

    loop(half, near_x)
    x_ready(half)
    to_x(half).start()
    y_ready(count - 1)

    v_rep(0, va).wait()
    vc[...] = va[...] + vb[0]
    v_rep(1, vc).start()
    load(0).wait()
    inner = (z == 1) | (z == 2)
    outer = (z == 0) | (z == 3)

    def planes(i):
        @pl.when((i < count) & is_far(i))
        def _():
            to_y(i).wait_recv()
            o[i] = (join(0, i) + f32(ry, i)).astype(BF)

        @pl.when((i < count) & jnp.logical_not(is_far(i)))
        def _():
            to_x(i).wait_recv()
            to_y(i).wait_recv()
            o[i] = (join(0, i) + f32(rx, i) + f32(ry, i)).astype(BF)

        @pl.when(outer & (i < count))
        def _():
            z_in(i).start()

        @pl.when(inner & (i >= 1) & (i < count + 1))
        def _():
            s = i - 1
            z_in(s).wait_recv()
            pz[s] = (f32(o, s) + f32(rz1, s)).astype(BF)
            z_swap(s).start()

        @pl.when(inner & (i >= 2) & (i < count + 2))
        def _():
            s = i - 2
            z_swap(s).wait_recv()
            fz[s] = (f32(pz, s) + f32(rz2, s)).astype(BF)
            z_out(s).start()
            keep(s).start()

        @pl.when(outer & (i >= 3))
        def _():
            s = i - 3
            z_out(s).wait_recv()
            keep(s).start()

    loop(count + 3, planes)
    v_rep(1, vc).wait()
    vec_out[...] = vc[...] + vb[1]

    def sent(s):
        for q in range(4):
            to_twin(q, s).wait_send()
        d_y(s).wait_send()
        to_y(s).wait_send()
        keep(s).wait()

    loop(count, sent)

    def sent_x(j):
        x_pair(far(j)).wait_send()
        to_x(near(j)).wait_send()

    loop(half, sent_x)
    to_x(half).wait_send()

    @pl.when(outer)
    def _():
        loop(count, lambda s: z_in(s).wait_send())

    @pl.when(inner)
    def _():
        def back(s):
            z_swap(s).wait_send()
            z_out(s).wait_send()

        loop(count, back)


def reduce_all(grads, shares, count):
    dma = pltpu.SemaphoreType.DMA
    part = pltpu.VMEM((count, BLK, D), BF)
    whole = pltpu.VMEM((4, count, BLK, D), BF)
    line = pltpu.VMEM((16, 128), F32)
    total, vec = pl.pallas_call(
        functools.partial(reduce_kernel, count, (count + 3) // 2),
        out_shape=(
            jax.ShapeDtypeStruct((count, BLK, D), BF),
            jax.ShapeDtypeStruct((16, 128), F32),
        ),
        in_specs=[ANY, VMEM],
        out_specs=(ANY, VMEM),
        scratch_shapes=[whole, whole]
        + [part] * 9
        + [pltpu.VMEM((8, 16, 128), F32), line, pltpu.VMEM((2, 16, 128), F32), line]
        + [dma((4,)), dma((count,))]
        + [dma((4, count))] * 2
        + [dma((count,))] * 14
        + [dma((8,))] * 2
        + [dma((2,))] * 2,
        compiler_params=pltpu.CompilerParams(
            collective_id=1, has_side_effects=True, vmem_limit_bytes=VMEM_LIMIT
        ),
        name="reduce",
    )(grads, shares)
    return total, vec[0:9].reshape(-1)


V_BQ, V_BV, V_BO, V_BD, V_G1, V_C1, V_G2, V_C2 = range(8)


def inverse(x):
    r = pl.reciprocal(x, approx=True)
    return r * (2.0 - x * r)


def erf_parts(v):
    t = inverse(1.0 + (0.3275911 / math.sqrt(2.0)) * jnp.abs(v))
    e = jnp.exp2((v * v) * (-0.5 / math.log(2.0)))
    poly = 0.5 * 1.061405429
    for c in (-1.453152027, 1.421413741, -0.284496736, 0.254829592):
        poly = poly * t + 0.5 * c
    tail = poly * (t * e)
    return jnp.where(v >= 0.0, 1.0 - tail, tail), e


def lane_sum(x):
    return jnp.sum(x, axis=1, keepdims=True)


def gelu_parts(v):
    phi, e = erf_parts(v)
    return v * phi, phi + v * (e * (1.0 / math.sqrt(2.0 * math.pi)))


def chain_kernel(
    cap,
    pos,
    slots,
    vecs,
    b_u,
    x_h,
    cot_h,
    meta,
    back_0,
    back_1,
    back_2,
    back_3,
    shares,
    heads_h,
    act_h,
    d_up_h,
    d_q_h,
    d_k_h,
    d_v_h,
    d_proj_h,
    hid_h,
    d_br_h,
    w,
    x_c,
    heads,
    act,
    d_up,
    d_q,
    d_k,
    d_v,
    d_proj,
    hid,
    d_br,
    out_c,
    ing_c,
    ent,
    gvec,
    g_bu,
    q_t,
    k_t,
    v_t,
    p_t,
    dh_t,
    n1_t,
    hid_t,
    w_sem,
    x_sem,
    o_sem,
):
    inv = 1.0 / math.sqrt(HD)

    def w_copy(b):
        return pltpu.make_async_copy(slots.at[pos[b]], w.at[pl.ds(b * BLK, BLK)], w_sem)

    get_x = pltpu.make_async_copy(x_h, x_c, x_sem.at[0])
    get_cot = pltpu.make_async_copy(cot_h, d_br, x_sem.at[1])
    get_x.start()
    loop(NBLK, lambda b: w_copy(b).start())
    get_cot.start()
    gvec[...] = jnp.zeros_like(gvec)
    g_bu[...] = jnp.zeros_like(g_bu)
    shares[...] = jnp.zeros_like(shares)
    get_x.wait()
    loop(NBLK, lambda b: w_copy(b).wait())
    get_cot.wait()

    wq, wk, wv, wo = (w.at[pl.ds(i * D, D)] for i in range(4))
    wu = w.at[pl.ds(4 * D, FF)]
    wd = w.at[pl.ds(4 * D + FF, FF)]

    lane = lax.broadcasted_iota(I32, (1, PW), 1)
    m0 = jnp.where(lane < HD, 1.0, 0.0).astype(BF)
    m1 = jnp.where(lane < HD, 0.0, 1.0).astype(BF)
    first_half = lax.broadcasted_iota(I32, (CL, PW), 1) < HD

    one = unit(CL)

    def apart(pair):
        return jnp.concatenate([pair * m0, pair * m1], axis=0)

    def vec(i):
        return vecs[i : i + 1, :]

    def add_vec(i, value):
        gvec[i : i + 1, :] += jnp.sum(value, axis=0, keepdims=True)

    saved = (
        (heads, heads_h),
        (act, act_h),
        (d_up, d_up_h),
        (d_q, d_q_h),
        (d_k, d_k_h),
        (d_v, d_v_h),
        (d_proj, d_proj_h),
        (hid, hid_h),
        (d_br, d_br_h),
    )

    def save(t, i):
        rows = pl.ds(pl.multiple_of(t * TM, TM), TM)
        src, dst = saved[i]
        return pltpu.make_async_copy(src.at[rows], dst.at[rows], o_sem.at[i])

    def tile(t):
        r0 = pl.multiple_of(t * TM, TM)
        rows = pl.ds(r0, TM)
        q_t[...] = ((mm(x_c[rows, :], wq[...]) + vec(V_BQ)).astype(BF).astype(F32) * inv).astype(BF)
        k_t[...] = mm(x_c[rows, :], wk[...]).astype(BF)
        v_t[...] = (mm(x_c[rows, :], wv[...]) + vec(V_BV)).astype(BF)

        def attend(c):
            cr = pl.ds(pl.multiple_of(c * CL, CL), CL)
            gr = pl.ds(pl.multiple_of(r0 + c * CL, CL), CL)
            total = jnp.zeros((1, CL), F32)
            for p in range(PAIRS):
                ps = slice(p * PW, (p + 1) * PW)
                scores = mm(apart(k_t[cr, ps]), q_t[cr, ps], NT)
                halves = []
                for h in range(2):
                    sh = scores[h * CL : (h + 1) * CL]
                    sh = sh - jnp.max(sh, axis=0, keepdims=True)
                    e = jnp.exp(sh)
                    tot = jnp.sum(e, axis=0, keepdims=True)
                    r = inverse(tot)
                    total += jnp.log(tot) - jnp.sum(e * sh, axis=0, keepdims=True) * r
                    halves.append((e * r).astype(BF))
                weights = jnp.concatenate(halves, axis=0)
                p_t[c, p] = weights
                heads[gr, ps] = mm(turned(weights, one), apart(v_t[cr, ps])).astype(BF)
            ent[:, gr] = jnp.broadcast_to(total * (1.0 / HEADS), (8, CL))

        loop(TM // CL, attend)

        r1 = x_c[rows, :].astype(F32) + mm(heads[rows, :], wo[...]) + vec(V_BO)
        c1 = r1 - lane_sum(r1) * (1.0 / D)
        rs1 = lax.rsqrt(lane_sum(c1 * c1) * (1.0 / D) + norm_epsilon)
        n1 = c1 * rs1
        hidden = n1 * vec(V_G1) + vec(V_C1)
        hid[rows, :] = hidden.astype(BF)
        n1_t[...] = n1
        hid_t[...] = hidden

        def widen(f):
            fs = pl.ds(pl.multiple_of(f * FC, FC), FC)
            g, g_slope = gelu_parts(mm(hid[rows, :], wu[fs, :], NT) + b_u[:, fs])
            act[rows, fs] = g.astype(BF)
            d_up[rows, fs] = g_slope.astype(BF)

        loop(FF // FC, widen)
        r2 = hid_t[...] + mm(act[rows, :], wd[...]) + vec(V_BD)
        c2 = r2 - lane_sum(r2) * (1.0 / D)
        rs2 = lax.rsqrt(lane_sum(c2 * c2) * (1.0 / D) + norm_epsilon)
        n2 = c2 * rs2
        out_c[rows, :] = (n2 * vec(V_G2) + vec(V_C2)).astype(BF)

        e2 = d_br[rows, :].astype(F32)
        add_vec(V_G2, e2 * n2)
        add_vec(V_C2, e2)
        eg = e2 * vec(V_G2)
        d_r2 = rs2 * (eg - lane_sum(eg) * (1.0 / D) - n2 * (lane_sum(eg * n2) * (1.0 / D)))
        d_br[rows, :] = d_r2.astype(BF)
        add_vec(V_BD, d_br[rows, :].astype(F32))
        hid_t[...] = d_r2

        def widen_back(f):
            fs = pl.ds(pl.multiple_of(f * FC, FC), FC)
            du = (mm(d_br[rows, :], wd[fs, :], NT) * d_up[rows, fs].astype(F32)).astype(BF)
            d_up[rows, fs] = du
            g_bu[:, fs] += jnp.sum(du.astype(F32), axis=0, keepdims=True)

        loop(FF // FC, widen_back)
        n1 = n1_t[...]
        d_h = hid_t[...] + mm(d_up[rows, :], wu[...])
        add_vec(V_G1, d_h * n1)
        add_vec(V_C1, d_h)
        eg = d_h * vec(V_G1)
        d_r1 = rs1 * (eg - lane_sum(eg) * (1.0 / D) - n1 * (lane_sum(eg * n1) * (1.0 / D)))
        d_proj[rows, :] = d_r1.astype(BF)
        hid_t[...] = d_r1
        add_vec(V_BO, d_proj[rows, :].astype(F32))
        dh_t[...] = mm(d_proj[rows, :], wo[...], NT).astype(BF)

        def attend_back(c):
            cr = pl.ds(pl.multiple_of(c * CL, CL), CL)
            gr = pl.ds(pl.multiple_of(r0 + c * CL, CL), CL)
            for p in range(PAIRS):
                ps = slice(p * PW, (p + 1) * PW)
                dh = dh_t[cr, ps]
                weights = p_t[c, p]
                d_w = mm(apart(v_t[cr, ps]), dh, NT)
                halves = []
                for h in range(2):
                    wh = weights[h * CL : (h + 1) * CL].astype(F32)
                    dwh = d_w[h * CL : (h + 1) * CL]
                    halves.append((wh * (dwh - jnp.sum(dwh * wh, axis=0, keepdims=True))).astype(BF))
                d_s = jnp.concatenate(halves, axis=0)
                d_q[gr, ps] = (mm(turned(d_s, one), apart(k_t[cr, ps])) * inv).astype(BF)
                dk = mm(d_s, q_t[cr, ps])
                d_k[gr, ps] = jnp.where(first_half, dk[0:CL], dk[CL:]).astype(BF)
                dv = mm(weights, dh)
                d_v[gr, ps] = jnp.where(first_half, dv[0:CL], dv[CL:]).astype(BF)

        loop(TM // CL, attend_back)
        add_vec(V_BQ, d_q[rows, :].astype(F32))
        add_vec(V_BV, d_v[rows, :].astype(F32))
        d_x = mm(d_q[rows, :], wq[...], NT) + mm(d_k[rows, :], wk[...], NT) + mm(d_v[rows, :], wv[...], NT)
        ing_c[rows, :] = (hid_t[...] + d_x.astype(BF).astype(F32)).astype(BF)
        for i in range(len(saved)):
            save(t, i).start()

    loop(ROWS // TM, tile)

    for k, back in enumerate((back_0, back_1, back_2, back_3)):
        own = seat_part(meta, k, cap)
        flipped = turned(own, unit(cap))
        back[0:cap, :] = mm(flipped, out_c[...]).astype(BF)
        back[cap : 2 * cap, :] = mm(flipped, ing_c[...]).astype(BF)
        line = mm(ent[...].astype(BF), own)
        back[2 * cap :, :] = jnp.concatenate([line, line], axis=1)[0:1].astype(BF) * jnp.ones((META, 1), BF)

    for chunk in range(72):
        row, lane = chunk // 6, chunk % 6 * 128
        if row < 8:
            part = gvec[row : row + 1, lane : lane + 128]
        else:
            lane += (row - 8) * D
            part = g_bu[:, lane : lane + 128]
        shares[chunk // 9, chunk % 9 : chunk % 9 + 1, :] = part

    def saved_all(t):
        for i in range(len(saved)):
            save(t, i).wait()

    loop(ROWS // TM, saved_all)


def chain(cap, positions, slots, vecs, b_u, x_c, cot_c, meta):
    rows = jax.ShapeDtypeStruct((ROWS, D), BF)
    wide = jax.ShapeDtypeStruct((ROWS, FF), BF)
    back = jax.ShapeDtypeStruct((2 * cap + META, D), BF)
    r_v, w_v, t_v, t_f = (pltpu.VMEM(shape, kind) for shape, kind in (
        ((ROWS, D), BF), ((ROWS, FF), BF), ((TM, D), BF), ((TM, D), F32)
    ))
    return pl.pallas_call(
        functools.partial(chain_kernel, cap),
        out_shape=(back,) * SD + (jax.ShapeDtypeStruct((8, 16, 128), F32), rows, wide, wide) + (rows,) * 6,
        in_specs=[SMEM, ANY, VMEM, VMEM, ANY, ANY, VMEM],
        out_specs=(VMEM,) * (SD + 1) + (ANY,) * 9,
        scratch_shapes=[
            pltpu.VMEM((WROWS, D), BF),
            r_v,
            r_v,
            w_v,
            w_v,
            r_v,
            r_v,
            r_v,
            r_v,
            r_v,
            r_v,
            r_v,
            r_v,
            pltpu.VMEM((8, ROWS), F32),
            pltpu.VMEM((8, D), F32),
            pltpu.VMEM((1, FF), F32),
            t_v,
            t_v,
            t_v,
            pltpu.VMEM((TM // CL, PAIRS, 2 * CL, CL), BF),
            t_v,
            t_f,
            t_f,
            pltpu.SemaphoreType.DMA,
            pltpu.SemaphoreType.DMA((2,)),
            pltpu.SemaphoreType.DMA((9,)),
        ],
        compiler_params=pltpu.CompilerParams(vmem_limit_bytes=VMEM_LIMIT),
        name="layer",
    )(positions, slots, vecs, b_u, x_c, cot_c, meta)


WC = 8 * BLK


def weight_kernel(
    pos,
    x_h,
    heads_h,
    act_h,
    d_up_h,
    d_q_h,
    d_k_h,
    d_v_h,
    d_proj_h,
    hid_h,
    d_br_h,
    grads,
    x_c,
    heads,
    act,
    d_up,
    d_q,
    d_k,
    d_v,
    d_proj,
    hid,
    d_br,
    stage,
    flipped,
    i_sem,
    g_sem,
):
    one = unit(256)
    refs = (
        (x_h, x_c),
        (d_q_h, d_q),
        (d_k_h, d_k),
        (d_v_h, d_v),
        (heads_h, heads),
        (d_proj_h, d_proj),
        (hid_h, hid),
        (d_up_h, d_up),
        (d_br_h, d_br),
        (act_h, act),
    )
    fetch = [pltpu.make_async_copy(src, dst, i_sem.at[i]) for i, (src, dst) in enumerate(refs)]
    for copy in fetch:
        copy.start()

    per = WC // BLK

    def g_copy(chunk, j, at):
        return pltpu.make_async_copy(
            stage.at[at, pl.ds(j * BLK, BLK)], grads.at[pos[chunk * per + j]], g_sem.at[at]
        )

    def put(chunk, left, right):
        at = lax.rem(chunk, 2)

        @pl.when(chunk >= 2)
        def _():
            for j in range(per):
                g_copy(chunk - 2, j, at).wait()

        for c in range(WC // 256):
            cs = slice(c * 256, (c + 1) * 256)
            flipped[cs, :] = turned(left[:, cs], one)
        stage[at] = mm(flipped[...], right).astype(BF)
        for j in range(per):
            g_copy(chunk, j, at).start()

    first = 0
    for left, right, needs in (
        (x_c, d_q, (0, 1)),
        (x_c, d_k, (2,)),
        (x_c, d_v, (3,)),
        (heads, d_proj, (4, 5)),
        (d_up, hid, (6, 7)),
        (act, d_br, (8, 9)),
    ):
        for i in needs:
            fetch[i].wait()

        def body(j, left=left, right=right, first=first):
            put(first + j, left[:, pl.ds(pl.multiple_of(j * WC, WC), WC)], right[...])

        loop(left.shape[1] // WC, body)
        first += left.shape[1] // WC
    for chunk in (first - 2, first - 1):
        for j in range(per):
            g_copy(chunk, j, chunk % 2).wait()


def weight_grads_of(total_slots, positions, x_c, saved):
    r_v, w_v = pltpu.VMEM((ROWS, D), BF), pltpu.VMEM((ROWS, FF), BF)
    return pl.pallas_call(
        weight_kernel,
        out_shape=jax.ShapeDtypeStruct((total_slots, BLK, D), BF),
        in_specs=[SMEM] + [ANY] * 10,
        out_specs=ANY,
        scratch_shapes=[r_v, r_v, w_v, w_v]
        + [r_v] * 6
        + [
            pltpu.VMEM((2, WC, D), BF),
            pltpu.VMEM((WC, ROWS), BF),
            pltpu.SemaphoreType.DMA((10,)),
            pltpu.SemaphoreType.DMA((2,)),
        ],
        compiler_params=pltpu.CompilerParams(vmem_limit_bytes=VMEM_LIMIT),
        cost_estimate=pl.CostEstimate(flops=2 * ROWS * WROWS * D, bytes_accessed=40 << 20, transcendentals=0),
        name="weight_grads",
    )(positions, x_c, *saved)


def local(
    tokens,
    cotangent,
    cluster_order,
    block_owner,
    master_slots,
    moment_one,
    moment_two,
    vector_master,
    vector_moment_one,
    vector_moment_two,
):
    tok_count = lax.axis_size("tok")
    tok_index = lax.axis_index("tok")
    slot_count = master_slots.shape[0]
    cap = tok_count // SD * (max(1, CPS // tok_count) * 3 * CL // (2 * SD))
    total_slots = tok_count * slot_count
    order = cluster_order.reshape(1, ROWS)

    block = jax.ShapeDtypeStruct((SD, cap, D), BF)
    meta_shape = jax.ShapeDtypeStruct((SD, META, D), BF)
    row_block = jax.ShapeDtypeStruct((ROWS, D), BF)
    four_planes = tok_count == 8 and lax.axis_size("rep") == 4
    if four_planes:
        slots_low, x_c, cot_c, recv_meta, vecs, b_u, occupancy, positions = gather_all(
            cap, tokens, cotangent, order, master_slots, vector_master, block_owner
        )
        positions = positions.reshape(NBLK)
    else:
        positions = slot_positions(block_owner, slot_count)
        slots_low = lax.all_gather(master_slots.astype(BF), "tok", axis=0, tiled=True)
        vectors = lax.all_gather(vector_master.astype(BF), "tok", axis=0, tiled=True).astype(F32)
        vecs, b_u = vectors[: 8 * D].reshape(8, D), vectors[8 * D :].reshape(1, FF)
        cluster = tok_index // SD * CPS + cluster_order // CL
        target = cluster % tok_count
        chosen = target[None, :] == jnp.arange(tok_count, dtype=jnp.int32)[:, None]
        sent_counts = jnp.sum(chosen.astype(F32), axis=1)
        own_row = (jnp.arange(tok_count, dtype=jnp.int32) == tok_index).astype(F32)
        occupancy = lax.psum(own_row[:, None] * sent_counts[None, :], ("tok", "rep")).astype(jnp.int32)
        send_x, send_c, meta = pl.pallas_call(
            functools.partial(send_kernel, cap),
            out_shape=(block, block, meta_shape),
            in_specs=[VMEM] * 3,
            out_specs=(VMEM,) * 3,
            compiler_params=pltpu.CompilerParams(vmem_limit_bytes=VMEM_LIMIT),
            name="send_rows",
        )(tokens, cotangent, order)
        recv_x, recv_c, recv_meta = (jnp.stack(swap_blocks(b)) for b in (send_x, send_c, meta))
        x_c, cot_c = (
            pl.pallas_call(
                functools.partial(seat_kernel, cap),
                out_shape=row_block,
                in_specs=[VMEM] * 2,
                out_specs=VMEM,
                compiler_params=pltpu.CompilerParams(vmem_limit_bytes=VMEM_LIMIT),
                name="seat_rows",
            )(rows, recv_meta)
            for rows in (recv_x, recv_c)
        )

    *backs, shares, heads, act, d_up, d_q, d_k, d_v, d_proj, hid, d_br = chain(
        cap, positions, slots_low, vecs, b_u, x_c, cot_c, recv_meta
    )
    returned = swap_blocks(backs)
    grads = weight_grads_of(
        total_slots, positions, x_c, (heads, act, d_up, d_q, d_k, d_v, d_proj, hid, d_br)
    )
    if four_planes:
        total, vec_owned = reduce_all(grads, shares, slot_count)
    else:
        total = lax.psum(lax.psum_scatter(grads, "tok", scatter_dimension=0, tiled=True), "rep")
        grad_vector = shares[:, 0:9].reshape(-1)
        vec_owned = lax.psum(lax.psum_scatter(grad_vector, "tok", scatter_dimension=0, tiled=True), "rep")
    output, input_grad, entropy = pl.pallas_call(
        functools.partial(return_kernel, cap),
        out_shape=(row_block, row_block, jax.ShapeDtypeStruct((1, ROWS), BF)),
        in_specs=[VMEM] * (SD + 1),
        out_specs=(VMEM,) * 3,
        compiler_params=pltpu.CompilerParams(vmem_limit_bytes=VMEM_LIMIT),
        name="return_rows",
    )(order, *returned)

    used = jnp.any(
        positions[None, :] == (tok_index * slot_count + jnp.arange(slot_count, dtype=I32))[:, None], axis=1
    )
    owned_grad = jnp.where(used[:, None, None], total.astype(F32), 0.0)
    first_new, second_new, master_new = adam_update(
        owned_grad, master_slots, moment_one, moment_two, rate_matrix
    )
    vec_first, vec_second, vec_new = adam_update(
        vec_owned, vector_master, vector_moment_one, vector_moment_two, rate_vector
    )
    return (
        output,
        input_grad,
        owned_grad,
        first_new,
        second_new,
        master_new,
        master_new.astype(BF),
        vec_owned,
        vec_first,
        vec_second,
        vec_new,
        vec_new.astype(BF),
        entropy.reshape(-1),
        occupancy,
    )


def solution(mesh):
    placed = (
        P(("rep", "tok"), None),
        P(("rep", "tok"), None),
        P(("rep", "tok")),
        P(),
        P("tok", None, None),
        P("tok", None, None),
        P("tok", None, None),
        P("tok"),
        P("tok"),
        P("tok"),
    )
    return jax.shard_map(
        local,
        mesh=mesh,
        in_specs=placed,
        out_specs=(
            P(("rep", "tok"), None),
            P(("rep", "tok"), None),
            P("tok", None, None),
            P("tok", None, None),
            P("tok", None, None),
            P("tok", None, None),
            P("tok", None, None),
            P("tok"),
            P("tok"),
            P("tok"),
            P("tok"),
            P("tok"),
            P(("rep", "tok")),
            P(),
        ),
        check_vma=False,
    )
```

```python
import functools
import math

import jax
import jax.numpy as jnp
from jax import lax
from jax.experimental import pallas as pl
from jax.experimental.pallas import tpu as pltpu
from jax.sharding import PartitionSpec as P

D = 768
HEADS = 12
HD = 64
FF = 3072
SD = 4
CL = 128
NBLK = 96
STEP = 10
CPS = 32
WROWS = 9216
BLK = 96
ROWS = 1024
PAIRS = HEADS // 2
PW = 2 * HD
TM = 512
META = 16
VMEM_LIMIT = 63 << 20
FC = 768

norm_epsilon = 1e-06
beta_first = 0.9
beta_second = 0.999
adam_epsilon = 1e-08
weight_decay = 0.01
rate_matrix = 0.02
rate_vector = 0.2

BF = jnp.bfloat16
F32 = jnp.float32
I32 = jnp.int32

VMEM = pl.BlockSpec(memory_space=pltpu.VMEM)
SMEM = pl.BlockSpec(memory_space=pltpu.SMEM)
ANY = pl.BlockSpec(memory_space=pl.ANY)

NN = (((1,), (0,)), ((), ()))
NT = (((1,), (1,)), ((), ()))
TN = (((0,), (0,)), ((), ()))


def mm(a, b, dims=NN):
    return lax.dot_general(a, b, dims, preferred_element_type=F32)


def slot_positions(block_owner, slot_count):
    owners = block_owner[:, 0]
    blocks = owners.shape[0]
    shared = owners[:, None] == owners[None, :]
    before = (
        jnp.arange(blocks, dtype=jnp.int32)[None, :] < jnp.arange(blocks, dtype=jnp.int32)[:, None]
    )
    earlier = jnp.sum((shared & before).astype(jnp.int32), axis=1)
    return owners * slot_count + earlier


def adam_update(grad_now, weight_old, first_old, second_old, rate_step):
    first_new = beta_first * first_old + (1.0 - beta_first) * grad_now
    second_new = beta_second * second_old + (1.0 - beta_second) * grad_now * grad_now
    first_hat = first_new / (1.0 - beta_first**STEP)
    second_hat = second_new / (1.0 - beta_second**STEP)
    weight_new = weight_old - rate_step * (
        first_hat / (jnp.sqrt(second_hat) + adam_epsilon) + weight_decay * weight_old
    )
    return (first_new, second_new, weight_new)


def route_slots(order, seat, cap):
    cluster = order // CL
    rel = lax.rem(cluster, SD) ^ seat
    place = (cluster // SD) * CL + lax.rem(order, CL) + 1
    chosen = lax.broadcasted_iota(I32, (8, ROWS), 0) == rel
    chosen_low = jnp.where(chosen, 1.0, 0.0).astype(BF)
    before = lax.broadcasted_iota(I32, (ROWS, ROWS), 0) < lax.broadcasted_iota(I32, (ROWS, ROWS), 1)
    before_low = jnp.where(before, 1.0, 0.0).astype(BF)
    running = mm(chosen_low, before_low)
    rank = jnp.sum(jnp.where(chosen, running, 0.0), axis=0, keepdims=True).astype(I32)
    return rel * cap + rank, place


def slot_matrix(slots, at, cap):
    rows = lax.broadcasted_iota(I32, (cap, ROWS), 0) + at * cap
    return jnp.where(rows == slots, 1.0, 0.0).astype(BF)


def send_kernel(cap, tokens, cotangent, order, send_x, send_c, meta):
    seat = lax.rem(lax.axis_index("tok"), SD)
    slots, place = route_slots(order[...], seat, cap)
    digits = jnp.concatenate([place // CL, lax.rem(place, CL)] + [place * 0] * 6, axis=0).astype(F32).astype(BF)
    for at in range(SD):
        picked = slot_matrix(slots, at, cap)
        send_x[at] = mm(picked, tokens[...]).astype(BF)
        send_c[at] = mm(picked, cotangent[...]).astype(BF)
        coded = mm(digits, picked, NT)
        line = jnp.concatenate([coded[0:1], coded[1:2]], axis=1)
        meta[at] = jnp.broadcast_to(line, (META, D)).astype(BF)


def remote(src, dst, send_sem, recv_sem, tok, rep):
    return pltpu.make_async_remote_copy(
        src_ref=src,
        dst_ref=dst,
        send_sem=send_sem,
        recv_sem=recv_sem,
        device_id={"tok": tok, "rep": rep},
        device_id_type=pl.DeviceIdType.MESH,
    )


def loop(n, body):
    def run(i, c):
        body(i)
        return c

    lax.fori_loop(0, n, run, 0)


class Place:
    def __init__(self):
        self.me = me = lax.axis_index("tok")
        self.z = z = lax.axis_index("rep")
        core, x, y = me % 2, (me // 2) % 2, me // 4
        self.twin = me + 1 - 2 * core
        self.xn = me + 2 - 4 * x
        self.yn = me + 4 - 8 * y
        self.dn = self.xn + 4 - 8 * y
        self.side = z % 2
        self.zp = z + 1 - 2 * self.side

    def twin_of(self, tok):
        return tok + 1 - 2 * (tok % 2)

    def greet(self, peers):
        barrier = pltpu.get_barrier_semaphore()
        for tok, rep in peers:
            pl.semaphore_signal(
                barrier, inc=1, device_id={"tok": tok, "rep": rep}, device_id_type=pl.DeviceIdType.MESH
            )
        return lambda: pl.semaphore_wait(barrier, len(peers))


def seat_matrix(meta, first, rows, cap):
    hi = jnp.concatenate([meta[k, 0:8, 0:cap] for k in range(SD)], axis=1).astype(F32)[0:1]
    lo = jnp.concatenate([meta[k, 0:8, cap : 2 * cap] for k in range(SD)], axis=1).astype(F32)[0:1]
    at = (hi * CL + lo).astype(I32)
    seats = lax.broadcasted_iota(I32, (rows, SD * cap), 0) + (first + 1)
    return jnp.where(seats == at, 1.0, 0.0).astype(BF)


def seat_part(meta, k, cap):
    hi = meta[k, 0:8, 0:cap].astype(F32)[0:1]
    lo = meta[k, 0:8, cap : 2 * cap].astype(F32)[0:1]
    at = (hi * CL + lo).astype(I32)
    seats = lax.broadcasted_iota(I32, (ROWS, cap), 0) + 1
    return jnp.where(seats == at, 1.0, 0.0).astype(BF)


def seat_rows(meta, blocks, cap, to):
    def body(t):
        r0 = pl.multiple_of(t * 256, 256)
        rows = blocks[...].reshape(SD * cap, D)
        to[pl.ds(r0, 256), :] = mm(seat_matrix(meta, r0, 256, cap), rows).astype(BF)

    loop(ROWS // 256, body)


def seat_kernel(cap, blocks, meta, to):
    seat_rows(meta, blocks, cap, to)


def gather_kernel(
    cap,
    count,
    tokens_h,
    cotangent_h,
    order,
    master_h,
    vector,
    owner_of,
    slots,
    x_c,
    cot_c,
    recv_meta,
    vecs,
    b_u,
    occupancy,
    positions,
    tokens,
    cotangent,
    master,
    own,
    send_x,
    send_c,
    meta,
    recv_x,
    recv_c,
    got_meta,
    mine,
    by_z,
    by_tok,
    x_s,
    x_r,
    y_s,
    y_r,
    d_s,
    d_r,
    zx_s,
    zx_r,
    zd_s,
    zd_r,
    zxt_s,
    zxt_r,
    zdt_s,
    zdt_r,
    p_s,
    p_r,
    row_s,
    row_r,
    z_s,
    z_r,
    t_s,
    t_r,
    local_s,
):
    at = Place()
    me, z, side = at.me, at.z, at.side
    n_tok, n_rep = 8, 4
    peers = [((me + d) % n_tok, z) for d in range(1, n_tok)] + [(me, (z + d) % n_rep) for d in range(1, n_rep)]
    fetch = [
        pltpu.make_async_copy(src, dst, local_s.at[i])
        for i, (src, dst) in enumerate(((master_h, master), (tokens_h, tokens), (cotangent_h, cotangent)))
    ]
    for copy in fetch:
        copy.start()
    wait_peers = at.greet(peers)
    fetch[0].wait()

    def cast(s):
        own[s] = master[s].astype(BF)

    loop(count, cast)
    wait_peers()

    half = count // 2

    def slot(owner, s):
        return slots.at[owner * count + s]

    def to_x(s):
        return remote(own.at[s], slot(me, s), x_s.at[s], x_r.at[s], at.xn, z)

    def to_y(s):
        return remote(own.at[s], slot(me, s), y_s.at[s], y_r.at[s], at.yn, z)

    def on_y(s):
        return remote(slot(at.xn, s), slot(at.xn, s), d_s.at[s], d_r.at[s], at.yn, z)

    def x_on_z(s):
        return remote(slot(at.xn, s), slot(at.xn, s), zx_s.at[s], zx_r.at[s], me, at.zp)

    def d_on_z(s):
        return remote(slot(at.dn, s), slot(at.dn, s), zd_s.at[s], zd_r.at[s], me, at.zp)

    def x_on_zt(s):
        return remote(slot(at.xn, s), slot(at.xn, s), zxt_s.at[s], zxt_r.at[s], at.twin, at.zp)

    def d_on_zt(s):
        return remote(slot(at.dn, s), slot(at.dn, s), zdt_s.at[s], zdt_r.at[s], at.twin, at.zp)

    owners = (me, at.xn, at.yn, at.dn)

    def to_twin(q, s):
        src = own.at[s] if q == 0 else slot(owners[q], s)
        return remote(src, slot(owners[q], s), p_s.at[q, s], p_r.at[q, s], at.twin, z)

    def near(j):
        return (half + 1) * side + j

    def far(j):
        return (half + 1) * (1 - side) + j

    loop(half, lambda j: to_x(near(j)).start())
    to_x(half).start()
    for s in range(3):
        to_y(s).start()
    loop(count, lambda s: to_twin(0, s).start())
    keep = pltpu.make_async_copy(own, slots.at[pl.ds(me * count, count)], local_s.at[3])
    keep.start()
    fetch[1].wait()
    fetch[2].wait()

    seat = me % SD
    slot_of, place = route_slots(order[...], seat, cap)
    digits = jnp.concatenate([place // CL, lax.rem(place, CL)] + [place * 0] * 6, axis=0).astype(F32).astype(BF)
    for k in range(SD):
        picked = slot_matrix(slot_of, k, cap)
        send_x[k] = mm(picked, tokens[...]).astype(BF)
        send_c[k] = mm(picked, cotangent[...]).astype(BF)
        coded = mm(digits, picked, NT)
        line = jnp.concatenate([coded[0:1], coded[1:2]], axis=1)
        meta[k] = jnp.broadcast_to(line, (META, D)).astype(BF)
    seats = (me, at.twin, at.xn, at.twin_of(at.xn))
    rows_of = ((meta, got_meta), (send_x, recv_x), (send_c, recv_c))

    def row_copy(i, k):
        src, dst = rows_of[i]
        return remote(src.at[k], dst.at[k], row_s.at[i, k], row_r.at[i, k], seats[k], z)

    for i in range(3):
        src, dst = rows_of[i]
        for k in (2, 3, 1):
            row_copy(i, k).start()
        dst[0] = src[0]

    residue = lax.rem(me // SD * CPS + order[...] // CL, n_tok)
    hit = lax.broadcasted_iota(I32, (128, ROWS), 0) == residue
    for i in range(9):
        mine[i : i + 1] = vector[i * 128 : (i + 1) * 128].reshape(1, 128).astype(BF).astype(F32)
    block_row = lax.broadcasted_iota(I32, (NBLK, NBLK), 0)
    block_col = lax.broadcasted_iota(I32, (NBLK, NBLK), 1)
    by_col = owner_of[...].astype(F32)
    by_row = lane_sum(jnp.where(block_row == block_col, by_col, 0.0))
    earlier = jnp.where((by_row == by_col) & (block_row < block_col), 1.0, 0.0)
    positions[...] = (by_col * count + jnp.sum(earlier, axis=0, keepdims=True)).astype(I32)
    by_z[0] = mm(jnp.ones((8, ROWS), BF), jnp.where(hit, 1.0, 0.0).astype(BF), NT)

    def z_copy(d):
        return remote(by_z.at[0], by_z.at[d], z_s.at[d], z_r.at[d], me, (z + d) % n_rep)

    def t_copy(d):
        return remote(mine, by_tok.at[d], t_s.at[d], t_r.at[d], (me + d) % n_tok, z)

    for d in range(1, n_rep):
        z_copy(d).start()
    for d in range(1, n_rep):
        z_copy(d).wait()
    mine[16:24] = by_z[0] + by_z[1] + by_z[2] + by_z[3]
    for d in range(1, n_tok):
        t_copy(d).start()

    def x_here(s):
        to_x_in(s).wait_recv()
        on_y(s).start()
        to_twin(1, s).start()

    def to_x_in(s):
        return remote(own.at[s], slot(at.xn, s), x_s.at[s], x_r.at[s], at.xn, z)

    def y_in(s):
        return remote(own.at[s], slot(at.yn, s), y_s.at[s], y_r.at[s], at.yn, z)

    def d_in(s):
        return remote(own.at[s], slot(at.dn, s), d_s.at[s], d_r.at[s], at.yn, z)

    def first(j):
        x_here(near(j))
        x_on_z(near(j)).start()
        x_on_zt(near(j)).start()
        to_y(3 + j).start()

    loop(half, first)
    x_here(half)
    for s in range(3 + half, count):
        to_y(s).start()

    def y_here(s):
        y_in(s).wait_recv()
        to_twin(2, s).start()

    def second(j):
        y_here(j)
        d_in(near(j)).wait_recv()
        d_on_z(near(j)).start()
        d_on_zt(near(j)).start()
        to_twin(3, near(j)).start()

    loop(half, second)
    d_in(half).wait_recv()
    to_twin(3, half).start()
    loop(count - half, lambda j: y_here(half + j))
    for i in (0, 1):
        for k in (2, 3, 1):
            row_copy(i, k).wait_recv()
    recv_meta[...] = got_meta[...]
    seat_rows(got_meta, recv_x, cap, x_c)

    def third(j):
        x_on_z(far(j)).wait_recv()
        x_on_zt(far(j)).wait_recv()
        d_on_z(far(j)).wait_recv()
        d_on_zt(far(j)).wait_recv()

    loop(half, third)

    by_tok[0] = mine[...]
    for d in range(1, n_tok):
        t_copy(d).wait()
    for owner in range(n_tok):
        share = by_tok[(me + n_tok - owner) % n_tok]
        occupancy[owner : owner + 1, :] = share[16:17, 0:n_tok].astype(I32)
        for i in range(9):
            chunk = owner * 9 + i
            row, lane = chunk // 6, chunk % 6 * 128
            if row < 8:
                vecs[row : row + 1, lane : lane + 128] = share[i : i + 1]
            else:
                lane += (row - 8) * D
                b_u[:, lane : lane + 128] = share[i : i + 1]
    for k in (2, 3, 1):
        row_copy(2, k).wait_recv()
    seat_rows(got_meta, recv_c, cap, cot_c)
    for i in range(3):
        for k in (2, 3, 1):
            row_copy(i, k).wait_send()
    keep.wait()

    def sent_half(j):
        to_x(near(j)).wait_send()
        on_y(near(j)).wait_send()
        x_on_z(near(j)).wait_send()
        d_on_z(near(j)).wait_send()
        x_on_zt(near(j)).wait_send()
        d_on_zt(near(j)).wait_send()
        to_twin(1, near(j)).wait()
        to_twin(3, near(j)).wait()

    loop(half, sent_half)
    to_x(half).wait_send()
    on_y(half).wait_send()
    to_twin(1, half).wait()
    to_twin(3, half).wait()

    def sent(s):
        to_y(s).wait_send()
        to_twin(0, s).wait()
        to_twin(2, s).wait()

    loop(count, sent)


def gather_all(cap, tokens, cotangent, order, master, vector, block_owner):
    count = master.shape[0]
    rows = jax.ShapeDtypeStruct((ROWS, D), BF)
    dma = pltpu.SemaphoreType.DMA
    block = pltpu.VMEM((SD, cap, D), BF)
    meta = pltpu.VMEM((SD, META, D), BF)
    return pl.pallas_call(
        functools.partial(gather_kernel, cap, count),
        out_shape=(
            jax.ShapeDtypeStruct((8 * count, BLK, D), BF),
            rows,
            rows,
            jax.ShapeDtypeStruct((SD, META, D), BF),
            jax.ShapeDtypeStruct((8, D), F32),
            jax.ShapeDtypeStruct((1, FF), F32),
            jax.ShapeDtypeStruct((8, 8), I32),
            jax.ShapeDtypeStruct((1, NBLK), I32),
        ),
        in_specs=[ANY, ANY, VMEM, ANY, VMEM, VMEM],
        out_specs=(ANY,) + (VMEM,) * 7,
        scratch_shapes=[
            pltpu.VMEM((ROWS, D), BF),
            pltpu.VMEM((ROWS, D), BF),
            pltpu.VMEM((count, BLK, D), F32),
            pltpu.VMEM((count, BLK, D), BF),
            block,
            block,
            meta,
            block,
            block,
            meta,
            pltpu.VMEM((24, 128), F32),
            pltpu.VMEM((4, 8, 128), F32),
            pltpu.VMEM((8, 24, 128), F32),
        ]
        + [dma((count,))] * 14
        + [dma((4, count))] * 2
        + [dma((3, SD))] * 2
        + [dma((4,))] * 2
        + [dma((8,))] * 2
        + [dma((4,))],
        compiler_params=pltpu.CompilerParams(collective_id=0, has_side_effects=True, vmem_limit_bytes=VMEM_LIMIT),
        name="gather",
    )(tokens, cotangent, order, master, vector, block_owner.reshape(1, NBLK))


def return_kernel(cap, order, *refs):
    blocks, (out, ing, entropy) = refs[:SD], refs[SD:]
    seat = lax.rem(lax.axis_index("tok"), SD)
    slots, _ = route_slots(order[...], seat, cap)
    picked = jnp.concatenate([slot_matrix(slots, at, cap) for at in range(SD)], axis=0)
    for to, first in ((out, 0), (ing, cap)):
        rows = jnp.concatenate([block[first : first + cap, :] for block in blocks], axis=0)
        to[...] = mm(picked, rows, TN).astype(BF)
    line = jnp.concatenate([block[2 * cap : 2 * cap + 8, 0:cap] for block in blocks], axis=1)
    entropy[...] = mm(line, picked)[0:1].astype(BF)


def swap_blocks(blocks):
    n = lax.axis_size("tok")
    parts = [blocks[0]]
    for k in range(1, SD):
        parts.append(lax.ppermute(blocks[k], "tok", [(i, i ^ k) for i in range(n)]))
    return parts


def reduce_kernel(
    count,
    split,
    grads,
    vec,
    total,
    vec_out,
    a,
    tw,
    rd,
    rx,
    ry,
    o,
    rz1,
    pz,
    rz2,
    fz,
    vt,
    va,
    vb,
    vc,
    a_l,
    keep_l,
    p_s,
    p_r,
    d_s,
    d_r,
    x_s,
    x_r,
    y_s,
    y_r,
    z1_s,
    z1_r,
    z2_s,
    z2_r,
    z3_s,
    z3_r,
    t_s,
    t_r,
    v_s,
    v_r,
):
    at = Place()
    me, z = at.me, at.z
    n_tok, n_rep = 8, 4
    peers = [((me + d) % n_tok, z) for d in range(1, n_tok)] + [(me, (z + d) % n_rep) for d in range(1, n_rep)]
    wait_peers = at.greet(peers)
    owners = (me, at.xn, at.yn, at.dn)

    def load(q):
        return pltpu.make_async_copy(grads.at[pl.ds(owners[q] * count, count)], a.at[q], a_l.at[q])

    for q in (3, 1, 2, 0):
        load(q).start()
    wait_peers()

    def to_twin(q, s):
        src = grads.at[at.twin_of(owners[q]) * count + s]
        return remote(src, tw.at[q, s], p_s.at[q, s], p_r.at[q, s], at.twin, z)

    def d_y(s):
        return remote(a.at[3, s], rd.at[s], d_s.at[s], d_r.at[s], at.yn, z)

    def d_x(s):
        return remote(a.at[3, s], rd.at[s], d_s.at[s], d_r.at[s], at.xn, z)

    def to_x(s):
        return remote(a.at[1, s], rx.at[s], x_s.at[s], x_r.at[s], at.xn, z)

    def to_y(s):
        return remote(a.at[2, s], ry.at[s], y_s.at[s], y_r.at[s], at.yn, z)

    def z_in(s):
        return remote(o.at[s], rz1.at[s], z1_s.at[s], z1_r.at[s], me, at.zp)

    def z_swap(s):
        return remote(pz.at[s], rz2.at[s], z2_s.at[s], z2_r.at[s], me, n_rep - 1 - z)

    def z_out(s):
        return remote(fz.at[s], fz.at[s], z3_s.at[s], z3_r.at[s], me, at.zp)

    def keep(s):
        return pltpu.make_async_copy(fz.at[s], total.at[s], keep_l.at[s])

    def f32(ref, *index):
        return ref[index].astype(F32)

    loop(count, lambda s: to_twin(3, s).start())

    def plane_pieces(s):
        to_twin(2, s).start()
        to_twin(1, s).start()

    def others(s):
        plane_pieces(s + 1)
        to_twin(0, s).start()

    plane_pieces(0)
    loop(count - 1, others)
    to_twin(0, count - 1).start()

    def v_tok(d):
        return remote(vec.at[(me + d) % n_tok], vt.at[d], t_s.at[d], t_r.at[d], (me + d) % n_tok, z)

    def v_rep(i, src):
        return remote(src, vb.at[i], v_s.at[i], v_r.at[i], me, at.zp if i == 0 else (z + 2) % n_rep)

    for d in range(1, n_tok):
        v_tok(d).start()

    load(3).wait()

    def join(q, s):
        to_twin(q, s).wait_recv()
        return f32(a, q, s) + f32(tw, q, s)

    def diagonal(s, send):
        a[3, s] = join(3, s).astype(BF)
        send(s).start()

    loop(split, lambda s: diagonal(s, d_y))
    loop(count - split, lambda j: diagonal(split + j, d_x))

    v_sum = vec[me]
    for d in range(1, n_tok):
        v_tok(d).wait()
        v_sum = v_sum + vt[d]
    va[...] = v_sum
    v_rep(0, va).start()

    load(1).wait()
    load(2).wait()

    def plane_y(s):
        a[2, s] = join(2, s).astype(BF)
        to_y(s).start()
        d_y(s).wait_recv()
        a[1, s] = (join(1, s) + f32(rd, s)).astype(BF)
        to_x(s).start()

    def plane_x(s):
        a[1, s] = join(1, s).astype(BF)
        to_x(s).start()
        d_x(s).wait_recv()
        a[2, s] = (join(2, s) + f32(rd, s)).astype(BF)
        to_y(s).start()

    loop(split, plane_y)
    loop(count - split, lambda j: plane_x(split + j))

    v_rep(0, va).wait()
    vc[...] = va[...] + vb[0]
    v_rep(1, vc).start()
    load(0).wait()
    inner = (z == 1) | (z == 2)
    outer = (z == 0) | (z == 3)

    def planes(i):
        @pl.when(i < count)
        def _():
            s = i
            to_x(s).wait_recv()
            to_y(s).wait_recv()
            o[s] = (join(0, s) + f32(rx, s) + f32(ry, s)).astype(BF)

        @pl.when(outer & (i < count))
        def _():
            z_in(i).start()

        @pl.when(inner & (i >= 1) & (i < count + 1))
        def _():
            s = i - 1
            z_in(s).wait_recv()
            pz[s] = (f32(o, s) + f32(rz1, s)).astype(BF)
            z_swap(s).start()

        @pl.when(inner & (i >= 2) & (i < count + 2))
        def _():
            s = i - 2
            z_swap(s).wait_recv()
            fz[s] = (f32(pz, s) + f32(rz2, s)).astype(BF)
            z_out(s).start()
            keep(s).start()

        @pl.when(outer & (i >= 3))
        def _():
            s = i - 3
            z_out(s).wait_recv()
            keep(s).start()

    loop(count + 3, planes)
    v_rep(1, vc).wait()
    vec_out[...] = vc[...] + vb[1]

    def sent(s):
        for q in range(4):
            to_twin(q, s).wait_send()
        d_y(s).wait_send()
        to_x(s).wait_send()
        to_y(s).wait_send()
        keep(s).wait()

    loop(count, sent)

    @pl.when(outer)
    def _():
        loop(count, lambda s: z_in(s).wait_send())

    @pl.when(inner)
    def _():
        def back(s):
            z_swap(s).wait_send()
            z_out(s).wait_send()

        loop(count, back)


def reduce_all(grads, shares, count):
    dma = pltpu.SemaphoreType.DMA
    part = pltpu.VMEM((count, BLK, D), BF)
    whole = pltpu.VMEM((4, count, BLK, D), BF)
    line = pltpu.VMEM((16, 128), F32)
    total, vec = pl.pallas_call(
        functools.partial(reduce_kernel, count, count - count // 4),
        out_shape=(
            jax.ShapeDtypeStruct((count, BLK, D), BF),
            jax.ShapeDtypeStruct((16, 128), F32),
        ),
        in_specs=[ANY, VMEM],
        out_specs=(ANY, VMEM),
        scratch_shapes=[whole, whole]
        + [part] * 8
        + [pltpu.VMEM((8, 16, 128), F32), line, pltpu.VMEM((2, 16, 128), F32), line]
        + [dma((4,)), dma((count,))]
        + [dma((4, count))] * 2
        + [dma((count,))] * 12
        + [dma((8,))] * 2
        + [dma((2,))] * 2,
        compiler_params=pltpu.CompilerParams(
            collective_id=1, has_side_effects=True, vmem_limit_bytes=VMEM_LIMIT
        ),
        name="reduce",
    )(grads, shares)
    return total, vec[0:9].reshape(-1)


V_BQ, V_BV, V_BO, V_BD, V_G1, V_C1, V_G2, V_C2 = range(8)


def inverse(x):
    r = pl.reciprocal(x, approx=True)
    return r * (2.0 - x * r)


def erf_parts(v):
    t = inverse(1.0 + (0.3275911 / math.sqrt(2.0)) * jnp.abs(v))
    e = jnp.exp2((v * v) * (-0.5 / math.log(2.0)))
    poly = 0.5 * 1.061405429
    for c in (-1.453152027, 1.421413741, -0.284496736, 0.254829592):
        poly = poly * t + 0.5 * c
    tail = poly * (t * e)
    return jnp.where(v >= 0.0, 1.0 - tail, tail), e


def lane_sum(x):
    return jnp.sum(x, axis=1, keepdims=True)


def gelu_parts(v):
    phi, e = erf_parts(v)
    return v * phi, phi + v * (e * (1.0 / math.sqrt(2.0 * math.pi)))


def chain_kernel(
    cap,
    pos,
    slots,
    vecs,
    b_u,
    x_h,
    cot_h,
    meta,
    back_0,
    back_1,
    back_2,
    back_3,
    shares,
    heads_h,
    act_h,
    d_up_h,
    d_q_h,
    d_k_h,
    d_v_h,
    d_proj_h,
    hid_h,
    d_br_h,
    wqkv,
    w,
    x_c,
    heads,
    act,
    d_up,
    d_q,
    d_k,
    d_v,
    d_proj,
    hid,
    d_br,
    out_c,
    ing_c,
    ent,
    gvec,
    g_bu,
    q_t,
    k_t,
    v_t,
    p_t,
    dh_t,
    n1_t,
    hid_t,
    w_sem,
    x_sem,
    o_sem,
):
    inv = 1.0 / math.sqrt(HD)

    def qkv_copy(b, part):
        rows, cols = pl.ds(b * BLK, BLK), pl.ds(part * D, D)
        return pltpu.make_async_copy(slots.at[pos[part * 8 + b]], wqkv.at[rows, cols], w_sem)

    def w_copy(b):
        return pltpu.make_async_copy(slots.at[pos[24 + b]], w.at[pl.ds(b * BLK, BLK)], w_sem)

    get_x = pltpu.make_async_copy(x_h, x_c, x_sem.at[0])
    get_cot = pltpu.make_async_copy(cot_h, d_br, x_sem.at[1])
    get_x.start()
    for part in range(3):
        loop(8, lambda b, part=part: qkv_copy(b, part).start())
    loop(NBLK - 24, lambda b: w_copy(b).start())
    get_cot.start()
    gvec[...] = jnp.zeros_like(gvec)
    g_bu[...] = jnp.zeros_like(g_bu)
    shares[...] = jnp.zeros_like(shares)
    get_x.wait()
    for part in range(3):
        loop(8, lambda b, part=part: qkv_copy(b, part).wait())
    loop(NBLK - 24, lambda b: w_copy(b).wait())
    get_cot.wait()

    wo = w.at[pl.ds(0, D)]
    wu = w.at[pl.ds(D, FF)]
    wd = w.at[pl.ds(D + FF, FF)]

    lane = lax.broadcasted_iota(I32, (1, PW), 1)
    m0 = jnp.where(lane < HD, 1.0, 0.0).astype(BF)
    m1 = jnp.where(lane < HD, 0.0, 1.0).astype(BF)
    first_half = lax.broadcasted_iota(I32, (CL, PW), 1) < HD

    def apart(pair):
        return jnp.concatenate([pair * m0, pair * m1], axis=0)

    def vec(i):
        return vecs[i : i + 1, :]

    def add_vec(i, value):
        gvec[i : i + 1, :] += jnp.sum(value, axis=0, keepdims=True)

    saved = (
        (heads, heads_h),
        (act, act_h),
        (d_up, d_up_h),
        (d_q, d_q_h),
        (d_k, d_k_h),
        (d_v, d_v_h),
        (d_proj, d_proj_h),
        (hid, hid_h),
        (d_br, d_br_h),
    )

    def save(t, i):
        rows = pl.ds(pl.multiple_of(t * TM, TM), TM)
        src, dst = saved[i]
        return pltpu.make_async_copy(src.at[rows], dst.at[rows], o_sem.at[i])

    def tile(t):
        r0 = pl.multiple_of(t * TM, TM)
        rows = pl.ds(r0, TM)
        qkv = mm(x_c[rows, :], wqkv[...])
        q_t[...] = ((qkv[:, 0:D] + vec(V_BQ)).astype(BF).astype(F32) * inv).astype(BF)
        k_t[...] = qkv[:, D : 2 * D].astype(BF)
        v_t[...] = (qkv[:, 2 * D :] + vec(V_BV)).astype(BF)

        def attend(c):
            cr = pl.ds(pl.multiple_of(c * CL, CL), CL)
            gr = pl.ds(pl.multiple_of(r0 + c * CL, CL), CL)
            total = jnp.zeros((1, CL), F32)
            for p in range(PAIRS):
                ps = slice(p * PW, (p + 1) * PW)
                scores = mm(apart(k_t[cr, ps]), q_t[cr, ps], NT)
                halves = []
                for h in range(2):
                    sh = scores[h * CL : (h + 1) * CL]
                    sh = sh - jnp.max(sh, axis=0, keepdims=True)
                    e = jnp.exp(sh)
                    tot = jnp.sum(e, axis=0, keepdims=True)
                    r = inverse(tot)
                    total += jnp.log(tot) - jnp.sum(e * sh, axis=0, keepdims=True) * r
                    halves.append((e * r).astype(BF))
                weights = jnp.concatenate(halves, axis=0)
                p_t[c, p] = weights
                heads[gr, ps] = mm(weights, apart(v_t[cr, ps]), TN).astype(BF)
            ent[:, gr] = jnp.broadcast_to(total * (1.0 / HEADS), (8, CL))

        loop(TM // CL, attend)

        r1 = x_c[rows, :].astype(F32) + mm(heads[rows, :], wo[...]) + vec(V_BO)
        c1 = r1 - lane_sum(r1) * (1.0 / D)
        rs1 = lax.rsqrt(lane_sum(c1 * c1) * (1.0 / D) + norm_epsilon)
        n1 = c1 * rs1
        hidden = n1 * vec(V_G1) + vec(V_C1)
        hid[rows, :] = hidden.astype(BF)
        n1_t[...] = n1
        hid_t[...] = hidden

        def widen(f):
            fs = pl.ds(pl.multiple_of(f * FC, FC), FC)
            g, g_slope = gelu_parts(mm(hid[rows, :], wu[fs, :], NT) + b_u[:, fs])
            act[rows, fs] = g.astype(BF)
            d_up[rows, fs] = g_slope.astype(BF)

        loop(FF // FC, widen)
        r2 = hid_t[...] + mm(act[rows, :], wd[...]) + vec(V_BD)
        c2 = r2 - lane_sum(r2) * (1.0 / D)
        rs2 = lax.rsqrt(lane_sum(c2 * c2) * (1.0 / D) + norm_epsilon)
        n2 = c2 * rs2
        out_c[rows, :] = (n2 * vec(V_G2) + vec(V_C2)).astype(BF)

        e2 = d_br[rows, :].astype(F32)
        add_vec(V_G2, e2 * n2)
        add_vec(V_C2, e2)
        eg = e2 * vec(V_G2)
        d_r2 = rs2 * (eg - lane_sum(eg) * (1.0 / D) - n2 * (lane_sum(eg * n2) * (1.0 / D)))
        d_br[rows, :] = d_r2.astype(BF)
        add_vec(V_BD, d_br[rows, :].astype(F32))
        hid_t[...] = d_r2

        def widen_back(f):
            fs = pl.ds(pl.multiple_of(f * FC, FC), FC)
            du = (mm(d_br[rows, :], wd[fs, :], NT) * d_up[rows, fs].astype(F32)).astype(BF)
            d_up[rows, fs] = du
            g_bu[:, fs] += jnp.sum(du.astype(F32), axis=0, keepdims=True)

        loop(FF // FC, widen_back)
        n1 = n1_t[...]
        d_h = hid_t[...] + mm(d_up[rows, :], wu[...])
        add_vec(V_G1, d_h * n1)
        add_vec(V_C1, d_h)
        eg = d_h * vec(V_G1)
        d_r1 = rs1 * (eg - lane_sum(eg) * (1.0 / D) - n1 * (lane_sum(eg * n1) * (1.0 / D)))
        d_proj[rows, :] = d_r1.astype(BF)
        hid_t[...] = d_r1
        add_vec(V_BO, d_proj[rows, :].astype(F32))
        dh_t[...] = mm(d_proj[rows, :], wo[...], NT).astype(BF)

        def attend_back(c):
            cr = pl.ds(pl.multiple_of(c * CL, CL), CL)
            gr = pl.ds(pl.multiple_of(r0 + c * CL, CL), CL)
            for p in range(PAIRS):
                ps = slice(p * PW, (p + 1) * PW)
                dh = dh_t[cr, ps]
                weights = p_t[c, p]
                d_w = mm(apart(v_t[cr, ps]), dh, NT)
                halves = []
                for h in range(2):
                    wh = weights[h * CL : (h + 1) * CL].astype(F32)
                    dwh = d_w[h * CL : (h + 1) * CL]
                    halves.append((wh * (dwh - jnp.sum(dwh * wh, axis=0, keepdims=True))).astype(BF))
                d_s = jnp.concatenate(halves, axis=0)
                d_q[gr, ps] = (mm(d_s, apart(k_t[cr, ps]), TN) * inv).astype(BF)
                dk = mm(d_s, q_t[cr, ps])
                d_k[gr, ps] = jnp.where(first_half, dk[0:CL], dk[CL:]).astype(BF)
                dv = mm(weights, dh)
                d_v[gr, ps] = jnp.where(first_half, dv[0:CL], dv[CL:]).astype(BF)

        loop(TM // CL, attend_back)
        add_vec(V_BQ, d_q[rows, :].astype(F32))
        add_vec(V_BV, d_v[rows, :].astype(F32))
        d_qkv = jnp.concatenate([d_q[rows, :], d_k[rows, :], d_v[rows, :]], axis=1)
        d_x = mm(d_qkv, wqkv[...], NT)
        ing_c[rows, :] = (hid_t[...] + d_x.astype(BF).astype(F32)).astype(BF)
        for i in range(len(saved)):
            save(t, i).start()

    loop(ROWS // TM, tile)

    for k, back in enumerate((back_0, back_1, back_2, back_3)):
        own = seat_part(meta, k, cap)
        back[0:cap, :] = mm(own, out_c[...], TN).astype(BF)
        back[cap : 2 * cap, :] = mm(own, ing_c[...], TN).astype(BF)
        line = mm(ent[...].astype(BF), own)
        back[2 * cap :, :] = jnp.concatenate([line, line], axis=1)[0:1].astype(BF) * jnp.ones((META, 1), BF)

    for chunk in range(72):
        row, lane = chunk // 6, chunk % 6 * 128
        if row < 8:
            part = gvec[row : row + 1, lane : lane + 128]
        else:
            lane += (row - 8) * D
            part = g_bu[:, lane : lane + 128]
        shares[chunk // 9, chunk % 9 : chunk % 9 + 1, :] = part

    def saved_all(t):
        for i in range(len(saved)):
            save(t, i).wait()

    loop(ROWS // TM, saved_all)


def chain(cap, positions, slots, vecs, b_u, x_c, cot_c, meta):
    rows = jax.ShapeDtypeStruct((ROWS, D), BF)
    wide = jax.ShapeDtypeStruct((ROWS, FF), BF)
    back = jax.ShapeDtypeStruct((2 * cap + META, D), BF)
    r_v, w_v, t_v, t_f = (pltpu.VMEM(shape, kind) for shape, kind in (
        ((ROWS, D), BF), ((ROWS, FF), BF), ((TM, D), BF), ((TM, D), F32)
    ))
    return pl.pallas_call(
        functools.partial(chain_kernel, cap),
        out_shape=(back,) * SD + (jax.ShapeDtypeStruct((8, 16, 128), F32), rows, wide, wide) + (rows,) * 6,
        in_specs=[SMEM, ANY, VMEM, VMEM, ANY, ANY, VMEM],
        out_specs=(VMEM,) * (SD + 1) + (ANY,) * 9,
        scratch_shapes=[
            pltpu.VMEM((D, 3 * D), BF),
            pltpu.VMEM((WROWS - 3 * D, D), BF),
            r_v,
            r_v,
            w_v,
            w_v,
            r_v,
            r_v,
            r_v,
            r_v,
            r_v,
            r_v,
            r_v,
            r_v,
            pltpu.VMEM((8, ROWS), F32),
            pltpu.VMEM((8, D), F32),
            pltpu.VMEM((1, FF), F32),
            t_v,
            t_v,
            t_v,
            pltpu.VMEM((TM // CL, PAIRS, 2 * CL, CL), BF),
            t_v,
            t_f,
            t_f,
            pltpu.SemaphoreType.DMA,
            pltpu.SemaphoreType.DMA((2,)),
            pltpu.SemaphoreType.DMA((9,)),
        ],
        compiler_params=pltpu.CompilerParams(vmem_limit_bytes=VMEM_LIMIT),
        name="layer",
    )(positions, slots, vecs, b_u, x_c, cot_c, meta)


WC = 4 * BLK


def weight_kernel(
    pos,
    x_h,
    heads_h,
    act_h,
    d_up_h,
    d_q_h,
    d_k_h,
    d_v_h,
    d_proj_h,
    hid_h,
    d_br_h,
    grads,
    x_c,
    heads,
    act,
    d_up,
    d_q,
    d_k,
    d_v,
    d_proj,
    hid,
    d_br,
    stage,
    i_sem,
    g_sem,
):
    refs = (
        (x_h, x_c),
        (d_q_h, d_q),
        (d_k_h, d_k),
        (d_v_h, d_v),
        (heads_h, heads),
        (d_proj_h, d_proj),
        (hid_h, hid),
        (d_up_h, d_up),
        (d_br_h, d_br),
        (act_h, act),
    )
    fetch = [pltpu.make_async_copy(src, dst, i_sem.at[i]) for i, (src, dst) in enumerate(refs)]
    for copy in fetch:
        copy.start()

    per = WC // BLK

    def g_copy(chunk, j, at):
        return pltpu.make_async_copy(
            stage.at[at, pl.ds(j * BLK, BLK)], grads.at[pos[chunk * per + j]], g_sem.at[at]
        )

    def put(chunk, left, right):
        at = lax.rem(chunk, 2)

        @pl.when(chunk >= 2)
        def _():
            for j in range(per):
                g_copy(chunk - 2, j, at).wait()

        stage[at] = mm(left, right, TN).astype(BF)
        for j in range(per):
            g_copy(chunk, j, at).start()

    first = 0
    for left, right, needs in (
        (x_c, d_q, (0, 1)),
        (x_c, d_k, (2,)),
        (x_c, d_v, (3,)),
        (heads, d_proj, (4, 5)),
        (d_up, hid, (6, 7)),
        (act, d_br, (8, 9)),
    ):
        for i in needs:
            fetch[i].wait()

        def body(j, left=left, right=right, first=first):
            put(first + j, left[:, pl.ds(pl.multiple_of(j * WC, WC), WC)], right[...])

        loop(left.shape[1] // WC, body)
        first += left.shape[1] // WC
    for chunk in (first - 2, first - 1):
        for j in range(per):
            g_copy(chunk, j, chunk % 2).wait()


def weight_grads_of(total_slots, positions, x_c, saved):
    r_v, w_v = pltpu.VMEM((ROWS, D), BF), pltpu.VMEM((ROWS, FF), BF)
    return pl.pallas_call(
        weight_kernel,
        out_shape=jax.ShapeDtypeStruct((total_slots, BLK, D), BF),
        in_specs=[SMEM] + [ANY] * 10,
        out_specs=ANY,
        scratch_shapes=[r_v, r_v, w_v, w_v]
        + [r_v] * 6
        + [
            pltpu.VMEM((2, WC, D), BF),
            pltpu.SemaphoreType.DMA((10,)),
            pltpu.SemaphoreType.DMA((2,)),
        ],
        compiler_params=pltpu.CompilerParams(vmem_limit_bytes=VMEM_LIMIT),
        cost_estimate=pl.CostEstimate(flops=2 * ROWS * WROWS * D, bytes_accessed=40 << 20, transcendentals=0),
        name="weight_grads",
    )(positions, x_c, *saved)


def local(
    tokens,
    cotangent,
    cluster_order,
    block_owner,
    master_slots,
    moment_one,
    moment_two,
    vector_master,
    vector_moment_one,
    vector_moment_two,
):
    tok_count = lax.axis_size("tok")
    tok_index = lax.axis_index("tok")
    slot_count = master_slots.shape[0]
    cap = tok_count // SD * (max(1, CPS // tok_count) * 3 * CL // (2 * SD))
    total_slots = tok_count * slot_count
    order = cluster_order.reshape(1, ROWS)

    block = jax.ShapeDtypeStruct((SD, cap, D), BF)
    meta_shape = jax.ShapeDtypeStruct((SD, META, D), BF)
    row_block = jax.ShapeDtypeStruct((ROWS, D), BF)
    four_planes = tok_count == 8 and lax.axis_size("rep") == 4
    if four_planes:
        slots_low, x_c, cot_c, recv_meta, vecs, b_u, occupancy, positions = gather_all(
            cap, tokens, cotangent, order, master_slots, vector_master, block_owner
        )
        positions = positions.reshape(NBLK)
    else:
        positions = slot_positions(block_owner, slot_count)
        slots_low = lax.all_gather(master_slots.astype(BF), "tok", axis=0, tiled=True)
        vectors = lax.all_gather(vector_master.astype(BF), "tok", axis=0, tiled=True).astype(F32)
        vecs, b_u = vectors[: 8 * D].reshape(8, D), vectors[8 * D :].reshape(1, FF)
        cluster = tok_index // SD * CPS + cluster_order // CL
        target = cluster % tok_count
        chosen = target[None, :] == jnp.arange(tok_count, dtype=jnp.int32)[:, None]
        sent_counts = jnp.sum(chosen.astype(F32), axis=1)
        own_row = (jnp.arange(tok_count, dtype=jnp.int32) == tok_index).astype(F32)
        occupancy = lax.psum(own_row[:, None] * sent_counts[None, :], ("tok", "rep")).astype(jnp.int32)
        send_x, send_c, meta = pl.pallas_call(
            functools.partial(send_kernel, cap),
            out_shape=(block, block, meta_shape),
            in_specs=[VMEM] * 3,
            out_specs=(VMEM,) * 3,
            compiler_params=pltpu.CompilerParams(vmem_limit_bytes=VMEM_LIMIT),
            name="send_rows",
        )(tokens, cotangent, order)
        recv_x, recv_c, recv_meta = (jnp.stack(swap_blocks(b)) for b in (send_x, send_c, meta))
        x_c, cot_c = (
            pl.pallas_call(
                functools.partial(seat_kernel, cap),
                out_shape=row_block,
                in_specs=[VMEM] * 2,
                out_specs=VMEM,
                compiler_params=pltpu.CompilerParams(vmem_limit_bytes=VMEM_LIMIT),
                name="seat_rows",
            )(rows, recv_meta)
            for rows in (recv_x, recv_c)
        )

    *backs, shares, heads, act, d_up, d_q, d_k, d_v, d_proj, hid, d_br = chain(
        cap, positions, slots_low, vecs, b_u, x_c, cot_c, recv_meta
    )
    returned = swap_blocks(backs)
    grads = weight_grads_of(
        total_slots, positions, x_c, (heads, act, d_up, d_q, d_k, d_v, d_proj, hid, d_br)
    )
    if four_planes:
        total, vec_owned = reduce_all(grads, shares, slot_count)
    else:
        total = lax.psum(lax.psum_scatter(grads, "tok", scatter_dimension=0, tiled=True), "rep")
        grad_vector = shares[:, 0:9].reshape(-1)
        vec_owned = lax.psum(lax.psum_scatter(grad_vector, "tok", scatter_dimension=0, tiled=True), "rep")
    output, input_grad, entropy = pl.pallas_call(
        functools.partial(return_kernel, cap),
        out_shape=(row_block, row_block, jax.ShapeDtypeStruct((1, ROWS), BF)),
        in_specs=[VMEM] * (SD + 1),
        out_specs=(VMEM,) * 3,
        compiler_params=pltpu.CompilerParams(vmem_limit_bytes=VMEM_LIMIT),
        name="return_rows",
    )(order, *returned)

    used = jnp.any(
        positions[None, :] == (tok_index * slot_count + jnp.arange(slot_count, dtype=I32))[:, None], axis=1
    )
    owned_grad = jnp.where(used[:, None, None], total.astype(F32), 0.0)
    first_new, second_new, master_new = adam_update(
        owned_grad, master_slots, moment_one, moment_two, rate_matrix
    )
    vec_first, vec_second, vec_new = adam_update(
        vec_owned, vector_master, vector_moment_one, vector_moment_two, rate_vector
    )
    return (
        output,
        input_grad,
        owned_grad,
        first_new,
        second_new,
        master_new,
        master_new.astype(BF),
        vec_owned,
        vec_first,
        vec_second,
        vec_new,
        vec_new.astype(BF),
        entropy.reshape(-1),
        occupancy,
    )


def solution(mesh):
    placed = (
        P(("rep", "tok"), None),
        P(("rep", "tok"), None),
        P(("rep", "tok")),
        P(),
        P("tok", None, None),
        P("tok", None, None),
        P("tok", None, None),
        P("tok"),
        P("tok"),
        P("tok"),
    )
    return jax.shard_map(
        local,
        mesh=mesh,
        in_specs=placed,
        out_specs=(
            P(("rep", "tok"), None),
            P(("rep", "tok"), None),
            P("tok", None, None),
            P("tok", None, None),
            P("tok", None, None),
            P("tok", None, None),
            P("tok", None, None),
            P("tok"),
            P("tok"),
            P("tok"),
            P("tok"),
            P("tok"),
            P(("rep", "tok")),
            P(),
        ),
        check_vma=False,
    )
```

```python
import functools
import math

import jax
import jax.numpy as jnp
from jax import lax
from jax.experimental import pallas as pl
from jax.experimental.pallas import tpu as pltpu
from jax.sharding import PartitionSpec as P

D = 768
HEADS = 12
HD = 64
FF = 3072
SD = 4
CL = 128
NBLK = 96
STEP = 10
CPS = 32
WROWS = 9216
BLK = 96
ROWS = 1024
PAIRS = HEADS // 2
PW = 2 * HD
TM = 512
META = 16
VMEM_LIMIT = 63 << 20
FC = 768

norm_epsilon = 1e-06
beta_first = 0.9
beta_second = 0.999
adam_epsilon = 1e-08
weight_decay = 0.01
rate_matrix = 0.02
rate_vector = 0.2

BF = jnp.bfloat16
F32 = jnp.float32
I32 = jnp.int32

VMEM = pl.BlockSpec(memory_space=pltpu.VMEM)
SMEM = pl.BlockSpec(memory_space=pltpu.SMEM)
ANY = pl.BlockSpec(memory_space=pl.ANY)

NN = (((1,), (0,)), ((), ()))
NT = (((1,), (1,)), ((), ()))
TN = (((0,), (0,)), ((), ()))


def mm(a, b, dims=NN):
    return lax.dot_general(a, b, dims, preferred_element_type=F32)


def slot_positions(block_owner, slot_count):
    owners = block_owner[:, 0]
    blocks = owners.shape[0]
    shared = owners[:, None] == owners[None, :]
    before = (
        jnp.arange(blocks, dtype=jnp.int32)[None, :] < jnp.arange(blocks, dtype=jnp.int32)[:, None]
    )
    earlier = jnp.sum((shared & before).astype(jnp.int32), axis=1)
    return owners * slot_count + earlier


def adam_update(grad_now, weight_old, first_old, second_old, rate_step):
    first_new = beta_first * first_old + (1.0 - beta_first) * grad_now
    second_new = beta_second * second_old + (1.0 - beta_second) * grad_now * grad_now
    first_hat = first_new / (1.0 - beta_first**STEP)
    second_hat = second_new / (1.0 - beta_second**STEP)
    weight_new = weight_old - rate_step * (
        first_hat / (jnp.sqrt(second_hat) + adam_epsilon) + weight_decay * weight_old
    )
    return (first_new, second_new, weight_new)


def route_slots(order, seat, cap):
    cluster = order // CL
    rel = lax.rem(cluster, SD) ^ seat
    place = (cluster // SD) * CL + lax.rem(order, CL) + 1
    chosen = lax.broadcasted_iota(I32, (8, ROWS), 0) == rel
    chosen_low = jnp.where(chosen, 1.0, 0.0).astype(BF)
    before = lax.broadcasted_iota(I32, (ROWS, ROWS), 0) < lax.broadcasted_iota(I32, (ROWS, ROWS), 1)
    before_low = jnp.where(before, 1.0, 0.0).astype(BF)
    running = mm(chosen_low, before_low)
    rank = jnp.sum(jnp.where(chosen, running, 0.0), axis=0, keepdims=True).astype(I32)
    return rel * cap + rank, place


def slot_matrix(slots, at, cap):
    rows = lax.broadcasted_iota(I32, (cap, ROWS), 0) + at * cap
    return jnp.where(rows == slots, 1.0, 0.0).astype(BF)


def send_kernel(cap, tokens, cotangent, order, send_x, send_c, meta):
    seat = lax.rem(lax.axis_index("tok"), SD)
    slots, place = route_slots(order[...], seat, cap)
    digits = jnp.concatenate([place // CL, lax.rem(place, CL)] + [place * 0] * 6, axis=0).astype(F32).astype(BF)
    for at in range(SD):
        picked = slot_matrix(slots, at, cap)
        send_x[at] = mm(picked, tokens[...]).astype(BF)
        send_c[at] = mm(picked, cotangent[...]).astype(BF)
        coded = mm(digits, picked, NT)
        line = jnp.concatenate([coded[0:1], coded[1:2]], axis=1)
        meta[at] = jnp.broadcast_to(line, (META, D)).astype(BF)


def remote(src, dst, send_sem, recv_sem, tok, rep):
    return pltpu.make_async_remote_copy(
        src_ref=src,
        dst_ref=dst,
        send_sem=send_sem,
        recv_sem=recv_sem,
        device_id={"tok": tok, "rep": rep},
        device_id_type=pl.DeviceIdType.MESH,
    )


def loop(n, body):
    def run(i, c):
        body(i)
        return c

    lax.fori_loop(0, n, run, 0)


class Place:
    def __init__(self):
        self.me = me = lax.axis_index("tok")
        self.z = z = lax.axis_index("rep")
        core, x, y = me % 2, (me // 2) % 2, me // 4
        self.twin = me + 1 - 2 * core
        self.xn = me + 2 - 4 * x
        self.yn = me + 4 - 8 * y
        self.dn = self.xn + 4 - 8 * y
        self.side = z % 2
        self.zp = z + 1 - 2 * self.side

    def twin_of(self, tok):
        return tok + 1 - 2 * (tok % 2)

    def greet(self, peers):
        barrier = pltpu.get_barrier_semaphore()
        for tok, rep in peers:
            pl.semaphore_signal(
                barrier, inc=1, device_id={"tok": tok, "rep": rep}, device_id_type=pl.DeviceIdType.MESH
            )
        return lambda: pl.semaphore_wait(barrier, len(peers))


def seat_matrix(meta, first, rows, cap):
    hi = jnp.concatenate([meta[k, 0:8, 0:cap] for k in range(SD)], axis=1).astype(F32)[0:1]
    lo = jnp.concatenate([meta[k, 0:8, cap : 2 * cap] for k in range(SD)], axis=1).astype(F32)[0:1]
    at = (hi * CL + lo).astype(I32)
    seats = lax.broadcasted_iota(I32, (rows, SD * cap), 0) + (first + 1)
    return jnp.where(seats == at, 1.0, 0.0).astype(BF)


def seat_part(meta, k, cap):
    hi = meta[k, 0:8, 0:cap].astype(F32)[0:1]
    lo = meta[k, 0:8, cap : 2 * cap].astype(F32)[0:1]
    at = (hi * CL + lo).astype(I32)
    seats = lax.broadcasted_iota(I32, (ROWS, cap), 0) + 1
    return jnp.where(seats == at, 1.0, 0.0).astype(BF)


def seat_rows(meta, blocks, cap, to):
    def body(t):
        r0 = pl.multiple_of(t * 256, 256)
        rows = blocks[...].reshape(SD * cap, D)
        to[pl.ds(r0, 256), :] = mm(seat_matrix(meta, r0, 256, cap), rows).astype(BF)

    loop(ROWS // 256, body)


def seat_kernel(cap, blocks, meta, to):
    seat_rows(meta, blocks, cap, to)


def gather_kernel(
    cap,
    count,
    tokens_h,
    cotangent_h,
    order,
    master_h,
    vector,
    owner_of,
    slots,
    x_c,
    cot_0,
    cot_1,
    cot_2,
    cot_3,
    recv_meta,
    vecs,
    b_u,
    occupancy,
    positions,
    tokens,
    cotangent,
    master,
    own,
    send_x,
    send_c,
    meta,
    recv_x,
    got_meta,
    mine,
    by_z,
    by_tok,
    x_s,
    x_r,
    y_s,
    y_r,
    d_s,
    d_r,
    zx_s,
    zx_r,
    zd_s,
    zd_r,
    zy_s,
    zy_r,
    p_s,
    p_r,
    row_s,
    row_r,
    z_s,
    z_r,
    t_s,
    t_r,
    local_s,
):
    at = Place()
    me, z, side = at.me, at.z, at.side
    n_tok, n_rep = 8, 4
    peers = [((me + d) % n_tok, z) for d in range(1, n_tok)] + [(me, (z + d) % n_rep) for d in range(1, n_rep)]
    fetch = [
        pltpu.make_async_copy(src, dst, local_s.at[i])
        for i, (src, dst) in enumerate(((master_h, master), (tokens_h, tokens), (cotangent_h, cotangent)))
    ]
    for copy in fetch:
        copy.start()
    wait_peers = at.greet(peers)
    fetch[0].wait()

    def cast(s):
        own[s] = master[s].astype(BF)

    loop(count, cast)
    wait_peers()

    half = count // 2

    def slot(owner, s):
        return slots.at[owner * count + s]

    def to_x(s):
        return remote(own.at[s], slot(me, s), x_s.at[s], x_r.at[s], at.xn, z)

    def to_y(s):
        return remote(own.at[s], slot(me, s), y_s.at[s], y_r.at[s], at.yn, z)

    def on_y(s):
        return remote(slot(at.xn, s), slot(at.xn, s), d_s.at[s], d_r.at[s], at.yn, z)

    def x_on_z(s):
        return remote(slot(at.xn, s), slot(at.xn, s), zx_s.at[s], zx_r.at[s], me, at.zp)

    def d_on_z(s):
        return remote(slot(at.dn, s), slot(at.dn, s), zd_s.at[s], zd_r.at[s], me, at.zp)

    def y_on_z(s):
        return remote(slot(at.yn, s), slot(at.yn, s), zy_s.at[s], zy_r.at[s], me, at.zp)

    few = count // 3
    most = count - few

    def straight(j):
        return few * side + j

    def shared(j):
        return most * side + j

    def lacking(j):
        return most * (1 - side) + j

    owners = (me, at.xn, at.yn, at.dn)

    def to_twin(q, s):
        src = own.at[s] if q == 0 else slot(owners[q], s)
        return remote(src, slot(owners[q], s), p_s.at[q, s], p_r.at[q, s], at.twin, z)

    def near(j):
        return (half + 1) * side + j

    def far(j):
        return (half + 1) * (1 - side) + j

    loop(half, lambda j: to_x(near(j)).start())
    to_x(half).start()
    for j in range(3):
        to_y(shared(j)).start()
    loop(count, lambda s: to_twin(0, s).start())
    keep = pltpu.make_async_copy(own, slots.at[pl.ds(me * count, count)], local_s.at[3])
    keep.start()
    fetch[1].wait()
    fetch[2].wait()

    seat = me % SD
    slot_of, place = route_slots(order[...], seat, cap)
    digits = jnp.concatenate([place // CL, lax.rem(place, CL)] + [place * 0] * 6, axis=0).astype(F32).astype(BF)
    for k in range(SD):
        picked = slot_matrix(slot_of, k, cap)
        send_x[k] = mm(picked, tokens[...]).astype(BF)
        send_c[k] = mm(picked, cotangent[...]).astype(BF)
        coded = mm(digits, picked, NT)
        line = jnp.concatenate([coded[0:1], coded[1:2]], axis=1)
        meta[k] = jnp.broadcast_to(line, (META, D)).astype(BF)
    seats = (me, at.twin, at.xn, at.twin_of(at.xn))
    rows_of = ((meta, got_meta), (send_x, recv_x))

    def row_copy(i, k):
        src, dst = rows_of[i]
        return remote(src.at[k], dst.at[k], row_s.at[i, k], row_r.at[i, k], seats[k], z)

    for i in range(2):
        src, dst = rows_of[i]
        for k in (2, 3, 1):
            row_copy(i, k).start()
        dst[0] = src[0]
    put_c = [
        pltpu.make_async_copy(send_c.at[k], to, local_s.at[4 + k])
        for k, to in enumerate((cot_0, cot_1, cot_2, cot_3))
    ]
    for copy in put_c:
        copy.start()

    residue = lax.rem(me // SD * CPS + order[...] // CL, n_tok)
    hit = lax.broadcasted_iota(I32, (128, ROWS), 0) == residue
    for i in range(9):
        mine[i : i + 1] = vector[i * 128 : (i + 1) * 128].reshape(1, 128).astype(BF).astype(F32)
    block_row = lax.broadcasted_iota(I32, (NBLK, NBLK), 0)
    block_col = lax.broadcasted_iota(I32, (NBLK, NBLK), 1)
    by_col = owner_of[...].astype(F32)
    by_row = lane_sum(jnp.where(block_row == block_col, by_col, 0.0))
    earlier = jnp.where((by_row == by_col) & (block_row < block_col), 1.0, 0.0)
    positions[...] = (by_col * count + jnp.sum(earlier, axis=0, keepdims=True)).astype(I32)
    by_z[0] = mm(jnp.ones((8, ROWS), BF), jnp.where(hit, 1.0, 0.0).astype(BF), NT)

    def z_copy(d):
        return remote(by_z.at[0], by_z.at[d], z_s.at[d], z_r.at[d], me, (z + d) % n_rep)

    def t_copy(d):
        return remote(mine, by_tok.at[d], t_s.at[d], t_r.at[d], (me + d) % n_tok, z)

    for d in range(1, n_rep):
        z_copy(d).start()
    for d in range(1, n_rep):
        z_copy(d).wait()
    mine[16:24] = by_z[0] + by_z[1] + by_z[2] + by_z[3]
    for d in range(1, n_tok):
        t_copy(d).start()

    def x_here(s):
        to_x_in(s).wait_recv()
        on_y(s).start()
        to_twin(1, s).start()

    def to_x_in(s):
        return remote(own.at[s], slot(at.xn, s), x_s.at[s], x_r.at[s], at.xn, z)

    def y_in(s):
        return remote(own.at[s], slot(at.yn, s), y_s.at[s], y_r.at[s], at.yn, z)

    def d_in(s):
        return remote(own.at[s], slot(at.dn, s), d_s.at[s], d_r.at[s], at.yn, z)

    def y_here(s):
        y_in(s).wait_recv()
        to_twin(2, s).start()

    def rest(j):
        return few + j

    for j in range(half):
        x_here(near(j))
        x_on_z(near(j)).start()
        if 3 + j < few:
            to_y(shared(3 + j)).start()
        else:
            to_y(rest(3 + j - few)).start()
    x_here(half)
    for j in range(3 + half, most):
        to_y(rest(j - few)).start()

    def shared_here(j):
        y_here(shared(j))
        y_on_z(shared(j)).start()

    loop(few, shared_here)

    def second(j):
        x_on_z(far(j)).wait_recv()
        to_twin(1, far(j)).start()
        d_in(near(j)).wait_recv()
        d_on_z(near(j)).start()
        to_twin(3, near(j)).start()

    loop(half, second)
    d_in(half).wait_recv()
    to_twin(3, half).start()
    loop(most - few, lambda j: y_here(rest(j)))

    def lacking_here(j):
        y_on_z(lacking(j)).wait_recv()
        to_twin(2, lacking(j)).start()

    loop(few, lacking_here)
    for i in (0, 1):
        for k in (2, 3, 1):
            row_copy(i, k).wait_recv()
    recv_meta[...] = got_meta[...]
    seat_rows(got_meta, recv_x, cap, x_c)

    def third(j):
        d_on_z(far(j)).wait_recv()
        to_twin(3, far(j)).start()

    loop(half, third)

    by_tok[0] = mine[...]
    for d in range(1, n_tok):
        t_copy(d).wait()
    for owner in range(n_tok):
        share = by_tok[(me + n_tok - owner) % n_tok]
        occupancy[owner : owner + 1, :] = share[16:17, 0:n_tok].astype(I32)
        for i in range(9):
            chunk = owner * 9 + i
            row, lane = chunk // 6, chunk % 6 * 128
            if row < 8:
                vecs[row : row + 1, lane : lane + 128] = share[i : i + 1]
            else:
                lane += (row - 8) * D
                b_u[:, lane : lane + 128] = share[i : i + 1]
    for i in range(2):
        for k in (2, 3, 1):
            row_copy(i, k).wait_send()
    for copy in put_c:
        copy.wait()
    keep.wait()

    def sent_half(j):
        to_x(near(j)).wait_send()
        on_y(near(j)).wait_send()
        x_on_z(near(j)).wait_send()
        d_on_z(near(j)).wait_send()

    loop(half, sent_half)
    to_x(half).wait_send()
    on_y(half).wait_send()

    def sent(s):
        for q in range(4):
            to_twin(q, s).wait()

    loop(count, sent)
    loop(most, lambda j: to_y(straight(j)).wait_send())
    loop(few, lambda j: y_on_z(shared(j)).wait_send())


def gather_all(cap, tokens, cotangent, order, master, vector, block_owner):
    count = master.shape[0]
    rows = jax.ShapeDtypeStruct((ROWS, D), BF)
    part = jax.ShapeDtypeStruct((cap, D), BF)
    dma = pltpu.SemaphoreType.DMA
    block = pltpu.VMEM((SD, cap, D), BF)
    meta = pltpu.VMEM((SD, META, D), BF)
    return pl.pallas_call(
        functools.partial(gather_kernel, cap, count),
        out_shape=(
            jax.ShapeDtypeStruct((8 * count, BLK, D), BF),
            rows,
            part,
            part,
            part,
            part,
            jax.ShapeDtypeStruct((SD, META, D), BF),
            jax.ShapeDtypeStruct((8, D), F32),
            jax.ShapeDtypeStruct((1, FF), F32),
            jax.ShapeDtypeStruct((8, 8), I32),
            jax.ShapeDtypeStruct((1, NBLK), I32),
        ),
        in_specs=[ANY, ANY, VMEM, ANY, VMEM, VMEM],
        out_specs=(ANY, VMEM) + (ANY,) * SD + (VMEM,) * 5,
        scratch_shapes=[
            pltpu.VMEM((ROWS, D), BF),
            pltpu.VMEM((ROWS, D), BF),
            pltpu.VMEM((count, BLK, D), F32),
            pltpu.VMEM((count, BLK, D), BF),
            block,
            block,
            meta,
            block,
            meta,
            pltpu.VMEM((24, 128), F32),
            pltpu.VMEM((4, 8, 128), F32),
            pltpu.VMEM((8, 24, 128), F32),
        ]
        + [dma((count,))] * 12
        + [dma((4, count))] * 2
        + [dma((2, SD))] * 2
        + [dma((4,))] * 2
        + [dma((8,))] * 2
        + [dma((8,))],
        compiler_params=pltpu.CompilerParams(collective_id=0, has_side_effects=True, vmem_limit_bytes=VMEM_LIMIT),
        name="gather",
    )(tokens, cotangent, order, master, vector, block_owner.reshape(1, NBLK))


def return_kernel(cap, order, *refs):
    outs, ings, (out, ing, entropy) = refs[:SD], refs[SD : 2 * SD], refs[2 * SD :]
    seat = lax.rem(lax.axis_index("tok"), SD)
    slots, _ = route_slots(order[...], seat, cap)
    picked = jnp.concatenate([slot_matrix(slots, at, cap) for at in range(SD)], axis=0)
    for to, blocks in ((out, outs), (ing, ings)):
        rows = jnp.concatenate([block[0:cap, :] for block in blocks], axis=0)
        to[...] = mm(picked, rows, TN).astype(BF)
    line = jnp.concatenate([block[cap : cap + 8, 0:cap] for block in outs], axis=1)
    entropy[...] = mm(line, picked)[0:1].astype(BF)


def swap_blocks(blocks):
    n = lax.axis_size("tok")
    parts = [blocks[0]]
    for k in range(1, SD):
        parts.append(lax.ppermute(blocks[k], "tok", [(i, i ^ k) for i in range(n)]))
    return parts


def reduce_kernel(
    count,
    split,
    grads,
    vec,
    total,
    vec_out,
    a,
    tw,
    rd,
    rx,
    ry,
    o,
    rz1,
    pz,
    rz2,
    fz,
    vt,
    va,
    vb,
    vc,
    a_l,
    keep_l,
    p_s,
    p_r,
    d_s,
    d_r,
    x_s,
    x_r,
    y_s,
    y_r,
    z1_s,
    z1_r,
    z2_s,
    z2_r,
    z3_s,
    z3_r,
    t_s,
    t_r,
    v_s,
    v_r,
):
    at = Place()
    me, z = at.me, at.z
    n_tok, n_rep = 8, 4
    peers = [((me + d) % n_tok, z) for d in range(1, n_tok)] + [(me, (z + d) % n_rep) for d in range(1, n_rep)]
    wait_peers = at.greet(peers)
    owners = (me, at.xn, at.yn, at.dn)

    def load(q):
        return pltpu.make_async_copy(grads.at[pl.ds(owners[q] * count, count)], a.at[q], a_l.at[q])

    for q in (3, 1, 2, 0):
        load(q).start()
    wait_peers()

    def to_twin(q, s):
        src = grads.at[at.twin_of(owners[q]) * count + s]
        return remote(src, tw.at[q, s], p_s.at[q, s], p_r.at[q, s], at.twin, z)

    def d_y(s):
        return remote(a.at[3, s], rd.at[s], d_s.at[s], d_r.at[s], at.yn, z)

    def d_x(s):
        return remote(a.at[3, s], rd.at[s], d_s.at[s], d_r.at[s], at.xn, z)

    def to_x(s):
        return remote(a.at[1, s], rx.at[s], x_s.at[s], x_r.at[s], at.xn, z)

    def to_y(s):
        return remote(a.at[2, s], ry.at[s], y_s.at[s], y_r.at[s], at.yn, z)

    def z_in(s):
        return remote(o.at[s], rz1.at[s], z1_s.at[s], z1_r.at[s], me, at.zp)

    def z_swap(s):
        return remote(pz.at[s], rz2.at[s], z2_s.at[s], z2_r.at[s], me, n_rep - 1 - z)

    def z_out(s):
        return remote(fz.at[s], fz.at[s], z3_s.at[s], z3_r.at[s], me, at.zp)

    def keep(s):
        return pltpu.make_async_copy(fz.at[s], total.at[s], keep_l.at[s])

    def f32(ref, *index):
        return ref[index].astype(F32)

    loop(count, lambda s: to_twin(3, s).start())

    def others(s):
        for q in (2, 1, 0):
            to_twin(q, s).start()

    loop(count, others)

    def v_tok(d):
        return remote(vec.at[(me + d) % n_tok], vt.at[d], t_s.at[d], t_r.at[d], (me + d) % n_tok, z)

    def v_rep(i, src):
        return remote(src, vb.at[i], v_s.at[i], v_r.at[i], me, at.zp if i == 0 else (z + 2) % n_rep)

    for d in range(1, n_tok):
        v_tok(d).start()

    load(3).wait()

    def join(q, s):
        to_twin(q, s).wait_recv()
        return f32(a, q, s) + f32(tw, q, s)

    def diagonal(s, send):
        a[3, s] = join(3, s).astype(BF)
        send(s).start()

    loop(split, lambda s: diagonal(s, d_y))
    loop(count - split, lambda j: diagonal(split + j, d_x))

    v_sum = vec[me]
    for d in range(1, n_tok):
        v_tok(d).wait()
        v_sum = v_sum + vt[d]
    va[...] = v_sum
    v_rep(0, va).start()

    load(1).wait()
    load(2).wait()

    def plane_y(s):
        a[2, s] = join(2, s).astype(BF)
        to_y(s).start()
        d_y(s).wait_recv()
        a[1, s] = (join(1, s) + f32(rd, s)).astype(BF)
        to_x(s).start()

    def plane_x(s):
        a[1, s] = join(1, s).astype(BF)
        to_x(s).start()
        d_x(s).wait_recv()
        a[2, s] = (join(2, s) + f32(rd, s)).astype(BF)
        to_y(s).start()

    loop(count - split, lambda j: plane_x(split + j))
    loop(split, plane_y)

    v_rep(0, va).wait()
    vc[...] = va[...] + vb[0]
    v_rep(1, vc).start()
    load(0).wait()
    inner = (z == 1) | (z == 2)
    outer = (z == 0) | (z == 3)

    def turn(i):
        return (i + split) % count

    def planes(i):
        @pl.when(i < count)
        def _():
            s = turn(i)
            to_x(s).wait_recv()
            to_y(s).wait_recv()
            o[s] = (join(0, s) + f32(rx, s) + f32(ry, s)).astype(BF)

        @pl.when(outer & (i < count))
        def _():
            z_in(turn(i)).start()

        @pl.when(inner & (i >= 1) & (i < count + 1))
        def _():
            s = turn(i - 1)
            z_in(s).wait_recv()
            pz[s] = (f32(o, s) + f32(rz1, s)).astype(BF)
            z_swap(s).start()

        @pl.when(inner & (i >= 2) & (i < count + 2))
        def _():
            s = turn(i - 2)
            z_swap(s).wait_recv()
            fz[s] = (f32(pz, s) + f32(rz2, s)).astype(BF)
            z_out(s).start()
            keep(s).start()

        @pl.when(outer & (i >= 3))
        def _():
            s = turn(i - 3)
            z_out(s).wait_recv()
            keep(s).start()

    loop(count + 3, planes)
    v_rep(1, vc).wait()
    vec_out[...] = vc[...] + vb[1]

    def sent(s):
        for q in range(4):
            to_twin(q, s).wait_send()
        d_y(s).wait_send()
        to_x(s).wait_send()
        to_y(s).wait_send()
        keep(s).wait()

    loop(count, sent)

    @pl.when(outer)
    def _():
        loop(count, lambda s: z_in(s).wait_send())

    @pl.when(inner)
    def _():
        def back(s):
            z_swap(s).wait_send()
            z_out(s).wait_send()

        loop(count, back)


def reduce_all(grads, shares, count):
    dma = pltpu.SemaphoreType.DMA
    part = pltpu.VMEM((count, BLK, D), BF)
    whole = pltpu.VMEM((4, count, BLK, D), BF)
    line = pltpu.VMEM((16, 128), F32)
    total, vec = pl.pallas_call(
        functools.partial(reduce_kernel, count, (count + 3) // 2),
        out_shape=(
            jax.ShapeDtypeStruct((count, BLK, D), BF),
            jax.ShapeDtypeStruct((16, 128), F32),
        ),
        in_specs=[ANY, VMEM],
        out_specs=(ANY, VMEM),
        scratch_shapes=[whole, whole]
        + [part] * 8
        + [pltpu.VMEM((8, 16, 128), F32), line, pltpu.VMEM((2, 16, 128), F32), line]
        + [dma((4,)), dma((count,))]
        + [dma((4, count))] * 2
        + [dma((count,))] * 12
        + [dma((8,))] * 2
        + [dma((2,))] * 2,
        compiler_params=pltpu.CompilerParams(
            collective_id=1, has_side_effects=True, vmem_limit_bytes=VMEM_LIMIT
        ),
        name="reduce",
    )(grads, shares)
    return total, vec[0:9].reshape(-1)


V_BQ, V_BV, V_BO, V_BD, V_G1, V_C1, V_G2, V_C2 = range(8)


def inverse(x):
    r = pl.reciprocal(x, approx=True)
    return r * (2.0 - x * r)


def erf_parts(v):
    t = inverse(1.0 + (0.3275911 / math.sqrt(2.0)) * jnp.abs(v))
    e = jnp.exp2((v * v) * (-0.5 / math.log(2.0)))
    poly = 0.5 * 1.061405429
    for c in (-1.453152027, 1.421413741, -0.284496736, 0.254829592):
        poly = poly * t + 0.5 * c
    tail = poly * (t * e)
    return jnp.where(v >= 0.0, 1.0 - tail, tail), e


def lane_sum(x):
    return jnp.sum(x, axis=1, keepdims=True)


def gelu_parts(v):
    phi, e = erf_parts(v)
    return v * phi, phi + v * (e * (1.0 / math.sqrt(2.0 * math.pi)))


def weight_copies(pos, slots, w, sem, first):
    def copy(b):
        return pltpu.make_async_copy(slots.at[pos[first + b]], w.at[pl.ds(b * BLK, BLK)], sem)

    n = w.shape[0] // BLK
    return (lambda: loop(n, lambda b: copy(b).start())), (lambda: loop(n, lambda b: copy(b).wait()))


def halves_of_heads():
    lane = lax.broadcasted_iota(I32, (1, PW), 1)
    m0 = jnp.where(lane < HD, 1.0, 0.0).astype(BF)
    m1 = jnp.where(lane < HD, 0.0, 1.0).astype(BF)
    return lambda pair: jnp.concatenate([pair * m0, pair * m1], axis=0)


def tile_rows(t):
    return pl.ds(pl.multiple_of(t * TM, TM), TM)


def forward_kernel(
    cap,
    pos,
    slots,
    vecs,
    b_u,
    x_h,
    meta,
    back_0,
    back_1,
    back_2,
    back_3,
    heads_h,
    act_h,
    hid_h,
    q_h,
    k_h,
    v_h,
    p_h,
    slope_h,
    n1_h,
    n2_h,
    rs1_h,
    rs2_h,
    wqkv,
    wo,
    wu,
    wd,
    x_c,
    heads,
    act,
    hid,
    q,
    k,
    v,
    p_all,
    slope,
    n1,
    n2,
    rs1,
    rs2,
    out_c,
    ent,
    hid_t,
    w_sem,
    x_sem,
    o_sem,
):
    inv = 1.0 / math.sqrt(HD)
    get_x = pltpu.make_async_copy(x_h, x_c, x_sem)
    get_x.start()
    weights = [
        weight_copies(pos, slots, w, w_sem.at[i], first)
        for i, (w, first) in enumerate(((wqkv, 0), (wo, 24), (wu, 32), (wd, 64)))
    ]
    for start, _ in weights:
        start()
    get_x.wait()
    apart = halves_of_heads()

    def vec(i):
        return vecs[i : i + 1, :]

    saved = (
        (heads, heads_h),
        (act, act_h),
        (hid, hid_h),
        (q, q_h),
        (k, k_h),
        (v, v_h),
        (slope, slope_h),
        (n1, n1_h),
        (n2, n2_h),
        (rs1, rs1_h),
        (rs2, rs2_h),
    )

    def save(t, i):
        src, dst = saved[i]
        return pltpu.make_async_copy(src.at[tile_rows(t)], dst.at[tile_rows(t)], o_sem.at[i])

    def save_p(t):
        n = TM // CL
        cs = pl.ds(t * n, n)
        return pltpu.make_async_copy(p_all.at[cs], p_h.at[cs], o_sem.at[len(saved)])

    def normal(r, n, rs, rows):
        c = r - lane_sum(r) * (1.0 / D)
        scale = lax.rsqrt(lane_sum(c * c) * (1.0 / D) + norm_epsilon)
        rs[rows, :] = jnp.broadcast_to(scale, (TM, 128))
        n[rows, :] = c * scale

    def tile(t):
        rows = tile_rows(t)
        first = t == 0
        pl.when(first)(weights[0][1])
        x = x_c[rows, :]
        q[rows, :] = ((mm(x, wqkv[0:D, :]) + vec(V_BQ)).astype(BF).astype(F32) * inv).astype(BF)
        k[rows, :] = mm(x, wqkv[D : 2 * D, :]).astype(BF)
        v[rows, :] = (mm(x, wqkv[2 * D :, :]) + vec(V_BV)).astype(BF)

        def attend(c):
            gr = pl.ds(pl.multiple_of(t * TM + c * CL, CL), CL)
            total = jnp.zeros((1, CL), F32)
            for p in range(PAIRS):
                ps = slice(p * PW, (p + 1) * PW)
                scores = mm(apart(k[gr, ps]), q[gr, ps], NT)
                halves = []
                for h in range(2):
                    sh = scores[h * CL : (h + 1) * CL]
                    sh = sh - jnp.max(sh, axis=0, keepdims=True)
                    e = jnp.exp(sh)
                    tot = jnp.sum(e, axis=0, keepdims=True)
                    r = 1.0 / tot
                    total += jnp.log(tot) - jnp.sum(e * sh, axis=0, keepdims=True) * r
                    halves.append((e * r).astype(BF))
                probs = jnp.concatenate(halves, axis=0)
                p_all[t * (TM // CL) + c, p] = probs
                heads[gr, ps] = mm(probs, apart(v[gr, ps]), TN).astype(BF)
            ent[:, gr] = jnp.broadcast_to(total * (1.0 / HEADS), (8, CL))

        loop(TM // CL, attend)
        pl.when(first)(weights[1][1])
        normal(x_c[rows, :].astype(F32) + mm(heads[rows, :], wo[...]) + vec(V_BO), n1, rs1, rows)
        hidden = n1[rows, :] * vec(V_G1) + vec(V_C1)
        hid[rows, :] = hidden.astype(BF)
        hid_t[...] = hidden
        pl.when(first)(weights[2][1])

        def widen(f):
            fs = pl.ds(pl.multiple_of(f * FC, FC), FC)
            g, g_slope = gelu_parts(mm(hid[rows, :], wu[fs, :], NT) + b_u[:, fs])
            act[rows, fs] = g.astype(BF)
            slope[rows, fs] = g_slope.astype(BF)

        loop(FF // FC, widen)
        pl.when(first)(weights[3][1])
        normal(hid_t[...] + mm(act[rows, :], wd[...]) + vec(V_BD), n2, rs2, rows)
        out_c[rows, :] = (n2[rows, :] * vec(V_G2) + vec(V_C2)).astype(BF)
        for i in range(len(saved)):
            save(t, i).start()
        save_p(t).start()

    loop(ROWS // TM, tile)

    for j, back in enumerate((back_0, back_1, back_2, back_3)):
        own = seat_part(meta, j, cap)
        back[0:cap, :] = mm(own, out_c[...], TN).astype(BF)
        line = mm(ent[...].astype(BF), own)
        back[cap:, :] = jnp.concatenate([line, line], axis=1)[0:1].astype(BF) * jnp.ones((META, 1), BF)

    def saved_all(t):
        for i in range(len(saved)):
            save(t, i).wait()
        save_p(t).wait()

    loop(ROWS // TM, saved_all)


def shape_of(kind, *shape):
    return jax.ShapeDtypeStruct(shape, kind)


def saved_shapes():
    rows, wide = ((ROWS, D), BF), ((ROWS, FF), BF)
    probs = ((ROWS // CL, PAIRS, 2 * CL, CL), BF)
    full, thin = ((ROWS, D), F32), ((ROWS, 128), F32)
    return rows, wide, probs, full, thin


def forward(cap, positions, slots, vecs, b_u, x_c, meta):
    rows, wide, probs, full, thin = saved_shapes()
    kept = (rows, wide, rows, rows, rows, rows, probs, wide, full, full, thin, thin)
    dma = pltpu.SemaphoreType.DMA
    return pl.pallas_call(
        functools.partial(forward_kernel, cap),
        out_shape=(shape_of(BF, cap + META, D),) * SD + tuple(shape_of(kind, *shape) for shape, kind in kept),
        in_specs=[SMEM, ANY, VMEM, VMEM, ANY, VMEM],
        out_specs=(VMEM,) * SD + (ANY,) * len(kept),
        scratch_shapes=[
            pltpu.VMEM((3 * D, D), BF),
            pltpu.VMEM((D, D), BF),
            pltpu.VMEM((FF, D), BF),
            pltpu.VMEM((FF, D), BF),
            pltpu.VMEM(*rows),
        ]
        + [pltpu.VMEM(*a) for a in kept]
        + [
            pltpu.VMEM(*rows),
            pltpu.VMEM((8, ROWS), F32),
            pltpu.VMEM((TM, D), F32),
            dma((4,)),
            dma,
            dma((12,)),
        ],
        compiler_params=pltpu.CompilerParams(vmem_limit_bytes=VMEM_LIMIT),
        name="forward",
    )(positions, slots, vecs, b_u, x_c, meta)


def backward_kernel(
    cap,
    pos,
    slots,
    vecs,
    meta,
    cot_0,
    cot_1,
    cot_2,
    cot_3,
    q_h,
    k_h,
    v_h,
    p_h,
    slope_h,
    n1_h,
    n2_h,
    rs1_h,
    rs2_h,
    back_0,
    back_1,
    back_2,
    back_3,
    shares,
    d_up_h,
    d_q_h,
    d_k_h,
    d_v_h,
    d_proj_h,
    d_br_h,
    wqkv,
    wo,
    wu,
    wd,
    blocks,
    q,
    k,
    v,
    p_all,
    d_up,
    n1,
    n2,
    rs1,
    rs2,
    d_proj,
    d_br,
    ing_c,
    d_h_t,
    res_t,
    gvec,
    g_bu,
    w_sem,
    c_sem,
    i_sem,
    o_sem,
):
    inv = 1.0 / math.sqrt(HD)
    get_c = [
        pltpu.make_async_copy(cot, blocks.at[j], c_sem.at[j]) for j, cot in enumerate((cot_0, cot_1, cot_2, cot_3))
    ]
    for copy in get_c:
        copy.start()
    fetch = [
        pltpu.make_async_copy(src, dst, i_sem.at[i])
        for i, (src, dst) in enumerate(
            (
                (n2_h, n2),
                (rs2_h, rs2),
                (slope_h, d_up),
                (n1_h, n1),
                (rs1_h, rs1),
                (v_h, v),
                (p_h, p_all),
                (k_h, k),
                (q_h, q),
            )
        )
    ]
    weights = [
        weight_copies(pos, slots, w, w_sem.at[i], first)
        for i, (w, first) in enumerate(((wd, 64), (wu, 32), (wo, 24), (wqkv, 0)))
    ]
    fetch[0].start()
    fetch[1].start()
    weights[0][0]()
    fetch[2].start()
    weights[1][0]()
    fetch[3].start()
    fetch[4].start()
    weights[2][0]()
    for i in range(5, 9):
        fetch[i].start()
    weights[3][0]()
    gvec[...] = jnp.zeros_like(gvec)
    g_bu[...] = jnp.zeros_like(g_bu)
    shares[...] = jnp.zeros_like(shares)
    for copy in get_c:
        copy.wait()
    seat_rows(meta, blocks, cap, d_br)
    apart = halves_of_heads()
    first_half = lax.broadcasted_iota(I32, (CL, PW), 1) < HD

    def vec(i):
        return vecs[i : i + 1, :]

    def add_vec(i, value):
        gvec[i : i + 1, :] += jnp.sum(value, axis=0, keepdims=True)

    saved = ((d_up, d_up_h), (q, d_q_h), (k, d_k_h), (v, d_v_h), (d_proj, d_proj_h), (d_br, d_br_h))

    def save(t, i):
        src, dst = saved[i]
        return pltpu.make_async_copy(src.at[tile_rows(t)], dst.at[tile_rows(t)], o_sem.at[i])

    def norm_back(e, n, rs, gain, shift):
        add_vec(gain, e * n)
        add_vec(shift, e)
        eg = e * vec(gain)
        return rs * (eg - lane_sum(eg) * (1.0 / D) - n * (lane_sum(eg * n) * (1.0 / D)))

    def tile(t):
        rows = tile_rows(t)
        start = t == 0

        @pl.when(start)
        def _():
            fetch[0].wait()
            fetch[1].wait()

        d_r2 = norm_back(d_br[rows, :].astype(F32), n2[rows, :], rs2[rows, 0:1], V_G2, V_C2)
        d_br[rows, :] = d_r2.astype(BF)
        add_vec(V_BD, d_br[rows, :].astype(F32))
        res_t[...] = d_r2

        @pl.when(start)
        def _():
            weights[0][1]()
            fetch[2].wait()

        def widen_back(f):
            fs = pl.ds(pl.multiple_of(f * FC, FC), FC)
            du = (mm(d_br[rows, :], wd[fs, :], NT) * d_up[rows, fs].astype(F32)).astype(BF)
            d_up[rows, fs] = du
            g_bu[:, fs] += jnp.sum(du.astype(F32), axis=0, keepdims=True)

        loop(FF // FC, widen_back)

        @pl.when(start)
        def _():
            weights[1][1]()
            fetch[3].wait()
            fetch[4].wait()

        d_h = res_t[...] + mm(d_up[rows, :], wu[...])
        d_r1 = norm_back(d_h, n1[rows, :], rs1[rows, 0:1], V_G1, V_C1)
        d_proj[rows, :] = d_r1.astype(BF)
        res_t[...] = d_r1
        add_vec(V_BO, d_proj[rows, :].astype(F32))

        @pl.when(start)
        def _():
            weights[2][1]()
            for i in range(5, 9):
                fetch[i].wait()

        d_h_t[...] = mm(d_proj[rows, :], wo[...], NT).astype(BF)

        def attend_back(c):
            cr = pl.ds(pl.multiple_of(c * CL, CL), CL)
            gr = pl.ds(pl.multiple_of(t * TM + c * CL, CL), CL)
            for p in range(PAIRS):
                ps = slice(p * PW, (p + 1) * PW)
                dh, qp, ks = d_h_t[cr, ps], q[gr, ps], apart(k[gr, ps])
                probs = p_all[t * (TM // CL) + c, p]
                d_w = mm(apart(v[gr, ps]), dh, NT)
                halves = []
                for h in range(2):
                    wh = probs[h * CL : (h + 1) * CL].astype(F32)
                    dwh = d_w[h * CL : (h + 1) * CL]
                    halves.append((wh * (dwh - jnp.sum(dwh * wh, axis=0, keepdims=True))).astype(BF))
                d_s = jnp.concatenate(halves, axis=0)
                q[gr, ps] = (mm(d_s, ks, TN) * inv).astype(BF)
                dk = mm(d_s, qp)
                k[gr, ps] = jnp.where(first_half, dk[0:CL], dk[CL:]).astype(BF)
                dv = mm(probs, dh)
                v[gr, ps] = jnp.where(first_half, dv[0:CL], dv[CL:]).astype(BF)

        loop(TM // CL, attend_back)
        add_vec(V_BQ, q[rows, :].astype(F32))
        add_vec(V_BV, v[rows, :].astype(F32))
        pl.when(start)(weights[3][1])
        d_x = (
            mm(q[rows, :], wqkv[0:D, :], NT)
            + mm(k[rows, :], wqkv[D : 2 * D, :], NT)
            + mm(v[rows, :], wqkv[2 * D :, :], NT)
        )
        ing_c[rows, :] = (res_t[...] + d_x.astype(BF).astype(F32)).astype(BF)
        for i in range(len(saved)):
            save(t, i).start()

    loop(ROWS // TM, tile)

    for j, back in enumerate((back_0, back_1, back_2, back_3)):
        back[...] = mm(seat_part(meta, j, cap), ing_c[...], TN).astype(BF)

    for chunk in range(72):
        row, lane = chunk // 6, chunk % 6 * 128
        if row < 8:
            part = gvec[row : row + 1, lane : lane + 128]
        else:
            lane += (row - 8) * D
            part = g_bu[:, lane : lane + 128]
        shares[chunk // 9, chunk % 9 : chunk % 9 + 1, :] = part

    def saved_all(t):
        for i in range(len(saved)):
            save(t, i).wait()

    loop(ROWS // TM, saved_all)


def backward(cap, positions, slots, vecs, meta, cots, saved):
    rows, wide, probs, full, thin = saved_shapes()
    dma = pltpu.SemaphoreType.DMA
    grads = (wide, rows, rows, rows, rows, rows)
    return pl.pallas_call(
        functools.partial(backward_kernel, cap),
        out_shape=(shape_of(BF, cap, D),) * SD
        + (shape_of(F32, 8, 16, 128),)
        + tuple(shape_of(kind, *shape) for shape, kind in grads),
        in_specs=[SMEM, ANY, VMEM, VMEM] + [ANY] * (SD + 9),
        out_specs=(VMEM,) * (SD + 1) + (ANY,) * len(grads),
        scratch_shapes=[
            pltpu.VMEM((3 * D, D), BF),
            pltpu.VMEM((D, D), BF),
            pltpu.VMEM((FF, D), BF),
            pltpu.VMEM((FF, D), BF),
            pltpu.VMEM((SD, cap, D), BF),
        ]
        + [pltpu.VMEM(*a) for a in (rows, rows, rows, probs, wide, full, full, thin, thin, rows, rows, rows)]
        + [
            pltpu.VMEM((TM, D), BF),
            pltpu.VMEM((TM, D), F32),
            pltpu.VMEM((8, D), F32),
            pltpu.VMEM((1, FF), F32),
            dma((4,)),
            dma((4,)),
            dma((9,)),
            dma((6,)),
        ],
        compiler_params=pltpu.CompilerParams(vmem_limit_bytes=VMEM_LIMIT),
        name="backward",
    )(positions, slots, vecs, meta, *cots, *saved)


WC = 8 * BLK


def weight_kernel(
    pos,
    x_h,
    heads_h,
    act_h,
    d_up_h,
    d_q_h,
    d_k_h,
    d_v_h,
    d_proj_h,
    hid_h,
    d_br_h,
    grads,
    x_c,
    heads,
    act,
    d_up,
    d_q,
    d_k,
    d_v,
    d_proj,
    hid,
    d_br,
    stage,
    i_sem,
    g_sem,
):
    refs = (
        (x_h, x_c),
        (d_q_h, d_q),
        (d_k_h, d_k),
        (d_v_h, d_v),
        (heads_h, heads),
        (d_proj_h, d_proj),
        (hid_h, hid),
        (d_up_h, d_up),
        (d_br_h, d_br),
        (act_h, act),
    )
    fetch = [pltpu.make_async_copy(src, dst, i_sem.at[i]) for i, (src, dst) in enumerate(refs)]
    for copy in fetch:
        copy.start()

    per = WC // BLK

    def g_copy(chunk, j, at):
        return pltpu.make_async_copy(
            stage.at[at, pl.ds(j * BLK, BLK)], grads.at[pos[chunk * per + j]], g_sem.at[at]
        )

    def put(chunk, left, right):
        at = lax.rem(chunk, 2)

        @pl.when(chunk >= 2)
        def _():
            for j in range(per):
                g_copy(chunk - 2, j, at).wait()

        stage[at] = mm(left, right, TN).astype(BF)
        for j in range(per):
            g_copy(chunk, j, at).start()

    first = 0
    for left, right, needs in (
        (x_c, d_q, (0, 1)),
        (x_c, d_k, (2,)),
        (x_c, d_v, (3,)),
        (heads, d_proj, (4, 5)),
        (d_up, hid, (6, 7)),
        (act, d_br, (8, 9)),
    ):
        for i in needs:
            fetch[i].wait()

        def body(j, left=left, right=right, first=first):
            put(first + j, left[:, pl.ds(pl.multiple_of(j * WC, WC), WC)], right[...])

        loop(left.shape[1] // WC, body)
        first += left.shape[1] // WC
    for chunk in (first - 2, first - 1):
        for j in range(per):
            g_copy(chunk, j, chunk % 2).wait()


def weight_grads_of(total_slots, positions, x_c, saved):
    r_v, w_v = pltpu.VMEM((ROWS, D), BF), pltpu.VMEM((ROWS, FF), BF)
    return pl.pallas_call(
        weight_kernel,
        out_shape=jax.ShapeDtypeStruct((total_slots, BLK, D), BF),
        in_specs=[SMEM] + [ANY] * 10,
        out_specs=ANY,
        scratch_shapes=[r_v, r_v, w_v, w_v]
        + [r_v] * 6
        + [
            pltpu.VMEM((2, WC, D), BF),
            pltpu.SemaphoreType.DMA((10,)),
            pltpu.SemaphoreType.DMA((2,)),
        ],
        compiler_params=pltpu.CompilerParams(vmem_limit_bytes=VMEM_LIMIT),
        cost_estimate=pl.CostEstimate(flops=2 * ROWS * WROWS * D, bytes_accessed=40 << 20, transcendentals=0),
        name="weight_grads",
    )(positions, x_c, *saved)


def local(
    tokens,
    cotangent,
    cluster_order,
    block_owner,
    master_slots,
    moment_one,
    moment_two,
    vector_master,
    vector_moment_one,
    vector_moment_two,
):
    tok_count = lax.axis_size("tok")
    tok_index = lax.axis_index("tok")
    slot_count = master_slots.shape[0]
    cap = tok_count // SD * (max(1, CPS // tok_count) * 3 * CL // (2 * SD))
    total_slots = tok_count * slot_count
    order = cluster_order.reshape(1, ROWS)

    block = jax.ShapeDtypeStruct((SD, cap, D), BF)
    meta_shape = jax.ShapeDtypeStruct((SD, META, D), BF)
    row_block = jax.ShapeDtypeStruct((ROWS, D), BF)
    four_planes = tok_count == 8 and lax.axis_size("rep") == 4
    if four_planes:
        slots_low, x_c, *cots, recv_meta, vecs, b_u, occupancy, positions = gather_all(
            cap, tokens, cotangent, order, master_slots, vector_master, block_owner
        )
        positions = positions.reshape(NBLK)
    else:
        positions = slot_positions(block_owner, slot_count)
        slots_low = lax.all_gather(master_slots.astype(BF), "tok", axis=0, tiled=True)
        vectors = lax.all_gather(vector_master.astype(BF), "tok", axis=0, tiled=True).astype(F32)
        vecs, b_u = vectors[: 8 * D].reshape(8, D), vectors[8 * D :].reshape(1, FF)
        cluster = tok_index // SD * CPS + cluster_order // CL
        target = cluster % tok_count
        chosen = target[None, :] == jnp.arange(tok_count, dtype=jnp.int32)[:, None]
        sent_counts = jnp.sum(chosen.astype(F32), axis=1)
        own_row = (jnp.arange(tok_count, dtype=jnp.int32) == tok_index).astype(F32)
        occupancy = lax.psum(own_row[:, None] * sent_counts[None, :], ("tok", "rep")).astype(jnp.int32)
        send_x, send_c, meta = pl.pallas_call(
            functools.partial(send_kernel, cap),
            out_shape=(block, block, meta_shape),
            in_specs=[VMEM] * 3,
            out_specs=(VMEM,) * 3,
            compiler_params=pltpu.CompilerParams(vmem_limit_bytes=VMEM_LIMIT),
            name="send_rows",
        )(tokens, cotangent, order)
        recv_x, recv_meta = (jnp.stack(swap_blocks(b)) for b in (send_x, meta))
        x_c = pl.pallas_call(
            functools.partial(seat_kernel, cap),
            out_shape=row_block,
            in_specs=[VMEM] * 2,
            out_specs=VMEM,
            compiler_params=pltpu.CompilerParams(vmem_limit_bytes=VMEM_LIMIT),
            name="seat_rows",
        )(recv_x, recv_meta)
        cots = [send_c[k] for k in range(SD)]

    cots = swap_blocks(cots)
    *out_blocks, heads, act, hid, q, k, v, p, slope, n1, n2, rs1, rs2 = forward(
        cap, positions, slots_low, vecs, b_u, x_c, recv_meta
    )
    out_blocks = swap_blocks(out_blocks)
    *ing_blocks, shares, d_up, d_q, d_k, d_v, d_proj, d_br = backward(
        cap, positions, slots_low, vecs, recv_meta, cots, (q, k, v, p, slope, n1, n2, rs1, rs2)
    )
    ing_blocks = swap_blocks(ing_blocks)
    grads = weight_grads_of(
        total_slots, positions, x_c, (heads, act, d_up, d_q, d_k, d_v, d_proj, hid, d_br)
    )
    if four_planes:
        total, vec_owned = reduce_all(grads, shares, slot_count)
    else:
        total = lax.psum(lax.psum_scatter(grads, "tok", scatter_dimension=0, tiled=True), "rep")
        grad_vector = shares[:, 0:9].reshape(-1)
        vec_owned = lax.psum(lax.psum_scatter(grad_vector, "tok", scatter_dimension=0, tiled=True), "rep")
    output, input_grad, entropy = pl.pallas_call(
        functools.partial(return_kernel, cap),
        out_shape=(row_block, row_block, jax.ShapeDtypeStruct((1, ROWS), BF)),
        in_specs=[VMEM] * (2 * SD + 1),
        out_specs=(VMEM,) * 3,
        compiler_params=pltpu.CompilerParams(vmem_limit_bytes=VMEM_LIMIT),
        name="return_rows",
    )(order, *out_blocks, *ing_blocks)

    used = jnp.any(
        positions[None, :] == (tok_index * slot_count + jnp.arange(slot_count, dtype=I32))[:, None], axis=1
    )
    owned_grad = jnp.where(used[:, None, None], total.astype(F32), 0.0)
    first_new, second_new, master_new = adam_update(
        owned_grad, master_slots, moment_one, moment_two, rate_matrix
    )
    vec_first, vec_second, vec_new = adam_update(
        vec_owned, vector_master, vector_moment_one, vector_moment_two, rate_vector
    )
    return (
        output,
        input_grad,
        owned_grad,
        first_new,
        second_new,
        master_new,
        master_new.astype(BF),
        vec_owned,
        vec_first,
        vec_second,
        vec_new,
        vec_new.astype(BF),
        entropy.reshape(-1),
        occupancy,
    )


def solution(mesh):
    placed = (
        P(("rep", "tok"), None),
        P(("rep", "tok"), None),
        P(("rep", "tok")),
        P(),
        P("tok", None, None),
        P("tok", None, None),
        P("tok", None, None),
        P("tok"),
        P("tok"),
        P("tok"),
    )
    return jax.shard_map(
        local,
        mesh=mesh,
        in_specs=placed,
        out_specs=(
            P(("rep", "tok"), None),
            P(("rep", "tok"), None),
            P("tok", None, None),
            P("tok", None, None),
            P("tok", None, None),
            P("tok", None, None),
            P("tok", None, None),
            P("tok"),
            P("tok"),
            P("tok"),
            P("tok"),
            P("tok"),
            P(("rep", "tok")),
            P(),
        ),
        check_vma=False,
    )
```

```python
import functools
import math

import jax
import jax.numpy as jnp
from jax import lax
from jax.experimental import pallas as pl
from jax.experimental.pallas import tpu as pltpu
from jax.sharding import PartitionSpec as P

D = 768
HEADS = 12
HD = 64
FF = 3072
SD = 4
CL = 128
NBLK = 96
STEP = 10
CPS = 32
WROWS = 9216
BLK = 96
ROWS = 1024
PAIRS = HEADS // 2
PW = 2 * HD
TM = 512
META = 16
VMEM_LIMIT = 63 << 20
FC = 768

norm_epsilon = 1e-06
beta_first = 0.9
beta_second = 0.999
adam_epsilon = 1e-08
weight_decay = 0.01
rate_matrix = 0.02
rate_vector = 0.2

BF = jnp.bfloat16
F32 = jnp.float32
I32 = jnp.int32

VMEM = pl.BlockSpec(memory_space=pltpu.VMEM)
SMEM = pl.BlockSpec(memory_space=pltpu.SMEM)
ANY = pl.BlockSpec(memory_space=pl.ANY)

NN = (((1,), (0,)), ((), ()))
NT = (((1,), (1,)), ((), ()))
TN = (((0,), (0,)), ((), ()))


def mm(a, b, dims=NN):
    return lax.dot_general(a, b, dims, preferred_element_type=F32)


def slot_positions(block_owner, slot_count):
    owners = block_owner[:, 0]
    blocks = owners.shape[0]
    shared = owners[:, None] == owners[None, :]
    before = (
        jnp.arange(blocks, dtype=jnp.int32)[None, :] < jnp.arange(blocks, dtype=jnp.int32)[:, None]
    )
    earlier = jnp.sum((shared & before).astype(jnp.int32), axis=1)
    return owners * slot_count + earlier


def adam_update(grad_now, weight_old, first_old, second_old, rate_step):
    first_new = beta_first * first_old + (1.0 - beta_first) * grad_now
    second_new = beta_second * second_old + (1.0 - beta_second) * grad_now * grad_now
    first_hat = first_new / (1.0 - beta_first**STEP)
    second_hat = second_new / (1.0 - beta_second**STEP)
    weight_new = weight_old - rate_step * (
        first_hat / (jnp.sqrt(second_hat) + adam_epsilon) + weight_decay * weight_old
    )
    return (first_new, second_new, weight_new)


def route_slots(order, seat, cap):
    cluster = order // CL
    rel = lax.rem(cluster, SD) ^ seat
    place = (cluster // SD) * CL + lax.rem(order, CL) + 1
    chosen = lax.broadcasted_iota(I32, (8, ROWS), 0) == rel
    chosen_low = jnp.where(chosen, 1.0, 0.0).astype(BF)
    before = lax.broadcasted_iota(I32, (ROWS, ROWS), 0) < lax.broadcasted_iota(I32, (ROWS, ROWS), 1)
    before_low = jnp.where(before, 1.0, 0.0).astype(BF)
    running = mm(chosen_low, before_low)
    rank = jnp.sum(jnp.where(chosen, running, 0.0), axis=0, keepdims=True).astype(I32)
    return rel * cap + rank, place


def slot_matrix(slots, at, cap):
    rows = lax.broadcasted_iota(I32, (cap, ROWS), 0) + at * cap
    return jnp.where(rows == slots, 1.0, 0.0).astype(BF)


def send_kernel(cap, tokens, cotangent, order, send_x, send_c, meta):
    seat = lax.rem(lax.axis_index("tok"), SD)
    slots, place = route_slots(order[...], seat, cap)
    digits = jnp.concatenate([place // CL, lax.rem(place, CL)] + [place * 0] * 6, axis=0).astype(F32).astype(BF)
    for at in range(SD):
        picked = slot_matrix(slots, at, cap)
        send_x[at] = mm(picked, tokens[...]).astype(BF)
        send_c[at] = mm(picked, cotangent[...]).astype(BF)
        coded = mm(digits, picked, NT)
        line = jnp.concatenate([coded[0:1], coded[1:2]], axis=1)
        meta[at] = jnp.broadcast_to(line, (META, D)).astype(BF)


def remote(src, dst, send_sem, recv_sem, tok, rep):
    return pltpu.make_async_remote_copy(
        src_ref=src,
        dst_ref=dst,
        send_sem=send_sem,
        recv_sem=recv_sem,
        device_id={"tok": tok, "rep": rep},
        device_id_type=pl.DeviceIdType.MESH,
    )


def loop(n, body):
    def run(i, c):
        body(i)
        return c

    lax.fori_loop(0, n, run, 0)


class Place:
    def __init__(self):
        self.me = me = lax.axis_index("tok")
        self.z = z = lax.axis_index("rep")
        core, x, y = me % 2, (me // 2) % 2, me // 4
        self.twin = me + 1 - 2 * core
        self.xn = me + 2 - 4 * x
        self.yn = me + 4 - 8 * y
        self.dn = self.xn + 4 - 8 * y
        self.side = z % 2
        self.zp = z + 1 - 2 * self.side

    def twin_of(self, tok):
        return tok + 1 - 2 * (tok % 2)

    def greet(self, peers):
        barrier = pltpu.get_barrier_semaphore()
        for tok, rep in peers:
            pl.semaphore_signal(
                barrier, inc=1, device_id={"tok": tok, "rep": rep}, device_id_type=pl.DeviceIdType.MESH
            )
        return lambda: pl.semaphore_wait(barrier, len(peers))


def seat_matrix(meta, first, rows, cap):
    hi = jnp.concatenate([meta[k, 0:8, 0:cap] for k in range(SD)], axis=1).astype(F32)[0:1]
    lo = jnp.concatenate([meta[k, 0:8, cap : 2 * cap] for k in range(SD)], axis=1).astype(F32)[0:1]
    at = (hi * CL + lo).astype(I32)
    seats = lax.broadcasted_iota(I32, (rows, SD * cap), 0) + (first + 1)
    return jnp.where(seats == at, 1.0, 0.0).astype(BF)


def seat_part(meta, k, cap):
    hi = meta[k, 0:8, 0:cap].astype(F32)[0:1]
    lo = meta[k, 0:8, cap : 2 * cap].astype(F32)[0:1]
    at = (hi * CL + lo).astype(I32)
    seats = lax.broadcasted_iota(I32, (ROWS, cap), 0) + 1
    return jnp.where(seats == at, 1.0, 0.0).astype(BF)


def seat_rows(meta, blocks, cap, to):
    def body(t):
        r0 = pl.multiple_of(t * 256, 256)
        rows = blocks[...].reshape(SD * cap, D)
        to[pl.ds(r0, 256), :] = mm(seat_matrix(meta, r0, 256, cap), rows).astype(BF)

    loop(ROWS // 256, body)


def seat_kernel(cap, blocks, meta, to):
    seat_rows(meta, blocks, cap, to)


def gather_kernel(
    cap,
    count,
    tokens_h,
    cotangent_h,
    order,
    master_h,
    vector,
    owner_of,
    slots,
    x_c,
    cot_0,
    cot_1,
    cot_2,
    cot_3,
    recv_meta,
    vecs,
    b_u,
    occupancy,
    positions,
    tokens,
    cotangent,
    master,
    own,
    send_x,
    send_c,
    meta,
    recv_x,
    got_meta,
    mine,
    by_z,
    by_tok,
    x_s,
    x_r,
    y_s,
    y_r,
    d_s,
    d_r,
    zx_s,
    zx_r,
    zd_s,
    zd_r,
    zy_s,
    zy_r,
    p_s,
    p_r,
    row_s,
    row_r,
    z_s,
    z_r,
    t_s,
    t_r,
    local_s,
):
    at = Place()
    me, z, side = at.me, at.z, at.side
    n_tok, n_rep = 8, 4
    peers = [((me + d) % n_tok, z) for d in range(1, n_tok)] + [(me, (z + d) % n_rep) for d in range(1, n_rep)]
    fetch = [
        pltpu.make_async_copy(src, dst, local_s.at[i])
        for i, (src, dst) in enumerate(((master_h, master), (tokens_h, tokens), (cotangent_h, cotangent)))
    ]
    for copy in fetch:
        copy.start()
    wait_peers = at.greet(peers)
    fetch[0].wait()

    def cast(s):
        own[s] = master[s].astype(BF)

    loop(count, cast)
    wait_peers()

    half = count // 2

    def slot(owner, s):
        return slots.at[owner * count + s]

    def to_x(s):
        return remote(own.at[s], slot(me, s), x_s.at[s], x_r.at[s], at.xn, z)

    def to_y(s):
        return remote(own.at[s], slot(me, s), y_s.at[s], y_r.at[s], at.yn, z)

    def on_y(s):
        return remote(slot(at.xn, s), slot(at.xn, s), d_s.at[s], d_r.at[s], at.yn, z)

    def x_on_z(s):
        return remote(slot(at.xn, s), slot(at.xn, s), zx_s.at[s], zx_r.at[s], me, at.zp)

    def d_on_z(s):
        return remote(slot(at.dn, s), slot(at.dn, s), zd_s.at[s], zd_r.at[s], me, at.zp)

    def y_on_z(s):
        return remote(slot(at.yn, s), slot(at.yn, s), zy_s.at[s], zy_r.at[s], me, at.zp)

    few = count // 3
    most = count - few

    def straight(j):
        return few * side + j

    def shared(j):
        return most * side + j

    def lacking(j):
        return most * (1 - side) + j

    owners = (me, at.xn, at.yn, at.dn)

    def to_twin(q, s):
        src = own.at[s] if q == 0 else slot(owners[q], s)
        return remote(src, slot(owners[q], s), p_s.at[q, s], p_r.at[q, s], at.twin, z)

    def near(j):
        return (half + 1) * side + j

    def far(j):
        return (half + 1) * (1 - side) + j

    loop(half, lambda j: to_x(near(j)).start())
    to_x(half).start()
    loop(few, lambda j: to_y(shared(j)).start())
    loop(count, lambda s: to_twin(0, s).start())
    keep = pltpu.make_async_copy(own, slots.at[pl.ds(me * count, count)], local_s.at[3])
    keep.start()
    fetch[1].wait()
    fetch[2].wait()

    seat = me % SD
    slot_of, place = route_slots(order[...], seat, cap)
    digits = jnp.concatenate([place // CL, lax.rem(place, CL)] + [place * 0] * 6, axis=0).astype(F32).astype(BF)
    for k in range(SD):
        picked = slot_matrix(slot_of, k, cap)
        send_x[k] = mm(picked, tokens[...]).astype(BF)
        send_c[k] = mm(picked, cotangent[...]).astype(BF)
        coded = mm(digits, picked, NT)
        line = jnp.concatenate([coded[0:1], coded[1:2]], axis=1)
        meta[k] = jnp.broadcast_to(line, (META, D)).astype(BF)
    seats = (me, at.twin, at.xn, at.twin_of(at.xn))
    rows_of = ((meta, got_meta), (send_x, recv_x))

    def row_copy(i, k):
        src, dst = rows_of[i]
        return remote(src.at[k], dst.at[k], row_s.at[i, k], row_r.at[i, k], seats[k], z)

    for i in range(2):
        src, dst = rows_of[i]
        for k in (2, 3, 1):
            row_copy(i, k).start()
        dst[0] = src[0]
    put_c = [
        pltpu.make_async_copy(send_c.at[k], to, local_s.at[4 + k])
        for k, to in enumerate((cot_0, cot_1, cot_2, cot_3))
    ]
    for copy in put_c:
        copy.start()

    residue = lax.rem(me // SD * CPS + order[...] // CL, n_tok)
    hit = lax.broadcasted_iota(I32, (128, ROWS), 0) == residue
    for i in range(9):
        mine[i : i + 1] = vector[i * 128 : (i + 1) * 128].reshape(1, 128).astype(BF).astype(F32)
    block_row = lax.broadcasted_iota(I32, (NBLK, NBLK), 0)
    block_col = lax.broadcasted_iota(I32, (NBLK, NBLK), 1)
    by_col = owner_of[...].astype(F32)
    by_row = lane_sum(jnp.where(block_row == block_col, by_col, 0.0))
    earlier = jnp.where((by_row == by_col) & (block_row < block_col), 1.0, 0.0)
    positions[...] = (by_col * count + jnp.sum(earlier, axis=0, keepdims=True)).astype(I32)
    by_z[0] = mm(jnp.ones((8, ROWS), BF), jnp.where(hit, 1.0, 0.0).astype(BF), NT)

    def z_copy(d):
        return remote(by_z.at[0], by_z.at[d], z_s.at[d], z_r.at[d], me, (z + d) % n_rep)

    def t_copy(d):
        return remote(mine, by_tok.at[d], t_s.at[d], t_r.at[d], (me + d) % n_tok, z)

    for d in range(1, n_rep):
        z_copy(d).start()
    for d in range(1, n_rep):
        z_copy(d).wait()
    mine[16:24] = by_z[0] + by_z[1] + by_z[2] + by_z[3]
    for d in range(1, n_tok):
        t_copy(d).start()

    def x_here(s):
        to_x_in(s).wait_recv()
        on_y(s).start()
        to_twin(1, s).start()

    def to_x_in(s):
        return remote(own.at[s], slot(at.xn, s), x_s.at[s], x_r.at[s], at.xn, z)

    def y_in(s):
        return remote(own.at[s], slot(at.yn, s), y_s.at[s], y_r.at[s], at.yn, z)

    def d_in(s):
        return remote(own.at[s], slot(at.dn, s), d_s.at[s], d_r.at[s], at.yn, z)

    def y_here(s):
        y_in(s).wait_recv()
        to_twin(2, s).start()

    def rest(j):
        return few + j

    for j in range(half):
        x_here(near(j))
        x_on_z(near(j)).start()
        if j < few:
            y_here(shared(j))
            y_on_z(shared(j)).start()
    x_here(half)
    loop(most - few, lambda j: to_y(rest(j)).start())

    def second(j):
        x_on_z(far(j)).wait_recv()
        to_twin(1, far(j)).start()
        d_in(near(j)).wait_recv()
        d_on_z(near(j)).start()
        to_twin(3, near(j)).start()

    loop(half, second)
    d_in(half).wait_recv()
    to_twin(3, half).start()
    loop(most - few, lambda j: y_here(rest(j)))

    def lacking_here(j):
        y_on_z(lacking(j)).wait_recv()
        to_twin(2, lacking(j)).start()

    loop(few, lacking_here)
    for i in (0, 1):
        for k in (2, 3, 1):
            row_copy(i, k).wait_recv()
    recv_meta[...] = got_meta[...]
    seat_rows(got_meta, recv_x, cap, x_c)

    def third(j):
        d_on_z(far(j)).wait_recv()
        to_twin(3, far(j)).start()

    loop(half, third)

    by_tok[0] = mine[...]
    for d in range(1, n_tok):
        t_copy(d).wait()
    for owner in range(n_tok):
        share = by_tok[(me + n_tok - owner) % n_tok]
        occupancy[owner : owner + 1, :] = share[16:17, 0:n_tok].astype(I32)
        for i in range(9):
            chunk = owner * 9 + i
            row, lane = chunk // 6, chunk % 6 * 128
            if row < 8:
                vecs[row : row + 1, lane : lane + 128] = share[i : i + 1]
            else:
                lane += (row - 8) * D
                b_u[:, lane : lane + 128] = share[i : i + 1]
    for i in range(2):
        for k in (2, 3, 1):
            row_copy(i, k).wait_send()
    for copy in put_c:
        copy.wait()
    keep.wait()

    def sent_half(j):
        to_x(near(j)).wait_send()
        on_y(near(j)).wait_send()
        x_on_z(near(j)).wait_send()
        d_on_z(near(j)).wait_send()

    loop(half, sent_half)
    to_x(half).wait_send()
    on_y(half).wait_send()

    def sent(s):
        for q in range(4):
            to_twin(q, s).wait()

    loop(count, sent)
    loop(most, lambda j: to_y(straight(j)).wait_send())
    loop(few, lambda j: y_on_z(shared(j)).wait_send())


def gather_all(cap, tokens, cotangent, order, master, vector, block_owner):
    count = master.shape[0]
    rows = jax.ShapeDtypeStruct((ROWS, D), BF)
    part = jax.ShapeDtypeStruct((cap, D), BF)
    dma = pltpu.SemaphoreType.DMA
    block = pltpu.VMEM((SD, cap, D), BF)
    meta = pltpu.VMEM((SD, META, D), BF)
    return pl.pallas_call(
        functools.partial(gather_kernel, cap, count),
        out_shape=(
            jax.ShapeDtypeStruct((8 * count, BLK, D), BF),
            rows,
            part,
            part,
            part,
            part,
            jax.ShapeDtypeStruct((SD, META, D), BF),
            jax.ShapeDtypeStruct((8, D), F32),
            jax.ShapeDtypeStruct((1, FF), F32),
            jax.ShapeDtypeStruct((8, 8), I32),
            jax.ShapeDtypeStruct((1, NBLK), I32),
        ),
        in_specs=[ANY, ANY, VMEM, ANY, VMEM, VMEM],
        out_specs=(ANY, VMEM) + (ANY,) * SD + (VMEM,) * 5,
        scratch_shapes=[
            pltpu.VMEM((ROWS, D), BF),
            pltpu.VMEM((ROWS, D), BF),
            pltpu.VMEM((count, BLK, D), F32),
            pltpu.VMEM((count, BLK, D), BF),
            block,
            block,
            meta,
            block,
            meta,
            pltpu.VMEM((24, 128), F32),
            pltpu.VMEM((4, 8, 128), F32),
            pltpu.VMEM((8, 24, 128), F32),
        ]
        + [dma((count,))] * 12
        + [dma((4, count))] * 2
        + [dma((2, SD))] * 2
        + [dma((4,))] * 2
        + [dma((8,))] * 2
        + [dma((8,))],
        compiler_params=pltpu.CompilerParams(collective_id=0, has_side_effects=True, vmem_limit_bytes=VMEM_LIMIT),
        name="gather",
    )(tokens, cotangent, order, master, vector, block_owner.reshape(1, NBLK))


def return_kernel(cap, order, *refs):
    outs, ings, (out, ing, entropy) = refs[:SD], refs[SD : 2 * SD], refs[2 * SD :]
    seat = lax.rem(lax.axis_index("tok"), SD)
    slots, _ = route_slots(order[...], seat, cap)
    picked = jnp.concatenate([slot_matrix(slots, at, cap) for at in range(SD)], axis=0)
    for to, blocks in ((out, outs), (ing, ings)):
        rows = jnp.concatenate([block[0:cap, :] for block in blocks], axis=0)
        to[...] = mm(picked, rows, TN).astype(BF)
    line = jnp.concatenate([block[cap : cap + 8, 0:cap] for block in outs], axis=1)
    entropy[...] = mm(line, picked)[0:1].astype(BF)


def swap_blocks(blocks):
    n = lax.axis_size("tok")
    parts = [blocks[0]]
    for k in range(1, SD):
        parts.append(lax.ppermute(blocks[k], "tok", [(i, i ^ k) for i in range(n)]))
    return parts


def reduce_kernel(
    cap,
    count,
    split,
    grads,
    vec,
    order,
    out_0,
    out_1,
    out_2,
    out_3,
    ing_0,
    ing_1,
    ing_2,
    ing_3,
    total,
    vec_out,
    output,
    input_grad,
    entropy,
    out_v,
    ing_v,
    slot_of,
    a,
    tw,
    rd,
    rx,
    ry,
    o,
    rz1,
    pz,
    rz2,
    fz,
    vt,
    va,
    vb,
    vc,
    a_l,
    keep_l,
    p_s,
    p_r,
    d_s,
    d_r,
    x_s,
    x_r,
    y_s,
    y_r,
    z1_s,
    z1_r,
    z2_s,
    z2_r,
    z3_s,
    z3_r,
    t_s,
    t_r,
    v_s,
    v_r,
    row_l,
):
    at = Place()
    me, z = at.me, at.z
    n_tok, n_rep = 8, 4
    peers = [((me + d) % n_tok, z) for d in range(1, n_tok)] + [(me, (z + d) % n_rep) for d in range(1, n_rep)]
    wait_peers = at.greet(peers)
    owners = (me, at.xn, at.yn, at.dn)

    def load(q):
        return pltpu.make_async_copy(grads.at[pl.ds(owners[q] * count, count)], a.at[q], a_l.at[q])

    for q in (3, 1, 2, 0):
        load(q).start()
    rows_in = [
        pltpu.make_async_copy(src, to.at[k], row_l.at[i, k])
        for i, (blocks, to) in enumerate((((out_0, out_1, out_2, out_3), out_v), ((ing_0, ing_1, ing_2, ing_3), ing_v)))
        for k, src in enumerate(blocks)
    ]
    for copy in rows_in:
        copy.start()
    wait_peers()

    def to_twin(q, s):
        src = grads.at[at.twin_of(owners[q]) * count + s]
        return remote(src, tw.at[q, s], p_s.at[q, s], p_r.at[q, s], at.twin, z)

    def d_y(s):
        return remote(a.at[3, s], rd.at[s], d_s.at[s], d_r.at[s], at.yn, z)

    def d_x(s):
        return remote(a.at[3, s], rd.at[s], d_s.at[s], d_r.at[s], at.xn, z)

    def to_x(s):
        return remote(a.at[1, s], rx.at[s], x_s.at[s], x_r.at[s], at.xn, z)

    def to_y(s):
        return remote(a.at[2, s], ry.at[s], y_s.at[s], y_r.at[s], at.yn, z)

    def z_in(s):
        return remote(o.at[s], rz1.at[s], z1_s.at[s], z1_r.at[s], me, at.zp)

    def z_swap(s):
        return remote(pz.at[s], rz2.at[s], z2_s.at[s], z2_r.at[s], me, n_rep - 1 - z)

    def z_out(s):
        return remote(fz.at[s], fz.at[s], z3_s.at[s], z3_r.at[s], me, at.zp)

    def keep(s):
        return pltpu.make_async_copy(fz.at[s], total.at[s], keep_l.at[s])

    def f32(ref, *index):
        return ref[index].astype(F32)

    def twin_round(i):
        for s in (i, split + i):
            to_twin(3, s).start()
        to_twin(1, i).start()
        to_twin(2, split + i).start()
        to_twin(2, i).start()
        to_twin(1, split + i).start()
        for s in (i, split + i):
            to_twin(0, s).start()

    loop(split, twin_round)
    for q in (3, 2, 1, 0):
        to_twin(q, count - 1).start()

    def v_tok(d):
        return remote(vec.at[(me + d) % n_tok], vt.at[d], t_s.at[d], t_r.at[d], (me + d) % n_tok, z)

    def v_rep(i, src):
        return remote(src, vb.at[i], v_s.at[i], v_r.at[i], me, at.zp if i == 0 else (z + 2) % n_rep)

    for d in range(1, n_tok):
        v_tok(d).start()

    slots_here, _ = route_slots(order[...], me % SD, cap)
    slot_of[...] = slots_here

    def join(q, s):
        to_twin(q, s).wait_recv()
        return f32(a, q, s) + f32(tw, q, s)

    def first(s, send):
        a[3, s] = join(3, s).astype(BF)
        send(s).start()

    def plain(q, s, send):
        a[q, s] = join(q, s).astype(BF)
        send(s).start()

    def joined(q, s, arrived, send):
        arrived(s).wait_recv()
        a[q, s] = (join(q, s) + f32(rd, s)).astype(BF)
        send(s).start()

    inner = (z == 1) | (z == 2)
    outer = (z == 0) | (z == 3)

    def own(s):
        to_x(s).wait_recv()
        to_y(s).wait_recv()
        o[s] = (join(0, s) + f32(rx, s) + f32(ry, s)).astype(BF)
        pl.when(outer)(lambda: z_in(s).start())

    def middle(s):
        @pl.when(inner)
        def _():
            z_in(s).wait_recv()
            pz[s] = (f32(o, s) + f32(rz1, s)).astype(BF)
            z_swap(s).start()

    def last(s):
        @pl.when(inner)
        def _():
            z_swap(s).wait_recv()
            fz[s] = (f32(pz, s) + f32(rz2, s)).astype(BF)
            z_out(s).start()
            keep(s).start()

    def taken(s):
        @pl.when(outer)
        def _():
            z_out(s).wait_recv()
            keep(s).start()

    def pick_rows(i):
        ts = pl.ds(pl.multiple_of(lax.rem(i, 4) * 256, 256), 256)
        hit = lax.broadcasted_iota(I32, (SD * cap, 256), 0) == slot_of[:, ts]
        picked = jnp.where(hit, 1.0, 0.0).astype(BF)

        @pl.when(i < 4)
        def _():
            rows = jnp.concatenate([out_v[k, 0:cap, :] for k in range(SD)], axis=0)
            output[ts, :] = mm(picked, rows, TN).astype(BF)
            line = jnp.concatenate([out_v[k, cap : cap + 8, 0:cap] for k in range(SD)], axis=1)
            entropy[:, ts] = mm(line, picked)[0:1].astype(BF)

        @pl.when(i >= 4)
        def _():
            rows = jnp.concatenate([ing_v[k] for k in range(SD)], axis=0)
            input_grad[ts, :] = mm(picked, rows, TN).astype(BF)

    for q in (3, 1, 2, 0):
        load(q).wait()
    for copy in rows_in:
        copy.wait()
    late = count - split

    def steps(i, lag, more):
        r = i - lag
        pl.when((r >= 0) & (r < split))(lambda: more(r, True))
        pl.when((r >= 0) & (r < late))(lambda: more(split + r, False))

    def round_of(i):
        steps(i, 0, lambda s, by_x: first(s, d_x if by_x else d_y))
        steps(i, 0, lambda s, by_x: plain(1, s, to_x) if by_x else plain(2, s, to_y))
        steps(i, 1, lambda s, by_x: joined(2, s, d_x, to_y) if by_x else joined(1, s, d_y, to_x))
        steps(i, 2, lambda s, _: own(s))
        steps(i, 3, lambda s, _: middle(s))
        steps(i, 4, lambda s, _: last(s))
        steps(i, 5, lambda s, _: taken(s))
        pl.when((i >= 1) & (i < 9))(lambda: pick_rows(i - 1))

    loop(2, round_of)

    v_sum = vec[me]
    for d in range(1, n_tok):
        v_tok(d).wait()
        v_sum = v_sum + vt[d]
    va[...] = v_sum
    v_rep(0, va).start()

    loop(2, lambda i: round_of(2 + i))
    v_rep(0, va).wait()
    vc[...] = va[...] + vb[0]
    v_rep(1, vc).start()
    loop(late + 1, lambda i: round_of(4 + i))
    v_rep(1, vc).wait()
    vec_out[...] = vc[...] + vb[1]

    def sent(s):
        for q in range(4):
            to_twin(q, s).wait_send()
        d_y(s).wait_send()
        to_x(s).wait_send()
        to_y(s).wait_send()
        keep(s).wait()

    loop(count, sent)

    @pl.when(outer)
    def _():
        loop(count, lambda s: z_in(s).wait_send())

    @pl.when(inner)
    def _():
        def back(s):
            z_swap(s).wait_send()
            z_out(s).wait_send()

        loop(count, back)


def reduce_all(cap, grads, shares, order, outs, ings, count):
    dma = pltpu.SemaphoreType.DMA
    part = pltpu.VMEM((count, BLK, D), BF)
    whole = pltpu.VMEM((4, count, BLK, D), BF)
    line = pltpu.VMEM((16, 128), F32)
    rows = jax.ShapeDtypeStruct((ROWS, D), BF)
    total, vec, output, input_grad, entropy = pl.pallas_call(
        functools.partial(reduce_kernel, cap, count, count // 2),
        out_shape=(
            jax.ShapeDtypeStruct((count, BLK, D), BF),
            jax.ShapeDtypeStruct((16, 128), F32),
            rows,
            rows,
            jax.ShapeDtypeStruct((1, ROWS), BF),
        ),
        in_specs=[ANY, VMEM, VMEM] + [ANY] * (2 * SD),
        out_specs=(ANY,) + (VMEM,) * 4,
        scratch_shapes=[
            pltpu.VMEM((SD, cap + META, D), BF),
            pltpu.VMEM((SD, cap, D), BF),
            pltpu.VMEM((1, ROWS), I32),
            whole,
            whole,
        ]
        + [part] * 8
        + [pltpu.VMEM((8, 16, 128), F32), line, pltpu.VMEM((2, 16, 128), F32), line]
        + [dma((4,)), dma((count,))]
        + [dma((4, count))] * 2
        + [dma((count,))] * 12
        + [dma((8,))] * 2
        + [dma((2,))] * 2
        + [dma((2, SD))],
        compiler_params=pltpu.CompilerParams(collective_id=1, has_side_effects=True, vmem_limit_bytes=VMEM_LIMIT),
        name="reduce",
    )(grads, shares, order, *outs, *ings)
    return total, vec[0:9].reshape(-1), output, input_grad, entropy


V_BQ, V_BV, V_BO, V_BD, V_G1, V_C1, V_G2, V_C2 = range(8)


def inverse(x):
    r = pl.reciprocal(x, approx=True)
    return r * (2.0 - x * r)


def erf_parts(v):
    t = inverse(1.0 + (0.3275911 / math.sqrt(2.0)) * jnp.abs(v))
    e = jnp.exp2((v * v) * (-0.5 / math.log(2.0)))
    poly = 0.5 * 1.061405429
    for c in (-1.453152027, 1.421413741, -0.284496736, 0.254829592):
        poly = poly * t + 0.5 * c
    tail = poly * (t * e)
    return jnp.where(v >= 0.0, 1.0 - tail, tail), e


def lane_sum(x):
    return jnp.sum(x, axis=1, keepdims=True)


def gelu_parts(v):
    phi, e = erf_parts(v)
    return v * phi, phi + v * (e * (1.0 / math.sqrt(2.0 * math.pi)))


def weight_copies(pos, slots, w, sem, first):
    def copy(b):
        return pltpu.make_async_copy(slots.at[pos[first + b]], w.at[pl.ds(b * BLK, BLK)], sem)

    n = w.shape[0] // BLK
    return (lambda: loop(n, lambda b: copy(b).start())), (lambda: loop(n, lambda b: copy(b).wait()))


def halves_of_heads():
    lane = lax.broadcasted_iota(I32, (1, PW), 1)
    m0 = jnp.where(lane < HD, 1.0, 0.0).astype(BF)
    m1 = jnp.where(lane < HD, 0.0, 1.0).astype(BF)
    return lambda pair: jnp.concatenate([pair * m0, pair * m1], axis=0)


def tile_rows(t):
    return pl.ds(pl.multiple_of(t * TM, TM), TM)


def forward_kernel(
    cap,
    pos,
    slots,
    vecs,
    b_u,
    x_h,
    meta,
    back_0,
    back_1,
    back_2,
    back_3,
    heads_h,
    act_h,
    hid_h,
    q_h,
    k_h,
    v_h,
    p_h,
    slope_h,
    n1_h,
    n2_h,
    rs1_h,
    rs2_h,
    wqkv,
    wo,
    wu,
    wd,
    x_c,
    heads,
    act,
    hid,
    q,
    k,
    v,
    p_all,
    slope,
    n1,
    n2,
    rs1,
    rs2,
    out_c,
    ent,
    hid_t,
    w_sem,
    x_sem,
    o_sem,
):
    inv = 1.0 / math.sqrt(HD)
    get_x = pltpu.make_async_copy(x_h, x_c, x_sem)
    get_x.start()
    weights = [
        weight_copies(pos, slots, w, w_sem.at[i], first)
        for i, (w, first) in enumerate(((wqkv, 0), (wo, 24), (wu, 32), (wd, 64)))
    ]
    for start, _ in weights:
        start()
    get_x.wait()
    apart = halves_of_heads()

    def vec(i):
        return vecs[i : i + 1, :]

    saved = (
        (heads, heads_h),
        (act, act_h),
        (hid, hid_h),
        (q, q_h),
        (k, k_h),
        (v, v_h),
        (slope, slope_h),
        (n1, n1_h),
        (n2, n2_h),
        (rs1, rs1_h),
        (rs2, rs2_h),
    )

    def save(t, i):
        src, dst = saved[i]
        return pltpu.make_async_copy(src.at[tile_rows(t)], dst.at[tile_rows(t)], o_sem.at[i])

    def save_p(t):
        n = TM // CL
        cs = pl.ds(t * n, n)
        return pltpu.make_async_copy(p_all.at[cs], p_h.at[cs], o_sem.at[len(saved)])

    def normal(r, n, rs, rows):
        c = r - lane_sum(r) * (1.0 / D)
        scale = lax.rsqrt(lane_sum(c * c) * (1.0 / D) + norm_epsilon)
        rs[rows, :] = jnp.broadcast_to(scale, (TM, 128))
        n[rows, :] = c * scale

    def tile(t):
        rows = tile_rows(t)
        first = t == 0
        pl.when(first)(weights[0][1])
        x = x_c[rows, :]
        q[rows, :] = ((mm(x, wqkv[0:D, :]) + vec(V_BQ)).astype(BF).astype(F32) * inv).astype(BF)
        k[rows, :] = mm(x, wqkv[D : 2 * D, :]).astype(BF)
        v[rows, :] = (mm(x, wqkv[2 * D :, :]) + vec(V_BV)).astype(BF)

        def attend(c):
            gr = pl.ds(pl.multiple_of(t * TM + c * CL, CL), CL)
            total = jnp.zeros((1, CL), F32)
            for p in range(PAIRS):
                ps = slice(p * PW, (p + 1) * PW)
                scores = mm(apart(k[gr, ps]), q[gr, ps], NT)
                halves = []
                for h in range(2):
                    sh = scores[h * CL : (h + 1) * CL]
                    sh = sh - jnp.max(sh, axis=0, keepdims=True)
                    e = jnp.exp(sh)
                    tot = jnp.sum(e, axis=0, keepdims=True)
                    r = 1.0 / tot
                    total += jnp.log(tot) - jnp.sum(e * sh, axis=0, keepdims=True) * r
                    halves.append((e * r).astype(BF))
                probs = jnp.concatenate(halves, axis=0)
                p_all[t * (TM // CL) + c, p] = probs
                heads[gr, ps] = mm(probs, apart(v[gr, ps]), TN).astype(BF)
            ent[:, gr] = jnp.broadcast_to(total * (1.0 / HEADS), (8, CL))

        loop(TM // CL, attend)
        pl.when(first)(weights[1][1])
        normal(x_c[rows, :].astype(F32) + mm(heads[rows, :], wo[...]) + vec(V_BO), n1, rs1, rows)
        hidden = n1[rows, :] * vec(V_G1) + vec(V_C1)
        hid[rows, :] = hidden.astype(BF)
        hid_t[...] = hidden
        pl.when(first)(weights[2][1])

        def widen(f):
            fs = pl.ds(pl.multiple_of(f * FC, FC), FC)
            g, g_slope = gelu_parts(mm(hid[rows, :], wu[fs, :], NT) + b_u[:, fs])
            act[rows, fs] = g.astype(BF)
            slope[rows, fs] = g_slope.astype(BF)

        loop(FF // FC, widen)
        pl.when(first)(weights[3][1])
        normal(hid_t[...] + mm(act[rows, :], wd[...]) + vec(V_BD), n2, rs2, rows)
        out_c[rows, :] = (n2[rows, :] * vec(V_G2) + vec(V_C2)).astype(BF)
        for i in range(len(saved)):
            save(t, i).start()
        save_p(t).start()

    loop(ROWS // TM, tile)

    for j, back in enumerate((back_0, back_1, back_2, back_3)):
        own = seat_part(meta, j, cap)
        back[0:cap, :] = mm(own, out_c[...], TN).astype(BF)
        line = mm(ent[...].astype(BF), own)
        back[cap:, :] = jnp.concatenate([line, line], axis=1)[0:1].astype(BF) * jnp.ones((META, 1), BF)

    def saved_all(t):
        for i in range(len(saved)):
            save(t, i).wait()
        save_p(t).wait()

    loop(ROWS // TM, saved_all)


def shape_of(kind, *shape):
    return jax.ShapeDtypeStruct(shape, kind)


def saved_shapes():
    rows, wide = ((ROWS, D), BF), ((ROWS, FF), BF)
    probs = ((ROWS // CL, PAIRS, 2 * CL, CL), BF)
    full, thin = ((ROWS, D), F32), ((ROWS, 128), F32)
    return rows, wide, probs, full, thin


def forward(cap, positions, slots, vecs, b_u, x_c, meta):
    rows, wide, probs, full, thin = saved_shapes()
    kept = (rows, wide, rows, rows, rows, rows, probs, wide, full, full, thin, thin)
    dma = pltpu.SemaphoreType.DMA
    return pl.pallas_call(
        functools.partial(forward_kernel, cap),
        out_shape=(shape_of(BF, cap + META, D),) * SD + tuple(shape_of(kind, *shape) for shape, kind in kept),
        in_specs=[SMEM, ANY, VMEM, VMEM, ANY, VMEM],
        out_specs=(VMEM,) * SD + (ANY,) * len(kept),
        scratch_shapes=[
            pltpu.VMEM((3 * D, D), BF),
            pltpu.VMEM((D, D), BF),
            pltpu.VMEM((FF, D), BF),
            pltpu.VMEM((FF, D), BF),
            pltpu.VMEM(*rows),
        ]
        + [pltpu.VMEM(*a) for a in kept]
        + [
            pltpu.VMEM(*rows),
            pltpu.VMEM((8, ROWS), F32),
            pltpu.VMEM((TM, D), F32),
            dma((4,)),
            dma,
            dma((12,)),
        ],
        compiler_params=pltpu.CompilerParams(vmem_limit_bytes=VMEM_LIMIT),
        name="forward",
    )(positions, slots, vecs, b_u, x_c, meta)


def backward_kernel(
    cap,
    pos,
    slots,
    vecs,
    meta,
    cot_0,
    cot_1,
    cot_2,
    cot_3,
    q_h,
    k_h,
    v_h,
    p_h,
    slope_h,
    n1_h,
    n2_h,
    rs1_h,
    rs2_h,
    back_0,
    back_1,
    back_2,
    back_3,
    shares,
    d_up_h,
    d_q_h,
    d_k_h,
    d_v_h,
    d_proj_h,
    d_br_h,
    wqkv,
    wo,
    wu,
    wd,
    blocks,
    q,
    k,
    v,
    p_all,
    d_up,
    n1,
    n2,
    rs1,
    rs2,
    d_proj,
    d_br,
    ing_c,
    d_h_t,
    res_t,
    gvec,
    g_bu,
    w_sem,
    c_sem,
    i_sem,
    o_sem,
):
    inv = 1.0 / math.sqrt(HD)
    get_c = [
        pltpu.make_async_copy(cot, blocks.at[j], c_sem.at[j]) for j, cot in enumerate((cot_0, cot_1, cot_2, cot_3))
    ]
    for copy in get_c:
        copy.start()
    fetch = [
        pltpu.make_async_copy(src, dst, i_sem.at[i])
        for i, (src, dst) in enumerate(
            (
                (n2_h, n2),
                (rs2_h, rs2),
                (slope_h, d_up),
                (n1_h, n1),
                (rs1_h, rs1),
                (v_h, v),
                (p_h, p_all),
                (k_h, k),
                (q_h, q),
            )
        )
    ]
    weights = [
        weight_copies(pos, slots, w, w_sem.at[i], first)
        for i, (w, first) in enumerate(((wd, 64), (wu, 32), (wo, 24), (wqkv, 0)))
    ]
    fetch[0].start()
    fetch[1].start()
    weights[0][0]()
    fetch[2].start()
    weights[1][0]()
    fetch[3].start()
    fetch[4].start()
    weights[2][0]()
    for i in range(5, 9):
        fetch[i].start()
    weights[3][0]()
    gvec[...] = jnp.zeros_like(gvec)
    g_bu[...] = jnp.zeros_like(g_bu)
    shares[...] = jnp.zeros_like(shares)
    for copy in get_c:
        copy.wait()
    seat_rows(meta, blocks, cap, d_br)
    apart = halves_of_heads()
    first_half = lax.broadcasted_iota(I32, (CL, PW), 1) < HD

    def vec(i):
        return vecs[i : i + 1, :]

    def add_vec(i, value):
        gvec[i : i + 1, :] += jnp.sum(value, axis=0, keepdims=True)

    saved = ((d_up, d_up_h), (q, d_q_h), (k, d_k_h), (v, d_v_h), (d_proj, d_proj_h), (d_br, d_br_h))

    def save(t, i):
        src, dst = saved[i]
        return pltpu.make_async_copy(src.at[tile_rows(t)], dst.at[tile_rows(t)], o_sem.at[i])

    def norm_back(e, n, rs, gain, shift):
        add_vec(gain, e * n)
        add_vec(shift, e)
        eg = e * vec(gain)
        return rs * (eg - lane_sum(eg) * (1.0 / D) - n * (lane_sum(eg * n) * (1.0 / D)))

    def tile(t):
        rows = tile_rows(t)
        start = t == 0

        @pl.when(start)
        def _():
            fetch[0].wait()
            fetch[1].wait()

        d_r2 = norm_back(d_br[rows, :].astype(F32), n2[rows, :], rs2[rows, 0:1], V_G2, V_C2)
        d_br[rows, :] = d_r2.astype(BF)
        add_vec(V_BD, d_br[rows, :].astype(F32))
        res_t[...] = d_r2

        @pl.when(start)
        def _():
            weights[0][1]()
            fetch[2].wait()

        def widen_back(f):
            fs = pl.ds(pl.multiple_of(f * FC, FC), FC)
            du = (mm(d_br[rows, :], wd[fs, :], NT) * d_up[rows, fs].astype(F32)).astype(BF)
            d_up[rows, fs] = du
            g_bu[:, fs] += jnp.sum(du.astype(F32), axis=0, keepdims=True)

        loop(FF // FC, widen_back)

        @pl.when(start)
        def _():
            weights[1][1]()
            fetch[3].wait()
            fetch[4].wait()

        d_h = res_t[...] + mm(d_up[rows, :], wu[...])
        d_r1 = norm_back(d_h, n1[rows, :], rs1[rows, 0:1], V_G1, V_C1)
        d_proj[rows, :] = d_r1.astype(BF)
        res_t[...] = d_r1
        add_vec(V_BO, d_proj[rows, :].astype(F32))

        @pl.when(start)
        def _():
            weights[2][1]()
            for i in range(5, 9):
                fetch[i].wait()

        d_h_t[...] = mm(d_proj[rows, :], wo[...], NT).astype(BF)

        def attend_back(c):
            cr = pl.ds(pl.multiple_of(c * CL, CL), CL)
            gr = pl.ds(pl.multiple_of(t * TM + c * CL, CL), CL)
            for p in range(PAIRS):
                ps = slice(p * PW, (p + 1) * PW)
                dh, qp, ks = d_h_t[cr, ps], q[gr, ps], apart(k[gr, ps])
                probs = p_all[t * (TM // CL) + c, p]
                d_w = mm(apart(v[gr, ps]), dh, NT)
                halves = []
                for h in range(2):
                    wh = probs[h * CL : (h + 1) * CL].astype(F32)
                    dwh = d_w[h * CL : (h + 1) * CL]
                    halves.append((wh * (dwh - jnp.sum(dwh * wh, axis=0, keepdims=True))).astype(BF))
                d_s = jnp.concatenate(halves, axis=0)
                q[gr, ps] = (mm(d_s, ks, TN) * inv).astype(BF)
                dk = mm(d_s, qp)
                k[gr, ps] = jnp.where(first_half, dk[0:CL], dk[CL:]).astype(BF)
                dv = mm(probs, dh)
                v[gr, ps] = jnp.where(first_half, dv[0:CL], dv[CL:]).astype(BF)

        loop(TM // CL, attend_back)
        add_vec(V_BQ, q[rows, :].astype(F32))
        add_vec(V_BV, v[rows, :].astype(F32))
        pl.when(start)(weights[3][1])
        d_x = (
            mm(q[rows, :], wqkv[0:D, :], NT)
            + mm(k[rows, :], wqkv[D : 2 * D, :], NT)
            + mm(v[rows, :], wqkv[2 * D :, :], NT)
        )
        ing_c[rows, :] = (res_t[...] + d_x.astype(BF).astype(F32)).astype(BF)
        for i in range(len(saved)):
            save(t, i).start()

    loop(ROWS // TM, tile)

    for j, back in enumerate((back_0, back_1, back_2, back_3)):
        back[...] = mm(seat_part(meta, j, cap), ing_c[...], TN).astype(BF)

    for chunk in range(72):
        row, lane = chunk // 6, chunk % 6 * 128
        if row < 8:
            part = gvec[row : row + 1, lane : lane + 128]
        else:
            lane += (row - 8) * D
            part = g_bu[:, lane : lane + 128]
        shares[chunk // 9, chunk % 9 : chunk % 9 + 1, :] = part

    def saved_all(t):
        for i in range(len(saved)):
            save(t, i).wait()

    loop(ROWS // TM, saved_all)


def backward(cap, positions, slots, vecs, meta, cots, saved):
    rows, wide, probs, full, thin = saved_shapes()
    dma = pltpu.SemaphoreType.DMA
    grads = (wide, rows, rows, rows, rows, rows)
    return pl.pallas_call(
        functools.partial(backward_kernel, cap),
        out_shape=(shape_of(BF, cap, D),) * SD
        + (shape_of(F32, 8, 16, 128),)
        + tuple(shape_of(kind, *shape) for shape, kind in grads),
        in_specs=[SMEM, ANY, VMEM, VMEM] + [ANY] * (SD + 9),
        out_specs=(VMEM,) * (SD + 1) + (ANY,) * len(grads),
        scratch_shapes=[
            pltpu.VMEM((3 * D, D), BF),
            pltpu.VMEM((D, D), BF),
            pltpu.VMEM((FF, D), BF),
            pltpu.VMEM((FF, D), BF),
            pltpu.VMEM((SD, cap, D), BF),
        ]
        + [pltpu.VMEM(*a) for a in (rows, rows, rows, probs, wide, full, full, thin, thin, rows, rows, rows)]
        + [
            pltpu.VMEM((TM, D), BF),
            pltpu.VMEM((TM, D), F32),
            pltpu.VMEM((8, D), F32),
            pltpu.VMEM((1, FF), F32),
            dma((4,)),
            dma((4,)),
            dma((9,)),
            dma((6,)),
        ],
        compiler_params=pltpu.CompilerParams(vmem_limit_bytes=VMEM_LIMIT),
        name="backward",
    )(positions, slots, vecs, meta, *cots, *saved)


WC = 8 * BLK


def weight_kernel(
    pos,
    x_h,
    heads_h,
    act_h,
    d_up_h,
    d_q_h,
    d_k_h,
    d_v_h,
    d_proj_h,
    hid_h,
    d_br_h,
    grads,
    x_c,
    heads,
    act,
    d_up,
    d_q,
    d_k,
    d_v,
    d_proj,
    hid,
    d_br,
    stage,
    i_sem,
    g_sem,
):
    refs = (
        (x_h, x_c),
        (d_q_h, d_q),
        (d_k_h, d_k),
        (d_v_h, d_v),
        (heads_h, heads),
        (d_proj_h, d_proj),
        (hid_h, hid),
        (d_up_h, d_up),
        (d_br_h, d_br),
        (act_h, act),
    )
    fetch = [pltpu.make_async_copy(src, dst, i_sem.at[i]) for i, (src, dst) in enumerate(refs)]
    for copy in fetch:
        copy.start()

    per = WC // BLK

    def g_copy(chunk, j, at):
        return pltpu.make_async_copy(
            stage.at[at, pl.ds(j * BLK, BLK)], grads.at[pos[chunk * per + j]], g_sem.at[at]
        )

    def put(chunk, left, right):
        at = lax.rem(chunk, 2)

        @pl.when(chunk >= 2)
        def _():
            for j in range(per):
                g_copy(chunk - 2, j, at).wait()

        stage[at] = mm(left, right, TN).astype(BF)
        for j in range(per):
            g_copy(chunk, j, at).start()

    first = 0
    for left, right, needs in (
        (x_c, d_q, (0, 1)),
        (x_c, d_k, (2,)),
        (x_c, d_v, (3,)),
        (heads, d_proj, (4, 5)),
        (d_up, hid, (6, 7)),
        (act, d_br, (8, 9)),
    ):
        for i in needs:
            fetch[i].wait()

        def body(j, left=left, right=right, first=first):
            put(first + j, left[:, pl.ds(pl.multiple_of(j * WC, WC), WC)], right[...])

        loop(left.shape[1] // WC, body)
        first += left.shape[1] // WC
    for chunk in (first - 2, first - 1):
        for j in range(per):
            g_copy(chunk, j, chunk % 2).wait()


def weight_grads_of(total_slots, positions, x_c, saved):
    r_v, w_v = pltpu.VMEM((ROWS, D), BF), pltpu.VMEM((ROWS, FF), BF)
    return pl.pallas_call(
        weight_kernel,
        out_shape=jax.ShapeDtypeStruct((total_slots, BLK, D), BF),
        in_specs=[SMEM] + [ANY] * 10,
        out_specs=ANY,
        scratch_shapes=[r_v, r_v, w_v, w_v]
        + [r_v] * 6
        + [
            pltpu.VMEM((2, WC, D), BF),
            pltpu.SemaphoreType.DMA((10,)),
            pltpu.SemaphoreType.DMA((2,)),
        ],
        compiler_params=pltpu.CompilerParams(vmem_limit_bytes=VMEM_LIMIT),
        cost_estimate=pl.CostEstimate(flops=2 * ROWS * WROWS * D, bytes_accessed=40 << 20, transcendentals=0),
        name="weight_grads",
    )(positions, x_c, *saved)


def local(
    tokens,
    cotangent,
    cluster_order,
    block_owner,
    master_slots,
    moment_one,
    moment_two,
    vector_master,
    vector_moment_one,
    vector_moment_two,
):
    tok_count = lax.axis_size("tok")
    tok_index = lax.axis_index("tok")
    slot_count = master_slots.shape[0]
    cap = tok_count // SD * (max(1, CPS // tok_count) * 3 * CL // (2 * SD))
    total_slots = tok_count * slot_count
    order = cluster_order.reshape(1, ROWS)

    block = jax.ShapeDtypeStruct((SD, cap, D), BF)
    meta_shape = jax.ShapeDtypeStruct((SD, META, D), BF)
    row_block = jax.ShapeDtypeStruct((ROWS, D), BF)
    four_planes = tok_count == 8 and lax.axis_size("rep") == 4
    if four_planes:
        slots_low, x_c, *cots, recv_meta, vecs, b_u, occupancy, positions = gather_all(
            cap, tokens, cotangent, order, master_slots, vector_master, block_owner
        )
        positions = positions.reshape(NBLK)
    else:
        positions = slot_positions(block_owner, slot_count)
        slots_low = lax.all_gather(master_slots.astype(BF), "tok", axis=0, tiled=True)
        vectors = lax.all_gather(vector_master.astype(BF), "tok", axis=0, tiled=True).astype(F32)
        vecs, b_u = vectors[: 8 * D].reshape(8, D), vectors[8 * D :].reshape(1, FF)
        cluster = tok_index // SD * CPS + cluster_order // CL
        target = cluster % tok_count
        chosen = target[None, :] == jnp.arange(tok_count, dtype=jnp.int32)[:, None]
        sent_counts = jnp.sum(chosen.astype(F32), axis=1)
        own_row = (jnp.arange(tok_count, dtype=jnp.int32) == tok_index).astype(F32)
        occupancy = lax.psum(own_row[:, None] * sent_counts[None, :], ("tok", "rep")).astype(jnp.int32)
        send_x, send_c, meta = pl.pallas_call(
            functools.partial(send_kernel, cap),
            out_shape=(block, block, meta_shape),
            in_specs=[VMEM] * 3,
            out_specs=(VMEM,) * 3,
            compiler_params=pltpu.CompilerParams(vmem_limit_bytes=VMEM_LIMIT),
            name="send_rows",
        )(tokens, cotangent, order)
        recv_x, recv_meta = (jnp.stack(swap_blocks(b)) for b in (send_x, meta))
        x_c = pl.pallas_call(
            functools.partial(seat_kernel, cap),
            out_shape=row_block,
            in_specs=[VMEM] * 2,
            out_specs=VMEM,
            compiler_params=pltpu.CompilerParams(vmem_limit_bytes=VMEM_LIMIT),
            name="seat_rows",
        )(recv_x, recv_meta)
        cots = [send_c[k] for k in range(SD)]

    cots = swap_blocks(cots)
    *out_blocks, heads, act, hid, q, k, v, p, slope, n1, n2, rs1, rs2 = forward(
        cap, positions, slots_low, vecs, b_u, x_c, recv_meta
    )
    out_blocks = swap_blocks(out_blocks)
    *ing_blocks, shares, d_up, d_q, d_k, d_v, d_proj, d_br = backward(
        cap, positions, slots_low, vecs, recv_meta, cots, (q, k, v, p, slope, n1, n2, rs1, rs2)
    )
    ing_blocks = swap_blocks(ing_blocks)
    grads = weight_grads_of(
        total_slots, positions, x_c, (heads, act, d_up, d_q, d_k, d_v, d_proj, hid, d_br)
    )
    if four_planes:
        total, vec_owned, output, input_grad, entropy = reduce_all(
            cap, grads, shares, order, out_blocks, ing_blocks, slot_count
        )
    else:
        total = lax.psum(lax.psum_scatter(grads, "tok", scatter_dimension=0, tiled=True), "rep")
        grad_vector = shares[:, 0:9].reshape(-1)
        vec_owned = lax.psum(lax.psum_scatter(grad_vector, "tok", scatter_dimension=0, tiled=True), "rep")
        output, input_grad, entropy = pl.pallas_call(
            functools.partial(return_kernel, cap),
            out_shape=(row_block, row_block, jax.ShapeDtypeStruct((1, ROWS), BF)),
            in_specs=[VMEM] * (2 * SD + 1),
            out_specs=(VMEM,) * 3,
            compiler_params=pltpu.CompilerParams(vmem_limit_bytes=VMEM_LIMIT),
            name="return_rows",
        )(order, *out_blocks, *ing_blocks)

    used = jnp.any(
        positions[None, :] == (tok_index * slot_count + jnp.arange(slot_count, dtype=I32))[:, None], axis=1
    )
    owned_grad = jnp.where(used[:, None, None], total.astype(F32), 0.0)
    first_new, second_new, master_new = adam_update(
        owned_grad, master_slots, moment_one, moment_two, rate_matrix
    )
    vec_first, vec_second, vec_new = adam_update(
        vec_owned, vector_master, vector_moment_one, vector_moment_two, rate_vector
    )
    return (
        output,
        input_grad,
        owned_grad,
        first_new,
        second_new,
        master_new,
        master_new.astype(BF),
        vec_owned,
        vec_first,
        vec_second,
        vec_new,
        vec_new.astype(BF),
        entropy.reshape(-1),
        occupancy,
    )


def solution(mesh):
    placed = (
        P(("rep", "tok"), None),
        P(("rep", "tok"), None),
        P(("rep", "tok")),
        P(),
        P("tok", None, None),
        P("tok", None, None),
        P("tok", None, None),
        P("tok"),
        P("tok"),
        P("tok"),
    )
    return jax.shard_map(
        local,
        mesh=mesh,
        in_specs=placed,
        out_specs=(
            P(("rep", "tok"), None),
            P(("rep", "tok"), None),
            P("tok", None, None),
            P("tok", None, None),
            P("tok", None, None),
            P("tok", None, None),
            P("tok", None, None),
            P("tok"),
            P("tok"),
            P("tok"),
            P("tok"),
            P("tok"),
            P(("rep", "tok")),
            P(),
        ),
        check_vma=False,
    )
```

```python
import functools
import math

import jax
import jax.numpy as jnp
from jax import lax
from jax.experimental import pallas as pl
from jax.experimental.pallas import tpu as pltpu
from jax.sharding import PartitionSpec as P

D = 768
HEADS = 12
HD = 64
FF = 3072
SD = 4
CL = 128
NBLK = 96
STEP = 10
CPS = 32
WROWS = 9216
BLK = 96
ROWS = 1024
PAIRS = HEADS // 2
PW = 2 * HD
TM = 512
META = 16
VMEM_LIMIT = 63 << 20
FC = 768

norm_epsilon = 1e-06
beta_first = 0.9
beta_second = 0.999
adam_epsilon = 1e-08
weight_decay = 0.01
rate_matrix = 0.02
rate_vector = 0.2

BF = jnp.bfloat16
F32 = jnp.float32
I32 = jnp.int32

VMEM = pl.BlockSpec(memory_space=pltpu.VMEM)
SMEM = pl.BlockSpec(memory_space=pltpu.SMEM)
ANY = pl.BlockSpec(memory_space=pl.ANY)

NN = (((1,), (0,)), ((), ()))
NT = (((1,), (1,)), ((), ()))
TN = (((0,), (0,)), ((), ()))


def mm(a, b, dims=NN):
    return lax.dot_general(a, b, dims, preferred_element_type=F32)


def slot_positions(block_owner, slot_count):
    owners = block_owner[:, 0]
    blocks = owners.shape[0]
    shared = owners[:, None] == owners[None, :]
    before = (
        jnp.arange(blocks, dtype=jnp.int32)[None, :] < jnp.arange(blocks, dtype=jnp.int32)[:, None]
    )
    earlier = jnp.sum((shared & before).astype(jnp.int32), axis=1)
    return owners * slot_count + earlier


def adam_update(grad_now, weight_old, first_old, second_old, rate_step):
    first_new = beta_first * first_old + (1.0 - beta_first) * grad_now
    second_new = beta_second * second_old + (1.0 - beta_second) * grad_now * grad_now
    first_hat = first_new / (1.0 - beta_first**STEP)
    second_hat = second_new / (1.0 - beta_second**STEP)
    weight_new = weight_old - rate_step * (
        first_hat / (jnp.sqrt(second_hat) + adam_epsilon) + weight_decay * weight_old
    )
    return (first_new, second_new, weight_new)


def route_slots(order, seat, cap):
    cluster = order // CL
    rel = lax.rem(cluster, SD) ^ seat
    place = (cluster // SD) * CL + lax.rem(order, CL) + 1
    chosen = lax.broadcasted_iota(I32, (8, ROWS), 0) == rel
    chosen_low = jnp.where(chosen, 1.0, 0.0).astype(BF)
    before = lax.broadcasted_iota(I32, (ROWS, ROWS), 0) < lax.broadcasted_iota(I32, (ROWS, ROWS), 1)
    before_low = jnp.where(before, 1.0, 0.0).astype(BF)
    running = mm(chosen_low, before_low)
    rank = jnp.sum(jnp.where(chosen, running, 0.0), axis=0, keepdims=True).astype(I32)
    return rel * cap + rank, place


def slot_matrix(slots, at, cap):
    rows = lax.broadcasted_iota(I32, (cap, ROWS), 0) + at * cap
    return jnp.where(rows == slots, 1.0, 0.0).astype(BF)


def send_kernel(cap, tokens, cotangent, order, send_x, send_c, meta):
    seat = lax.rem(lax.axis_index("tok"), SD)
    slots, place = route_slots(order[...], seat, cap)
    digits = jnp.concatenate([place // CL, lax.rem(place, CL)] + [place * 0] * 6, axis=0).astype(F32).astype(BF)
    for at in range(SD):
        picked = slot_matrix(slots, at, cap)
        send_x[at] = mm(picked, tokens[...]).astype(BF)
        send_c[at] = mm(picked, cotangent[...]).astype(BF)
        coded = mm(digits, picked, NT)
        line = jnp.concatenate([coded[0:1], coded[1:2]], axis=1)
        meta[at] = jnp.broadcast_to(line, (META, D)).astype(BF)


def remote(src, dst, send_sem, recv_sem, tok, rep):
    return pltpu.make_async_remote_copy(
        src_ref=src,
        dst_ref=dst,
        send_sem=send_sem,
        recv_sem=recv_sem,
        device_id={"tok": tok, "rep": rep},
        device_id_type=pl.DeviceIdType.MESH,
    )


def loop(n, body):
    def run(i, c):
        body(i)
        return c

    lax.fori_loop(0, n, run, 0)


class Place:
    def __init__(self):
        self.me = me = lax.axis_index("tok")
        self.z = z = lax.axis_index("rep")
        core, x, y = me % 2, (me // 2) % 2, me // 4
        self.twin = me + 1 - 2 * core
        self.xn = me + 2 - 4 * x
        self.yn = me + 4 - 8 * y
        self.dn = self.xn + 4 - 8 * y
        self.side = z % 2
        self.zp = z + 1 - 2 * self.side

    def twin_of(self, tok):
        return tok + 1 - 2 * (tok % 2)

    def greet(self, peers):
        barrier = pltpu.get_barrier_semaphore()
        for tok, rep in peers:
            pl.semaphore_signal(
                barrier, inc=1, device_id={"tok": tok, "rep": rep}, device_id_type=pl.DeviceIdType.MESH
            )
        return lambda: pl.semaphore_wait(barrier, len(peers))


def seat_matrix(meta, first, rows, cap):
    hi = jnp.concatenate([meta[k, 0:8, 0:cap] for k in range(SD)], axis=1).astype(F32)[0:1]
    lo = jnp.concatenate([meta[k, 0:8, cap : 2 * cap] for k in range(SD)], axis=1).astype(F32)[0:1]
    at = (hi * CL + lo).astype(I32)
    seats = lax.broadcasted_iota(I32, (rows, SD * cap), 0) + (first + 1)
    return jnp.where(seats == at, 1.0, 0.0).astype(BF)


def seat_part(meta, k, cap):
    hi = meta[k, 0:8, 0:cap].astype(F32)[0:1]
    lo = meta[k, 0:8, cap : 2 * cap].astype(F32)[0:1]
    at = (hi * CL + lo).astype(I32)
    seats = lax.broadcasted_iota(I32, (ROWS, cap), 0) + 1
    return jnp.where(seats == at, 1.0, 0.0).astype(BF)


def seat_rows(meta, blocks, cap, to):
    def body(t):
        r0 = pl.multiple_of(t * 256, 256)
        rows = blocks[...].reshape(SD * cap, D)
        to[pl.ds(r0, 256), :] = mm(seat_matrix(meta, r0, 256, cap), rows).astype(BF)

    loop(ROWS // 256, body)


def seat_kernel(cap, blocks, meta, to):
    seat_rows(meta, blocks, cap, to)


def gather_kernel(
    cap,
    count,
    tokens_h,
    cotangent_h,
    order,
    master_h,
    vector,
    owner_of,
    slots,
    x_c,
    cot_0,
    cot_1,
    cot_2,
    cot_3,
    recv_meta,
    vecs,
    b_u,
    occupancy,
    positions,
    tokens,
    cotangent,
    master,
    own,
    send_x,
    send_c,
    meta,
    recv_x,
    got_meta,
    slot_of,
    digits,
    mine,
    by_z,
    by_tok,
    x_s,
    x_r,
    y_s,
    y_r,
    d_s,
    d_r,
    zx_s,
    zx_r,
    zd_s,
    zd_r,
    zy_s,
    zy_r,
    p_s,
    p_r,
    row_s,
    row_r,
    z_s,
    z_r,
    t_s,
    t_r,
    local_s,
):
    at = Place()
    me, z, side = at.me, at.z, at.side
    n_tok, n_rep = 8, 4
    peers = [((me + d) % n_tok, z) for d in range(1, n_tok)] + [(me, (z + d) % n_rep) for d in range(1, n_rep)]
    fetch = [
        pltpu.make_async_copy(src, dst, local_s.at[i])
        for i, (src, dst) in enumerate(((master_h, master), (tokens_h, tokens), (cotangent_h, cotangent)))
    ]
    for copy in fetch:
        copy.start()
    wait_peers = at.greet(peers)
    fetch[0].wait()

    def cast(s):
        own[s] = master[s].astype(BF)

    loop(count, cast)
    wait_peers()

    half = count // 2

    def slot(owner, s):
        return slots.at[owner * count + s]

    def to_x(s):
        return remote(own.at[s], slot(me, s), x_s.at[s], x_r.at[s], at.xn, z)

    def to_y(s):
        return remote(own.at[s], slot(me, s), y_s.at[s], y_r.at[s], at.yn, z)

    def on_y(s):
        return remote(slot(at.xn, s), slot(at.xn, s), d_s.at[s], d_r.at[s], at.yn, z)

    def x_on_z(s):
        return remote(slot(at.xn, s), slot(at.xn, s), zx_s.at[s], zx_r.at[s], me, at.zp)

    def d_on_z(s):
        return remote(slot(at.dn, s), slot(at.dn, s), zd_s.at[s], zd_r.at[s], me, at.zp)

    def y_on_z(s):
        return remote(slot(at.yn, s), slot(at.yn, s), zy_s.at[s], zy_r.at[s], me, at.zp)

    few = count // 3
    most = count - few

    def straight(j):
        return few * side + j

    def shared(j):
        return most * side + j

    def lacking(j):
        return most * (1 - side) + j

    owners = (me, at.xn, at.yn, at.dn)

    def to_twin(q, s):
        src = own.at[s] if q == 0 else slot(owners[q], s)
        return remote(src, slot(owners[q], s), p_s.at[q, s], p_r.at[q, s], at.twin, z)

    def near(j):
        return (half + 1) * side + j

    def far(j):
        return (half + 1) * (1 - side) + j

    loop(half, lambda j: to_x(near(j)).start())
    to_x(half).start()
    loop(few, lambda j: to_y(shared(j)).start())
    loop(count, lambda s: to_twin(0, s).start())
    keep = pltpu.make_async_copy(own, slots.at[pl.ds(me * count, count)], local_s.at[3])
    keep.start()

    seat = me % SD
    seats = (me, at.twin, at.xn, at.twin_of(at.xn))
    rows_of = ((meta, got_meta), (send_x, recv_x))

    def row_copy(i, k):
        src, dst = rows_of[i]
        return remote(src.at[k], dst.at[k], row_s.at[i, k], row_r.at[i, k], seats[k], z)

    put_c = [
        pltpu.make_async_copy(send_c.at[k], to, local_s.at[4 + k])
        for k, to in enumerate((cot_0, cot_1, cot_2, cot_3))
    ]

    def route():
        fetch[1].wait()
        fetch[2].wait()
        slots_here, place = route_slots(order[...], seat, cap)
        slot_of[...] = slots_here
        digits[...] = (
            jnp.concatenate([place // CL, lax.rem(place, CL)] + [place * 0] * 6, axis=0).astype(F32).astype(BF)
        )

    def sort_tokens(k):
        picked = slot_matrix(slot_of[...], k, cap)
        send_x[k] = mm(picked, tokens[...]).astype(BF)
        coded = mm(digits[...], picked, NT)
        line = jnp.concatenate([coded[0:1], coded[1:2]], axis=1)
        meta[k] = jnp.broadcast_to(line, (META, D)).astype(BF)
        for i in range(2):
            if k:
                row_copy(i, k).start()
            else:
                src, dst = rows_of[i]
                dst[0] = src[0]

    def sort_cotangent(k):
        send_c[k] = mm(slot_matrix(slot_of[...], k, cap), cotangent[...]).astype(BF)
        put_c[k].start()

    def z_copy(d):
        return remote(by_z.at[0], by_z.at[d], z_s.at[d], z_r.at[d], me, (z + d) % n_rep)

    def t_copy(d):
        return remote(mine, by_tok.at[d], t_s.at[d], t_r.at[d], (me + d) % n_tok, z)

    def count_rows():
        residue = lax.rem(me // SD * CPS + order[...] // CL, n_tok)
        hit = lax.broadcasted_iota(I32, (128, ROWS), 0) == residue
        by_z[0] = mm(jnp.ones((8, ROWS), BF), jnp.where(hit, 1.0, 0.0).astype(BF), NT)
        for d in range(1, n_rep):
            z_copy(d).start()
        for i in range(9):
            mine[i : i + 1] = vector[i * 128 : (i + 1) * 128].reshape(1, 128).astype(BF).astype(F32)
        block_row = lax.broadcasted_iota(I32, (NBLK, NBLK), 0)
        block_col = lax.broadcasted_iota(I32, (NBLK, NBLK), 1)
        by_col = owner_of[...].astype(F32)
        by_row = lane_sum(jnp.where(block_row == block_col, by_col, 0.0))
        earlier = jnp.where((by_row == by_col) & (block_row < block_col), 1.0, 0.0)
        positions[...] = (by_col * count + jnp.sum(earlier, axis=0, keepdims=True)).astype(I32)

    def share_vectors():
        for d in range(1, n_rep):
            z_copy(d).wait()
        mine[16:24] = by_z[0] + by_z[1] + by_z[2] + by_z[3]
        for d in range(1, n_tok):
            t_copy(d).start()

    def lay_out_vectors():
        by_tok[0] = mine[...]
        for d in range(1, n_tok):
            t_copy(d).wait()
        for owner in range(n_tok):
            share = by_tok[(me + n_tok - owner) % n_tok]
            occupancy[owner : owner + 1, :] = share[16:17, 0:n_tok].astype(I32)
            for i in range(9):
                chunk = owner * 9 + i
                row, lane = chunk // 6, chunk % 6 * 128
                if row < 8:
                    vecs[row : row + 1, lane : lane + 128] = share[i : i + 1]
                else:
                    lane += (row - 8) * D
                    b_u[:, lane : lane + 128] = share[i : i + 1]

    def to_x_in(s):
        return remote(own.at[s], slot(at.xn, s), x_s.at[s], x_r.at[s], at.xn, z)

    def y_in(s):
        return remote(own.at[s], slot(at.yn, s), y_s.at[s], y_r.at[s], at.yn, z)

    def d_in(s):
        return remote(own.at[s], slot(at.dn, s), d_s.at[s], d_r.at[s], at.yn, z)

    def x_here(s):
        to_x_in(s).wait_recv()
        on_y(s).start()
        to_twin(1, s).start()

    def y_here(s):
        y_in(s).wait_recv()
        to_twin(2, s).start()

    def rest(j):
        return few + j

    between = (
        lambda: (route(), sort_tokens(2)),
        lambda: sort_tokens(3),
        lambda: sort_tokens(1),
        lambda: (sort_tokens(0), count_rows()),
        lambda: sort_cotangent(1),
        lambda: sort_cotangent(2),
    )
    for j in range(half):
        x_here(near(j))
        x_on_z(near(j)).start()
        if j < few:
            y_here(shared(j))
            y_on_z(shared(j)).start()
        if j < len(between):
            between[j]()
    x_here(half)
    loop(most - few, lambda j: to_y(rest(j)).start())
    share_vectors()
    sort_cotangent(3)
    sort_cotangent(0)

    def second(j):
        x_on_z(far(j)).wait_recv()
        to_twin(1, far(j)).start()
        d_in(near(j)).wait_recv()
        d_on_z(near(j)).start()
        to_twin(3, near(j)).start()

    loop(half, second)
    d_in(half).wait_recv()
    to_twin(3, half).start()
    lay_out_vectors()
    loop(most - few, lambda j: y_here(rest(j)))

    def lacking_here(j):
        y_on_z(lacking(j)).wait_recv()
        to_twin(2, lacking(j)).start()

    loop(few, lacking_here)
    for i in (0, 1):
        for k in (2, 3, 1):
            row_copy(i, k).wait_recv()
    recv_meta[...] = got_meta[...]
    seat_rows(got_meta, recv_x, cap, x_c)

    def third(j):
        d_on_z(far(j)).wait_recv()
        to_twin(3, far(j)).start()

    loop(half, third)

    for i in range(2):
        for k in (2, 3, 1):
            row_copy(i, k).wait_send()
    for copy in put_c:
        copy.wait()
    keep.wait()

    def sent_half(j):
        to_x(near(j)).wait_send()
        on_y(near(j)).wait_send()
        x_on_z(near(j)).wait_send()
        d_on_z(near(j)).wait_send()

    loop(half, sent_half)
    to_x(half).wait_send()
    on_y(half).wait_send()

    def sent(s):
        for q in range(4):
            to_twin(q, s).wait()

    loop(count, sent)
    loop(most, lambda j: to_y(straight(j)).wait_send())
    loop(few, lambda j: y_on_z(shared(j)).wait_send())


def gather_all(cap, tokens, cotangent, order, master, vector, block_owner):
    count = master.shape[0]
    rows = jax.ShapeDtypeStruct((ROWS, D), BF)
    part = jax.ShapeDtypeStruct((cap, D), BF)
    dma = pltpu.SemaphoreType.DMA
    block = pltpu.VMEM((SD, cap, D), BF)
    meta = pltpu.VMEM((SD, META, D), BF)
    return pl.pallas_call(
        functools.partial(gather_kernel, cap, count),
        out_shape=(
            jax.ShapeDtypeStruct((8 * count, BLK, D), BF),
            rows,
            part,
            part,
            part,
            part,
            jax.ShapeDtypeStruct((SD, META, D), BF),
            jax.ShapeDtypeStruct((8, D), F32),
            jax.ShapeDtypeStruct((1, FF), F32),
            jax.ShapeDtypeStruct((8, 8), I32),
            jax.ShapeDtypeStruct((1, NBLK), I32),
        ),
        in_specs=[ANY, ANY, VMEM, ANY, VMEM, VMEM],
        out_specs=(ANY, VMEM) + (ANY,) * SD + (VMEM,) * 5,
        scratch_shapes=[
            pltpu.VMEM((ROWS, D), BF),
            pltpu.VMEM((ROWS, D), BF),
            pltpu.VMEM((count, BLK, D), F32),
            pltpu.VMEM((count, BLK, D), BF),
            block,
            block,
            meta,
            block,
            meta,
            pltpu.VMEM((1, ROWS), I32),
            pltpu.VMEM((8, ROWS), BF),
            pltpu.VMEM((24, 128), F32),
            pltpu.VMEM((4, 8, 128), F32),
            pltpu.VMEM((8, 24, 128), F32),
        ]
        + [dma((count,))] * 12
        + [dma((4, count))] * 2
        + [dma((2, SD))] * 2
        + [dma((4,))] * 2
        + [dma((8,))] * 2
        + [dma((8,))],
        compiler_params=pltpu.CompilerParams(collective_id=0, has_side_effects=True, vmem_limit_bytes=VMEM_LIMIT),
        cost_estimate=pl.CostEstimate(flops=8 * ROWS * ROWS * D, bytes_accessed=64 << 20, transcendentals=0),
        name="gather",
    )(tokens, cotangent, order, master, vector, block_owner.reshape(1, NBLK))


def return_kernel(cap, order, *refs):
    outs, ings, (out, ing, entropy) = refs[:SD], refs[SD : 2 * SD], refs[2 * SD :]
    seat = lax.rem(lax.axis_index("tok"), SD)
    slots, _ = route_slots(order[...], seat, cap)
    picked = jnp.concatenate([slot_matrix(slots, at, cap) for at in range(SD)], axis=0)
    for to, blocks in ((out, outs), (ing, ings)):
        rows = jnp.concatenate([block[0:cap, :] for block in blocks], axis=0)
        to[...] = mm(picked, rows, TN).astype(BF)
    line = jnp.concatenate([block[cap : cap + 8, 0:cap] for block in outs], axis=1)
    entropy[...] = mm(line, picked)[0:1].astype(BF)


def swap_blocks(blocks):
    n = lax.axis_size("tok")
    parts = [blocks[0]]
    for k in range(1, SD):
        parts.append(lax.ppermute(blocks[k], "tok", [(i, i ^ k) for i in range(n)]))
    return parts


def reduce_kernel(
    cap,
    count,
    split,
    grads,
    vec,
    order,
    out_0,
    out_1,
    out_2,
    out_3,
    ing_0,
    ing_1,
    ing_2,
    ing_3,
    total,
    vec_out,
    output,
    input_grad,
    entropy,
    out_v,
    ing_v,
    slot_of,
    a,
    tw,
    rd,
    rx,
    ry,
    o,
    rz1,
    pz,
    rz2,
    fz,
    vt,
    va,
    vb,
    vc,
    a_l,
    keep_l,
    p_s,
    p_r,
    d_s,
    d_r,
    x_s,
    x_r,
    y_s,
    y_r,
    z1_s,
    z1_r,
    z2_s,
    z2_r,
    z3_s,
    z3_r,
    t_s,
    t_r,
    v_s,
    v_r,
    row_l,
):
    at = Place()
    me, z = at.me, at.z
    n_tok, n_rep = 8, 4
    peers = [((me + d) % n_tok, z) for d in range(1, n_tok)] + [(me, (z + d) % n_rep) for d in range(1, n_rep)]
    wait_peers = at.greet(peers)
    owners = (me, at.xn, at.yn, at.dn)

    def load(q):
        return pltpu.make_async_copy(grads.at[pl.ds(owners[q] * count, count)], a.at[q], a_l.at[q])

    for q in (3, 1, 2, 0):
        load(q).start()
    rows_in = [
        pltpu.make_async_copy(src, to.at[k], row_l.at[i, k])
        for i, (blocks, to) in enumerate((((out_0, out_1, out_2, out_3), out_v), ((ing_0, ing_1, ing_2, ing_3), ing_v)))
        for k, src in enumerate(blocks)
    ]
    for copy in rows_in:
        copy.start()
    wait_peers()

    def to_twin(q, s):
        src = grads.at[at.twin_of(owners[q]) * count + s]
        return remote(src, tw.at[q, s], p_s.at[q, s], p_r.at[q, s], at.twin, z)

    def d_y(s):
        return remote(a.at[3, s], rd.at[s], d_s.at[s], d_r.at[s], at.yn, z)

    def d_x(s):
        return remote(a.at[3, s], rd.at[s], d_s.at[s], d_r.at[s], at.xn, z)

    def to_x(s):
        return remote(a.at[1, s], rx.at[s], x_s.at[s], x_r.at[s], at.xn, z)

    def to_y(s):
        return remote(a.at[2, s], ry.at[s], y_s.at[s], y_r.at[s], at.yn, z)

    def z_in(s):
        return remote(o.at[s], rz1.at[s], z1_s.at[s], z1_r.at[s], me, at.zp)

    def z_swap(s):
        return remote(pz.at[s], rz2.at[s], z2_s.at[s], z2_r.at[s], me, n_rep - 1 - z)

    def z_out(s):
        return remote(fz.at[s], fz.at[s], z3_s.at[s], z3_r.at[s], me, at.zp)

    def keep(s):
        return pltpu.make_async_copy(fz.at[s], total.at[s], keep_l.at[s])

    def f32(ref, *index):
        return ref[index].astype(F32)

    def twin_round(i):
        for s in (i, split + i):
            to_twin(3, s).start()
        to_twin(1, i).start()
        to_twin(2, split + i).start()
        to_twin(2, i).start()
        to_twin(1, split + i).start()
        for s in (i, split + i):
            to_twin(0, s).start()

    loop(split, twin_round)
    for q in (3, 2, 1, 0):
        to_twin(q, count - 1).start()

    def v_tok(d):
        return remote(vec.at[(me + d) % n_tok], vt.at[d], t_s.at[d], t_r.at[d], (me + d) % n_tok, z)

    def v_rep(i, src):
        return remote(src, vb.at[i], v_s.at[i], v_r.at[i], me, at.zp if i == 0 else (z + 2) % n_rep)

    for d in range(1, n_tok):
        v_tok(d).start()

    slots_here, _ = route_slots(order[...], me % SD, cap)
    slot_of[...] = slots_here

    def join(q, s):
        to_twin(q, s).wait_recv()
        return f32(a, q, s) + f32(tw, q, s)

    def first(s, send):
        a[3, s] = join(3, s).astype(BF)
        send(s).start()

    def plain(q, s, send):
        a[q, s] = join(q, s).astype(BF)
        send(s).start()

    def joined(q, s, arrived, send):
        arrived(s).wait_recv()
        a[q, s] = (join(q, s) + f32(rd, s)).astype(BF)
        send(s).start()

    inner = (z == 1) | (z == 2)
    outer = (z == 0) | (z == 3)

    def own(s):
        to_x(s).wait_recv()
        to_y(s).wait_recv()
        o[s] = (join(0, s) + f32(rx, s) + f32(ry, s)).astype(BF)
        pl.when(outer)(lambda: z_in(s).start())

    def middle(s):
        @pl.when(inner)
        def _():
            z_in(s).wait_recv()
            pz[s] = (f32(o, s) + f32(rz1, s)).astype(BF)
            z_swap(s).start()

    def last(s):
        @pl.when(inner)
        def _():
            z_swap(s).wait_recv()
            fz[s] = (f32(pz, s) + f32(rz2, s)).astype(BF)
            z_out(s).start()
            keep(s).start()

    def taken(s):
        @pl.when(outer)
        def _():
            z_out(s).wait_recv()
            keep(s).start()

    def pick_rows(i):
        ts = pl.ds(pl.multiple_of(lax.rem(i, 4) * 256, 256), 256)
        hit = lax.broadcasted_iota(I32, (SD * cap, 256), 0) == slot_of[:, ts]
        picked = jnp.where(hit, 1.0, 0.0).astype(BF)

        @pl.when(i < 4)
        def _():
            rows = jnp.concatenate([out_v[k, 0:cap, :] for k in range(SD)], axis=0)
            output[ts, :] = mm(picked, rows, TN).astype(BF)
            line = jnp.concatenate([out_v[k, cap : cap + 8, 0:cap] for k in range(SD)], axis=1)
            entropy[:, ts] = mm(line, picked)[0:1].astype(BF)

        @pl.when(i >= 4)
        def _():
            rows = jnp.concatenate([ing_v[k] for k in range(SD)], axis=0)
            input_grad[ts, :] = mm(picked, rows, TN).astype(BF)

    for q in (3, 1, 2, 0):
        load(q).wait()
    for copy in rows_in:
        copy.wait()

    def steps(i, lag, more):
        r = i - lag
        by_x = (r % 2 == 0) & (r < 2 * split)
        live = (r >= 0) & (r < count)
        pl.when(live & by_x)(lambda: more(r // 2, True))
        pl.when(live & jnp.logical_not(by_x))(lambda: more(split + r // 2, False))

    def round_of(i):
        steps(i, 0, lambda s, by_x: first(s, d_x if by_x else d_y))
        steps(i, 0, lambda s, by_x: plain(1, s, to_x) if by_x else plain(2, s, to_y))
        steps(i, 2, lambda s, by_x: joined(2, s, d_x, to_y) if by_x else joined(1, s, d_y, to_x))
        steps(i, 4, lambda s, _: own(s))
        steps(i, 6, lambda s, _: middle(s))
        steps(i, 8, lambda s, _: last(s))
        steps(i, 10, lambda s, _: taken(s))
        pl.when((i >= 3) & (i < 11))(lambda: pick_rows(i - 3))

    loop(3, round_of)

    v_sum = vec[me]
    for d in range(1, n_tok):
        v_tok(d).wait()
        v_sum = v_sum + vt[d]
    va[...] = v_sum
    v_rep(0, va).start()

    loop(3, lambda i: round_of(3 + i))
    v_rep(0, va).wait()
    vc[...] = va[...] + vb[0]
    v_rep(1, vc).start()
    loop(count + 4, lambda i: round_of(6 + i))
    v_rep(1, vc).wait()
    vec_out[...] = vc[...] + vb[1]

    def sent(s):
        for q in range(4):
            to_twin(q, s).wait_send()
        d_y(s).wait_send()
        to_x(s).wait_send()
        to_y(s).wait_send()
        keep(s).wait()

    loop(count, sent)

    @pl.when(outer)
    def _():
        loop(count, lambda s: z_in(s).wait_send())

    @pl.when(inner)
    def _():
        def back(s):
            z_swap(s).wait_send()
            z_out(s).wait_send()

        loop(count, back)


def reduce_all(cap, grads, shares, order, outs, ings, count):
    dma = pltpu.SemaphoreType.DMA
    part = pltpu.VMEM((count, BLK, D), BF)
    whole = pltpu.VMEM((4, count, BLK, D), BF)
    line = pltpu.VMEM((16, 128), F32)
    rows = jax.ShapeDtypeStruct((ROWS, D), BF)
    total, vec, output, input_grad, entropy = pl.pallas_call(
        functools.partial(reduce_kernel, cap, count, count // 2),
        out_shape=(
            jax.ShapeDtypeStruct((count, BLK, D), BF),
            jax.ShapeDtypeStruct((16, 128), F32),
            rows,
            rows,
            jax.ShapeDtypeStruct((1, ROWS), BF),
        ),
        in_specs=[ANY, VMEM, VMEM] + [ANY] * (2 * SD),
        out_specs=(ANY,) + (VMEM,) * 4,
        scratch_shapes=[
            pltpu.VMEM((SD, cap + META, D), BF),
            pltpu.VMEM((SD, cap, D), BF),
            pltpu.VMEM((1, ROWS), I32),
            whole,
            whole,
        ]
        + [part] * 8
        + [pltpu.VMEM((8, 16, 128), F32), line, pltpu.VMEM((2, 16, 128), F32), line]
        + [dma((4,)), dma((count,))]
        + [dma((4, count))] * 2
        + [dma((count,))] * 12
        + [dma((8,))] * 2
        + [dma((2,))] * 2
        + [dma((2, SD))],
        compiler_params=pltpu.CompilerParams(collective_id=1, has_side_effects=True, vmem_limit_bytes=VMEM_LIMIT),
        cost_estimate=pl.CostEstimate(flops=4 * ROWS * ROWS * D, bytes_accessed=64 << 20, transcendentals=0),
        name="reduce",
    )(grads, shares, order, *outs, *ings)
    return total, vec[0:9].reshape(-1), output, input_grad, entropy


V_BQ, V_BV, V_BO, V_BD, V_G1, V_C1, V_G2, V_C2 = range(8)


def inverse(x):
    r = pl.reciprocal(x, approx=True)
    return r * (2.0 - x * r)


def erf_parts(v):
    t = inverse(1.0 + (0.3275911 / math.sqrt(2.0)) * jnp.abs(v))
    e = jnp.exp2((v * v) * (-0.5 / math.log(2.0)))
    poly = 0.5 * 1.061405429
    for c in (-1.453152027, 1.421413741, -0.284496736, 0.254829592):
        poly = poly * t + 0.5 * c
    tail = poly * (t * e)
    return jnp.where(v >= 0.0, 1.0 - tail, tail), e


def lane_sum(x):
    return jnp.sum(x, axis=1, keepdims=True)


def gelu_parts(v):
    phi, e = erf_parts(v)
    return v * phi, phi + v * (e * (1.0 / math.sqrt(2.0 * math.pi)))


def weight_copies(pos, slots, w, sem, first):
    def copy(b):
        return pltpu.make_async_copy(slots.at[pos[first + b]], w.at[pl.ds(b * BLK, BLK)], sem)

    n = w.shape[0] // BLK
    return (lambda: loop(n, lambda b: copy(b).start())), (lambda: loop(n, lambda b: copy(b).wait()))


def halves_of_heads():
    lane = lax.broadcasted_iota(I32, (1, PW), 1)
    m0 = jnp.where(lane < HD, 1.0, 0.0).astype(BF)
    m1 = jnp.where(lane < HD, 0.0, 1.0).astype(BF)
    return lambda pair: jnp.concatenate([pair * m0, pair * m1], axis=0)


def tile_rows(t):
    return pl.ds(pl.multiple_of(t * TM, TM), TM)


def forward_kernel(
    cap,
    pos,
    slots,
    vecs,
    b_u,
    x_h,
    meta,
    back_0,
    back_1,
    back_2,
    back_3,
    heads_h,
    act_h,
    hid_h,
    q_h,
    k_h,
    v_h,
    p_h,
    slope_h,
    n1_h,
    n2_h,
    rs1_h,
    rs2_h,
    wqkv,
    wo,
    wu,
    wd,
    x_c,
    heads,
    act,
    hid,
    q,
    k,
    v,
    p_all,
    slope,
    n1,
    n2,
    rs1,
    rs2,
    out_c,
    ent,
    hid_t,
    w_sem,
    x_sem,
    o_sem,
):
    inv = 1.0 / math.sqrt(HD)
    get_x = pltpu.make_async_copy(x_h, x_c, x_sem)
    get_x.start()
    weights = [
        weight_copies(pos, slots, w, w_sem.at[i], first)
        for i, (w, first) in enumerate(((wqkv, 0), (wo, 24), (wu, 32), (wd, 64)))
    ]
    for start, _ in weights:
        start()
    get_x.wait()
    apart = halves_of_heads()

    def vec(i):
        return vecs[i : i + 1, :]

    saved = (
        (heads, heads_h),
        (act, act_h),
        (hid, hid_h),
        (q, q_h),
        (k, k_h),
        (v, v_h),
        (slope, slope_h),
        (n1, n1_h),
        (n2, n2_h),
        (rs1, rs1_h),
        (rs2, rs2_h),
    )

    def save(t, i):
        src, dst = saved[i]
        return pltpu.make_async_copy(src.at[tile_rows(t)], dst.at[tile_rows(t)], o_sem.at[i])

    def save_p(t):
        n = TM // CL
        cs = pl.ds(t * n, n)
        return pltpu.make_async_copy(p_all.at[cs], p_h.at[cs], o_sem.at[len(saved)])

    def normal(r, n, rs, rows):
        c = r - lane_sum(r) * (1.0 / D)
        scale = lax.rsqrt(lane_sum(c * c) * (1.0 / D) + norm_epsilon)
        rs[rows, :] = jnp.broadcast_to(scale, (TM, 128))
        n[rows, :] = c * scale

    def tile(t):
        rows = tile_rows(t)
        first = t == 0
        pl.when(first)(weights[0][1])
        x = x_c[rows, :]
        q[rows, :] = ((mm(x, wqkv[0:D, :]) + vec(V_BQ)).astype(BF).astype(F32) * inv).astype(BF)
        k[rows, :] = mm(x, wqkv[D : 2 * D, :]).astype(BF)
        v[rows, :] = (mm(x, wqkv[2 * D :, :]) + vec(V_BV)).astype(BF)

        def attend(c):
            gr = pl.ds(pl.multiple_of(t * TM + c * CL, CL), CL)
            total = jnp.zeros((1, CL), F32)
            for p in range(PAIRS):
                ps = slice(p * PW, (p + 1) * PW)
                scores = mm(apart(k[gr, ps]), q[gr, ps], NT)
                halves = []
                for h in range(2):
                    sh = scores[h * CL : (h + 1) * CL]
                    sh = sh - jnp.max(sh, axis=0, keepdims=True)
                    e = jnp.exp(sh)
                    tot = jnp.sum(e, axis=0, keepdims=True)
                    r = 1.0 / tot
                    total += jnp.log(tot) - jnp.sum(e * sh, axis=0, keepdims=True) * r
                    halves.append((e * r).astype(BF))
                probs = jnp.concatenate(halves, axis=0)
                p_all[t * (TM // CL) + c, p] = probs
                heads[gr, ps] = mm(probs, apart(v[gr, ps]), TN).astype(BF)
            ent[:, gr] = jnp.broadcast_to(total * (1.0 / HEADS), (8, CL))

        loop(TM // CL, attend)
        for i in (0, 3, 4, 5):
            save(t, i).start()
        save_p(t).start()
        pl.when(first)(weights[1][1])
        normal(x_c[rows, :].astype(F32) + mm(heads[rows, :], wo[...]) + vec(V_BO), n1, rs1, rows)
        hidden = n1[rows, :] * vec(V_G1) + vec(V_C1)
        hid[rows, :] = hidden.astype(BF)
        hid_t[...] = hidden
        pl.when(first)(weights[2][1])

        def widen(f):
            fs = pl.ds(pl.multiple_of(f * FC, FC), FC)
            g, g_slope = gelu_parts(mm(hid[rows, :], wu[fs, :], NT) + b_u[:, fs])
            act[rows, fs] = g.astype(BF)
            slope[rows, fs] = g_slope.astype(BF)

        loop(FF // FC, widen)
        for i in (1, 2, 6, 7, 9):
            save(t, i).start()
        pl.when(first)(weights[3][1])
        normal(hid_t[...] + mm(act[rows, :], wd[...]) + vec(V_BD), n2, rs2, rows)
        out_c[rows, :] = (n2[rows, :] * vec(V_G2) + vec(V_C2)).astype(BF)
        for i in (8, 10):
            save(t, i).start()

    loop(ROWS // TM, tile)

    for j, back in enumerate((back_0, back_1, back_2, back_3)):
        own = seat_part(meta, j, cap)
        back[0:cap, :] = mm(own, out_c[...], TN).astype(BF)
        line = mm(ent[...].astype(BF), own)
        back[cap:, :] = jnp.concatenate([line, line], axis=1)[0:1].astype(BF) * jnp.ones((META, 1), BF)

    def saved_all(t):
        for i in range(len(saved)):
            save(t, i).wait()
        save_p(t).wait()

    loop(ROWS // TM, saved_all)


def shape_of(kind, *shape):
    return jax.ShapeDtypeStruct(shape, kind)


def saved_shapes():
    rows, wide = ((ROWS, D), BF), ((ROWS, FF), BF)
    probs = ((ROWS // CL, PAIRS, 2 * CL, CL), BF)
    full, thin = ((ROWS, D), F32), ((ROWS, 128), F32)
    return rows, wide, probs, full, thin


def forward(cap, positions, slots, vecs, b_u, x_c, meta):
    rows, wide, probs, full, thin = saved_shapes()
    kept = (rows, wide, rows, rows, rows, rows, probs, wide, full, full, thin, thin)
    dma = pltpu.SemaphoreType.DMA
    return pl.pallas_call(
        functools.partial(forward_kernel, cap),
        out_shape=(shape_of(BF, cap + META, D),) * SD + tuple(shape_of(kind, *shape) for shape, kind in kept),
        in_specs=[SMEM, ANY, VMEM, VMEM, ANY, VMEM],
        out_specs=(VMEM,) * SD + (ANY,) * len(kept),
        scratch_shapes=[
            pltpu.VMEM((3 * D, D), BF),
            pltpu.VMEM((D, D), BF),
            pltpu.VMEM((FF, D), BF),
            pltpu.VMEM((FF, D), BF),
            pltpu.VMEM(*rows),
        ]
        + [pltpu.VMEM(*a) for a in kept]
        + [
            pltpu.VMEM(*rows),
            pltpu.VMEM((8, ROWS), F32),
            pltpu.VMEM((TM, D), F32),
            dma((4,)),
            dma,
            dma((12,)),
        ],
        compiler_params=pltpu.CompilerParams(vmem_limit_bytes=VMEM_LIMIT),
        cost_estimate=pl.CostEstimate(flops=2 * ROWS * WROWS * D, bytes_accessed=64 << 20, transcendentals=0),
        name="forward",
    )(positions, slots, vecs, b_u, x_c, meta)


def backward_kernel(
    cap,
    pos,
    slots,
    vecs,
    meta,
    cot_0,
    cot_1,
    cot_2,
    cot_3,
    q_h,
    k_h,
    v_h,
    p_h,
    slope_h,
    n1_h,
    n2_h,
    rs1_h,
    rs2_h,
    back_0,
    back_1,
    back_2,
    back_3,
    shares,
    d_up_h,
    d_q_h,
    d_k_h,
    d_v_h,
    d_proj_h,
    d_br_h,
    wqkv,
    wo,
    wu,
    wd,
    blocks,
    q,
    k,
    v,
    p_all,
    d_up,
    n1,
    n2,
    rs1,
    rs2,
    d_proj,
    d_br,
    ing_c,
    d_h_t,
    res_t,
    gvec,
    g_bu,
    w_sem,
    c_sem,
    i_sem,
    o_sem,
):
    inv = 1.0 / math.sqrt(HD)
    get_c = [
        pltpu.make_async_copy(cot, blocks.at[j], c_sem.at[j]) for j, cot in enumerate((cot_0, cot_1, cot_2, cot_3))
    ]
    for copy in get_c:
        copy.start()
    fetch = [
        pltpu.make_async_copy(src, dst, i_sem.at[i])
        for i, (src, dst) in enumerate(
            (
                (n2_h, n2),
                (rs2_h, rs2),
                (slope_h, d_up),
                (n1_h, n1),
                (rs1_h, rs1),
                (v_h, v),
                (p_h, p_all),
                (k_h, k),
                (q_h, q),
            )
        )
    ]
    weights = [
        weight_copies(pos, slots, w, w_sem.at[i], first)
        for i, (w, first) in enumerate(((wd, 64), (wu, 32), (wo, 24), (wqkv, 0)))
    ]
    fetch[0].start()
    fetch[1].start()
    weights[0][0]()
    fetch[2].start()
    weights[1][0]()
    fetch[3].start()
    fetch[4].start()
    weights[2][0]()
    for i in range(5, 9):
        fetch[i].start()
    weights[3][0]()
    gvec[...] = jnp.zeros_like(gvec)
    g_bu[...] = jnp.zeros_like(g_bu)
    shares[...] = jnp.zeros_like(shares)
    for copy in get_c:
        copy.wait()
    seat_rows(meta, blocks, cap, d_br)
    apart = halves_of_heads()
    first_half = lax.broadcasted_iota(I32, (CL, PW), 1) < HD

    def vec(i):
        return vecs[i : i + 1, :]

    def add_vec(i, value):
        gvec[i : i + 1, :] += jnp.sum(value, axis=0, keepdims=True)

    saved = ((d_up, d_up_h), (q, d_q_h), (k, d_k_h), (v, d_v_h), (d_proj, d_proj_h), (d_br, d_br_h))

    def save(t, i):
        src, dst = saved[i]
        return pltpu.make_async_copy(src.at[tile_rows(t)], dst.at[tile_rows(t)], o_sem.at[i])

    def norm_back(e, n, rs, gain, shift):
        add_vec(gain, e * n)
        add_vec(shift, e)
        eg = e * vec(gain)
        return rs * (eg - lane_sum(eg) * (1.0 / D) - n * (lane_sum(eg * n) * (1.0 / D)))

    def tile(t):
        rows = tile_rows(t)
        start = t == 0

        @pl.when(start)
        def _():
            fetch[0].wait()
            fetch[1].wait()

        d_r2 = norm_back(d_br[rows, :].astype(F32), n2[rows, :], rs2[rows, 0:1], V_G2, V_C2)
        d_br[rows, :] = d_r2.astype(BF)
        add_vec(V_BD, d_br[rows, :].astype(F32))
        res_t[...] = d_r2

        @pl.when(start)
        def _():
            weights[0][1]()
            fetch[2].wait()

        def widen_back(f):
            fs = pl.ds(pl.multiple_of(f * FC, FC), FC)
            du = (mm(d_br[rows, :], wd[fs, :], NT) * d_up[rows, fs].astype(F32)).astype(BF)
            d_up[rows, fs] = du
            g_bu[:, fs] += jnp.sum(du.astype(F32), axis=0, keepdims=True)

        loop(FF // FC, widen_back)
        for i in (0, 5):
            save(t, i).start()

        @pl.when(start)
        def _():
            weights[1][1]()
            fetch[3].wait()
            fetch[4].wait()

        d_h = res_t[...] + mm(d_up[rows, :], wu[...])
        d_r1 = norm_back(d_h, n1[rows, :], rs1[rows, 0:1], V_G1, V_C1)
        d_proj[rows, :] = d_r1.astype(BF)
        res_t[...] = d_r1
        add_vec(V_BO, d_proj[rows, :].astype(F32))
        save(t, 4).start()

        @pl.when(start)
        def _():
            weights[2][1]()
            for i in range(5, 9):
                fetch[i].wait()

        d_h_t[...] = mm(d_proj[rows, :], wo[...], NT).astype(BF)

        def attend_back(c):
            cr = pl.ds(pl.multiple_of(c * CL, CL), CL)
            gr = pl.ds(pl.multiple_of(t * TM + c * CL, CL), CL)
            for p in range(PAIRS):
                ps = slice(p * PW, (p + 1) * PW)
                dh, qp, ks = d_h_t[cr, ps], q[gr, ps], apart(k[gr, ps])
                probs = p_all[t * (TM // CL) + c, p]
                d_w = mm(apart(v[gr, ps]), dh, NT)
                halves = []
                for h in range(2):
                    wh = probs[h * CL : (h + 1) * CL].astype(F32)
                    dwh = d_w[h * CL : (h + 1) * CL]
                    halves.append((wh * (dwh - jnp.sum(dwh * wh, axis=0, keepdims=True))).astype(BF))
                d_s = jnp.concatenate(halves, axis=0)
                q[gr, ps] = (mm(d_s, ks, TN) * inv).astype(BF)
                dk = mm(d_s, qp)
                k[gr, ps] = jnp.where(first_half, dk[0:CL], dk[CL:]).astype(BF)
                dv = mm(probs, dh)
                v[gr, ps] = jnp.where(first_half, dv[0:CL], dv[CL:]).astype(BF)

        loop(TM // CL, attend_back)
        for i in (1, 2, 3):
            save(t, i).start()
        add_vec(V_BQ, q[rows, :].astype(F32))
        add_vec(V_BV, v[rows, :].astype(F32))
        pl.when(start)(weights[3][1])
        d_x = (
            mm(q[rows, :], wqkv[0:D, :], NT)
            + mm(k[rows, :], wqkv[D : 2 * D, :], NT)
            + mm(v[rows, :], wqkv[2 * D :, :], NT)
        )
        ing_c[rows, :] = (res_t[...] + d_x.astype(BF).astype(F32)).astype(BF)

    loop(ROWS // TM, tile)

    for j, back in enumerate((back_0, back_1, back_2, back_3)):
        back[...] = mm(seat_part(meta, j, cap), ing_c[...], TN).astype(BF)

    for chunk in range(72):
        row, lane = chunk // 6, chunk % 6 * 128
        if row < 8:
            part = gvec[row : row + 1, lane : lane + 128]
        else:
            lane += (row - 8) * D
            part = g_bu[:, lane : lane + 128]
        shares[chunk // 9, chunk % 9 : chunk % 9 + 1, :] = part

    def saved_all(t):
        for i in range(len(saved)):
            save(t, i).wait()

    loop(ROWS // TM, saved_all)


def backward(cap, positions, slots, vecs, meta, cots, saved):
    rows, wide, probs, full, thin = saved_shapes()
    dma = pltpu.SemaphoreType.DMA
    grads = (wide, rows, rows, rows, rows, rows)
    return pl.pallas_call(
        functools.partial(backward_kernel, cap),
        out_shape=(shape_of(BF, cap, D),) * SD
        + (shape_of(F32, 8, 16, 128),)
        + tuple(shape_of(kind, *shape) for shape, kind in grads),
        in_specs=[SMEM, ANY, VMEM, VMEM] + [ANY] * (SD + 9),
        out_specs=(VMEM,) * (SD + 1) + (ANY,) * len(grads),
        scratch_shapes=[
            pltpu.VMEM((3 * D, D), BF),
            pltpu.VMEM((D, D), BF),
            pltpu.VMEM((FF, D), BF),
            pltpu.VMEM((FF, D), BF),
            pltpu.VMEM((SD, cap, D), BF),
        ]
        + [pltpu.VMEM(*a) for a in (rows, rows, rows, probs, wide, full, full, thin, thin, rows, rows, rows)]
        + [
            pltpu.VMEM((TM, D), BF),
            pltpu.VMEM((TM, D), F32),
            pltpu.VMEM((8, D), F32),
            pltpu.VMEM((1, FF), F32),
            dma((4,)),
            dma((4,)),
            dma((9,)),
            dma((6,)),
        ],
        compiler_params=pltpu.CompilerParams(vmem_limit_bytes=VMEM_LIMIT),
        cost_estimate=pl.CostEstimate(flops=2 * ROWS * WROWS * D, bytes_accessed=64 << 20, transcendentals=0),
        name="backward",
    )(positions, slots, vecs, meta, *cots, *saved)


WC = 8 * BLK


def weight_kernel(
    pos,
    x_h,
    heads_h,
    act_h,
    d_up_h,
    d_q_h,
    d_k_h,
    d_v_h,
    d_proj_h,
    hid_h,
    d_br_h,
    grads,
    x_c,
    heads,
    act,
    d_up,
    d_q,
    d_k,
    d_v,
    d_proj,
    hid,
    d_br,
    stage,
    i_sem,
    g_sem,
):
    refs = (
        (x_h, x_c),
        (d_q_h, d_q),
        (d_k_h, d_k),
        (d_v_h, d_v),
        (heads_h, heads),
        (d_proj_h, d_proj),
        (hid_h, hid),
        (d_up_h, d_up),
        (d_br_h, d_br),
        (act_h, act),
    )
    fetch = [pltpu.make_async_copy(src, dst, i_sem.at[i]) for i, (src, dst) in enumerate(refs)]
    for copy in fetch:
        copy.start()

    per = WC // BLK

    def g_copy(chunk, j, at):
        return pltpu.make_async_copy(
            stage.at[at, pl.ds(j * BLK, BLK)], grads.at[pos[chunk * per + j]], g_sem.at[at]
        )

    def put(chunk, left, right):
        at = lax.rem(chunk, 2)

        @pl.when(chunk >= 2)
        def _():
            for j in range(per):
                g_copy(chunk - 2, j, at).wait()

        stage[at] = mm(left, right, TN).astype(BF)
        for j in range(per):
            g_copy(chunk, j, at).start()

    first = 0
    for left, right, needs in (
        (x_c, d_q, (0, 1)),
        (x_c, d_k, (2,)),
        (x_c, d_v, (3,)),
        (heads, d_proj, (4, 5)),
        (d_up, hid, (6, 7)),
        (act, d_br, (8, 9)),
    ):
        for i in needs:
            fetch[i].wait()

        def body(j, left=left, right=right, first=first):
            put(first + j, left[:, pl.ds(pl.multiple_of(j * WC, WC), WC)], right[...])

        loop(left.shape[1] // WC, body)
        first += left.shape[1] // WC
    for chunk in (first - 2, first - 1):
        for j in range(per):
            g_copy(chunk, j, chunk % 2).wait()


def weight_grads_of(total_slots, positions, x_c, saved):
    r_v, w_v = pltpu.VMEM((ROWS, D), BF), pltpu.VMEM((ROWS, FF), BF)
    return pl.pallas_call(
        weight_kernel,
        out_shape=jax.ShapeDtypeStruct((total_slots, BLK, D), BF),
        in_specs=[SMEM] + [ANY] * 10,
        out_specs=ANY,
        scratch_shapes=[r_v, r_v, w_v, w_v]
        + [r_v] * 6
        + [
            pltpu.VMEM((2, WC, D), BF),
            pltpu.SemaphoreType.DMA((10,)),
            pltpu.SemaphoreType.DMA((2,)),
        ],
        compiler_params=pltpu.CompilerParams(vmem_limit_bytes=VMEM_LIMIT),
        cost_estimate=pl.CostEstimate(flops=2 * ROWS * WROWS * D, bytes_accessed=40 << 20, transcendentals=0),
        name="weight_grads",
    )(positions, x_c, *saved)


def local(
    tokens,
    cotangent,
    cluster_order,
    block_owner,
    master_slots,
    moment_one,
    moment_two,
    vector_master,
    vector_moment_one,
    vector_moment_two,
):
    tok_count = lax.axis_size("tok")
    tok_index = lax.axis_index("tok")
    slot_count = master_slots.shape[0]
    cap = tok_count // SD * (max(1, CPS // tok_count) * 3 * CL // (2 * SD))
    total_slots = tok_count * slot_count
    order = cluster_order.reshape(1, ROWS)

    block = jax.ShapeDtypeStruct((SD, cap, D), BF)
    meta_shape = jax.ShapeDtypeStruct((SD, META, D), BF)
    row_block = jax.ShapeDtypeStruct((ROWS, D), BF)
    four_planes = tok_count == 8 and lax.axis_size("rep") == 4
    if four_planes:
        slots_low, x_c, *cots, recv_meta, vecs, b_u, occupancy, positions = gather_all(
            cap, tokens, cotangent, order, master_slots, vector_master, block_owner
        )
        positions = positions.reshape(NBLK)
    else:
        positions = slot_positions(block_owner, slot_count)
        slots_low = lax.all_gather(master_slots.astype(BF), "tok", axis=0, tiled=True)
        vectors = lax.all_gather(vector_master.astype(BF), "tok", axis=0, tiled=True).astype(F32)
        vecs, b_u = vectors[: 8 * D].reshape(8, D), vectors[8 * D :].reshape(1, FF)
        cluster = tok_index // SD * CPS + cluster_order // CL
        target = cluster % tok_count
        chosen = target[None, :] == jnp.arange(tok_count, dtype=jnp.int32)[:, None]
        sent_counts = jnp.sum(chosen.astype(F32), axis=1)
        own_row = (jnp.arange(tok_count, dtype=jnp.int32) == tok_index).astype(F32)
        occupancy = lax.psum(own_row[:, None] * sent_counts[None, :], ("tok", "rep")).astype(jnp.int32)
        send_x, send_c, meta = pl.pallas_call(
            functools.partial(send_kernel, cap),
            out_shape=(block, block, meta_shape),
            in_specs=[VMEM] * 3,
            out_specs=(VMEM,) * 3,
            compiler_params=pltpu.CompilerParams(vmem_limit_bytes=VMEM_LIMIT),
            name="send_rows",
        )(tokens, cotangent, order)
        recv_x, recv_meta = (jnp.stack(swap_blocks(b)) for b in (send_x, meta))
        x_c = pl.pallas_call(
            functools.partial(seat_kernel, cap),
            out_shape=row_block,
            in_specs=[VMEM] * 2,
            out_specs=VMEM,
            compiler_params=pltpu.CompilerParams(vmem_limit_bytes=VMEM_LIMIT),
            name="seat_rows",
        )(recv_x, recv_meta)
        cots = [send_c[k] for k in range(SD)]

    cots = swap_blocks(cots)
    *out_blocks, heads, act, hid, q, k, v, p, slope, n1, n2, rs1, rs2 = forward(
        cap, positions, slots_low, vecs, b_u, x_c, recv_meta
    )
    out_blocks = swap_blocks(out_blocks)
    *ing_blocks, shares, d_up, d_q, d_k, d_v, d_proj, d_br = backward(
        cap, positions, slots_low, vecs, recv_meta, cots, (q, k, v, p, slope, n1, n2, rs1, rs2)
    )
    ing_blocks = swap_blocks(ing_blocks)
    grads = weight_grads_of(
        total_slots, positions, x_c, (heads, act, d_up, d_q, d_k, d_v, d_proj, hid, d_br)
    )
    if four_planes:
        total, vec_owned, output, input_grad, entropy = reduce_all(
            cap, grads, shares, order, out_blocks, ing_blocks, slot_count
        )
    else:
        total = lax.psum(lax.psum_scatter(grads, "tok", scatter_dimension=0, tiled=True), "rep")
        grad_vector = shares[:, 0:9].reshape(-1)
        vec_owned = lax.psum(lax.psum_scatter(grad_vector, "tok", scatter_dimension=0, tiled=True), "rep")
        output, input_grad, entropy = pl.pallas_call(
            functools.partial(return_kernel, cap),
            out_shape=(row_block, row_block, jax.ShapeDtypeStruct((1, ROWS), BF)),
            in_specs=[VMEM] * (2 * SD + 1),
            out_specs=(VMEM,) * 3,
            compiler_params=pltpu.CompilerParams(vmem_limit_bytes=VMEM_LIMIT),
            name="return_rows",
        )(order, *out_blocks, *ing_blocks)

    used = jnp.any(
        positions[None, :] == (tok_index * slot_count + jnp.arange(slot_count, dtype=I32))[:, None], axis=1
    )
    owned_grad = jnp.where(used[:, None, None], total.astype(F32), 0.0)
    first_new, second_new, master_new = adam_update(
        owned_grad, master_slots, moment_one, moment_two, rate_matrix
    )
    vec_first, vec_second, vec_new = adam_update(
        vec_owned, vector_master, vector_moment_one, vector_moment_two, rate_vector
    )
    return (
        output,
        input_grad,
        owned_grad,
        first_new,
        second_new,
        master_new,
        master_new.astype(BF),
        vec_owned,
        vec_first,
        vec_second,
        vec_new,
        vec_new.astype(BF),
        entropy.reshape(-1),
        occupancy,
    )


def solution(mesh):
    placed = (
        P(("rep", "tok"), None),
        P(("rep", "tok"), None),
        P(("rep", "tok")),
        P(),
        P("tok", None, None),
        P("tok", None, None),
        P("tok", None, None),
        P("tok"),
        P("tok"),
        P("tok"),
    )
    return jax.shard_map(
        local,
        mesh=mesh,
        in_specs=placed,
        out_specs=(
            P(("rep", "tok"), None),
            P(("rep", "tok"), None),
            P("tok", None, None),
            P("tok", None, None),
            P("tok", None, None),
            P("tok", None, None),
            P("tok", None, None),
            P("tok"),
            P("tok"),
            P("tok"),
            P("tok"),
            P("tok"),
            P(("rep", "tok")),
            P(),
        ),
        check_vma=False,
    )
```

```python
import functools
import math

import jax
import jax.numpy as jnp
from jax import lax
from jax.experimental import pallas as pl
from jax.experimental.pallas import tpu as pltpu
from jax.sharding import PartitionSpec as P

D = 768
HEADS = 12
HD = 64
FF = 3072
SD = 4
CL = 128
NBLK = 96
STEP = 10
CPS = 32
WROWS = 9216
BLK = 96
ROWS = 1024
PAIRS = HEADS // 2
PW = 2 * HD
TM = 1024
META = 16
VMEM_LIMIT = 63 << 20
FC = 768

norm_epsilon = 1e-06
beta_first = 0.9
beta_second = 0.999
adam_epsilon = 1e-08
weight_decay = 0.01
rate_matrix = 0.02
rate_vector = 0.2

BF = jnp.bfloat16
F32 = jnp.float32
I32 = jnp.int32

VMEM = pl.BlockSpec(memory_space=pltpu.VMEM)
SMEM = pl.BlockSpec(memory_space=pltpu.SMEM)
ANY = pl.BlockSpec(memory_space=pl.ANY)

NN = (((1,), (0,)), ((), ()))
NT = (((1,), (1,)), ((), ()))
TN = (((0,), (0,)), ((), ()))


def mm(a, b, dims=NN):
    return lax.dot_general(a, b, dims, preferred_element_type=F32)


def slot_positions(block_owner, slot_count):
    owners = block_owner[:, 0]
    blocks = owners.shape[0]
    shared = owners[:, None] == owners[None, :]
    before = (
        jnp.arange(blocks, dtype=jnp.int32)[None, :] < jnp.arange(blocks, dtype=jnp.int32)[:, None]
    )
    earlier = jnp.sum((shared & before).astype(jnp.int32), axis=1)
    return owners * slot_count + earlier


def adam_update(grad_now, weight_old, first_old, second_old, rate_step):
    first_new = beta_first * first_old + (1.0 - beta_first) * grad_now
    second_new = beta_second * second_old + (1.0 - beta_second) * grad_now * grad_now
    first_hat = first_new / (1.0 - beta_first**STEP)
    second_hat = second_new / (1.0 - beta_second**STEP)
    weight_new = weight_old - rate_step * (
        first_hat / (jnp.sqrt(second_hat) + adam_epsilon) + weight_decay * weight_old
    )
    return (first_new, second_new, weight_new)


def route_slots(order, seat, cap):
    cluster = order // CL
    rel = lax.rem(cluster, SD) ^ seat
    place = (cluster // SD) * CL + lax.rem(order, CL) + 1
    chosen = lax.broadcasted_iota(I32, (8, ROWS), 0) == rel
    chosen_low = jnp.where(chosen, 1.0, 0.0).astype(BF)
    before = lax.broadcasted_iota(I32, (ROWS, ROWS), 0) < lax.broadcasted_iota(I32, (ROWS, ROWS), 1)
    before_low = jnp.where(before, 1.0, 0.0).astype(BF)
    running = mm(chosen_low, before_low)
    rank = jnp.sum(jnp.where(chosen, running, 0.0), axis=0, keepdims=True).astype(I32)
    return rel * cap + rank, place


def slot_matrix(slots, at, cap):
    rows = lax.broadcasted_iota(I32, (cap, ROWS), 0) + at * cap
    return jnp.where(rows == slots, 1.0, 0.0).astype(BF)


def send_kernel(cap, tokens, cotangent, order, send_x, send_c, meta):
    seat = lax.rem(lax.axis_index("tok"), SD)
    slots, place = route_slots(order[...], seat, cap)
    digits = jnp.concatenate([place // CL, lax.rem(place, CL)] + [place * 0] * 6, axis=0).astype(F32).astype(BF)
    for at in range(SD):
        picked = slot_matrix(slots, at, cap)
        send_x[at] = mm(picked, tokens[...]).astype(BF)
        send_c[at] = mm(picked, cotangent[...]).astype(BF)
        coded = mm(digits, picked, NT)
        line = jnp.concatenate([coded[0:1], coded[1:2]], axis=1)
        meta[at] = jnp.broadcast_to(line, (META, D)).astype(BF)


def remote(src, dst, send_sem, recv_sem, tok, rep):
    return pltpu.make_async_remote_copy(
        src_ref=src,
        dst_ref=dst,
        send_sem=send_sem,
        recv_sem=recv_sem,
        device_id={"tok": tok, "rep": rep},
        device_id_type=pl.DeviceIdType.MESH,
    )


def loop(n, body):
    def run(i, c):
        body(i)
        return c

    lax.fori_loop(0, n, run, 0)


class Place:
    def __init__(self):
        self.me = me = lax.axis_index("tok")
        self.z = z = lax.axis_index("rep")
        core, x, y = me % 2, (me // 2) % 2, me // 4
        self.twin = me + 1 - 2 * core
        self.xn = me + 2 - 4 * x
        self.yn = me + 4 - 8 * y
        self.dn = self.xn + 4 - 8 * y
        self.side = z % 2
        self.zp = z + 1 - 2 * self.side

    def twin_of(self, tok):
        return tok + 1 - 2 * (tok % 2)

    def greet(self, peers):
        barrier = pltpu.get_barrier_semaphore()
        for tok, rep in peers:
            pl.semaphore_signal(
                barrier, inc=1, device_id={"tok": tok, "rep": rep}, device_id_type=pl.DeviceIdType.MESH
            )
        return lambda: pl.semaphore_wait(barrier, len(peers))


def seat_matrix(meta, first, rows, cap):
    hi = jnp.concatenate([meta[k, 0:8, 0:cap] for k in range(SD)], axis=1).astype(F32)[0:1]
    lo = jnp.concatenate([meta[k, 0:8, cap : 2 * cap] for k in range(SD)], axis=1).astype(F32)[0:1]
    at = (hi * CL + lo).astype(I32)
    seats = lax.broadcasted_iota(I32, (rows, SD * cap), 0) + (first + 1)
    return jnp.where(seats == at, 1.0, 0.0).astype(BF)


def seat_part(meta, k, cap):
    hi = meta[k, 0:8, 0:cap].astype(F32)[0:1]
    lo = meta[k, 0:8, cap : 2 * cap].astype(F32)[0:1]
    at = (hi * CL + lo).astype(I32)
    seats = lax.broadcasted_iota(I32, (ROWS, cap), 0) + 1
    return jnp.where(seats == at, 1.0, 0.0).astype(BF)


def seat_rows(meta, blocks, cap, to):
    def body(t):
        r0 = pl.multiple_of(t * 256, 256)
        rows = blocks[...].reshape(SD * cap, D)
        to[pl.ds(r0, 256), :] = mm(seat_matrix(meta, r0, 256, cap), rows).astype(BF)

    loop(ROWS // 256, body)


def seat_kernel(cap, blocks, meta, to):
    seat_rows(meta, blocks, cap, to)


def gather_kernel(
    cap,
    count,
    tokens_h,
    cotangent_h,
    order,
    master_h,
    vector,
    owner_of,
    slots,
    x_c,
    cot_0,
    cot_1,
    cot_2,
    cot_3,
    recv_meta,
    vecs,
    b_u,
    occupancy,
    positions,
    tokens,
    cotangent,
    master,
    own,
    send_x,
    send_c,
    meta,
    recv_x,
    got_meta,
    slot_of,
    digits,
    mine,
    by_z,
    by_tok,
    x_s,
    x_r,
    y_s,
    y_r,
    d_s,
    d_r,
    zx_s,
    zx_r,
    zd_s,
    zd_r,
    zy_s,
    zy_r,
    p_s,
    p_r,
    row_s,
    row_r,
    z_s,
    z_r,
    t_s,
    t_r,
    local_s,
):
    at = Place()
    me, z, side = at.me, at.z, at.side
    n_tok, n_rep = 8, 4
    peers = [((me + d) % n_tok, z) for d in range(1, n_tok)] + [(me, (z + d) % n_rep) for d in range(1, n_rep)]
    fetch = [
        pltpu.make_async_copy(src, dst, local_s.at[i])
        for i, (src, dst) in enumerate(((master_h, master), (tokens_h, tokens), (cotangent_h, cotangent)))
    ]
    for copy in fetch:
        copy.start()
    wait_peers = at.greet(peers)
    fetch[0].wait()

    def cast(s):
        own[s] = master[s].astype(BF)

    loop(count, cast)
    wait_peers()

    half = count // 2

    def slot(owner, s):
        return slots.at[owner * count + s]

    def to_x(s):
        return remote(own.at[s], slot(me, s), x_s.at[s], x_r.at[s], at.xn, z)

    def to_y(s):
        return remote(own.at[s], slot(me, s), y_s.at[s], y_r.at[s], at.yn, z)

    def on_y(s):
        return remote(slot(at.xn, s), slot(at.xn, s), d_s.at[s], d_r.at[s], at.yn, z)

    def x_on_z(s):
        return remote(slot(at.xn, s), slot(at.xn, s), zx_s.at[s], zx_r.at[s], me, at.zp)

    def d_on_z(s):
        return remote(slot(at.dn, s), slot(at.dn, s), zd_s.at[s], zd_r.at[s], me, at.zp)

    def y_on_z(s):
        return remote(slot(at.yn, s), slot(at.yn, s), zy_s.at[s], zy_r.at[s], me, at.zp)

    few = count // 3
    most = count - few

    def straight(j):
        return few * side + j

    def shared(j):
        return most * side + j

    def lacking(j):
        return most * (1 - side) + j

    owners = (me, at.xn, at.yn, at.dn)

    runs = (
        (0, 0, count),
        (1, half * side, half + 1),
        (2, most * side, few),
        (2, few, most - few),
        (3, half * side, half + 1),
        (1, (half + 1) * (1 - side), half),
        (2, most * (1 - side), few),
        (3, (half + 1) * (1 - side), half // 2),
        (3, (half + 1) * (1 - side) + half // 2, half - half // 2),
    )

    def to_twin(i):
        q, s, n = runs[i]
        src = own if q == 0 else slots.at[pl.ds(owners[q] * count + s, n)]
        dst = slots.at[pl.ds(owners[q] * count + s, n)]
        return remote(src, dst, p_s.at[i], p_r.at[i], at.twin, z)

    def near(j):
        return (half + 1) * side + j

    def far(j):
        return (half + 1) * (1 - side) + j

    loop(half, lambda j: to_x(near(j)).start())
    to_x(half).start()
    loop(few, lambda j: to_y(shared(j)).start())
    to_twin(0).start()
    keep = pltpu.make_async_copy(own, slots.at[pl.ds(me * count, count)], local_s.at[3])
    keep.start()

    seat = me % SD
    seats = (me, at.twin, at.xn, at.twin_of(at.xn))
    rows_of = ((meta, got_meta), (send_x, recv_x))

    def row_copy(i, k):
        src, dst = rows_of[i]
        return remote(src.at[k], dst.at[k], row_s.at[i, k], row_r.at[i, k], seats[k], z)

    put_c = [
        pltpu.make_async_copy(send_c.at[k], to, local_s.at[4 + k])
        for k, to in enumerate((cot_0, cot_1, cot_2, cot_3))
    ]

    def route():
        fetch[1].wait()
        fetch[2].wait()
        slots_here, place = route_slots(order[...], seat, cap)
        slot_of[...] = slots_here
        digits[...] = (
            jnp.concatenate([place // CL, lax.rem(place, CL)] + [place * 0] * 6, axis=0).astype(F32).astype(BF)
        )

    def sort_tokens(k):
        picked = slot_matrix(slot_of[...], k, cap)
        send_x[k] = mm(picked, tokens[...]).astype(BF)
        coded = mm(digits[...], picked, NT)
        line = jnp.concatenate([coded[0:1], coded[1:2]], axis=1)
        meta[k] = jnp.broadcast_to(line, (META, D)).astype(BF)
        for i in range(2):
            if k:
                row_copy(i, k).start()
            else:
                src, dst = rows_of[i]
                dst[0] = src[0]

    def sort_cotangent(k):
        send_c[k] = mm(slot_matrix(slot_of[...], k, cap), cotangent[...]).astype(BF)
        put_c[k].start()

    def z_copy(d):
        return remote(by_z.at[0], by_z.at[d], z_s.at[d], z_r.at[d], me, (z + d) % n_rep)

    def t_copy(d):
        return remote(mine, by_tok.at[d], t_s.at[d], t_r.at[d], (me + d) % n_tok, z)

    def count_rows():
        residue = lax.rem(me // SD * CPS + order[...] // CL, n_tok)
        hit = lax.broadcasted_iota(I32, (128, ROWS), 0) == residue
        by_z[0] = mm(jnp.ones((8, ROWS), BF), jnp.where(hit, 1.0, 0.0).astype(BF), NT)
        for d in range(1, n_rep):
            z_copy(d).start()
        for i in range(9):
            mine[i : i + 1] = vector[i * 128 : (i + 1) * 128].reshape(1, 128).astype(BF).astype(F32)
        block_row = lax.broadcasted_iota(I32, (NBLK, NBLK), 0)
        block_col = lax.broadcasted_iota(I32, (NBLK, NBLK), 1)
        by_col = owner_of[...].astype(F32)
        by_row = lane_sum(jnp.where(block_row == block_col, by_col, 0.0))
        earlier = jnp.where((by_row == by_col) & (block_row < block_col), 1.0, 0.0)
        positions[...] = (by_col * count + jnp.sum(earlier, axis=0, keepdims=True)).astype(I32)

    def share_vectors():
        for d in range(1, n_rep):
            z_copy(d).wait()
        mine[16:24] = by_z[0] + by_z[1] + by_z[2] + by_z[3]
        for d in range(1, n_tok):
            t_copy(d).start()

    def lay_out_vectors():
        by_tok[0] = mine[...]
        for d in range(1, n_tok):
            t_copy(d).wait()
        for owner in range(n_tok):
            share = by_tok[(me + n_tok - owner) % n_tok]
            occupancy[owner : owner + 1, :] = share[16:17, 0:n_tok].astype(I32)
            for i in range(9):
                chunk = owner * 9 + i
                row, lane = chunk // 6, chunk % 6 * 128
                if row < 8:
                    vecs[row : row + 1, lane : lane + 128] = share[i : i + 1]
                else:
                    lane += (row - 8) * D
                    b_u[:, lane : lane + 128] = share[i : i + 1]

    def to_x_in(s):
        return remote(own.at[s], slot(at.xn, s), x_s.at[s], x_r.at[s], at.xn, z)

    def y_in(s):
        return remote(own.at[s], slot(at.yn, s), y_s.at[s], y_r.at[s], at.yn, z)

    def d_in(s):
        return remote(own.at[s], slot(at.dn, s), d_s.at[s], d_r.at[s], at.yn, z)

    def x_here(s):
        to_x_in(s).wait_recv()
        on_y(s).start()

    def rest(j):
        return few + j

    between = (
        lambda: (route(), sort_tokens(2)),
        lambda: sort_tokens(3),
        lambda: sort_tokens(1),
        lambda: (sort_tokens(0), count_rows()),
        lambda: sort_cotangent(1),
        lambda: sort_cotangent(2),
    )
    for j in range(half):
        x_here(near(j))
        x_on_z(near(j)).start()
        if j < few:
            y_in(shared(j)).wait_recv()
            y_on_z(shared(j)).start()
        if j == few:
            to_twin(2).start()
        between[j]()
    x_here(half)
    to_twin(1).start()
    loop(most - few, lambda j: to_y(rest(j)).start())
    share_vectors()
    sort_cotangent(3)
    sort_cotangent(0)

    def second(j):
        d_in(near(j)).wait_recv()
        d_on_z(near(j)).start()

    loop(half, second)
    d_in(half).wait_recv()
    to_twin(4).start()
    loop(half, lambda j: x_on_z(far(j)).wait_recv())
    to_twin(5).start()
    lay_out_vectors()
    loop(most - few, lambda j: y_in(rest(j)).wait_recv())
    to_twin(3).start()
    loop(few, lambda j: y_on_z(lacking(j)).wait_recv())
    to_twin(6).start()
    for i in (0, 1):
        for k in (2, 3, 1):
            row_copy(i, k).wait_recv()
    recv_meta[...] = got_meta[...]
    seat_rows(got_meta, recv_x, cap, x_c)
    loop(half // 2, lambda j: d_on_z(far(j)).wait_recv())
    to_twin(7).start()
    loop(half - half // 2, lambda j: d_on_z(far(half // 2 + j)).wait_recv())
    to_twin(8).start()

    for i in range(2):
        for k in (2, 3, 1):
            row_copy(i, k).wait_send()
    for copy in put_c:
        copy.wait()
    keep.wait()

    def sent_half(j):
        to_x(near(j)).wait_send()
        on_y(near(j)).wait_send()
        x_on_z(near(j)).wait_send()
        d_on_z(near(j)).wait_send()

    loop(half, sent_half)
    to_x(half).wait_send()
    on_y(half).wait_send()

    for i in range(len(runs)):
        to_twin(i).wait()
    loop(most, lambda j: to_y(straight(j)).wait_send())
    loop(few, lambda j: y_on_z(shared(j)).wait_send())


def gather_all(cap, tokens, cotangent, order, master, vector, block_owner):
    count = master.shape[0]
    rows = jax.ShapeDtypeStruct((ROWS, D), BF)
    part = jax.ShapeDtypeStruct((cap, D), BF)
    dma = pltpu.SemaphoreType.DMA
    block = pltpu.VMEM((SD, cap, D), BF)
    meta = pltpu.VMEM((SD, META, D), BF)
    return pl.pallas_call(
        functools.partial(gather_kernel, cap, count),
        out_shape=(
            jax.ShapeDtypeStruct((8 * count, BLK, D), BF),
            rows,
            part,
            part,
            part,
            part,
            jax.ShapeDtypeStruct((SD, META, D), BF),
            jax.ShapeDtypeStruct((8, D), F32),
            jax.ShapeDtypeStruct((1, FF), F32),
            jax.ShapeDtypeStruct((8, 8), I32),
            jax.ShapeDtypeStruct((1, NBLK), I32),
        ),
        in_specs=[ANY, ANY, VMEM, ANY, VMEM, VMEM],
        out_specs=(ANY, VMEM) + (ANY,) * SD + (VMEM,) * 5,
        scratch_shapes=[
            pltpu.VMEM((ROWS, D), BF),
            pltpu.VMEM((ROWS, D), BF),
            pltpu.VMEM((count, BLK, D), F32),
            pltpu.VMEM((count, BLK, D), BF),
            block,
            block,
            meta,
            block,
            meta,
            pltpu.VMEM((1, ROWS), I32),
            pltpu.VMEM((8, ROWS), BF),
            pltpu.VMEM((24, 128), F32),
            pltpu.VMEM((4, 8, 128), F32),
            pltpu.VMEM((8, 24, 128), F32),
        ]
        + [dma((count,))] * 12
        + [dma((9,))] * 2
        + [dma((2, SD))] * 2
        + [dma((4,))] * 2
        + [dma((8,))] * 2
        + [dma((8,))],
        compiler_params=pltpu.CompilerParams(collective_id=0, has_side_effects=True, vmem_limit_bytes=VMEM_LIMIT),
        cost_estimate=pl.CostEstimate(flops=8 * ROWS * ROWS * D, bytes_accessed=64 << 20, transcendentals=0),
        name="gather",
    )(tokens, cotangent, order, master, vector, block_owner.reshape(1, NBLK))


def return_kernel(cap, order, *refs):
    outs, ings, (out, ing, entropy) = refs[:SD], refs[SD : 2 * SD], refs[2 * SD :]
    seat = lax.rem(lax.axis_index("tok"), SD)
    slots, _ = route_slots(order[...], seat, cap)
    picked = jnp.concatenate([slot_matrix(slots, at, cap) for at in range(SD)], axis=0)
    for to, blocks in ((out, outs), (ing, ings)):
        rows = jnp.concatenate([block[0:cap, :] for block in blocks], axis=0)
        to[...] = mm(picked, rows, TN).astype(BF)
    line = jnp.concatenate([block[cap : cap + 8, 0:cap] for block in outs], axis=1)
    entropy[...] = mm(line, picked)[0:1].astype(BF)


def swap_blocks(blocks):
    n = lax.axis_size("tok")
    parts = [blocks[0]]
    for k in range(1, SD):
        parts.append(lax.ppermute(blocks[k], "tok", [(i, i ^ k) for i in range(n)]))
    return parts


def reduce_kernel(
    cap,
    count,
    split,
    grads,
    vec,
    order,
    out_0,
    out_1,
    out_2,
    out_3,
    ing_0,
    ing_1,
    ing_2,
    ing_3,
    total,
    vec_out,
    output,
    input_grad,
    entropy,
    out_v,
    ing_v,
    slot_of,
    a,
    tw,
    rd,
    rx,
    ry,
    o,
    rz1,
    pz,
    rz2,
    fz,
    vt,
    va,
    vb,
    vc,
    a_l,
    keep_l,
    p_s,
    p_r,
    d_s,
    d_r,
    x_s,
    x_r,
    y_s,
    y_r,
    z1_s,
    z1_r,
    z2_s,
    z2_r,
    z3_s,
    z3_r,
    t_s,
    t_r,
    v_s,
    v_r,
    row_l,
):
    at = Place()
    me, z = at.me, at.z
    n_tok, n_rep = 8, 4
    peers = [((me + d) % n_tok, z) for d in range(1, n_tok)] + [(me, (z + d) % n_rep) for d in range(1, n_rep)]
    wait_peers = at.greet(peers)
    owners = (me, at.xn, at.yn, at.dn)

    def load(q):
        return pltpu.make_async_copy(grads.at[pl.ds(owners[q] * count, count)], a.at[q], a_l.at[q])

    for q in (3, 1, 2, 0):
        load(q).start()
    rows_in = [
        pltpu.make_async_copy(src, to.at[k], row_l.at[i, k])
        for i, (blocks, to) in enumerate((((out_0, out_1, out_2, out_3), out_v), ((ing_0, ing_1, ing_2, ing_3), ing_v)))
        for k, src in enumerate(blocks)
    ]
    for copy in rows_in:
        copy.start()
    wait_peers()

    groups = [(g, g * (count // 4), count // 4 if g < 3 else count - 3 * (count // 4)) for g in range(4)]

    def to_twin(q, group):
        g, s, n = group
        src = grads.at[pl.ds(at.twin_of(owners[q]) * count + s, n)]
        return remote(src, tw.at[q, pl.ds(s, n)], p_s.at[q, g], p_r.at[q, g], at.twin, z)

    def d_y(s):
        return remote(a.at[3, s], rd.at[s], d_s.at[s], d_r.at[s], at.yn, z)

    def d_x(s):
        return remote(a.at[3, s], rd.at[s], d_s.at[s], d_r.at[s], at.xn, z)

    def to_x(s):
        return remote(a.at[1, s], rx.at[s], x_s.at[s], x_r.at[s], at.xn, z)

    def to_y(s):
        return remote(a.at[2, s], ry.at[s], y_s.at[s], y_r.at[s], at.yn, z)

    def z_in(s):
        return remote(o.at[s], rz1.at[s], z1_s.at[s], z1_r.at[s], me, at.zp)

    def z_swap(s):
        return remote(pz.at[s], rz2.at[s], z2_s.at[s], z2_r.at[s], me, n_rep - 1 - z)

    def z_out(s):
        return remote(fz.at[s], fz.at[s], z3_s.at[s], z3_r.at[s], me, at.zp)

    def keep(s):
        return pltpu.make_async_copy(fz.at[s], total.at[s], keep_l.at[s])

    for group in groups:
        for q in (3, 1, 2, 0):
            to_twin(q, group).start()

    def v_tok(d):
        return remote(vec.at[(me + d) % n_tok], vt.at[d], t_s.at[d], t_r.at[d], (me + d) % n_tok, z)

    def v_rep(i, src):
        return remote(src, vb.at[i], v_s.at[i], v_r.at[i], me, at.zp if i == 0 else (z + 2) % n_rep)

    for d in range(1, n_tok):
        v_tok(d).start()

    slots_here, _ = route_slots(order[...], me % SD, cap)
    slot_of[...] = slots_here

    def join(q, s):
        return a[q, s] + tw[q, s]

    def first(s, send):
        a[3, s] = join(3, s)
        send(s).start()

    def plain(q, s, send):
        a[q, s] = join(q, s)
        send(s).start()

    def joined(q, s, arrived, send):
        arrived(s).wait_recv()
        a[q, s] = join(q, s) + rd[s]
        send(s).start()

    inner = (z == 1) | (z == 2)
    outer = (z == 0) | (z == 3)

    def own(s):
        to_x(s).wait_recv()
        to_y(s).wait_recv()
        o[s] = join(0, s) + (rx[s] + ry[s])
        pl.when(outer)(lambda: z_in(s).start())

    def middle(s):
        @pl.when(inner)
        def _():
            z_in(s).wait_recv()
            pz[s] = o[s] + rz1[s]
            z_swap(s).start()

    def last(s):
        @pl.when(inner)
        def _():
            z_swap(s).wait_recv()
            fz[s] = pz[s] + rz2[s]
            z_out(s).start()
            keep(s).start()

    def taken(s):
        @pl.when(outer)
        def _():
            z_out(s).wait_recv()
            keep(s).start()

    def pick_rows(i):
        ts = pl.ds(pl.multiple_of(i * 256, 256), 256)
        hit = lax.broadcasted_iota(I32, (SD * cap, 256), 0) == slot_of[:, ts]
        picked = jnp.where(hit, 1.0, 0.0).astype(BF)
        outs = jnp.concatenate([out_v[k, 0:cap, :] for k in range(SD)], axis=0)
        ings = jnp.concatenate([ing_v[k] for k in range(SD)], axis=0)
        both = mm(picked, jnp.concatenate([outs, ings], axis=1), TN)
        output[ts, :] = both[:, 0:D].astype(BF)
        input_grad[ts, :] = both[:, D:].astype(BF)
        line = jnp.concatenate([out_v[k, cap : cap + 8, 0:cap] for k in range(SD)], axis=1)
        entropy[:, ts] = mm(line, picked)[0:1].astype(BF)

    for q in (3, 1, 2, 0):
        load(q).wait()
    for copy in rows_in:
        copy.wait()

    def steps(i, lag, more):
        s = i - lag
        by_x = (s % 2 == 0) & (s < 2 * split)
        live = (s >= 0) & (s < count)
        pl.when(live & by_x)(lambda: more(s, True))
        pl.when(live & jnp.logical_not(by_x))(lambda: more(s, False))

    def steps_of(i, lag, more):
        pl.when((i >= lag) & (i < count + lag))(lambda: more(i - lag))

    def round_of(i):
        for group in groups:

            @pl.when(i == group[1])
            def _(group=group):
                for q in (3, 1, 2):
                    to_twin(q, group).wait_recv()

            @pl.when(i == group[1] + 4)
            def _(group=group):
                to_twin(0, group).wait_recv()

        steps(i, 0, lambda s, by_x: first(s, d_x if by_x else d_y))
        steps(i, 0, lambda s, by_x: plain(1, s, to_x) if by_x else plain(2, s, to_y))
        steps(i, 2, lambda s, by_x: joined(2, s, d_x, to_y) if by_x else joined(1, s, d_y, to_x))
        steps_of(i, 4, own)
        steps_of(i, 6, middle)
        steps_of(i, 8, last)
        steps_of(i, 10, taken)
        pl.when((i == 3) | (i == 5) | (i == 7) | (i == 9))(lambda: pick_rows((i - 3) // 2))

    loop(3, round_of)

    v_sum = vec[me]
    for d in range(1, n_tok):
        v_tok(d).wait()
        v_sum = v_sum + vt[d]
    va[...] = v_sum
    v_rep(0, va).start()

    loop(3, lambda i: round_of(3 + i))
    v_rep(0, va).wait()
    vc[...] = va[...] + vb[0]
    v_rep(1, vc).start()
    loop(count + 4, lambda i: round_of(6 + i))
    v_rep(1, vc).wait()
    vec_out[...] = vc[...] + vb[1]

    for group in groups:
        for q in range(4):
            to_twin(q, group).wait_send()

    def sent(s):
        d_y(s).wait_send()
        to_x(s).wait_send()
        to_y(s).wait_send()
        keep(s).wait()

    loop(count, sent)

    @pl.when(outer)
    def _():
        loop(count, lambda s: z_in(s).wait_send())

    @pl.when(inner)
    def _():
        def back(s):
            z_swap(s).wait_send()
            z_out(s).wait_send()

        loop(count, back)


def reduce_all(cap, grads, shares, order, outs, ings, count):
    dma = pltpu.SemaphoreType.DMA
    part = pltpu.VMEM((count, BLK, D), BF)
    whole = pltpu.VMEM((4, count, BLK, D), BF)
    line = pltpu.VMEM((16, 128), F32)
    rows = jax.ShapeDtypeStruct((ROWS, D), BF)
    total, vec, output, input_grad, entropy = pl.pallas_call(
        functools.partial(reduce_kernel, cap, count, count // 2),
        out_shape=(
            jax.ShapeDtypeStruct((count, BLK, D), BF),
            jax.ShapeDtypeStruct((16, 128), F32),
            rows,
            rows,
            jax.ShapeDtypeStruct((1, ROWS), BF),
        ),
        in_specs=[ANY, VMEM, VMEM] + [ANY] * (2 * SD),
        out_specs=(ANY,) + (VMEM,) * 4,
        scratch_shapes=[
            pltpu.VMEM((SD, cap + META, D), BF),
            pltpu.VMEM((SD, cap, D), BF),
            pltpu.VMEM((1, ROWS), I32),
            whole,
            whole,
        ]
        + [part] * 8
        + [pltpu.VMEM((8, 16, 128), F32), line, pltpu.VMEM((2, 16, 128), F32), line]
        + [dma((4,)), dma((count,))]
        + [dma((4, 4))] * 2
        + [dma((count,))] * 12
        + [dma((8,))] * 2
        + [dma((2,))] * 2
        + [dma((2, SD))],
        compiler_params=pltpu.CompilerParams(collective_id=1, has_side_effects=True, vmem_limit_bytes=VMEM_LIMIT),
        cost_estimate=pl.CostEstimate(flops=4 * ROWS * ROWS * D, bytes_accessed=64 << 20, transcendentals=0),
        name="reduce",
    )(grads, shares, order, *outs, *ings)
    return total, vec[0:9].reshape(-1), output, input_grad, entropy


V_BQ, V_BV, V_BO, V_BD, V_G1, V_C1, V_G2, V_C2 = range(8)


def inverse(x):
    r = pl.reciprocal(x, approx=True)
    return r * (2.0 - x * r)


def erf_parts(v):
    t = inverse(1.0 + (0.3275911 / math.sqrt(2.0)) * jnp.abs(v))
    e = jnp.exp2((v * v) * (-0.5 / math.log(2.0)))
    poly = 0.5 * 1.061405429
    for c in (-1.453152027, 1.421413741, -0.284496736, 0.254829592):
        poly = poly * t + 0.5 * c
    tail = poly * (t * e)
    return jnp.where(v >= 0.0, 1.0 - tail, tail), e


def lane_sum(x):
    return jnp.sum(x, axis=1, keepdims=True)


def gelu_parts(v):
    phi, e = erf_parts(v)
    return v * phi, phi + v * (e * (1.0 / math.sqrt(2.0 * math.pi)))


def weight_copies(pos, slots, w, sem, first):
    def copy(b):
        return pltpu.make_async_copy(slots.at[pos[first + b]], w.at[pl.ds(b * BLK, BLK)], sem)

    n = w.shape[0] // BLK
    return (lambda: loop(n, lambda b: copy(b).start())), (lambda: loop(n, lambda b: copy(b).wait()))


def halves_of_heads():
    lane = lax.broadcasted_iota(I32, (1, PW), 1)
    m0 = jnp.where(lane < HD, 1.0, 0.0).astype(BF)
    m1 = jnp.where(lane < HD, 0.0, 1.0).astype(BF)
    return lambda pair: jnp.concatenate([pair * m0, pair * m1], axis=0)


def tile_rows(t):
    return pl.ds(pl.multiple_of(t * TM, TM), TM)


def forward_kernel(
    cap,
    pos,
    slots,
    vecs,
    b_u,
    x_h,
    meta,
    back_0,
    back_1,
    back_2,
    back_3,
    heads_h,
    act_h,
    hid_h,
    q_h,
    k_h,
    v_h,
    p_h,
    slope_h,
    n1_h,
    n2_h,
    rs1_h,
    rs2_h,
    wqkv,
    wo,
    wu,
    wd,
    x_c,
    heads,
    act,
    hid,
    q,
    k,
    v,
    p_all,
    slope,
    n1,
    n2,
    rs1,
    rs2,
    out_c,
    ent,
    hid_t,
    w_sem,
    x_sem,
    o_sem,
):
    inv = 1.0 / math.sqrt(HD)
    get_x = pltpu.make_async_copy(x_h, x_c, x_sem)
    get_x.start()
    weights = [
        weight_copies(pos, slots, w, w_sem.at[i], first)
        for i, (w, first) in enumerate(((wqkv, 0), (wo, 24), (wu, 32), (wd, 64)))
    ]
    for start, _ in weights:
        start()
    get_x.wait()
    apart = halves_of_heads()

    def vec(i):
        return vecs[i : i + 1, :]

    saved = (
        (heads, heads_h),
        (act, act_h),
        (hid, hid_h),
        (q, q_h),
        (k, k_h),
        (v, v_h),
        (slope, slope_h),
        (n1, n1_h),
        (n2, n2_h),
        (rs1, rs1_h),
        (rs2, rs2_h),
    )

    def save(t, i):
        src, dst = saved[i]
        return pltpu.make_async_copy(src.at[tile_rows(t)], dst.at[tile_rows(t)], o_sem.at[i])

    def save_p(t):
        n = TM // CL
        cs = pl.ds(t * n, n)
        return pltpu.make_async_copy(p_all.at[cs], p_h.at[cs], o_sem.at[len(saved)])

    def normal(r, n, rs, rows):
        c = r - lane_sum(r) * (1.0 / D)
        scale = lax.rsqrt(lane_sum(c * c) * (1.0 / D) + norm_epsilon)
        rs[rows, :] = jnp.broadcast_to(scale, (TM, 128))
        n[rows, :] = c * scale

    def tile(t):
        rows = tile_rows(t)
        first = t == 0
        pl.when(first)(weights[0][1])
        x = x_c[rows, :]
        q[rows, :] = ((mm(x, wqkv[0:D, :]) + vec(V_BQ)).astype(BF).astype(F32) * inv).astype(BF)
        k[rows, :] = mm(x, wqkv[D : 2 * D, :]).astype(BF)
        v[rows, :] = (mm(x, wqkv[2 * D :, :]) + vec(V_BV)).astype(BF)

        def attend(c):
            gr = pl.ds(pl.multiple_of(t * TM + c * CL, CL), CL)
            total = jnp.zeros((1, CL), F32)
            for p in range(PAIRS):
                ps = slice(p * PW, (p + 1) * PW)
                scores = mm(apart(k[gr, ps]), q[gr, ps], NT)
                halves = []
                for h in range(2):
                    sh = scores[h * CL : (h + 1) * CL]
                    sh = sh - jnp.max(sh, axis=0, keepdims=True)
                    e = jnp.exp(sh)
                    tot = jnp.sum(e, axis=0, keepdims=True)
                    r = 1.0 / tot
                    total += jnp.log(tot) - jnp.sum(e * sh, axis=0, keepdims=True) * r
                    halves.append((e * r).astype(BF))
                probs = jnp.concatenate(halves, axis=0)
                p_all[t * (TM // CL) + c, p] = probs
                heads[gr, ps] = mm(probs, apart(v[gr, ps]), TN).astype(BF)
            ent[:, gr] = jnp.broadcast_to(total * (1.0 / HEADS), (8, CL))

        loop(TM // CL, attend)
        for i in (0, 3, 4, 5):
            save(t, i).start()
        save_p(t).start()
        pl.when(first)(weights[1][1])
        normal(x_c[rows, :].astype(F32) + mm(heads[rows, :], wo[...]) + vec(V_BO), n1, rs1, rows)
        hidden = n1[rows, :] * vec(V_G1) + vec(V_C1)
        hid[rows, :] = hidden.astype(BF)
        hid_t[...] = hidden
        pl.when(first)(weights[2][1])

        def widen(f):
            fs = pl.ds(pl.multiple_of(f * FC, FC), FC)
            g, g_slope = gelu_parts(mm(hid[rows, :], wu[fs, :], NT) + b_u[:, fs])
            act[rows, fs] = g.astype(BF)
            slope[rows, fs] = g_slope.astype(BF)

        loop(FF // FC, widen)
        for i in (1, 2, 6, 7, 9):
            save(t, i).start()
        pl.when(first)(weights[3][1])
        normal(hid_t[...] + mm(act[rows, :], wd[...]) + vec(V_BD), n2, rs2, rows)
        out_c[rows, :] = (n2[rows, :] * vec(V_G2) + vec(V_C2)).astype(BF)
        for i in (8, 10):
            save(t, i).start()

    loop(ROWS // TM, tile)

    for j, back in enumerate((back_0, back_1, back_2, back_3)):
        own = seat_part(meta, j, cap)
        back[0:cap, :] = mm(own, out_c[...], TN).astype(BF)
        line = mm(ent[...].astype(BF), own)
        back[cap:, :] = jnp.concatenate([line, line], axis=1)[0:1].astype(BF) * jnp.ones((META, 1), BF)

    def saved_all(t):
        for i in range(len(saved)):
            save(t, i).wait()
        save_p(t).wait()

    loop(ROWS // TM, saved_all)


def shape_of(kind, *shape):
    return jax.ShapeDtypeStruct(shape, kind)


def saved_shapes():
    rows, wide = ((ROWS, D), BF), ((ROWS, FF), BF)
    probs = ((ROWS // CL, PAIRS, 2 * CL, CL), BF)
    full, thin = ((ROWS, D), F32), ((ROWS, 128), F32)
    return rows, wide, probs, full, thin


def forward(cap, positions, slots, vecs, b_u, x_c, meta):
    rows, wide, probs, full, thin = saved_shapes()
    kept = (rows, wide, rows, rows, rows, rows, probs, wide, full, full, thin, thin)
    dma = pltpu.SemaphoreType.DMA
    return pl.pallas_call(
        functools.partial(forward_kernel, cap),
        out_shape=(shape_of(BF, cap + META, D),) * SD + tuple(shape_of(kind, *shape) for shape, kind in kept),
        in_specs=[SMEM, ANY, VMEM, VMEM, ANY, VMEM],
        out_specs=(VMEM,) * SD + (ANY,) * len(kept),
        scratch_shapes=[
            pltpu.VMEM((3 * D, D), BF),
            pltpu.VMEM((D, D), BF),
            pltpu.VMEM((FF, D), BF),
            pltpu.VMEM((FF, D), BF),
            pltpu.VMEM(*rows),
        ]
        + [pltpu.VMEM(*a) for a in kept]
        + [
            pltpu.VMEM(*rows),
            pltpu.VMEM((8, ROWS), F32),
            pltpu.VMEM((TM, D), F32),
            dma((4,)),
            dma,
            dma((12,)),
        ],
        compiler_params=pltpu.CompilerParams(vmem_limit_bytes=VMEM_LIMIT),
        cost_estimate=pl.CostEstimate(flops=2 * ROWS * WROWS * D, bytes_accessed=64 << 20, transcendentals=0),
        name="forward",
    )(positions, slots, vecs, b_u, x_c, meta)


def backward_kernel(
    cap,
    pos,
    slots,
    vecs,
    meta,
    cot_0,
    cot_1,
    cot_2,
    cot_3,
    q_h,
    k_h,
    v_h,
    p_h,
    slope_h,
    n1_h,
    n2_h,
    rs1_h,
    rs2_h,
    back_0,
    back_1,
    back_2,
    back_3,
    shares,
    d_up_h,
    d_q_h,
    d_k_h,
    d_v_h,
    d_proj_h,
    d_br_h,
    wqkv,
    wo,
    wu,
    wd,
    blocks,
    q,
    k,
    v,
    p_all,
    d_up,
    n1,
    n2,
    rs1,
    rs2,
    d_proj,
    d_br,
    ing_c,
    d_h_t,
    res_t,
    gvec,
    g_bu,
    w_sem,
    c_sem,
    i_sem,
    o_sem,
):
    inv = 1.0 / math.sqrt(HD)
    get_c = [
        pltpu.make_async_copy(cot, blocks.at[j], c_sem.at[j]) for j, cot in enumerate((cot_0, cot_1, cot_2, cot_3))
    ]
    for copy in get_c:
        copy.start()
    fetch = [
        pltpu.make_async_copy(src, dst, i_sem.at[i])
        for i, (src, dst) in enumerate(
            (
                (n2_h, n2),
                (rs2_h, rs2),
                (slope_h, d_up),
                (n1_h, n1),
                (rs1_h, rs1),
                (v_h, v),
                (p_h, p_all),
                (k_h, k),
                (q_h, q),
            )
        )
    ]
    weights = [
        weight_copies(pos, slots, w, w_sem.at[i], first)
        for i, (w, first) in enumerate(((wd, 64), (wu, 32), (wo, 24), (wqkv, 0)))
    ]
    fetch[0].start()
    fetch[1].start()
    weights[0][0]()
    fetch[2].start()
    weights[1][0]()
    fetch[3].start()
    fetch[4].start()
    weights[2][0]()
    for i in range(5, 9):
        fetch[i].start()
    weights[3][0]()
    gvec[...] = jnp.zeros_like(gvec)
    g_bu[...] = jnp.zeros_like(g_bu)
    shares[...] = jnp.zeros_like(shares)
    for copy in get_c:
        copy.wait()
    seat_rows(meta, blocks, cap, d_br)
    apart = halves_of_heads()
    first_half = lax.broadcasted_iota(I32, (CL, PW), 1) < HD

    def vec(i):
        return vecs[i : i + 1, :]

    def add_vec(i, value):
        gvec[i : i + 1, :] += jnp.sum(value, axis=0, keepdims=True)

    saved = ((d_up, d_up_h), (q, d_q_h), (k, d_k_h), (v, d_v_h), (d_proj, d_proj_h), (d_br, d_br_h))

    def save(t, i):
        src, dst = saved[i]
        return pltpu.make_async_copy(src.at[tile_rows(t)], dst.at[tile_rows(t)], o_sem.at[i])

    def norm_back(e, n, rs, gain, shift):
        add_vec(gain, e * n)
        add_vec(shift, e)
        eg = e * vec(gain)
        return rs * (eg - lane_sum(eg) * (1.0 / D) - n * (lane_sum(eg * n) * (1.0 / D)))

    def tile(t):
        rows = tile_rows(t)
        start = t == 0

        @pl.when(start)
        def _():
            fetch[0].wait()
            fetch[1].wait()

        d_r2 = norm_back(d_br[rows, :].astype(F32), n2[rows, :], rs2[rows, 0:1], V_G2, V_C2)
        d_br[rows, :] = d_r2.astype(BF)
        add_vec(V_BD, d_br[rows, :].astype(F32))
        res_t[...] = d_r2

        @pl.when(start)
        def _():
            weights[0][1]()
            fetch[2].wait()

        def widen_back(f):
            fs = pl.ds(pl.multiple_of(f * FC, FC), FC)
            du = (mm(d_br[rows, :], wd[fs, :], NT) * d_up[rows, fs].astype(F32)).astype(BF)
            d_up[rows, fs] = du
            g_bu[:, fs] += jnp.sum(du.astype(F32), axis=0, keepdims=True)

        loop(FF // FC, widen_back)
        for i in (0, 5):
            save(t, i).start()

        @pl.when(start)
        def _():
            weights[1][1]()
            fetch[3].wait()
            fetch[4].wait()

        d_h = res_t[...] + mm(d_up[rows, :], wu[...])
        d_r1 = norm_back(d_h, n1[rows, :], rs1[rows, 0:1], V_G1, V_C1)
        d_proj[rows, :] = d_r1.astype(BF)
        res_t[...] = d_r1
        add_vec(V_BO, d_proj[rows, :].astype(F32))
        save(t, 4).start()

        @pl.when(start)
        def _():
            weights[2][1]()
            for i in range(5, 9):
                fetch[i].wait()

        d_h_t[...] = mm(d_proj[rows, :], wo[...], NT).astype(BF)

        def attend_back(c):
            cr = pl.ds(pl.multiple_of(c * CL, CL), CL)
            gr = pl.ds(pl.multiple_of(t * TM + c * CL, CL), CL)
            for p in range(PAIRS):
                ps = slice(p * PW, (p + 1) * PW)
                dh, qp, ks = d_h_t[cr, ps], q[gr, ps], apart(k[gr, ps])
                probs = p_all[t * (TM // CL) + c, p]
                d_w = mm(apart(v[gr, ps]), dh, NT)
                halves = []
                for h in range(2):
                    wh = probs[h * CL : (h + 1) * CL].astype(F32)
                    dwh = d_w[h * CL : (h + 1) * CL]
                    halves.append((wh * (dwh - jnp.sum(dwh * wh, axis=0, keepdims=True))).astype(BF))
                d_s = jnp.concatenate(halves, axis=0)
                q[gr, ps] = (mm(d_s, ks, TN) * inv).astype(BF)
                dk = mm(d_s, qp)
                k[gr, ps] = jnp.where(first_half, dk[0:CL], dk[CL:]).astype(BF)
                dv = mm(probs, dh)
                v[gr, ps] = jnp.where(first_half, dv[0:CL], dv[CL:]).astype(BF)

        loop(TM // CL, attend_back)
        for i in (1, 2, 3):
            save(t, i).start()
        add_vec(V_BQ, q[rows, :].astype(F32))
        add_vec(V_BV, v[rows, :].astype(F32))
        pl.when(start)(weights[3][1])
        d_x = (
            mm(q[rows, :], wqkv[0:D, :], NT)
            + mm(k[rows, :], wqkv[D : 2 * D, :], NT)
            + mm(v[rows, :], wqkv[2 * D :, :], NT)
        )
        ing_c[rows, :] = (res_t[...] + d_x.astype(BF).astype(F32)).astype(BF)

    loop(ROWS // TM, tile)

    for j, back in enumerate((back_0, back_1, back_2, back_3)):
        back[...] = mm(seat_part(meta, j, cap), ing_c[...], TN).astype(BF)

    for chunk in range(72):
        row, lane = chunk // 6, chunk % 6 * 128
        if row < 8:
            part = gvec[row : row + 1, lane : lane + 128]
        else:
            lane += (row - 8) * D
            part = g_bu[:, lane : lane + 128]
        shares[chunk // 9, chunk % 9 : chunk % 9 + 1, :] = part

    def saved_all(t):
        for i in range(len(saved)):
            save(t, i).wait()

    loop(ROWS // TM, saved_all)


def backward(cap, positions, slots, vecs, meta, cots, saved):
    rows, wide, probs, full, thin = saved_shapes()
    dma = pltpu.SemaphoreType.DMA
    grads = (wide, rows, rows, rows, rows, rows)
    return pl.pallas_call(
        functools.partial(backward_kernel, cap),
        out_shape=(shape_of(BF, cap, D),) * SD
        + (shape_of(F32, 8, 16, 128),)
        + tuple(shape_of(kind, *shape) for shape, kind in grads),
        in_specs=[SMEM, ANY, VMEM, VMEM] + [ANY] * (SD + 9),
        out_specs=(VMEM,) * (SD + 1) + (ANY,) * len(grads),
        scratch_shapes=[
            pltpu.VMEM((3 * D, D), BF),
            pltpu.VMEM((D, D), BF),
            pltpu.VMEM((FF, D), BF),
            pltpu.VMEM((FF, D), BF),
            pltpu.VMEM((SD, cap, D), BF),
        ]
        + [pltpu.VMEM(*a) for a in (rows, rows, rows, probs, wide, full, full, thin, thin, rows, rows, rows)]
        + [
            pltpu.VMEM((TM, D), BF),
            pltpu.VMEM((TM, D), F32),
            pltpu.VMEM((8, D), F32),
            pltpu.VMEM((1, FF), F32),
            dma((4,)),
            dma((4,)),
            dma((9,)),
            dma((6,)),
        ],
        compiler_params=pltpu.CompilerParams(vmem_limit_bytes=VMEM_LIMIT),
        cost_estimate=pl.CostEstimate(flops=2 * ROWS * WROWS * D, bytes_accessed=64 << 20, transcendentals=0),
        name="backward",
    )(positions, slots, vecs, meta, *cots, *saved)


WC = 8 * BLK


def weight_kernel(
    pos,
    x_h,
    heads_h,
    act_h,
    d_up_h,
    d_q_h,
    d_k_h,
    d_v_h,
    d_proj_h,
    hid_h,
    d_br_h,
    grads,
    x_c,
    heads,
    act,
    d_up,
    d_q,
    d_k,
    d_v,
    d_proj,
    hid,
    d_br,
    stage,
    i_sem,
    g_sem,
):
    refs = (
        (x_h, x_c),
        (d_q_h, d_q),
        (d_k_h, d_k),
        (d_v_h, d_v),
        (heads_h, heads),
        (d_proj_h, d_proj),
        (hid_h, hid),
        (d_up_h, d_up),
        (d_br_h, d_br),
        (act_h, act),
    )
    fetch = [pltpu.make_async_copy(src, dst, i_sem.at[i]) for i, (src, dst) in enumerate(refs)]
    for copy in fetch:
        copy.start()

    per = WC // BLK

    def g_copy(chunk, j, at):
        return pltpu.make_async_copy(
            stage.at[at, pl.ds(j * BLK, BLK)], grads.at[pos[chunk * per + j]], g_sem.at[at]
        )

    def put(chunk, left, right):
        at = lax.rem(chunk, 2)

        @pl.when(chunk >= 2)
        def _():
            for j in range(per):
                g_copy(chunk - 2, j, at).wait()

        stage[at] = mm(left, right, TN).astype(BF)
        for j in range(per):
            g_copy(chunk, j, at).start()

    first = 0
    for left, right, needs in (
        (x_c, d_q, (0, 1)),
        (x_c, d_k, (2,)),
        (x_c, d_v, (3,)),
        (heads, d_proj, (4, 5)),
        (d_up, hid, (6, 7)),
        (act, d_br, (8, 9)),
    ):
        for i in needs:
            fetch[i].wait()

        def body(j, left=left, right=right, first=first):
            put(first + j, left[:, pl.ds(pl.multiple_of(j * WC, WC), WC)], right[...])

        loop(left.shape[1] // WC, body)
        first += left.shape[1] // WC
    for chunk in (first - 2, first - 1):
        for j in range(per):
            g_copy(chunk, j, chunk % 2).wait()


def weight_grads_of(total_slots, positions, x_c, saved):
    r_v, w_v = pltpu.VMEM((ROWS, D), BF), pltpu.VMEM((ROWS, FF), BF)
    return pl.pallas_call(
        weight_kernel,
        out_shape=jax.ShapeDtypeStruct((total_slots, BLK, D), BF),
        in_specs=[SMEM] + [ANY] * 10,
        out_specs=ANY,
        scratch_shapes=[r_v, r_v, w_v, w_v]
        + [r_v] * 6
        + [
            pltpu.VMEM((2, WC, D), BF),
            pltpu.SemaphoreType.DMA((10,)),
            pltpu.SemaphoreType.DMA((2,)),
        ],
        compiler_params=pltpu.CompilerParams(vmem_limit_bytes=VMEM_LIMIT),
        cost_estimate=pl.CostEstimate(flops=2 * ROWS * WROWS * D, bytes_accessed=40 << 20, transcendentals=0),
        name="weight_grads",
    )(positions, x_c, *saved)


def local(
    tokens,
    cotangent,
    cluster_order,
    block_owner,
    master_slots,
    moment_one,
    moment_two,
    vector_master,
    vector_moment_one,
    vector_moment_two,
):
    tok_count = lax.axis_size("tok")
    tok_index = lax.axis_index("tok")
    slot_count = master_slots.shape[0]
    cap = tok_count // SD * (max(1, CPS // tok_count) * 3 * CL // (2 * SD))
    total_slots = tok_count * slot_count
    order = cluster_order.reshape(1, ROWS)

    block = jax.ShapeDtypeStruct((SD, cap, D), BF)
    meta_shape = jax.ShapeDtypeStruct((SD, META, D), BF)
    row_block = jax.ShapeDtypeStruct((ROWS, D), BF)
    four_planes = tok_count == 8 and lax.axis_size("rep") == 4
    if four_planes:
        slots_low, x_c, *cots, recv_meta, vecs, b_u, occupancy, positions = gather_all(
            cap, tokens, cotangent, order, master_slots, vector_master, block_owner
        )
        positions = positions.reshape(NBLK)
    else:
        positions = slot_positions(block_owner, slot_count)
        slots_low = lax.all_gather(master_slots.astype(BF), "tok", axis=0, tiled=True)
        vectors = lax.all_gather(vector_master.astype(BF), "tok", axis=0, tiled=True).astype(F32)
        vecs, b_u = vectors[: 8 * D].reshape(8, D), vectors[8 * D :].reshape(1, FF)
        cluster = tok_index // SD * CPS + cluster_order // CL
        target = cluster % tok_count
        chosen = target[None, :] == jnp.arange(tok_count, dtype=jnp.int32)[:, None]
        sent_counts = jnp.sum(chosen.astype(F32), axis=1)
        own_row = (jnp.arange(tok_count, dtype=jnp.int32) == tok_index).astype(F32)
        occupancy = lax.psum(own_row[:, None] * sent_counts[None, :], ("tok", "rep")).astype(jnp.int32)
        send_x, send_c, meta = pl.pallas_call(
            functools.partial(send_kernel, cap),
            out_shape=(block, block, meta_shape),
            in_specs=[VMEM] * 3,
            out_specs=(VMEM,) * 3,
            compiler_params=pltpu.CompilerParams(vmem_limit_bytes=VMEM_LIMIT),
            name="send_rows",
        )(tokens, cotangent, order)
        recv_x, recv_meta = (jnp.stack(swap_blocks(b)) for b in (send_x, meta))
        x_c = pl.pallas_call(
            functools.partial(seat_kernel, cap),
            out_shape=row_block,
            in_specs=[VMEM] * 2,
            out_specs=VMEM,
            compiler_params=pltpu.CompilerParams(vmem_limit_bytes=VMEM_LIMIT),
            name="seat_rows",
        )(recv_x, recv_meta)
        cots = [send_c[k] for k in range(SD)]

    cots = swap_blocks(cots)
    *out_blocks, heads, act, hid, q, k, v, p, slope, n1, n2, rs1, rs2 = forward(
        cap, positions, slots_low, vecs, b_u, x_c, recv_meta
    )
    out_blocks = swap_blocks(out_blocks)
    *ing_blocks, shares, d_up, d_q, d_k, d_v, d_proj, d_br = backward(
        cap, positions, slots_low, vecs, recv_meta, cots, (q, k, v, p, slope, n1, n2, rs1, rs2)
    )
    ing_blocks = swap_blocks(ing_blocks)
    grads = weight_grads_of(
        total_slots, positions, x_c, (heads, act, d_up, d_q, d_k, d_v, d_proj, hid, d_br)
    )
    if four_planes:
        total, vec_owned, output, input_grad, entropy = reduce_all(
            cap, grads, shares, order, out_blocks, ing_blocks, slot_count
        )
    else:
        total = lax.psum(lax.psum_scatter(grads, "tok", scatter_dimension=0, tiled=True), "rep")
        grad_vector = shares[:, 0:9].reshape(-1)
        vec_owned = lax.psum(lax.psum_scatter(grad_vector, "tok", scatter_dimension=0, tiled=True), "rep")
        output, input_grad, entropy = pl.pallas_call(
            functools.partial(return_kernel, cap),
            out_shape=(row_block, row_block, jax.ShapeDtypeStruct((1, ROWS), BF)),
            in_specs=[VMEM] * (2 * SD + 1),
            out_specs=(VMEM,) * 3,
            compiler_params=pltpu.CompilerParams(vmem_limit_bytes=VMEM_LIMIT),
            name="return_rows",
        )(order, *out_blocks, *ing_blocks)

    used = jnp.any(
        positions[None, :] == (tok_index * slot_count + jnp.arange(slot_count, dtype=I32))[:, None], axis=1
    )
    owned_grad = jnp.where(used[:, None, None], total.astype(F32), 0.0)
    first_new, second_new, master_new = adam_update(
        owned_grad, master_slots, moment_one, moment_two, rate_matrix
    )
    vec_first, vec_second, vec_new = adam_update(
        vec_owned, vector_master, vector_moment_one, vector_moment_two, rate_vector
    )
    return (
        output,
        input_grad,
        owned_grad,
        first_new,
        second_new,
        master_new,
        master_new.astype(BF),
        vec_owned,
        vec_first,
        vec_second,
        vec_new,
        vec_new.astype(BF),
        entropy.reshape(-1),
        occupancy,
    )


def solution(mesh):
    placed = (
        P(("rep", "tok"), None),
        P(("rep", "tok"), None),
        P(("rep", "tok")),
        P(),
        P("tok", None, None),
        P("tok", None, None),
        P("tok", None, None),
        P("tok"),
        P("tok"),
        P("tok"),
    )
    return jax.shard_map(
        local,
        mesh=mesh,
        in_specs=placed,
        out_specs=(
            P(("rep", "tok"), None),
            P(("rep", "tok"), None),
            P("tok", None, None),
            P("tok", None, None),
            P("tok", None, None),
            P("tok", None, None),
            P("tok", None, None),
            P("tok"),
            P("tok"),
            P("tok"),
            P("tok"),
            P("tok"),
            P(("rep", "tok")),
            P(),
        ),
        check_vma=False,
    )
```

```python
import functools
import math

import jax
import jax.numpy as jnp
from jax import lax
from jax.experimental import pallas as pl
from jax.experimental.pallas import tpu as pltpu
from jax.sharding import PartitionSpec as P

D = 768
HEADS = 12
HD = 64
FF = 3072
SD = 4
CL = 128
NBLK = 96
STEP = 10
CPS = 32
WROWS = 9216
BLK = 96
ROWS = 1024
PAIRS = HEADS // 2
PW = 2 * HD
TM = 512
PART = 48
META = 16
VMEM_LIMIT = 63 << 20
FC = 768

norm_epsilon = 1e-06
beta_first = 0.9
beta_second = 0.999
adam_epsilon = 1e-08
weight_decay = 0.01
rate_matrix = 0.02
rate_vector = 0.2

BF = jnp.bfloat16
F32 = jnp.float32
I32 = jnp.int32

VMEM = pl.BlockSpec(memory_space=pltpu.VMEM)
SMEM = pl.BlockSpec(memory_space=pltpu.SMEM)
ANY = pl.BlockSpec(memory_space=pl.ANY)

NN = (((1,), (0,)), ((), ()))
NT = (((1,), (1,)), ((), ()))
TN = (((0,), (0,)), ((), ()))


def mm(a, b, dims=NN):
    return lax.dot_general(a, b, dims, preferred_element_type=F32)


def slot_positions(block_owner, slot_count):
    owners = block_owner[:, 0]
    blocks = owners.shape[0]
    shared = owners[:, None] == owners[None, :]
    before = (
        jnp.arange(blocks, dtype=jnp.int32)[None, :] < jnp.arange(blocks, dtype=jnp.int32)[:, None]
    )
    earlier = jnp.sum((shared & before).astype(jnp.int32), axis=1)
    return owners * slot_count + earlier


def adam_update(grad_now, weight_old, first_old, second_old, rate_step):
    first_new = beta_first * first_old + (1.0 - beta_first) * grad_now
    second_new = beta_second * second_old + (1.0 - beta_second) * grad_now * grad_now
    first_hat = first_new / (1.0 - beta_first**STEP)
    second_hat = second_new / (1.0 - beta_second**STEP)
    weight_new = weight_old - rate_step * (
        first_hat / (jnp.sqrt(second_hat) + adam_epsilon) + weight_decay * weight_old
    )
    return (first_new, second_new, weight_new)


def route_slots(order, seat, cap):
    cluster = order // CL
    rel = lax.rem(cluster, SD) ^ seat
    place = (cluster // SD) * CL + lax.rem(order, CL) + 1
    chosen = lax.broadcasted_iota(I32, (8, ROWS), 0) == rel
    chosen_low = jnp.where(chosen, 1.0, 0.0).astype(BF)
    before = lax.broadcasted_iota(I32, (ROWS, ROWS), 0) < lax.broadcasted_iota(I32, (ROWS, ROWS), 1)
    before_low = jnp.where(before, 1.0, 0.0).astype(BF)
    running = mm(chosen_low, before_low)
    rank = jnp.sum(jnp.where(chosen, running, 0.0), axis=0, keepdims=True).astype(I32)
    return rel * cap + rank, place


def slot_matrix(slots, at, cap):
    rows = lax.broadcasted_iota(I32, (cap, ROWS), 0) + at * cap
    return jnp.where(rows == slots, 1.0, 0.0).astype(BF)


def send_kernel(cap, tokens, cotangent, order, send_x, send_c, meta):
    seat = lax.rem(lax.axis_index("tok"), SD)
    slots, place = route_slots(order[...], seat, cap)
    digits = jnp.concatenate([place // CL, lax.rem(place, CL)] + [place * 0] * 6, axis=0).astype(F32).astype(BF)
    for at in range(SD):
        picked = slot_matrix(slots, at, cap)
        send_x[at] = mm(picked, tokens[...]).astype(BF)
        send_c[at] = mm(picked, cotangent[...]).astype(BF)
        coded = mm(digits, picked, NT)
        line = jnp.concatenate([coded[0:1], coded[1:2]], axis=1)
        meta[at] = jnp.broadcast_to(line, (META, D)).astype(BF)


def remote(src, dst, send_sem, recv_sem, tok, rep):
    return pltpu.make_async_remote_copy(
        src_ref=src,
        dst_ref=dst,
        send_sem=send_sem,
        recv_sem=recv_sem,
        device_id={"tok": tok, "rep": rep},
        device_id_type=pl.DeviceIdType.MESH,
    )


def loop(n, body):
    def run(i, c):
        body(i)
        return c

    lax.fori_loop(0, n, run, 0)


class Place:
    def __init__(self):
        self.me = me = lax.axis_index("tok")
        self.z = z = lax.axis_index("rep")
        core, x, y = me % 2, (me // 2) % 2, me // 4
        self.twin = me + 1 - 2 * core
        self.xn = me + 2 - 4 * x
        self.yn = me + 4 - 8 * y
        self.dn = self.xn + 4 - 8 * y
        self.side = z % 2
        self.zp = z + 1 - 2 * self.side

    def twin_of(self, tok):
        return tok + 1 - 2 * (tok % 2)

    def greet(self, peers):
        barrier = pltpu.get_barrier_semaphore()
        for tok, rep in peers:
            pl.semaphore_signal(
                barrier, inc=1, device_id={"tok": tok, "rep": rep}, device_id_type=pl.DeviceIdType.MESH
            )
        return lambda: pl.semaphore_wait(barrier, len(peers))


def seat_matrix(meta, first, rows, cap):
    hi = jnp.concatenate([meta[k, 0:8, 0:cap] for k in range(SD)], axis=1).astype(F32)[0:1]
    lo = jnp.concatenate([meta[k, 0:8, cap : 2 * cap] for k in range(SD)], axis=1).astype(F32)[0:1]
    at = (hi * CL + lo).astype(I32)
    seats = lax.broadcasted_iota(I32, (rows, SD * cap), 0) + (first + 1)
    return jnp.where(seats == at, 1.0, 0.0).astype(BF)


def seat_part(meta, k, cap):
    hi = meta[k, 0:8, 0:cap].astype(F32)[0:1]
    lo = meta[k, 0:8, cap : 2 * cap].astype(F32)[0:1]
    at = (hi * CL + lo).astype(I32)
    seats = lax.broadcasted_iota(I32, (ROWS, cap), 0) + 1
    return jnp.where(seats == at, 1.0, 0.0).astype(BF)


def seat_rows(meta, blocks, cap, to):
    def body(t):
        r0 = pl.multiple_of(t * 256, 256)
        rows = blocks[...].reshape(SD * cap, D)
        to[pl.ds(r0, 256), :] = mm(seat_matrix(meta, r0, 256, cap), rows).astype(BF)

    loop(ROWS // 256, body)


def seat_kernel(cap, blocks, meta, to):
    seat_rows(meta, blocks, cap, to)


def gather_kernel(
    cap,
    count,
    tokens_h,
    cotangent_h,
    order,
    master_h,
    vector,
    owner_of,
    slots,
    x_c,
    cot_0,
    cot_1,
    cot_2,
    cot_3,
    recv_meta,
    vecs,
    b_u,
    occupancy,
    positions,
    tokens,
    cotangent,
    master,
    own,
    send_x,
    send_c,
    meta,
    recv_x,
    got_meta,
    slot_of,
    digits,
    mine,
    by_z,
    by_tok,
    x_s,
    x_r,
    y_s,
    y_r,
    d_s,
    d_r,
    zx_s,
    zx_r,
    zd_s,
    zd_r,
    zy_s,
    zy_r,
    p_s,
    p_r,
    row_s,
    row_r,
    z_s,
    z_r,
    t_s,
    t_r,
    local_s,
):
    at = Place()
    me, z, side = at.me, at.z, at.side
    n_tok, n_rep = 8, 4
    peers = [((me + d) % n_tok, z) for d in range(1, n_tok)] + [(me, (z + d) % n_rep) for d in range(1, n_rep)]
    fetch = [
        pltpu.make_async_copy(src, dst, local_s.at[i])
        for i, (src, dst) in enumerate(((master_h, master), (tokens_h, tokens), (cotangent_h, cotangent)))
    ]
    for copy in fetch:
        copy.start()
    wait_peers = at.greet(peers)
    fetch[0].wait()

    last = count - 1

    def near(j):
        return side * last + (1 - 2 * side) * j

    def far(j):
        return (1 - side) * last - (1 - 2 * side) * j

    few_x, few_d, few_y = 11 * count // 26, 12 * count // 26, 8 * count // 26
    most_x, most_d, most_y = count - few_x, count - few_d, count - few_y

    def piece(owner, s):
        return slots.at[owner * count + s]

    def to_x(s):
        return remote(own.at[s], piece(me, s), x_s.at[s], x_r.at[s], at.xn, z)

    def to_y(s):
        return remote(own.at[s], piece(me, s), y_s.at[s], y_r.at[s], at.yn, z)

    def on_y(s):
        return remote(piece(at.xn, s), piece(at.xn, s), d_s.at[s], d_r.at[s], at.yn, z)

    def x_on_z(s):
        return remote(piece(at.xn, s), piece(at.xn, s), zx_s.at[s], zx_r.at[s], me, at.zp)

    def d_on_z(s):
        return remote(piece(at.dn, s), piece(at.dn, s), zd_s.at[s], zd_r.at[s], me, at.zp)

    def y_on_z(s):
        return remote(piece(at.yn, s), piece(at.yn, s), zy_s.at[s], zy_r.at[s], me, at.zp)

    def x_in(s):
        return remote(own.at[s], piece(at.xn, s), x_s.at[s], x_r.at[s], at.xn, z)

    def y_in(s):
        return remote(own.at[s], piece(at.yn, s), y_s.at[s], y_r.at[s], at.yn, z)

    def d_in(s):
        return remote(own.at[s], piece(at.dn, s), d_s.at[s], d_r.at[s], at.yn, z)

    owners = (me, at.xn, at.yn, at.dn)

    def near_run(q, j0, j1):
        return (q, (1 - side) * j0 + side * (count - j1), j1 - j0)

    def far_run(q, j0, j1):
        return (q, side * j0 + (1 - side) * (count - j1), j1 - j0)

    runs = (
        (0, 0, count),
        near_run(2, 0, few_y),
        near_run(1, 0, most_x),
        near_run(3, 0, most_d),
        far_run(1, 0, few_x),
        near_run(2, few_y, most_y),
        far_run(2, 0, few_y),
        far_run(3, 0, few_d // 2),
        far_run(3, few_d // 2, few_d - 2),
        far_run(3, few_d - 2, few_d),
    )

    def to_twin(i):
        q, s, n = runs[i]
        src = own if q == 0 else slots.at[pl.ds(owners[q] * count + s, n)]
        dst = slots.at[pl.ds(owners[q] * count + s, n)]
        return remote(src, dst, p_s.at[i], p_r.at[i], at.twin, z)

    def cast(j):
        own[near(j)] = master[near(j)].astype(BF)

    loop(most_x, cast)
    wait_peers()
    loop(most_x, lambda j: to_x(near(j)).start())
    loop(few_y, lambda j: to_y(near(j)).start())
    loop(count - most_x, lambda j: cast(most_x + j))
    to_twin(0).start()
    keep = pltpu.make_async_copy(own, slots.at[pl.ds(me * count, count)], local_s.at[3])
    keep.start()

    seat = me % SD
    seats = (me, at.twin, at.xn, at.twin_of(at.xn))
    rows_of = ((meta, got_meta), (send_x, recv_x))

    def row_copy(i, k):
        src, dst = rows_of[i]
        return remote(src.at[k], dst.at[k], row_s.at[i, k], row_r.at[i, k], seats[k], z)

    put_c = [
        pltpu.make_async_copy(send_c.at[k], to, local_s.at[4 + k])
        for k, to in enumerate((cot_0, cot_1, cot_2, cot_3))
    ]

    def route():
        fetch[1].wait()
        fetch[2].wait()
        slots_here, place = route_slots(order[...], seat, cap)
        slot_of[...] = slots_here
        digits[...] = (
            jnp.concatenate([place // CL, lax.rem(place, CL)] + [place * 0] * 6, axis=0).astype(F32).astype(BF)
        )

    def sort_tokens(k):
        picked = slot_matrix(slot_of[...], k, cap)
        send_x[k] = mm(picked, tokens[...]).astype(BF)
        coded = mm(digits[...], picked, NT)
        line = jnp.concatenate([coded[0:1], coded[1:2]], axis=1)
        meta[k] = jnp.broadcast_to(line, (META, D)).astype(BF)
        for i in range(2):
            if k:
                row_copy(i, k).start()
            else:
                src, dst = rows_of[i]
                dst[0] = src[0]

    def sort_cotangent(k):
        send_c[k] = mm(slot_matrix(slot_of[...], k, cap), cotangent[...]).astype(BF)
        put_c[k].start()

    def z_copy(d):
        return remote(by_z.at[0], by_z.at[d], z_s.at[d], z_r.at[d], me, (z + d) % n_rep)

    def t_copy(d):
        return remote(mine, by_tok.at[d], t_s.at[d], t_r.at[d], (me + d) % n_tok, z)

    def count_rows():
        residue = lax.rem(me // SD * CPS + order[...] // CL, n_tok)
        hit = lax.broadcasted_iota(I32, (128, ROWS), 0) == residue
        by_z[0] = mm(jnp.ones((8, ROWS), BF), jnp.where(hit, 1.0, 0.0).astype(BF), NT)
        for d in range(1, n_rep):
            z_copy(d).start()
        for i in range(9):
            mine[i : i + 1] = vector[i * 128 : (i + 1) * 128].reshape(1, 128).astype(BF).astype(F32)
        block_row = lax.broadcasted_iota(I32, (NBLK, NBLK), 0)
        block_col = lax.broadcasted_iota(I32, (NBLK, NBLK), 1)
        by_col = owner_of[...].astype(F32)
        by_row = lane_sum(jnp.where(block_row == block_col, by_col, 0.0))
        earlier = jnp.where((by_row == by_col) & (block_row < block_col), 1.0, 0.0)
        positions[...] = (by_col * (count * PART // BLK) + jnp.sum(earlier, axis=0, keepdims=True)).astype(I32)

    def share_vectors():
        for d in range(1, n_rep):
            z_copy(d).wait()
        mine[16:24] = by_z[0] + by_z[1] + by_z[2] + by_z[3]
        for d in range(1, n_tok):
            t_copy(d).start()

    def lay_out_vectors():
        by_tok[0] = mine[...]
        for d in range(1, n_tok):
            t_copy(d).wait()
        for owner in range(n_tok):
            share = by_tok[(me + n_tok - owner) % n_tok]
            occupancy[owner : owner + 1, :] = share[16:17, 0:n_tok].astype(I32)
            for i in range(9):
                chunk = owner * 9 + i
                row, lane = chunk // 6, chunk % 6 * 128
                if row < 8:
                    vecs[row : row + 1, lane : lane + 128] = share[i : i + 1]
                else:
                    lane += (row - 8) * D
                    b_u[:, lane : lane + 128] = share[i : i + 1]

    between = {
        1: lambda: (route(), sort_tokens(2)),
        3: lambda: sort_tokens(3),
        5: lambda: sort_tokens(1),
        7: lambda: (sort_tokens(0), count_rows()),
        9: lambda: sort_cotangent(1),
        11: lambda: sort_cotangent(2),
        13: lambda: sort_cotangent(3),
    }
    for j in range(most_x):
        x_in(near(j)).wait_recv()
        if j < most_d:
            on_y(near(j)).start()
        if j < few_x:
            x_on_z(near(j)).start()
        if j < few_y:
            y_in(near(j)).wait_recv()
            y_on_z(near(j)).start()
        if j == few_y:
            to_twin(1).start()
        if j in between:
            between[j]()
    to_twin(2).start()
    loop(most_y - few_y, lambda j: to_y(near(few_y + j)).start())
    share_vectors()
    sort_cotangent(0)

    def diagonal(j):
        d_in(near(j)).wait_recv()
        d_on_z(near(j)).start()

    loop(few_d, diagonal)
    loop(most_d - few_d, lambda j: d_in(near(few_d + j)).wait_recv())
    to_twin(3).start()
    loop(few_x, lambda j: x_on_z(far(j)).wait_recv())
    to_twin(4).start()
    lay_out_vectors()
    loop(most_y - few_y, lambda j: y_in(near(few_y + j)).wait_recv())
    to_twin(5).start()
    loop(few_y, lambda j: y_on_z(far(j)).wait_recv())
    to_twin(6).start()
    for i in (0, 1):
        for k in (2, 3, 1):
            row_copy(i, k).wait_recv()
    recv_meta[...] = got_meta[...]
    seat_rows(got_meta, recv_x, cap, x_c)
    done = 0
    for i, upto in ((7, few_d // 2), (8, few_d - 2), (9, few_d)):
        loop(upto - done, lambda j, done=done: d_on_z(far(done + j)).wait_recv())
        to_twin(i).start()
        done = upto

    for i in range(2):
        for k in (2, 3, 1):
            row_copy(i, k).wait_send()
    for copy in put_c:
        copy.wait()
    keep.wait()

    loop(most_x, lambda j: to_x(near(j)).wait_send())
    loop(most_y, lambda j: to_y(near(j)).wait_send())
    loop(most_d, lambda j: on_y(near(j)).wait_send())
    loop(few_x, lambda j: x_on_z(near(j)).wait_send())
    loop(few_d, lambda j: d_on_z(near(j)).wait_send())
    loop(few_y, lambda j: y_on_z(near(j)).wait_send())
    for i in range(len(runs)):
        to_twin(i).wait()


def gather_all(cap, tokens, cotangent, order, master, vector, block_owner):
    count = master.shape[0] * BLK // PART
    rows = jax.ShapeDtypeStruct((ROWS, D), BF)
    part = jax.ShapeDtypeStruct((cap, D), BF)
    dma = pltpu.SemaphoreType.DMA
    block = pltpu.VMEM((SD, cap, D), BF)
    meta = pltpu.VMEM((SD, META, D), BF)
    return pl.pallas_call(
        functools.partial(gather_kernel, cap, count),
        out_shape=(
            jax.ShapeDtypeStruct((8 * count, PART, D), BF),
            rows,
            part,
            part,
            part,
            part,
            jax.ShapeDtypeStruct((SD, META, D), BF),
            jax.ShapeDtypeStruct((8, D), F32),
            jax.ShapeDtypeStruct((1, FF), F32),
            jax.ShapeDtypeStruct((8, 8), I32),
            jax.ShapeDtypeStruct((1, NBLK), I32),
        ),
        in_specs=[ANY, ANY, VMEM, ANY, VMEM, VMEM],
        out_specs=(ANY, VMEM) + (ANY,) * SD + (VMEM,) * 5,
        scratch_shapes=[
            pltpu.VMEM((ROWS, D), BF),
            pltpu.VMEM((ROWS, D), BF),
            pltpu.VMEM((count, PART, D), F32),
            pltpu.VMEM((count, PART, D), BF),
            block,
            block,
            meta,
            block,
            meta,
            pltpu.VMEM((1, ROWS), I32),
            pltpu.VMEM((8, ROWS), BF),
            pltpu.VMEM((24, 128), F32),
            pltpu.VMEM((4, 8, 128), F32),
            pltpu.VMEM((8, 24, 128), F32),
        ]
        + [dma((count,))] * 12
        + [dma((10,))] * 2
        + [dma((2, SD))] * 2
        + [dma((4,))] * 2
        + [dma((8,))] * 2
        + [dma((8,))],
        compiler_params=pltpu.CompilerParams(collective_id=0, has_side_effects=True, vmem_limit_bytes=VMEM_LIMIT),
        cost_estimate=pl.CostEstimate(flops=8 * ROWS * ROWS * D, bytes_accessed=64 << 20, transcendentals=0),
        name="gather",
    )(tokens, cotangent, order, master.reshape(count, PART, D), vector, block_owner.reshape(1, NBLK))


def return_kernel(cap, order, *refs):
    outs, ings, (out, ing, entropy) = refs[:SD], refs[SD : 2 * SD], refs[2 * SD :]
    seat = lax.rem(lax.axis_index("tok"), SD)
    slots, _ = route_slots(order[...], seat, cap)
    picked = jnp.concatenate([slot_matrix(slots, at, cap) for at in range(SD)], axis=0)
    for to, blocks in ((out, outs), (ing, ings)):
        rows = jnp.concatenate([block[0:cap, :] for block in blocks], axis=0)
        to[...] = mm(picked, rows, TN).astype(BF)
    line = jnp.concatenate([block[cap : cap + 8, 0:cap] for block in outs], axis=1)
    entropy[...] = mm(line, picked)[0:1].astype(BF)


def swap_blocks(blocks):
    n = lax.axis_size("tok")
    parts = [blocks[0]]
    for k in range(1, SD):
        parts.append(lax.ppermute(blocks[k], "tok", [(i, i ^ k) for i in range(n)]))
    return parts


def reduce_kernel(
    cap,
    count,
    split,
    grads,
    vec,
    order,
    out_0,
    out_1,
    out_2,
    out_3,
    ing_0,
    ing_1,
    ing_2,
    ing_3,
    total,
    vec_out,
    output,
    input_grad,
    entropy,
    out_v,
    ing_v,
    slot_of,
    a,
    tw,
    rd,
    rx,
    ry,
    o,
    rz1,
    pz,
    rz2,
    fz,
    vt,
    va,
    vb,
    vc,
    a_l,
    keep_l,
    p_s,
    p_r,
    d_s,
    d_r,
    x_s,
    x_r,
    y_s,
    y_r,
    z1_s,
    z1_r,
    z2_s,
    z2_r,
    z3_s,
    z3_r,
    t_s,
    t_r,
    v_s,
    v_r,
    row_l,
):
    at = Place()
    me, z = at.me, at.z
    n_tok, n_rep = 8, 4
    peers = [((me + d) % n_tok, z) for d in range(1, n_tok)] + [(me, (z + d) % n_rep) for d in range(1, n_rep)]
    wait_peers = at.greet(peers)
    owners = (me, at.xn, at.yn, at.dn)

    def load(q):
        return pltpu.make_async_copy(grads.at[pl.ds(owners[q] * count, count)], a.at[q], a_l.at[q])

    for q in (3, 1, 2, 0):
        load(q).start()
    rows_in = [
        pltpu.make_async_copy(src, to.at[k], row_l.at[i, k])
        for i, (blocks, to) in enumerate((((out_0, out_1, out_2, out_3), out_v), ((ing_0, ing_1, ing_2, ing_3), ing_v)))
        for k, src in enumerate(blocks)
    ]
    for copy in rows_in:
        copy.start()
    wait_peers()

    groups = [(g, g * (count // 4), count // 4 if g < 3 else count - 3 * (count // 4)) for g in range(4)]

    def to_twin(q, group):
        g, s, n = group
        src = grads.at[pl.ds(at.twin_of(owners[q]) * count + s, n)]
        return remote(src, tw.at[q, pl.ds(s, n)], p_s.at[q, g], p_r.at[q, g], at.twin, z)

    def d_y(s):
        return remote(a.at[3, s], rd.at[s], d_s.at[s], d_r.at[s], at.yn, z)

    def d_x(s):
        return remote(a.at[3, s], rd.at[s], d_s.at[s], d_r.at[s], at.xn, z)

    def to_x(s):
        return remote(a.at[1, s], rx.at[s], x_s.at[s], x_r.at[s], at.xn, z)

    def to_y(s):
        return remote(a.at[2, s], ry.at[s], y_s.at[s], y_r.at[s], at.yn, z)

    def z_in(s):
        return remote(o.at[s], rz1.at[s], z1_s.at[s], z1_r.at[s], me, at.zp)

    def z_swap(s):
        return remote(pz.at[s], rz2.at[s], z2_s.at[s], z2_r.at[s], me, n_rep - 1 - z)

    def z_out(s):
        return remote(fz.at[s], fz.at[s], z3_s.at[s], z3_r.at[s], me, at.zp)

    def keep(s):
        return pltpu.make_async_copy(fz.at[s], total.at[s], keep_l.at[s])

    for group in groups:
        for q in (3, 1, 2, 0):
            to_twin(q, group).start()

    def v_tok(d):
        return remote(vec.at[(me + d) % n_tok], vt.at[d], t_s.at[d], t_r.at[d], (me + d) % n_tok, z)

    def v_rep(i, src):
        return remote(src, vb.at[i], v_s.at[i], v_r.at[i], me, at.zp if i == 0 else (z + 2) % n_rep)

    for d in range(1, n_tok):
        v_tok(d).start()

    def join(q, s):
        return a[q, s] + tw[q, s]

    def first(s, send):
        a[3, s] = join(3, s)
        send(s).start()

    def plain(q, s, send):
        a[q, s] = join(q, s)
        send(s).start()

    def joined(q, s, arrived, send):
        arrived(s).wait_recv()
        a[q, s] = join(q, s) + rd[s]
        send(s).start()

    inner = (z == 1) | (z == 2)
    outer = (z == 0) | (z == 3)

    def own(s):
        to_x(s).wait_recv()
        to_y(s).wait_recv()
        o[s] = join(0, s) + (rx[s] + ry[s])
        pl.when(outer)(lambda: z_in(s).start())

    def middle(s):
        @pl.when(inner)
        def _():
            z_in(s).wait_recv()
            pz[s] = o[s] + rz1[s]
            z_swap(s).start()

    def last(s):
        @pl.when(inner)
        def _():
            z_swap(s).wait_recv()
            fz[s] = pz[s] + rz2[s]
            z_out(s).start()
            keep(s).start()

    def taken(s):
        @pl.when(outer)
        def _():
            z_out(s).wait_recv()
            keep(s).start()

    def pick_rows(i):
        ts = pl.ds(pl.multiple_of(i * 256, 256), 256)
        hit = lax.broadcasted_iota(I32, (SD * cap, 256), 0) == slot_of[:, ts]
        picked = jnp.where(hit, 1.0, 0.0).astype(BF)
        outs = jnp.concatenate([out_v[k, 0:cap, :] for k in range(SD)], axis=0)
        ings = jnp.concatenate([ing_v[k] for k in range(SD)], axis=0)
        both = mm(picked, jnp.concatenate([outs, ings], axis=1), TN)
        output[ts, :] = both[:, 0:D].astype(BF)
        input_grad[ts, :] = both[:, D:].astype(BF)
        line = jnp.concatenate([out_v[k, cap : cap + 8, 0:cap] for k in range(SD)], axis=1)
        entropy[:, ts] = mm(line, picked)[0:1].astype(BF)

    for q in (3, 1, 2, 0):
        load(q).wait()

    def steps(i, lag, more):
        s = i - lag
        by_x = (s % 2 == 0) & (s < 2 * split)
        live = (s >= 0) & (s < count)
        pl.when(live & by_x)(lambda: more(s, True))
        pl.when(live & jnp.logical_not(by_x))(lambda: more(s, False))

    def steps_of(i, lag, more):
        pl.when((i >= lag) & (i < count + lag))(lambda: more(i - lag))

    def round_of(i):
        for group in groups:

            @pl.when(i == group[1])
            def _(group=group):
                to_twin(3, group).wait_recv()

            @pl.when(i == group[1] + 1)
            def _(group=group):
                to_twin(1, group).wait_recv()
                to_twin(2, group).wait_recv()

            @pl.when(i == group[1] + 6)
            def _(group=group):
                to_twin(0, group).wait_recv()

        steps(i, 0, lambda s, by_x: first(s, d_x if by_x else d_y))
        steps(i, 1, lambda s, by_x: plain(1, s, to_x) if by_x else plain(2, s, to_y))
        steps(i, 3, lambda s, by_x: joined(2, s, d_x, to_y) if by_x else joined(1, s, d_y, to_x))
        steps_of(i, 6, own)
        steps_of(i, 8, middle)
        steps_of(i, 10, last)
        steps_of(i, 12, taken)

    loop(3, round_of)
    for copy in rows_in:
        copy.wait()
    slots_here, _ = route_slots(order[...], me % SD, cap)
    slot_of[...] = slots_here

    v_sum = vec[me]
    for d in range(1, n_tok):
        v_tok(d).wait()
        v_sum = v_sum + vt[d]
    va[...] = v_sum
    v_rep(0, va).start()

    def four_rounds(i):
        loop(4, lambda j: round_of(3 + 4 * i + j))
        pick_rows(i)

    four_rounds(0)
    v_rep(0, va).wait()
    vc[...] = va[...] + vb[0]
    v_rep(1, vc).start()
    loop(3, lambda i: four_rounds(1 + i))
    loop(count + 12 - 19, lambda i: round_of(19 + i))
    v_rep(1, vc).wait()
    vec_out[...] = vc[...] + vb[1]

    for group in groups:
        for q in range(4):
            to_twin(q, group).wait_send()

    def sent(s):
        d_y(s).wait_send()
        to_x(s).wait_send()
        to_y(s).wait_send()
        keep(s).wait()

    loop(count, sent)

    @pl.when(outer)
    def _():
        loop(count, lambda s: z_in(s).wait_send())

    @pl.when(inner)
    def _():
        def back(s):
            z_swap(s).wait_send()
            z_out(s).wait_send()

        loop(count, back)


def reduce_all(cap, grads, shares, order, outs, ings, count):
    dma = pltpu.SemaphoreType.DMA
    count = count * BLK // PART
    part = pltpu.VMEM((count, PART, D), BF)
    whole = pltpu.VMEM((4, count, PART, D), BF)
    line = pltpu.VMEM((16, 128), F32)
    rows = jax.ShapeDtypeStruct((ROWS, D), BF)
    total, vec, output, input_grad, entropy = pl.pallas_call(
        functools.partial(reduce_kernel, cap, count, count // 2),
        out_shape=(
            jax.ShapeDtypeStruct((count, PART, D), BF),
            jax.ShapeDtypeStruct((16, 128), F32),
            rows,
            rows,
            jax.ShapeDtypeStruct((1, ROWS), BF),
        ),
        in_specs=[ANY, VMEM, VMEM] + [ANY] * (2 * SD),
        out_specs=(ANY,) + (VMEM,) * 4,
        scratch_shapes=[
            pltpu.VMEM((SD, cap + META, D), BF),
            pltpu.VMEM((SD, cap, D), BF),
            pltpu.VMEM((1, ROWS), I32),
            whole,
            whole,
        ]
        + [part] * 8
        + [pltpu.VMEM((8, 16, 128), F32), line, pltpu.VMEM((2, 16, 128), F32), line]
        + [dma((4,)), dma((count,))]
        + [dma((4, 4))] * 2
        + [dma((count,))] * 12
        + [dma((8,))] * 2
        + [dma((2,))] * 2
        + [dma((2, SD))],
        compiler_params=pltpu.CompilerParams(collective_id=1, has_side_effects=True, vmem_limit_bytes=VMEM_LIMIT),
        cost_estimate=pl.CostEstimate(flops=4 * ROWS * ROWS * D, bytes_accessed=64 << 20, transcendentals=0),
        name="reduce",
    )(grads.reshape(-1, PART, D), shares, order, *outs, *ings)
    return total.reshape(-1, BLK, D), vec[0:9].reshape(-1), output, input_grad, entropy


V_BQ, V_BV, V_BO, V_BD, V_G1, V_C1, V_G2, V_C2 = range(8)


def inverse(x):
    r = pl.reciprocal(x, approx=True)
    return r * (2.0 - x * r)


def erf_parts(v):
    t = inverse(1.0 + (0.3275911 / math.sqrt(2.0)) * jnp.abs(v))
    e = jnp.exp2((v * v) * (-0.5 / math.log(2.0)))
    poly = 0.5 * 1.061405429
    for c in (-1.453152027, 1.421413741, -0.284496736, 0.254829592):
        poly = poly * t + 0.5 * c
    tail = poly * (t * e)
    return jnp.where(v >= 0.0, 1.0 - tail, tail), e


def lane_sum(x):
    return jnp.sum(x, axis=1, keepdims=True)


def gelu_parts(v):
    phi, e = erf_parts(v)
    return v * phi, phi + v * (e * (1.0 / math.sqrt(2.0 * math.pi)))


def weight_copies(pos, slots, w, sem, first):
    def copy(b):
        return pltpu.make_async_copy(slots.at[pos[first + b]], w.at[pl.ds(b * BLK, BLK)], sem)

    n = w.shape[0] // BLK
    return (lambda: loop(n, lambda b: copy(b).start())), (lambda: loop(n, lambda b: copy(b).wait()))


def halves_of_heads():
    lane = lax.broadcasted_iota(I32, (1, PW), 1)
    m0 = jnp.where(lane < HD, 1.0, 0.0).astype(BF)
    m1 = jnp.where(lane < HD, 0.0, 1.0).astype(BF)
    return lambda pair: jnp.concatenate([pair * m0, pair * m1], axis=0)


def tile_rows(t):
    return pl.ds(pl.multiple_of(t * TM, TM), TM)


def forward_kernel(
    cap,
    pos,
    slots,
    vecs,
    b_u,
    x_h,
    meta,
    back_0,
    back_1,
    back_2,
    back_3,
    heads_h,
    act_h,
    hid_h,
    q_h,
    k_h,
    v_h,
    p_h,
    slope_h,
    n1_h,
    n2_h,
    rs1_h,
    rs2_h,
    wqkv,
    wo,
    wu,
    wd,
    x_c,
    heads,
    act,
    hid,
    q,
    k,
    v,
    p_all,
    slope,
    n1,
    n2,
    rs1,
    rs2,
    out_c,
    ent,
    hid_t,
    w_sem,
    x_sem,
    o_sem,
):
    inv = 1.0 / math.sqrt(HD)
    get_x = pltpu.make_async_copy(x_h, x_c, x_sem)
    get_x.start()
    weights = [
        weight_copies(pos, slots, w, w_sem.at[i], first)
        for i, (w, first) in enumerate(((wqkv, 0), (wo, 24), (wu, 32), (wd, 64)))
    ]
    for start, _ in weights:
        start()
    get_x.wait()
    apart = halves_of_heads()

    def vec(i):
        return vecs[i : i + 1, :]

    saved = (
        (heads, heads_h),
        (act, act_h),
        (hid, hid_h),
        (q, q_h),
        (k, k_h),
        (v, v_h),
        (slope, slope_h),
        (n1, n1_h),
        (n2, n2_h),
        (rs1, rs1_h),
        (rs2, rs2_h),
    )

    def save(t, i):
        src, dst = saved[i]
        return pltpu.make_async_copy(src.at[tile_rows(t)], dst.at[tile_rows(t)], o_sem.at[i])

    def save_p(t):
        n = TM // CL
        cs = pl.ds(t * n, n)
        return pltpu.make_async_copy(p_all.at[cs], p_h.at[cs], o_sem.at[len(saved)])

    def normal(r, n, rs, rows):
        c = r - lane_sum(r) * (1.0 / D)
        scale = lax.rsqrt(lane_sum(c * c) * (1.0 / D) + norm_epsilon)
        rs[rows, :] = jnp.broadcast_to(scale, (TM, 128))
        n[rows, :] = c * scale

    def tile(t):
        rows = tile_rows(t)
        first = t == 0
        pl.when(first)(weights[0][1])
        x = x_c[rows, :]
        q[rows, :] = ((mm(x, wqkv[0:D, :]) + vec(V_BQ)).astype(BF).astype(F32) * inv).astype(BF)
        k[rows, :] = mm(x, wqkv[D : 2 * D, :]).astype(BF)
        v[rows, :] = (mm(x, wqkv[2 * D :, :]) + vec(V_BV)).astype(BF)

        def attend(c):
            gr = pl.ds(pl.multiple_of(t * TM + c * CL, CL), CL)
            total = jnp.zeros((1, CL), F32)
            for p in range(PAIRS):
                ps = slice(p * PW, (p + 1) * PW)
                scores = mm(apart(k[gr, ps]), q[gr, ps], NT)
                halves = []
                for h in range(2):
                    sh = scores[h * CL : (h + 1) * CL]
                    sh = sh - jnp.max(sh, axis=0, keepdims=True)
                    e = jnp.exp(sh)
                    tot = jnp.sum(e, axis=0, keepdims=True)
                    r = 1.0 / tot
                    total += jnp.log(tot) - jnp.sum(e * sh, axis=0, keepdims=True) * r
                    halves.append((e * r).astype(BF))
                probs = jnp.concatenate(halves, axis=0)
                p_all[t * (TM // CL) + c, p] = probs
                heads[gr, ps] = mm(probs, apart(v[gr, ps]), TN).astype(BF)
            ent[:, gr] = jnp.broadcast_to(total * (1.0 / HEADS), (8, CL))

        loop(TM // CL, attend)
        for i in (0, 3, 4, 5):
            save(t, i).start()
        save_p(t).start()
        pl.when(first)(weights[1][1])
        normal(x_c[rows, :].astype(F32) + mm(heads[rows, :], wo[...]) + vec(V_BO), n1, rs1, rows)
        hidden = n1[rows, :] * vec(V_G1) + vec(V_C1)
        hid[rows, :] = hidden.astype(BF)
        hid_t[...] = hidden
        pl.when(first)(weights[2][1])

        def widen(f):
            fs = pl.ds(pl.multiple_of(f * FC, FC), FC)
            g, g_slope = gelu_parts(mm(hid[rows, :], wu[fs, :], NT) + b_u[:, fs])
            act[rows, fs] = g.astype(BF)
            slope[rows, fs] = g_slope.astype(BF)

        loop(FF // FC, widen)
        for i in (1, 2, 6, 7, 9):
            save(t, i).start()
        pl.when(first)(weights[3][1])
        normal(hid_t[...] + mm(act[rows, :], wd[...]) + vec(V_BD), n2, rs2, rows)
        out_c[rows, :] = (n2[rows, :] * vec(V_G2) + vec(V_C2)).astype(BF)
        for i in (8, 10):
            save(t, i).start()

    loop(ROWS // TM, tile)

    for j, back in enumerate((back_0, back_1, back_2, back_3)):
        own = seat_part(meta, j, cap)
        back[0:cap, :] = mm(own, out_c[...], TN).astype(BF)
        line = mm(ent[...].astype(BF), own)
        back[cap:, :] = jnp.concatenate([line, line], axis=1)[0:1].astype(BF) * jnp.ones((META, 1), BF)

    def saved_all(t):
        for i in range(len(saved)):
            save(t, i).wait()
        save_p(t).wait()

    loop(ROWS // TM, saved_all)


def shape_of(kind, *shape):
    return jax.ShapeDtypeStruct(shape, kind)


def saved_shapes():
    rows, wide = ((ROWS, D), BF), ((ROWS, FF), BF)
    probs = ((ROWS // CL, PAIRS, 2 * CL, CL), BF)
    full, thin = ((ROWS, D), F32), ((ROWS, 128), F32)
    return rows, wide, probs, full, thin


def forward(cap, positions, slots, vecs, b_u, x_c, meta):
    rows, wide, probs, full, thin = saved_shapes()
    kept = (rows, wide, rows, rows, rows, rows, probs, wide, full, full, thin, thin)
    dma = pltpu.SemaphoreType.DMA
    return pl.pallas_call(
        functools.partial(forward_kernel, cap),
        out_shape=(shape_of(BF, cap + META, D),) * SD + tuple(shape_of(kind, *shape) for shape, kind in kept),
        in_specs=[SMEM, ANY, VMEM, VMEM, ANY, VMEM],
        out_specs=(VMEM,) * SD + (ANY,) * len(kept),
        scratch_shapes=[
            pltpu.VMEM((3 * D, D), BF),
            pltpu.VMEM((D, D), BF),
            pltpu.VMEM((FF, D), BF),
            pltpu.VMEM((FF, D), BF),
            pltpu.VMEM(*rows),
        ]
        + [pltpu.VMEM(*a) for a in kept]
        + [
            pltpu.VMEM(*rows),
            pltpu.VMEM((8, ROWS), F32),
            pltpu.VMEM((TM, D), F32),
            dma((4,)),
            dma,
            dma((12,)),
        ],
        compiler_params=pltpu.CompilerParams(vmem_limit_bytes=VMEM_LIMIT),
        cost_estimate=pl.CostEstimate(flops=2 * ROWS * WROWS * D, bytes_accessed=64 << 20, transcendentals=0),
        name="forward",
    )(positions, slots, vecs, b_u, x_c, meta)


def backward_kernel(
    cap,
    pos,
    slots,
    vecs,
    meta,
    cot_0,
    cot_1,
    cot_2,
    cot_3,
    q_h,
    k_h,
    v_h,
    p_h,
    slope_h,
    n1_h,
    n2_h,
    rs1_h,
    rs2_h,
    back_0,
    back_1,
    back_2,
    back_3,
    shares,
    d_up_h,
    d_q_h,
    d_k_h,
    d_v_h,
    d_proj_h,
    d_br_h,
    wqkv,
    wo,
    wu,
    wd,
    blocks,
    q,
    k,
    v,
    p_all,
    d_up,
    n1,
    n2,
    rs1,
    rs2,
    d_proj,
    d_br,
    ing_c,
    d_h_t,
    res_t,
    gvec,
    g_bu,
    w_sem,
    c_sem,
    i_sem,
    o_sem,
):
    inv = 1.0 / math.sqrt(HD)
    get_c = [
        pltpu.make_async_copy(cot, blocks.at[j], c_sem.at[j]) for j, cot in enumerate((cot_0, cot_1, cot_2, cot_3))
    ]
    for copy in get_c:
        copy.start()
    fetch = [
        pltpu.make_async_copy(src, dst, i_sem.at[i])
        for i, (src, dst) in enumerate(
            (
                (n2_h, n2),
                (rs2_h, rs2),
                (slope_h, d_up),
                (n1_h, n1),
                (rs1_h, rs1),
                (v_h, v),
                (p_h, p_all),
                (k_h, k),
                (q_h, q),
            )
        )
    ]
    weights = [
        weight_copies(pos, slots, w, w_sem.at[i], first)
        for i, (w, first) in enumerate(((wd, 64), (wu, 32), (wo, 24), (wqkv, 0)))
    ]
    fetch[0].start()
    fetch[1].start()
    weights[0][0]()
    fetch[2].start()
    weights[1][0]()
    fetch[3].start()
    fetch[4].start()
    weights[2][0]()
    for i in range(5, 9):
        fetch[i].start()
    weights[3][0]()
    gvec[...] = jnp.zeros_like(gvec)
    g_bu[...] = jnp.zeros_like(g_bu)
    shares[...] = jnp.zeros_like(shares)
    for copy in get_c:
        copy.wait()
    seat_rows(meta, blocks, cap, d_br)
    apart = halves_of_heads()
    first_half = lax.broadcasted_iota(I32, (CL, PW), 1) < HD

    def vec(i):
        return vecs[i : i + 1, :]

    def add_vec(i, value):
        gvec[i : i + 1, :] += jnp.sum(value, axis=0, keepdims=True)

    saved = ((d_up, d_up_h), (q, d_q_h), (k, d_k_h), (v, d_v_h), (d_proj, d_proj_h), (d_br, d_br_h))

    def save(t, i):
        src, dst = saved[i]
        return pltpu.make_async_copy(src.at[tile_rows(t)], dst.at[tile_rows(t)], o_sem.at[i])

    def norm_back(e, n, rs, gain, shift):
        add_vec(gain, e * n)
        add_vec(shift, e)
        eg = e * vec(gain)
        return rs * (eg - lane_sum(eg) * (1.0 / D) - n * (lane_sum(eg * n) * (1.0 / D)))

    def tile(t):
        rows = tile_rows(t)
        start = t == 0

        @pl.when(start)
        def _():
            fetch[0].wait()
            fetch[1].wait()

        d_r2 = norm_back(d_br[rows, :].astype(F32), n2[rows, :], rs2[rows, 0:1], V_G2, V_C2)
        d_br[rows, :] = d_r2.astype(BF)
        add_vec(V_BD, d_br[rows, :].astype(F32))
        res_t[...] = d_r2

        @pl.when(start)
        def _():
            weights[0][1]()
            fetch[2].wait()

        def widen_back(f):
            fs = pl.ds(pl.multiple_of(f * FC, FC), FC)
            du = (mm(d_br[rows, :], wd[fs, :], NT) * d_up[rows, fs].astype(F32)).astype(BF)
            d_up[rows, fs] = du
            g_bu[:, fs] += jnp.sum(du.astype(F32), axis=0, keepdims=True)

        loop(FF // FC, widen_back)
        for i in (0, 5):
            save(t, i).start()

        @pl.when(start)
        def _():
            weights[1][1]()
            fetch[3].wait()
            fetch[4].wait()

        d_h = res_t[...] + mm(d_up[rows, :], wu[...])
        d_r1 = norm_back(d_h, n1[rows, :], rs1[rows, 0:1], V_G1, V_C1)
        d_proj[rows, :] = d_r1.astype(BF)
        res_t[...] = d_r1
        add_vec(V_BO, d_proj[rows, :].astype(F32))
        save(t, 4).start()

        @pl.when(start)
        def _():
            weights[2][1]()
            for i in range(5, 9):
                fetch[i].wait()

        d_h_t[...] = mm(d_proj[rows, :], wo[...], NT).astype(BF)

        def attend_back(c):
            cr = pl.ds(pl.multiple_of(c * CL, CL), CL)
            gr = pl.ds(pl.multiple_of(t * TM + c * CL, CL), CL)
            for p in range(PAIRS):
                ps = slice(p * PW, (p + 1) * PW)
                dh, qp, ks = d_h_t[cr, ps], q[gr, ps], apart(k[gr, ps])
                probs = p_all[t * (TM // CL) + c, p]
                d_w = mm(apart(v[gr, ps]), dh, NT)
                halves = []
                for h in range(2):
                    wh = probs[h * CL : (h + 1) * CL].astype(F32)
                    dwh = d_w[h * CL : (h + 1) * CL]
                    halves.append((wh * (dwh - jnp.sum(dwh * wh, axis=0, keepdims=True))).astype(BF))
                d_s = jnp.concatenate(halves, axis=0)
                q[gr, ps] = (mm(d_s, ks, TN) * inv).astype(BF)
                dk = mm(d_s, qp)
                k[gr, ps] = jnp.where(first_half, dk[0:CL], dk[CL:]).astype(BF)
                dv = mm(probs, dh)
                v[gr, ps] = jnp.where(first_half, dv[0:CL], dv[CL:]).astype(BF)

        loop(TM // CL, attend_back)
        for i in (1, 2, 3):
            save(t, i).start()
        add_vec(V_BQ, q[rows, :].astype(F32))
        add_vec(V_BV, v[rows, :].astype(F32))
        pl.when(start)(weights[3][1])
        d_x = (
            mm(q[rows, :], wqkv[0:D, :], NT)
            + mm(k[rows, :], wqkv[D : 2 * D, :], NT)
            + mm(v[rows, :], wqkv[2 * D :, :], NT)
        )
        ing_c[rows, :] = (res_t[...] + d_x.astype(BF).astype(F32)).astype(BF)

    loop(ROWS // TM, tile)

    for j, back in enumerate((back_0, back_1, back_2, back_3)):
        back[...] = mm(seat_part(meta, j, cap), ing_c[...], TN).astype(BF)

    for chunk in range(72):
        row, lane = chunk // 6, chunk % 6 * 128
        if row < 8:
            part = gvec[row : row + 1, lane : lane + 128]
        else:
            lane += (row - 8) * D
            part = g_bu[:, lane : lane + 128]
        shares[chunk // 9, chunk % 9 : chunk % 9 + 1, :] = part

    def saved_all(t):
        for i in range(len(saved)):
            save(t, i).wait()

    loop(ROWS // TM, saved_all)


def backward(cap, positions, slots, vecs, meta, cots, saved):
    rows, wide, probs, full, thin = saved_shapes()
    dma = pltpu.SemaphoreType.DMA
    grads = (wide, rows, rows, rows, rows, rows)
    return pl.pallas_call(
        functools.partial(backward_kernel, cap),
        out_shape=(shape_of(BF, cap, D),) * SD
        + (shape_of(F32, 8, 16, 128),)
        + tuple(shape_of(kind, *shape) for shape, kind in grads),
        in_specs=[SMEM, ANY, VMEM, VMEM] + [ANY] * (SD + 9),
        out_specs=(VMEM,) * (SD + 1) + (ANY,) * len(grads),
        scratch_shapes=[
            pltpu.VMEM((3 * D, D), BF),
            pltpu.VMEM((D, D), BF),
            pltpu.VMEM((FF, D), BF),
            pltpu.VMEM((FF, D), BF),
            pltpu.VMEM((SD, cap, D), BF),
        ]
        + [pltpu.VMEM(*a) for a in (rows, rows, rows, probs, wide, full, full, thin, thin, rows, rows, rows)]
        + [
            pltpu.VMEM((TM, D), BF),
            pltpu.VMEM((TM, D), F32),
            pltpu.VMEM((8, D), F32),
            pltpu.VMEM((1, FF), F32),
            dma((4,)),
            dma((4,)),
            dma((9,)),
            dma((6,)),
        ],
        compiler_params=pltpu.CompilerParams(vmem_limit_bytes=VMEM_LIMIT),
        cost_estimate=pl.CostEstimate(flops=2 * ROWS * WROWS * D, bytes_accessed=64 << 20, transcendentals=0),
        name="backward",
    )(positions, slots, vecs, meta, *cots, *saved)


WC = 8 * BLK


def weight_kernel(
    pos,
    x_h,
    heads_h,
    act_h,
    d_up_h,
    d_q_h,
    d_k_h,
    d_v_h,
    d_proj_h,
    hid_h,
    d_br_h,
    grads,
    x_c,
    heads,
    act,
    d_up,
    d_q,
    d_k,
    d_v,
    d_proj,
    hid,
    d_br,
    stage,
    i_sem,
    g_sem,
):
    refs = (
        (x_h, x_c),
        (d_q_h, d_q),
        (d_k_h, d_k),
        (d_v_h, d_v),
        (heads_h, heads),
        (d_proj_h, d_proj),
        (hid_h, hid),
        (d_up_h, d_up),
        (d_br_h, d_br),
        (act_h, act),
    )
    fetch = [pltpu.make_async_copy(src, dst, i_sem.at[i]) for i, (src, dst) in enumerate(refs)]
    for copy in fetch:
        copy.start()

    per = WC // BLK

    def g_copy(chunk, j, at):
        return pltpu.make_async_copy(
            stage.at[at, pl.ds(j * BLK, BLK)], grads.at[pos[chunk * per + j]], g_sem.at[at]
        )

    def put(chunk, left, right):
        at = lax.rem(chunk, 2)

        @pl.when(chunk >= 2)
        def _():
            for j in range(per):
                g_copy(chunk - 2, j, at).wait()

        stage[at] = mm(left, right, TN).astype(BF)
        for j in range(per):
            g_copy(chunk, j, at).start()

    first = 0
    for left, right, needs in (
        (x_c, d_q, (0, 1)),
        (x_c, d_k, (2,)),
        (x_c, d_v, (3,)),
        (heads, d_proj, (4, 5)),
        (d_up, hid, (6, 7)),
        (act, d_br, (8, 9)),
    ):
        for i in needs:
            fetch[i].wait()

        def body(j, left=left, right=right, first=first):
            put(first + j, left[:, pl.ds(pl.multiple_of(j * WC, WC), WC)], right[...])

        loop(left.shape[1] // WC, body)
        first += left.shape[1] // WC
    for chunk in (first - 2, first - 1):
        for j in range(per):
            g_copy(chunk, j, chunk % 2).wait()


def weight_grads_of(total_slots, positions, x_c, saved):
    r_v, w_v = pltpu.VMEM((ROWS, D), BF), pltpu.VMEM((ROWS, FF), BF)
    return pl.pallas_call(
        weight_kernel,
        out_shape=jax.ShapeDtypeStruct((total_slots, BLK, D), BF),
        in_specs=[SMEM] + [ANY] * 10,
        out_specs=ANY,
        scratch_shapes=[r_v, r_v, w_v, w_v]
        + [r_v] * 6
        + [
            pltpu.VMEM((2, WC, D), BF),
            pltpu.SemaphoreType.DMA((10,)),
            pltpu.SemaphoreType.DMA((2,)),
        ],
        compiler_params=pltpu.CompilerParams(vmem_limit_bytes=VMEM_LIMIT),
        cost_estimate=pl.CostEstimate(flops=2 * ROWS * WROWS * D, bytes_accessed=40 << 20, transcendentals=0),
        name="weight_grads",
    )(positions, x_c, *saved)


def local(
    tokens,
    cotangent,
    cluster_order,
    block_owner,
    master_slots,
    moment_one,
    moment_two,
    vector_master,
    vector_moment_one,
    vector_moment_two,
):
    tok_count = lax.axis_size("tok")
    tok_index = lax.axis_index("tok")
    slot_count = master_slots.shape[0]
    cap = tok_count // SD * (max(1, CPS // tok_count) * 3 * CL // (2 * SD))
    total_slots = tok_count * slot_count
    order = cluster_order.reshape(1, ROWS)

    block = jax.ShapeDtypeStruct((SD, cap, D), BF)
    meta_shape = jax.ShapeDtypeStruct((SD, META, D), BF)
    row_block = jax.ShapeDtypeStruct((ROWS, D), BF)
    four_planes = tok_count == 8 and lax.axis_size("rep") == 4
    if four_planes:
        slots_low, x_c, *cots, recv_meta, vecs, b_u, occupancy, positions = gather_all(
            cap, tokens, cotangent, order, master_slots, vector_master, block_owner
        )
        positions = positions.reshape(NBLK)
        slots_low = slots_low.reshape(total_slots, BLK, D)
    else:
        positions = slot_positions(block_owner, slot_count)
        slots_low = lax.all_gather(master_slots.astype(BF), "tok", axis=0, tiled=True)
        vectors = lax.all_gather(vector_master.astype(BF), "tok", axis=0, tiled=True).astype(F32)
        vecs, b_u = vectors[: 8 * D].reshape(8, D), vectors[8 * D :].reshape(1, FF)
        cluster = tok_index // SD * CPS + cluster_order // CL
        target = cluster % tok_count
        chosen = target[None, :] == jnp.arange(tok_count, dtype=jnp.int32)[:, None]
        sent_counts = jnp.sum(chosen.astype(F32), axis=1)
        own_row = (jnp.arange(tok_count, dtype=jnp.int32) == tok_index).astype(F32)
        occupancy = lax.psum(own_row[:, None] * sent_counts[None, :], ("tok", "rep")).astype(jnp.int32)
        send_x, send_c, meta = pl.pallas_call(
            functools.partial(send_kernel, cap),
            out_shape=(block, block, meta_shape),
            in_specs=[VMEM] * 3,
            out_specs=(VMEM,) * 3,
            compiler_params=pltpu.CompilerParams(vmem_limit_bytes=VMEM_LIMIT),
            name="send_rows",
        )(tokens, cotangent, order)
        recv_x, recv_meta = (jnp.stack(swap_blocks(b)) for b in (send_x, meta))
        x_c = pl.pallas_call(
            functools.partial(seat_kernel, cap),
            out_shape=row_block,
            in_specs=[VMEM] * 2,
            out_specs=VMEM,
            compiler_params=pltpu.CompilerParams(vmem_limit_bytes=VMEM_LIMIT),
            name="seat_rows",
        )(recv_x, recv_meta)
        cots = [send_c[k] for k in range(SD)]

    cots = swap_blocks(cots)
    *out_blocks, heads, act, hid, q, k, v, p, slope, n1, n2, rs1, rs2 = forward(
        cap, positions, slots_low, vecs, b_u, x_c, recv_meta
    )
    out_blocks = swap_blocks(out_blocks)
    *ing_blocks, shares, d_up, d_q, d_k, d_v, d_proj, d_br = backward(
        cap, positions, slots_low, vecs, recv_meta, cots, (q, k, v, p, slope, n1, n2, rs1, rs2)
    )
    ing_blocks = swap_blocks(ing_blocks)
    grads = weight_grads_of(
        total_slots, positions, x_c, (heads, act, d_up, d_q, d_k, d_v, d_proj, hid, d_br)
    )
    if four_planes:
        total, vec_owned, output, input_grad, entropy = reduce_all(
            cap, grads, shares, order, out_blocks, ing_blocks, slot_count
        )
    else:
        total = lax.psum(lax.psum_scatter(grads, "tok", scatter_dimension=0, tiled=True), "rep")
        grad_vector = shares[:, 0:9].reshape(-1)
        vec_owned = lax.psum(lax.psum_scatter(grad_vector, "tok", scatter_dimension=0, tiled=True), "rep")
        output, input_grad, entropy = pl.pallas_call(
            functools.partial(return_kernel, cap),
            out_shape=(row_block, row_block, jax.ShapeDtypeStruct((1, ROWS), BF)),
            in_specs=[VMEM] * (2 * SD + 1),
            out_specs=(VMEM,) * 3,
            compiler_params=pltpu.CompilerParams(vmem_limit_bytes=VMEM_LIMIT),
            name="return_rows",
        )(order, *out_blocks, *ing_blocks)

    used = jnp.any(
        positions[None, :] == (tok_index * slot_count + jnp.arange(slot_count, dtype=I32))[:, None], axis=1
    )
    owned_grad = jnp.where(used[:, None, None], total.astype(F32), 0.0)
    first_new, second_new, master_new = adam_update(
        owned_grad, master_slots, moment_one, moment_two, rate_matrix
    )
    vec_first, vec_second, vec_new = adam_update(
        vec_owned, vector_master, vector_moment_one, vector_moment_two, rate_vector
    )
    return (
        output,
        input_grad,
        owned_grad,
        first_new,
        second_new,
        master_new,
        master_new.astype(BF),
        vec_owned,
        vec_first,
        vec_second,
        vec_new,
        vec_new.astype(BF),
        entropy.reshape(-1),
        occupancy,
    )


def solution(mesh):
    placed = (
        P(("rep", "tok"), None),
        P(("rep", "tok"), None),
        P(("rep", "tok")),
        P(),
        P("tok", None, None),
        P("tok", None, None),
        P("tok", None, None),
        P("tok"),
        P("tok"),
        P("tok"),
    )
    return jax.shard_map(
        local,
        mesh=mesh,
        in_specs=placed,
        out_specs=(
            P(("rep", "tok"), None),
            P(("rep", "tok"), None),
            P("tok", None, None),
            P("tok", None, None),
            P("tok", None, None),
            P("tok", None, None),
            P("tok", None, None),
            P("tok"),
            P("tok"),
            P("tok"),
            P("tok"),
            P("tok"),
            P(("rep", "tok")),
            P(),
        ),
        check_vma=False,
    )
```

```python
import functools
import math

import jax
import jax.numpy as jnp
from jax import lax
from jax.experimental import pallas as pl
from jax.experimental.pallas import tpu as pltpu
from jax.sharding import PartitionSpec as P

D = 768
HEADS = 12
HD = 64
FF = 3072
SD = 4
CL = 128
NBLK = 96
STEP = 10
CPS = 32
WROWS = 9216
BLK = 96
ROWS = 1024
PAIRS = HEADS // 2
PW = 2 * HD
TM = 512
PART = 48
META = 16
VMEM_LIMIT = 63 << 20
FC = 768

norm_epsilon = 1e-06
beta_first = 0.9
beta_second = 0.999
adam_epsilon = 1e-08
weight_decay = 0.01
rate_matrix = 0.02
rate_vector = 0.2

BF = jnp.bfloat16
F32 = jnp.float32
I32 = jnp.int32

VMEM = pl.BlockSpec(memory_space=pltpu.VMEM)
SMEM = pl.BlockSpec(memory_space=pltpu.SMEM)
ANY = pl.BlockSpec(memory_space=pl.ANY)

NN = (((1,), (0,)), ((), ()))
NT = (((1,), (1,)), ((), ()))
TN = (((0,), (0,)), ((), ()))


def mm(a, b, dims=NN):
    return lax.dot_general(a, b, dims, preferred_element_type=F32)


def slot_positions(block_owner, slot_count):
    owners = block_owner[:, 0]
    blocks = owners.shape[0]
    shared = owners[:, None] == owners[None, :]
    before = (
        jnp.arange(blocks, dtype=jnp.int32)[None, :] < jnp.arange(blocks, dtype=jnp.int32)[:, None]
    )
    earlier = jnp.sum((shared & before).astype(jnp.int32), axis=1)
    return owners * slot_count + earlier


def adam_update(grad_now, weight_old, first_old, second_old, rate_step):
    first_new = beta_first * first_old + (1.0 - beta_first) * grad_now
    second_new = beta_second * second_old + (1.0 - beta_second) * grad_now * grad_now
    first_hat = first_new / (1.0 - beta_first**STEP)
    second_hat = second_new / (1.0 - beta_second**STEP)
    weight_new = weight_old - rate_step * (
        first_hat / (jnp.sqrt(second_hat) + adam_epsilon) + weight_decay * weight_old
    )
    return (first_new, second_new, weight_new)


def route_slots(order, seat, cap):
    cluster = order // CL
    rel = lax.rem(cluster, SD) ^ seat
    place = (cluster // SD) * CL + lax.rem(order, CL) + 1
    chosen = lax.broadcasted_iota(I32, (8, ROWS), 0) == rel
    chosen_low = jnp.where(chosen, 1.0, 0.0).astype(BF)
    before = lax.broadcasted_iota(I32, (ROWS, ROWS), 0) < lax.broadcasted_iota(I32, (ROWS, ROWS), 1)
    before_low = jnp.where(before, 1.0, 0.0).astype(BF)
    running = mm(chosen_low, before_low)
    rank = jnp.sum(jnp.where(chosen, running, 0.0), axis=0, keepdims=True).astype(I32)
    return rel * cap + rank, place


def slot_matrix(slots, at, cap):
    rows = lax.broadcasted_iota(I32, (cap, ROWS), 0) + at * cap
    return jnp.where(rows == slots, 1.0, 0.0).astype(BF)


def send_kernel(cap, tokens, cotangent, order, send_x, send_c, meta):
    seat = lax.rem(lax.axis_index("tok"), SD)
    slots, place = route_slots(order[...], seat, cap)
    digits = jnp.concatenate([place // CL, lax.rem(place, CL)] + [place * 0] * 6, axis=0).astype(F32).astype(BF)
    for at in range(SD):
        picked = slot_matrix(slots, at, cap)
        send_x[at] = mm(picked, tokens[...]).astype(BF)
        send_c[at] = mm(picked, cotangent[...]).astype(BF)
        coded = mm(digits, picked, NT)
        line = jnp.concatenate([coded[0:1], coded[1:2]], axis=1)
        meta[at] = jnp.broadcast_to(line, (META, D)).astype(BF)


def remote(src, dst, send_sem, recv_sem, tok, rep):
    return pltpu.make_async_remote_copy(
        src_ref=src,
        dst_ref=dst,
        send_sem=send_sem,
        recv_sem=recv_sem,
        device_id={"tok": tok, "rep": rep},
        device_id_type=pl.DeviceIdType.MESH,
    )


def loop(n, body):
    def run(i, c):
        body(i)
        return c

    lax.fori_loop(0, n, run, 0)


class Place:
    def __init__(self):
        self.me = me = lax.axis_index("tok")
        self.z = z = lax.axis_index("rep")
        core, x, y = me % 2, (me // 2) % 2, me // 4
        self.twin = me + 1 - 2 * core
        self.xn = me + 2 - 4 * x
        self.yn = me + 4 - 8 * y
        self.dn = self.xn + 4 - 8 * y
        self.side = z % 2
        self.zp = z + 1 - 2 * self.side

    def twin_of(self, tok):
        return tok + 1 - 2 * (tok % 2)

    def greet(self, peers):
        barrier = pltpu.get_barrier_semaphore()
        for tok, rep in peers:
            pl.semaphore_signal(
                barrier, inc=1, device_id={"tok": tok, "rep": rep}, device_id_type=pl.DeviceIdType.MESH
            )
        return lambda: pl.semaphore_wait(barrier, len(peers))


def seat_matrix(meta, first, rows, cap):
    hi = jnp.concatenate([meta[k, 0:8, 0:cap] for k in range(SD)], axis=1).astype(F32)[0:1]
    lo = jnp.concatenate([meta[k, 0:8, cap : 2 * cap] for k in range(SD)], axis=1).astype(F32)[0:1]
    at = (hi * CL + lo).astype(I32)
    seats = lax.broadcasted_iota(I32, (rows, SD * cap), 0) + (first + 1)
    return jnp.where(seats == at, 1.0, 0.0).astype(BF)


def seat_part(meta, k, cap):
    hi = meta[k, 0:8, 0:cap].astype(F32)[0:1]
    lo = meta[k, 0:8, cap : 2 * cap].astype(F32)[0:1]
    at = (hi * CL + lo).astype(I32)
    seats = lax.broadcasted_iota(I32, (ROWS, cap), 0) + 1
    return jnp.where(seats == at, 1.0, 0.0).astype(BF)


def seat_rows(meta, blocks, cap, to):
    def body(t):
        r0 = pl.multiple_of(t * 256, 256)
        rows = blocks[...].reshape(SD * cap, D)
        to[pl.ds(r0, 256), :] = mm(seat_matrix(meta, r0, 256, cap), rows).astype(BF)

    loop(ROWS // 256, body)


def seat_kernel(cap, blocks, meta, to):
    seat_rows(meta, blocks, cap, to)


def gather_kernel(
    cap,
    count,
    tokens_h,
    cotangent_h,
    order,
    master_h,
    vector,
    owner_of,
    slots,
    x_c,
    cot_0,
    cot_1,
    cot_2,
    cot_3,
    recv_meta,
    vecs,
    b_u,
    occupancy,
    positions,
    tokens,
    cotangent,
    master,
    own,
    send_x,
    send_c,
    meta,
    recv_x,
    got_meta,
    slot_of,
    digits,
    mine,
    by_z,
    by_tok,
    x_s,
    x_r,
    y_s,
    y_r,
    d_s,
    d_r,
    zx_s,
    zx_r,
    zd_s,
    zd_r,
    zy_s,
    zy_r,
    p_s,
    p_r,
    row_s,
    row_r,
    z_s,
    z_r,
    t_s,
    t_r,
    local_s,
):
    at = Place()
    me, z, side = at.me, at.z, at.side
    n_tok, n_rep = 8, 4
    peers = [((me + d) % n_tok, z) for d in range(1, n_tok)] + [(me, (z + d) % n_rep) for d in range(1, n_rep)]
    fetch = [
        pltpu.make_async_copy(src, dst, local_s.at[i])
        for i, (src, dst) in enumerate(((master_h, master), (tokens_h, tokens), (cotangent_h, cotangent)))
    ]
    for copy in fetch:
        copy.start()
    wait_peers = at.greet(peers)
    fetch[0].wait()

    last = count - 1

    def near(j):
        return side * last + (1 - 2 * side) * j

    def far(j):
        return (1 - side) * last - (1 - 2 * side) * j

    few_x, few_d, few_y = 11 * count // 26, 12 * count // 26, 8 * count // 26
    most_x, most_d, most_y = count - few_x, count - few_d, count - few_y

    def piece(owner, s):
        return slots.at[owner * count + s]

    def to_x(s):
        return remote(own.at[s], piece(me, s), x_s.at[s], x_r.at[s], at.xn, z)

    def to_y(s):
        return remote(own.at[s], piece(me, s), y_s.at[s], y_r.at[s], at.yn, z)

    def on_y(s):
        return remote(piece(at.xn, s), piece(at.xn, s), d_s.at[s], d_r.at[s], at.yn, z)

    def x_on_z(s):
        return remote(piece(at.xn, s), piece(at.xn, s), zx_s.at[s], zx_r.at[s], me, at.zp)

    def d_on_z(s):
        return remote(piece(at.dn, s), piece(at.dn, s), zd_s.at[s], zd_r.at[s], me, at.zp)

    def y_on_z(s):
        return remote(piece(at.yn, s), piece(at.yn, s), zy_s.at[s], zy_r.at[s], me, at.zp)

    def x_in(s):
        return remote(own.at[s], piece(at.xn, s), x_s.at[s], x_r.at[s], at.xn, z)

    def y_in(s):
        return remote(own.at[s], piece(at.yn, s), y_s.at[s], y_r.at[s], at.yn, z)

    def d_in(s):
        return remote(own.at[s], piece(at.dn, s), d_s.at[s], d_r.at[s], at.yn, z)

    owners = (me, at.xn, at.yn, at.dn)

    def near_run(q, j0, j1):
        return (q, (1 - side) * j0 + side * (count - j1), j1 - j0)

    def far_run(q, j0, j1):
        return (q, side * j0 + (1 - side) * (count - j1), j1 - j0)

    runs = (
        (0, 0, count),
        near_run(2, 0, few_y),
        near_run(1, 0, most_x),
        near_run(3, 0, most_d),
        far_run(1, 0, few_x),
        near_run(2, few_y, most_y),
        far_run(2, 0, few_y),
        far_run(3, 0, few_d // 2),
        far_run(3, few_d // 2, few_d - 2),
        far_run(3, few_d - 2, few_d),
    )

    def to_twin(i):
        q, s, n = runs[i]
        src = own if q == 0 else slots.at[pl.ds(owners[q] * count + s, n)]
        dst = slots.at[pl.ds(owners[q] * count + s, n)]
        return remote(src, dst, p_s.at[i], p_r.at[i], at.twin, z)

    def cast(j):
        own[near(j)] = master[near(j)].astype(BF)

    loop(most_x, cast)
    wait_peers()
    loop(most_x, lambda j: to_x(near(j)).start())
    loop(few_y, lambda j: to_y(near(j)).start())
    loop(count - most_x, lambda j: cast(most_x + j))
    to_twin(0).start()
    keep = pltpu.make_async_copy(own, slots.at[pl.ds(me * count, count)], local_s.at[3])
    keep.start()

    seat = me % SD
    seats = (me, at.twin, at.xn, at.twin_of(at.xn))
    rows_of = ((meta, got_meta), (send_x, recv_x))

    def row_copy(i, k):
        src, dst = rows_of[i]
        return remote(src.at[k], dst.at[k], row_s.at[i, k], row_r.at[i, k], seats[k], z)

    put_c = [
        pltpu.make_async_copy(send_c.at[k], to, local_s.at[4 + k])
        for k, to in enumerate((cot_0, cot_1, cot_2, cot_3))
    ]

    def route():
        fetch[1].wait()
        fetch[2].wait()
        slots_here, place = route_slots(order[...], seat, cap)
        slot_of[...] = slots_here
        digits[...] = (
            jnp.concatenate([place // CL, lax.rem(place, CL)] + [place * 0] * 6, axis=0).astype(F32).astype(BF)
        )

    def sort_tokens(k):
        picked = slot_matrix(slot_of[...], k, cap)
        send_x[k] = mm(picked, tokens[...]).astype(BF)
        coded = mm(digits[...], picked, NT)
        line = jnp.concatenate([coded[0:1], coded[1:2]], axis=1)
        meta[k] = jnp.broadcast_to(line, (META, D)).astype(BF)
        for i in range(2):
            if k:
                row_copy(i, k).start()
            else:
                src, dst = rows_of[i]
                dst[0] = src[0]

    def sort_cotangent(k):
        send_c[k] = mm(slot_matrix(slot_of[...], k, cap), cotangent[...]).astype(BF)
        put_c[k].start()

    def z_copy(d):
        return remote(by_z.at[0], by_z.at[d], z_s.at[d], z_r.at[d], me, (z + d) % n_rep)

    def t_copy(d):
        return remote(mine, by_tok.at[d], t_s.at[d], t_r.at[d], (me + d) % n_tok, z)

    def count_rows():
        residue = lax.rem(me // SD * CPS + order[...] // CL, n_tok)
        hit = lax.broadcasted_iota(I32, (128, ROWS), 0) == residue
        by_z[0] = mm(jnp.ones((8, ROWS), BF), jnp.where(hit, 1.0, 0.0).astype(BF), NT)
        for d in range(1, n_rep):
            z_copy(d).start()
        for i in range(9):
            mine[i : i + 1] = vector[i * 128 : (i + 1) * 128].reshape(1, 128).astype(BF).astype(F32)
        block_row = lax.broadcasted_iota(I32, (NBLK, NBLK), 0)
        block_col = lax.broadcasted_iota(I32, (NBLK, NBLK), 1)
        by_col = owner_of[...].astype(F32)
        by_row = lane_sum(jnp.where(block_row == block_col, by_col, 0.0))
        earlier = jnp.where((by_row == by_col) & (block_row < block_col), 1.0, 0.0)
        positions[...] = (by_col * (count * PART // BLK) + jnp.sum(earlier, axis=0, keepdims=True)).astype(I32)

    def share_vectors():
        for d in range(1, n_rep):
            z_copy(d).wait()
        mine[16:24] = by_z[0] + by_z[1] + by_z[2] + by_z[3]
        for d in range(1, n_tok):
            t_copy(d).start()

    def lay_out_vectors():
        by_tok[0] = mine[...]
        for d in range(1, n_tok):
            t_copy(d).wait()
        for owner in range(n_tok):
            share = by_tok[(me + n_tok - owner) % n_tok]
            occupancy[owner : owner + 1, :] = share[16:17, 0:n_tok].astype(I32)
            for i in range(9):
                chunk = owner * 9 + i
                row, lane = chunk // 6, chunk % 6 * 128
                if row < 8:
                    vecs[row : row + 1, lane : lane + 128] = share[i : i + 1]
                else:
                    lane += (row - 8) * D
                    b_u[:, lane : lane + 128] = share[i : i + 1]

    between = {
        1: lambda: (route(), sort_tokens(2)),
        3: lambda: sort_tokens(3),
        5: lambda: sort_tokens(1),
        7: lambda: (sort_tokens(0), count_rows()),
        9: lambda: sort_cotangent(1),
        11: lambda: sort_cotangent(2),
        13: lambda: sort_cotangent(3),
    }
    for j in range(most_x):
        x_in(near(j)).wait_recv()
        if j < most_d:
            on_y(near(j)).start()
        if j < few_x:
            x_on_z(near(j)).start()
        if j < few_y:
            y_in(near(j)).wait_recv()
            y_on_z(near(j)).start()
        if j == few_y:
            to_twin(1).start()
        if j in between:
            between[j]()
    to_twin(2).start()
    loop(most_y - few_y, lambda j: to_y(near(few_y + j)).start())
    share_vectors()
    sort_cotangent(0)

    def diagonal(j):
        d_in(near(j)).wait_recv()
        d_on_z(near(j)).start()

    loop(few_d, diagonal)
    loop(most_d - few_d, lambda j: d_in(near(few_d + j)).wait_recv())
    to_twin(3).start()
    loop(few_x, lambda j: x_on_z(far(j)).wait_recv())
    to_twin(4).start()
    lay_out_vectors()
    loop(most_y - few_y, lambda j: y_in(near(few_y + j)).wait_recv())
    to_twin(5).start()
    loop(few_y, lambda j: y_on_z(far(j)).wait_recv())
    to_twin(6).start()
    for i in (0, 1):
        for k in (2, 3, 1):
            row_copy(i, k).wait_recv()
    recv_meta[...] = got_meta[...]
    seat_rows(got_meta, recv_x, cap, x_c)
    done = 0
    for i, upto in ((7, few_d // 2), (8, few_d - 2), (9, few_d)):
        loop(upto - done, lambda j, done=done: d_on_z(far(done + j)).wait_recv())
        to_twin(i).start()
        done = upto

    for i in range(2):
        for k in (2, 3, 1):
            row_copy(i, k).wait_send()
    for copy in put_c:
        copy.wait()
    keep.wait()

    loop(most_x, lambda j: to_x(near(j)).wait_send())
    loop(most_y, lambda j: to_y(near(j)).wait_send())
    loop(most_d, lambda j: on_y(near(j)).wait_send())
    loop(few_x, lambda j: x_on_z(near(j)).wait_send())
    loop(few_d, lambda j: d_on_z(near(j)).wait_send())
    loop(few_y, lambda j: y_on_z(near(j)).wait_send())
    for i in range(len(runs)):
        to_twin(i).wait()


def gather_all(cap, tokens, cotangent, order, master, vector, block_owner):
    count = master.shape[0] * BLK // PART
    rows = jax.ShapeDtypeStruct((ROWS, D), BF)
    part = jax.ShapeDtypeStruct((cap, D), BF)
    dma = pltpu.SemaphoreType.DMA
    block = pltpu.VMEM((SD, cap, D), BF)
    meta = pltpu.VMEM((SD, META, D), BF)
    return pl.pallas_call(
        functools.partial(gather_kernel, cap, count),
        out_shape=(
            jax.ShapeDtypeStruct((8 * count, PART, D), BF),
            rows,
            part,
            part,
            part,
            part,
            jax.ShapeDtypeStruct((SD, META, D), BF),
            jax.ShapeDtypeStruct((8, D), F32),
            jax.ShapeDtypeStruct((1, FF), F32),
            jax.ShapeDtypeStruct((8, 8), I32),
            jax.ShapeDtypeStruct((1, NBLK), I32),
        ),
        in_specs=[ANY, ANY, VMEM, ANY, VMEM, VMEM],
        out_specs=(ANY, VMEM) + (ANY,) * SD + (VMEM,) * 5,
        scratch_shapes=[
            pltpu.VMEM((ROWS, D), BF),
            pltpu.VMEM((ROWS, D), BF),
            pltpu.VMEM((count, PART, D), F32),
            pltpu.VMEM((count, PART, D), BF),
            block,
            block,
            meta,
            block,
            meta,
            pltpu.VMEM((1, ROWS), I32),
            pltpu.VMEM((8, ROWS), BF),
            pltpu.VMEM((24, 128), F32),
            pltpu.VMEM((4, 8, 128), F32),
            pltpu.VMEM((8, 24, 128), F32),
        ]
        + [dma((count,))] * 12
        + [dma((10,))] * 2
        + [dma((2, SD))] * 2
        + [dma((4,))] * 2
        + [dma((8,))] * 2
        + [dma((8,))],
        compiler_params=pltpu.CompilerParams(collective_id=0, has_side_effects=True, vmem_limit_bytes=VMEM_LIMIT),
        cost_estimate=pl.CostEstimate(flops=8 * ROWS * ROWS * D, bytes_accessed=64 << 20, transcendentals=0),
        name="gather",
    )(tokens, cotangent, order, master.reshape(count, PART, D), vector, block_owner.reshape(1, NBLK))


def return_kernel(cap, order, *refs):
    outs, ings, (out, ing, entropy) = refs[:SD], refs[SD : 2 * SD], refs[2 * SD :]
    seat = lax.rem(lax.axis_index("tok"), SD)
    slots, _ = route_slots(order[...], seat, cap)
    picked = jnp.concatenate([slot_matrix(slots, at, cap) for at in range(SD)], axis=0)
    for to, blocks in ((out, outs), (ing, ings)):
        rows = jnp.concatenate([block[0:cap, :] for block in blocks], axis=0)
        to[...] = mm(picked, rows, TN).astype(BF)
    line = jnp.concatenate([block[cap : cap + 8, 0:cap] for block in outs], axis=1)
    entropy[...] = mm(line, picked)[0:1].astype(BF)


def swap_blocks(blocks):
    n = lax.axis_size("tok")
    parts = [blocks[0]]
    for k in range(1, SD):
        parts.append(lax.ppermute(blocks[k], "tok", [(i, i ^ k) for i in range(n)]))
    return parts


def reduce_kernel(
    cap,
    count,
    split,
    grads,
    vec,
    order,
    out_0,
    out_1,
    out_2,
    out_3,
    ing_0,
    ing_1,
    ing_2,
    ing_3,
    total,
    vec_out,
    output,
    input_grad,
    entropy,
    out_v,
    ing_v,
    slot_of,
    a,
    tw,
    rd,
    rx,
    ry,
    o,
    rz1,
    pz,
    rz2,
    fz,
    vt,
    va,
    vb,
    vc,
    a_l,
    keep_l,
    p_s,
    p_r,
    d_s,
    d_r,
    x_s,
    x_r,
    y_s,
    y_r,
    z1_s,
    z1_r,
    z2_s,
    z2_r,
    z3_s,
    z3_r,
    t_s,
    t_r,
    v_s,
    v_r,
    row_l,
):
    at = Place()
    me, z = at.me, at.z
    n_tok, n_rep = 8, 4
    peers = [((me + d) % n_tok, z) for d in range(1, n_tok)] + [(me, (z + d) % n_rep) for d in range(1, n_rep)]
    wait_peers = at.greet(peers)
    owners = (me, at.xn, at.yn, at.dn)

    def load(q):
        return pltpu.make_async_copy(grads.at[pl.ds(owners[q] * count, count)], a.at[q], a_l.at[q])

    for q in (3, 1, 2, 0):
        load(q).start()
    rows_in = [
        pltpu.make_async_copy(src, to.at[k], row_l.at[i, k])
        for i, (blocks, to) in enumerate((((out_0, out_1, out_2, out_3), out_v), ((ing_0, ing_1, ing_2, ing_3), ing_v)))
        for k, src in enumerate(blocks)
    ]
    for copy in rows_in:
        copy.start()
    wait_peers()

    groups = [(g, g * (count // 4), count // 4 if g < 3 else count - 3 * (count // 4)) for g in range(4)]

    def to_twin(q, group):
        g, s, n = group
        src = grads.at[pl.ds(at.twin_of(owners[q]) * count + s, n)]
        return remote(src, tw.at[q, pl.ds(s, n)], p_s.at[q, g], p_r.at[q, g], at.twin, z)

    def d_y(s):
        return remote(a.at[3, s], rd.at[s], d_s.at[s], d_r.at[s], at.yn, z)

    def d_x(s):
        return remote(a.at[3, s], rd.at[s], d_s.at[s], d_r.at[s], at.xn, z)

    def to_x(s):
        return remote(a.at[1, s], rx.at[s], x_s.at[s], x_r.at[s], at.xn, z)

    def to_y(s):
        return remote(a.at[2, s], ry.at[s], y_s.at[s], y_r.at[s], at.yn, z)

    def z_in(s):
        return remote(o.at[s], rz1.at[s], z1_s.at[s], z1_r.at[s], me, at.zp)

    def z_swap(s):
        return remote(pz.at[s], rz2.at[s], z2_s.at[s], z2_r.at[s], me, n_rep - 1 - z)

    def z_out(s):
        return remote(fz.at[s], fz.at[s], z3_s.at[s], z3_r.at[s], me, at.zp)

    def keep(s):
        return pltpu.make_async_copy(fz.at[s], total.at[s], keep_l.at[s])

    for group in groups:
        for q in (3, 1, 2, 0):
            to_twin(q, group).start()

    def v_tok(d):
        return remote(vec.at[(me + d) % n_tok], vt.at[d], t_s.at[d], t_r.at[d], (me + d) % n_tok, z)

    def v_rep(i, src):
        return remote(src, vb.at[i], v_s.at[i], v_r.at[i], me, at.zp if i == 0 else (z + 2) % n_rep)

    for d in range(1, n_tok):
        v_tok(d).start()

    def join(q, s):
        return a[q, s] + tw[q, s]

    def first(s, send):
        a[3, s] = join(3, s)
        send(s).start()

    def plain(q, s, send):
        a[q, s] = join(q, s)
        send(s).start()

    def joined(q, s, arrived, send):
        arrived(s).wait_recv()
        a[q, s] = join(q, s) + rd[s]
        send(s).start()

    inner = (z == 1) | (z == 2)
    outer = (z == 0) | (z == 3)

    def own(s):
        to_x(s).wait_recv()
        to_y(s).wait_recv()
        o[s] = join(0, s) + (rx[s] + ry[s])
        pl.when(outer)(lambda: z_in(s).start())

    def middle(s):
        @pl.when(inner)
        def _():
            z_in(s).wait_recv()
            pz[s] = o[s] + rz1[s]
            z_swap(s).start()

    def last(s):
        @pl.when(inner)
        def _():
            z_swap(s).wait_recv()
            fz[s] = pz[s] + rz2[s]
            z_out(s).start()
            keep(s).start()

    def taken(s):
        @pl.when(outer)
        def _():
            z_out(s).wait_recv()
            keep(s).start()

    def pick_rows(i):
        ts = pl.ds(pl.multiple_of(i * 256, 256), 256)
        hit = lax.broadcasted_iota(I32, (SD * cap, 256), 0) == slot_of[:, ts]
        picked = jnp.where(hit, 1.0, 0.0).astype(BF)
        outs = jnp.concatenate([out_v[k, 0:cap, :] for k in range(SD)], axis=0)
        ings = jnp.concatenate([ing_v[k] for k in range(SD)], axis=0)
        both = mm(picked, jnp.concatenate([outs, ings], axis=1), TN)
        output[ts, :] = both[:, 0:D].astype(BF)
        input_grad[ts, :] = both[:, D:].astype(BF)
        line = jnp.concatenate([out_v[k, cap : cap + 8, 0:cap] for k in range(SD)], axis=1)
        entropy[:, ts] = mm(line, picked)[0:1].astype(BF)

    for q in (3, 1, 2, 0):
        load(q).wait()

    def steps(i, lag, more):
        s = i - lag
        by_x = (s % 2 == 0) & (s < 2 * split)
        live = (s >= 0) & (s < count)
        pl.when(live & by_x)(lambda: more(s, True))
        pl.when(live & jnp.logical_not(by_x))(lambda: more(s, False))

    def steps_of(i, lag, more):
        pl.when((i >= lag) & (i < count + lag))(lambda: more(i - lag))

    def round_of(i):
        for group in groups:

            @pl.when(i == group[1])
            def _(group=group):
                to_twin(3, group).wait_recv()

            @pl.when(i == group[1] + 1)
            def _(group=group):
                to_twin(1, group).wait_recv()
                to_twin(2, group).wait_recv()

            @pl.when(i == group[1] + 6)
            def _(group=group):
                to_twin(0, group).wait_recv()

        steps(i, 0, lambda s, by_x: first(s, d_x if by_x else d_y))
        steps(i, 1, lambda s, by_x: plain(1, s, to_x) if by_x else plain(2, s, to_y))
        steps(i, 3, lambda s, by_x: joined(2, s, d_x, to_y) if by_x else joined(1, s, d_y, to_x))
        steps_of(i, 6, own)
        steps_of(i, 8, middle)
        steps_of(i, 10, last)
        steps_of(i, 12, taken)

    loop(3, round_of)
    for copy in rows_in:
        copy.wait()
    slots_here, _ = route_slots(order[...], me % SD, cap)
    slot_of[...] = slots_here

    v_sum = vec[me]
    for d in range(1, n_tok):
        v_tok(d).wait()
        v_sum = v_sum + vt[d]
    va[...] = v_sum
    v_rep(0, va).start()

    def four_rounds(i):
        loop(4, lambda j: round_of(3 + 4 * i + j))
        pick_rows(i)

    four_rounds(0)
    v_rep(0, va).wait()
    vc[...] = va[...] + vb[0]
    v_rep(1, vc).start()
    loop(3, lambda i: four_rounds(1 + i))
    loop(count + 12 - 19, lambda i: round_of(19 + i))
    v_rep(1, vc).wait()
    vec_out[...] = vc[...] + vb[1]

    for group in groups:
        for q in range(4):
            to_twin(q, group).wait_send()

    def sent(s):
        d_y(s).wait_send()
        to_x(s).wait_send()
        to_y(s).wait_send()
        keep(s).wait()

    loop(count, sent)

    @pl.when(outer)
    def _():
        loop(count, lambda s: z_in(s).wait_send())

    @pl.when(inner)
    def _():
        def back(s):
            z_swap(s).wait_send()
            z_out(s).wait_send()

        loop(count, back)


def reduce_all(cap, grads, shares, order, outs, ings, count):
    dma = pltpu.SemaphoreType.DMA
    count = count * BLK // PART
    part = pltpu.VMEM((count, PART, D), BF)
    whole = pltpu.VMEM((4, count, PART, D), BF)
    line = pltpu.VMEM((16, 128), F32)
    rows = jax.ShapeDtypeStruct((ROWS, D), BF)
    total, vec, output, input_grad, entropy = pl.pallas_call(
        functools.partial(reduce_kernel, cap, count, count // 2),
        out_shape=(
            jax.ShapeDtypeStruct((count, PART, D), BF),
            jax.ShapeDtypeStruct((16, 128), F32),
            rows,
            rows,
            jax.ShapeDtypeStruct((1, ROWS), BF),
        ),
        in_specs=[ANY, VMEM, VMEM] + [ANY] * (2 * SD),
        out_specs=(ANY,) + (VMEM,) * 4,
        scratch_shapes=[
            pltpu.VMEM((SD, cap + META, D), BF),
            pltpu.VMEM((SD, cap, D), BF),
            pltpu.VMEM((1, ROWS), I32),
            whole,
            whole,
        ]
        + [part] * 8
        + [pltpu.VMEM((8, 16, 128), F32), line, pltpu.VMEM((2, 16, 128), F32), line]
        + [dma((4,)), dma((count,))]
        + [dma((4, 4))] * 2
        + [dma((count,))] * 12
        + [dma((8,))] * 2
        + [dma((2,))] * 2
        + [dma((2, SD))],
        compiler_params=pltpu.CompilerParams(collective_id=1, has_side_effects=True, vmem_limit_bytes=50 << 20),
        cost_estimate=pl.CostEstimate(flops=4 * ROWS * ROWS * D, bytes_accessed=64 << 20, transcendentals=0),
        name="reduce",
    )(grads.reshape(-1, PART, D), shares, order, *outs, *ings)
    return total.reshape(-1, BLK, D), vec[0:9].reshape(-1), output, input_grad, entropy


V_BQ, V_BV, V_BO, V_BD, V_G1, V_C1, V_G2, V_C2 = range(8)


def inverse(x):
    r = pl.reciprocal(x, approx=True)
    return r * (2.0 - x * r)


def erf_parts(v):
    t = inverse(1.0 + (0.3275911 / math.sqrt(2.0)) * jnp.abs(v))
    e = jnp.exp2((v * v) * (-0.5 / math.log(2.0)))
    poly = 0.5 * 1.061405429
    for c in (-1.453152027, 1.421413741, -0.284496736, 0.254829592):
        poly = poly * t + 0.5 * c
    tail = poly * (t * e)
    return jnp.where(v >= 0.0, 1.0 - tail, tail), e


def lane_sum(x):
    return jnp.sum(x, axis=1, keepdims=True)


def gelu_parts(v):
    phi, e = erf_parts(v)
    return v * phi, phi + v * (e * (1.0 / math.sqrt(2.0 * math.pi)))


def weight_copies(pos, slots, w, sem, first):
    def copy(b):
        return pltpu.make_async_copy(slots.at[pos[first + b]], w.at[pl.ds(b * BLK, BLK)], sem)

    n = w.shape[0] // BLK
    return (lambda: loop(n, lambda b: copy(b).start())), (lambda: loop(n, lambda b: copy(b).wait()))


def halves_of_heads():
    lane = lax.broadcasted_iota(I32, (1, PW), 1)
    m0 = jnp.where(lane < HD, 1.0, 0.0).astype(BF)
    m1 = jnp.where(lane < HD, 0.0, 1.0).astype(BF)
    return lambda pair: jnp.concatenate([pair * m0, pair * m1], axis=0)


def tile_rows(t):
    return pl.ds(pl.multiple_of(t * TM, TM), TM)


def forward_kernel(
    cap,
    pos,
    slots,
    vecs,
    b_u,
    x_h,
    meta,
    back_0,
    back_1,
    back_2,
    back_3,
    heads_h,
    act_h,
    hid_h,
    q_h,
    k_h,
    v_h,
    p_h,
    slope_h,
    n1_h,
    n2_h,
    rs1_h,
    rs2_h,
    wqkv,
    wo,
    wu,
    wd,
    x_c,
    heads,
    act,
    hid,
    q,
    k,
    v,
    p_all,
    slope,
    n1,
    n2,
    rs1,
    rs2,
    out_c,
    ent,
    hid_t,
    w_sem,
    x_sem,
    o_sem,
):
    inv = 1.0 / math.sqrt(HD)
    get_x = pltpu.make_async_copy(x_h, x_c, x_sem)
    get_x.start()
    weights = [
        weight_copies(pos, slots, w, w_sem.at[i], first)
        for i, (w, first) in enumerate(((wqkv, 0), (wo, 24), (wu, 32), (wd, 64)))
    ]
    for start, _ in weights:
        start()
    get_x.wait()
    apart = halves_of_heads()

    def vec(i):
        return vecs[i : i + 1, :]

    saved = (
        (heads, heads_h),
        (act, act_h),
        (hid, hid_h),
        (q, q_h),
        (k, k_h),
        (v, v_h),
        (slope, slope_h),
        (n1, n1_h),
        (n2, n2_h),
        (rs1, rs1_h),
        (rs2, rs2_h),
    )

    def save(t, i):
        src, dst = saved[i]
        return pltpu.make_async_copy(src.at[tile_rows(t)], dst.at[tile_rows(t)], o_sem.at[i])

    def save_p(t):
        n = TM // CL
        cs = pl.ds(t * n, n)
        return pltpu.make_async_copy(p_all.at[cs], p_h.at[cs], o_sem.at[len(saved)])

    def normal(r, n, rs, rows):
        c = r - lane_sum(r) * (1.0 / D)
        scale = lax.rsqrt(lane_sum(c * c) * (1.0 / D) + norm_epsilon)
        rs[rows, :] = jnp.broadcast_to(scale, (TM, 128))
        n[rows, :] = c * scale

    def tile(t):
        rows = tile_rows(t)
        first = t == 0
        pl.when(first)(weights[0][1])
        x = x_c[rows, :]
        q[rows, :] = ((mm(x, wqkv[0:D, :]) + vec(V_BQ)).astype(BF).astype(F32) * inv).astype(BF)
        k[rows, :] = mm(x, wqkv[D : 2 * D, :]).astype(BF)
        v[rows, :] = (mm(x, wqkv[2 * D :, :]) + vec(V_BV)).astype(BF)

        def attend(c):
            groups = [pl.ds(pl.multiple_of(t * TM + (2 * c + i) * CL, CL), CL) for i in range(2)]
            pairs = [(i, p, slice(p * PW, (p + 1) * PW)) for i in range(2) for p in range(PAIRS)]
            scores = [mm(apart(k[groups[i], ps]), q[groups[i], ps], NT) for i, _, ps in pairs]
            total = [jnp.zeros((1, CL), F32)] * 2
            probs = []
            for (i, _, _), both in zip(pairs, scores):
                halves = []
                for h in range(2):
                    sh = both[h * CL : (h + 1) * CL]
                    sh = sh - jnp.max(sh, axis=0, keepdims=True)
                    e = jnp.exp(sh)
                    tot = jnp.sum(e, axis=0, keepdims=True)
                    r = 1.0 / tot
                    total[i] += jnp.log(tot) - jnp.sum(e * sh, axis=0, keepdims=True) * r
                    halves.append((e * r).astype(BF))
                probs.append(jnp.concatenate(halves, axis=0))
            mixed = [mm(w, apart(v[groups[i], ps]), TN).astype(BF) for (i, _, ps), w in zip(pairs, probs)]
            for (i, p, ps), w, o in zip(pairs, probs, mixed):
                p_all[t * (TM // CL) + 2 * c + i, p] = w
                heads[groups[i], ps] = o
            for i in range(2):
                ent[:, groups[i]] = jnp.broadcast_to(total[i] * (1.0 / HEADS), (8, CL))

        loop(TM // CL // 2, attend)
        for i in (0, 3, 4, 5):
            save(t, i).start()
        save_p(t).start()
        pl.when(first)(weights[1][1])
        normal(x_c[rows, :].astype(F32) + mm(heads[rows, :], wo[...]) + vec(V_BO), n1, rs1, rows)
        hidden = n1[rows, :] * vec(V_G1) + vec(V_C1)
        hid[rows, :] = hidden.astype(BF)
        hid_t[...] = hidden
        pl.when(first)(weights[2][1])

        def widen(f):
            fs = pl.ds(pl.multiple_of(f * FC, FC), FC)
            g, g_slope = gelu_parts(mm(hid[rows, :], wu[fs, :], NT) + b_u[:, fs])
            act[rows, fs] = g.astype(BF)
            slope[rows, fs] = g_slope.astype(BF)

        loop(FF // FC, widen)
        for i in (1, 2, 6, 7, 9):
            save(t, i).start()
        pl.when(first)(weights[3][1])
        normal(hid_t[...] + mm(act[rows, :], wd[...]) + vec(V_BD), n2, rs2, rows)
        out_c[rows, :] = (n2[rows, :] * vec(V_G2) + vec(V_C2)).astype(BF)
        for i in (8, 10):
            save(t, i).start()

    loop(ROWS // TM, tile)

    for j, back in enumerate((back_0, back_1, back_2, back_3)):
        own = seat_part(meta, j, cap)
        back[0:cap, :] = mm(own, out_c[...], TN).astype(BF)
        line = mm(ent[...].astype(BF), own)
        back[cap:, :] = jnp.concatenate([line, line], axis=1)[0:1].astype(BF) * jnp.ones((META, 1), BF)

    def saved_all(t):
        for i in range(len(saved)):
            save(t, i).wait()
        save_p(t).wait()

    loop(ROWS // TM, saved_all)


def shape_of(kind, *shape):
    return jax.ShapeDtypeStruct(shape, kind)


def saved_shapes():
    rows, wide = ((ROWS, D), BF), ((ROWS, FF), BF)
    probs = ((ROWS // CL, PAIRS, 2 * CL, CL), BF)
    full, thin = ((ROWS, D), F32), ((ROWS, 128), F32)
    return rows, wide, probs, full, thin


def forward(cap, positions, slots, vecs, b_u, x_c, meta):
    rows, wide, probs, full, thin = saved_shapes()
    kept = (rows, wide, rows, rows, rows, rows, probs, wide, full, full, thin, thin)
    dma = pltpu.SemaphoreType.DMA
    return pl.pallas_call(
        functools.partial(forward_kernel, cap),
        out_shape=(shape_of(BF, cap + META, D),) * SD + tuple(shape_of(kind, *shape) for shape, kind in kept),
        in_specs=[SMEM, ANY, VMEM, VMEM, ANY, VMEM],
        out_specs=(VMEM,) * SD + (ANY,) * len(kept),
        scratch_shapes=[
            pltpu.VMEM((3 * D, D), BF),
            pltpu.VMEM((D, D), BF),
            pltpu.VMEM((FF, D), BF),
            pltpu.VMEM((FF, D), BF),
            pltpu.VMEM(*rows),
        ]
        + [pltpu.VMEM(*a) for a in kept]
        + [
            pltpu.VMEM(*rows),
            pltpu.VMEM((8, ROWS), F32),
            pltpu.VMEM((TM, D), F32),
            dma((4,)),
            dma,
            dma((12,)),
        ],
        compiler_params=pltpu.CompilerParams(vmem_limit_bytes=VMEM_LIMIT),
        cost_estimate=pl.CostEstimate(flops=2 * ROWS * WROWS * D, bytes_accessed=64 << 20, transcendentals=0),
        name="forward",
    )(positions, slots, vecs, b_u, x_c, meta)


def backward_kernel(
    cap,
    pos,
    slots,
    vecs,
    meta,
    cot_0,
    cot_1,
    cot_2,
    cot_3,
    q_h,
    k_h,
    v_h,
    p_h,
    slope_h,
    n1_h,
    n2_h,
    rs1_h,
    rs2_h,
    back_0,
    back_1,
    back_2,
    back_3,
    shares,
    d_up_h,
    d_q_h,
    d_k_h,
    d_v_h,
    d_proj_h,
    d_br_h,
    wqkv,
    wo,
    wu,
    wd,
    blocks,
    q,
    k,
    v,
    p_all,
    d_up,
    n1,
    n2,
    rs1,
    rs2,
    d_proj,
    d_br,
    ing_c,
    d_h_t,
    res_t,
    gvec,
    g_bu,
    w_sem,
    c_sem,
    i_sem,
    o_sem,
):
    inv = 1.0 / math.sqrt(HD)
    get_c = [
        pltpu.make_async_copy(cot, blocks.at[j], c_sem.at[j]) for j, cot in enumerate((cot_0, cot_1, cot_2, cot_3))
    ]
    for copy in get_c:
        copy.start()
    fetch = [
        pltpu.make_async_copy(src, dst, i_sem.at[i])
        for i, (src, dst) in enumerate(
            (
                (n2_h, n2),
                (rs2_h, rs2),
                (slope_h, d_up),
                (n1_h, n1),
                (rs1_h, rs1),
                (v_h, v),
                (p_h, p_all),
                (k_h, k),
                (q_h, q),
            )
        )
    ]
    weights = [
        weight_copies(pos, slots, w, w_sem.at[i], first)
        for i, (w, first) in enumerate(((wd, 64), (wu, 32), (wo, 24), (wqkv, 0)))
    ]
    fetch[0].start()
    fetch[1].start()
    weights[0][0]()
    fetch[2].start()
    weights[1][0]()
    fetch[3].start()
    fetch[4].start()
    weights[2][0]()
    for i in range(5, 9):
        fetch[i].start()
    weights[3][0]()
    gvec[...] = jnp.zeros_like(gvec)
    g_bu[...] = jnp.zeros_like(g_bu)
    shares[...] = jnp.zeros_like(shares)
    for copy in get_c:
        copy.wait()
    seat_rows(meta, blocks, cap, d_br)
    apart = halves_of_heads()
    first_half = lax.broadcasted_iota(I32, (CL, PW), 1) < HD

    def vec(i):
        return vecs[i : i + 1, :]

    def add_vec(i, value):
        gvec[i : i + 1, :] += jnp.sum(value, axis=0, keepdims=True)

    saved = ((d_up, d_up_h), (q, d_q_h), (k, d_k_h), (v, d_v_h), (d_proj, d_proj_h), (d_br, d_br_h))

    def save(t, i):
        src, dst = saved[i]
        return pltpu.make_async_copy(src.at[tile_rows(t)], dst.at[tile_rows(t)], o_sem.at[i])

    def norm_back(e, n, rs, gain, shift):
        add_vec(gain, e * n)
        add_vec(shift, e)
        eg = e * vec(gain)
        return rs * (eg - lane_sum(eg) * (1.0 / D) - n * (lane_sum(eg * n) * (1.0 / D)))

    def tile(t):
        rows = tile_rows(t)
        start = t == 0

        @pl.when(start)
        def _():
            fetch[0].wait()
            fetch[1].wait()

        d_r2 = norm_back(d_br[rows, :].astype(F32), n2[rows, :], rs2[rows, 0:1], V_G2, V_C2)
        d_br[rows, :] = d_r2.astype(BF)
        add_vec(V_BD, d_br[rows, :].astype(F32))
        res_t[...] = d_r2

        @pl.when(start)
        def _():
            weights[0][1]()
            fetch[2].wait()

        def widen_back(f):
            fs = pl.ds(pl.multiple_of(f * FC, FC), FC)
            du = (mm(d_br[rows, :], wd[fs, :], NT) * d_up[rows, fs].astype(F32)).astype(BF)
            d_up[rows, fs] = du
            g_bu[:, fs] += jnp.sum(du.astype(F32), axis=0, keepdims=True)

        loop(FF // FC, widen_back)
        for i in (0, 5):
            save(t, i).start()

        @pl.when(start)
        def _():
            weights[1][1]()
            fetch[3].wait()
            fetch[4].wait()

        d_h = res_t[...] + mm(d_up[rows, :], wu[...])
        d_r1 = norm_back(d_h, n1[rows, :], rs1[rows, 0:1], V_G1, V_C1)
        d_proj[rows, :] = d_r1.astype(BF)
        res_t[...] = d_r1
        add_vec(V_BO, d_proj[rows, :].astype(F32))
        save(t, 4).start()

        @pl.when(start)
        def _():
            weights[2][1]()
            for i in range(5, 9):
                fetch[i].wait()

        d_h_t[...] = mm(d_proj[rows, :], wo[...], NT).astype(BF)

        def attend_back(c):
            cr = pl.ds(pl.multiple_of(c * CL, CL), CL)
            gr = pl.ds(pl.multiple_of(t * TM + c * CL, CL), CL)
            pairs = [slice(p * PW, (p + 1) * PW) for p in range(PAIRS)]
            probs = [p_all[t * (TM // CL) + c, p] for p in range(PAIRS)]
            d_heads = [d_h_t[cr, ps] for ps in pairs]
            d_probs = [mm(apart(v[gr, ps]), dh, NT) for ps, dh in zip(pairs, d_heads)]
            d_values = [mm(w, dh) for w, dh in zip(probs, d_heads)]
            d_scores = []
            for w, dw in zip(probs, d_probs):
                halves = []
                for h in range(2):
                    wh = w[h * CL : (h + 1) * CL].astype(F32)
                    dwh = dw[h * CL : (h + 1) * CL]
                    halves.append((wh * (dwh - jnp.sum(dwh * wh, axis=0, keepdims=True))).astype(BF))
                d_scores.append(jnp.concatenate(halves, axis=0))
            d_keys = [mm(ds, q[gr, ps]) for ps, ds in zip(pairs, d_scores)]
            d_queries = [mm(ds, apart(k[gr, ps]), TN) for ps, ds in zip(pairs, d_scores)]
            for ps, dq, dk, dv in zip(pairs, d_queries, d_keys, d_values):
                q[gr, ps] = (dq * inv).astype(BF)
                k[gr, ps] = jnp.where(first_half, dk[0:CL], dk[CL:]).astype(BF)
                v[gr, ps] = jnp.where(first_half, dv[0:CL], dv[CL:]).astype(BF)

        loop(TM // CL, attend_back)
        for i in (1, 2, 3):
            save(t, i).start()
        add_vec(V_BQ, q[rows, :].astype(F32))
        add_vec(V_BV, v[rows, :].astype(F32))
        pl.when(start)(weights[3][1])
        d_x = (
            mm(q[rows, :], wqkv[0:D, :], NT)
            + mm(k[rows, :], wqkv[D : 2 * D, :], NT)
            + mm(v[rows, :], wqkv[2 * D :, :], NT)
        )
        ing_c[rows, :] = (res_t[...] + d_x.astype(BF).astype(F32)).astype(BF)

    loop(ROWS // TM, tile)

    for j, back in enumerate((back_0, back_1, back_2, back_3)):
        back[...] = mm(seat_part(meta, j, cap), ing_c[...], TN).astype(BF)

    for chunk in range(72):
        row, lane = chunk // 6, chunk % 6 * 128
        if row < 8:
            part = gvec[row : row + 1, lane : lane + 128]
        else:
            lane += (row - 8) * D
            part = g_bu[:, lane : lane + 128]
        shares[chunk // 9, chunk % 9 : chunk % 9 + 1, :] = part

    def saved_all(t):
        for i in range(len(saved)):
            save(t, i).wait()

    loop(ROWS // TM, saved_all)


def backward(cap, positions, slots, vecs, meta, cots, saved):
    rows, wide, probs, full, thin = saved_shapes()
    dma = pltpu.SemaphoreType.DMA
    grads = (wide, rows, rows, rows, rows, rows)
    return pl.pallas_call(
        functools.partial(backward_kernel, cap),
        out_shape=(shape_of(BF, cap, D),) * SD
        + (shape_of(F32, 8, 16, 128),)
        + tuple(shape_of(kind, *shape) for shape, kind in grads),
        in_specs=[SMEM, ANY, VMEM, VMEM] + [ANY] * (SD + 9),
        out_specs=(VMEM,) * (SD + 1) + (ANY,) * len(grads),
        scratch_shapes=[
            pltpu.VMEM((3 * D, D), BF),
            pltpu.VMEM((D, D), BF),
            pltpu.VMEM((FF, D), BF),
            pltpu.VMEM((FF, D), BF),
            pltpu.VMEM((SD, cap, D), BF),
        ]
        + [pltpu.VMEM(*a) for a in (rows, rows, rows, probs, wide, full, full, thin, thin, rows, rows, rows)]
        + [
            pltpu.VMEM((TM, D), BF),
            pltpu.VMEM((TM, D), F32),
            pltpu.VMEM((8, D), F32),
            pltpu.VMEM((1, FF), F32),
            dma((4,)),
            dma((4,)),
            dma((9,)),
            dma((6,)),
        ],
        compiler_params=pltpu.CompilerParams(vmem_limit_bytes=VMEM_LIMIT),
        cost_estimate=pl.CostEstimate(flops=2 * ROWS * WROWS * D, bytes_accessed=64 << 20, transcendentals=0),
        name="backward",
    )(positions, slots, vecs, meta, *cots, *saved)


WC = 8 * BLK


def weight_kernel(
    pos,
    x_h,
    heads_h,
    act_h,
    d_up_h,
    d_q_h,
    d_k_h,
    d_v_h,
    d_proj_h,
    hid_h,
    d_br_h,
    grads,
    x_c,
    heads,
    act,
    d_up,
    d_q,
    d_k,
    d_v,
    d_proj,
    hid,
    d_br,
    stage,
    i_sem,
    g_sem,
):
    refs = (
        (x_h, x_c),
        (d_q_h, d_q),
        (d_k_h, d_k),
        (d_v_h, d_v),
        (heads_h, heads),
        (d_proj_h, d_proj),
        (hid_h, hid),
        (d_up_h, d_up),
        (d_br_h, d_br),
        (act_h, act),
    )
    fetch = [pltpu.make_async_copy(src, dst, i_sem.at[i]) for i, (src, dst) in enumerate(refs)]
    for copy in fetch:
        copy.start()

    per = WC // BLK

    def g_copy(chunk, j, at):
        return pltpu.make_async_copy(
            stage.at[at, pl.ds(j * BLK, BLK)], grads.at[pos[chunk * per + j]], g_sem.at[at]
        )

    def put(chunk, left, right):
        at = lax.rem(chunk, 2)

        @pl.when(chunk >= 2)
        def _():
            for j in range(per):
                g_copy(chunk - 2, j, at).wait()

        stage[at] = mm(left, right, TN).astype(BF)
        for j in range(per):
            g_copy(chunk, j, at).start()

    first = 0
    for left, right, needs in (
        (x_c, d_q, (0, 1)),
        (x_c, d_k, (2,)),
        (x_c, d_v, (3,)),
        (heads, d_proj, (4, 5)),
        (d_up, hid, (6, 7)),
        (act, d_br, (8, 9)),
    ):
        for i in needs:
            fetch[i].wait()

        def body(j, left=left, right=right, first=first):
            put(first + j, left[:, pl.ds(pl.multiple_of(j * WC, WC), WC)], right[...])

        loop(left.shape[1] // WC, body)
        first += left.shape[1] // WC
    for chunk in (first - 2, first - 1):
        for j in range(per):
            g_copy(chunk, j, chunk % 2).wait()


def weight_grads_of(total_slots, positions, x_c, saved):
    r_v, w_v = pltpu.VMEM((ROWS, D), BF), pltpu.VMEM((ROWS, FF), BF)
    return pl.pallas_call(
        weight_kernel,
        out_shape=jax.ShapeDtypeStruct((total_slots, BLK, D), BF),
        in_specs=[SMEM] + [ANY] * 10,
        out_specs=ANY,
        scratch_shapes=[r_v, r_v, w_v, w_v]
        + [r_v] * 6
        + [
            pltpu.VMEM((2, WC, D), BF),
            pltpu.SemaphoreType.DMA((10,)),
            pltpu.SemaphoreType.DMA((2,)),
        ],
        compiler_params=pltpu.CompilerParams(vmem_limit_bytes=VMEM_LIMIT),
        cost_estimate=pl.CostEstimate(flops=2 * ROWS * WROWS * D, bytes_accessed=40 << 20, transcendentals=0),
        name="weight_grads",
    )(positions, x_c, *saved)


def local(
    tokens,
    cotangent,
    cluster_order,
    block_owner,
    master_slots,
    moment_one,
    moment_two,
    vector_master,
    vector_moment_one,
    vector_moment_two,
):
    tok_count = lax.axis_size("tok")
    tok_index = lax.axis_index("tok")
    slot_count = master_slots.shape[0]
    cap = tok_count // SD * (max(1, CPS // tok_count) * 3 * CL // (2 * SD))
    total_slots = tok_count * slot_count
    order = cluster_order.reshape(1, ROWS)

    block = jax.ShapeDtypeStruct((SD, cap, D), BF)
    meta_shape = jax.ShapeDtypeStruct((SD, META, D), BF)
    row_block = jax.ShapeDtypeStruct((ROWS, D), BF)
    four_planes = tok_count == 8 and lax.axis_size("rep") == 4
    if four_planes:
        slots_low, x_c, *cots, recv_meta, vecs, b_u, occupancy, positions = gather_all(
            cap, tokens, cotangent, order, master_slots, vector_master, block_owner
        )
        positions = positions.reshape(NBLK)
        slots_low = slots_low.reshape(total_slots, BLK, D)
    else:
        positions = slot_positions(block_owner, slot_count)
        slots_low = lax.all_gather(master_slots.astype(BF), "tok", axis=0, tiled=True)
        vectors = lax.all_gather(vector_master.astype(BF), "tok", axis=0, tiled=True).astype(F32)
        vecs, b_u = vectors[: 8 * D].reshape(8, D), vectors[8 * D :].reshape(1, FF)
        cluster = tok_index // SD * CPS + cluster_order // CL
        target = cluster % tok_count
        chosen = target[None, :] == jnp.arange(tok_count, dtype=jnp.int32)[:, None]
        sent_counts = jnp.sum(chosen.astype(F32), axis=1)
        own_row = (jnp.arange(tok_count, dtype=jnp.int32) == tok_index).astype(F32)
        occupancy = lax.psum(own_row[:, None] * sent_counts[None, :], ("tok", "rep")).astype(jnp.int32)
        send_x, send_c, meta = pl.pallas_call(
            functools.partial(send_kernel, cap),
            out_shape=(block, block, meta_shape),
            in_specs=[VMEM] * 3,
            out_specs=(VMEM,) * 3,
            compiler_params=pltpu.CompilerParams(vmem_limit_bytes=VMEM_LIMIT),
            name="send_rows",
        )(tokens, cotangent, order)
        recv_x, recv_meta = (jnp.stack(swap_blocks(b)) for b in (send_x, meta))
        x_c = pl.pallas_call(
            functools.partial(seat_kernel, cap),
            out_shape=row_block,
            in_specs=[VMEM] * 2,
            out_specs=VMEM,
            compiler_params=pltpu.CompilerParams(vmem_limit_bytes=VMEM_LIMIT),
            name="seat_rows",
        )(recv_x, recv_meta)
        cots = [send_c[k] for k in range(SD)]

    cots = swap_blocks(cots)
    *out_blocks, heads, act, hid, q, k, v, p, slope, n1, n2, rs1, rs2 = forward(
        cap, positions, slots_low, vecs, b_u, x_c, recv_meta
    )
    out_blocks = swap_blocks(out_blocks)
    *ing_blocks, shares, d_up, d_q, d_k, d_v, d_proj, d_br = backward(
        cap, positions, slots_low, vecs, recv_meta, cots, (q, k, v, p, slope, n1, n2, rs1, rs2)
    )
    ing_blocks = swap_blocks(ing_blocks)
    grads = weight_grads_of(
        total_slots, positions, x_c, (heads, act, d_up, d_q, d_k, d_v, d_proj, hid, d_br)
    )
    if four_planes:
        total, vec_owned, output, input_grad, entropy = reduce_all(
            cap, grads, shares, order, out_blocks, ing_blocks, slot_count
        )
    else:
        total = lax.psum(lax.psum_scatter(grads, "tok", scatter_dimension=0, tiled=True), "rep")
        grad_vector = shares[:, 0:9].reshape(-1)
        vec_owned = lax.psum(lax.psum_scatter(grad_vector, "tok", scatter_dimension=0, tiled=True), "rep")
        output, input_grad, entropy = pl.pallas_call(
            functools.partial(return_kernel, cap),
            out_shape=(row_block, row_block, jax.ShapeDtypeStruct((1, ROWS), BF)),
            in_specs=[VMEM] * (2 * SD + 1),
            out_specs=(VMEM,) * 3,
            compiler_params=pltpu.CompilerParams(vmem_limit_bytes=VMEM_LIMIT),
            name="return_rows",
        )(order, *out_blocks, *ing_blocks)

    used = jnp.any(
        positions[None, :] == (tok_index * slot_count + jnp.arange(slot_count, dtype=I32))[:, None], axis=1
    )
    owned_grad = jnp.where(used[:, None, None], total.astype(F32), 0.0)
    first_new, second_new, master_new = adam_update(
        owned_grad, master_slots, moment_one, moment_two, rate_matrix
    )
    vec_first, vec_second, vec_new = adam_update(
        vec_owned, vector_master, vector_moment_one, vector_moment_two, rate_vector
    )
    return (
        output,
        input_grad,
        owned_grad,
        first_new,
        second_new,
        master_new,
        master_new.astype(BF),
        vec_owned,
        vec_first,
        vec_second,
        vec_new,
        vec_new.astype(BF),
        entropy.reshape(-1),
        occupancy,
    )


def solution(mesh):
    placed = (
        P(("rep", "tok"), None),
        P(("rep", "tok"), None),
        P(("rep", "tok")),
        P(),
        P("tok", None, None),
        P("tok", None, None),
        P("tok", None, None),
        P("tok"),
        P("tok"),
        P("tok"),
    )
    return jax.shard_map(
        local,
        mesh=mesh,
        in_specs=placed,
        out_specs=(
            P(("rep", "tok"), None),
            P(("rep", "tok"), None),
            P("tok", None, None),
            P("tok", None, None),
            P("tok", None, None),
            P("tok", None, None),
            P("tok", None, None),
            P("tok"),
            P("tok"),
            P("tok"),
            P("tok"),
            P("tok"),
            P(("rep", "tok")),
            P(),
        ),
        check_vma=False,
    )
```

```python
import functools
import math

import jax
import jax.numpy as jnp
from jax import lax
from jax.experimental import pallas as pl
from jax.experimental.pallas import tpu as pltpu
from jax.sharding import PartitionSpec as P

D = 768
HEADS = 12
HD = 64
FF = 3072
SD = 4
CL = 128
NBLK = 96
STEP = 10
CPS = 32
WROWS = 9216
BLK = 96
ROWS = 1024
PAIRS = HEADS // 2
PW = 2 * HD
TM = 512
PART = 48
META = 16
VMEM_LIMIT = 63 << 20
FC = 768
FWD_AT = 4
BWD_AT = 2

norm_epsilon = 1e-06
beta_first = 0.9
beta_second = 0.999
adam_epsilon = 1e-08
weight_decay = 0.01
rate_matrix = 0.02
rate_vector = 0.2

BF = jnp.bfloat16
F32 = jnp.float32
I32 = jnp.int32

VMEM = pl.BlockSpec(memory_space=pltpu.VMEM)
SMEM = pl.BlockSpec(memory_space=pltpu.SMEM)
ANY = pl.BlockSpec(memory_space=pl.ANY)

NN = (((1,), (0,)), ((), ()))
NT = (((1,), (1,)), ((), ()))
TN = (((0,), (0,)), ((), ()))


def mm(a, b, dims=NN):
    return lax.dot_general(a, b, dims, preferred_element_type=F32)


def slot_positions(block_owner, slot_count):
    owners = block_owner[:, 0]
    blocks = owners.shape[0]
    shared = owners[:, None] == owners[None, :]
    before = (
        jnp.arange(blocks, dtype=jnp.int32)[None, :] < jnp.arange(blocks, dtype=jnp.int32)[:, None]
    )
    earlier = jnp.sum((shared & before).astype(jnp.int32), axis=1)
    return owners * slot_count + earlier


def adam_update(grad_now, weight_old, first_old, second_old, rate_step):
    first_new = beta_first * first_old + (1.0 - beta_first) * grad_now
    second_new = beta_second * second_old + (1.0 - beta_second) * grad_now * grad_now
    first_hat = first_new / (1.0 - beta_first**STEP)
    second_hat = second_new / (1.0 - beta_second**STEP)
    weight_new = weight_old - rate_step * (
        first_hat / (jnp.sqrt(second_hat) + adam_epsilon) + weight_decay * weight_old
    )
    return (first_new, second_new, weight_new)


def route_slots(order, seat, cap):
    cluster = order // CL
    rel = lax.rem(cluster, SD) ^ seat
    place = (cluster // SD) * CL + lax.rem(order, CL) + 1
    chosen = lax.broadcasted_iota(I32, (8, ROWS), 0) == rel
    chosen_low = jnp.where(chosen, 1.0, 0.0).astype(BF)
    before = lax.broadcasted_iota(I32, (ROWS, ROWS), 0) < lax.broadcasted_iota(I32, (ROWS, ROWS), 1)
    before_low = jnp.where(before, 1.0, 0.0).astype(BF)
    running = mm(chosen_low, before_low)
    rank = jnp.sum(jnp.where(chosen, running, 0.0), axis=0, keepdims=True).astype(I32)
    return rel * cap + rank, place


def slot_matrix(slots, at, cap):
    rows = lax.broadcasted_iota(I32, (cap, ROWS), 0) + at * cap
    return jnp.where(rows == slots, 1.0, 0.0).astype(BF)


def send_kernel(cap, tokens, cotangent, order, send_x, send_c, meta):
    seat = lax.rem(lax.axis_index("tok"), SD)
    slots, place = route_slots(order[...], seat, cap)
    digits = jnp.concatenate([place // CL, lax.rem(place, CL)] + [place * 0] * 6, axis=0).astype(F32).astype(BF)
    for at in range(SD):
        picked = slot_matrix(slots, at, cap)
        send_x[at] = mm(picked, tokens[...]).astype(BF)
        send_c[at] = mm(picked, cotangent[...]).astype(BF)
        coded = mm(digits, picked, NT)
        line = jnp.concatenate([coded[0:1], coded[1:2]], axis=1)
        meta[at] = jnp.broadcast_to(line, (META, D)).astype(BF)


def remote(src, dst, send_sem, recv_sem, tok, rep):
    return pltpu.make_async_remote_copy(
        src_ref=src,
        dst_ref=dst,
        send_sem=send_sem,
        recv_sem=recv_sem,
        device_id={"tok": tok, "rep": rep},
        device_id_type=pl.DeviceIdType.MESH,
    )


def loop(n, body):
    def run(i, c):
        body(i)
        return c

    lax.fori_loop(0, n, run, 0)


class Place:
    def __init__(self):
        self.me = me = lax.axis_index("tok")
        self.z = z = lax.axis_index("rep")
        core, x, y = me % 2, (me // 2) % 2, me // 4
        self.twin = me + 1 - 2 * core
        self.xn = me + 2 - 4 * x
        self.yn = me + 4 - 8 * y
        self.dn = self.xn + 4 - 8 * y
        self.side = z % 2
        self.zp = z + 1 - 2 * self.side

    def twin_of(self, tok):
        return tok + 1 - 2 * (tok % 2)

    def greet(self, peers):
        barrier = pltpu.get_barrier_semaphore()
        for tok, rep in peers:
            pl.semaphore_signal(
                barrier, inc=1, device_id={"tok": tok, "rep": rep}, device_id_type=pl.DeviceIdType.MESH
            )
        return lambda: pl.semaphore_wait(barrier, len(peers))


def seat_matrix(meta, first, rows, cap):
    hi = jnp.concatenate([meta[k, 0:8, 0:cap] for k in range(SD)], axis=1).astype(F32)[0:1]
    lo = jnp.concatenate([meta[k, 0:8, cap : 2 * cap] for k in range(SD)], axis=1).astype(F32)[0:1]
    at = (hi * CL + lo).astype(I32)
    seats = lax.broadcasted_iota(I32, (rows, SD * cap), 0) + (first + 1)
    return jnp.where(seats == at, 1.0, 0.0).astype(BF)


def seat_part(meta, k, cap):
    hi = meta[k, 0:8, 0:cap].astype(F32)[0:1]
    lo = meta[k, 0:8, cap : 2 * cap].astype(F32)[0:1]
    at = (hi * CL + lo).astype(I32)
    seats = lax.broadcasted_iota(I32, (ROWS, cap), 0) + 1
    return jnp.where(seats == at, 1.0, 0.0).astype(BF)


def seat_rows(meta, blocks, cap, to):
    def body(t):
        r0 = pl.multiple_of(t * 256, 256)
        rows = blocks[...].reshape(SD * cap, D)
        to[pl.ds(r0, 256), :] = mm(seat_matrix(meta, r0, 256, cap), rows).astype(BF)

    loop(ROWS // 256, body)


def seat_kernel(cap, blocks, meta, to):
    seat_rows(meta, blocks, cap, to)


def gather_kernel(
    cap,
    count,
    tokens_h,
    cotangent_h,
    order,
    master_h,
    vector,
    owner_of,
    slots,
    x_c,
    cot_0,
    cot_1,
    cot_2,
    cot_3,
    recv_meta,
    vecs,
    b_u,
    occupancy,
    positions,
    tokens,
    cotangent,
    master,
    own,
    send_x,
    send_c,
    meta,
    recv_x,
    got_meta,
    slot_of,
    digits,
    mine,
    by_z,
    by_tok,
    x_s,
    x_r,
    y_s,
    y_r,
    d_s,
    d_r,
    zx_s,
    zx_r,
    zd_s,
    zd_r,
    zy_s,
    zy_r,
    p_s,
    p_r,
    row_s,
    row_r,
    z_s,
    z_r,
    t_s,
    t_r,
    local_s,
):
    at = Place()
    me, z, side = at.me, at.z, at.side
    n_tok, n_rep = 8, 4
    peers = [((me + d) % n_tok, z) for d in range(1, n_tok)] + [(me, (z + d) % n_rep) for d in range(1, n_rep)]
    fetch = [
        pltpu.make_async_copy(src, dst, local_s.at[i])
        for i, (src, dst) in enumerate(((master_h, master), (tokens_h, tokens), (cotangent_h, cotangent)))
    ]
    for copy in fetch:
        copy.start()
    wait_peers = at.greet(peers)
    fetch[0].wait()

    last = count - 1

    def near(j):
        return side * last + (1 - 2 * side) * j

    def far(j):
        return (1 - side) * last - (1 - 2 * side) * j

    few_x, few_d, few_y = 11 * count // 26, 12 * count // 26, 8 * count // 26
    most_x, most_d, most_y = count - few_x, count - few_d, count - few_y

    def piece(owner, s):
        return slots.at[owner * count + s]

    def to_x(s):
        return remote(own.at[s], piece(me, s), x_s.at[s], x_r.at[s], at.xn, z)

    def to_y(s):
        return remote(own.at[s], piece(me, s), y_s.at[s], y_r.at[s], at.yn, z)

    def on_y(s):
        return remote(piece(at.xn, s), piece(at.xn, s), d_s.at[s], d_r.at[s], at.yn, z)

    def x_on_z(s):
        return remote(piece(at.xn, s), piece(at.xn, s), zx_s.at[s], zx_r.at[s], me, at.zp)

    def d_on_z(s):
        return remote(piece(at.dn, s), piece(at.dn, s), zd_s.at[s], zd_r.at[s], me, at.zp)

    def y_on_z(s):
        return remote(piece(at.yn, s), piece(at.yn, s), zy_s.at[s], zy_r.at[s], me, at.zp)

    def x_in(s):
        return remote(own.at[s], piece(at.xn, s), x_s.at[s], x_r.at[s], at.xn, z)

    def y_in(s):
        return remote(own.at[s], piece(at.yn, s), y_s.at[s], y_r.at[s], at.yn, z)

    def d_in(s):
        return remote(own.at[s], piece(at.dn, s), d_s.at[s], d_r.at[s], at.yn, z)

    owners = (me, at.xn, at.yn, at.dn)

    def near_run(q, j0, j1):
        return (q, (1 - side) * j0 + side * (count - j1), j1 - j0)

    def far_run(q, j0, j1):
        return (q, side * j0 + (1 - side) * (count - j1), j1 - j0)

    runs = (
        (0, 0, count),
        near_run(2, 0, few_y),
        near_run(1, 0, most_x),
        near_run(3, 0, most_d),
        far_run(1, 0, few_x),
        near_run(2, few_y, most_y),
        far_run(2, 0, few_y),
        far_run(3, 0, few_d // 2),
        far_run(3, few_d // 2, few_d - 2),
        far_run(3, few_d - 2, few_d),
    )

    def to_twin(i):
        q, s, n = runs[i]
        src = own if q == 0 else slots.at[pl.ds(owners[q] * count + s, n)]
        dst = slots.at[pl.ds(owners[q] * count + s, n)]
        return remote(src, dst, p_s.at[i], p_r.at[i], at.twin, z)

    def cast(j):
        own[near(j)] = master[near(j)].astype(BF)

    loop(most_x, cast)
    wait_peers()
    loop(most_x, lambda j: to_x(near(j)).start())
    loop(few_y, lambda j: to_y(near(j)).start())
    loop(count - most_x, lambda j: cast(most_x + j))
    to_twin(0).start()
    keep = pltpu.make_async_copy(own, slots.at[pl.ds(me * count, count)], local_s.at[3])
    keep.start()

    seat = me % SD
    seats = (me, at.twin, at.xn, at.twin_of(at.xn))
    rows_of = ((meta, got_meta), (send_x, recv_x))

    def row_copy(i, k):
        src, dst = rows_of[i]
        return remote(src.at[k], dst.at[k], row_s.at[i, k], row_r.at[i, k], seats[k], z)

    put_c = [
        pltpu.make_async_copy(send_c.at[k], to, local_s.at[4 + k])
        for k, to in enumerate((cot_0, cot_1, cot_2, cot_3))
    ]

    def route():
        fetch[1].wait()
        fetch[2].wait()
        slots_here, place = route_slots(order[...], seat, cap)
        slot_of[...] = slots_here
        digits[...] = (
            jnp.concatenate([place // CL, lax.rem(place, CL)] + [place * 0] * 6, axis=0).astype(F32).astype(BF)
        )

    def sort_tokens(k):
        picked = slot_matrix(slot_of[...], k, cap)
        send_x[k] = mm(picked, tokens[...]).astype(BF)
        coded = mm(digits[...], picked, NT)
        line = jnp.concatenate([coded[0:1], coded[1:2]], axis=1)
        meta[k] = jnp.broadcast_to(line, (META, D)).astype(BF)
        for i in range(2):
            if k:
                row_copy(i, k).start()
            else:
                src, dst = rows_of[i]
                dst[0] = src[0]

    def sort_cotangent(k):
        send_c[k] = mm(slot_matrix(slot_of[...], k, cap), cotangent[...]).astype(BF)
        put_c[k].start()

    def z_copy(d):
        return remote(by_z.at[0], by_z.at[d], z_s.at[d], z_r.at[d], me, (z + d) % n_rep)

    def t_copy(d):
        return remote(mine, by_tok.at[d], t_s.at[d], t_r.at[d], (me + d) % n_tok, z)

    def count_rows():
        residue = lax.rem(me // SD * CPS + order[...] // CL, n_tok)
        hit = lax.broadcasted_iota(I32, (128, ROWS), 0) == residue
        by_z[0] = mm(jnp.ones((8, ROWS), BF), jnp.where(hit, 1.0, 0.0).astype(BF), NT)
        for d in range(1, n_rep):
            z_copy(d).start()
        for i in range(9):
            mine[i : i + 1] = vector[i * 128 : (i + 1) * 128].reshape(1, 128).astype(BF).astype(F32)
        block_row = lax.broadcasted_iota(I32, (NBLK, NBLK), 0)
        block_col = lax.broadcasted_iota(I32, (NBLK, NBLK), 1)
        by_col = owner_of[...].astype(F32)
        by_row = lane_sum(jnp.where(block_row == block_col, by_col, 0.0))
        earlier = jnp.where((by_row == by_col) & (block_row < block_col), 1.0, 0.0)
        positions[...] = (by_col * (count * PART // BLK) + jnp.sum(earlier, axis=0, keepdims=True)).astype(I32)

    def share_vectors():
        for d in range(1, n_rep):
            z_copy(d).wait()
        mine[16:24] = by_z[0] + by_z[1] + by_z[2] + by_z[3]
        for d in range(1, n_tok):
            t_copy(d).start()

    def lay_out_vectors():
        by_tok[0] = mine[...]
        for d in range(1, n_tok):
            t_copy(d).wait()
        for owner in range(n_tok):
            share = by_tok[(me + n_tok - owner) % n_tok]
            occupancy[owner : owner + 1, :] = share[16:17, 0:n_tok].astype(I32)
            for i in range(9):
                chunk = owner * 9 + i
                row, lane = chunk // 6, chunk % 6 * 128
                if row < 8:
                    vecs[row : row + 1, lane : lane + 128] = share[i : i + 1]
                else:
                    lane += (row - 8) * D
                    b_u[:, lane : lane + 128] = share[i : i + 1]

    between = {
        1: lambda: (route(), sort_tokens(2)),
        3: lambda: sort_tokens(3),
        5: lambda: sort_tokens(1),
        7: lambda: (sort_tokens(0), count_rows()),
        9: lambda: sort_cotangent(1),
        11: lambda: sort_cotangent(2),
        13: lambda: sort_cotangent(3),
    }
    for j in range(most_x):
        x_in(near(j)).wait_recv()
        if j < most_d:
            on_y(near(j)).start()
        if j < few_x:
            x_on_z(near(j)).start()
        if j < few_y:
            y_in(near(j)).wait_recv()
            y_on_z(near(j)).start()
        if j == few_y:
            to_twin(1).start()
        if j in between:
            between[j]()
    to_twin(2).start()
    loop(most_y - few_y, lambda j: to_y(near(few_y + j)).start())
    share_vectors()
    sort_cotangent(0)

    def diagonal(j):
        d_in(near(j)).wait_recv()
        d_on_z(near(j)).start()

    loop(few_d, diagonal)
    loop(most_d - few_d, lambda j: d_in(near(few_d + j)).wait_recv())
    to_twin(3).start()
    loop(few_x, lambda j: x_on_z(far(j)).wait_recv())
    to_twin(4).start()
    lay_out_vectors()
    loop(most_y - few_y, lambda j: y_in(near(few_y + j)).wait_recv())
    to_twin(5).start()
    loop(few_y, lambda j: y_on_z(far(j)).wait_recv())
    to_twin(6).start()
    for i in (0, 1):
        for k in (2, 3, 1):
            row_copy(i, k).wait_recv()
    recv_meta[...] = got_meta[...]
    seat_rows(got_meta, recv_x, cap, x_c)
    done = 0
    for i, upto in ((7, few_d // 2), (8, few_d - 2), (9, few_d)):
        loop(upto - done, lambda j, done=done: d_on_z(far(done + j)).wait_recv())
        to_twin(i).start()
        done = upto

    for i in range(2):
        for k in (2, 3, 1):
            row_copy(i, k).wait_send()
    for copy in put_c:
        copy.wait()
    keep.wait()

    loop(most_x, lambda j: to_x(near(j)).wait_send())
    loop(most_y, lambda j: to_y(near(j)).wait_send())
    loop(most_d, lambda j: on_y(near(j)).wait_send())
    loop(few_x, lambda j: x_on_z(near(j)).wait_send())
    loop(few_d, lambda j: d_on_z(near(j)).wait_send())
    loop(few_y, lambda j: y_on_z(near(j)).wait_send())
    for i in range(len(runs)):
        to_twin(i).wait()


def gather_all(cap, tokens, cotangent, order, master, vector, block_owner):
    count = master.shape[0] * BLK // PART
    rows = jax.ShapeDtypeStruct((ROWS, D), BF)
    part = jax.ShapeDtypeStruct((cap, D), BF)
    dma = pltpu.SemaphoreType.DMA
    block = pltpu.VMEM((SD, cap, D), BF)
    meta = pltpu.VMEM((SD, META, D), BF)
    return pl.pallas_call(
        functools.partial(gather_kernel, cap, count),
        out_shape=(
            jax.ShapeDtypeStruct((8 * count, PART, D), BF),
            rows,
            part,
            part,
            part,
            part,
            jax.ShapeDtypeStruct((SD, META, D), BF),
            jax.ShapeDtypeStruct((8, D), F32),
            jax.ShapeDtypeStruct((1, FF), F32),
            jax.ShapeDtypeStruct((8, 8), I32),
            jax.ShapeDtypeStruct((1, NBLK), I32),
        ),
        in_specs=[ANY, ANY, VMEM, ANY, VMEM, VMEM],
        out_specs=(ANY, VMEM) + (ANY,) * SD + (VMEM,) * 5,
        scratch_shapes=[
            pltpu.VMEM((ROWS, D), BF),
            pltpu.VMEM((ROWS, D), BF),
            pltpu.VMEM((count, PART, D), F32),
            pltpu.VMEM((count, PART, D), BF),
            block,
            block,
            meta,
            block,
            meta,
            pltpu.VMEM((1, ROWS), I32),
            pltpu.VMEM((8, ROWS), BF),
            pltpu.VMEM((24, 128), F32),
            pltpu.VMEM((4, 8, 128), F32),
            pltpu.VMEM((8, 24, 128), F32),
        ]
        + [dma((count,))] * 12
        + [dma((10,))] * 2
        + [dma((2, SD))] * 2
        + [dma((4,))] * 2
        + [dma((8,))] * 2
        + [dma((8,))],
        compiler_params=pltpu.CompilerParams(collective_id=0, has_side_effects=True, vmem_limit_bytes=VMEM_LIMIT),
        cost_estimate=pl.CostEstimate(flops=8 * ROWS * ROWS * D, bytes_accessed=64 << 20, transcendentals=0),
        name="gather",
    )(tokens, cotangent, order, master.reshape(count, PART, D), vector, block_owner.reshape(1, NBLK))


def return_kernel(cap, order, *refs):
    outs, ings, (out, ing, entropy) = refs[:SD], refs[SD : 2 * SD], refs[2 * SD :]
    seat = lax.rem(lax.axis_index("tok"), SD)
    slots, _ = route_slots(order[...], seat, cap)
    picked = jnp.concatenate([slot_matrix(slots, at, cap) for at in range(SD)], axis=0)
    for to, blocks in ((out, outs), (ing, ings)):
        rows = jnp.concatenate([block[0:cap, :] for block in blocks], axis=0)
        to[...] = mm(picked, rows, TN).astype(BF)
    line = jnp.concatenate([block[cap : cap + 8, 0:cap] for block in outs], axis=1)
    entropy[...] = mm(line, picked)[0:1].astype(BF)


def swap_blocks(blocks):
    n = lax.axis_size("tok")
    parts = [blocks[0]]
    for k in range(1, SD):
        parts.append(lax.ppermute(blocks[k], "tok", [(i, i ^ k) for i in range(n)]))
    return parts


def reduce_kernel(
    cap,
    count,
    split,
    grads,
    vec,
    order,
    out_0,
    out_1,
    out_2,
    out_3,
    ing_0,
    ing_1,
    ing_2,
    ing_3,
    total,
    vec_out,
    output,
    input_grad,
    entropy,
    out_v,
    ing_v,
    slot_of,
    a,
    tw,
    rd,
    rx,
    ry,
    o,
    rz1,
    pz,
    rz2,
    fz,
    vt,
    va,
    vb,
    vc,
    a_l,
    keep_l,
    p_s,
    p_r,
    d_s,
    d_r,
    x_s,
    x_r,
    y_s,
    y_r,
    z1_s,
    z1_r,
    z2_s,
    z2_r,
    z3_s,
    z3_r,
    t_s,
    t_r,
    v_s,
    v_r,
    row_l,
):
    at = Place()
    me, z = at.me, at.z
    n_tok, n_rep = 8, 4
    peers = [((me + d) % n_tok, z) for d in range(1, n_tok)] + [(me, (z + d) % n_rep) for d in range(1, n_rep)]
    wait_peers = at.greet(peers)
    owners = (me, at.xn, at.yn, at.dn)

    def load(q):
        return pltpu.make_async_copy(grads.at[pl.ds(owners[q] * count, count)], a.at[q], a_l.at[q])

    for q in (3, 1, 2, 0):
        load(q).start()
    rows_in = [
        pltpu.make_async_copy(src, to.at[k], row_l.at[i, k])
        for i, (blocks, to) in enumerate((((out_0, out_1, out_2, out_3), out_v), ((ing_0, ing_1, ing_2, ing_3), ing_v)))
        for k, src in enumerate(blocks)
    ]
    for copy in rows_in:
        copy.start()
    wait_peers()

    groups = [(g, g * (count // 4), count // 4 if g < 3 else count - 3 * (count // 4)) for g in range(4)]

    def to_twin(q, group):
        g, s, n = group
        src = grads.at[pl.ds(at.twin_of(owners[q]) * count + s, n)]
        return remote(src, tw.at[q, pl.ds(s, n)], p_s.at[q, g], p_r.at[q, g], at.twin, z)

    def d_y(s):
        return remote(a.at[3, s], rd.at[s], d_s.at[s], d_r.at[s], at.yn, z)

    def d_x(s):
        return remote(a.at[3, s], rd.at[s], d_s.at[s], d_r.at[s], at.xn, z)

    def to_x(s):
        return remote(a.at[1, s], rx.at[s], x_s.at[s], x_r.at[s], at.xn, z)

    def to_y(s):
        return remote(a.at[2, s], ry.at[s], y_s.at[s], y_r.at[s], at.yn, z)

    def z_in(s):
        return remote(o.at[s], rz1.at[s], z1_s.at[s], z1_r.at[s], me, at.zp)

    def z_swap(s):
        return remote(pz.at[s], rz2.at[s], z2_s.at[s], z2_r.at[s], me, n_rep - 1 - z)

    def z_out(s):
        return remote(fz.at[s], fz.at[s], z3_s.at[s], z3_r.at[s], me, at.zp)

    def keep(s):
        return pltpu.make_async_copy(fz.at[s], total.at[s], keep_l.at[s])

    for group in groups:
        for q in (3, 1, 2, 0):
            to_twin(q, group).start()

    def v_tok(d):
        return remote(vec.at[(me + d) % n_tok], vt.at[d], t_s.at[d], t_r.at[d], (me + d) % n_tok, z)

    def v_rep(i, src):
        return remote(src, vb.at[i], v_s.at[i], v_r.at[i], me, at.zp if i == 0 else (z + 2) % n_rep)

    for d in range(1, n_tok):
        v_tok(d).start()

    def join(q, s):
        return a[q, s] + tw[q, s]

    def first(s, send):
        a[3, s] = join(3, s)
        send(s).start()

    def plain(q, s, send):
        a[q, s] = join(q, s)
        send(s).start()

    def joined(q, s, arrived, send):
        arrived(s).wait_recv()
        a[q, s] = join(q, s) + rd[s]
        send(s).start()

    inner = (z == 1) | (z == 2)
    outer = (z == 0) | (z == 3)

    def own(s):
        to_x(s).wait_recv()
        to_y(s).wait_recv()
        o[s] = join(0, s) + (rx[s] + ry[s])
        pl.when(outer)(lambda: z_in(s).start())

    def middle(s):
        @pl.when(inner)
        def _():
            z_in(s).wait_recv()
            pz[s] = o[s] + rz1[s]
            z_swap(s).start()

    def last(s):
        @pl.when(inner)
        def _():
            z_swap(s).wait_recv()
            fz[s] = pz[s] + rz2[s]
            z_out(s).start()
            keep(s).start()

    def taken(s):
        @pl.when(outer)
        def _():
            z_out(s).wait_recv()
            keep(s).start()

    def pick_rows(i):
        ts = pl.ds(pl.multiple_of(i * 256, 256), 256)
        hit = lax.broadcasted_iota(I32, (SD * cap, 256), 0) == slot_of[:, ts]
        picked = jnp.where(hit, 1.0, 0.0).astype(BF)
        outs = jnp.concatenate([out_v[k, 0:cap, :] for k in range(SD)], axis=0)
        ings = jnp.concatenate([ing_v[k] for k in range(SD)], axis=0)
        both = mm(picked, jnp.concatenate([outs, ings], axis=1), TN)
        output[ts, :] = both[:, 0:D].astype(BF)
        input_grad[ts, :] = both[:, D:].astype(BF)
        line = jnp.concatenate([out_v[k, cap : cap + 8, 0:cap] for k in range(SD)], axis=1)
        entropy[:, ts] = mm(line, picked)[0:1].astype(BF)

    for q in (3, 1, 2, 0):
        load(q).wait()

    def steps(i, lag, more):
        s = i - lag
        by_x = (s % 2 == 0) & (s < 2 * split)
        live = (s >= 0) & (s < count)
        pl.when(live & by_x)(lambda: more(s, True))
        pl.when(live & jnp.logical_not(by_x))(lambda: more(s, False))

    def steps_of(i, lag, more):
        pl.when((i >= lag) & (i < count + lag))(lambda: more(i - lag))

    def round_of(i):
        for group in groups:

            @pl.when(i == group[1])
            def _(group=group):
                to_twin(3, group).wait_recv()

            @pl.when(i == group[1] + 1)
            def _(group=group):
                to_twin(1, group).wait_recv()
                to_twin(2, group).wait_recv()

            @pl.when(i == group[1] + 6)
            def _(group=group):
                to_twin(0, group).wait_recv()

        steps(i, 0, lambda s, by_x: first(s, d_x if by_x else d_y))
        steps(i, 1, lambda s, by_x: plain(1, s, to_x) if by_x else plain(2, s, to_y))
        steps(i, 3, lambda s, by_x: joined(2, s, d_x, to_y) if by_x else joined(1, s, d_y, to_x))
        steps_of(i, 6, own)
        steps_of(i, 8, middle)
        steps_of(i, 10, last)
        steps_of(i, 12, taken)

    loop(3, round_of)
    for copy in rows_in:
        copy.wait()
    slots_here, _ = route_slots(order[...], me % SD, cap)
    slot_of[...] = slots_here

    v_sum = vec[me]
    for d in range(1, n_tok):
        v_tok(d).wait()
        v_sum = v_sum + vt[d]
    va[...] = v_sum
    v_rep(0, va).start()

    def four_rounds(i):
        loop(4, lambda j: round_of(3 + 4 * i + j))
        pick_rows(i)

    four_rounds(0)
    v_rep(0, va).wait()
    vc[...] = va[...] + vb[0]
    v_rep(1, vc).start()
    loop(3, lambda i: four_rounds(1 + i))
    loop(count + 12 - 19, lambda i: round_of(19 + i))
    v_rep(1, vc).wait()
    vec_out[...] = vc[...] + vb[1]

    for group in groups:
        for q in range(4):
            to_twin(q, group).wait_send()

    def sent(s):
        d_y(s).wait_send()
        to_x(s).wait_send()
        to_y(s).wait_send()
        keep(s).wait()

    loop(count, sent)

    @pl.when(outer)
    def _():
        loop(count, lambda s: z_in(s).wait_send())

    @pl.when(inner)
    def _():
        def back(s):
            z_swap(s).wait_send()
            z_out(s).wait_send()

        loop(count, back)


def reduce_all(cap, grads, shares, order, outs, ings, count):
    dma = pltpu.SemaphoreType.DMA
    count = count * BLK // PART
    part = pltpu.VMEM((count, PART, D), BF)
    whole = pltpu.VMEM((4, count, PART, D), BF)
    line = pltpu.VMEM((16, 128), F32)
    rows = jax.ShapeDtypeStruct((ROWS, D), BF)
    total, vec, output, input_grad, entropy = pl.pallas_call(
        functools.partial(reduce_kernel, cap, count, count // 2),
        out_shape=(
            jax.ShapeDtypeStruct((count, PART, D), BF),
            jax.ShapeDtypeStruct((16, 128), F32),
            rows,
            rows,
            jax.ShapeDtypeStruct((1, ROWS), BF),
        ),
        in_specs=[ANY, VMEM, VMEM] + [ANY] * (2 * SD),
        out_specs=(ANY,) + (VMEM,) * 4,
        scratch_shapes=[
            pltpu.VMEM((SD, cap + META, D), BF),
            pltpu.VMEM((SD, cap, D), BF),
            pltpu.VMEM((1, ROWS), I32),
            whole,
            whole,
        ]
        + [part] * 8
        + [pltpu.VMEM((8, 16, 128), F32), line, pltpu.VMEM((2, 16, 128), F32), line]
        + [dma((4,)), dma((count,))]
        + [dma((4, 4))] * 2
        + [dma((count,))] * 12
        + [dma((8,))] * 2
        + [dma((2,))] * 2
        + [dma((2, SD))],
        compiler_params=pltpu.CompilerParams(collective_id=1, has_side_effects=True, vmem_limit_bytes=VMEM_LIMIT),
        cost_estimate=pl.CostEstimate(flops=4 * ROWS * ROWS * D, bytes_accessed=64 << 20, transcendentals=0),
        name="reduce",
    )(grads.reshape(-1, PART, D), shares, order, *outs, *ings)
    return total.reshape(-1, BLK, D), vec[0:9].reshape(-1), output, input_grad, entropy


V_BQ, V_BV, V_BO, V_BD, V_G1, V_C1, V_G2, V_C2 = range(8)


def inverse(x):
    r = pl.reciprocal(x, approx=True)
    return r * (2.0 - x * r)


def erf_parts(v):
    t = inverse(1.0 + (0.3275911 / math.sqrt(2.0)) * jnp.abs(v))
    e = jnp.exp2((v * v) * (-0.5 / math.log(2.0)))
    poly = 0.5 * 1.061405429
    for c in (-1.453152027, 1.421413741, -0.284496736, 0.254829592):
        poly = poly * t + 0.5 * c
    tail = poly * (t * e)
    return jnp.where(v >= 0.0, 1.0 - tail, tail), e


def lane_sum(x):
    return jnp.sum(x, axis=1, keepdims=True)


def gelu_parts(v):
    phi, e = erf_parts(v)
    return v * phi, phi + v * (e * (1.0 / math.sqrt(2.0 * math.pi)))


def weight_copies(pos, slots, w, sem, first):
    def copy(b):
        return pltpu.make_async_copy(slots.at[pos[first + b]], w.at[pl.ds(b * BLK, BLK)], sem)

    n = w.shape[0] // BLK
    return (lambda: loop(n, lambda b: copy(b).start())), (lambda: loop(n, lambda b: copy(b).wait()))


def halves_of_heads():
    lane = lax.broadcasted_iota(I32, (1, PW), 1)
    m0 = jnp.where(lane < HD, 1.0, 0.0).astype(BF)
    m1 = jnp.where(lane < HD, 0.0, 1.0).astype(BF)
    return lambda pair: jnp.concatenate([pair * m0, pair * m1], axis=0)


def tile_rows(t):
    return pl.ds(pl.multiple_of(t * TM, TM), TM)


def forward_kernel(
    cap,
    pos,
    slots,
    vecs,
    b_u,
    x_h,
    meta,
    back_0,
    back_1,
    back_2,
    back_3,
    heads_h,
    act_h,
    hid_h,
    q_h,
    k_h,
    v_h,
    p_h,
    slope_h,
    n1_h,
    n2_h,
    rs1_h,
    rs2_h,
    wqkv,
    wo,
    wu,
    wd,
    x_c,
    heads,
    act,
    hid,
    q,
    k,
    v,
    p_all,
    slope,
    n1,
    n2,
    rs1,
    rs2,
    out_c,
    ent,
    hid_t,
    w_sem,
    x_sem,
    o_sem,
):
    inv = 1.0 / math.sqrt(HD)
    get_x = pltpu.make_async_copy(x_h, x_c, x_sem)
    get_x.start()
    weights = [
        weight_copies(pos, slots, w, w_sem.at[i], first)
        for i, (w, first) in enumerate(((wqkv, 0), (wo, 24), (wu, 32), (wd, 64)))
    ]
    for start, _ in weights:
        start()
    get_x.wait()
    apart = halves_of_heads()

    def vec(i):
        return vecs[i : i + 1, :]

    saved = (
        (heads, heads_h),
        (act, act_h),
        (hid, hid_h),
        (q, q_h),
        (k, k_h),
        (v, v_h),
        (slope, slope_h),
        (n1, n1_h),
        (n2, n2_h),
        (rs1, rs1_h),
        (rs2, rs2_h),
    )

    def save(t, i):
        src, dst = saved[i]
        return pltpu.make_async_copy(src.at[tile_rows(t)], dst.at[tile_rows(t)], o_sem.at[i])

    def save_p(t):
        n = TM // CL
        cs = pl.ds(t * n, n)
        return pltpu.make_async_copy(p_all.at[cs], p_h.at[cs], o_sem.at[len(saved)])

    def normal(r, n, rs, rows):
        c = r - lane_sum(r) * (1.0 / D)
        scale = lax.rsqrt(lane_sum(c * c) * (1.0 / D) + norm_epsilon)
        rs[rows, :] = jnp.broadcast_to(scale, (TM, 128))
        n[rows, :] = c * scale

    def tile(t):
        rows = tile_rows(t)
        first = t == 0
        pl.when(first)(weights[0][1])
        x = x_c[rows, :]
        q[rows, :] = ((mm(x, wqkv[0:D, :]) + vec(V_BQ)).astype(BF).astype(F32) * inv).astype(BF)
        k[rows, :] = mm(x, wqkv[D : 2 * D, :]).astype(BF)
        v[rows, :] = (mm(x, wqkv[2 * D :, :]) + vec(V_BV)).astype(BF)

        def attend(c):
            groups = [pl.ds(pl.multiple_of(t * TM + (FWD_AT * c + i) * CL, CL), CL) for i in range(FWD_AT)]
            pairs = [(i, p, slice(p * PW, (p + 1) * PW)) for i in range(FWD_AT) for p in range(PAIRS)]
            scores = [mm(apart(k[groups[i], ps]), q[groups[i], ps], NT) for i, _, ps in pairs]
            total = [jnp.zeros((1, CL), F32)] * FWD_AT
            probs = []
            for (i, _, _), both in zip(pairs, scores):
                halves = []
                for h in range(2):
                    sh = both[h * CL : (h + 1) * CL]
                    sh = sh - jnp.max(sh, axis=0, keepdims=True)
                    e = jnp.exp(sh)
                    tot = jnp.sum(e, axis=0, keepdims=True)
                    r = 1.0 / tot
                    total[i] += jnp.log(tot) - jnp.sum(e * sh, axis=0, keepdims=True) * r
                    halves.append((e * r).astype(BF))
                probs.append(jnp.concatenate(halves, axis=0))
            mixed = [mm(w, apart(v[groups[i], ps]), TN).astype(BF) for (i, _, ps), w in zip(pairs, probs)]
            for (i, p, ps), w, o in zip(pairs, probs, mixed):
                p_all[t * (TM // CL) + FWD_AT * c + i, p] = w
                heads[groups[i], ps] = o
            for i in range(FWD_AT):
                ent[:, groups[i]] = jnp.broadcast_to(total[i] * (1.0 / HEADS), (8, CL))

        loop(TM // CL // FWD_AT, attend)
        for i in (0, 3, 4, 5):
            save(t, i).start()
        save_p(t).start()
        pl.when(first)(weights[1][1])
        normal(x_c[rows, :].astype(F32) + mm(heads[rows, :], wo[...]) + vec(V_BO), n1, rs1, rows)
        hidden = n1[rows, :] * vec(V_G1) + vec(V_C1)
        hid[rows, :] = hidden.astype(BF)
        hid_t[...] = hidden
        pl.when(first)(weights[2][1])

        def widen(f):
            parts = [pl.ds(pl.multiple_of((2 * f + i) * FC, FC), FC) for i in range(2)]
            ups = [mm(hid[rows, :], wu[fs, :], NT) for fs in parts]
            for fs, up in zip(parts, ups):
                g, g_slope = gelu_parts(up + b_u[:, fs])
                act[rows, fs] = g.astype(BF)
                slope[rows, fs] = g_slope.astype(BF)

        loop(FF // FC // 2, widen)
        for i in (1, 2, 6, 7, 9):
            save(t, i).start()
        pl.when(first)(weights[3][1])
        normal(hid_t[...] + mm(act[rows, :], wd[...]) + vec(V_BD), n2, rs2, rows)
        out_c[rows, :] = (n2[rows, :] * vec(V_G2) + vec(V_C2)).astype(BF)
        for i in (8, 10):
            save(t, i).start()

    loop(ROWS // TM, tile)

    for j, back in enumerate((back_0, back_1, back_2, back_3)):
        own = seat_part(meta, j, cap)
        back[0:cap, :] = mm(own, out_c[...], TN).astype(BF)
        line = mm(ent[...].astype(BF), own)
        back[cap:, :] = jnp.concatenate([line, line], axis=1)[0:1].astype(BF) * jnp.ones((META, 1), BF)

    def saved_all(t):
        for i in range(len(saved)):
            save(t, i).wait()
        save_p(t).wait()

    loop(ROWS // TM, saved_all)


def shape_of(kind, *shape):
    return jax.ShapeDtypeStruct(shape, kind)


def saved_shapes():
    rows, wide = ((ROWS, D), BF), ((ROWS, FF), BF)
    probs = ((ROWS // CL, PAIRS, 2 * CL, CL), BF)
    full, thin = ((ROWS, D), F32), ((ROWS, 128), F32)
    return rows, wide, probs, full, thin


def forward(cap, positions, slots, vecs, b_u, x_c, meta):
    rows, wide, probs, full, thin = saved_shapes()
    kept = (rows, wide, rows, rows, rows, rows, probs, wide, full, full, thin, thin)
    dma = pltpu.SemaphoreType.DMA
    return pl.pallas_call(
        functools.partial(forward_kernel, cap),
        out_shape=(shape_of(BF, cap + META, D),) * SD + tuple(shape_of(kind, *shape) for shape, kind in kept),
        in_specs=[SMEM, ANY, VMEM, VMEM, ANY, VMEM],
        out_specs=(VMEM,) * SD + (ANY,) * len(kept),
        scratch_shapes=[
            pltpu.VMEM((3 * D, D), BF),
            pltpu.VMEM((D, D), BF),
            pltpu.VMEM((FF, D), BF),
            pltpu.VMEM((FF, D), BF),
            pltpu.VMEM(*rows),
        ]
        + [pltpu.VMEM(*a) for a in kept]
        + [
            pltpu.VMEM(*rows),
            pltpu.VMEM((8, ROWS), F32),
            pltpu.VMEM((TM, D), F32),
            dma((4,)),
            dma,
            dma((12,)),
        ],
        compiler_params=pltpu.CompilerParams(vmem_limit_bytes=VMEM_LIMIT),
        cost_estimate=pl.CostEstimate(flops=2 * ROWS * WROWS * D, bytes_accessed=64 << 20, transcendentals=0),
        name="forward",
    )(positions, slots, vecs, b_u, x_c, meta)


def backward_kernel(
    cap,
    pos,
    slots,
    vecs,
    meta,
    cot_0,
    cot_1,
    cot_2,
    cot_3,
    q_h,
    k_h,
    v_h,
    p_h,
    slope_h,
    n1_h,
    n2_h,
    rs1_h,
    rs2_h,
    back_0,
    back_1,
    back_2,
    back_3,
    shares,
    d_up_h,
    d_q_h,
    d_k_h,
    d_v_h,
    d_proj_h,
    d_br_h,
    wqkv,
    wo,
    wu,
    wd,
    blocks,
    q,
    k,
    v,
    p_all,
    d_up,
    n1,
    n2,
    rs1,
    rs2,
    d_proj,
    d_br,
    ing_c,
    d_h_t,
    res_t,
    gvec,
    g_bu,
    w_sem,
    c_sem,
    i_sem,
    o_sem,
):
    inv = 1.0 / math.sqrt(HD)
    get_c = [
        pltpu.make_async_copy(cot, blocks.at[j], c_sem.at[j]) for j, cot in enumerate((cot_0, cot_1, cot_2, cot_3))
    ]
    for copy in get_c:
        copy.start()
    fetch = [
        pltpu.make_async_copy(src, dst, i_sem.at[i])
        for i, (src, dst) in enumerate(
            (
                (n2_h, n2),
                (rs2_h, rs2),
                (slope_h, d_up),
                (n1_h, n1),
                (rs1_h, rs1),
                (v_h, v),
                (p_h, p_all),
                (k_h, k),
                (q_h, q),
            )
        )
    ]
    weights = [
        weight_copies(pos, slots, w, w_sem.at[i], first)
        for i, (w, first) in enumerate(((wd, 64), (wu, 32), (wo, 24), (wqkv, 0)))
    ]
    fetch[0].start()
    fetch[1].start()
    weights[0][0]()
    fetch[2].start()
    weights[1][0]()
    fetch[3].start()
    fetch[4].start()
    weights[2][0]()
    for i in range(5, 9):
        fetch[i].start()
    weights[3][0]()
    gvec[...] = jnp.zeros_like(gvec)
    g_bu[...] = jnp.zeros_like(g_bu)
    shares[...] = jnp.zeros_like(shares)
    for copy in get_c:
        copy.wait()
    seat_rows(meta, blocks, cap, d_br)
    apart = halves_of_heads()
    first_half = lax.broadcasted_iota(I32, (CL, PW), 1) < HD

    def vec(i):
        return vecs[i : i + 1, :]

    def add_vec(i, value):
        gvec[i : i + 1, :] += jnp.sum(value, axis=0, keepdims=True)

    saved = ((d_up, d_up_h), (q, d_q_h), (k, d_k_h), (v, d_v_h), (d_proj, d_proj_h), (d_br, d_br_h))

    def save(t, i):
        src, dst = saved[i]
        return pltpu.make_async_copy(src.at[tile_rows(t)], dst.at[tile_rows(t)], o_sem.at[i])

    def norm_back(e, n, rs, gain, shift):
        add_vec(gain, e * n)
        add_vec(shift, e)
        eg = e * vec(gain)
        return rs * (eg - lane_sum(eg) * (1.0 / D) - n * (lane_sum(eg * n) * (1.0 / D)))

    def tile(t):
        rows = tile_rows(t)
        start = t == 0

        @pl.when(start)
        def _():
            fetch[0].wait()
            fetch[1].wait()

        d_r2 = norm_back(d_br[rows, :].astype(F32), n2[rows, :], rs2[rows, 0:1], V_G2, V_C2)
        d_br[rows, :] = d_r2.astype(BF)
        add_vec(V_BD, d_br[rows, :].astype(F32))
        res_t[...] = d_r2

        @pl.when(start)
        def _():
            weights[0][1]()
            fetch[2].wait()

        def widen_back(f):
            parts = [pl.ds(pl.multiple_of((2 * f + i) * FC, FC), FC) for i in range(2)]
            ups = [mm(d_br[rows, :], wd[fs, :], NT) for fs in parts]
            for fs, up in zip(parts, ups):
                du = (up * d_up[rows, fs].astype(F32)).astype(BF)
                d_up[rows, fs] = du
                g_bu[:, fs] += jnp.sum(du.astype(F32), axis=0, keepdims=True)

        loop(FF // FC // 2, widen_back)
        for i in (0, 5):
            save(t, i).start()

        @pl.when(start)
        def _():
            weights[1][1]()
            fetch[3].wait()
            fetch[4].wait()

        d_h = res_t[...] + mm(d_up[rows, :], wu[...])
        d_r1 = norm_back(d_h, n1[rows, :], rs1[rows, 0:1], V_G1, V_C1)
        d_proj[rows, :] = d_r1.astype(BF)
        res_t[...] = d_r1
        add_vec(V_BO, d_proj[rows, :].astype(F32))
        save(t, 4).start()

        @pl.when(start)
        def _():
            weights[2][1]()
            for i in range(5, 9):
                fetch[i].wait()

        d_h_t[...] = mm(d_proj[rows, :], wo[...], NT).astype(BF)

        def attend_back(c):
            groups = [
                (t * (TM // CL) + BWD_AT * c + i, BWD_AT * c + i) for i in range(BWD_AT)
            ]
            pairs = [
                (g, p, pl.ds(pl.multiple_of(g * CL, CL), CL), pl.ds(pl.multiple_of(n * CL, CL), CL), slice(p * PW, (p + 1) * PW))
                for g, n in groups
                for p in range(PAIRS)
            ]
            probs = [p_all[g, p] for g, p, _, _, _ in pairs]
            d_heads = [d_h_t[cr, ps] for _, _, _, cr, ps in pairs]
            d_probs = [mm(apart(v[gr, ps]), dh, NT) for (_, _, gr, _, ps), dh in zip(pairs, d_heads)]
            d_values = [mm(w, dh) for w, dh in zip(probs, d_heads)]
            d_scores = []
            for w, dw in zip(probs, d_probs):
                halves = []
                for h in range(2):
                    wh = w[h * CL : (h + 1) * CL].astype(F32)
                    dwh = dw[h * CL : (h + 1) * CL]
                    halves.append((wh * (dwh - jnp.sum(dwh * wh, axis=0, keepdims=True))).astype(BF))
                d_scores.append(jnp.concatenate(halves, axis=0))
            d_keys = [mm(ds, q[gr, ps]) for (_, _, gr, _, ps), ds in zip(pairs, d_scores)]
            d_queries = [mm(ds, apart(k[gr, ps]), TN) for (_, _, gr, _, ps), ds in zip(pairs, d_scores)]
            for (_, _, gr, _, ps), dq, dk, dv in zip(pairs, d_queries, d_keys, d_values):
                q[gr, ps] = (dq * inv).astype(BF)
                k[gr, ps] = jnp.where(first_half, dk[0:CL], dk[CL:]).astype(BF)
                v[gr, ps] = jnp.where(first_half, dv[0:CL], dv[CL:]).astype(BF)

        loop(TM // CL // BWD_AT, attend_back)
        for i in (1, 2, 3):
            save(t, i).start()
        add_vec(V_BQ, q[rows, :].astype(F32))
        add_vec(V_BV, v[rows, :].astype(F32))
        pl.when(start)(weights[3][1])
        d_x = (
            mm(q[rows, :], wqkv[0:D, :], NT)
            + mm(k[rows, :], wqkv[D : 2 * D, :], NT)
            + mm(v[rows, :], wqkv[2 * D :, :], NT)
        )
        ing_c[rows, :] = (res_t[...] + d_x.astype(BF).astype(F32)).astype(BF)

    loop(ROWS // TM, tile)

    for j, back in enumerate((back_0, back_1, back_2, back_3)):
        back[...] = mm(seat_part(meta, j, cap), ing_c[...], TN).astype(BF)

    for chunk in range(72):
        row, lane = chunk // 6, chunk % 6 * 128
        if row < 8:
            part = gvec[row : row + 1, lane : lane + 128]
        else:
            lane += (row - 8) * D
            part = g_bu[:, lane : lane + 128]
        shares[chunk // 9, chunk % 9 : chunk % 9 + 1, :] = part

    def saved_all(t):
        for i in range(len(saved)):
            save(t, i).wait()

    loop(ROWS // TM, saved_all)


def backward(cap, positions, slots, vecs, meta, cots, saved):
    rows, wide, probs, full, thin = saved_shapes()
    dma = pltpu.SemaphoreType.DMA
    grads = (wide, rows, rows, rows, rows, rows)
    return pl.pallas_call(
        functools.partial(backward_kernel, cap),
        out_shape=(shape_of(BF, cap, D),) * SD
        + (shape_of(F32, 8, 16, 128),)
        + tuple(shape_of(kind, *shape) for shape, kind in grads),
        in_specs=[SMEM, ANY, VMEM, VMEM] + [ANY] * (SD + 9),
        out_specs=(VMEM,) * (SD + 1) + (ANY,) * len(grads),
        scratch_shapes=[
            pltpu.VMEM((3 * D, D), BF),
            pltpu.VMEM((D, D), BF),
            pltpu.VMEM((FF, D), BF),
            pltpu.VMEM((FF, D), BF),
            pltpu.VMEM((SD, cap, D), BF),
        ]
        + [pltpu.VMEM(*a) for a in (rows, rows, rows, probs, wide, full, full, thin, thin, rows, rows, rows)]
        + [
            pltpu.VMEM((TM, D), BF),
            pltpu.VMEM((TM, D), F32),
            pltpu.VMEM((8, D), F32),
            pltpu.VMEM((1, FF), F32),
            dma((4,)),
            dma((4,)),
            dma((9,)),
            dma((6,)),
        ],
        compiler_params=pltpu.CompilerParams(vmem_limit_bytes=VMEM_LIMIT),
        cost_estimate=pl.CostEstimate(flops=2 * ROWS * WROWS * D, bytes_accessed=64 << 20, transcendentals=0),
        name="backward",
    )(positions, slots, vecs, meta, *cots, *saved)


WC = 8 * BLK


def weight_kernel(
    pos,
    x_h,
    heads_h,
    act_h,
    d_up_h,
    d_q_h,
    d_k_h,
    d_v_h,
    d_proj_h,
    hid_h,
    d_br_h,
    grads,
    x_c,
    heads,
    act,
    d_up,
    d_q,
    d_k,
    d_v,
    d_proj,
    hid,
    d_br,
    stage,
    i_sem,
    g_sem,
):
    refs = (
        (x_h, x_c),
        (d_q_h, d_q),
        (d_k_h, d_k),
        (d_v_h, d_v),
        (heads_h, heads),
        (d_proj_h, d_proj),
        (hid_h, hid),
        (d_up_h, d_up),
        (d_br_h, d_br),
        (act_h, act),
    )
    fetch = [pltpu.make_async_copy(src, dst, i_sem.at[i]) for i, (src, dst) in enumerate(refs)]
    for copy in fetch:
        copy.start()

    per = WC // BLK

    def g_copy(chunk, j, at):
        return pltpu.make_async_copy(
            stage.at[at, pl.ds(j * BLK, BLK)], grads.at[pos[chunk * per + j]], g_sem.at[at]
        )

    def put(chunk, left, right):
        at = lax.rem(chunk, 2)

        @pl.when(chunk >= 2)
        def _():
            for j in range(per):
                g_copy(chunk - 2, j, at).wait()

        stage[at] = mm(left, right, TN).astype(BF)
        for j in range(per):
            g_copy(chunk, j, at).start()

    first = 0
    for left, right, needs in (
        (x_c, d_q, (0, 1)),
        (x_c, d_k, (2,)),
        (x_c, d_v, (3,)),
        (heads, d_proj, (4, 5)),
        (d_up, hid, (6, 7)),
        (act, d_br, (8, 9)),
    ):
        for i in needs:
            fetch[i].wait()

        def body(j, left=left, right=right, first=first):
            put(first + j, left[:, pl.ds(pl.multiple_of(j * WC, WC), WC)], right[...])

        loop(left.shape[1] // WC, body)
        first += left.shape[1] // WC
    for chunk in (first - 2, first - 1):
        for j in range(per):
            g_copy(chunk, j, chunk % 2).wait()


def weight_grads_of(total_slots, positions, x_c, saved):
    r_v, w_v = pltpu.VMEM((ROWS, D), BF), pltpu.VMEM((ROWS, FF), BF)
    return pl.pallas_call(
        weight_kernel,
        out_shape=jax.ShapeDtypeStruct((total_slots, BLK, D), BF),
        in_specs=[SMEM] + [ANY] * 10,
        out_specs=ANY,
        scratch_shapes=[r_v, r_v, w_v, w_v]
        + [r_v] * 6
        + [
            pltpu.VMEM((2, WC, D), BF),
            pltpu.SemaphoreType.DMA((10,)),
            pltpu.SemaphoreType.DMA((2,)),
        ],
        compiler_params=pltpu.CompilerParams(vmem_limit_bytes=VMEM_LIMIT),
        cost_estimate=pl.CostEstimate(flops=2 * ROWS * WROWS * D, bytes_accessed=40 << 20, transcendentals=0),
        name="weight_grads",
    )(positions, x_c, *saved)


def local(
    tokens,
    cotangent,
    cluster_order,
    block_owner,
    master_slots,
    moment_one,
    moment_two,
    vector_master,
    vector_moment_one,
    vector_moment_two,
):
    tok_count = lax.axis_size("tok")
    tok_index = lax.axis_index("tok")
    slot_count = master_slots.shape[0]
    cap = tok_count // SD * (max(1, CPS // tok_count) * 3 * CL // (2 * SD))
    total_slots = tok_count * slot_count
    order = cluster_order.reshape(1, ROWS)

    block = jax.ShapeDtypeStruct((SD, cap, D), BF)
    meta_shape = jax.ShapeDtypeStruct((SD, META, D), BF)
    row_block = jax.ShapeDtypeStruct((ROWS, D), BF)
    four_planes = tok_count == 8 and lax.axis_size("rep") == 4
    if four_planes:
        slots_low, x_c, *cots, recv_meta, vecs, b_u, occupancy, positions = gather_all(
            cap, tokens, cotangent, order, master_slots, vector_master, block_owner
        )
        positions = positions.reshape(NBLK)
        slots_low = slots_low.reshape(total_slots, BLK, D)
    else:
        positions = slot_positions(block_owner, slot_count)
        slots_low = lax.all_gather(master_slots.astype(BF), "tok", axis=0, tiled=True)
        vectors = lax.all_gather(vector_master.astype(BF), "tok", axis=0, tiled=True).astype(F32)
        vecs, b_u = vectors[: 8 * D].reshape(8, D), vectors[8 * D :].reshape(1, FF)
        cluster = tok_index // SD * CPS + cluster_order // CL
        target = cluster % tok_count
        chosen = target[None, :] == jnp.arange(tok_count, dtype=jnp.int32)[:, None]
        sent_counts = jnp.sum(chosen.astype(F32), axis=1)
        own_row = (jnp.arange(tok_count, dtype=jnp.int32) == tok_index).astype(F32)
        occupancy = lax.psum(own_row[:, None] * sent_counts[None, :], ("tok", "rep")).astype(jnp.int32)
        send_x, send_c, meta = pl.pallas_call(
            functools.partial(send_kernel, cap),
            out_shape=(block, block, meta_shape),
            in_specs=[VMEM] * 3,
            out_specs=(VMEM,) * 3,
            compiler_params=pltpu.CompilerParams(vmem_limit_bytes=VMEM_LIMIT),
            name="send_rows",
        )(tokens, cotangent, order)
        recv_x, recv_meta = (jnp.stack(swap_blocks(b)) for b in (send_x, meta))
        x_c = pl.pallas_call(
            functools.partial(seat_kernel, cap),
            out_shape=row_block,
            in_specs=[VMEM] * 2,
            out_specs=VMEM,
            compiler_params=pltpu.CompilerParams(vmem_limit_bytes=VMEM_LIMIT),
            name="seat_rows",
        )(recv_x, recv_meta)
        cots = [send_c[k] for k in range(SD)]

    cots = swap_blocks(cots)
    *out_blocks, heads, act, hid, q, k, v, p, slope, n1, n2, rs1, rs2 = forward(
        cap, positions, slots_low, vecs, b_u, x_c, recv_meta
    )
    out_blocks = swap_blocks(out_blocks)
    *ing_blocks, shares, d_up, d_q, d_k, d_v, d_proj, d_br = backward(
        cap, positions, slots_low, vecs, recv_meta, cots, (q, k, v, p, slope, n1, n2, rs1, rs2)
    )
    ing_blocks = swap_blocks(ing_blocks)
    grads = weight_grads_of(
        total_slots, positions, x_c, (heads, act, d_up, d_q, d_k, d_v, d_proj, hid, d_br)
    )
    if four_planes:
        total, vec_owned, output, input_grad, entropy = reduce_all(
            cap, grads, shares, order, out_blocks, ing_blocks, slot_count
        )
    else:
        total = lax.psum(lax.psum_scatter(grads, "tok", scatter_dimension=0, tiled=True), "rep")
        grad_vector = shares[:, 0:9].reshape(-1)
        vec_owned = lax.psum(lax.psum_scatter(grad_vector, "tok", scatter_dimension=0, tiled=True), "rep")
        output, input_grad, entropy = pl.pallas_call(
            functools.partial(return_kernel, cap),
            out_shape=(row_block, row_block, jax.ShapeDtypeStruct((1, ROWS), BF)),
            in_specs=[VMEM] * (2 * SD + 1),
            out_specs=(VMEM,) * 3,
            compiler_params=pltpu.CompilerParams(vmem_limit_bytes=VMEM_LIMIT),
            name="return_rows",
        )(order, *out_blocks, *ing_blocks)

    used = jnp.any(
        positions[None, :] == (tok_index * slot_count + jnp.arange(slot_count, dtype=I32))[:, None], axis=1
    )
    owned_grad = jnp.where(used[:, None, None], total.astype(F32), 0.0)
    first_new, second_new, master_new = adam_update(
        owned_grad, master_slots, moment_one, moment_two, rate_matrix
    )
    vec_first, vec_second, vec_new = adam_update(
        vec_owned, vector_master, vector_moment_one, vector_moment_two, rate_vector
    )
    return (
        output,
        input_grad,
        owned_grad,
        first_new,
        second_new,
        master_new,
        master_new.astype(BF),
        vec_owned,
        vec_first,
        vec_second,
        vec_new,
        vec_new.astype(BF),
        entropy.reshape(-1),
        occupancy,
    )


def solution(mesh):
    placed = (
        P(("rep", "tok"), None),
        P(("rep", "tok"), None),
        P(("rep", "tok")),
        P(),
        P("tok", None, None),
        P("tok", None, None),
        P("tok", None, None),
        P("tok"),
        P("tok"),
        P("tok"),
    )
    return jax.shard_map(
        local,
        mesh=mesh,
        in_specs=placed,
        out_specs=(
            P(("rep", "tok"), None),
            P(("rep", "tok"), None),
            P("tok", None, None),
            P("tok", None, None),
            P("tok", None, None),
            P("tok", None, None),
            P("tok", None, None),
            P("tok"),
            P("tok"),
            P("tok"),
            P("tok"),
            P("tok"),
            P(("rep", "tok")),
            P(),
        ),
        check_vma=False,
    )
```

```python
import functools
import math

import jax
import jax.numpy as jnp
from jax import lax
from jax.experimental import pallas as pl
from jax.experimental.pallas import tpu as pltpu
from jax.sharding import PartitionSpec as P

D = 768
HEADS = 12
HD = 64
FF = 3072
SD = 4
CL = 128
NBLK = 96
STEP = 10
CPS = 32
WROWS = 9216
BLK = 96
ROWS = 1024
PAIRS = HEADS // 2
PW = 2 * HD
TM = 512
PART = 48
META = 16
VMEM_LIMIT = 63 << 20
FC = 768
BWD_AT = 2

norm_epsilon = 1e-06
beta_first = 0.9
beta_second = 0.999
adam_epsilon = 1e-08
weight_decay = 0.01
rate_matrix = 0.02
rate_vector = 0.2

BF = jnp.bfloat16
F32 = jnp.float32
I32 = jnp.int32

VMEM = pl.BlockSpec(memory_space=pltpu.VMEM)
SMEM = pl.BlockSpec(memory_space=pltpu.SMEM)
ANY = pl.BlockSpec(memory_space=pl.ANY)

NN = (((1,), (0,)), ((), ()))
NT = (((1,), (1,)), ((), ()))
TN = (((0,), (0,)), ((), ()))


def mm(a, b, dims=NN):
    return lax.dot_general(a, b, dims, preferred_element_type=F32)


def slot_positions(block_owner, slot_count):
    owners = block_owner[:, 0]
    blocks = owners.shape[0]
    shared = owners[:, None] == owners[None, :]
    before = (
        jnp.arange(blocks, dtype=jnp.int32)[None, :] < jnp.arange(blocks, dtype=jnp.int32)[:, None]
    )
    earlier = jnp.sum((shared & before).astype(jnp.int32), axis=1)
    return owners * slot_count + earlier


def adam_update(grad_now, weight_old, first_old, second_old, rate_step):
    first_new = beta_first * first_old + (1.0 - beta_first) * grad_now
    second_new = beta_second * second_old + (1.0 - beta_second) * grad_now * grad_now
    first_hat = first_new / (1.0 - beta_first**STEP)
    second_hat = second_new / (1.0 - beta_second**STEP)
    weight_new = weight_old - rate_step * (
        first_hat / (jnp.sqrt(second_hat) + adam_epsilon) + weight_decay * weight_old
    )
    return (first_new, second_new, weight_new)


def route_slots(order, seat, cap):
    cluster = order // CL
    rel = lax.rem(cluster, SD) ^ seat
    place = (cluster // SD) * CL + lax.rem(order, CL) + 1
    chosen = lax.broadcasted_iota(I32, (8, ROWS), 0) == rel
    chosen_low = jnp.where(chosen, 1.0, 0.0).astype(BF)
    before = lax.broadcasted_iota(I32, (ROWS, ROWS), 0) < lax.broadcasted_iota(I32, (ROWS, ROWS), 1)
    before_low = jnp.where(before, 1.0, 0.0).astype(BF)
    running = mm(chosen_low, before_low)
    rank = jnp.sum(jnp.where(chosen, running, 0.0), axis=0, keepdims=True).astype(I32)
    return rel * cap + rank, place


def slot_matrix(slots, at, cap):
    rows = lax.broadcasted_iota(I32, (cap, ROWS), 0) + at * cap
    return jnp.where(rows == slots, 1.0, 0.0).astype(BF)


def send_kernel(cap, tokens, cotangent, order, send_x, send_c, meta):
    seat = lax.rem(lax.axis_index("tok"), SD)
    slots, place = route_slots(order[...], seat, cap)
    digits = jnp.concatenate([place // CL, lax.rem(place, CL)] + [place * 0] * 6, axis=0).astype(F32).astype(BF)
    for at in range(SD):
        picked = slot_matrix(slots, at, cap)
        send_x[at] = mm(picked, tokens[...]).astype(BF)
        send_c[at] = mm(picked, cotangent[...]).astype(BF)
        coded = mm(digits, picked, NT)
        line = jnp.concatenate([coded[0:1], coded[1:2]], axis=1)
        meta[at] = jnp.broadcast_to(line, (META, D)).astype(BF)


def remote(src, dst, send_sem, recv_sem, tok, rep):
    return pltpu.make_async_remote_copy(
        src_ref=src,
        dst_ref=dst,
        send_sem=send_sem,
        recv_sem=recv_sem,
        device_id={"tok": tok, "rep": rep},
        device_id_type=pl.DeviceIdType.MESH,
    )


def loop(n, body):
    def run(i, c):
        body(i)
        return c

    lax.fori_loop(0, n, run, 0)


class Place:
    def __init__(self):
        self.me = me = lax.axis_index("tok")
        self.z = z = lax.axis_index("rep")
        core, x, y = me % 2, (me // 2) % 2, me // 4
        self.twin = me + 1 - 2 * core
        self.xn = me + 2 - 4 * x
        self.yn = me + 4 - 8 * y
        self.dn = self.xn + 4 - 8 * y
        self.side = z % 2
        self.zp = z + 1 - 2 * self.side

    def twin_of(self, tok):
        return tok + 1 - 2 * (tok % 2)

    def greet(self, peers):
        barrier = pltpu.get_barrier_semaphore()
        for tok, rep in peers:
            pl.semaphore_signal(
                barrier, inc=1, device_id={"tok": tok, "rep": rep}, device_id_type=pl.DeviceIdType.MESH
            )
        return lambda: pl.semaphore_wait(barrier, len(peers))


def seat_matrix(meta, first, rows, cap):
    hi = jnp.concatenate([meta[k, 0:8, 0:cap] for k in range(SD)], axis=1).astype(F32)[0:1]
    lo = jnp.concatenate([meta[k, 0:8, cap : 2 * cap] for k in range(SD)], axis=1).astype(F32)[0:1]
    at = (hi * CL + lo).astype(I32)
    seats = lax.broadcasted_iota(I32, (rows, SD * cap), 0) + (first + 1)
    return jnp.where(seats == at, 1.0, 0.0).astype(BF)


def seat_part(meta, k, cap):
    hi = meta[k, 0:8, 0:cap].astype(F32)[0:1]
    lo = meta[k, 0:8, cap : 2 * cap].astype(F32)[0:1]
    at = (hi * CL + lo).astype(I32)
    seats = lax.broadcasted_iota(I32, (ROWS, cap), 0) + 1
    return jnp.where(seats == at, 1.0, 0.0).astype(BF)


def seat_rows(meta, blocks, cap, to):
    def body(t):
        r0 = pl.multiple_of(t * 256, 256)
        rows = blocks[...].reshape(SD * cap, D)
        to[pl.ds(r0, 256), :] = mm(seat_matrix(meta, r0, 256, cap), rows).astype(BF)

    loop(ROWS // 256, body)


def seat_kernel(cap, blocks, meta, to):
    seat_rows(meta, blocks, cap, to)


def gather_kernel(
    cap,
    count,
    tokens_h,
    cotangent_h,
    order,
    master_h,
    vector,
    owner_of,
    slots,
    x_c,
    cot_0,
    cot_1,
    cot_2,
    cot_3,
    recv_meta,
    vecs,
    b_u,
    occupancy,
    positions,
    tokens,
    cotangent,
    master,
    own,
    send_x,
    send_c,
    meta,
    recv_x,
    got_meta,
    slot_of,
    digits,
    mine,
    by_z,
    by_tok,
    x_s,
    x_r,
    y_s,
    y_r,
    d_s,
    d_r,
    zx_s,
    zx_r,
    zd_s,
    zd_r,
    zy_s,
    zy_r,
    p_s,
    p_r,
    row_s,
    row_r,
    z_s,
    z_r,
    t_s,
    t_r,
    local_s,
):
    at = Place()
    me, z, side = at.me, at.z, at.side
    n_tok, n_rep = 8, 4
    peers = [((me + d) % n_tok, z) for d in range(1, n_tok)] + [(me, (z + d) % n_rep) for d in range(1, n_rep)]
    fetch = [
        pltpu.make_async_copy(src, dst, local_s.at[i])
        for i, (src, dst) in enumerate(((master_h, master), (tokens_h, tokens), (cotangent_h, cotangent)))
    ]
    for copy in fetch:
        copy.start()
    wait_peers = at.greet(peers)
    fetch[0].wait()

    last = count - 1

    def near(j):
        return side * last + (1 - 2 * side) * j

    def far(j):
        return (1 - side) * last - (1 - 2 * side) * j

    few_x, few_d, few_y = 11 * count // 26, 12 * count // 26, 8 * count // 26
    most_x, most_d, most_y = count - few_x, count - few_d, count - few_y

    def piece(owner, s):
        return slots.at[owner * count + s]

    def to_x(s):
        return remote(own.at[s], piece(me, s), x_s.at[s], x_r.at[s], at.xn, z)

    def to_y(s):
        return remote(own.at[s], piece(me, s), y_s.at[s], y_r.at[s], at.yn, z)

    def on_y(s):
        return remote(piece(at.xn, s), piece(at.xn, s), d_s.at[s], d_r.at[s], at.yn, z)

    def x_on_z(s):
        return remote(piece(at.xn, s), piece(at.xn, s), zx_s.at[s], zx_r.at[s], me, at.zp)

    def d_on_z(s):
        return remote(piece(at.dn, s), piece(at.dn, s), zd_s.at[s], zd_r.at[s], me, at.zp)

    def y_on_z(s):
        return remote(piece(at.yn, s), piece(at.yn, s), zy_s.at[s], zy_r.at[s], me, at.zp)

    def x_in(s):
        return remote(own.at[s], piece(at.xn, s), x_s.at[s], x_r.at[s], at.xn, z)

    def y_in(s):
        return remote(own.at[s], piece(at.yn, s), y_s.at[s], y_r.at[s], at.yn, z)

    def d_in(s):
        return remote(own.at[s], piece(at.dn, s), d_s.at[s], d_r.at[s], at.yn, z)

    owners = (me, at.xn, at.yn, at.dn)

    def near_run(q, j0, j1):
        return (q, (1 - side) * j0 + side * (count - j1), j1 - j0)

    def far_run(q, j0, j1):
        return (q, side * j0 + (1 - side) * (count - j1), j1 - j0)

    runs = (
        (0, 0, count),
        near_run(2, 0, few_y),
        near_run(1, 0, most_x),
        near_run(3, 0, most_d),
        far_run(1, 0, few_x),
        near_run(2, few_y, most_y),
        far_run(2, 0, few_y),
        far_run(3, 0, few_d // 2),
        far_run(3, few_d // 2, few_d - 2),
        far_run(3, few_d - 2, few_d),
    )

    def to_twin(i):
        q, s, n = runs[i]
        src = own if q == 0 else slots.at[pl.ds(owners[q] * count + s, n)]
        dst = slots.at[pl.ds(owners[q] * count + s, n)]
        return remote(src, dst, p_s.at[i], p_r.at[i], at.twin, z)

    def cast(j):
        own[near(j)] = master[near(j)].astype(BF)

    loop(most_x, cast)
    wait_peers()
    loop(most_x, lambda j: to_x(near(j)).start())
    loop(few_y, lambda j: to_y(near(j)).start())
    loop(count - most_x, lambda j: cast(most_x + j))
    to_twin(0).start()
    keep = pltpu.make_async_copy(own, slots.at[pl.ds(me * count, count)], local_s.at[3])
    keep.start()

    seat = me % SD
    seats = (me, at.twin, at.xn, at.twin_of(at.xn))
    rows_of = ((meta, got_meta), (send_x, recv_x))

    def row_copy(i, k):
        src, dst = rows_of[i]
        return remote(src.at[k], dst.at[k], row_s.at[i, k], row_r.at[i, k], seats[k], z)

    put_c = [
        pltpu.make_async_copy(send_c.at[k], to, local_s.at[4 + k])
        for k, to in enumerate((cot_0, cot_1, cot_2, cot_3))
    ]

    def route():
        fetch[1].wait()
        fetch[2].wait()
        slots_here, place = route_slots(order[...], seat, cap)
        slot_of[...] = slots_here
        digits[...] = (
            jnp.concatenate([place // CL, lax.rem(place, CL)] + [place * 0] * 6, axis=0).astype(F32).astype(BF)
        )

    def sort_tokens(k):
        picked = slot_matrix(slot_of[...], k, cap)
        send_x[k] = mm(picked, tokens[...]).astype(BF)
        coded = mm(digits[...], picked, NT)
        line = jnp.concatenate([coded[0:1], coded[1:2]], axis=1)
        meta[k] = jnp.broadcast_to(line, (META, D)).astype(BF)
        for i in range(2):
            if k:
                row_copy(i, k).start()
            else:
                src, dst = rows_of[i]
                dst[0] = src[0]

    def sort_cotangent(k):
        send_c[k] = mm(slot_matrix(slot_of[...], k, cap), cotangent[...]).astype(BF)
        put_c[k].start()

    def z_copy(d):
        return remote(by_z.at[0], by_z.at[d], z_s.at[d], z_r.at[d], me, (z + d) % n_rep)

    def t_copy(d):
        return remote(mine, by_tok.at[d], t_s.at[d], t_r.at[d], (me + d) % n_tok, z)

    def count_rows():
        residue = lax.rem(me // SD * CPS + order[...] // CL, n_tok)
        hit = lax.broadcasted_iota(I32, (128, ROWS), 0) == residue
        by_z[0] = mm(jnp.ones((8, ROWS), BF), jnp.where(hit, 1.0, 0.0).astype(BF), NT)
        for d in range(1, n_rep):
            z_copy(d).start()
        for i in range(9):
            mine[i : i + 1] = vector[i * 128 : (i + 1) * 128].reshape(1, 128).astype(BF).astype(F32)
        block_row = lax.broadcasted_iota(I32, (NBLK, NBLK), 0)
        block_col = lax.broadcasted_iota(I32, (NBLK, NBLK), 1)
        by_col = owner_of[...].astype(F32)
        by_row = lane_sum(jnp.where(block_row == block_col, by_col, 0.0))
        earlier = jnp.where((by_row == by_col) & (block_row < block_col), 1.0, 0.0)
        positions[...] = (by_col * (count * PART // BLK) + jnp.sum(earlier, axis=0, keepdims=True)).astype(I32)

    def share_vectors():
        for d in range(1, n_rep):
            z_copy(d).wait()
        mine[16:24] = by_z[0] + by_z[1] + by_z[2] + by_z[3]
        for d in range(1, n_tok):
            t_copy(d).start()

    def lay_out_vectors():
        by_tok[0] = mine[...]
        for d in range(1, n_tok):
            t_copy(d).wait()
        for owner in range(n_tok):
            share = by_tok[(me + n_tok - owner) % n_tok]
            occupancy[owner : owner + 1, :] = share[16:17, 0:n_tok].astype(I32)
            for i in range(9):
                chunk = owner * 9 + i
                row, lane = chunk // 6, chunk % 6 * 128
                if row < 8:
                    vecs[row : row + 1, lane : lane + 128] = share[i : i + 1]
                else:
                    lane += (row - 8) * D
                    b_u[:, lane : lane + 128] = share[i : i + 1]

    between = {
        1: lambda: (route(), sort_tokens(2)),
        3: lambda: sort_tokens(3),
        5: lambda: sort_tokens(1),
        7: lambda: (sort_tokens(0), count_rows()),
        9: lambda: sort_cotangent(1),
        11: lambda: sort_cotangent(2),
        13: lambda: sort_cotangent(3),
    }
    for j in range(most_x):
        x_in(near(j)).wait_recv()
        if j < most_d:
            on_y(near(j)).start()
        if j < few_x:
            x_on_z(near(j)).start()
        if j < few_y:
            y_in(near(j)).wait_recv()
            y_on_z(near(j)).start()
        if j == few_y:
            to_twin(1).start()
        if j in between:
            between[j]()
    to_twin(2).start()
    loop(most_y - few_y, lambda j: to_y(near(few_y + j)).start())
    share_vectors()
    sort_cotangent(0)

    def diagonal(j):
        d_in(near(j)).wait_recv()
        d_on_z(near(j)).start()

    loop(few_d, diagonal)
    loop(most_d - few_d, lambda j: d_in(near(few_d + j)).wait_recv())
    to_twin(3).start()
    loop(few_x, lambda j: x_on_z(far(j)).wait_recv())
    to_twin(4).start()
    lay_out_vectors()
    loop(most_y - few_y, lambda j: y_in(near(few_y + j)).wait_recv())
    to_twin(5).start()
    loop(few_y, lambda j: y_on_z(far(j)).wait_recv())
    to_twin(6).start()
    for i in (0, 1):
        for k in (2, 3, 1):
            row_copy(i, k).wait_recv()
    recv_meta[...] = got_meta[...]
    seat_rows(got_meta, recv_x, cap, x_c)
    done = 0
    for i, upto in ((7, few_d // 2), (8, few_d - 2), (9, few_d)):
        loop(upto - done, lambda j, done=done: d_on_z(far(done + j)).wait_recv())
        to_twin(i).start()
        done = upto

    for i in range(2):
        for k in (2, 3, 1):
            row_copy(i, k).wait_send()
    for copy in put_c:
        copy.wait()
    keep.wait()

    loop(most_x, lambda j: to_x(near(j)).wait_send())
    loop(most_y, lambda j: to_y(near(j)).wait_send())
    loop(most_d, lambda j: on_y(near(j)).wait_send())
    loop(few_x, lambda j: x_on_z(near(j)).wait_send())
    loop(few_d, lambda j: d_on_z(near(j)).wait_send())
    loop(few_y, lambda j: y_on_z(near(j)).wait_send())
    for i in range(len(runs)):
        to_twin(i).wait()


def gather_all(cap, tokens, cotangent, order, master, vector, block_owner):
    count = master.shape[0] * BLK // PART
    rows = jax.ShapeDtypeStruct((ROWS, D), BF)
    part = jax.ShapeDtypeStruct((cap, D), BF)
    dma = pltpu.SemaphoreType.DMA
    block = pltpu.VMEM((SD, cap, D), BF)
    meta = pltpu.VMEM((SD, META, D), BF)
    return pl.pallas_call(
        functools.partial(gather_kernel, cap, count),
        out_shape=(
            jax.ShapeDtypeStruct((8 * count, PART, D), BF),
            rows,
            part,
            part,
            part,
            part,
            jax.ShapeDtypeStruct((SD, META, D), BF),
            jax.ShapeDtypeStruct((8, D), F32),
            jax.ShapeDtypeStruct((1, FF), F32),
            jax.ShapeDtypeStruct((8, 8), I32),
            jax.ShapeDtypeStruct((1, NBLK), I32),
        ),
        in_specs=[ANY, ANY, VMEM, ANY, VMEM, VMEM],
        out_specs=(ANY, VMEM) + (ANY,) * SD + (VMEM,) * 5,
        scratch_shapes=[
            pltpu.VMEM((ROWS, D), BF),
            pltpu.VMEM((ROWS, D), BF),
            pltpu.VMEM((count, PART, D), F32),
            pltpu.VMEM((count, PART, D), BF),
            block,
            block,
            meta,
            block,
            meta,
            pltpu.VMEM((1, ROWS), I32),
            pltpu.VMEM((8, ROWS), BF),
            pltpu.VMEM((24, 128), F32),
            pltpu.VMEM((4, 8, 128), F32),
            pltpu.VMEM((8, 24, 128), F32),
        ]
        + [dma((count,))] * 12
        + [dma((10,))] * 2
        + [dma((2, SD))] * 2
        + [dma((4,))] * 2
        + [dma((8,))] * 2
        + [dma((8,))],
        compiler_params=pltpu.CompilerParams(collective_id=0, has_side_effects=True, vmem_limit_bytes=VMEM_LIMIT),
        cost_estimate=pl.CostEstimate(flops=8 * ROWS * ROWS * D, bytes_accessed=64 << 20, transcendentals=0),
        name="gather",
    )(tokens, cotangent, order, master.reshape(count, PART, D), vector, block_owner.reshape(1, NBLK))


def return_kernel(cap, order, *refs):
    outs, ings, (out, ing, entropy) = refs[:SD], refs[SD : 2 * SD], refs[2 * SD :]
    seat = lax.rem(lax.axis_index("tok"), SD)
    slots, _ = route_slots(order[...], seat, cap)
    picked = jnp.concatenate([slot_matrix(slots, at, cap) for at in range(SD)], axis=0)
    for to, blocks in ((out, outs), (ing, ings)):
        rows = jnp.concatenate([block[0:cap, :] for block in blocks], axis=0)
        to[...] = mm(picked, rows, TN).astype(BF)
    line = jnp.concatenate([block[cap : cap + 8, 0:cap] for block in outs], axis=1)
    entropy[...] = mm(line, picked)[0:1].astype(BF)


def swap_blocks(blocks):
    n = lax.axis_size("tok")
    parts = [blocks[0]]
    for k in range(1, SD):
        parts.append(lax.ppermute(blocks[k], "tok", [(i, i ^ k) for i in range(n)]))
    return parts


def reduce_kernel(
    cap,
    count,
    split,
    grads,
    vec,
    order,
    out_0,
    out_1,
    out_2,
    out_3,
    ing_0,
    ing_1,
    ing_2,
    ing_3,
    total,
    vec_out,
    output,
    input_grad,
    entropy,
    out_v,
    ing_v,
    slot_of,
    a,
    tw,
    rd,
    rx,
    ry,
    o,
    rz1,
    pz,
    rz2,
    fz,
    vt,
    va,
    vb,
    vc,
    a_l,
    keep_l,
    p_s,
    p_r,
    d_s,
    d_r,
    x_s,
    x_r,
    y_s,
    y_r,
    z1_s,
    z1_r,
    z2_s,
    z2_r,
    z3_s,
    z3_r,
    t_s,
    t_r,
    v_s,
    v_r,
    row_l,
):
    at = Place()
    me, z = at.me, at.z
    n_tok, n_rep = 8, 4
    peers = [((me + d) % n_tok, z) for d in range(1, n_tok)] + [(me, (z + d) % n_rep) for d in range(1, n_rep)]
    wait_peers = at.greet(peers)
    owners = (me, at.xn, at.yn, at.dn)

    def load(q):
        return pltpu.make_async_copy(grads.at[pl.ds(owners[q] * count, count)], a.at[q], a_l.at[q])

    for q in (3, 1, 2, 0):
        load(q).start()
    rows_in = [
        pltpu.make_async_copy(src, to.at[k], row_l.at[i, k])
        for i, (blocks, to) in enumerate((((out_0, out_1, out_2, out_3), out_v), ((ing_0, ing_1, ing_2, ing_3), ing_v)))
        for k, src in enumerate(blocks)
    ]
    for copy in rows_in:
        copy.start()
    wait_peers()

    groups = [(g, g * (count // 4), count // 4 if g < 3 else count - 3 * (count // 4)) for g in range(4)]

    def to_twin(q, group):
        g, s, n = group
        src = grads.at[pl.ds(at.twin_of(owners[q]) * count + s, n)]
        return remote(src, tw.at[q, pl.ds(s, n)], p_s.at[q, g], p_r.at[q, g], at.twin, z)

    def d_y(s):
        return remote(a.at[3, s], rd.at[s], d_s.at[s], d_r.at[s], at.yn, z)

    def d_x(s):
        return remote(a.at[3, s], rd.at[s], d_s.at[s], d_r.at[s], at.xn, z)

    def to_x(s):
        return remote(a.at[1, s], rx.at[s], x_s.at[s], x_r.at[s], at.xn, z)

    def to_y(s):
        return remote(a.at[2, s], ry.at[s], y_s.at[s], y_r.at[s], at.yn, z)

    def z_in(s):
        return remote(o.at[s], rz1.at[s], z1_s.at[s], z1_r.at[s], me, at.zp)

    def z_swap(s):
        return remote(pz.at[s], rz2.at[s], z2_s.at[s], z2_r.at[s], me, n_rep - 1 - z)

    def z_out(s):
        return remote(fz.at[s], fz.at[s], z3_s.at[s], z3_r.at[s], me, at.zp)

    def keep(s):
        return pltpu.make_async_copy(fz.at[s], total.at[s], keep_l.at[s])

    for group in groups:
        for q in (3, 1, 2, 0):
            to_twin(q, group).start()

    def v_tok(d):
        return remote(vec.at[(me + d) % n_tok], vt.at[d], t_s.at[d], t_r.at[d], (me + d) % n_tok, z)

    def v_rep(i, src):
        return remote(src, vb.at[i], v_s.at[i], v_r.at[i], me, at.zp if i == 0 else (z + 2) % n_rep)

    for d in range(1, n_tok):
        v_tok(d).start()

    def join(q, s):
        return a[q, s] + tw[q, s]

    def first(s, send):
        a[3, s] = join(3, s)
        send(s).start()

    def plain(q, s, send):
        a[q, s] = join(q, s)
        send(s).start()

    def joined(q, s, arrived, send):
        arrived(s).wait_recv()
        a[q, s] = join(q, s) + rd[s]
        send(s).start()

    inner = (z == 1) | (z == 2)
    outer = (z == 0) | (z == 3)

    def own(s):
        to_x(s).wait_recv()
        to_y(s).wait_recv()
        o[s] = join(0, s) + (rx[s] + ry[s])
        pl.when(outer)(lambda: z_in(s).start())

    def middle(s):
        @pl.when(inner)
        def _():
            z_in(s).wait_recv()
            pz[s] = o[s] + rz1[s]
            z_swap(s).start()

    def last(s):
        @pl.when(inner)
        def _():
            z_swap(s).wait_recv()
            fz[s] = pz[s] + rz2[s]
            z_out(s).start()
            keep(s).start()

    def taken(s):
        @pl.when(outer)
        def _():
            z_out(s).wait_recv()
            keep(s).start()

    def pick_rows(i):
        ts = pl.ds(pl.multiple_of(i * 256, 256), 256)
        hit = lax.broadcasted_iota(I32, (SD * cap, 256), 0) == slot_of[:, ts]
        picked = jnp.where(hit, 1.0, 0.0).astype(BF)
        outs = jnp.concatenate([out_v[k, 0:cap, :] for k in range(SD)], axis=0)
        ings = jnp.concatenate([ing_v[k] for k in range(SD)], axis=0)
        both = mm(picked, jnp.concatenate([outs, ings], axis=1), TN)
        output[ts, :] = both[:, 0:D].astype(BF)
        input_grad[ts, :] = both[:, D:].astype(BF)
        line = jnp.concatenate([out_v[k, cap : cap + 8, 0:cap] for k in range(SD)], axis=1)
        entropy[:, ts] = mm(line, picked)[0:1].astype(BF)

    for q in (3, 1, 2, 0):
        load(q).wait()

    def steps(i, lag, more):
        s = i - lag
        by_x = (s % 2 == 0) & (s < 2 * split)
        live = (s >= 0) & (s < count)
        pl.when(live & by_x)(lambda: more(s, True))
        pl.when(live & jnp.logical_not(by_x))(lambda: more(s, False))

    def steps_of(i, lag, more):
        pl.when((i >= lag) & (i < count + lag))(lambda: more(i - lag))

    def round_of(i):
        for group in groups:

            @pl.when(i == group[1])
            def _(group=group):
                to_twin(3, group).wait_recv()

            @pl.when(i == group[1] + 1)
            def _(group=group):
                to_twin(1, group).wait_recv()
                to_twin(2, group).wait_recv()

            @pl.when(i == group[1] + 6)
            def _(group=group):
                to_twin(0, group).wait_recv()

        steps(i, 0, lambda s, by_x: first(s, d_x if by_x else d_y))
        steps(i, 1, lambda s, by_x: plain(1, s, to_x) if by_x else plain(2, s, to_y))
        steps(i, 3, lambda s, by_x: joined(2, s, d_x, to_y) if by_x else joined(1, s, d_y, to_x))
        steps_of(i, 6, own)
        steps_of(i, 8, middle)
        steps_of(i, 10, last)
        steps_of(i, 12, taken)

    loop(3, round_of)
    for copy in rows_in:
        copy.wait()
    slots_here, _ = route_slots(order[...], me % SD, cap)
    slot_of[...] = slots_here

    v_sum = vec[me]
    for d in range(1, n_tok):
        v_tok(d).wait()
        v_sum = v_sum + vt[d]
    va[...] = v_sum
    v_rep(0, va).start()

    def four_rounds(i):
        loop(4, lambda j: round_of(3 + 4 * i + j))
        pick_rows(i)

    four_rounds(0)
    v_rep(0, va).wait()
    vc[...] = va[...] + vb[0]
    v_rep(1, vc).start()
    loop(3, lambda i: four_rounds(1 + i))
    loop(count + 12 - 19, lambda i: round_of(19 + i))
    v_rep(1, vc).wait()
    vec_out[...] = vc[...] + vb[1]

    for group in groups:
        for q in range(4):
            to_twin(q, group).wait_send()

    def sent(s):
        d_y(s).wait_send()
        to_x(s).wait_send()
        to_y(s).wait_send()
        keep(s).wait()

    loop(count, sent)

    @pl.when(outer)
    def _():
        loop(count, lambda s: z_in(s).wait_send())

    @pl.when(inner)
    def _():
        def back(s):
            z_swap(s).wait_send()
            z_out(s).wait_send()

        loop(count, back)


def reduce_all(cap, grads, shares, order, outs, ings, count):
    dma = pltpu.SemaphoreType.DMA
    count = count * BLK // PART
    part = pltpu.VMEM((count, PART, D), BF)
    whole = pltpu.VMEM((4, count, PART, D), BF)
    line = pltpu.VMEM((16, 128), F32)
    rows = jax.ShapeDtypeStruct((ROWS, D), BF)
    total, vec, output, input_grad, entropy = pl.pallas_call(
        functools.partial(reduce_kernel, cap, count, count // 2),
        out_shape=(
            jax.ShapeDtypeStruct((count, PART, D), BF),
            jax.ShapeDtypeStruct((16, 128), F32),
            rows,
            rows,
            jax.ShapeDtypeStruct((1, ROWS), BF),
        ),
        in_specs=[ANY, VMEM, VMEM] + [ANY] * (2 * SD),
        out_specs=(ANY,) + (VMEM,) * 4,
        scratch_shapes=[
            pltpu.VMEM((SD, cap + META, D), BF),
            pltpu.VMEM((SD, cap, D), BF),
            pltpu.VMEM((1, ROWS), I32),
            whole,
            whole,
        ]
        + [part] * 8
        + [pltpu.VMEM((8, 16, 128), F32), line, pltpu.VMEM((2, 16, 128), F32), line]
        + [dma((4,)), dma((count,))]
        + [dma((4, 4))] * 2
        + [dma((count,))] * 12
        + [dma((8,))] * 2
        + [dma((2,))] * 2
        + [dma((2, SD))],
        compiler_params=pltpu.CompilerParams(collective_id=1, has_side_effects=True, vmem_limit_bytes=VMEM_LIMIT),
        cost_estimate=pl.CostEstimate(flops=4 * ROWS * ROWS * D, bytes_accessed=64 << 20, transcendentals=0),
        name="reduce",
    )(grads.reshape(-1, PART, D), shares, order, *outs, *ings)
    return total.reshape(-1, BLK, D), vec[0:9].reshape(-1), output, input_grad, entropy


V_BQ, V_BV, V_BO, V_BD, V_G1, V_C1, V_G2, V_C2 = range(8)


def inverse(x):
    r = pl.reciprocal(x, approx=True)
    return r * (2.0 - x * r)


def erf_parts(v):
    t = inverse(1.0 + (0.3275911 / math.sqrt(2.0)) * jnp.abs(v))
    e = jnp.exp2((v * v) * (-0.5 / math.log(2.0)))
    poly = 0.5 * 1.061405429
    for c in (-1.453152027, 1.421413741, -0.284496736, 0.254829592):
        poly = poly * t + 0.5 * c
    tail = poly * (t * e)
    return jnp.where(v >= 0.0, 1.0 - tail, tail), e


def lane_sum(x):
    return jnp.sum(x, axis=1, keepdims=True)


def gelu_parts(v):
    phi, e = erf_parts(v)
    return v * phi, phi + v * (e * (1.0 / math.sqrt(2.0 * math.pi)))


def weight_copies(pos, slots, w, sem, first):
    def copy(b):
        return pltpu.make_async_copy(slots.at[pos[first + b]], w.at[pl.ds(b * BLK, BLK)], sem)

    n = w.shape[0] // BLK
    return (lambda: loop(n, lambda b: copy(b).start())), (lambda: loop(n, lambda b: copy(b).wait()))


def halves_of_heads():
    lane = lax.broadcasted_iota(I32, (1, PW), 1)
    m0 = jnp.where(lane < HD, 1.0, 0.0).astype(BF)
    m1 = jnp.where(lane < HD, 0.0, 1.0).astype(BF)
    return lambda pair: jnp.concatenate([pair * m0, pair * m1], axis=0)


def tile_rows(t):
    return pl.ds(pl.multiple_of(t * TM, TM), TM)


def forward_kernel(
    cap,
    pos,
    slots,
    vecs,
    b_u,
    x_h,
    meta,
    back_0,
    back_1,
    back_2,
    back_3,
    heads_h,
    act_h,
    hid_h,
    q_h,
    k_h,
    v_h,
    p_h,
    slope_h,
    n1_h,
    n2_h,
    rs1_h,
    rs2_h,
    wqkv,
    wo,
    wu,
    wd,
    x_c,
    heads,
    act,
    hid,
    q,
    k,
    v,
    p_all,
    slope,
    n1,
    n2,
    rs1,
    rs2,
    out_c,
    ent,
    w_sem,
    x_sem,
    o_sem,
):
    inv = 1.0 / math.sqrt(HD)
    get_x = pltpu.make_async_copy(x_h, x_c, x_sem)
    get_x.start()
    weights = [
        weight_copies(pos, slots, w, w_sem.at[i], first)
        for i, (w, first) in enumerate(((wqkv, 0), (wo, 24), (wu, 32), (wd, 64)))
    ]
    for start, _ in weights:
        start()
    get_x.wait()
    apart = halves_of_heads()

    def vec(i):
        return vecs[i : i + 1, :]

    saved = (
        (heads, heads_h),
        (act, act_h),
        (hid, hid_h),
        (q, q_h),
        (k, k_h),
        (v, v_h),
        (slope, slope_h),
        (n1, n1_h),
        (n2, n2_h),
        (rs1, rs1_h),
        (rs2, rs2_h),
    )

    def save(t, i):
        src, dst = saved[i]
        return pltpu.make_async_copy(src.at[tile_rows(t)], dst.at[tile_rows(t)], o_sem.at[i])

    def save_p(t):
        n = TM // CL
        cs = pl.ds(t * n, n)
        return pltpu.make_async_copy(p_all.at[cs], p_h.at[cs], o_sem.at[len(saved)])

    def normal(r, n, rs, rows):
        c = r - lane_sum(r) * (1.0 / D)
        scale = lax.rsqrt(lane_sum(c * c) * (1.0 / D) + norm_epsilon)
        rs[rows, :] = jnp.broadcast_to(scale, (TM, 128))
        n[rows, :] = c * scale

    def project(t):
        rows = tile_rows(t)
        x = x_c[rows, :]
        q[rows, :] = ((mm(x, wqkv[0:D, :]) + vec(V_BQ)).astype(BF).astype(F32) * inv).astype(BF)
        k[rows, :] = mm(x, wqkv[D : 2 * D, :]).astype(BF)
        v[rows, :] = (mm(x, wqkv[2 * D :, :]) + vec(V_BV)).astype(BF)

    def attend(clusters, meanwhile=lambda: None):
        groups = [pl.ds(pl.multiple_of(c * CL, CL), CL) for c in clusters]
        pairs = [(i, p, slice(p * PW, (p + 1) * PW)) for i in range(len(groups)) for p in range(PAIRS)]
        scores = [mm(apart(k[groups[i], ps]), q[groups[i], ps], NT) for i, _, ps in pairs]
        finish = meanwhile()
        total = [jnp.zeros((1, CL), F32)] * len(groups)
        probs = []
        for (i, _, _), both in zip(pairs, scores):
            halves = []
            for h in range(2):
                sh = both[h * CL : (h + 1) * CL]
                sh = sh - jnp.max(sh, axis=0, keepdims=True)
                e = jnp.exp(sh)
                tot = jnp.sum(e, axis=0, keepdims=True)
                r = 1.0 / tot
                total[i] += jnp.log(tot) - jnp.sum(e * sh, axis=0, keepdims=True) * r
                halves.append((e * r).astype(BF))
            probs.append(jnp.concatenate(halves, axis=0))
        mixed = [mm(w, apart(v[groups[i], ps]), TN).astype(BF) for (i, _, ps), w in zip(pairs, probs)]
        if finish is not None:
            finish()
        for (i, p, ps), w, o in zip(pairs, probs, mixed):
            p_all[clusters[i], p] = w
            heads[groups[i], ps] = o
        for i, group in enumerate(groups):
            ent[:, group] = jnp.broadcast_to(total[i] * (1.0 / HEADS), (8, CL))

    def resid_one(t):
        rows = tile_rows(t)
        return x_c[rows, :].astype(F32) + mm(heads[rows, :], wo[...]) + vec(V_BO)

    def norm_one(t, r1):
        rows = tile_rows(t)
        normal(r1, n1, rs1, rows)
        hidden = n1[rows, :] * vec(V_G1) + vec(V_C1)
        hid[rows, :] = hidden.astype(BF)
        n2[rows, :] = hidden

    def widen(t, columns):
        rows = tile_rows(t)
        parts = [pl.ds(pl.multiple_of(f * FC, FC), FC) for f in columns]
        ups = [mm(hid[rows, :], wu[fs, :], NT) for fs in parts]

        def finish():
            for fs, up in zip(parts, ups):
                g, g_slope = gelu_parts(up + b_u[:, fs])
                act[rows, fs] = g.astype(BF)
                slope[rows, fs] = g_slope.astype(BF)

        return finish

    def resid_two(t):
        rows = tile_rows(t)
        return n2[rows, :] + mm(act[rows, :], wd[...]) + vec(V_BD)

    def norm_two(t, r2):
        rows = tile_rows(t)
        normal(r2, n2, rs2, rows)
        out_c[rows, :] = (n2[rows, :] * vec(V_G2) + vec(V_C2)).astype(BF)

    def save_all(t, which):
        for i in which:
            save(t, i).start()

    per = TM // CL
    weights[0][1]()
    project(0)
    attend(range(per))
    weights[1][1]()
    r1 = resid_one(0)
    project(1)
    norm_one(0, r1)
    save_all(0, (0, 3, 4, 5))
    save_p(0).start()
    weights[2][1]()
    loop(per, lambda c: attend([per + c], lambda: widen(0, [c])))
    save_all(0, (1, 2, 6, 7, 9))
    save_all(1, (0, 3, 4, 5))
    save_p(1).start()
    weights[3][1]()
    r2 = resid_two(0)
    r1 = resid_one(1)
    norm_two(0, r2)
    norm_one(1, r1)
    save_all(0, (8, 10))
    loop(FF // FC // 2, lambda f: widen(1, [2 * f, 2 * f + 1])())
    save_all(1, (1, 2, 6, 7, 9))
    norm_two(1, resid_two(1))
    save_all(1, (8, 10))

    for j, back in enumerate((back_0, back_1, back_2, back_3)):
        own = seat_part(meta, j, cap)
        back[0:cap, :] = mm(own, out_c[...], TN).astype(BF)
        line = mm(ent[...].astype(BF), own)
        back[cap:, :] = jnp.concatenate([line, line], axis=1)[0:1].astype(BF) * jnp.ones((META, 1), BF)

    def saved_all(t):
        for i in range(len(saved)):
            save(t, i).wait()
        save_p(t).wait()

    loop(ROWS // TM, saved_all)


def shape_of(kind, *shape):
    return jax.ShapeDtypeStruct(shape, kind)


def saved_shapes():
    rows, wide = ((ROWS, D), BF), ((ROWS, FF), BF)
    probs = ((ROWS // CL, PAIRS, 2 * CL, CL), BF)
    full, thin = ((ROWS, D), F32), ((ROWS, 128), F32)
    return rows, wide, probs, full, thin


def forward(cap, positions, slots, vecs, b_u, x_c, meta):
    rows, wide, probs, full, thin = saved_shapes()
    kept = (rows, wide, rows, rows, rows, rows, probs, wide, full, full, thin, thin)
    dma = pltpu.SemaphoreType.DMA
    return pl.pallas_call(
        functools.partial(forward_kernel, cap),
        out_shape=(shape_of(BF, cap + META, D),) * SD + tuple(shape_of(kind, *shape) for shape, kind in kept),
        in_specs=[SMEM, ANY, VMEM, VMEM, ANY, VMEM],
        out_specs=(VMEM,) * SD + (ANY,) * len(kept),
        scratch_shapes=[
            pltpu.VMEM((3 * D, D), BF),
            pltpu.VMEM((D, D), BF),
            pltpu.VMEM((FF, D), BF),
            pltpu.VMEM((FF, D), BF),
            pltpu.VMEM(*rows),
        ]
        + [pltpu.VMEM(*a) for a in kept]
        + [
            pltpu.VMEM(*rows),
            pltpu.VMEM((8, ROWS), F32),
            dma((4,)),
            dma,
            dma((12,)),
        ],
        compiler_params=pltpu.CompilerParams(vmem_limit_bytes=VMEM_LIMIT),
        cost_estimate=pl.CostEstimate(flops=2 * ROWS * WROWS * D, bytes_accessed=64 << 20, transcendentals=0),
        name="forward",
    )(positions, slots, vecs, b_u, x_c, meta)


def backward_kernel(
    cap,
    pos,
    slots,
    vecs,
    meta,
    cot_0,
    cot_1,
    cot_2,
    cot_3,
    q_h,
    k_h,
    v_h,
    p_h,
    slope_h,
    n1_h,
    n2_h,
    rs1_h,
    rs2_h,
    back_0,
    back_1,
    back_2,
    back_3,
    shares,
    d_up_h,
    d_q_h,
    d_k_h,
    d_v_h,
    d_proj_h,
    d_br_h,
    wqkv,
    wo,
    wu,
    wd,
    blocks,
    q,
    k,
    v,
    p_all,
    d_up,
    n1,
    n2,
    rs1,
    rs2,
    d_proj,
    d_br,
    ing_c,
    d_h_t,
    gvec,
    g_bu,
    w_sem,
    c_sem,
    i_sem,
    o_sem,
):
    inv = 1.0 / math.sqrt(HD)
    get_c = [
        pltpu.make_async_copy(cot, blocks.at[j], c_sem.at[j]) for j, cot in enumerate((cot_0, cot_1, cot_2, cot_3))
    ]
    for copy in get_c:
        copy.start()
    fetch = [
        pltpu.make_async_copy(src, dst, i_sem.at[i])
        for i, (src, dst) in enumerate(
            (
                (n2_h, n2),
                (rs2_h, rs2),
                (slope_h, d_up),
                (n1_h, n1),
                (rs1_h, rs1),
                (v_h, v),
                (p_h, p_all),
                (k_h, k),
                (q_h, q),
            )
        )
    ]
    weights = [
        weight_copies(pos, slots, w, w_sem.at[i], first)
        for i, (w, first) in enumerate(((wd, 64), (wu, 32), (wo, 24), (wqkv, 0)))
    ]
    fetch[0].start()
    fetch[1].start()
    weights[0][0]()
    fetch[2].start()
    weights[1][0]()
    fetch[3].start()
    fetch[4].start()
    weights[2][0]()
    for i in range(5, 9):
        fetch[i].start()
    weights[3][0]()
    gvec[...] = jnp.zeros_like(gvec)
    g_bu[...] = jnp.zeros_like(g_bu)
    shares[...] = jnp.zeros_like(shares)
    for copy in get_c:
        copy.wait()
    seat_rows(meta, blocks, cap, d_br)
    apart = halves_of_heads()

    def vec(i):
        return vecs[i : i + 1, :]

    def add_vec(i, value):
        gvec[i : i + 1, :] += jnp.sum(value, axis=0, keepdims=True)

    saved = ((d_up, d_up_h), (q, d_q_h), (k, d_k_h), (v, d_v_h), (d_proj, d_proj_h), (d_br, d_br_h))

    def save(t, i):
        src, dst = saved[i]
        return pltpu.make_async_copy(src.at[tile_rows(t)], dst.at[tile_rows(t)], o_sem.at[i])

    def norm_back(e, n, rs, gain, shift):
        add_vec(gain, e * n)
        add_vec(shift, e)
        eg = e * vec(gain)
        return rs * (eg - lane_sum(eg) * (1.0 / D) - n * (lane_sum(eg * n) * (1.0 / D)))

    def norm_two_back(t):
        rows = tile_rows(t)
        d_r2 = norm_back(d_br[rows, :].astype(F32), n2[rows, :], rs2[rows, 0:1], V_G2, V_C2)
        d_br[rows, :] = d_r2.astype(BF)
        add_vec(V_BD, d_br[rows, :].astype(F32))
        n2[rows, :] = d_r2

    def widen_back(t, columns):
        rows = tile_rows(t)
        parts = [pl.ds(pl.multiple_of(f * FC, FC), FC) for f in columns]
        ups = [mm(d_br[rows, :], wd[fs, :], NT) for fs in parts]

        def finish():
            for fs, up in zip(parts, ups):
                du = (up * d_up[rows, fs].astype(F32)).astype(BF)
                d_up[rows, fs] = du
                g_bu[:, fs] += jnp.sum(du.astype(F32), axis=0, keepdims=True)

        return finish

    def hidden_back(t):
        rows = tile_rows(t)
        return n2[rows, :] + mm(d_up[rows, :], wu[...])

    def norm_one_back(t, d_h):
        rows = tile_rows(t)
        d_r1 = norm_back(d_h, n1[rows, :], rs1[rows, 0:1], V_G1, V_C1)
        d_proj[rows, :] = d_r1.astype(BF)
        n2[rows, :] = d_r1
        add_vec(V_BO, d_proj[rows, :].astype(F32))

    def heads_back(t):
        rows = tile_rows(t)
        d_h_t[rows, :] = mm(d_proj[rows, :], wo[...], NT).astype(BF)

    def attend_back(clusters, meanwhile=lambda: None):
        pairs = [
            (c, p, pl.ds(pl.multiple_of(c * CL, CL), CL), slice(p * PW, (p + 1) * PW))
            for c in clusters
            for p in range(PAIRS)
        ]
        probs = [p_all[c, p] for c, p, _, _ in pairs]
        d_heads = [d_h_t[gr, ps] for _, _, gr, ps in pairs]
        d_probs = [mm(apart(v[gr, ps]), dh, NT) for (_, _, gr, ps), dh in zip(pairs, d_heads)]
        d_values = [
            mm(jnp.concatenate([w[0:CL], w[CL:]], axis=1), apart(dh)).astype(BF) for w, dh in zip(probs, d_heads)
        ]
        finish = meanwhile()
        d_scores = []
        for w, dw in zip(probs, d_probs):
            halves = []
            for h in range(2):
                wh = w[h * CL : (h + 1) * CL].astype(F32)
                dwh = dw[h * CL : (h + 1) * CL]
                halves.append((wh * (dwh - jnp.sum(dwh * wh, axis=0, keepdims=True))).astype(BF))
            d_scores.append(halves)
        d_keys = [
            mm(jnp.concatenate(ds, axis=1), apart(q[gr, ps])).astype(BF) for (_, _, gr, ps), ds in zip(pairs, d_scores)
        ]
        d_queries = [
            (mm(jnp.concatenate(ds, axis=0), apart(k[gr, ps]), TN) * inv).astype(BF)
            for (_, _, gr, ps), ds in zip(pairs, d_scores)
        ]
        if finish is not None:
            finish()
        for (_, _, gr, ps), dq, dk, dv in zip(pairs, d_queries, d_keys, d_values):
            q[gr, ps] = dq
            k[gr, ps] = dk
            v[gr, ps] = dv

    def rows_back(t):
        rows = tile_rows(t)
        return (
            mm(q[rows, :], wqkv[0:D, :], NT)
            + mm(k[rows, :], wqkv[D : 2 * D, :], NT)
            + mm(v[rows, :], wqkv[2 * D :, :], NT)
        )

    def rows_done(t, d_x):
        rows = tile_rows(t)
        add_vec(V_BQ, q[rows, :].astype(F32))
        add_vec(V_BV, v[rows, :].astype(F32))
        ing_c[rows, :] = (n2[rows, :] + d_x.astype(BF).astype(F32)).astype(BF)

    def save_all(t, which):
        for i in which:
            save(t, i).start()

    per = TM // CL
    fetch[0].wait()
    fetch[1].wait()
    norm_two_back(0)
    norm_two_back(1)
    weights[0][1]()
    fetch[2].wait()
    loop(FF // FC // 2, lambda f: widen_back(0, [2 * f, 2 * f + 1])())
    save_all(0, (0, 5))
    weights[1][1]()
    fetch[3].wait()
    fetch[4].wait()
    norm_one_back(0, hidden_back(0))
    weights[2][1]()
    for i in range(5, 9):
        fetch[i].wait()
    heads_back(0)
    save_all(0, (4,))
    loop(per, lambda c: attend_back([c], lambda: widen_back(1, [c])))
    save_all(0, (1, 2, 3))
    save_all(1, (0, 5))
    weights[3][1]()
    d_h = hidden_back(1)
    d_x = rows_back(0)
    norm_one_back(1, d_h)
    heads_back(1)
    rows_done(0, d_x)
    save_all(1, (4,))
    loop(per // BWD_AT, lambda c: attend_back([per + BWD_AT * c + i for i in range(BWD_AT)]))
    save_all(1, (1, 2, 3))
    rows_done(1, rows_back(1))

    for j, back in enumerate((back_0, back_1, back_2, back_3)):
        back[...] = mm(seat_part(meta, j, cap), ing_c[...], TN).astype(BF)

    for chunk in range(72):
        row, lane = chunk // 6, chunk % 6 * 128
        if row < 8:
            part = gvec[row : row + 1, lane : lane + 128]
        else:
            lane += (row - 8) * D
            part = g_bu[:, lane : lane + 128]
        shares[chunk // 9, chunk % 9 : chunk % 9 + 1, :] = part

    def saved_all(t):
        for i in range(len(saved)):
            save(t, i).wait()

    loop(ROWS // TM, saved_all)


def backward(cap, positions, slots, vecs, meta, cots, saved):
    rows, wide, probs, full, thin = saved_shapes()
    dma = pltpu.SemaphoreType.DMA
    grads = (wide, rows, rows, rows, rows, rows)
    return pl.pallas_call(
        functools.partial(backward_kernel, cap),
        out_shape=(shape_of(BF, cap, D),) * SD
        + (shape_of(F32, 8, 16, 128),)
        + tuple(shape_of(kind, *shape) for shape, kind in grads),
        in_specs=[SMEM, ANY, VMEM, VMEM] + [ANY] * (SD + 9),
        out_specs=(VMEM,) * (SD + 1) + (ANY,) * len(grads),
        scratch_shapes=[
            pltpu.VMEM((3 * D, D), BF),
            pltpu.VMEM((D, D), BF),
            pltpu.VMEM((FF, D), BF),
            pltpu.VMEM((FF, D), BF),
            pltpu.VMEM((SD, cap, D), BF),
        ]
        + [pltpu.VMEM(*a) for a in (rows, rows, rows, probs, wide, full, full, thin, thin, rows, rows, rows)]
        + [
            pltpu.VMEM(*rows),
            pltpu.VMEM((8, D), F32),
            pltpu.VMEM((1, FF), F32),
            dma((4,)),
            dma((4,)),
            dma((9,)),
            dma((6,)),
        ],
        compiler_params=pltpu.CompilerParams(vmem_limit_bytes=VMEM_LIMIT),
        cost_estimate=pl.CostEstimate(flops=2 * ROWS * WROWS * D, bytes_accessed=64 << 20, transcendentals=0),
        name="backward",
    )(positions, slots, vecs, meta, *cots, *saved)


WC = 8 * BLK


def weight_kernel(
    pos,
    x_h,
    heads_h,
    act_h,
    d_up_h,
    d_q_h,
    d_k_h,
    d_v_h,
    d_proj_h,
    hid_h,
    d_br_h,
    grads,
    x_c,
    heads,
    act,
    d_up,
    d_q,
    d_k,
    d_v,
    d_proj,
    hid,
    d_br,
    stage,
    i_sem,
    g_sem,
):
    refs = (
        (x_h, x_c),
        (d_q_h, d_q),
        (d_k_h, d_k),
        (d_v_h, d_v),
        (heads_h, heads),
        (d_proj_h, d_proj),
        (hid_h, hid),
        (d_up_h, d_up),
        (d_br_h, d_br),
        (act_h, act),
    )
    fetch = [pltpu.make_async_copy(src, dst, i_sem.at[i]) for i, (src, dst) in enumerate(refs)]
    for copy in fetch:
        copy.start()

    per = WC // BLK

    def g_copy(chunk, j, at):
        return pltpu.make_async_copy(
            stage.at[at, pl.ds(j * BLK, BLK)], grads.at[pos[chunk * per + j]], g_sem.at[at]
        )

    def put(chunk, left, right):
        at = lax.rem(chunk, 2)

        @pl.when(chunk >= 2)
        def _():
            for j in range(per):
                g_copy(chunk - 2, j, at).wait()

        stage[at] = mm(left, right, TN).astype(BF)
        for j in range(per):
            g_copy(chunk, j, at).start()

    first = 0
    for left, right, needs in (
        (x_c, d_q, (0, 1)),
        (x_c, d_k, (2,)),
        (x_c, d_v, (3,)),
        (heads, d_proj, (4, 5)),
        (d_up, hid, (6, 7)),
        (act, d_br, (8, 9)),
    ):
        for i in needs:
            fetch[i].wait()

        def body(j, left=left, right=right, first=first):
            put(first + j, left[:, pl.ds(pl.multiple_of(j * WC, WC), WC)], right[...])

        loop(left.shape[1] // WC, body)
        first += left.shape[1] // WC
    for chunk in (first - 2, first - 1):
        for j in range(per):
            g_copy(chunk, j, chunk % 2).wait()


def weight_grads_of(total_slots, positions, x_c, saved):
    r_v, w_v = pltpu.VMEM((ROWS, D), BF), pltpu.VMEM((ROWS, FF), BF)
    return pl.pallas_call(
        weight_kernel,
        out_shape=jax.ShapeDtypeStruct((total_slots, BLK, D), BF),
        in_specs=[SMEM] + [ANY] * 10,
        out_specs=ANY,
        scratch_shapes=[r_v, r_v, w_v, w_v]
        + [r_v] * 6
        + [
            pltpu.VMEM((2, WC, D), BF),
            pltpu.SemaphoreType.DMA((10,)),
            pltpu.SemaphoreType.DMA((2,)),
        ],
        compiler_params=pltpu.CompilerParams(vmem_limit_bytes=VMEM_LIMIT),
        cost_estimate=pl.CostEstimate(flops=2 * ROWS * WROWS * D, bytes_accessed=40 << 20, transcendentals=0),
        name="weight_grads",
    )(positions, x_c, *saved)


def local(
    tokens,
    cotangent,
    cluster_order,
    block_owner,
    master_slots,
    moment_one,
    moment_two,
    vector_master,
    vector_moment_one,
    vector_moment_two,
):
    tok_count = lax.axis_size("tok")
    tok_index = lax.axis_index("tok")
    slot_count = master_slots.shape[0]
    cap = tok_count // SD * (max(1, CPS // tok_count) * 3 * CL // (2 * SD))
    total_slots = tok_count * slot_count
    order = cluster_order.reshape(1, ROWS)

    block = jax.ShapeDtypeStruct((SD, cap, D), BF)
    meta_shape = jax.ShapeDtypeStruct((SD, META, D), BF)
    row_block = jax.ShapeDtypeStruct((ROWS, D), BF)
    four_planes = tok_count == 8 and lax.axis_size("rep") == 4
    if four_planes:
        slots_low, x_c, *cots, recv_meta, vecs, b_u, occupancy, positions = gather_all(
            cap, tokens, cotangent, order, master_slots, vector_master, block_owner
        )
        positions = positions.reshape(NBLK)
        slots_low = slots_low.reshape(total_slots, BLK, D)
    else:
        positions = slot_positions(block_owner, slot_count)
        slots_low = lax.all_gather(master_slots.astype(BF), "tok", axis=0, tiled=True)
        vectors = lax.all_gather(vector_master.astype(BF), "tok", axis=0, tiled=True).astype(F32)
        vecs, b_u = vectors[: 8 * D].reshape(8, D), vectors[8 * D :].reshape(1, FF)
        cluster = tok_index // SD * CPS + cluster_order // CL
        target = cluster % tok_count
        chosen = target[None, :] == jnp.arange(tok_count, dtype=jnp.int32)[:, None]
        sent_counts = jnp.sum(chosen.astype(F32), axis=1)
        own_row = (jnp.arange(tok_count, dtype=jnp.int32) == tok_index).astype(F32)
        occupancy = lax.psum(own_row[:, None] * sent_counts[None, :], ("tok", "rep")).astype(jnp.int32)
        send_x, send_c, meta = pl.pallas_call(
            functools.partial(send_kernel, cap),
            out_shape=(block, block, meta_shape),
            in_specs=[VMEM] * 3,
            out_specs=(VMEM,) * 3,
            compiler_params=pltpu.CompilerParams(vmem_limit_bytes=VMEM_LIMIT),
            name="send_rows",
        )(tokens, cotangent, order)
        recv_x, recv_meta = (jnp.stack(swap_blocks(b)) for b in (send_x, meta))
        x_c = pl.pallas_call(
            functools.partial(seat_kernel, cap),
            out_shape=row_block,
            in_specs=[VMEM] * 2,
            out_specs=VMEM,
            compiler_params=pltpu.CompilerParams(vmem_limit_bytes=VMEM_LIMIT),
            name="seat_rows",
        )(recv_x, recv_meta)
        cots = [send_c[k] for k in range(SD)]

    cots = swap_blocks(cots)
    *out_blocks, heads, act, hid, q, k, v, p, slope, n1, n2, rs1, rs2 = forward(
        cap, positions, slots_low, vecs, b_u, x_c, recv_meta
    )
    out_blocks = swap_blocks(out_blocks)
    *ing_blocks, shares, d_up, d_q, d_k, d_v, d_proj, d_br = backward(
        cap, positions, slots_low, vecs, recv_meta, cots, (q, k, v, p, slope, n1, n2, rs1, rs2)
    )
    ing_blocks = swap_blocks(ing_blocks)
    grads = weight_grads_of(
        total_slots, positions, x_c, (heads, act, d_up, d_q, d_k, d_v, d_proj, hid, d_br)
    )
    if four_planes:
        total, vec_owned, output, input_grad, entropy = reduce_all(
            cap, grads, shares, order, out_blocks, ing_blocks, slot_count
        )
    else:
        total = lax.psum(lax.psum_scatter(grads, "tok", scatter_dimension=0, tiled=True), "rep")
        grad_vector = shares[:, 0:9].reshape(-1)
        vec_owned = lax.psum(lax.psum_scatter(grad_vector, "tok", scatter_dimension=0, tiled=True), "rep")
        output, input_grad, entropy = pl.pallas_call(
            functools.partial(return_kernel, cap),
            out_shape=(row_block, row_block, jax.ShapeDtypeStruct((1, ROWS), BF)),
            in_specs=[VMEM] * (2 * SD + 1),
            out_specs=(VMEM,) * 3,
            compiler_params=pltpu.CompilerParams(vmem_limit_bytes=VMEM_LIMIT),
            name="return_rows",
        )(order, *out_blocks, *ing_blocks)

    used = jnp.any(
        positions[None, :] == (tok_index * slot_count + jnp.arange(slot_count, dtype=I32))[:, None], axis=1
    )
    owned_grad = jnp.where(used[:, None, None], total.astype(F32), 0.0)
    first_new, second_new, master_new = adam_update(
        owned_grad, master_slots, moment_one, moment_two, rate_matrix
    )
    vec_first, vec_second, vec_new = adam_update(
        vec_owned, vector_master, vector_moment_one, vector_moment_two, rate_vector
    )
    return (
        output,
        input_grad,
        owned_grad,
        first_new,
        second_new,
        master_new,
        master_new.astype(BF),
        vec_owned,
        vec_first,
        vec_second,
        vec_new,
        vec_new.astype(BF),
        entropy.reshape(-1),
        occupancy,
    )


def solution(mesh):
    placed = (
        P(("rep", "tok"), None),
        P(("rep", "tok"), None),
        P(("rep", "tok")),
        P(),
        P("tok", None, None),
        P("tok", None, None),
        P("tok", None, None),
        P("tok"),
        P("tok"),
        P("tok"),
    )
    return jax.shard_map(
        local,
        mesh=mesh,
        in_specs=placed,
        out_specs=(
            P(("rep", "tok"), None),
            P(("rep", "tok"), None),
            P("tok", None, None),
            P("tok", None, None),
            P("tok", None, None),
            P("tok", None, None),
            P("tok", None, None),
            P("tok"),
            P("tok"),
            P("tok"),
            P("tok"),
            P("tok"),
            P(("rep", "tok")),
            P(),
        ),
        check_vma=False,
    )
```

```python
import functools
import math

import jax
import jax.numpy as jnp
from jax import lax
from jax.experimental import pallas as pl
from jax.experimental.pallas import tpu as pltpu
from jax.sharding import PartitionSpec as P

D = 768
HEADS = 12
HD = 64
FF = 3072
SD = 4
CL = 128
NBLK = 96
STEP = 10
CPS = 32
WROWS = 9216
BLK = 96
ROWS = 1024
PAIRS = HEADS // 2
PW = 2 * HD
TM = 512
PART = 48
META = 16
VMEM_LIMIT = 63 << 20
FC = 768
FWD_AT = 4
BWD_AT = 2
NC = 256

norm_epsilon = 1e-06
beta_first = 0.9
beta_second = 0.999
adam_epsilon = 1e-08
weight_decay = 0.01
rate_matrix = 0.02
rate_vector = 0.2

BF = jnp.bfloat16
F32 = jnp.float32
I32 = jnp.int32

VMEM = pl.BlockSpec(memory_space=pltpu.VMEM)
SMEM = pl.BlockSpec(memory_space=pltpu.SMEM)
ANY = pl.BlockSpec(memory_space=pl.ANY)

NN = (((1,), (0,)), ((), ()))
NT = (((1,), (1,)), ((), ()))
TN = (((0,), (0,)), ((), ()))


def mm(a, b, dims=NN):
    return lax.dot_general(a, b, dims, preferred_element_type=F32)


def slot_positions(block_owner, slot_count):
    owners = block_owner[:, 0]
    blocks = owners.shape[0]
    shared = owners[:, None] == owners[None, :]
    before = (
        jnp.arange(blocks, dtype=jnp.int32)[None, :] < jnp.arange(blocks, dtype=jnp.int32)[:, None]
    )
    earlier = jnp.sum((shared & before).astype(jnp.int32), axis=1)
    return owners * slot_count + earlier


def adam_update(grad_now, weight_old, first_old, second_old, rate_step):
    first_new = beta_first * first_old + (1.0 - beta_first) * grad_now
    second_new = beta_second * second_old + (1.0 - beta_second) * grad_now * grad_now
    first_hat = first_new / (1.0 - beta_first**STEP)
    second_hat = second_new / (1.0 - beta_second**STEP)
    weight_new = weight_old - rate_step * (
        first_hat / (jnp.sqrt(second_hat) + adam_epsilon) + weight_decay * weight_old
    )
    return (first_new, second_new, weight_new)


def route_slots(order, seat, cap):
    cluster = order // CL
    rel = lax.rem(cluster, SD) ^ seat
    place = (cluster // SD) * CL + lax.rem(order, CL) + 1
    chosen = lax.broadcasted_iota(I32, (8, ROWS), 0) == rel
    chosen_low = jnp.where(chosen, 1.0, 0.0).astype(BF)
    before = lax.broadcasted_iota(I32, (ROWS, ROWS), 0) < lax.broadcasted_iota(I32, (ROWS, ROWS), 1)
    before_low = jnp.where(before, 1.0, 0.0).astype(BF)
    running = mm(chosen_low, before_low)
    rank = jnp.sum(jnp.where(chosen, running, 0.0), axis=0, keepdims=True).astype(I32)
    return rel * cap + rank, place


def slot_matrix(slots, at, cap):
    rows = lax.broadcasted_iota(I32, (cap, ROWS), 0) + at * cap
    return jnp.where(rows == slots, 1.0, 0.0).astype(BF)


def send_kernel(cap, tokens, cotangent, order, send_x, send_c, meta):
    seat = lax.rem(lax.axis_index("tok"), SD)
    slots, place = route_slots(order[...], seat, cap)
    digits = jnp.concatenate([place // CL, lax.rem(place, CL)] + [place * 0] * 6, axis=0).astype(F32).astype(BF)
    for at in range(SD):
        picked = slot_matrix(slots, at, cap)
        send_x[at] = mm(picked, tokens[...]).astype(BF)
        send_c[at] = mm(picked, cotangent[...]).astype(BF)
        coded = mm(digits, picked, NT)
        line = jnp.concatenate([coded[0:1], coded[1:2]], axis=1)
        meta[at] = jnp.broadcast_to(line, (META, D)).astype(BF)


def remote(src, dst, send_sem, recv_sem, tok, rep):
    return pltpu.make_async_remote_copy(
        src_ref=src,
        dst_ref=dst,
        send_sem=send_sem,
        recv_sem=recv_sem,
        device_id={"tok": tok, "rep": rep},
        device_id_type=pl.DeviceIdType.MESH,
    )


def loop(n, body):
    def run(i, c):
        body(i)
        return c

    lax.fori_loop(0, n, run, 0)


class Place:
    def __init__(self):
        self.me = me = lax.axis_index("tok")
        self.z = z = lax.axis_index("rep")
        core, x, y = me % 2, (me // 2) % 2, me // 4
        self.twin = me + 1 - 2 * core
        self.xn = me + 2 - 4 * x
        self.yn = me + 4 - 8 * y
        self.dn = self.xn + 4 - 8 * y
        self.side = z % 2
        self.zp = z + 1 - 2 * self.side

    def twin_of(self, tok):
        return tok + 1 - 2 * (tok % 2)

    def greet(self, peers):
        barrier = pltpu.get_barrier_semaphore()
        for tok, rep in peers:
            pl.semaphore_signal(
                barrier, inc=1, device_id={"tok": tok, "rep": rep}, device_id_type=pl.DeviceIdType.MESH
            )
        return lambda: pl.semaphore_wait(barrier, len(peers))


def seat_matrix(meta, first, rows, cap):
    hi = jnp.concatenate([meta[k, 0:8, 0:cap] for k in range(SD)], axis=1).astype(F32)[0:1]
    lo = jnp.concatenate([meta[k, 0:8, cap : 2 * cap] for k in range(SD)], axis=1).astype(F32)[0:1]
    at = (hi * CL + lo).astype(I32)
    seats = lax.broadcasted_iota(I32, (rows, SD * cap), 0) + (first + 1)
    return jnp.where(seats == at, 1.0, 0.0).astype(BF)


def seat_part(meta, k, cap):
    hi = meta[k, 0:8, 0:cap].astype(F32)[0:1]
    lo = meta[k, 0:8, cap : 2 * cap].astype(F32)[0:1]
    at = (hi * CL + lo).astype(I32)
    seats = lax.broadcasted_iota(I32, (ROWS, cap), 0) + 1
    return jnp.where(seats == at, 1.0, 0.0).astype(BF)


def seat_rows(meta, blocks, cap, to):
    def body(t):
        r0 = pl.multiple_of(t * 256, 256)
        rows = blocks[...].reshape(SD * cap, D)
        to[pl.ds(r0, 256), :] = mm(seat_matrix(meta, r0, 256, cap), rows).astype(BF)

    loop(ROWS // 256, body)


def seat_kernel(cap, blocks, meta, to):
    seat_rows(meta, blocks, cap, to)


def gather_kernel(
    cap,
    count,
    tokens_h,
    cotangent_h,
    order,
    master_h,
    vector,
    owner_of,
    slots,
    x_c,
    cot_0,
    cot_1,
    cot_2,
    cot_3,
    recv_meta,
    vecs,
    b_u,
    occupancy,
    positions,
    tokens,
    cotangent,
    master,
    own,
    send_x,
    send_c,
    meta,
    recv_x,
    got_meta,
    slot_of,
    digits,
    mine,
    by_z,
    by_tok,
    x_s,
    x_r,
    y_s,
    y_r,
    d_s,
    d_r,
    zx_s,
    zx_r,
    zd_s,
    zd_r,
    zy_s,
    zy_r,
    p_s,
    p_r,
    row_s,
    row_r,
    z_s,
    z_r,
    t_s,
    t_r,
    local_s,
):
    at = Place()
    me, z, side = at.me, at.z, at.side
    n_tok, n_rep = 8, 4
    peers = [((me + d) % n_tok, z) for d in range(1, n_tok)] + [(me, (z + d) % n_rep) for d in range(1, n_rep)]
    fetch = [
        pltpu.make_async_copy(src, dst, local_s.at[i])
        for i, (src, dst) in enumerate(((master_h, master), (tokens_h, tokens), (cotangent_h, cotangent)))
    ]
    for copy in fetch:
        copy.start()
    wait_peers = at.greet(peers)
    fetch[0].wait()

    last = count - 1

    def near(j):
        return side * last + (1 - 2 * side) * j

    def far(j):
        return (1 - side) * last - (1 - 2 * side) * j

    few_x, few_d, few_y = 11 * count // 26, 12 * count // 26, 8 * count // 26
    most_x, most_d, most_y = count - few_x, count - few_d, count - few_y

    def piece(owner, s):
        return slots.at[owner * count + s]

    def to_x(s):
        return remote(own.at[s], piece(me, s), x_s.at[s], x_r.at[s], at.xn, z)

    def to_y(s):
        return remote(own.at[s], piece(me, s), y_s.at[s], y_r.at[s], at.yn, z)

    def on_y(s):
        return remote(piece(at.xn, s), piece(at.xn, s), d_s.at[s], d_r.at[s], at.yn, z)

    def x_on_z(s):
        return remote(piece(at.xn, s), piece(at.xn, s), zx_s.at[s], zx_r.at[s], me, at.zp)

    def d_on_z(s):
        return remote(piece(at.dn, s), piece(at.dn, s), zd_s.at[s], zd_r.at[s], me, at.zp)

    def y_on_z(s):
        return remote(piece(at.yn, s), piece(at.yn, s), zy_s.at[s], zy_r.at[s], me, at.zp)

    def x_in(s):
        return remote(own.at[s], piece(at.xn, s), x_s.at[s], x_r.at[s], at.xn, z)

    def y_in(s):
        return remote(own.at[s], piece(at.yn, s), y_s.at[s], y_r.at[s], at.yn, z)

    def d_in(s):
        return remote(own.at[s], piece(at.dn, s), d_s.at[s], d_r.at[s], at.yn, z)

    owners = (me, at.xn, at.yn, at.dn)

    def near_run(q, j0, j1):
        return (q, (1 - side) * j0 + side * (count - j1), j1 - j0)

    def far_run(q, j0, j1):
        return (q, side * j0 + (1 - side) * (count - j1), j1 - j0)

    runs = (
        (0, 0, count),
        near_run(2, 0, few_y),
        near_run(1, 0, most_x),
        near_run(3, 0, most_d),
        far_run(1, 0, few_x),
        near_run(2, few_y, most_y),
        far_run(2, 0, few_y),
        far_run(3, 0, few_d // 2),
        far_run(3, few_d // 2, few_d - 2),
        far_run(3, few_d - 2, few_d),
    )

    def to_twin(i):
        q, s, n = runs[i]
        src = own if q == 0 else slots.at[pl.ds(owners[q] * count + s, n)]
        dst = slots.at[pl.ds(owners[q] * count + s, n)]
        return remote(src, dst, p_s.at[i], p_r.at[i], at.twin, z)

    def cast(j):
        own[near(j)] = master[near(j)].astype(BF)

    loop(most_x, cast)
    wait_peers()
    loop(most_x, lambda j: to_x(near(j)).start())
    loop(few_y, lambda j: to_y(near(j)).start())
    loop(count - most_x, lambda j: cast(most_x + j))
    to_twin(0).start()
    keep = pltpu.make_async_copy(own, slots.at[pl.ds(me * count, count)], local_s.at[3])
    keep.start()

    seat = me % SD
    seats = (me, at.twin, at.xn, at.twin_of(at.xn))
    rows_of = ((meta, got_meta), (send_x, recv_x))

    def row_copy(i, k):
        src, dst = rows_of[i]
        return remote(src.at[k], dst.at[k], row_s.at[i, k], row_r.at[i, k], seats[k], z)

    put_c = [
        pltpu.make_async_copy(send_c.at[k], to, local_s.at[4 + k])
        for k, to in enumerate((cot_0, cot_1, cot_2, cot_3))
    ]

    def route():
        fetch[1].wait()
        fetch[2].wait()
        slots_here, place = route_slots(order[...], seat, cap)
        slot_of[...] = slots_here
        digits[...] = (
            jnp.concatenate([place // CL, lax.rem(place, CL)] + [place * 0] * 6, axis=0).astype(F32).astype(BF)
        )

    def sort_tokens(k):
        picked = slot_matrix(slot_of[...], k, cap)
        send_x[k] = mm(picked, tokens[...]).astype(BF)
        coded = mm(digits[...], picked, NT)
        line = jnp.concatenate([coded[0:1], coded[1:2]], axis=1)
        meta[k] = jnp.broadcast_to(line, (META, D)).astype(BF)
        for i in range(2):
            if k:
                row_copy(i, k).start()
            else:
                src, dst = rows_of[i]
                dst[0] = src[0]

    def sort_cotangent(k):
        send_c[k] = mm(slot_matrix(slot_of[...], k, cap), cotangent[...]).astype(BF)
        put_c[k].start()

    def z_copy(d):
        return remote(by_z.at[0], by_z.at[d], z_s.at[d], z_r.at[d], me, (z + d) % n_rep)

    def t_copy(d):
        return remote(mine, by_tok.at[d], t_s.at[d], t_r.at[d], (me + d) % n_tok, z)

    def count_rows():
        residue = lax.rem(me // SD * CPS + order[...] // CL, n_tok)
        hit = lax.broadcasted_iota(I32, (128, ROWS), 0) == residue
        by_z[0] = mm(jnp.ones((8, ROWS), BF), jnp.where(hit, 1.0, 0.0).astype(BF), NT)
        for d in range(1, n_rep):
            z_copy(d).start()
        for i in range(9):
            mine[i : i + 1] = vector[i * 128 : (i + 1) * 128].reshape(1, 128).astype(BF).astype(F32)
        block_row = lax.broadcasted_iota(I32, (NBLK, NBLK), 0)
        block_col = lax.broadcasted_iota(I32, (NBLK, NBLK), 1)
        by_col = owner_of[...].astype(F32)
        by_row = lane_sum(jnp.where(block_row == block_col, by_col, 0.0))
        earlier = jnp.where((by_row == by_col) & (block_row < block_col), 1.0, 0.0)
        positions[...] = (by_col * (count * PART // BLK) + jnp.sum(earlier, axis=0, keepdims=True)).astype(I32)

    def share_vectors():
        for d in range(1, n_rep):
            z_copy(d).wait()
        mine[16:24] = by_z[0] + by_z[1] + by_z[2] + by_z[3]
        for d in range(1, n_tok):
            t_copy(d).start()

    def lay_out_vectors():
        by_tok[0] = mine[...]
        for d in range(1, n_tok):
            t_copy(d).wait()
        for owner in range(n_tok):
            share = by_tok[(me + n_tok - owner) % n_tok]
            occupancy[owner : owner + 1, :] = share[16:17, 0:n_tok].astype(I32)
            for i in range(9):
                chunk = owner * 9 + i
                row, lane = chunk // 6, chunk % 6 * 128
                if row < 8:
                    vecs[row : row + 1, lane : lane + 128] = share[i : i + 1]
                else:
                    lane += (row - 8) * D
                    b_u[:, lane : lane + 128] = share[i : i + 1]

    between = {
        1: lambda: (route(), sort_tokens(2)),
        3: lambda: sort_tokens(3),
        5: lambda: sort_tokens(1),
        7: lambda: (sort_tokens(0), count_rows()),
        9: lambda: sort_cotangent(1),
        11: lambda: sort_cotangent(2),
        13: lambda: sort_cotangent(3),
    }
    for j in range(most_x):
        x_in(near(j)).wait_recv()
        if j < most_d:
            on_y(near(j)).start()
        if j < few_x:
            x_on_z(near(j)).start()
        if j < few_y:
            y_in(near(j)).wait_recv()
            y_on_z(near(j)).start()
        if j == few_y:
            to_twin(1).start()
        if j in between:
            between[j]()
    to_twin(2).start()
    loop(most_y - few_y, lambda j: to_y(near(few_y + j)).start())
    share_vectors()
    sort_cotangent(0)

    def diagonal(j):
        d_in(near(j)).wait_recv()
        d_on_z(near(j)).start()

    loop(few_d, diagonal)
    loop(most_d - few_d, lambda j: d_in(near(few_d + j)).wait_recv())
    to_twin(3).start()
    loop(few_x, lambda j: x_on_z(far(j)).wait_recv())
    to_twin(4).start()
    lay_out_vectors()
    loop(most_y - few_y, lambda j: y_in(near(few_y + j)).wait_recv())
    to_twin(5).start()
    loop(few_y, lambda j: y_on_z(far(j)).wait_recv())
    to_twin(6).start()
    for i in (0, 1):
        for k in (2, 3, 1):
            row_copy(i, k).wait_recv()
    recv_meta[...] = got_meta[...]
    seat_rows(got_meta, recv_x, cap, x_c)
    done = 0
    for i, upto in ((7, few_d // 2), (8, few_d - 2), (9, few_d)):
        loop(upto - done, lambda j, done=done: d_on_z(far(done + j)).wait_recv())
        to_twin(i).start()
        done = upto

    for i in range(2):
        for k in (2, 3, 1):
            row_copy(i, k).wait_send()
    for copy in put_c:
        copy.wait()
    keep.wait()

    loop(most_x, lambda j: to_x(near(j)).wait_send())
    loop(most_y, lambda j: to_y(near(j)).wait_send())
    loop(most_d, lambda j: on_y(near(j)).wait_send())
    loop(few_x, lambda j: x_on_z(near(j)).wait_send())
    loop(few_d, lambda j: d_on_z(near(j)).wait_send())
    loop(few_y, lambda j: y_on_z(near(j)).wait_send())
    for i in range(len(runs)):
        to_twin(i).wait()


def gather_all(cap, tokens, cotangent, order, master, vector, block_owner):
    count = master.shape[0] * BLK // PART
    rows = jax.ShapeDtypeStruct((ROWS, D), BF)
    part = jax.ShapeDtypeStruct((cap, D), BF)
    dma = pltpu.SemaphoreType.DMA
    block = pltpu.VMEM((SD, cap, D), BF)
    meta = pltpu.VMEM((SD, META, D), BF)
    return pl.pallas_call(
        functools.partial(gather_kernel, cap, count),
        out_shape=(
            jax.ShapeDtypeStruct((8 * count, PART, D), BF),
            rows,
            part,
            part,
            part,
            part,
            jax.ShapeDtypeStruct((SD, META, D), BF),
            jax.ShapeDtypeStruct((8, D), F32),
            jax.ShapeDtypeStruct((1, FF), F32),
            jax.ShapeDtypeStruct((8, 8), I32),
            jax.ShapeDtypeStruct((1, NBLK), I32),
        ),
        in_specs=[ANY, ANY, VMEM, ANY, VMEM, VMEM],
        out_specs=(ANY, VMEM) + (ANY,) * SD + (VMEM,) * 5,
        scratch_shapes=[
            pltpu.VMEM((ROWS, D), BF),
            pltpu.VMEM((ROWS, D), BF),
            pltpu.VMEM((count, PART, D), F32),
            pltpu.VMEM((count, PART, D), BF),
            block,
            block,
            meta,
            block,
            meta,
            pltpu.VMEM((1, ROWS), I32),
            pltpu.VMEM((8, ROWS), BF),
            pltpu.VMEM((24, 128), F32),
            pltpu.VMEM((4, 8, 128), F32),
            pltpu.VMEM((8, 24, 128), F32),
        ]
        + [dma((count,))] * 12
        + [dma((10,))] * 2
        + [dma((2, SD))] * 2
        + [dma((4,))] * 2
        + [dma((8,))] * 2
        + [dma((8,))],
        compiler_params=pltpu.CompilerParams(collective_id=0, has_side_effects=True, vmem_limit_bytes=VMEM_LIMIT),
        cost_estimate=pl.CostEstimate(flops=8 * ROWS * ROWS * D, bytes_accessed=64 << 20, transcendentals=0),
        name="gather",
    )(tokens, cotangent, order, master.reshape(count, PART, D), vector, block_owner.reshape(1, NBLK))


def return_kernel(cap, order, *refs):
    outs, ings, (out, ing, entropy) = refs[:SD], refs[SD : 2 * SD], refs[2 * SD :]
    seat = lax.rem(lax.axis_index("tok"), SD)
    slots, _ = route_slots(order[...], seat, cap)
    picked = jnp.concatenate([slot_matrix(slots, at, cap) for at in range(SD)], axis=0)
    for to, blocks in ((out, outs), (ing, ings)):
        rows = jnp.concatenate([block[0:cap, :] for block in blocks], axis=0)
        to[...] = mm(picked, rows, TN).astype(BF)
    line = jnp.concatenate([block[cap : cap + 8, 0:cap] for block in outs], axis=1)
    entropy[...] = mm(line, picked)[0:1].astype(BF)


def swap_blocks(blocks):
    n = lax.axis_size("tok")
    parts = [blocks[0]]
    for k in range(1, SD):
        parts.append(lax.ppermute(blocks[k], "tok", [(i, i ^ k) for i in range(n)]))
    return parts


def reduce_kernel(
    cap,
    count,
    split,
    grads,
    vec,
    order,
    out_0,
    out_1,
    out_2,
    out_3,
    ing_0,
    ing_1,
    ing_2,
    ing_3,
    total,
    vec_out,
    output,
    input_grad,
    entropy,
    out_v,
    ing_v,
    slot_of,
    a,
    tw,
    rd,
    rx,
    ry,
    o,
    rz1,
    pz,
    rz2,
    fz,
    vt,
    va,
    vb,
    vc,
    a_l,
    keep_l,
    p_s,
    p_r,
    d_s,
    d_r,
    x_s,
    x_r,
    y_s,
    y_r,
    z1_s,
    z1_r,
    z2_s,
    z2_r,
    z3_s,
    z3_r,
    t_s,
    t_r,
    v_s,
    v_r,
    row_l,
):
    at = Place()
    me, z = at.me, at.z
    n_tok, n_rep = 8, 4
    peers = [((me + d) % n_tok, z) for d in range(1, n_tok)] + [(me, (z + d) % n_rep) for d in range(1, n_rep)]
    wait_peers = at.greet(peers)
    owners = (me, at.xn, at.yn, at.dn)

    def load(q):
        return pltpu.make_async_copy(grads.at[pl.ds(owners[q] * count, count)], a.at[q], a_l.at[q])

    for q in (3, 1, 2, 0):
        load(q).start()
    rows_in = [
        pltpu.make_async_copy(src, to.at[k], row_l.at[i, k])
        for i, (blocks, to) in enumerate((((out_0, out_1, out_2, out_3), out_v), ((ing_0, ing_1, ing_2, ing_3), ing_v)))
        for k, src in enumerate(blocks)
    ]
    for copy in rows_in:
        copy.start()
    wait_peers()

    groups = [(g, g * (count // 4), count // 4 if g < 3 else count - 3 * (count // 4)) for g in range(4)]

    def to_twin(q, group):
        g, s, n = group
        src = grads.at[pl.ds(at.twin_of(owners[q]) * count + s, n)]
        return remote(src, tw.at[q, pl.ds(s, n)], p_s.at[q, g], p_r.at[q, g], at.twin, z)

    def d_y(s):
        return remote(a.at[3, s], rd.at[s], d_s.at[s], d_r.at[s], at.yn, z)

    def d_x(s):
        return remote(a.at[3, s], rd.at[s], d_s.at[s], d_r.at[s], at.xn, z)

    def to_x(s):
        return remote(a.at[1, s], rx.at[s], x_s.at[s], x_r.at[s], at.xn, z)

    def to_y(s):
        return remote(a.at[2, s], ry.at[s], y_s.at[s], y_r.at[s], at.yn, z)

    def z_in(s):
        return remote(o.at[s], rz1.at[s], z1_s.at[s], z1_r.at[s], me, at.zp)

    def z_swap(s):
        return remote(pz.at[s], rz2.at[s], z2_s.at[s], z2_r.at[s], me, n_rep - 1 - z)

    def z_out(s):
        return remote(fz.at[s], fz.at[s], z3_s.at[s], z3_r.at[s], me, at.zp)

    def keep(s):
        return pltpu.make_async_copy(fz.at[s], total.at[s], keep_l.at[s])

    for group in groups:
        for q in (3, 1, 2, 0):
            to_twin(q, group).start()

    def v_tok(d):
        return remote(vec.at[(me + d) % n_tok], vt.at[d], t_s.at[d], t_r.at[d], (me + d) % n_tok, z)

    def v_rep(i, src):
        return remote(src, vb.at[i], v_s.at[i], v_r.at[i], me, at.zp if i == 0 else (z + 2) % n_rep)

    for d in range(1, n_tok):
        v_tok(d).start()

    def join(q, s):
        return a[q, s] + tw[q, s]

    def first(s, send):
        a[3, s] = join(3, s)
        send(s).start()

    def plain(q, s, send):
        a[q, s] = join(q, s)
        send(s).start()

    def joined(q, s, arrived, send):
        arrived(s).wait_recv()
        a[q, s] = join(q, s) + rd[s]
        send(s).start()

    inner = (z == 1) | (z == 2)
    outer = (z == 0) | (z == 3)

    def own(s):
        to_x(s).wait_recv()
        to_y(s).wait_recv()
        o[s] = join(0, s) + (rx[s] + ry[s])
        pl.when(outer)(lambda: z_in(s).start())

    def middle(s):
        @pl.when(inner)
        def _():
            z_in(s).wait_recv()
            pz[s] = o[s] + rz1[s]
            z_swap(s).start()

    def last(s):
        @pl.when(inner)
        def _():
            z_swap(s).wait_recv()
            fz[s] = pz[s] + rz2[s]
            z_out(s).start()
            keep(s).start()

    def taken(s):
        @pl.when(outer)
        def _():
            z_out(s).wait_recv()
            keep(s).start()

    def pick_rows(i):
        ts = pl.ds(pl.multiple_of(i * 256, 256), 256)
        hit = lax.broadcasted_iota(I32, (SD * cap, 256), 0) == slot_of[:, ts]
        picked = jnp.where(hit, 1.0, 0.0).astype(BF)
        outs = jnp.concatenate([out_v[k, 0:cap, :] for k in range(SD)], axis=0)
        ings = jnp.concatenate([ing_v[k] for k in range(SD)], axis=0)
        both = mm(picked, jnp.concatenate([outs, ings], axis=1), TN)
        output[ts, :] = both[:, 0:D].astype(BF)
        input_grad[ts, :] = both[:, D:].astype(BF)
        line = jnp.concatenate([out_v[k, cap : cap + 8, 0:cap] for k in range(SD)], axis=1)
        entropy[:, ts] = mm(line, picked)[0:1].astype(BF)

    for q in (3, 1, 2, 0):
        load(q).wait()

    def steps(i, lag, more):
        s = i - lag
        by_x = (s % 2 == 0) & (s < 2 * split)
        live = (s >= 0) & (s < count)
        pl.when(live & by_x)(lambda: more(s, True))
        pl.when(live & jnp.logical_not(by_x))(lambda: more(s, False))

    def steps_of(i, lag, more):
        pl.when((i >= lag) & (i < count + lag))(lambda: more(i - lag))

    def round_of(i):
        for group in groups:

            @pl.when(i == group[1])
            def _(group=group):
                to_twin(3, group).wait_recv()

            @pl.when(i == group[1] + 1)
            def _(group=group):
                to_twin(1, group).wait_recv()
                to_twin(2, group).wait_recv()

            @pl.when(i == group[1] + 6)
            def _(group=group):
                to_twin(0, group).wait_recv()

        steps(i, 0, lambda s, by_x: first(s, d_x if by_x else d_y))
        steps(i, 1, lambda s, by_x: plain(1, s, to_x) if by_x else plain(2, s, to_y))
        steps(i, 3, lambda s, by_x: joined(2, s, d_x, to_y) if by_x else joined(1, s, d_y, to_x))
        steps_of(i, 6, own)
        steps_of(i, 8, middle)
        steps_of(i, 10, last)
        steps_of(i, 12, taken)

    loop(3, round_of)
    for copy in rows_in:
        copy.wait()
    slots_here, _ = route_slots(order[...], me % SD, cap)
    slot_of[...] = slots_here

    v_sum = vec[me]
    for d in range(1, n_tok):
        v_tok(d).wait()
        v_sum = v_sum + vt[d]
    va[...] = v_sum
    v_rep(0, va).start()

    def four_rounds(i):
        loop(4, lambda j: round_of(3 + 4 * i + j))
        pick_rows(i)

    four_rounds(0)
    v_rep(0, va).wait()
    vc[...] = va[...] + vb[0]
    v_rep(1, vc).start()
    loop(3, lambda i: four_rounds(1 + i))
    loop(count + 12 - 19, lambda i: round_of(19 + i))
    v_rep(1, vc).wait()
    vec_out[...] = vc[...] + vb[1]

    for group in groups:
        for q in range(4):
            to_twin(q, group).wait_send()

    def sent(s):
        d_y(s).wait_send()
        to_x(s).wait_send()
        to_y(s).wait_send()
        keep(s).wait()

    loop(count, sent)

    @pl.when(outer)
    def _():
        loop(count, lambda s: z_in(s).wait_send())

    @pl.when(inner)
    def _():
        def back(s):
            z_swap(s).wait_send()
            z_out(s).wait_send()

        loop(count, back)


def reduce_all(cap, grads, shares, order, outs, ings, count):
    dma = pltpu.SemaphoreType.DMA
    count = count * BLK // PART
    part = pltpu.VMEM((count, PART, D), BF)
    whole = pltpu.VMEM((4, count, PART, D), BF)
    line = pltpu.VMEM((16, 128), F32)
    rows = jax.ShapeDtypeStruct((ROWS, D), BF)
    total, vec, output, input_grad, entropy = pl.pallas_call(
        functools.partial(reduce_kernel, cap, count, count // 2),
        out_shape=(
            jax.ShapeDtypeStruct((count, PART, D), BF),
            jax.ShapeDtypeStruct((16, 128), F32),
            rows,
            rows,
            jax.ShapeDtypeStruct((1, ROWS), BF),
        ),
        in_specs=[ANY, VMEM, VMEM] + [ANY] * (2 * SD),
        out_specs=(ANY,) + (VMEM,) * 4,
        scratch_shapes=[
            pltpu.VMEM((SD, cap + META, D), BF),
            pltpu.VMEM((SD, cap, D), BF),
            pltpu.VMEM((1, ROWS), I32),
            whole,
            whole,
        ]
        + [part] * 8
        + [pltpu.VMEM((8, 16, 128), F32), line, pltpu.VMEM((2, 16, 128), F32), line]
        + [dma((4,)), dma((count,))]
        + [dma((4, 4))] * 2
        + [dma((count,))] * 12
        + [dma((8,))] * 2
        + [dma((2,))] * 2
        + [dma((2, SD))],
        compiler_params=pltpu.CompilerParams(collective_id=1, has_side_effects=True, vmem_limit_bytes=VMEM_LIMIT),
        cost_estimate=pl.CostEstimate(flops=4 * ROWS * ROWS * D, bytes_accessed=64 << 20, transcendentals=0),
        name="reduce",
    )(grads.reshape(-1, PART, D), shares, order, *outs, *ings)
    return total.reshape(-1, BLK, D), vec[0:9].reshape(-1), output, input_grad, entropy


V_BQ, V_BV, V_BO, V_BD, V_G1, V_C1, V_G2, V_C2 = range(8)


def inverse(x):
    r = pl.reciprocal(x, approx=True)
    return r * (2.0 - x * r)


def erf_parts(v):
    t = inverse(1.0 + (0.3275911 / math.sqrt(2.0)) * jnp.abs(v))
    e = jnp.exp2((v * v) * (-0.5 / math.log(2.0)))
    poly = 0.5 * 1.061405429
    for c in (-1.453152027, 1.421413741, -0.284496736, 0.254829592):
        poly = poly * t + 0.5 * c
    tail = poly * (t * e)
    return jnp.where(v >= 0.0, 1.0 - tail, tail), e


def lane_sum(x):
    return jnp.sum(x, axis=1, keepdims=True)


def gelu_parts(v):
    phi, e = erf_parts(v)
    return v * phi, phi + v * (e * (1.0 / math.sqrt(2.0 * math.pi)))


def weight_copies(pos, slots, w, sem, first):
    def copy(b):
        return pltpu.make_async_copy(slots.at[pos[first + b]], w.at[pl.ds(b * BLK, BLK)], sem)

    n = w.shape[0] // BLK
    return (lambda: loop(n, lambda b: copy(b).start())), (lambda: loop(n, lambda b: copy(b).wait()))


def halves_of_heads():
    lane = lax.broadcasted_iota(I32, (1, PW), 1)
    m0 = jnp.where(lane < HD, 1.0, 0.0).astype(BF)
    m1 = jnp.where(lane < HD, 0.0, 1.0).astype(BF)
    return lambda pair: jnp.concatenate([pair * m0, pair * m1], axis=0)


def tile_rows(t):
    return pl.ds(pl.multiple_of(t * TM, TM), TM)


def forward_kernel(
    cap,
    pos,
    slots,
    vecs,
    b_u,
    x_h,
    meta,
    back_0,
    back_1,
    back_2,
    back_3,
    heads_h,
    act_h,
    hid_h,
    q_h,
    k_h,
    v_h,
    p_h,
    slope_h,
    n1_h,
    n2_h,
    rs1_h,
    rs2_h,
    wqkv,
    wo,
    wu,
    wd,
    x_c,
    heads,
    act,
    hid,
    q,
    k,
    v,
    p_all,
    slope,
    n1,
    n2,
    rs1,
    rs2,
    out_c,
    ent,
    hid_t,
    w_sem,
    x_sem,
    o_sem,
):
    inv = 1.0 / math.sqrt(HD)
    get_x = pltpu.make_async_copy(x_h, x_c, x_sem)
    get_x.start()
    weights = [
        weight_copies(pos, slots, w, w_sem.at[i], first)
        for i, (w, first) in enumerate(((wqkv, 0), (wo, 24), (wu, 32), (wd, 64)))
    ]
    for start, _ in weights:
        start()
    get_x.wait()
    apart = halves_of_heads()

    def vec(i):
        return vecs[i : i + 1, :]

    saved = (
        (heads, heads_h),
        (act, act_h),
        (hid, hid_h),
        (q, q_h),
        (k, k_h),
        (v, v_h),
        (slope, slope_h),
        (n1, n1_h),
        (n2, n2_h),
        (rs1, rs1_h),
        (rs2, rs2_h),
    )

    def save(t, i):
        src, dst = saved[i]
        return pltpu.make_async_copy(src.at[tile_rows(t)], dst.at[tile_rows(t)], o_sem.at[i])

    def save_p(t):
        n = TM // CL
        cs = pl.ds(t * n, n)
        return pltpu.make_async_copy(p_all.at[cs], p_h.at[cs], o_sem.at[len(saved)])

    def normal(r, n, rs, rows):
        c = r - lane_sum(r) * (1.0 / D)
        scale = lax.rsqrt(lane_sum(c * c) * (1.0 / D) + norm_epsilon)
        rs[rows, :] = jnp.broadcast_to(scale, (TM, 128))
        n[rows, :] = c * scale

    def tile(t):
        rows = tile_rows(t)
        first = t == 0
        pl.when(first)(weights[0][1])
        x = x_c[rows, :]
        for n in range(D // NC):
            ns = slice(n * NC, (n + 1) * NC)
            b_q, b_v = vecs[V_BQ : V_BQ + 1, ns], vecs[V_BV : V_BV + 1, ns]
            q[rows, ns] = ((mm(x, wqkv[0:D, ns]) + b_q).astype(BF).astype(F32) * inv).astype(BF)
            k[rows, ns] = mm(x, wqkv[D : 2 * D, ns]).astype(BF)
            v[rows, ns] = (mm(x, wqkv[2 * D :, ns]) + b_v).astype(BF)

        def attend(c):
            groups = [pl.ds(pl.multiple_of(t * TM + (FWD_AT * c + i) * CL, CL), CL) for i in range(FWD_AT)]
            pairs = [(i, p, slice(p * PW, (p + 1) * PW)) for i in range(FWD_AT) for p in range(PAIRS)]
            scores = [mm(apart(k[groups[i], ps]), q[groups[i], ps], NT) for i, _, ps in pairs]
            total = [jnp.zeros((1, CL), F32)] * FWD_AT
            probs = []
            for (i, _, _), both in zip(pairs, scores):
                halves = []
                for h in range(2):
                    sh = both[h * CL : (h + 1) * CL]
                    sh = sh - jnp.max(sh, axis=0, keepdims=True)
                    e = jnp.exp(sh)
                    tot = jnp.sum(e, axis=0, keepdims=True)
                    r = 1.0 / tot
                    total[i] += jnp.log(tot) - jnp.sum(e * sh, axis=0, keepdims=True) * r
                    halves.append((e * r).astype(BF))
                probs.append(jnp.concatenate(halves, axis=0))
            mixed = [mm(w, apart(v[groups[i], ps]), TN).astype(BF) for (i, _, ps), w in zip(pairs, probs)]
            for (i, p, ps), w, o in zip(pairs, probs, mixed):
                p_all[t * (TM // CL) + FWD_AT * c + i, p] = w
                heads[groups[i], ps] = o
            for i in range(FWD_AT):
                ent[:, groups[i]] = jnp.broadcast_to(total[i] * (1.0 / HEADS), (8, CL))

        loop(TM // CL // FWD_AT, attend)
        for i in (0, 3, 4, 5):
            save(t, i).start()
        save_p(t).start()
        pl.when(first)(weights[1][1])
        normal(x_c[rows, :].astype(F32) + mm(heads[rows, :], wo[...]) + vec(V_BO), n1, rs1, rows)
        hidden = n1[rows, :] * vec(V_G1) + vec(V_C1)
        hid[rows, :] = hidden.astype(BF)
        hid_t[...] = hidden
        pl.when(first)(weights[2][1])

        def widen(f):
            parts = [pl.ds(pl.multiple_of(f * FC + i * NC, NC), NC) for i in range(FC // NC)]
            h_low = hid[rows, :]

            def gelu(fs, up):
                g, g_slope = gelu_parts(up + b_u[:, fs])
                act[rows, fs] = g.astype(BF)
                slope[rows, fs] = g_slope.astype(BF)

            before = None
            for fs in parts:
                up = mm(h_low, wu[fs, :], NT)
                if before is not None:
                    gelu(*before)
                before = (fs, up)
            gelu(*before)

        loop(FF // FC, widen)
        for i in (1, 2, 6, 7, 9):
            save(t, i).start()
        pl.when(first)(weights[3][1])
        normal(hid_t[...] + mm(act[rows, :], wd[...]) + vec(V_BD), n2, rs2, rows)
        out_c[rows, :] = (n2[rows, :] * vec(V_G2) + vec(V_C2)).astype(BF)
        for i in (8, 10):
            save(t, i).start()

    loop(ROWS // TM, tile)

    for j, back in enumerate((back_0, back_1, back_2, back_3)):
        own = seat_part(meta, j, cap)
        back[0:cap, :] = mm(own, out_c[...], TN).astype(BF)
        line = mm(ent[...].astype(BF), own)
        back[cap:, :] = jnp.concatenate([line, line], axis=1)[0:1].astype(BF) * jnp.ones((META, 1), BF)

    def saved_all(t):
        for i in range(len(saved)):
            save(t, i).wait()
        save_p(t).wait()

    loop(ROWS // TM, saved_all)


def shape_of(kind, *shape):
    return jax.ShapeDtypeStruct(shape, kind)


def saved_shapes():
    rows, wide = ((ROWS, D), BF), ((ROWS, FF), BF)
    probs = ((ROWS // CL, PAIRS, 2 * CL, CL), BF)
    full, thin = ((ROWS, D), F32), ((ROWS, 128), F32)
    return rows, wide, probs, full, thin


def forward(cap, positions, slots, vecs, b_u, x_c, meta):
    rows, wide, probs, full, thin = saved_shapes()
    kept = (rows, wide, rows, rows, rows, rows, probs, wide, full, full, thin, thin)
    dma = pltpu.SemaphoreType.DMA
    return pl.pallas_call(
        functools.partial(forward_kernel, cap),
        out_shape=(shape_of(BF, cap + META, D),) * SD + tuple(shape_of(kind, *shape) for shape, kind in kept),
        in_specs=[SMEM, ANY, VMEM, VMEM, ANY, VMEM],
        out_specs=(VMEM,) * SD + (ANY,) * len(kept),
        scratch_shapes=[
            pltpu.VMEM((3 * D, D), BF),
            pltpu.VMEM((D, D), BF),
            pltpu.VMEM((FF, D), BF),
            pltpu.VMEM((FF, D), BF),
            pltpu.VMEM(*rows),
        ]
        + [pltpu.VMEM(*a) for a in kept]
        + [
            pltpu.VMEM(*rows),
            pltpu.VMEM((8, ROWS), F32),
            pltpu.VMEM((TM, D), F32),
            dma((4,)),
            dma,
            dma((12,)),
        ],
        compiler_params=pltpu.CompilerParams(vmem_limit_bytes=VMEM_LIMIT),
        cost_estimate=pl.CostEstimate(flops=2 * ROWS * WROWS * D, bytes_accessed=64 << 20, transcendentals=0),
        name="forward",
    )(positions, slots, vecs, b_u, x_c, meta)


def backward_kernel(
    cap,
    pos,
    slots,
    vecs,
    meta,
    cot_0,
    cot_1,
    cot_2,
    cot_3,
    q_h,
    k_h,
    v_h,
    p_h,
    slope_h,
    n1_h,
    n2_h,
    rs1_h,
    rs2_h,
    back_0,
    back_1,
    back_2,
    back_3,
    shares,
    d_up_h,
    d_q_h,
    d_k_h,
    d_v_h,
    d_proj_h,
    d_br_h,
    wqkv,
    wo,
    wu,
    wd,
    blocks,
    q,
    k,
    v,
    p_all,
    d_up,
    n1,
    n2,
    rs1,
    rs2,
    d_proj,
    d_br,
    ing_c,
    d_h_t,
    gvec,
    g_bu,
    w_sem,
    c_sem,
    i_sem,
    o_sem,
):
    inv = 1.0 / math.sqrt(HD)
    get_c = [
        pltpu.make_async_copy(cot, blocks.at[j], c_sem.at[j]) for j, cot in enumerate((cot_0, cot_1, cot_2, cot_3))
    ]
    for copy in get_c:
        copy.start()
    fetch = [
        pltpu.make_async_copy(src, dst, i_sem.at[i])
        for i, (src, dst) in enumerate(
            (
                (n2_h, n2),
                (rs2_h, rs2),
                (slope_h, d_up),
                (n1_h, n1),
                (rs1_h, rs1),
                (v_h, v),
                (p_h, p_all),
                (k_h, k),
                (q_h, q),
            )
        )
    ]
    weights = [
        weight_copies(pos, slots, w, w_sem.at[i], first)
        for i, (w, first) in enumerate(((wd, 64), (wu, 32), (wo, 24), (wqkv, 0)))
    ]
    fetch[0].start()
    fetch[1].start()
    weights[0][0]()
    fetch[2].start()
    weights[1][0]()
    fetch[3].start()
    fetch[4].start()
    weights[2][0]()
    for i in range(5, 9):
        fetch[i].start()
    weights[3][0]()
    gvec[...] = jnp.zeros_like(gvec)
    g_bu[...] = jnp.zeros_like(g_bu)
    shares[...] = jnp.zeros_like(shares)
    for copy in get_c:
        copy.wait()
    seat_rows(meta, blocks, cap, d_br)
    apart = halves_of_heads()

    def vec(i):
        return vecs[i : i + 1, :]

    def add_vec(i, value):
        gvec[i : i + 1, :] += jnp.sum(value, axis=0, keepdims=True)

    saved = ((d_up, d_up_h), (q, d_q_h), (k, d_k_h), (v, d_v_h), (d_proj, d_proj_h), (d_br, d_br_h))

    def save(t, i):
        src, dst = saved[i]
        return pltpu.make_async_copy(src.at[tile_rows(t)], dst.at[tile_rows(t)], o_sem.at[i])

    def norm_back(e, n, rs, gain, shift):
        add_vec(gain, e * n)
        add_vec(shift, e)
        eg = e * vec(gain)
        return rs * (eg - lane_sum(eg) * (1.0 / D) - n * (lane_sum(eg * n) * (1.0 / D)))

    def norm_two_back(t):
        rows = tile_rows(t)
        d_r2 = norm_back(d_br[rows, :].astype(F32), n2[rows, :], rs2[rows, 0:1], V_G2, V_C2)
        d_br[rows, :] = d_r2.astype(BF)
        add_vec(V_BD, d_br[rows, :].astype(F32))
        n2[rows, :] = d_r2

    def widen_back(t, columns):
        rows = tile_rows(t)
        parts = [pl.ds(pl.multiple_of(f * FC + i * NC, NC), NC) for f in columns for i in range(FC // NC)]
        ups = [mm(d_br[rows, :], wd[fs, :], NT) for fs in parts]

        def finish():
            for fs, up in zip(parts, ups):
                du = (up * d_up[rows, fs].astype(F32)).astype(BF)
                d_up[rows, fs] = du
                g_bu[:, fs] += jnp.sum(du.astype(F32), axis=0, keepdims=True)

        return finish

    def hidden_back(t):
        rows = tile_rows(t)
        return n2[rows, :] + mm(d_up[rows, :], wu[...])

    def norm_one_back(t, d_h):
        rows = tile_rows(t)
        d_r1 = norm_back(d_h, n1[rows, :], rs1[rows, 0:1], V_G1, V_C1)
        d_proj[rows, :] = d_r1.astype(BF)
        n2[rows, :] = d_r1
        add_vec(V_BO, d_proj[rows, :].astype(F32))

    def heads_back(t):
        rows = tile_rows(t)
        d_h_t[rows, :] = mm(d_proj[rows, :], wo[...], NT).astype(BF)

    def attend_back(clusters, meanwhile=lambda: None):
        pairs = [
            (c, p, pl.ds(pl.multiple_of(c * CL, CL), CL), slice(p * PW, (p + 1) * PW))
            for c in clusters
            for p in range(PAIRS)
        ]
        probs = [p_all[c, p] for c, p, _, _ in pairs]
        d_heads = [d_h_t[gr, ps] for _, _, gr, ps in pairs]
        d_probs = [mm(apart(v[gr, ps]), dh, NT) for (_, _, gr, ps), dh in zip(pairs, d_heads)]
        d_values = [
            mm(jnp.concatenate([w[0:CL], w[CL:]], axis=1), apart(dh)).astype(BF) for w, dh in zip(probs, d_heads)
        ]
        finish = meanwhile()
        d_scores = []
        for w, dw in zip(probs, d_probs):
            halves = []
            for h in range(2):
                wh = w[h * CL : (h + 1) * CL].astype(F32)
                dwh = dw[h * CL : (h + 1) * CL]
                halves.append((wh * (dwh - jnp.sum(dwh * wh, axis=0, keepdims=True))).astype(BF))
            d_scores.append(halves)
        d_keys = [
            mm(jnp.concatenate(ds, axis=1), apart(q[gr, ps])).astype(BF) for (_, _, gr, ps), ds in zip(pairs, d_scores)
        ]
        d_queries = [
            (mm(jnp.concatenate(ds, axis=0), apart(k[gr, ps]), TN) * inv).astype(BF)
            for (_, _, gr, ps), ds in zip(pairs, d_scores)
        ]
        if finish is not None:
            finish()
        for (_, _, gr, ps), dq, dk, dv in zip(pairs, d_queries, d_keys, d_values):
            q[gr, ps] = dq
            k[gr, ps] = dk
            v[gr, ps] = dv

    def rows_back(t):
        rows = tile_rows(t)
        return (
            mm(q[rows, :], wqkv[0:D, :], NT)
            + mm(k[rows, :], wqkv[D : 2 * D, :], NT)
            + mm(v[rows, :], wqkv[2 * D :, :], NT)
        )

    def rows_done(t, d_x):
        rows = tile_rows(t)
        add_vec(V_BQ, q[rows, :].astype(F32))
        add_vec(V_BV, v[rows, :].astype(F32))
        ing_c[rows, :] = (n2[rows, :] + d_x.astype(BF).astype(F32)).astype(BF)

    def save_all(t, which):
        for i in which:
            save(t, i).start()

    per = TM // CL
    fetch[0].wait()
    fetch[1].wait()
    norm_two_back(0)
    norm_two_back(1)
    weights[0][1]()
    fetch[2].wait()
    loop(FF // FC // 2, lambda f: widen_back(0, [2 * f, 2 * f + 1])())
    save_all(0, (0, 5))
    weights[1][1]()
    fetch[3].wait()
    fetch[4].wait()
    norm_one_back(0, hidden_back(0))
    weights[2][1]()
    for i in range(5, 9):
        fetch[i].wait()
    heads_back(0)
    save_all(0, (4,))
    loop(per, lambda c: attend_back([c], lambda: widen_back(1, [c])))
    save_all(0, (1, 2, 3))
    save_all(1, (0, 5))
    weights[3][1]()
    d_h = hidden_back(1)
    d_x = rows_back(0)
    norm_one_back(1, d_h)
    heads_back(1)
    rows_done(0, d_x)
    save_all(1, (4,))
    loop(per // BWD_AT, lambda c: attend_back([per + BWD_AT * c + i for i in range(BWD_AT)]))
    save_all(1, (1, 2, 3))
    rows_done(1, rows_back(1))

    for j, back in enumerate((back_0, back_1, back_2, back_3)):
        back[...] = mm(seat_part(meta, j, cap), ing_c[...], TN).astype(BF)

    for chunk in range(72):
        row, lane = chunk // 6, chunk % 6 * 128
        if row < 8:
            part = gvec[row : row + 1, lane : lane + 128]
        else:
            lane += (row - 8) * D
            part = g_bu[:, lane : lane + 128]
        shares[chunk // 9, chunk % 9 : chunk % 9 + 1, :] = part

    def saved_all(t):
        for i in range(len(saved)):
            save(t, i).wait()

    loop(ROWS // TM, saved_all)


def backward(cap, positions, slots, vecs, meta, cots, saved):
    rows, wide, probs, full, thin = saved_shapes()
    dma = pltpu.SemaphoreType.DMA
    grads = (wide, rows, rows, rows, rows, rows)
    return pl.pallas_call(
        functools.partial(backward_kernel, cap),
        out_shape=(shape_of(BF, cap, D),) * SD
        + (shape_of(F32, 8, 16, 128),)
        + tuple(shape_of(kind, *shape) for shape, kind in grads),
        in_specs=[SMEM, ANY, VMEM, VMEM] + [ANY] * (SD + 9),
        out_specs=(VMEM,) * (SD + 1) + (ANY,) * len(grads),
        scratch_shapes=[
            pltpu.VMEM((3 * D, D), BF),
            pltpu.VMEM((D, D), BF),
            pltpu.VMEM((FF, D), BF),
            pltpu.VMEM((FF, D), BF),
            pltpu.VMEM((SD, cap, D), BF),
        ]
        + [pltpu.VMEM(*a) for a in (rows, rows, rows, probs, wide, full, full, thin, thin, rows, rows, rows)]
        + [
            pltpu.VMEM(*rows),
            pltpu.VMEM((8, D), F32),
            pltpu.VMEM((1, FF), F32),
            dma((4,)),
            dma((4,)),
            dma((9,)),
            dma((6,)),
        ],
        compiler_params=pltpu.CompilerParams(vmem_limit_bytes=VMEM_LIMIT),
        cost_estimate=pl.CostEstimate(flops=2 * ROWS * WROWS * D, bytes_accessed=64 << 20, transcendentals=0),
        name="backward",
    )(positions, slots, vecs, meta, *cots, *saved)


WC = 8 * BLK


def weight_kernel(
    pos,
    x_h,
    heads_h,
    act_h,
    d_up_h,
    d_q_h,
    d_k_h,
    d_v_h,
    d_proj_h,
    hid_h,
    d_br_h,
    grads,
    x_c,
    heads,
    act,
    d_up,
    d_q,
    d_k,
    d_v,
    d_proj,
    hid,
    d_br,
    stage,
    i_sem,
    g_sem,
):
    refs = (
        (x_h, x_c),
        (d_q_h, d_q),
        (d_k_h, d_k),
        (d_v_h, d_v),
        (heads_h, heads),
        (d_proj_h, d_proj),
        (hid_h, hid),
        (d_up_h, d_up),
        (d_br_h, d_br),
        (act_h, act),
    )
    fetch = [pltpu.make_async_copy(src, dst, i_sem.at[i]) for i, (src, dst) in enumerate(refs)]
    for copy in fetch:
        copy.start()

    per = WC // BLK

    def g_copy(chunk, j, at):
        return pltpu.make_async_copy(
            stage.at[at, pl.ds(j * BLK, BLK)], grads.at[pos[chunk * per + j]], g_sem.at[at]
        )

    def put(chunk, left, right):
        at = lax.rem(chunk, 2)

        @pl.when(chunk >= 2)
        def _():
            for j in range(per):
                g_copy(chunk - 2, j, at).wait()

        stage[at] = mm(left, right, TN).astype(BF)
        for j in range(per):
            g_copy(chunk, j, at).start()

    first = 0
    for left, right, needs in (
        (x_c, d_q, (0, 1)),
        (x_c, d_k, (2,)),
        (x_c, d_v, (3,)),
        (heads, d_proj, (4, 5)),
        (d_up, hid, (6, 7)),
        (act, d_br, (8, 9)),
    ):
        for i in needs:
            fetch[i].wait()

        def body(j, left=left, right=right, first=first):
            put(first + j, left[:, pl.ds(pl.multiple_of(j * WC, WC), WC)], right[...])

        loop(left.shape[1] // WC, body)
        first += left.shape[1] // WC
    for chunk in (first - 2, first - 1):
        for j in range(per):
            g_copy(chunk, j, chunk % 2).wait()


def weight_grads_of(total_slots, positions, x_c, saved):
    r_v, w_v = pltpu.VMEM((ROWS, D), BF), pltpu.VMEM((ROWS, FF), BF)
    return pl.pallas_call(
        weight_kernel,
        out_shape=jax.ShapeDtypeStruct((total_slots, BLK, D), BF),
        in_specs=[SMEM] + [ANY] * 10,
        out_specs=ANY,
        scratch_shapes=[r_v, r_v, w_v, w_v]
        + [r_v] * 6
        + [
            pltpu.VMEM((2, WC, D), BF),
            pltpu.SemaphoreType.DMA((10,)),
            pltpu.SemaphoreType.DMA((2,)),
        ],
        compiler_params=pltpu.CompilerParams(vmem_limit_bytes=VMEM_LIMIT),
        cost_estimate=pl.CostEstimate(flops=2 * ROWS * WROWS * D, bytes_accessed=40 << 20, transcendentals=0),
        name="weight_grads",
    )(positions, x_c, *saved)


def local(
    tokens,
    cotangent,
    cluster_order,
    block_owner,
    master_slots,
    moment_one,
    moment_two,
    vector_master,
    vector_moment_one,
    vector_moment_two,
):
    tok_count = lax.axis_size("tok")
    tok_index = lax.axis_index("tok")
    slot_count = master_slots.shape[0]
    cap = tok_count // SD * (max(1, CPS // tok_count) * 3 * CL // (2 * SD))
    total_slots = tok_count * slot_count
    order = cluster_order.reshape(1, ROWS)

    block = jax.ShapeDtypeStruct((SD, cap, D), BF)
    meta_shape = jax.ShapeDtypeStruct((SD, META, D), BF)
    row_block = jax.ShapeDtypeStruct((ROWS, D), BF)
    four_planes = tok_count == 8 and lax.axis_size("rep") == 4
    if four_planes:
        slots_low, x_c, *cots, recv_meta, vecs, b_u, occupancy, positions = gather_all(
            cap, tokens, cotangent, order, master_slots, vector_master, block_owner
        )
        positions = positions.reshape(NBLK)
        slots_low = slots_low.reshape(total_slots, BLK, D)
    else:
        positions = slot_positions(block_owner, slot_count)
        slots_low = lax.all_gather(master_slots.astype(BF), "tok", axis=0, tiled=True)
        vectors = lax.all_gather(vector_master.astype(BF), "tok", axis=0, tiled=True).astype(F32)
        vecs, b_u = vectors[: 8 * D].reshape(8, D), vectors[8 * D :].reshape(1, FF)
        cluster = tok_index // SD * CPS + cluster_order // CL
        target = cluster % tok_count
        chosen = target[None, :] == jnp.arange(tok_count, dtype=jnp.int32)[:, None]
        sent_counts = jnp.sum(chosen.astype(F32), axis=1)
        own_row = (jnp.arange(tok_count, dtype=jnp.int32) == tok_index).astype(F32)
        occupancy = lax.psum(own_row[:, None] * sent_counts[None, :], ("tok", "rep")).astype(jnp.int32)
        send_x, send_c, meta = pl.pallas_call(
            functools.partial(send_kernel, cap),
            out_shape=(block, block, meta_shape),
            in_specs=[VMEM] * 3,
            out_specs=(VMEM,) * 3,
            compiler_params=pltpu.CompilerParams(vmem_limit_bytes=VMEM_LIMIT),
            name="send_rows",
        )(tokens, cotangent, order)
        recv_x, recv_meta = (jnp.stack(swap_blocks(b)) for b in (send_x, meta))
        x_c = pl.pallas_call(
            functools.partial(seat_kernel, cap),
            out_shape=row_block,
            in_specs=[VMEM] * 2,
            out_specs=VMEM,
            compiler_params=pltpu.CompilerParams(vmem_limit_bytes=VMEM_LIMIT),
            name="seat_rows",
        )(recv_x, recv_meta)
        cots = [send_c[k] for k in range(SD)]

    cots = swap_blocks(cots)
    *out_blocks, heads, act, hid, q, k, v, p, slope, n1, n2, rs1, rs2 = forward(
        cap, positions, slots_low, vecs, b_u, x_c, recv_meta
    )
    out_blocks = swap_blocks(out_blocks)
    *ing_blocks, shares, d_up, d_q, d_k, d_v, d_proj, d_br = backward(
        cap, positions, slots_low, vecs, recv_meta, cots, (q, k, v, p, slope, n1, n2, rs1, rs2)
    )
    ing_blocks = swap_blocks(ing_blocks)
    grads = weight_grads_of(
        total_slots, positions, x_c, (heads, act, d_up, d_q, d_k, d_v, d_proj, hid, d_br)
    )
    if four_planes:
        total, vec_owned, output, input_grad, entropy = reduce_all(
            cap, grads, shares, order, out_blocks, ing_blocks, slot_count
        )
    else:
        total = lax.psum(lax.psum_scatter(grads, "tok", scatter_dimension=0, tiled=True), "rep")
        grad_vector = shares[:, 0:9].reshape(-1)
        vec_owned = lax.psum(lax.psum_scatter(grad_vector, "tok", scatter_dimension=0, tiled=True), "rep")
        output, input_grad, entropy = pl.pallas_call(
            functools.partial(return_kernel, cap),
            out_shape=(row_block, row_block, jax.ShapeDtypeStruct((1, ROWS), BF)),
            in_specs=[VMEM] * (2 * SD + 1),
            out_specs=(VMEM,) * 3,
            compiler_params=pltpu.CompilerParams(vmem_limit_bytes=VMEM_LIMIT),
            name="return_rows",
        )(order, *out_blocks, *ing_blocks)

    used = jnp.any(
        positions[None, :] == (tok_index * slot_count + jnp.arange(slot_count, dtype=I32))[:, None], axis=1
    )
    owned_grad = jnp.where(used[:, None, None], total.astype(F32), 0.0)
    first_new, second_new, master_new = adam_update(
        owned_grad, master_slots, moment_one, moment_two, rate_matrix
    )
    vec_first, vec_second, vec_new = adam_update(
        vec_owned, vector_master, vector_moment_one, vector_moment_two, rate_vector
    )
    return (
        output,
        input_grad,
        owned_grad,
        first_new,
        second_new,
        master_new,
        master_new.astype(BF),
        vec_owned,
        vec_first,
        vec_second,
        vec_new,
        vec_new.astype(BF),
        entropy.reshape(-1),
        occupancy,
    )


def solution(mesh):
    placed = (
        P(("rep", "tok"), None),
        P(("rep", "tok"), None),
        P(("rep", "tok")),
        P(),
        P("tok", None, None),
        P("tok", None, None),
        P("tok", None, None),
        P("tok"),
        P("tok"),
        P("tok"),
    )
    return jax.shard_map(
        local,
        mesh=mesh,
        in_specs=placed,
        out_specs=(
            P(("rep", "tok"), None),
            P(("rep", "tok"), None),
            P("tok", None, None),
            P("tok", None, None),
            P("tok", None, None),
            P("tok", None, None),
            P("tok", None, None),
            P("tok"),
            P("tok"),
            P("tok"),
            P("tok"),
            P("tok"),
            P(("rep", "tok")),
            P(),
        ),
        check_vma=False,
    )
```

```python
import functools
import math

import jax
import jax.numpy as jnp
from jax import lax
from jax.experimental import pallas as pl
from jax.experimental.pallas import tpu as pltpu
from jax.sharding import PartitionSpec as P

D = 768
HEADS = 12
HD = 64
FF = 3072
SD = 4
CL = 128
NBLK = 96
STEP = 10
CPS = 32
WROWS = 9216
BLK = 96
ROWS = 1024
PAIRS = HEADS // 2
PW = 2 * HD
TM = 256
PART = 48
META = 16
VMEM_LIMIT = 63 << 20
FC = 768
FWD_AT = 2
BWD_AT = 2

norm_epsilon = 1e-06
beta_first = 0.9
beta_second = 0.999
adam_epsilon = 1e-08
weight_decay = 0.01
rate_matrix = 0.02
rate_vector = 0.2

BF = jnp.bfloat16
F32 = jnp.float32
I32 = jnp.int32

VMEM = pl.BlockSpec(memory_space=pltpu.VMEM)
SMEM = pl.BlockSpec(memory_space=pltpu.SMEM)
ANY = pl.BlockSpec(memory_space=pl.ANY)

NN = (((1,), (0,)), ((), ()))
NT = (((1,), (1,)), ((), ()))
TN = (((0,), (0,)), ((), ()))


def mm(a, b, dims=NN):
    return lax.dot_general(a, b, dims, preferred_element_type=F32)


def slot_positions(block_owner, slot_count):
    owners = block_owner[:, 0]
    blocks = owners.shape[0]
    shared = owners[:, None] == owners[None, :]
    before = (
        jnp.arange(blocks, dtype=jnp.int32)[None, :] < jnp.arange(blocks, dtype=jnp.int32)[:, None]
    )
    earlier = jnp.sum((shared & before).astype(jnp.int32), axis=1)
    return owners * slot_count + earlier


def adam_update(grad_now, weight_old, first_old, second_old, rate_step):
    first_new = beta_first * first_old + (1.0 - beta_first) * grad_now
    second_new = beta_second * second_old + (1.0 - beta_second) * grad_now * grad_now
    first_hat = first_new / (1.0 - beta_first**STEP)
    second_hat = second_new / (1.0 - beta_second**STEP)
    weight_new = weight_old - rate_step * (
        first_hat / (jnp.sqrt(second_hat) + adam_epsilon) + weight_decay * weight_old
    )
    return (first_new, second_new, weight_new)


def route_slots(order, seat, cap):
    cluster = order // CL
    rel = lax.rem(cluster, SD) ^ seat
    place = (cluster // SD) * CL + lax.rem(order, CL) + 1
    chosen = lax.broadcasted_iota(I32, (8, ROWS), 0) == rel
    chosen_low = jnp.where(chosen, 1.0, 0.0).astype(BF)
    before = lax.broadcasted_iota(I32, (ROWS, ROWS), 0) < lax.broadcasted_iota(I32, (ROWS, ROWS), 1)
    before_low = jnp.where(before, 1.0, 0.0).astype(BF)
    running = mm(chosen_low, before_low)
    rank = jnp.sum(jnp.where(chosen, running, 0.0), axis=0, keepdims=True).astype(I32)
    return rel * cap + rank, place


def slot_matrix(slots, at, cap):
    rows = lax.broadcasted_iota(I32, (cap, ROWS), 0) + at * cap
    return jnp.where(rows == slots, 1.0, 0.0).astype(BF)


def column_of(picked, digits):
    wide = jnp.concatenate([digits] + [digits * 0] * 15, axis=0)
    return mm(picked, wide, NT).astype(BF)


def send_kernel(cap, tokens, cotangent, order, send_x, send_c, meta, column):
    seat = lax.rem(lax.axis_index("tok"), SD)
    slots, place = route_slots(order[...], seat, cap)
    digits = jnp.concatenate([place // CL, lax.rem(place, CL)] + [place * 0] * 6, axis=0).astype(F32).astype(BF)
    for at in range(SD):
        picked = slot_matrix(slots, at, cap)
        send_x[at] = mm(picked, tokens[...]).astype(BF)
        send_c[at] = mm(picked, cotangent[...]).astype(BF)
        coded = mm(digits, picked, NT)
        line = jnp.concatenate([coded[0:1], coded[1:2]], axis=1)
        meta[at] = jnp.broadcast_to(line, (META, D)).astype(BF)
        column[at] = column_of(picked, digits)


def remote(src, dst, send_sem, recv_sem, tok, rep):
    return pltpu.make_async_remote_copy(
        src_ref=src,
        dst_ref=dst,
        send_sem=send_sem,
        recv_sem=recv_sem,
        device_id={"tok": tok, "rep": rep},
        device_id_type=pl.DeviceIdType.MESH,
    )


def loop(n, body):
    def run(i, c):
        body(i)
        return c

    lax.fori_loop(0, n, run, 0)


class Place:
    def __init__(self):
        self.me = me = lax.axis_index("tok")
        self.z = z = lax.axis_index("rep")
        core, x, y = me % 2, (me // 2) % 2, me // 4
        self.twin = me + 1 - 2 * core
        self.xn = me + 2 - 4 * x
        self.yn = me + 4 - 8 * y
        self.dn = self.xn + 4 - 8 * y
        self.side = z % 2
        self.zp = z + 1 - 2 * self.side

    def twin_of(self, tok):
        return tok + 1 - 2 * (tok % 2)

    def greet(self, peers):
        barrier = pltpu.get_barrier_semaphore()
        for tok, rep in peers:
            pl.semaphore_signal(
                barrier, inc=1, device_id={"tok": tok, "rep": rep}, device_id_type=pl.DeviceIdType.MESH
            )
        return lambda: pl.semaphore_wait(barrier, len(peers))


def seat_matrix(meta, first, rows, cap):
    hi = jnp.concatenate([meta[k, 0:8, 0:cap] for k in range(SD)], axis=1).astype(F32)[0:1]
    lo = jnp.concatenate([meta[k, 0:8, cap : 2 * cap] for k in range(SD)], axis=1).astype(F32)[0:1]
    at = (hi * CL + lo).astype(I32)
    seats = lax.broadcasted_iota(I32, (rows, SD * cap), 0) + (first + 1)
    return jnp.where(seats == at, 1.0, 0.0).astype(BF)


def seat_part(column, k, cap):
    digits = column[k].astype(F32)
    at = (digits[:, 0:1] * CL + digits[:, 1:2]).astype(I32)
    seats = lax.broadcasted_iota(I32, (cap, ROWS), 1) + 1
    return jnp.where(seats == at, 1.0, 0.0).astype(BF)


def seat_rows(meta, blocks, cap, to):
    def body(t):
        r0 = pl.multiple_of(t * 256, 256)
        rows = blocks[...].reshape(SD * cap, D)
        to[pl.ds(r0, 256), :] = mm(seat_matrix(meta, r0, 256, cap), rows).astype(BF)

    loop(ROWS // 256, body)


def seat_kernel(cap, blocks, meta, to):
    seat_rows(meta, blocks, cap, to)


def gather_kernel(
    cap,
    count,
    tokens_h,
    cotangent_h,
    order,
    master_h,
    vector,
    owner_of,
    slots,
    x_c,
    cot_0,
    cot_1,
    cot_2,
    cot_3,
    recv_meta,
    recv_column,
    vecs,
    b_u,
    occupancy,
    positions,
    tokens,
    cotangent,
    master,
    own,
    send_x,
    send_c,
    meta,
    recv_x,
    got_meta,
    column,
    got_column,
    slot_of,
    digits,
    mine,
    by_z,
    by_tok,
    x_s,
    x_r,
    y_s,
    y_r,
    d_s,
    d_r,
    zx_s,
    zx_r,
    zd_s,
    zd_r,
    zy_s,
    zy_r,
    p_s,
    p_r,
    row_s,
    row_r,
    z_s,
    z_r,
    t_s,
    t_r,
    local_s,
):
    at = Place()
    me, z, side = at.me, at.z, at.side
    n_tok, n_rep = 8, 4
    peers = [((me + d) % n_tok, z) for d in range(1, n_tok)] + [(me, (z + d) % n_rep) for d in range(1, n_rep)]
    fetch = [
        pltpu.make_async_copy(src, dst, local_s.at[i])
        for i, (src, dst) in enumerate(((master_h, master), (tokens_h, tokens), (cotangent_h, cotangent)))
    ]
    for copy in fetch:
        copy.start()
    wait_peers = at.greet(peers)
    fetch[0].wait()

    last = count - 1

    def near(j):
        return side * last + (1 - 2 * side) * j

    def far(j):
        return (1 - side) * last - (1 - 2 * side) * j

    few_x, few_d, few_y = 11 * count // 26, 12 * count // 26, 8 * count // 26
    most_x, most_d, most_y = count - few_x, count - few_d, count - few_y

    def piece(owner, s):
        return slots.at[owner * count + s]

    def to_x(s):
        return remote(own.at[s], piece(me, s), x_s.at[s], x_r.at[s], at.xn, z)

    def to_y(s):
        return remote(own.at[s], piece(me, s), y_s.at[s], y_r.at[s], at.yn, z)

    def on_y(s):
        return remote(piece(at.xn, s), piece(at.xn, s), d_s.at[s], d_r.at[s], at.yn, z)

    def x_on_z(s):
        return remote(piece(at.xn, s), piece(at.xn, s), zx_s.at[s], zx_r.at[s], me, at.zp)

    def d_on_z(s):
        return remote(piece(at.dn, s), piece(at.dn, s), zd_s.at[s], zd_r.at[s], me, at.zp)

    def y_on_z(s):
        return remote(piece(at.yn, s), piece(at.yn, s), zy_s.at[s], zy_r.at[s], me, at.zp)

    def x_in(s):
        return remote(own.at[s], piece(at.xn, s), x_s.at[s], x_r.at[s], at.xn, z)

    def y_in(s):
        return remote(own.at[s], piece(at.yn, s), y_s.at[s], y_r.at[s], at.yn, z)

    def d_in(s):
        return remote(own.at[s], piece(at.dn, s), d_s.at[s], d_r.at[s], at.yn, z)

    owners = (me, at.xn, at.yn, at.dn)

    def near_run(q, j0, j1):
        return (q, (1 - side) * j0 + side * (count - j1), j1 - j0)

    def far_run(q, j0, j1):
        return (q, side * j0 + (1 - side) * (count - j1), j1 - j0)

    runs = (
        (0, 0, count),
        near_run(2, 0, few_y),
        near_run(1, 0, most_x),
        near_run(3, 0, most_d),
        far_run(1, 0, few_x),
        near_run(2, few_y, most_y),
        far_run(2, 0, few_y),
        far_run(3, 0, few_d // 2),
        far_run(3, few_d // 2, few_d - 2),
        far_run(3, few_d - 2, few_d),
    )

    def to_twin(i):
        q, s, n = runs[i]
        src = own if q == 0 else slots.at[pl.ds(owners[q] * count + s, n)]
        dst = slots.at[pl.ds(owners[q] * count + s, n)]
        return remote(src, dst, p_s.at[i], p_r.at[i], at.twin, z)

    def cast(j):
        own[near(j)] = master[near(j)].astype(BF)

    loop(most_x, cast)
    wait_peers()
    loop(most_x, lambda j: to_x(near(j)).start())
    loop(few_y, lambda j: to_y(near(j)).start())
    loop(count - most_x, lambda j: cast(most_x + j))
    to_twin(0).start()
    keep = pltpu.make_async_copy(own, slots.at[pl.ds(me * count, count)], local_s.at[3])
    keep.start()

    seat = me % SD
    seats = (me, at.twin, at.xn, at.twin_of(at.xn))
    rows_of = ((meta, got_meta), (send_x, recv_x), (column, got_column))

    def row_copy(i, k):
        src, dst = rows_of[i]
        return remote(src.at[k], dst.at[k], row_s.at[i, k], row_r.at[i, k], seats[k], z)

    put_c = [
        pltpu.make_async_copy(send_c.at[k], to, local_s.at[4 + k])
        for k, to in enumerate((cot_0, cot_1, cot_2, cot_3))
    ]

    def route():
        fetch[1].wait()
        fetch[2].wait()
        slots_here, place = route_slots(order[...], seat, cap)
        slot_of[...] = slots_here
        digits[...] = (
            jnp.concatenate([place // CL, lax.rem(place, CL)] + [place * 0] * 6, axis=0).astype(F32).astype(BF)
        )

    def sort_tokens(k):
        picked = slot_matrix(slot_of[...], k, cap)
        send_x[k] = mm(picked, tokens[...]).astype(BF)
        coded = mm(digits[...], picked, NT)
        line = jnp.concatenate([coded[0:1], coded[1:2]], axis=1)
        meta[k] = jnp.broadcast_to(line, (META, D)).astype(BF)
        column[k] = column_of(picked, digits[...])
        for i in range(3):
            if k:
                row_copy(i, k).start()
            else:
                src, dst = rows_of[i]
                dst[0] = src[0]

    def sort_cotangent(k):
        send_c[k] = mm(slot_matrix(slot_of[...], k, cap), cotangent[...]).astype(BF)
        put_c[k].start()

    def z_copy(d):
        return remote(by_z.at[0], by_z.at[d], z_s.at[d], z_r.at[d], me, (z + d) % n_rep)

    def t_copy(d):
        return remote(mine, by_tok.at[d], t_s.at[d], t_r.at[d], (me + d) % n_tok, z)

    def count_rows():
        residue = lax.rem(me // SD * CPS + order[...] // CL, n_tok)
        hit = lax.broadcasted_iota(I32, (128, ROWS), 0) == residue
        by_z[0] = mm(jnp.ones((8, ROWS), BF), jnp.where(hit, 1.0, 0.0).astype(BF), NT)
        for d in range(1, n_rep):
            z_copy(d).start()
        for i in range(9):
            mine[i : i + 1] = vector[i * 128 : (i + 1) * 128].reshape(1, 128).astype(BF).astype(F32)
        block_row = lax.broadcasted_iota(I32, (NBLK, NBLK), 0)
        block_col = lax.broadcasted_iota(I32, (NBLK, NBLK), 1)
        by_col = owner_of[...].astype(F32)
        by_row = lane_sum(jnp.where(block_row == block_col, by_col, 0.0))
        earlier = jnp.where((by_row == by_col) & (block_row < block_col), 1.0, 0.0)
        positions[...] = (by_col * (count * PART // BLK) + jnp.sum(earlier, axis=0, keepdims=True)).astype(I32)

    def share_vectors():
        for d in range(1, n_rep):
            z_copy(d).wait()
        mine[16:24] = by_z[0] + by_z[1] + by_z[2] + by_z[3]
        for d in range(1, n_tok):
            t_copy(d).start()

    def lay_out_vectors():
        by_tok[0] = mine[...]
        for d in range(1, n_tok):
            t_copy(d).wait()
        for owner in range(n_tok):
            share = by_tok[(me + n_tok - owner) % n_tok]
            occupancy[owner : owner + 1, :] = share[16:17, 0:n_tok].astype(I32)
            for i in range(9):
                chunk = owner * 9 + i
                row, lane = chunk // 6, chunk % 6 * 128
                if row < 8:
                    vecs[row : row + 1, lane : lane + 128] = share[i : i + 1]
                else:
                    lane += (row - 8) * D
                    b_u[:, lane : lane + 128] = share[i : i + 1]

    between = {
        1: lambda: (route(), sort_tokens(2)),
        3: lambda: sort_tokens(3),
        5: lambda: sort_tokens(1),
        7: lambda: (sort_tokens(0), count_rows()),
        9: lambda: sort_cotangent(1),
        11: lambda: sort_cotangent(2),
        13: lambda: sort_cotangent(3),
    }
    for j in range(most_x):
        x_in(near(j)).wait_recv()
        if j < most_d:
            on_y(near(j)).start()
        if j < few_x:
            x_on_z(near(j)).start()
        if j < few_y:
            y_in(near(j)).wait_recv()
            y_on_z(near(j)).start()
        if j == few_y:
            to_twin(1).start()
        if j in between:
            between[j]()
    to_twin(2).start()
    loop(most_y - few_y, lambda j: to_y(near(few_y + j)).start())
    share_vectors()
    sort_cotangent(0)

    def diagonal(j):
        d_in(near(j)).wait_recv()
        d_on_z(near(j)).start()

    loop(few_d, diagonal)
    loop(most_d - few_d, lambda j: d_in(near(few_d + j)).wait_recv())
    to_twin(3).start()
    loop(few_x, lambda j: x_on_z(far(j)).wait_recv())
    to_twin(4).start()
    lay_out_vectors()
    loop(most_y - few_y, lambda j: y_in(near(few_y + j)).wait_recv())
    to_twin(5).start()
    loop(few_y, lambda j: y_on_z(far(j)).wait_recv())
    to_twin(6).start()
    for i in range(3):
        for k in (2, 3, 1):
            row_copy(i, k).wait_recv()
    recv_meta[...] = got_meta[...]
    recv_column[...] = got_column[...]
    seat_rows(got_meta, recv_x, cap, x_c)
    done = 0
    for i, upto in ((7, few_d // 2), (8, few_d - 2), (9, few_d)):
        loop(upto - done, lambda j, done=done: d_on_z(far(done + j)).wait_recv())
        to_twin(i).start()
        done = upto

    for i in range(3):
        for k in (2, 3, 1):
            row_copy(i, k).wait_send()
    for copy in put_c:
        copy.wait()
    keep.wait()

    loop(most_x, lambda j: to_x(near(j)).wait_send())
    loop(most_y, lambda j: to_y(near(j)).wait_send())
    loop(most_d, lambda j: on_y(near(j)).wait_send())
    loop(few_x, lambda j: x_on_z(near(j)).wait_send())
    loop(few_d, lambda j: d_on_z(near(j)).wait_send())
    loop(few_y, lambda j: y_on_z(near(j)).wait_send())
    for i in range(len(runs)):
        to_twin(i).wait()


def gather_all(cap, tokens, cotangent, order, master, vector, block_owner):
    count = master.shape[0] * BLK // PART
    rows = jax.ShapeDtypeStruct((ROWS, D), BF)
    part = jax.ShapeDtypeStruct((cap, D), BF)
    dma = pltpu.SemaphoreType.DMA
    block = pltpu.VMEM((SD, cap, D), BF)
    meta = pltpu.VMEM((SD, META, D), BF)
    return pl.pallas_call(
        functools.partial(gather_kernel, cap, count),
        out_shape=(
            jax.ShapeDtypeStruct((8 * count, PART, D), BF),
            rows,
            part,
            part,
            part,
            part,
            jax.ShapeDtypeStruct((SD, META, D), BF),
            jax.ShapeDtypeStruct((SD, cap, 128), BF),
            jax.ShapeDtypeStruct((8, D), F32),
            jax.ShapeDtypeStruct((1, FF), F32),
            jax.ShapeDtypeStruct((8, 8), I32),
            jax.ShapeDtypeStruct((1, NBLK), I32),
        ),
        in_specs=[ANY, ANY, VMEM, ANY, VMEM, VMEM],
        out_specs=(ANY, VMEM) + (ANY,) * SD + (VMEM,) * 6,
        scratch_shapes=[
            pltpu.VMEM((ROWS, D), BF),
            pltpu.VMEM((ROWS, D), BF),
            pltpu.VMEM((count, PART, D), F32),
            pltpu.VMEM((count, PART, D), BF),
            block,
            block,
            meta,
            block,
            meta,
            pltpu.VMEM((SD, cap, 128), BF),
            pltpu.VMEM((SD, cap, 128), BF),
            pltpu.VMEM((1, ROWS), I32),
            pltpu.VMEM((8, ROWS), BF),
            pltpu.VMEM((24, 128), F32),
            pltpu.VMEM((4, 8, 128), F32),
            pltpu.VMEM((8, 24, 128), F32),
        ]
        + [dma((count,))] * 12
        + [dma((10,))] * 2
        + [dma((3, SD))] * 2
        + [dma((4,))] * 2
        + [dma((8,))] * 2
        + [dma((8,))],
        compiler_params=pltpu.CompilerParams(collective_id=0, has_side_effects=True, vmem_limit_bytes=VMEM_LIMIT),
        cost_estimate=pl.CostEstimate(flops=8 * ROWS * ROWS * D, bytes_accessed=64 << 20, transcendentals=0),
        name="gather",
    )(tokens, cotangent, order, master.reshape(count, PART, D), vector, block_owner.reshape(1, NBLK))


def return_kernel(cap, order, *refs):
    outs, ings, (out, ing, entropy) = refs[:SD], refs[SD : 2 * SD], refs[2 * SD :]
    seat = lax.rem(lax.axis_index("tok"), SD)
    slots, _ = route_slots(order[...], seat, cap)
    picked = jnp.concatenate([slot_matrix(slots, at, cap) for at in range(SD)], axis=0)
    for to, blocks in ((out, outs), (ing, ings)):
        rows = jnp.concatenate([block[0:cap, :] for block in blocks], axis=0)
        to[...] = mm(picked, rows, TN).astype(BF)
    line = jnp.concatenate([block[cap : cap + 8, 0:cap] for block in outs], axis=1)
    entropy[...] = mm(line, picked)[0:1].astype(BF)


def swap_blocks(blocks):
    n = lax.axis_size("tok")
    parts = [blocks[0]]
    for k in range(1, SD):
        parts.append(lax.ppermute(blocks[k], "tok", [(i, i ^ k) for i in range(n)]))
    return parts


def reduce_kernel(
    cap,
    count,
    split,
    grads,
    vec,
    order,
    out_0,
    out_1,
    out_2,
    out_3,
    ing_0,
    ing_1,
    ing_2,
    ing_3,
    total,
    vec_out,
    output,
    input_grad,
    entropy,
    out_v,
    ing_v,
    slot_of,
    a,
    tw,
    rd,
    rx,
    ry,
    o,
    rz1,
    pz,
    rz2,
    fz,
    vt,
    va,
    vb,
    vc,
    a_l,
    keep_l,
    p_s,
    p_r,
    d_s,
    d_r,
    x_s,
    x_r,
    y_s,
    y_r,
    z1_s,
    z1_r,
    z2_s,
    z2_r,
    z3_s,
    z3_r,
    t_s,
    t_r,
    v_s,
    v_r,
    row_l,
):
    at = Place()
    me, z = at.me, at.z
    n_tok, n_rep = 8, 4
    peers = [((me + d) % n_tok, z) for d in range(1, n_tok)] + [(me, (z + d) % n_rep) for d in range(1, n_rep)]
    wait_peers = at.greet(peers)
    owners = (me, at.xn, at.yn, at.dn)

    def load(q):
        return pltpu.make_async_copy(grads.at[pl.ds(owners[q] * count, count)], a.at[q], a_l.at[q])

    for q in (3, 1, 2, 0):
        load(q).start()
    rows_in = [
        pltpu.make_async_copy(src, to.at[k], row_l.at[i, k])
        for i, (blocks, to) in enumerate((((out_0, out_1, out_2, out_3), out_v), ((ing_0, ing_1, ing_2, ing_3), ing_v)))
        for k, src in enumerate(blocks)
    ]
    for copy in rows_in:
        copy.start()
    wait_peers()

    groups = [(g, g * (count // 4), count // 4 if g < 3 else count - 3 * (count // 4)) for g in range(4)]

    def to_twin(q, group):
        g, s, n = group
        src = grads.at[pl.ds(at.twin_of(owners[q]) * count + s, n)]
        return remote(src, tw.at[q, pl.ds(s, n)], p_s.at[q, g], p_r.at[q, g], at.twin, z)

    def d_y(s):
        return remote(a.at[3, s], rd.at[s], d_s.at[s], d_r.at[s], at.yn, z)

    def d_x(s):
        return remote(a.at[3, s], rd.at[s], d_s.at[s], d_r.at[s], at.xn, z)

    def to_x(s):
        return remote(a.at[1, s], rx.at[s], x_s.at[s], x_r.at[s], at.xn, z)

    def to_y(s):
        return remote(a.at[2, s], ry.at[s], y_s.at[s], y_r.at[s], at.yn, z)

    def z_in(s):
        return remote(o.at[s], rz1.at[s], z1_s.at[s], z1_r.at[s], me, at.zp)

    def z_swap(s):
        return remote(pz.at[s], rz2.at[s], z2_s.at[s], z2_r.at[s], me, n_rep - 1 - z)

    def z_out(s):
        return remote(fz.at[s], fz.at[s], z3_s.at[s], z3_r.at[s], me, at.zp)

    def keep(s):
        return pltpu.make_async_copy(fz.at[s], total.at[s], keep_l.at[s])

    for group in groups:
        for q in (3, 1, 2, 0):
            to_twin(q, group).start()

    def v_tok(d):
        return remote(vec.at[(me + d) % n_tok], vt.at[d], t_s.at[d], t_r.at[d], (me + d) % n_tok, z)

    def v_rep(i, src):
        return remote(src, vb.at[i], v_s.at[i], v_r.at[i], me, at.zp if i == 0 else (z + 2) % n_rep)

    for d in range(1, n_tok):
        v_tok(d).start()

    def join(q, s):
        return a[q, s] + tw[q, s]

    def first(s, send):
        a[3, s] = join(3, s)
        send(s).start()

    def plain(q, s, send):
        a[q, s] = join(q, s)
        send(s).start()

    def joined(q, s, arrived, send):
        arrived(s).wait_recv()
        a[q, s] = join(q, s) + rd[s]
        send(s).start()

    inner = (z == 1) | (z == 2)
    outer = (z == 0) | (z == 3)

    def own(s):
        to_x(s).wait_recv()
        to_y(s).wait_recv()
        o[s] = join(0, s) + (rx[s] + ry[s])
        pl.when(outer)(lambda: z_in(s).start())

    def middle(s):
        @pl.when(inner)
        def _():
            z_in(s).wait_recv()
            pz[s] = o[s] + rz1[s]
            z_swap(s).start()

    def last(s):
        @pl.when(inner)
        def _():
            z_swap(s).wait_recv()
            fz[s] = pz[s] + rz2[s]
            z_out(s).start()
            keep(s).start()

    def taken(s):
        @pl.when(outer)
        def _():
            z_out(s).wait_recv()
            keep(s).start()

    def pick_rows(i):
        ts = pl.ds(pl.multiple_of(i * 256, 256), 256)
        hit = lax.broadcasted_iota(I32, (SD * cap, 256), 0) == slot_of[:, ts]
        picked = jnp.where(hit, 1.0, 0.0).astype(BF)
        outs = jnp.concatenate([out_v[k, 0:cap, :] for k in range(SD)], axis=0)
        ings = jnp.concatenate([ing_v[k] for k in range(SD)], axis=0)
        both = mm(picked, jnp.concatenate([outs, ings], axis=1), TN)
        output[ts, :] = both[:, 0:D].astype(BF)
        input_grad[ts, :] = both[:, D:].astype(BF)
        line = jnp.concatenate([out_v[k, cap : cap + 8, 0:cap] for k in range(SD)], axis=1)
        entropy[:, ts] = mm(line, picked)[0:1].astype(BF)

    for q in (3, 1, 2, 0):
        load(q).wait()

    def steps(i, lag, more):
        s = i - lag
        by_x = (s % 2 == 0) & (s < 2 * split)
        live = (s >= 0) & (s < count)
        pl.when(live & by_x)(lambda: more(s, True))
        pl.when(live & jnp.logical_not(by_x))(lambda: more(s, False))

    def steps_of(i, lag, more):
        pl.when((i >= lag) & (i < count + lag))(lambda: more(i - lag))

    def round_of(i):
        for group in groups:

            @pl.when(i == group[1])
            def _(group=group):
                to_twin(3, group).wait_recv()

            @pl.when(i == group[1] + 1)
            def _(group=group):
                to_twin(1, group).wait_recv()
                to_twin(2, group).wait_recv()

            @pl.when(i == group[1] + 6)
            def _(group=group):
                to_twin(0, group).wait_recv()

        steps(i, 0, lambda s, by_x: first(s, d_x if by_x else d_y))
        steps(i, 1, lambda s, by_x: plain(1, s, to_x) if by_x else plain(2, s, to_y))
        steps(i, 3, lambda s, by_x: joined(2, s, d_x, to_y) if by_x else joined(1, s, d_y, to_x))
        steps_of(i, 6, own)
        steps_of(i, 8, middle)
        steps_of(i, 10, last)
        steps_of(i, 12, taken)

    loop(3, round_of)
    for copy in rows_in:
        copy.wait()
    slots_here, _ = route_slots(order[...], me % SD, cap)
    slot_of[...] = slots_here

    v_sum = vec[me]
    for d in range(1, n_tok):
        v_tok(d).wait()
        v_sum = v_sum + vt[d]
    va[...] = v_sum
    v_rep(0, va).start()

    def four_rounds(i):
        loop(4, lambda j: round_of(3 + 4 * i + j))
        pick_rows(i)

    four_rounds(0)
    v_rep(0, va).wait()
    vc[...] = va[...] + vb[0]
    v_rep(1, vc).start()
    loop(3, lambda i: four_rounds(1 + i))
    loop(count + 12 - 19, lambda i: round_of(19 + i))
    v_rep(1, vc).wait()
    vec_out[...] = vc[...] + vb[1]

    for group in groups:
        for q in range(4):
            to_twin(q, group).wait_send()

    def sent(s):
        d_y(s).wait_send()
        to_x(s).wait_send()
        to_y(s).wait_send()
        keep(s).wait()

    loop(count, sent)

    @pl.when(outer)
    def _():
        loop(count, lambda s: z_in(s).wait_send())

    @pl.when(inner)
    def _():
        def back(s):
            z_swap(s).wait_send()
            z_out(s).wait_send()

        loop(count, back)


def reduce_all(cap, grads, shares, order, outs, ings, count):
    dma = pltpu.SemaphoreType.DMA
    count = count * BLK // PART
    part = pltpu.VMEM((count, PART, D), BF)
    whole = pltpu.VMEM((4, count, PART, D), BF)
    line = pltpu.VMEM((16, 128), F32)
    rows = jax.ShapeDtypeStruct((ROWS, D), BF)
    total, vec, output, input_grad, entropy = pl.pallas_call(
        functools.partial(reduce_kernel, cap, count, count // 2),
        out_shape=(
            jax.ShapeDtypeStruct((count, PART, D), BF),
            jax.ShapeDtypeStruct((16, 128), F32),
            rows,
            rows,
            jax.ShapeDtypeStruct((1, ROWS), BF),
        ),
        in_specs=[ANY, VMEM, VMEM] + [ANY] * (2 * SD),
        out_specs=(ANY,) + (VMEM,) * 4,
        scratch_shapes=[
            pltpu.VMEM((SD, cap + META, D), BF),
            pltpu.VMEM((SD, cap, D), BF),
            pltpu.VMEM((1, ROWS), I32),
            whole,
            whole,
        ]
        + [part] * 8
        + [pltpu.VMEM((8, 16, 128), F32), line, pltpu.VMEM((2, 16, 128), F32), line]
        + [dma((4,)), dma((count,))]
        + [dma((4, 4))] * 2
        + [dma((count,))] * 12
        + [dma((8,))] * 2
        + [dma((2,))] * 2
        + [dma((2, SD))],
        compiler_params=pltpu.CompilerParams(collective_id=1, has_side_effects=True, vmem_limit_bytes=VMEM_LIMIT),
        cost_estimate=pl.CostEstimate(flops=4 * ROWS * ROWS * D, bytes_accessed=64 << 20, transcendentals=0),
        name="reduce",
    )(grads.reshape(-1, PART, D), shares, order, *outs, *ings)
    return total.reshape(-1, BLK, D), vec[0:9].reshape(-1), output, input_grad, entropy


V_BQ, V_BV, V_BO, V_BD, V_G1, V_C1, V_G2, V_C2 = range(8)


def inverse(x):
    r = pl.reciprocal(x, approx=True)
    return r * (2.0 - x * r)


def erf_parts(v):
    t = inverse(1.0 + (0.3275911 / math.sqrt(2.0)) * jnp.abs(v))
    e = jnp.exp2((v * v) * (-0.5 / math.log(2.0)))
    poly = 0.5 * 1.061405429
    for c in (-1.453152027, 1.421413741, -0.284496736, 0.254829592):
        poly = poly * t + 0.5 * c
    tail = poly * (t * e)
    return jnp.where(v >= 0.0, 1.0 - tail, tail), e


def lane_sum(x):
    return jnp.sum(x, axis=1, keepdims=True)


def gelu_parts(v):
    phi, e = erf_parts(v)
    return v * phi, phi + v * (e * (1.0 / math.sqrt(2.0 * math.pi)))


def weight_copies(pos, slots, w, sem, first):
    def copy(b):
        return pltpu.make_async_copy(slots.at[pos[first + b]], w.at[pl.ds(b * BLK, BLK)], sem)

    n = w.shape[0] // BLK
    return (lambda: loop(n, lambda b: copy(b).start())), (lambda: loop(n, lambda b: copy(b).wait()))


def halves_of_heads():
    lane = lax.broadcasted_iota(I32, (1, PW), 1)
    m0 = jnp.where(lane < HD, 1.0, 0.0).astype(BF)
    m1 = jnp.where(lane < HD, 0.0, 1.0).astype(BF)
    return lambda pair: jnp.concatenate([pair * m0, pair * m1], axis=0)


def tile_rows(t):
    return pl.ds(pl.multiple_of(t * TM, TM), TM)


def forward_kernel(
    cap,
    pos,
    slots,
    vecs,
    b_u,
    x_h,
    column,
    back_0,
    back_1,
    back_2,
    back_3,
    heads_h,
    act_h,
    hid_h,
    q_h,
    k_h,
    v_h,
    p_h,
    slope_h,
    n1_h,
    n2_h,
    rs1_h,
    rs2_h,
    wqkv,
    wo,
    wu,
    wd,
    x_c,
    heads,
    act,
    hid,
    q,
    k,
    v,
    p_all,
    slope,
    n1,
    n2,
    rs1,
    rs2,
    out_c,
    ent,
    hid_t,
    w_sem,
    x_sem,
    o_sem,
):
    inv = 1.0 / math.sqrt(HD)
    get_x = pltpu.make_async_copy(x_h, x_c, x_sem)
    get_x.start()
    weights = [
        weight_copies(pos, slots, w, w_sem.at[i], first)
        for i, (w, first) in enumerate(((wqkv, 0), (wo, 24), (wu, 32), (wd, 64)))
    ]
    for start, _ in weights:
        start()
    get_x.wait()
    apart = halves_of_heads()

    def vec(i):
        return vecs[i : i + 1, :]

    saved = (
        (heads, heads_h),
        (act, act_h),
        (hid, hid_h),
        (q, q_h),
        (k, k_h),
        (v, v_h),
        (slope, slope_h),
        (n1, n1_h),
        (n2, n2_h),
        (rs1, rs1_h),
        (rs2, rs2_h),
    )

    def save(t, i):
        src, dst = saved[i]
        return pltpu.make_async_copy(src.at[tile_rows(t)], dst.at[tile_rows(t)], o_sem.at[i])

    def save_p(t):
        n = TM // CL
        cs = pl.ds(t * n, n)
        return pltpu.make_async_copy(p_all.at[cs], p_h.at[cs], o_sem.at[len(saved)])

    def normal(r, n, rs, rows):
        c = r - lane_sum(r) * (1.0 / D)
        scale = lax.rsqrt(lane_sum(c * c) * (1.0 / D) + norm_epsilon)
        rs[rows, :] = jnp.broadcast_to(scale, (TM, 128))
        n[rows, :] = c * scale

    def tile(t):
        rows = tile_rows(t)
        first = t == 0
        pl.when(first)(weights[0][1])
        x = x_c[rows, :]
        q[rows, :] = ((mm(x, wqkv[0:D, :]) + vec(V_BQ)).astype(BF).astype(F32) * inv).astype(BF)
        k[rows, :] = mm(x, wqkv[D : 2 * D, :]).astype(BF)
        v[rows, :] = (mm(x, wqkv[2 * D :, :]) + vec(V_BV)).astype(BF)

        def attend(c):
            groups = [pl.ds(pl.multiple_of(t * TM + (FWD_AT * c + i) * CL, CL), CL) for i in range(FWD_AT)]
            pairs = [(i, p, slice(p * PW, (p + 1) * PW)) for i in range(FWD_AT) for p in range(PAIRS)]
            scores = [mm(apart(k[groups[i], ps]), q[groups[i], ps], NT) for i, _, ps in pairs]
            total = [jnp.zeros((1, CL), F32)] * FWD_AT
            probs = []
            for (i, _, _), both in zip(pairs, scores):
                halves = []
                for h in range(2):
                    sh = both[h * CL : (h + 1) * CL]
                    sh = sh - jnp.max(sh, axis=0, keepdims=True)
                    e = jnp.exp(sh)
                    tot = jnp.sum(e, axis=0, keepdims=True)
                    r = 1.0 / tot
                    total[i] += jnp.log(tot) - jnp.sum(e * sh, axis=0, keepdims=True) * r
                    halves.append((e * r).astype(BF))
                probs.append(jnp.concatenate(halves, axis=0))
            mixed = [mm(w, apart(v[groups[i], ps]), TN).astype(BF) for (i, _, ps), w in zip(pairs, probs)]
            for (i, p, ps), w, o in zip(pairs, probs, mixed):
                p_all[t * (TM // CL) + FWD_AT * c + i, p] = w
                heads[groups[i], ps] = o
            for i in range(FWD_AT):
                ent[:, groups[i]] = jnp.broadcast_to(total[i] * (1.0 / HEADS), (8, CL))

        loop(TM // CL // FWD_AT, attend)
        for i in (0, 3, 4, 5):
            save(t, i).start()
        save_p(t).start()
        pl.when(first)(weights[1][1])
        normal(x_c[rows, :].astype(F32) + mm(heads[rows, :], wo[...]) + vec(V_BO), n1, rs1, rows)
        hidden = n1[rows, :] * vec(V_G1) + vec(V_C1)
        hid[rows, :] = hidden.astype(BF)
        hid_t[...] = hidden
        pl.when(first)(weights[2][1])

        def widen(f):
            parts = [pl.ds(pl.multiple_of((2 * f + i) * FC, FC), FC) for i in range(2)]
            ups = [mm(hid[rows, :], wu[fs, :], NT) for fs in parts]
            for fs, up in zip(parts, ups):
                g, g_slope = gelu_parts(up + b_u[:, fs])
                act[rows, fs] = g.astype(BF)
                slope[rows, fs] = g_slope.astype(BF)

        loop(FF // FC // 2, widen)
        for i in (1, 2, 6, 7, 9):
            save(t, i).start()
        pl.when(first)(weights[3][1])
        normal(hid_t[...] + mm(act[rows, :], wd[...]) + vec(V_BD), n2, rs2, rows)
        out_c[rows, :] = (n2[rows, :] * vec(V_G2) + vec(V_C2)).astype(BF)
        for i in (8, 10):
            save(t, i).start()

    loop(ROWS // TM, tile)

    for j, back in enumerate((back_0, back_1, back_2, back_3)):
        own = seat_part(column, j, cap)
        back[0:cap, :] = mm(own, out_c[...]).astype(BF)
        line = mm(ent[...].astype(BF), own, NT)
        back[cap:, :] = jnp.concatenate([line, line], axis=1)[0:1].astype(BF) * jnp.ones((META, 1), BF)

    def saved_all(t):
        for i in range(len(saved)):
            save(t, i).wait()
        save_p(t).wait()

    loop(ROWS // TM, saved_all)


def shape_of(kind, *shape):
    return jax.ShapeDtypeStruct(shape, kind)


def saved_shapes():
    rows, wide = ((ROWS, D), BF), ((ROWS, FF), BF)
    probs = ((ROWS // CL, PAIRS, 2 * CL, CL), BF)
    full, thin = ((ROWS, D), F32), ((ROWS, 128), F32)
    return rows, wide, probs, full, thin


def forward(cap, positions, slots, vecs, b_u, x_c, column):
    rows, wide, probs, full, thin = saved_shapes()
    kept = (rows, wide, rows, rows, rows, rows, probs, wide, full, full, thin, thin)
    dma = pltpu.SemaphoreType.DMA
    return pl.pallas_call(
        functools.partial(forward_kernel, cap),
        out_shape=(shape_of(BF, cap + META, D),) * SD + tuple(shape_of(kind, *shape) for shape, kind in kept),
        in_specs=[SMEM, ANY, VMEM, VMEM, ANY, VMEM],
        out_specs=(VMEM,) * SD + (ANY,) * len(kept),
        scratch_shapes=[
            pltpu.VMEM((3 * D, D), BF),
            pltpu.VMEM((D, D), BF),
            pltpu.VMEM((FF, D), BF),
            pltpu.VMEM((FF, D), BF),
            pltpu.VMEM(*rows),
        ]
        + [pltpu.VMEM(*a) for a in kept]
        + [
            pltpu.VMEM(*rows),
            pltpu.VMEM((8, ROWS), F32),
            pltpu.VMEM((TM, D), F32),
            dma((4,)),
            dma,
            dma((12,)),
        ],
        compiler_params=pltpu.CompilerParams(vmem_limit_bytes=VMEM_LIMIT),
        cost_estimate=pl.CostEstimate(flops=2 * ROWS * WROWS * D, bytes_accessed=64 << 20, transcendentals=0),
        name="forward",
    )(positions, slots, vecs, b_u, x_c, column)


def backward_kernel(
    cap,
    pos,
    slots,
    vecs,
    meta,
    column,
    cot_0,
    cot_1,
    cot_2,
    cot_3,
    q_h,
    k_h,
    v_h,
    p_h,
    slope_h,
    n1_h,
    n2_h,
    rs1_h,
    rs2_h,
    back_0,
    back_1,
    back_2,
    back_3,
    shares,
    d_up_h,
    d_q_h,
    d_k_h,
    d_v_h,
    d_proj_h,
    d_br_h,
    wqkv,
    wo,
    wu,
    wd,
    blocks,
    q,
    k,
    v,
    p_all,
    d_up,
    n1,
    n2,
    rs1,
    rs2,
    d_proj,
    d_br,
    ing_c,
    d_h_t,
    gvec,
    g_bu,
    w_sem,
    c_sem,
    i_sem,
    o_sem,
):
    inv = 1.0 / math.sqrt(HD)
    get_c = [
        pltpu.make_async_copy(cot, blocks.at[j], c_sem.at[j]) for j, cot in enumerate((cot_0, cot_1, cot_2, cot_3))
    ]
    for copy in get_c:
        copy.start()
    fetch = [
        pltpu.make_async_copy(src, dst, i_sem.at[i])
        for i, (src, dst) in enumerate(
            (
                (n2_h, n2),
                (rs2_h, rs2),
                (slope_h, d_up),
                (n1_h, n1),
                (rs1_h, rs1),
                (v_h, v),
                (p_h, p_all),
                (k_h, k),
                (q_h, q),
            )
        )
    ]
    weights = [
        weight_copies(pos, slots, w, w_sem.at[i], first)
        for i, (w, first) in enumerate(((wd, 64), (wu, 32), (wo, 24), (wqkv, 0)))
    ]
    fetch[0].start()
    fetch[1].start()
    weights[0][0]()
    fetch[2].start()
    weights[1][0]()
    fetch[3].start()
    fetch[4].start()
    weights[2][0]()
    for i in range(5, 9):
        fetch[i].start()
    weights[3][0]()
    gvec[...] = jnp.zeros_like(gvec)
    g_bu[...] = jnp.zeros_like(g_bu)
    shares[...] = jnp.zeros_like(shares)
    for copy in get_c:
        copy.wait()
    seat_rows(meta, blocks, cap, d_br)
    apart = halves_of_heads()

    def vec(i):
        return vecs[i : i + 1, :]

    def add_vec(i, value):
        gvec[i : i + 1, :] += jnp.sum(value, axis=0, keepdims=True)

    saved = ((d_up, d_up_h), (q, d_q_h), (k, d_k_h), (v, d_v_h), (d_proj, d_proj_h), (d_br, d_br_h))

    def save(t, i):
        src, dst = saved[i]
        return pltpu.make_async_copy(src.at[tile_rows(t)], dst.at[tile_rows(t)], o_sem.at[i])

    def norm_back(e, n, rs, gain, shift):
        add_vec(gain, e * n)
        add_vec(shift, e)
        eg = e * vec(gain)
        return rs * (eg - lane_sum(eg) * (1.0 / D) - n * (lane_sum(eg * n) * (1.0 / D)))

    def norm_two_back(t):
        rows = tile_rows(t)
        d_r2 = norm_back(d_br[rows, :].astype(F32), n2[rows, :], rs2[rows, 0:1], V_G2, V_C2)
        d_br[rows, :] = d_r2.astype(BF)
        add_vec(V_BD, d_br[rows, :].astype(F32))
        n2[rows, :] = d_r2

    def widen_back(t, columns):
        rows = tile_rows(t)
        parts = [pl.ds(pl.multiple_of(f * FC, FC), FC) for f in columns]
        ups = [mm(d_br[rows, :], wd[fs, :], NT) for fs in parts]

        def finish():
            for fs, up in zip(parts, ups):
                du = (up * d_up[rows, fs].astype(F32)).astype(BF)
                d_up[rows, fs] = du
                g_bu[:, fs] += jnp.sum(du.astype(F32), axis=0, keepdims=True)

        return finish

    def hidden_back(t):
        rows = tile_rows(t)
        return n2[rows, :] + mm(d_up[rows, :], wu[...])

    def norm_one_back(t, d_h):
        rows = tile_rows(t)
        d_r1 = norm_back(d_h, n1[rows, :], rs1[rows, 0:1], V_G1, V_C1)
        d_proj[rows, :] = d_r1.astype(BF)
        n2[rows, :] = d_r1
        add_vec(V_BO, d_proj[rows, :].astype(F32))

    def heads_back(t):
        rows = tile_rows(t)
        d_h_t[rows, :] = mm(d_proj[rows, :], wo[...], NT).astype(BF)

    def attend_back(clusters, meanwhile=lambda: None):
        pairs = [
            (c, p, pl.ds(pl.multiple_of(c * CL, CL), CL), slice(p * PW, (p + 1) * PW))
            for c in clusters
            for p in range(PAIRS)
        ]
        probs = [p_all[c, p] for c, p, _, _ in pairs]
        d_heads = [d_h_t[gr, ps] for _, _, gr, ps in pairs]
        d_probs = [mm(apart(v[gr, ps]), dh, NT) for (_, _, gr, ps), dh in zip(pairs, d_heads)]
        d_values = [
            mm(jnp.concatenate([w[0:CL], w[CL:]], axis=1), apart(dh)).astype(BF) for w, dh in zip(probs, d_heads)
        ]
        finish = meanwhile()
        d_scores = []
        for w, dw in zip(probs, d_probs):
            halves = []
            for h in range(2):
                wh = w[h * CL : (h + 1) * CL].astype(F32)
                dwh = dw[h * CL : (h + 1) * CL]
                halves.append((wh * (dwh - jnp.sum(dwh * wh, axis=0, keepdims=True))).astype(BF))
            d_scores.append(halves)
        d_keys = [
            mm(jnp.concatenate(ds, axis=1), apart(q[gr, ps])).astype(BF) for (_, _, gr, ps), ds in zip(pairs, d_scores)
        ]
        d_queries = [
            (mm(jnp.concatenate(ds, axis=0), apart(k[gr, ps]), TN) * inv).astype(BF)
            for (_, _, gr, ps), ds in zip(pairs, d_scores)
        ]
        if finish is not None:
            finish()
        for (_, _, gr, ps), dq, dk, dv in zip(pairs, d_queries, d_keys, d_values):
            q[gr, ps] = dq
            k[gr, ps] = dk
            v[gr, ps] = dv

    def rows_back(t):
        rows = tile_rows(t)
        return (
            mm(q[rows, :], wqkv[0:D, :], NT)
            + mm(k[rows, :], wqkv[D : 2 * D, :], NT)
            + mm(v[rows, :], wqkv[2 * D :, :], NT)
        )

    def rows_done(t, d_x):
        rows = tile_rows(t)
        add_vec(V_BQ, q[rows, :].astype(F32))
        add_vec(V_BV, v[rows, :].astype(F32))
        ing_c[rows, :] = (n2[rows, :] + d_x.astype(BF).astype(F32)).astype(BF)

    def save_all(t, which):
        for i in which:
            save(t, i).start()

    per = TM // CL

    def tile(t):
        def once(*waits):
            @pl.when(t == 0)
            def _():
                for wait in waits:
                    wait()

        once(fetch[0].wait, fetch[1].wait)
        norm_two_back(t)
        once(weights[0][1], fetch[2].wait)
        loop(FF // FC // 2, lambda f: widen_back(t, [2 * f, 2 * f + 1])())
        save_all(t, (0, 5))
        once(weights[1][1], fetch[3].wait, fetch[4].wait)
        norm_one_back(t, hidden_back(t))
        once(weights[2][1], *(fetch[i].wait for i in range(5, 9)))
        heads_back(t)
        save_all(t, (4,))
        loop(per // BWD_AT, lambda c: attend_back([t * per + BWD_AT * c + i for i in range(BWD_AT)]))
        save_all(t, (1, 2, 3))
        once(weights[3][1])
        rows_done(t, rows_back(t))

    loop(ROWS // TM, tile)

    for j, back in enumerate((back_0, back_1, back_2, back_3)):
        back[...] = mm(seat_part(column, j, cap), ing_c[...]).astype(BF)

    for chunk in range(72):
        row, lane = chunk // 6, chunk % 6 * 128
        if row < 8:
            part = gvec[row : row + 1, lane : lane + 128]
        else:
            lane += (row - 8) * D
            part = g_bu[:, lane : lane + 128]
        shares[chunk // 9, chunk % 9 : chunk % 9 + 1, :] = part

    def saved_all(t):
        for i in range(len(saved)):
            save(t, i).wait()

    loop(ROWS // TM, saved_all)


def backward(cap, positions, slots, vecs, meta, column, cots, saved):
    rows, wide, probs, full, thin = saved_shapes()
    dma = pltpu.SemaphoreType.DMA
    grads = (wide, rows, rows, rows, rows, rows)
    return pl.pallas_call(
        functools.partial(backward_kernel, cap),
        out_shape=(shape_of(BF, cap, D),) * SD
        + (shape_of(F32, 8, 16, 128),)
        + tuple(shape_of(kind, *shape) for shape, kind in grads),
        in_specs=[SMEM, ANY, VMEM, VMEM, VMEM] + [ANY] * (SD + 9),
        out_specs=(VMEM,) * (SD + 1) + (ANY,) * len(grads),
        scratch_shapes=[
            pltpu.VMEM((3 * D, D), BF),
            pltpu.VMEM((D, D), BF),
            pltpu.VMEM((FF, D), BF),
            pltpu.VMEM((FF, D), BF),
            pltpu.VMEM((SD, cap, D), BF),
        ]
        + [pltpu.VMEM(*a) for a in (rows, rows, rows, probs, wide, full, full, thin, thin, rows, rows, rows)]
        + [
            pltpu.VMEM(*rows),
            pltpu.VMEM((8, D), F32),
            pltpu.VMEM((1, FF), F32),
            dma((4,)),
            dma((4,)),
            dma((9,)),
            dma((6,)),
        ],
        compiler_params=pltpu.CompilerParams(vmem_limit_bytes=VMEM_LIMIT),
        cost_estimate=pl.CostEstimate(flops=2 * ROWS * WROWS * D, bytes_accessed=64 << 20, transcendentals=0),
        name="backward",
    )(positions, slots, vecs, meta, column, *cots, *saved)


WC = 8 * BLK


def weight_kernel(
    pos,
    x_h,
    heads_h,
    act_h,
    d_up_h,
    d_q_h,
    d_k_h,
    d_v_h,
    d_proj_h,
    hid_h,
    d_br_h,
    grads,
    x_c,
    heads,
    act,
    d_up,
    d_q,
    d_k,
    d_v,
    d_proj,
    hid,
    d_br,
    stage,
    i_sem,
    g_sem,
):
    refs = (
        (x_h, x_c),
        (d_q_h, d_q),
        (d_k_h, d_k),
        (d_v_h, d_v),
        (heads_h, heads),
        (d_proj_h, d_proj),
        (hid_h, hid),
        (d_up_h, d_up),
        (d_br_h, d_br),
        (act_h, act),
    )
    fetch = [pltpu.make_async_copy(src, dst, i_sem.at[i]) for i, (src, dst) in enumerate(refs)]
    for copy in fetch:
        copy.start()

    per = WC // BLK

    def g_copy(chunk, j, at):
        return pltpu.make_async_copy(
            stage.at[at, pl.ds(j * BLK, BLK)], grads.at[pos[chunk * per + j]], g_sem.at[at]
        )

    def put(chunk, left, right):
        at = lax.rem(chunk, 2)

        @pl.when(chunk >= 2)
        def _():
            for j in range(per):
                g_copy(chunk - 2, j, at).wait()

        stage[at] = mm(left, right, TN).astype(BF)
        for j in range(per):
            g_copy(chunk, j, at).start()

    first = 0
    for left, right, needs in (
        (x_c, d_q, (0, 1)),
        (x_c, d_k, (2,)),
        (x_c, d_v, (3,)),
        (heads, d_proj, (4, 5)),
        (d_up, hid, (6, 7)),
        (act, d_br, (8, 9)),
    ):
        for i in needs:
            fetch[i].wait()

        def body(j, left=left, right=right, first=first):
            put(first + j, left[:, pl.ds(pl.multiple_of(j * WC, WC), WC)], right[...])

        loop(left.shape[1] // WC, body)
        first += left.shape[1] // WC
    for chunk in (first - 2, first - 1):
        for j in range(per):
            g_copy(chunk, j, chunk % 2).wait()


def weight_grads_of(total_slots, positions, x_c, saved):
    r_v, w_v = pltpu.VMEM((ROWS, D), BF), pltpu.VMEM((ROWS, FF), BF)
    return pl.pallas_call(
        weight_kernel,
        out_shape=jax.ShapeDtypeStruct((total_slots, BLK, D), BF),
        in_specs=[SMEM] + [ANY] * 10,
        out_specs=ANY,
        scratch_shapes=[r_v, r_v, w_v, w_v]
        + [r_v] * 6
        + [
            pltpu.VMEM((2, WC, D), BF),
            pltpu.SemaphoreType.DMA((10,)),
            pltpu.SemaphoreType.DMA((2,)),
        ],
        compiler_params=pltpu.CompilerParams(vmem_limit_bytes=VMEM_LIMIT),
        cost_estimate=pl.CostEstimate(flops=2 * ROWS * WROWS * D, bytes_accessed=40 << 20, transcendentals=0),
        name="weight_grads",
    )(positions, x_c, *saved)


def local(
    tokens,
    cotangent,
    cluster_order,
    block_owner,
    master_slots,
    moment_one,
    moment_two,
    vector_master,
    vector_moment_one,
    vector_moment_two,
):
    tok_count = lax.axis_size("tok")
    tok_index = lax.axis_index("tok")
    slot_count = master_slots.shape[0]
    cap = tok_count // SD * (max(1, CPS // tok_count) * 3 * CL // (2 * SD))
    total_slots = tok_count * slot_count
    order = cluster_order.reshape(1, ROWS)

    block = jax.ShapeDtypeStruct((SD, cap, D), BF)
    meta_shape = jax.ShapeDtypeStruct((SD, META, D), BF)
    row_block = jax.ShapeDtypeStruct((ROWS, D), BF)
    four_planes = tok_count == 8 and lax.axis_size("rep") == 4
    if four_planes:
        slots_low, x_c, *cots, recv_meta, column, vecs, b_u, occupancy, positions = gather_all(
            cap, tokens, cotangent, order, master_slots, vector_master, block_owner
        )
        positions = positions.reshape(NBLK)
        slots_low = slots_low.reshape(total_slots, BLK, D)
    else:
        positions = slot_positions(block_owner, slot_count)
        slots_low = lax.all_gather(master_slots.astype(BF), "tok", axis=0, tiled=True)
        vectors = lax.all_gather(vector_master.astype(BF), "tok", axis=0, tiled=True).astype(F32)
        vecs, b_u = vectors[: 8 * D].reshape(8, D), vectors[8 * D :].reshape(1, FF)
        cluster = tok_index // SD * CPS + cluster_order // CL
        target = cluster % tok_count
        chosen = target[None, :] == jnp.arange(tok_count, dtype=jnp.int32)[:, None]
        sent_counts = jnp.sum(chosen.astype(F32), axis=1)
        own_row = (jnp.arange(tok_count, dtype=jnp.int32) == tok_index).astype(F32)
        occupancy = lax.psum(own_row[:, None] * sent_counts[None, :], ("tok", "rep")).astype(jnp.int32)
        send_x, send_c, meta, column = pl.pallas_call(
            functools.partial(send_kernel, cap),
            out_shape=(block, block, meta_shape, jax.ShapeDtypeStruct((SD, cap, 128), BF)),
            in_specs=[VMEM] * 3,
            out_specs=(VMEM,) * 4,
            compiler_params=pltpu.CompilerParams(vmem_limit_bytes=VMEM_LIMIT),
            name="send_rows",
        )(tokens, cotangent, order)
        recv_x, recv_meta, column = (jnp.stack(swap_blocks(b)) for b in (send_x, meta, column))
        x_c = pl.pallas_call(
            functools.partial(seat_kernel, cap),
            out_shape=row_block,
            in_specs=[VMEM] * 2,
            out_specs=VMEM,
            compiler_params=pltpu.CompilerParams(vmem_limit_bytes=VMEM_LIMIT),
            name="seat_rows",
        )(recv_x, recv_meta)
        cots = [send_c[k] for k in range(SD)]

    cots = swap_blocks(cots)
    *out_blocks, heads, act, hid, q, k, v, p, slope, n1, n2, rs1, rs2 = forward(
        cap, positions, slots_low, vecs, b_u, x_c, column
    )
    out_blocks = swap_blocks(out_blocks)
    *ing_blocks, shares, d_up, d_q, d_k, d_v, d_proj, d_br = backward(
        cap, positions, slots_low, vecs, recv_meta, column, cots, (q, k, v, p, slope, n1, n2, rs1, rs2)
    )
    ing_blocks = swap_blocks(ing_blocks)
    grads = weight_grads_of(
        total_slots, positions, x_c, (heads, act, d_up, d_q, d_k, d_v, d_proj, hid, d_br)
    )
    if four_planes:
        total, vec_owned, output, input_grad, entropy = reduce_all(
            cap, grads, shares, order, out_blocks, ing_blocks, slot_count
        )
    else:
        total = lax.psum(lax.psum_scatter(grads, "tok", scatter_dimension=0, tiled=True), "rep")
        grad_vector = shares[:, 0:9].reshape(-1)
        vec_owned = lax.psum(lax.psum_scatter(grad_vector, "tok", scatter_dimension=0, tiled=True), "rep")
        output, input_grad, entropy = pl.pallas_call(
            functools.partial(return_kernel, cap),
            out_shape=(row_block, row_block, jax.ShapeDtypeStruct((1, ROWS), BF)),
            in_specs=[VMEM] * (2 * SD + 1),
            out_specs=(VMEM,) * 3,
            compiler_params=pltpu.CompilerParams(vmem_limit_bytes=VMEM_LIMIT),
            name="return_rows",
        )(order, *out_blocks, *ing_blocks)

    used = jnp.any(
        positions[None, :] == (tok_index * slot_count + jnp.arange(slot_count, dtype=I32))[:, None], axis=1
    )
    owned_grad = jnp.where(used[:, None, None], total.astype(F32), 0.0)
    first_new, second_new, master_new = adam_update(
        owned_grad, master_slots, moment_one, moment_two, rate_matrix
    )
    vec_first, vec_second, vec_new = adam_update(
        vec_owned, vector_master, vector_moment_one, vector_moment_two, rate_vector
    )
    return (
        output,
        input_grad,
        owned_grad,
        first_new,
        second_new,
        master_new,
        master_new.astype(BF),
        vec_owned,
        vec_first,
        vec_second,
        vec_new,
        vec_new.astype(BF),
        entropy.reshape(-1),
        occupancy,
    )


def solution(mesh):
    placed = (
        P(("rep", "tok"), None),
        P(("rep", "tok"), None),
        P(("rep", "tok")),
        P(),
        P("tok", None, None),
        P("tok", None, None),
        P("tok", None, None),
        P("tok"),
        P("tok"),
        P("tok"),
    )
    return jax.shard_map(
        local,
        mesh=mesh,
        in_specs=placed,
        out_specs=(
            P(("rep", "tok"), None),
            P(("rep", "tok"), None),
            P("tok", None, None),
            P("tok", None, None),
            P("tok", None, None),
            P("tok", None, None),
            P("tok", None, None),
            P("tok"),
            P("tok"),
            P("tok"),
            P("tok"),
            P("tok"),
            P(("rep", "tok")),
            P(),
        ),
        check_vma=False,
    )
```

```python
import functools
import math

import jax
import jax.numpy as jnp
from jax import lax
from jax.experimental import pallas as pl
from jax.experimental.pallas import tpu as pltpu
from jax.sharding import PartitionSpec as P

D = 768
HEADS = 12
HD = 64
FF = 3072
SD = 4
CL = 128
NBLK = 96
STEP = 10
CPS = 32
WROWS = 9216
BLK = 96
ROWS = 1024
PAIRS = HEADS // 2
PW = 2 * HD
TM = 512
PART = 48
META = 16
VMEM_LIMIT = 63 << 20
FC = 768
FWD_AT = 4
BWD_AT = 2

norm_epsilon = 1e-06
beta_first = 0.9
beta_second = 0.999
adam_epsilon = 1e-08
weight_decay = 0.01
rate_matrix = 0.02
rate_vector = 0.2

BF = jnp.bfloat16
F32 = jnp.float32
I32 = jnp.int32

VMEM = pl.BlockSpec(memory_space=pltpu.VMEM)
SMEM = pl.BlockSpec(memory_space=pltpu.SMEM)
ANY = pl.BlockSpec(memory_space=pl.ANY)

NN = (((1,), (0,)), ((), ()))
NT = (((1,), (1,)), ((), ()))
TN = (((0,), (0,)), ((), ()))


def mm(a, b, dims=NN):
    return lax.dot_general(a, b, dims, preferred_element_type=F32)


def slot_positions(block_owner, slot_count):
    owners = block_owner[:, 0]
    blocks = owners.shape[0]
    shared = owners[:, None] == owners[None, :]
    before = (
        jnp.arange(blocks, dtype=jnp.int32)[None, :] < jnp.arange(blocks, dtype=jnp.int32)[:, None]
    )
    earlier = jnp.sum((shared & before).astype(jnp.int32), axis=1)
    return owners * slot_count + earlier


def adam_update(grad_now, weight_old, first_old, second_old, rate_step):
    first_new = beta_first * first_old + (1.0 - beta_first) * grad_now
    second_new = beta_second * second_old + (1.0 - beta_second) * grad_now * grad_now
    first_hat = first_new / (1.0 - beta_first**STEP)
    second_hat = second_new / (1.0 - beta_second**STEP)
    weight_new = weight_old - rate_step * (
        first_hat / (jnp.sqrt(second_hat) + adam_epsilon) + weight_decay * weight_old
    )
    return (first_new, second_new, weight_new)


def unit(n):
    same = lax.broadcasted_iota(I32, (n, n), 0) == lax.broadcasted_iota(I32, (n, n), 1)
    return jnp.where(same, 1.0, 0.0).astype(BF)


def route_slots(order, seat, cap):
    cluster = order // CL
    rel = lax.rem(cluster, SD) ^ seat
    place = (cluster // SD) * CL + lax.rem(order, CL) + 1
    chosen = lax.broadcasted_iota(I32, (8, ROWS), 0) == rel
    chosen_low = jnp.where(chosen, 1.0, 0.0).astype(BF)
    before = lax.broadcasted_iota(I32, (ROWS, ROWS), 0) < lax.broadcasted_iota(I32, (ROWS, ROWS), 1)
    before_low = jnp.where(before, 1.0, 0.0).astype(BF)
    running = mm(chosen_low, before_low)
    rank = jnp.sum(jnp.where(chosen, running, 0.0), axis=0, keepdims=True).astype(I32)
    return rel * cap + rank, place


def slot_matrix(slots, at, cap):
    rows = lax.broadcasted_iota(I32, (cap, ROWS), 0) + at * cap
    return jnp.where(rows == slots, 1.0, 0.0).astype(BF)


def send_kernel(cap, tokens, cotangent, order, send_x, send_c, meta):
    seat = lax.rem(lax.axis_index("tok"), SD)
    slots, place = route_slots(order[...], seat, cap)
    digits = jnp.concatenate([place // CL, lax.rem(place, CL)] + [place * 0] * 6, axis=0).astype(F32).astype(BF)
    for at in range(SD):
        picked = slot_matrix(slots, at, cap)
        send_x[at] = mm(picked, tokens[...]).astype(BF)
        send_c[at] = mm(picked, cotangent[...]).astype(BF)
        coded = mm(digits, picked, NT)
        line = jnp.concatenate([coded[0:1], coded[1:2]], axis=1)
        meta[at] = jnp.broadcast_to(line, (META, D)).astype(BF)


def remote(src, dst, send_sem, recv_sem, tok, rep):
    return pltpu.make_async_remote_copy(
        src_ref=src,
        dst_ref=dst,
        send_sem=send_sem,
        recv_sem=recv_sem,
        device_id={"tok": tok, "rep": rep},
        device_id_type=pl.DeviceIdType.MESH,
    )


def loop(n, body):
    def run(i, c):
        body(i)
        return c

    lax.fori_loop(0, n, run, 0)


class Place:
    def __init__(self):
        self.me = me = lax.axis_index("tok")
        self.z = z = lax.axis_index("rep")
        core, x, y = me % 2, (me // 2) % 2, me // 4
        self.twin = me + 1 - 2 * core
        self.xn = me + 2 - 4 * x
        self.yn = me + 4 - 8 * y
        self.dn = self.xn + 4 - 8 * y
        self.side = z % 2
        self.zp = z + 1 - 2 * self.side

    def twin_of(self, tok):
        return tok + 1 - 2 * (tok % 2)

    def greet(self, peers):
        barrier = pltpu.get_barrier_semaphore()
        for tok, rep in peers:
            pl.semaphore_signal(
                barrier, inc=1, device_id={"tok": tok, "rep": rep}, device_id_type=pl.DeviceIdType.MESH
            )
        return lambda: pl.semaphore_wait(barrier, len(peers))


def seat_matrix(meta, first, rows, cap):
    hi = jnp.concatenate([meta[k, 0:8, 0:cap] for k in range(SD)], axis=1).astype(F32)[0:1]
    lo = jnp.concatenate([meta[k, 0:8, cap : 2 * cap] for k in range(SD)], axis=1).astype(F32)[0:1]
    at = (hi * CL + lo).astype(I32)
    seats = lax.broadcasted_iota(I32, (rows, SD * cap), 0) + (first + 1)
    return jnp.where(seats == at, 1.0, 0.0).astype(BF)


def seat_part(meta, k, cap):
    one = unit(cap)
    hi = mm(one, meta[k, :, 0:cap], NT)[:, 0:1]
    lo = mm(one, meta[k, :, cap : 2 * cap], NT)[:, 0:1]
    at = (hi * CL + lo).astype(I32)
    seats = lax.broadcasted_iota(I32, (cap, ROWS), 1) + 1
    return jnp.where(seats == at, 1.0, 0.0).astype(BF)


def seat_rows(meta, blocks, cap, to):
    def body(t):
        r0 = pl.multiple_of(t * 256, 256)
        rows = blocks[...].reshape(SD * cap, D)
        to[pl.ds(r0, 256), :] = mm(seat_matrix(meta, r0, 256, cap), rows).astype(BF)

    loop(ROWS // 256, body)


def seat_kernel(cap, blocks, meta, to):
    seat_rows(meta, blocks, cap, to)


def gather_kernel(
    cap,
    count,
    tokens_h,
    cotangent_h,
    order,
    master_h,
    vector,
    owner_of,
    slots,
    x_c,
    cot_0,
    cot_1,
    cot_2,
    cot_3,
    recv_meta,
    vecs,
    b_u,
    occupancy,
    positions,
    tokens,
    cotangent,
    master,
    own,
    send_x,
    send_c,
    meta,
    recv_x,
    got_meta,
    slot_of,
    digits,
    mine,
    by_z,
    by_tok,
    x_s,
    x_r,
    y_s,
    y_r,
    d_s,
    d_r,
    zx_s,
    zx_r,
    zd_s,
    zd_r,
    zy_s,
    zy_r,
    p_s,
    p_r,
    row_s,
    row_r,
    z_s,
    z_r,
    t_s,
    t_r,
    local_s,
):
    at = Place()
    me, z, side = at.me, at.z, at.side
    n_tok, n_rep = 8, 4
    peers = [((me + d) % n_tok, z) for d in range(1, n_tok)] + [(me, (z + d) % n_rep) for d in range(1, n_rep)]
    fetch = [
        pltpu.make_async_copy(src, dst, local_s.at[i])
        for i, (src, dst) in enumerate(((master_h, master), (tokens_h, tokens), (cotangent_h, cotangent)))
    ]
    for copy in fetch:
        copy.start()
    wait_peers = at.greet(peers)
    fetch[0].wait()

    last = count - 1

    def near(j):
        return side * last + (1 - 2 * side) * j

    def far(j):
        return (1 - side) * last - (1 - 2 * side) * j

    few_x, few_d, few_y = 11 * count // 26, 12 * count // 26, 8 * count // 26
    most_x, most_d, most_y = count - few_x, count - few_d, count - few_y

    def piece(owner, s):
        return slots.at[owner * count + s]

    def to_x(s):
        return remote(own.at[s], piece(me, s), x_s.at[s], x_r.at[s], at.xn, z)

    def to_y(s):
        return remote(own.at[s], piece(me, s), y_s.at[s], y_r.at[s], at.yn, z)

    def on_y(s):
        return remote(piece(at.xn, s), piece(at.xn, s), d_s.at[s], d_r.at[s], at.yn, z)

    def x_on_z(s):
        return remote(piece(at.xn, s), piece(at.xn, s), zx_s.at[s], zx_r.at[s], me, at.zp)

    def d_on_z(s):
        return remote(piece(at.dn, s), piece(at.dn, s), zd_s.at[s], zd_r.at[s], me, at.zp)

    def y_on_z(s):
        return remote(piece(at.yn, s), piece(at.yn, s), zy_s.at[s], zy_r.at[s], me, at.zp)

    def x_in(s):
        return remote(own.at[s], piece(at.xn, s), x_s.at[s], x_r.at[s], at.xn, z)

    def y_in(s):
        return remote(own.at[s], piece(at.yn, s), y_s.at[s], y_r.at[s], at.yn, z)

    def d_in(s):
        return remote(own.at[s], piece(at.dn, s), d_s.at[s], d_r.at[s], at.yn, z)

    owners = (me, at.xn, at.yn, at.dn)

    def near_run(q, j0, j1):
        return (q, (1 - side) * j0 + side * (count - j1), j1 - j0)

    def far_run(q, j0, j1):
        return (q, side * j0 + (1 - side) * (count - j1), j1 - j0)

    runs = (
        (0, 0, count),
        near_run(2, 0, few_y),
        near_run(1, 0, most_x),
        near_run(3, 0, most_d),
        far_run(1, 0, few_x),
        near_run(2, few_y, most_y),
        far_run(2, 0, few_y),
        far_run(3, 0, few_d // 2),
        far_run(3, few_d // 2, few_d - 2),
        far_run(3, few_d - 2, few_d),
    )

    def to_twin(i):
        q, s, n = runs[i]
        src = own if q == 0 else slots.at[pl.ds(owners[q] * count + s, n)]
        dst = slots.at[pl.ds(owners[q] * count + s, n)]
        return remote(src, dst, p_s.at[i], p_r.at[i], at.twin, z)

    def cast(j):
        own[near(j)] = master[near(j)].astype(BF)

    loop(most_x, cast)
    wait_peers()
    loop(most_x, lambda j: to_x(near(j)).start())
    loop(few_y, lambda j: to_y(near(j)).start())
    loop(count - most_x, lambda j: cast(most_x + j))
    to_twin(0).start()
    keep = pltpu.make_async_copy(own, slots.at[pl.ds(me * count, count)], local_s.at[3])
    keep.start()

    seat = me % SD
    seats = (me, at.twin, at.xn, at.twin_of(at.xn))
    rows_of = ((meta, got_meta), (send_x, recv_x))

    def row_copy(i, k):
        src, dst = rows_of[i]
        return remote(src.at[k], dst.at[k], row_s.at[i, k], row_r.at[i, k], seats[k], z)

    put_c = [
        pltpu.make_async_copy(send_c.at[k], to, local_s.at[4 + k])
        for k, to in enumerate((cot_0, cot_1, cot_2, cot_3))
    ]

    def route():
        fetch[1].wait()
        fetch[2].wait()
        slots_here, place = route_slots(order[...], seat, cap)
        slot_of[...] = slots_here
        digits[...] = (
            jnp.concatenate([place // CL, lax.rem(place, CL)] + [place * 0] * 6, axis=0).astype(F32).astype(BF)
        )

    def sort_tokens(k):
        picked = slot_matrix(slot_of[...], k, cap)
        send_x[k] = mm(picked, tokens[...]).astype(BF)
        coded = mm(digits[...], picked, NT)
        line = jnp.concatenate([coded[0:1], coded[1:2]], axis=1)
        meta[k] = jnp.broadcast_to(line, (META, D)).astype(BF)
        for i in range(2):
            if k:
                row_copy(i, k).start()
            else:
                src, dst = rows_of[i]
                dst[0] = src[0]

    def sort_cotangent(k):
        send_c[k] = mm(slot_matrix(slot_of[...], k, cap), cotangent[...]).astype(BF)
        put_c[k].start()

    def z_copy(d):
        return remote(by_z.at[0], by_z.at[d], z_s.at[d], z_r.at[d], me, (z + d) % n_rep)

    def t_copy(d):
        return remote(mine, by_tok.at[d], t_s.at[d], t_r.at[d], (me + d) % n_tok, z)

    def count_rows():
        residue = lax.rem(me // SD * CPS + order[...] // CL, n_tok)
        hit = lax.broadcasted_iota(I32, (128, ROWS), 0) == residue
        by_z[0] = mm(jnp.ones((8, ROWS), BF), jnp.where(hit, 1.0, 0.0).astype(BF), NT)
        for d in range(1, n_rep):
            z_copy(d).start()
        for i in range(9):
            mine[i : i + 1] = vector[i * 128 : (i + 1) * 128].reshape(1, 128).astype(BF).astype(F32)
        block_row = lax.broadcasted_iota(I32, (NBLK, NBLK), 0)
        block_col = lax.broadcasted_iota(I32, (NBLK, NBLK), 1)
        by_col = owner_of[...].astype(F32)
        by_row = lane_sum(jnp.where(block_row == block_col, by_col, 0.0))
        earlier = jnp.where((by_row == by_col) & (block_row < block_col), 1.0, 0.0)
        positions[...] = (by_col * (count * PART // BLK) + jnp.sum(earlier, axis=0, keepdims=True)).astype(I32)

    def share_vectors():
        for d in range(1, n_rep):
            z_copy(d).wait()
        mine[16:24] = by_z[0] + by_z[1] + by_z[2] + by_z[3]
        for d in range(1, n_tok):
            t_copy(d).start()

    def lay_out_vectors():
        by_tok[0] = mine[...]
        for d in range(1, n_tok):
            t_copy(d).wait()
        for owner in range(n_tok):
            share = by_tok[(me + n_tok - owner) % n_tok]
            occupancy[owner : owner + 1, :] = share[16:17, 0:n_tok].astype(I32)
            for i in range(9):
                chunk = owner * 9 + i
                row, lane = chunk // 6, chunk % 6 * 128
                if row < 8:
                    vecs[row : row + 1, lane : lane + 128] = share[i : i + 1]
                else:
                    lane += (row - 8) * D
                    b_u[:, lane : lane + 128] = share[i : i + 1]

    between = {
        1: lambda: (route(), sort_tokens(2)),
        3: lambda: sort_tokens(3),
        5: lambda: sort_tokens(1),
        7: lambda: (sort_tokens(0), count_rows()),
        9: lambda: sort_cotangent(1),
        11: lambda: sort_cotangent(2),
        13: lambda: sort_cotangent(3),
    }
    for j in range(most_x):
        x_in(near(j)).wait_recv()
        if j < most_d:
            on_y(near(j)).start()
        if j < few_x:
            x_on_z(near(j)).start()
        if j < few_y:
            y_in(near(j)).wait_recv()
            y_on_z(near(j)).start()
        if j == few_y:
            to_twin(1).start()
        if j in between:
            between[j]()
    to_twin(2).start()
    loop(most_y - few_y, lambda j: to_y(near(few_y + j)).start())
    share_vectors()
    sort_cotangent(0)

    def diagonal(j):
        d_in(near(j)).wait_recv()
        d_on_z(near(j)).start()

    loop(few_d, diagonal)
    loop(most_d - few_d, lambda j: d_in(near(few_d + j)).wait_recv())
    to_twin(3).start()
    loop(few_x, lambda j: x_on_z(far(j)).wait_recv())
    to_twin(4).start()
    lay_out_vectors()
    loop(most_y - few_y, lambda j: y_in(near(few_y + j)).wait_recv())
    to_twin(5).start()
    loop(few_y, lambda j: y_on_z(far(j)).wait_recv())
    to_twin(6).start()
    for i in (0, 1):
        for k in (2, 3, 1):
            row_copy(i, k).wait_recv()
    recv_meta[...] = got_meta[...]
    seat_rows(got_meta, recv_x, cap, x_c)
    done = 0
    for i, upto in ((7, few_d // 2), (8, few_d - 2), (9, few_d)):
        loop(upto - done, lambda j, done=done: d_on_z(far(done + j)).wait_recv())
        to_twin(i).start()
        done = upto

    for i in range(2):
        for k in (2, 3, 1):
            row_copy(i, k).wait_send()
    for copy in put_c:
        copy.wait()
    keep.wait()

    loop(most_x, lambda j: to_x(near(j)).wait_send())
    loop(most_y, lambda j: to_y(near(j)).wait_send())
    loop(most_d, lambda j: on_y(near(j)).wait_send())
    loop(few_x, lambda j: x_on_z(near(j)).wait_send())
    loop(few_d, lambda j: d_on_z(near(j)).wait_send())
    loop(few_y, lambda j: y_on_z(near(j)).wait_send())
    for i in range(len(runs)):
        to_twin(i).wait()


def gather_all(cap, tokens, cotangent, order, master, vector, block_owner):
    count = master.shape[0] * BLK // PART
    rows = jax.ShapeDtypeStruct((ROWS, D), BF)
    part = jax.ShapeDtypeStruct((cap, D), BF)
    dma = pltpu.SemaphoreType.DMA
    block = pltpu.VMEM((SD, cap, D), BF)
    meta = pltpu.VMEM((SD, META, D), BF)
    return pl.pallas_call(
        functools.partial(gather_kernel, cap, count),
        out_shape=(
            jax.ShapeDtypeStruct((8 * count, PART, D), BF),
            rows,
            part,
            part,
            part,
            part,
            jax.ShapeDtypeStruct((SD, META, D), BF),
            jax.ShapeDtypeStruct((8, D), F32),
            jax.ShapeDtypeStruct((1, FF), F32),
            jax.ShapeDtypeStruct((8, 8), I32),
            jax.ShapeDtypeStruct((1, NBLK), I32),
        ),
        in_specs=[ANY, ANY, VMEM, ANY, VMEM, VMEM],
        out_specs=(ANY, VMEM) + (ANY,) * SD + (VMEM,) * 5,
        scratch_shapes=[
            pltpu.VMEM((ROWS, D), BF),
            pltpu.VMEM((ROWS, D), BF),
            pltpu.VMEM((count, PART, D), F32),
            pltpu.VMEM((count, PART, D), BF),
            block,
            block,
            meta,
            block,
            meta,
            pltpu.VMEM((1, ROWS), I32),
            pltpu.VMEM((8, ROWS), BF),
            pltpu.VMEM((24, 128), F32),
            pltpu.VMEM((4, 8, 128), F32),
            pltpu.VMEM((8, 24, 128), F32),
        ]
        + [dma((count,))] * 12
        + [dma((10,))] * 2
        + [dma((2, SD))] * 2
        + [dma((4,))] * 2
        + [dma((8,))] * 2
        + [dma((8,))],
        compiler_params=pltpu.CompilerParams(collective_id=0, has_side_effects=True, vmem_limit_bytes=VMEM_LIMIT),
        cost_estimate=pl.CostEstimate(flops=8 * ROWS * ROWS * D, bytes_accessed=64 << 20, transcendentals=0),
        name="gather",
    )(tokens, cotangent, order, master.reshape(count, PART, D), vector, block_owner.reshape(1, NBLK))


def return_kernel(cap, order, *refs):
    outs, ings, (out, ing, entropy) = refs[:SD], refs[SD : 2 * SD], refs[2 * SD :]
    seat = lax.rem(lax.axis_index("tok"), SD)
    slots, _ = route_slots(order[...], seat, cap)
    picked = jnp.concatenate([slot_matrix(slots, at, cap) for at in range(SD)], axis=0)
    for to, blocks in ((out, outs), (ing, ings)):
        rows = jnp.concatenate([block[0:cap, :] for block in blocks], axis=0)
        to[...] = mm(picked, rows, TN).astype(BF)
    line = jnp.concatenate([block[cap : cap + 8, 0:cap] for block in outs], axis=1)
    entropy[...] = mm(line, picked)[0:1].astype(BF)


def swap_blocks(blocks):
    n = lax.axis_size("tok")
    parts = [blocks[0]]
    for k in range(1, SD):
        parts.append(lax.ppermute(blocks[k], "tok", [(i, i ^ k) for i in range(n)]))
    return parts


def reduce_kernel(
    cap,
    count,
    split,
    grads,
    vec,
    order,
    out_0,
    out_1,
    out_2,
    out_3,
    ing_0,
    ing_1,
    ing_2,
    ing_3,
    total,
    vec_out,
    output,
    input_grad,
    entropy,
    out_v,
    ing_v,
    slot_of,
    a,
    tw,
    rd,
    rx,
    ry,
    o,
    rz1,
    pz,
    rz2,
    fz,
    vt,
    va,
    vb,
    vc,
    a_l,
    keep_l,
    p_s,
    p_r,
    d_s,
    d_r,
    x_s,
    x_r,
    y_s,
    y_r,
    z1_s,
    z1_r,
    z2_s,
    z2_r,
    z3_s,
    z3_r,
    t_s,
    t_r,
    v_s,
    v_r,
    row_l,
):
    at = Place()
    me, z = at.me, at.z
    n_tok, n_rep = 8, 4
    peers = [((me + d) % n_tok, z) for d in range(1, n_tok)] + [(me, (z + d) % n_rep) for d in range(1, n_rep)]
    wait_peers = at.greet(peers)
    owners = (me, at.xn, at.yn, at.dn)

    def load(q):
        return pltpu.make_async_copy(grads.at[pl.ds(owners[q] * count, count)], a.at[q], a_l.at[q])

    for q in (3, 1, 2, 0):
        load(q).start()
    rows_in = [
        pltpu.make_async_copy(src, to.at[k], row_l.at[i, k])
        for i, (blocks, to) in enumerate((((out_0, out_1, out_2, out_3), out_v), ((ing_0, ing_1, ing_2, ing_3), ing_v)))
        for k, src in enumerate(blocks)
    ]
    for copy in rows_in:
        copy.start()
    wait_peers()

    groups = [(g, g * (count // 4), count // 4 if g < 3 else count - 3 * (count // 4)) for g in range(4)]

    def to_twin(q, group):
        g, s, n = group
        src = grads.at[pl.ds(at.twin_of(owners[q]) * count + s, n)]
        return remote(src, tw.at[q, pl.ds(s, n)], p_s.at[q, g], p_r.at[q, g], at.twin, z)

    def d_y(s):
        return remote(a.at[3, s], rd.at[s], d_s.at[s], d_r.at[s], at.yn, z)

    def d_x(s):
        return remote(a.at[3, s], rd.at[s], d_s.at[s], d_r.at[s], at.xn, z)

    def to_x(s):
        return remote(a.at[1, s], rx.at[s], x_s.at[s], x_r.at[s], at.xn, z)

    def to_y(s):
        return remote(a.at[2, s], ry.at[s], y_s.at[s], y_r.at[s], at.yn, z)

    def z_in(s):
        return remote(o.at[s], rz1.at[s], z1_s.at[s], z1_r.at[s], me, at.zp)

    def z_swap(s):
        return remote(pz.at[s], rz2.at[s], z2_s.at[s], z2_r.at[s], me, n_rep - 1 - z)

    def z_out(s):
        return remote(fz.at[s], fz.at[s], z3_s.at[s], z3_r.at[s], me, at.zp)

    def keep(s):
        return pltpu.make_async_copy(fz.at[s], total.at[s], keep_l.at[s])

    for group in groups:
        for q in (3, 1, 2, 0):
            to_twin(q, group).start()

    def v_tok(d):
        return remote(vec.at[(me + d) % n_tok], vt.at[d], t_s.at[d], t_r.at[d], (me + d) % n_tok, z)

    def v_rep(i, src):
        return remote(src, vb.at[i], v_s.at[i], v_r.at[i], me, at.zp if i == 0 else (z + 2) % n_rep)

    for d in range(1, n_tok):
        v_tok(d).start()

    def join(q, s):
        return a[q, s] + tw[q, s]

    def first(s, send):
        a[3, s] = join(3, s)
        send(s).start()

    def plain(q, s, send):
        a[q, s] = join(q, s)
        send(s).start()

    def joined(q, s, arrived, send):
        arrived(s).wait_recv()
        a[q, s] = join(q, s) + rd[s]
        send(s).start()

    inner = (z == 1) | (z == 2)
    outer = (z == 0) | (z == 3)

    def own(s):
        to_x(s).wait_recv()
        to_y(s).wait_recv()
        o[s] = join(0, s) + (rx[s] + ry[s])
        pl.when(outer)(lambda: z_in(s).start())

    def middle(s):
        @pl.when(inner)
        def _():
            z_in(s).wait_recv()
            pz[s] = o[s] + rz1[s]
            z_swap(s).start()

    def last(s):
        @pl.when(inner)
        def _():
            z_swap(s).wait_recv()
            fz[s] = pz[s] + rz2[s]
            z_out(s).start()
            keep(s).start()

    def taken(s):
        @pl.when(outer)
        def _():
            z_out(s).wait_recv()
            keep(s).start()

    def pick_rows(i):
        ts = pl.ds(pl.multiple_of(i * 256, 256), 256)
        hit = lax.broadcasted_iota(I32, (SD * cap, 256), 0) == slot_of[:, ts]
        picked = jnp.where(hit, 1.0, 0.0).astype(BF)
        outs = jnp.concatenate([out_v[k, 0:cap, :] for k in range(SD)], axis=0)
        ings = jnp.concatenate([ing_v[k] for k in range(SD)], axis=0)
        both = mm(picked, jnp.concatenate([outs, ings], axis=1), TN)
        output[ts, :] = both[:, 0:D].astype(BF)
        input_grad[ts, :] = both[:, D:].astype(BF)
        line = jnp.concatenate([out_v[k, cap : cap + 8, 0:cap] for k in range(SD)], axis=1)
        entropy[:, ts] = mm(line, picked)[0:1].astype(BF)

    for q in (3, 1, 2, 0):
        load(q).wait()

    def steps(i, lag, more):
        s = i - lag
        by_x = (s % 2 == 0) & (s < 2 * split)
        live = (s >= 0) & (s < count)
        pl.when(live & by_x)(lambda: more(s, True))
        pl.when(live & jnp.logical_not(by_x))(lambda: more(s, False))

    def steps_of(i, lag, more):
        pl.when((i >= lag) & (i < count + lag))(lambda: more(i - lag))

    def round_of(i):
        for group in groups:

            @pl.when(i == group[1])
            def _(group=group):
                to_twin(3, group).wait_recv()

            @pl.when(i == group[1] + 1)
            def _(group=group):
                to_twin(1, group).wait_recv()
                to_twin(2, group).wait_recv()

            @pl.when(i == group[1] + 6)
            def _(group=group):
                to_twin(0, group).wait_recv()

        steps(i, 0, lambda s, by_x: first(s, d_x if by_x else d_y))
        steps(i, 1, lambda s, by_x: plain(1, s, to_x) if by_x else plain(2, s, to_y))
        steps(i, 3, lambda s, by_x: joined(2, s, d_x, to_y) if by_x else joined(1, s, d_y, to_x))
        steps_of(i, 6, own)
        steps_of(i, 8, middle)
        steps_of(i, 10, last)
        steps_of(i, 12, taken)

    loop(3, round_of)
    for copy in rows_in:
        copy.wait()
    slots_here, _ = route_slots(order[...], me % SD, cap)
    slot_of[...] = slots_here

    v_sum = vec[me]
    for d in range(1, n_tok):
        v_tok(d).wait()
        v_sum = v_sum + vt[d]
    va[...] = v_sum
    v_rep(0, va).start()

    def four_rounds(i):
        loop(4, lambda j: round_of(3 + 4 * i + j))
        pick_rows(i)

    four_rounds(0)
    v_rep(0, va).wait()
    vc[...] = va[...] + vb[0]
    v_rep(1, vc).start()
    loop(3, lambda i: four_rounds(1 + i))
    loop(count + 12 - 19, lambda i: round_of(19 + i))
    v_rep(1, vc).wait()
    vec_out[...] = vc[...] + vb[1]

    for group in groups:
        for q in range(4):
            to_twin(q, group).wait_send()

    def sent(s):
        d_y(s).wait_send()
        to_x(s).wait_send()
        to_y(s).wait_send()
        keep(s).wait()

    loop(count, sent)

    @pl.when(outer)
    def _():
        loop(count, lambda s: z_in(s).wait_send())

    @pl.when(inner)
    def _():
        def back(s):
            z_swap(s).wait_send()
            z_out(s).wait_send()

        loop(count, back)


def reduce_all(cap, grads, shares, order, outs, ings, count):
    dma = pltpu.SemaphoreType.DMA
    count = count * BLK // PART
    part = pltpu.VMEM((count, PART, D), BF)
    whole = pltpu.VMEM((4, count, PART, D), BF)
    line = pltpu.VMEM((16, 128), F32)
    rows = jax.ShapeDtypeStruct((ROWS, D), BF)
    total, vec, output, input_grad, entropy = pl.pallas_call(
        functools.partial(reduce_kernel, cap, count, count // 2),
        out_shape=(
            jax.ShapeDtypeStruct((count, PART, D), BF),
            jax.ShapeDtypeStruct((16, 128), F32),
            rows,
            rows,
            jax.ShapeDtypeStruct((1, ROWS), BF),
        ),
        in_specs=[ANY, VMEM, VMEM] + [ANY] * (2 * SD),
        out_specs=(ANY,) + (VMEM,) * 4,
        scratch_shapes=[
            pltpu.VMEM((SD, cap + META, D), BF),
            pltpu.VMEM((SD, cap, D), BF),
            pltpu.VMEM((1, ROWS), I32),
            whole,
            whole,
        ]
        + [part] * 8
        + [pltpu.VMEM((8, 16, 128), F32), line, pltpu.VMEM((2, 16, 128), F32), line]
        + [dma((4,)), dma((count,))]
        + [dma((4, 4))] * 2
        + [dma((count,))] * 12
        + [dma((8,))] * 2
        + [dma((2,))] * 2
        + [dma((2, SD))],
        compiler_params=pltpu.CompilerParams(collective_id=1, has_side_effects=True, vmem_limit_bytes=VMEM_LIMIT),
        cost_estimate=pl.CostEstimate(flops=4 * ROWS * ROWS * D, bytes_accessed=64 << 20, transcendentals=0),
        name="reduce",
    )(grads.reshape(-1, PART, D), shares, order, *outs, *ings)
    return total.reshape(-1, BLK, D), vec, output, input_grad, entropy


V_BQ, V_BV, V_BO, V_BD, V_G1, V_C1, V_G2, V_C2 = range(8)


def inverse(x):
    r = pl.reciprocal(x, approx=True)
    return r * (2.0 - x * r)


def erf_parts(v):
    t = inverse(1.0 + (0.3275911 / math.sqrt(2.0)) * jnp.abs(v))
    e = jnp.exp2((v * v) * (-0.5 / math.log(2.0)))
    poly = 0.5 * 1.061405429
    for c in (-1.453152027, 1.421413741, -0.284496736, 0.254829592):
        poly = poly * t + 0.5 * c
    tail = poly * (t * e)
    return jnp.where(v >= 0.0, 1.0 - tail, tail), e


def lane_sum(x):
    return jnp.sum(x, axis=1, keepdims=True)


def gelu_parts(v):
    phi, e = erf_parts(v)
    return v * phi, phi + v * (e * (1.0 / math.sqrt(2.0 * math.pi)))


def weight_copies(pos, slots, w, sem, first):
    def copy(b):
        return pltpu.make_async_copy(slots.at[pos[first + b]], w.at[pl.ds(b * BLK, BLK)], sem)

    n = w.shape[0] // BLK
    return (lambda: loop(n, lambda b: copy(b).start())), (lambda: loop(n, lambda b: copy(b).wait()))


def halves_of_heads():
    lane = lax.broadcasted_iota(I32, (1, PW), 1)
    m0 = jnp.where(lane < HD, 1.0, 0.0).astype(BF)
    m1 = jnp.where(lane < HD, 0.0, 1.0).astype(BF)
    return lambda pair: jnp.concatenate([pair * m0, pair * m1], axis=0)


def tile_rows(t):
    return pl.ds(pl.multiple_of(t * TM, TM), TM)


def forward_kernel(
    cap,
    pos,
    slots,
    vecs,
    b_u,
    x_h,
    meta,
    back_0,
    back_1,
    back_2,
    back_3,
    heads_h,
    act_h,
    hid_h,
    q_h,
    k_h,
    v_h,
    p_h,
    slope_h,
    n1_h,
    n2_h,
    rs1_h,
    rs2_h,
    wqkv,
    wo,
    wu,
    wd,
    x_c,
    heads,
    act,
    hid,
    q,
    k,
    v,
    p_all,
    slope,
    n1,
    n2,
    rs1,
    rs2,
    out_c,
    ent,
    hid_t,
    w_sem,
    x_sem,
    o_sem,
):
    inv = 1.0 / math.sqrt(HD)
    get_x = pltpu.make_async_copy(x_h, x_c, x_sem)
    get_x.start()
    weights = [
        weight_copies(pos, slots, w, w_sem.at[i], first)
        for i, (w, first) in enumerate(((wqkv, 0), (wo, 24), (wu, 32), (wd, 64)))
    ]
    for start, _ in weights:
        start()
    get_x.wait()
    apart = halves_of_heads()

    def vec(i):
        return vecs[i : i + 1, :]

    saved = (
        (heads, heads_h),
        (act, act_h),
        (hid, hid_h),
        (q, q_h),
        (k, k_h),
        (v, v_h),
        (slope, slope_h),
        (n1, n1_h),
        (n2, n2_h),
        (rs1, rs1_h),
        (rs2, rs2_h),
    )

    def save(t, i):
        src, dst = saved[i]
        return pltpu.make_async_copy(src.at[tile_rows(t)], dst.at[tile_rows(t)], o_sem.at[i])

    def save_p(t):
        n = TM // CL
        cs = pl.ds(t * n, n)
        return pltpu.make_async_copy(p_all.at[cs], p_h.at[cs], o_sem.at[len(saved)])

    def normal(r, n, rs, rows):
        c = r - lane_sum(r) * (1.0 / D)
        scale = lax.rsqrt(lane_sum(c * c) * (1.0 / D) + norm_epsilon)
        rs[rows, :] = jnp.broadcast_to(scale, (TM, 128))
        n[rows, :] = c * scale

    def tile(t):
        rows = tile_rows(t)
        first = t == 0
        pl.when(first)(weights[0][1])
        x = x_c[rows, :]
        q[rows, :] = ((mm(x, wqkv[0:D, :]) + vec(V_BQ)).astype(BF).astype(F32) * inv).astype(BF)
        k[rows, :] = mm(x, wqkv[D : 2 * D, :]).astype(BF)
        v[rows, :] = (mm(x, wqkv[2 * D :, :]) + vec(V_BV)).astype(BF)

        def attend(c):
            groups = [pl.ds(pl.multiple_of(t * TM + (FWD_AT * c + i) * CL, CL), CL) for i in range(FWD_AT)]
            pairs = [(i, p, slice(p * PW, (p + 1) * PW)) for i in range(FWD_AT) for p in range(PAIRS)]
            scores = [mm(apart(k[groups[i], ps]), q[groups[i], ps], NT) for i, _, ps in pairs]
            total = [jnp.zeros((1, CL), F32)] * FWD_AT
            probs = []
            for (i, _, _), both in zip(pairs, scores):
                halves = []
                for h in range(2):
                    sh = both[h * CL : (h + 1) * CL]
                    sh = sh - jnp.max(sh, axis=0, keepdims=True)
                    e = jnp.exp(sh)
                    tot = jnp.sum(e, axis=0, keepdims=True)
                    r = 1.0 / tot
                    total[i] += jnp.log(tot) - jnp.sum(e * sh, axis=0, keepdims=True) * r
                    halves.append((e * r).astype(BF))
                probs.append(jnp.concatenate(halves, axis=0))
            mixed = [mm(w, apart(v[groups[i], ps]), TN).astype(BF) for (i, _, ps), w in zip(pairs, probs)]
            for (i, p, ps), w, o in zip(pairs, probs, mixed):
                p_all[t * (TM // CL) + FWD_AT * c + i, p] = w
                heads[groups[i], ps] = o
            for i in range(FWD_AT):
                ent[:, groups[i]] = jnp.broadcast_to(total[i] * (1.0 / HEADS), (8, CL))

        loop(TM // CL // FWD_AT, attend)
        for i in (0, 3, 4, 5):
            save(t, i).start()
        save_p(t).start()
        pl.when(first)(weights[1][1])
        normal(x_c[rows, :].astype(F32) + mm(heads[rows, :], wo[...]) + vec(V_BO), n1, rs1, rows)
        hidden = n1[rows, :] * vec(V_G1) + vec(V_C1)
        hid[rows, :] = hidden.astype(BF)
        hid_t[...] = hidden
        pl.when(first)(weights[2][1])

        def widen(f):
            parts = [pl.ds(pl.multiple_of((2 * f + i) * FC, FC), FC) for i in range(2)]
            ups = [mm(hid[rows, :], wu[fs, :], NT) for fs in parts]
            for fs, up in zip(parts, ups):
                g, g_slope = gelu_parts(up + b_u[:, fs])
                act[rows, fs] = g.astype(BF)
                slope[rows, fs] = g_slope.astype(BF)

        loop(FF // FC // 2, widen)
        for i in (1, 2, 6, 7, 9):
            save(t, i).start()
        pl.when(first)(weights[3][1])
        normal(hid_t[...] + mm(act[rows, :], wd[...]) + vec(V_BD), n2, rs2, rows)
        out_c[rows, :] = (n2[rows, :] * vec(V_G2) + vec(V_C2)).astype(BF)
        for i in (8, 10):
            save(t, i).start()

    loop(ROWS // TM, tile)

    for j, back in enumerate((back_0, back_1, back_2, back_3)):
        own = seat_part(meta, j, cap)
        back[0:cap, :] = mm(own, out_c[...]).astype(BF)
        line = mm(ent[...].astype(BF), own, NT)
        back[cap:, :] = jnp.concatenate([line, line], axis=1)[0:1].astype(BF) * jnp.ones((META, 1), BF)

    def saved_all(t):
        for i in range(len(saved)):
            save(t, i).wait()
        save_p(t).wait()

    loop(ROWS // TM, saved_all)


def shape_of(kind, *shape):
    return jax.ShapeDtypeStruct(shape, kind)


def saved_shapes():
    rows, wide = ((ROWS, D), BF), ((ROWS, FF), BF)
    probs = ((ROWS // CL, PAIRS, 2 * CL, CL), BF)
    full, thin = ((ROWS, D), F32), ((ROWS, 128), F32)
    return rows, wide, probs, full, thin


def forward(cap, positions, slots, vecs, b_u, x_c, meta):
    rows, wide, probs, full, thin = saved_shapes()
    kept = (rows, wide, rows, rows, rows, rows, probs, wide, full, full, thin, thin)
    dma = pltpu.SemaphoreType.DMA
    return pl.pallas_call(
        functools.partial(forward_kernel, cap),
        out_shape=(shape_of(BF, cap + META, D),) * SD + tuple(shape_of(kind, *shape) for shape, kind in kept),
        in_specs=[SMEM, ANY, VMEM, VMEM, ANY, VMEM],
        out_specs=(VMEM,) * SD + (ANY,) * len(kept),
        scratch_shapes=[
            pltpu.VMEM((3 * D, D), BF),
            pltpu.VMEM((D, D), BF),
            pltpu.VMEM((FF, D), BF),
            pltpu.VMEM((FF, D), BF),
            pltpu.VMEM(*rows),
        ]
        + [pltpu.VMEM(*a) for a in kept]
        + [
            pltpu.VMEM(*rows),
            pltpu.VMEM((8, ROWS), F32),
            pltpu.VMEM((TM, D), F32),
            dma((4,)),
            dma,
            dma((12,)),
        ],
        compiler_params=pltpu.CompilerParams(vmem_limit_bytes=VMEM_LIMIT),
        cost_estimate=pl.CostEstimate(flops=2 * ROWS * WROWS * D, bytes_accessed=64 << 20, transcendentals=0),
        name="forward",
    )(positions, slots, vecs, b_u, x_c, meta)


def backward_kernel(
    cap,
    pos,
    slots,
    vecs,
    meta,
    cot_0,
    cot_1,
    cot_2,
    cot_3,
    q_h,
    k_h,
    v_h,
    p_h,
    slope_h,
    n1_h,
    n2_h,
    rs1_h,
    rs2_h,
    back_0,
    back_1,
    back_2,
    back_3,
    shares,
    d_up_h,
    d_q_h,
    d_k_h,
    d_v_h,
    d_proj_h,
    d_br_h,
    wqkv,
    wo,
    wu,
    wd,
    blocks,
    q,
    k,
    v,
    p_all,
    d_up,
    n1,
    n2,
    rs1,
    rs2,
    d_proj,
    d_br,
    ing_c,
    d_h_t,
    gvec,
    g_bu,
    w_sem,
    c_sem,
    i_sem,
    o_sem,
):
    inv = 1.0 / math.sqrt(HD)
    get_c = [
        pltpu.make_async_copy(cot, blocks.at[j], c_sem.at[j]) for j, cot in enumerate((cot_0, cot_1, cot_2, cot_3))
    ]
    for copy in get_c:
        copy.start()
    fetch = [
        pltpu.make_async_copy(src, dst, i_sem.at[i])
        for i, (src, dst) in enumerate(
            (
                (n2_h, n2),
                (rs2_h, rs2),
                (slope_h, d_up),
                (n1_h, n1),
                (rs1_h, rs1),
                (v_h, v),
                (p_h, p_all),
                (k_h, k),
                (q_h, q),
            )
        )
    ]
    weights = [
        weight_copies(pos, slots, w, w_sem.at[i], first)
        for i, (w, first) in enumerate(((wd, 64), (wu, 32), (wo, 24), (wqkv, 0)))
    ]
    fetch[0].start()
    fetch[1].start()
    weights[0][0]()
    fetch[2].start()
    weights[1][0]()
    fetch[3].start()
    fetch[4].start()
    weights[2][0]()
    for i in range(5, 9):
        fetch[i].start()
    weights[3][0]()
    gvec[...] = jnp.zeros_like(gvec)
    g_bu[...] = jnp.zeros_like(g_bu)
    shares[...] = jnp.zeros_like(shares)
    for copy in get_c:
        copy.wait()
    seat_rows(meta, blocks, cap, d_br)
    apart = halves_of_heads()

    def vec(i):
        return vecs[i : i + 1, :]

    def add_vec(i, value):
        gvec[i : i + 1, :] += jnp.sum(value, axis=0, keepdims=True)

    saved = ((d_up, d_up_h), (q, d_q_h), (k, d_k_h), (v, d_v_h), (d_proj, d_proj_h), (d_br, d_br_h))

    def save(t, i):
        src, dst = saved[i]
        return pltpu.make_async_copy(src.at[tile_rows(t)], dst.at[tile_rows(t)], o_sem.at[i])

    def norm_back(e, n, rs, gain, shift):
        add_vec(gain, e * n)
        add_vec(shift, e)
        eg = e * vec(gain)
        return rs * (eg - lane_sum(eg) * (1.0 / D) - n * (lane_sum(eg * n) * (1.0 / D)))

    def norm_two_back(t):
        rows = tile_rows(t)
        d_r2 = norm_back(d_br[rows, :].astype(F32), n2[rows, :], rs2[rows, 0:1], V_G2, V_C2)
        d_br[rows, :] = d_r2.astype(BF)
        add_vec(V_BD, d_br[rows, :].astype(F32))
        n2[rows, :] = d_r2

    def widen_back(t, columns):
        rows = tile_rows(t)
        parts = [pl.ds(pl.multiple_of(f * FC, FC), FC) for f in columns]
        ups = [mm(d_br[rows, :], wd[fs, :], NT) for fs in parts]

        def finish():
            for fs, up in zip(parts, ups):
                du = (up * d_up[rows, fs].astype(F32)).astype(BF)
                d_up[rows, fs] = du
                g_bu[:, fs] += jnp.sum(du.astype(F32), axis=0, keepdims=True)

        return finish

    def hidden_back(t):
        rows = tile_rows(t)
        return n2[rows, :] + mm(d_up[rows, :], wu[...])

    def norm_one_back(t, d_h):
        rows = tile_rows(t)
        d_r1 = norm_back(d_h, n1[rows, :], rs1[rows, 0:1], V_G1, V_C1)
        d_proj[rows, :] = d_r1.astype(BF)
        n2[rows, :] = d_r1
        add_vec(V_BO, d_proj[rows, :].astype(F32))

    def heads_back(t):
        rows = tile_rows(t)
        d_h_t[rows, :] = mm(d_proj[rows, :], wo[...], NT).astype(BF)

    def attend_back(clusters, meanwhile=lambda: None):
        pairs = [
            (c, p, pl.ds(pl.multiple_of(c * CL, CL), CL), slice(p * PW, (p + 1) * PW))
            for c in clusters
            for p in range(PAIRS)
        ]
        probs = [p_all[c, p] for c, p, _, _ in pairs]
        d_heads = [d_h_t[gr, ps] for _, _, gr, ps in pairs]
        d_probs = [mm(apart(v[gr, ps]), dh, NT) for (_, _, gr, ps), dh in zip(pairs, d_heads)]
        d_values = [
            mm(jnp.concatenate([w[0:CL], w[CL:]], axis=1), apart(dh)).astype(BF) for w, dh in zip(probs, d_heads)
        ]
        finish = meanwhile()
        d_scores = []
        for w, dw in zip(probs, d_probs):
            halves = []
            for h in range(2):
                wh = w[h * CL : (h + 1) * CL].astype(F32)
                dwh = dw[h * CL : (h + 1) * CL]
                halves.append((wh * (dwh - jnp.sum(dwh * wh, axis=0, keepdims=True))).astype(BF))
            d_scores.append(halves)
        d_keys = [
            mm(jnp.concatenate(ds, axis=1), apart(q[gr, ps])).astype(BF) for (_, _, gr, ps), ds in zip(pairs, d_scores)
        ]
        d_queries = [
            (mm(jnp.concatenate(ds, axis=0), apart(k[gr, ps]), TN) * inv).astype(BF)
            for (_, _, gr, ps), ds in zip(pairs, d_scores)
        ]
        if finish is not None:
            finish()
        for (_, _, gr, ps), dq, dk, dv in zip(pairs, d_queries, d_keys, d_values):
            q[gr, ps] = dq
            k[gr, ps] = dk
            v[gr, ps] = dv

    def rows_back(t):
        rows = tile_rows(t)
        return (
            mm(q[rows, :], wqkv[0:D, :], NT)
            + mm(k[rows, :], wqkv[D : 2 * D, :], NT)
            + mm(v[rows, :], wqkv[2 * D :, :], NT)
        )

    def rows_done(t, d_x):
        rows = tile_rows(t)
        add_vec(V_BQ, q[rows, :].astype(F32))
        add_vec(V_BV, v[rows, :].astype(F32))
        ing_c[rows, :] = (n2[rows, :] + d_x.astype(BF).astype(F32)).astype(BF)

    def save_all(t, which):
        for i in which:
            save(t, i).start()

    per = TM // CL
    fetch[0].wait()
    fetch[1].wait()
    norm_two_back(0)
    norm_two_back(1)
    weights[0][1]()
    fetch[2].wait()
    loop(FF // FC // 2, lambda f: widen_back(0, [2 * f, 2 * f + 1])())
    save_all(0, (0, 5))
    weights[1][1]()
    fetch[3].wait()
    fetch[4].wait()
    norm_one_back(0, hidden_back(0))
    weights[2][1]()
    for i in range(5, 9):
        fetch[i].wait()
    heads_back(0)
    save_all(0, (4,))
    loop(per, lambda c: attend_back([c], lambda: widen_back(1, [c])))
    save_all(0, (1, 2, 3))
    save_all(1, (0, 5))
    weights[3][1]()
    d_h = hidden_back(1)
    d_x = rows_back(0)
    norm_one_back(1, d_h)
    heads_back(1)
    rows_done(0, d_x)
    save_all(1, (4,))
    loop(per // BWD_AT, lambda c: attend_back([per + BWD_AT * c + i for i in range(BWD_AT)]))
    save_all(1, (1, 2, 3))
    rows_done(1, rows_back(1))

    for j, back in enumerate((back_0, back_1, back_2, back_3)):
        back[...] = mm(seat_part(meta, j, cap), ing_c[...]).astype(BF)

    for chunk in range(72):
        row, lane = chunk // 6, chunk % 6 * 128
        if row < 8:
            part = gvec[row : row + 1, lane : lane + 128]
        else:
            lane += (row - 8) * D
            part = g_bu[:, lane : lane + 128]
        shares[chunk // 9, chunk % 9 : chunk % 9 + 1, :] = part

    def saved_all(t):
        for i in range(len(saved)):
            save(t, i).wait()

    loop(ROWS // TM, saved_all)


def backward(cap, positions, slots, vecs, meta, cots, saved):
    rows, wide, probs, full, thin = saved_shapes()
    dma = pltpu.SemaphoreType.DMA
    grads = (wide, rows, rows, rows, rows, rows)
    return pl.pallas_call(
        functools.partial(backward_kernel, cap),
        out_shape=(shape_of(BF, cap, D),) * SD
        + (shape_of(F32, 8, 16, 128),)
        + tuple(shape_of(kind, *shape) for shape, kind in grads),
        in_specs=[SMEM, ANY, VMEM, VMEM] + [ANY] * (SD + 9),
        out_specs=(VMEM,) * (SD + 1) + (ANY,) * len(grads),
        scratch_shapes=[
            pltpu.VMEM((3 * D, D), BF),
            pltpu.VMEM((D, D), BF),
            pltpu.VMEM((FF, D), BF),
            pltpu.VMEM((FF, D), BF),
            pltpu.VMEM((SD, cap, D), BF),
        ]
        + [pltpu.VMEM(*a) for a in (rows, rows, rows, probs, wide, full, full, thin, thin, rows, rows, rows)]
        + [
            pltpu.VMEM(*rows),
            pltpu.VMEM((8, D), F32),
            pltpu.VMEM((1, FF), F32),
            dma((4,)),
            dma((4,)),
            dma((9,)),
            dma((6,)),
        ],
        compiler_params=pltpu.CompilerParams(vmem_limit_bytes=VMEM_LIMIT),
        cost_estimate=pl.CostEstimate(flops=2 * ROWS * WROWS * D, bytes_accessed=64 << 20, transcendentals=0),
        name="backward",
    )(positions, slots, vecs, meta, *cots, *saved)


WC = 8 * BLK


def weight_kernel(
    pos,
    x_h,
    heads_h,
    act_h,
    d_up_h,
    d_q_h,
    d_k_h,
    d_v_h,
    d_proj_h,
    hid_h,
    d_br_h,
    grads,
    x_c,
    heads,
    act,
    d_up,
    d_q,
    d_k,
    d_v,
    d_proj,
    hid,
    d_br,
    stage,
    i_sem,
    g_sem,
):
    refs = (
        (x_h, x_c),
        (d_q_h, d_q),
        (d_k_h, d_k),
        (d_v_h, d_v),
        (heads_h, heads),
        (d_proj_h, d_proj),
        (hid_h, hid),
        (d_up_h, d_up),
        (d_br_h, d_br),
        (act_h, act),
    )
    fetch = [pltpu.make_async_copy(src, dst, i_sem.at[i]) for i, (src, dst) in enumerate(refs)]
    for copy in fetch:
        copy.start()

    per = WC // BLK

    def g_copy(chunk, j, at):
        return pltpu.make_async_copy(
            stage.at[at, pl.ds(j * BLK, BLK)], grads.at[pos[chunk * per + j]], g_sem.at[at]
        )

    def put(chunk, left, right):
        at = lax.rem(chunk, 2)

        @pl.when(chunk >= 2)
        def _():
            for j in range(per):
                g_copy(chunk - 2, j, at).wait()

        stage[at] = mm(left, right, TN).astype(BF)
        for j in range(per):
            g_copy(chunk, j, at).start()

    first = 0
    for left, right, needs in (
        (x_c, d_q, (0, 1)),
        (x_c, d_k, (2,)),
        (x_c, d_v, (3,)),
        (heads, d_proj, (4, 5)),
        (d_up, hid, (6, 7)),
        (act, d_br, (8, 9)),
    ):
        for i in needs:
            fetch[i].wait()

        def body(j, left=left, right=right, first=first):
            put(first + j, left[:, pl.ds(pl.multiple_of(j * WC, WC), WC)], right[...])

        loop(left.shape[1] // WC, body)
        first += left.shape[1] // WC
    for chunk in (first - 2, first - 1):
        for j in range(per):
            g_copy(chunk, j, chunk % 2).wait()


def weight_grads_of(total_slots, positions, x_c, saved):
    r_v, w_v = pltpu.VMEM((ROWS, D), BF), pltpu.VMEM((ROWS, FF), BF)
    return pl.pallas_call(
        weight_kernel,
        out_shape=jax.ShapeDtypeStruct((total_slots, BLK, D), BF),
        in_specs=[SMEM] + [ANY] * 10,
        out_specs=ANY,
        scratch_shapes=[r_v, r_v, w_v, w_v]
        + [r_v] * 6
        + [
            pltpu.VMEM((2, WC, D), BF),
            pltpu.SemaphoreType.DMA((10,)),
            pltpu.SemaphoreType.DMA((2,)),
        ],
        compiler_params=pltpu.CompilerParams(vmem_limit_bytes=VMEM_LIMIT),
        cost_estimate=pl.CostEstimate(flops=2 * ROWS * WROWS * D, bytes_accessed=40 << 20, transcendentals=0),
        name="weight_grads",
    )(positions, x_c, *saved)


def finish_kernel(
    used,
    total,
    master,
    first,
    second,
    v_grad,
    v_master,
    v_first,
    v_second,
    line,
    counts,
    out_h,
    ing_h,
    grad_new,
    first_new,
    second_new,
    master_new,
    low_new,
    v_grad_new,
    v_first_new,
    v_second_new,
    v_master_new,
    v_low_new,
    entropy,
    occupancy,
    output,
    input_grad,
    sem,
):
    i = pl.program_id(0)
    moves = [pltpu.make_async_copy(src, dst, sem.at[n]) for n, (src, dst) in enumerate(((out_h, output), (ing_h, input_grad)))]

    @pl.when(i == 0)
    def _():
        for move in moves:
            move.start()
        entropy[...] = line[...].reshape(ROWS)
        occupancy[...] = counts[...]
        length = v_master.shape[0]
        for n in range(-(-length // 128)):
            part = slice(n * 128, min((n + 1) * 128, length))
            g = v_grad[n : n + 1, 0 : part.stop - part.start].reshape(part.stop - part.start)
            m, v, w = adam_update(g, v_master[part], v_first[part], v_second[part], rate_vector)
            v_grad_new[part] = g
            v_first_new[part] = m
            v_second_new[part] = v
            v_master_new[part] = w
        v_low_new[...] = v_master_new[...].astype(BF)

    g = jnp.where(used[i] > 0, total[...].astype(F32), 0.0)
    m, v, w = adam_update(g, master[...], first[...], second[...], rate_matrix)
    grad_new[...] = g
    first_new[...] = m
    second_new[...] = v
    master_new[...] = w
    low_new[...] = w.astype(BF)

    @pl.when(i == pl.num_programs(0) - 1)
    def _():
        for move in moves:
            move.wait()


def finish(used, total, weights, v_grad, vectors, line, counts, out, ing):
    count = total.shape[0]
    slot = pl.BlockSpec((1, BLK, D), lambda i: (i, 0, 0))

    def whole(array):
        return pl.BlockSpec(array.shape, lambda i: (0,) * array.ndim)

    f32_slots, f32_vector = shape_of(F32, count, BLK, D), shape_of(F32, *vectors[0].shape)
    shapes = (
        (f32_slots,) * 4
        + (shape_of(BF, count, BLK, D),)
        + (f32_vector,) * 4
        + (shape_of(BF, *vectors[0].shape), shape_of(BF, ROWS), shape_of(I32, *counts.shape))
        + (shape_of(BF, ROWS, D),) * 2
    )
    return pl.pallas_call(
        finish_kernel,
        grid=(count,),
        out_shape=shapes,
        in_specs=[SMEM] + [slot] * 4 + [whole(a) for a in (v_grad, *vectors, line, counts)] + [ANY] * 2,
        out_specs=(slot,) * 5 + tuple(whole(a) for a in shapes[5:12]) + (ANY,) * 2,
        scratch_shapes=[pltpu.SemaphoreType.DMA((2,))],
        compiler_params=pltpu.CompilerParams(vmem_limit_bytes=VMEM_LIMIT),
        name="finish",
    )(used, total, *weights, v_grad, *vectors, line, counts, out, ing)


def local(
    tokens,
    cotangent,
    cluster_order,
    block_owner,
    master_slots,
    moment_one,
    moment_two,
    vector_master,
    vector_moment_one,
    vector_moment_two,
):
    tok_count = lax.axis_size("tok")
    tok_index = lax.axis_index("tok")
    slot_count = master_slots.shape[0]
    cap = tok_count // SD * (max(1, CPS // tok_count) * 3 * CL // (2 * SD))
    total_slots = tok_count * slot_count
    order = cluster_order.reshape(1, ROWS)

    block = jax.ShapeDtypeStruct((SD, cap, D), BF)
    meta_shape = jax.ShapeDtypeStruct((SD, META, D), BF)
    row_block = jax.ShapeDtypeStruct((ROWS, D), BF)
    four_planes = tok_count == 8 and lax.axis_size("rep") == 4
    if four_planes:
        slots_low, x_c, *cots, recv_meta, vecs, b_u, occupancy, positions = gather_all(
            cap, tokens, cotangent, order, master_slots, vector_master, block_owner
        )
        positions = positions.reshape(NBLK)
        slots_low = slots_low.reshape(total_slots, BLK, D)
    else:
        positions = slot_positions(block_owner, slot_count)
        slots_low = lax.all_gather(master_slots.astype(BF), "tok", axis=0, tiled=True)
        vectors = lax.all_gather(vector_master.astype(BF), "tok", axis=0, tiled=True).astype(F32)
        vecs, b_u = vectors[: 8 * D].reshape(8, D), vectors[8 * D :].reshape(1, FF)
        cluster = tok_index // SD * CPS + cluster_order // CL
        target = cluster % tok_count
        chosen = target[None, :] == jnp.arange(tok_count, dtype=jnp.int32)[:, None]
        sent_counts = jnp.sum(chosen.astype(F32), axis=1)
        own_row = (jnp.arange(tok_count, dtype=jnp.int32) == tok_index).astype(F32)
        occupancy = lax.psum(own_row[:, None] * sent_counts[None, :], ("tok", "rep")).astype(jnp.int32)
        send_x, send_c, meta = pl.pallas_call(
            functools.partial(send_kernel, cap),
            out_shape=(block, block, meta_shape),
            in_specs=[VMEM] * 3,
            out_specs=(VMEM,) * 3,
            compiler_params=pltpu.CompilerParams(vmem_limit_bytes=VMEM_LIMIT),
            name="send_rows",
        )(tokens, cotangent, order)
        recv_x, recv_meta = (jnp.stack(swap_blocks(b)) for b in (send_x, meta))
        x_c = pl.pallas_call(
            functools.partial(seat_kernel, cap),
            out_shape=row_block,
            in_specs=[VMEM] * 2,
            out_specs=VMEM,
            compiler_params=pltpu.CompilerParams(vmem_limit_bytes=VMEM_LIMIT),
            name="seat_rows",
        )(recv_x, recv_meta)
        cots = [send_c[k] for k in range(SD)]

    cots = swap_blocks(cots)
    *out_blocks, heads, act, hid, q, k, v, p, slope, n1, n2, rs1, rs2 = forward(
        cap, positions, slots_low, vecs, b_u, x_c, recv_meta
    )
    out_blocks = swap_blocks(out_blocks)
    *ing_blocks, shares, d_up, d_q, d_k, d_v, d_proj, d_br = backward(
        cap, positions, slots_low, vecs, recv_meta, cots, (q, k, v, p, slope, n1, n2, rs1, rs2)
    )
    ing_blocks = swap_blocks(ing_blocks)
    grads = weight_grads_of(
        total_slots, positions, x_c, (heads, act, d_up, d_q, d_k, d_v, d_proj, hid, d_br)
    )
    if four_planes:
        total, vec_owned, output, input_grad, entropy = reduce_all(
            cap, grads, shares, order, out_blocks, ing_blocks, slot_count
        )
    else:
        total = lax.psum(lax.psum_scatter(grads, "tok", scatter_dimension=0, tiled=True), "rep")
        grad_vector = shares[:, 0:9].reshape(-1)
        vec_owned = lax.psum(lax.psum_scatter(grad_vector, "tok", scatter_dimension=0, tiled=True), "rep")
        vec_owned = jnp.pad(vec_owned, (0, -vec_owned.shape[0] % 128)).reshape(-1, 128)
        output, input_grad, entropy = pl.pallas_call(
            functools.partial(return_kernel, cap),
            out_shape=(row_block, row_block, jax.ShapeDtypeStruct((1, ROWS), BF)),
            in_specs=[VMEM] * (2 * SD + 1),
            out_specs=(VMEM,) * 3,
            compiler_params=pltpu.CompilerParams(vmem_limit_bytes=VMEM_LIMIT),
            name="return_rows",
        )(order, *out_blocks, *ing_blocks)

    used = jnp.any(
        positions[None, :] == (tok_index * slot_count + jnp.arange(slot_count, dtype=I32))[:, None], axis=1
    )
    (
        owned_grad,
        first_new,
        second_new,
        master_new,
        low_new,
        vec_owned,
        vec_first,
        vec_second,
        vec_new,
        vec_low_new,
        row_entropy,
        occupancy,
        output,
        input_grad,
    ) = finish(
        used.astype(I32),
        total,
        (master_slots, moment_one, moment_two),
        vec_owned,
        (vector_master, vector_moment_one, vector_moment_two),
        entropy,
        occupancy,
        output,
        input_grad,
    )
    return (
        output,
        input_grad,
        owned_grad,
        first_new,
        second_new,
        master_new,
        low_new,
        vec_owned,
        vec_first,
        vec_second,
        vec_new,
        vec_low_new,
        row_entropy,
        occupancy,
    )


def solution(mesh):
    placed = (
        P(("rep", "tok"), None),
        P(("rep", "tok"), None),
        P(("rep", "tok")),
        P(),
        P("tok", None, None),
        P("tok", None, None),
        P("tok", None, None),
        P("tok"),
        P("tok"),
        P("tok"),
    )
    return jax.shard_map(
        local,
        mesh=mesh,
        in_specs=placed,
        out_specs=(
            P(("rep", "tok"), None),
            P(("rep", "tok"), None),
            P("tok", None, None),
            P("tok", None, None),
            P("tok", None, None),
            P("tok", None, None),
            P("tok", None, None),
            P("tok"),
            P("tok"),
            P("tok"),
            P("tok"),
            P("tok"),
            P(("rep", "tok")),
            P(),
        ),
        check_vma=False,
    )
```

```python
import functools
import math

import jax
import jax.numpy as jnp
from jax import lax
from jax.experimental import pallas as pl
from jax.experimental.pallas import tpu as pltpu
from jax.sharding import PartitionSpec as P

D = 768
HEADS = 12
HD = 64
FF = 3072
SD = 4
CL = 128
NBLK = 96
STEP = 10
CPS = 32
WROWS = 9216
BLK = 96
ROWS = 1024
PAIRS = HEADS // 2
PW = 2 * HD
TM = 512
PART = 48
META = 16
VMEM_LIMIT = 63 << 20
FC = 768
FWD_AT = 4
BWD_AT = 2

norm_epsilon = 1e-06
beta_first = 0.9
beta_second = 0.999
adam_epsilon = 1e-08
weight_decay = 0.01
rate_matrix = 0.02
rate_vector = 0.2

BF = jnp.bfloat16
F32 = jnp.float32
I32 = jnp.int32

VMEM = pl.BlockSpec(memory_space=pltpu.VMEM)
SMEM = pl.BlockSpec(memory_space=pltpu.SMEM)
ANY = pl.BlockSpec(memory_space=pl.ANY)

NN = (((1,), (0,)), ((), ()))
NT = (((1,), (1,)), ((), ()))
TN = (((0,), (0,)), ((), ()))


def mm(a, b, dims=NN):
    return lax.dot_general(a, b, dims, preferred_element_type=F32)


def slot_positions(block_owner, slot_count):
    owners = block_owner[:, 0]
    blocks = owners.shape[0]
    shared = owners[:, None] == owners[None, :]
    before = (
        jnp.arange(blocks, dtype=jnp.int32)[None, :] < jnp.arange(blocks, dtype=jnp.int32)[:, None]
    )
    earlier = jnp.sum((shared & before).astype(jnp.int32), axis=1)
    return owners * slot_count + earlier


def adam_update(grad_now, weight_old, first_old, second_old, rate_step):
    first_new = beta_first * first_old + (1.0 - beta_first) * grad_now
    second_new = beta_second * second_old + (1.0 - beta_second) * grad_now * grad_now
    first_hat = first_new / (1.0 - beta_first**STEP)
    second_hat = second_new / (1.0 - beta_second**STEP)
    weight_new = weight_old - rate_step * (
        first_hat / (jnp.sqrt(second_hat) + adam_epsilon) + weight_decay * weight_old
    )
    return (first_new, second_new, weight_new)


def route_slots(order, seat, cap):
    cluster = order // CL
    rel = lax.rem(cluster, SD) ^ seat
    place = (cluster // SD) * CL + lax.rem(order, CL) + 1
    chosen = lax.broadcasted_iota(I32, (8, ROWS), 0) == rel
    chosen_low = jnp.where(chosen, 1.0, 0.0).astype(BF)
    before = lax.broadcasted_iota(I32, (ROWS, ROWS), 0) < lax.broadcasted_iota(I32, (ROWS, ROWS), 1)
    before_low = jnp.where(before, 1.0, 0.0).astype(BF)
    running = mm(chosen_low, before_low)
    rank = jnp.sum(jnp.where(chosen, running, 0.0), axis=0, keepdims=True).astype(I32)
    return rel * cap + rank, place


def slot_matrix(slots, at, cap):
    rows = lax.broadcasted_iota(I32, (cap, ROWS), 0) + at * cap
    return jnp.where(rows == slots, 1.0, 0.0).astype(BF)


def send_kernel(cap, tokens, cotangent, order, send_x, send_c, meta):
    seat = lax.rem(lax.axis_index("tok"), SD)
    slots, place = route_slots(order[...], seat, cap)
    digits = jnp.concatenate([place // CL, lax.rem(place, CL)] + [place * 0] * 6, axis=0).astype(F32).astype(BF)
    for at in range(SD):
        picked = slot_matrix(slots, at, cap)
        send_x[at] = mm(picked, tokens[...]).astype(BF)
        send_c[at] = mm(picked, cotangent[...]).astype(BF)
        coded = mm(digits, picked, NT)
        line = jnp.concatenate([coded[0:1], coded[1:2]], axis=1)
        meta[at] = jnp.broadcast_to(line, (META, D)).astype(BF)


def remote(src, dst, send_sem, recv_sem, tok, rep):
    return pltpu.make_async_remote_copy(
        src_ref=src,
        dst_ref=dst,
        send_sem=send_sem,
        recv_sem=recv_sem,
        device_id={"tok": tok, "rep": rep},
        device_id_type=pl.DeviceIdType.MESH,
    )


def loop(n, body):
    def run(i, c):
        body(i)
        return c

    lax.fori_loop(0, n, run, 0)


class Place:
    def __init__(self):
        self.me = me = lax.axis_index("tok")
        self.z = z = lax.axis_index("rep")
        core, x, y = me % 2, (me // 2) % 2, me // 4
        self.twin = me + 1 - 2 * core
        self.xn = me + 2 - 4 * x
        self.yn = me + 4 - 8 * y
        self.dn = self.xn + 4 - 8 * y
        self.side = z % 2
        self.zp = z + 1 - 2 * self.side

    def twin_of(self, tok):
        return tok + 1 - 2 * (tok % 2)

    def greet(self, peers):
        barrier = pltpu.get_barrier_semaphore()
        for tok, rep in peers:
            pl.semaphore_signal(
                barrier, inc=1, device_id={"tok": tok, "rep": rep}, device_id_type=pl.DeviceIdType.MESH
            )
        return lambda: pl.semaphore_wait(barrier, len(peers))


def seat_matrix(meta, first, rows, cap):
    hi = jnp.concatenate([meta[k, 0:8, 0:cap] for k in range(SD)], axis=1).astype(F32)[0:1]
    lo = jnp.concatenate([meta[k, 0:8, cap : 2 * cap] for k in range(SD)], axis=1).astype(F32)[0:1]
    at = (hi * CL + lo).astype(I32)
    seats = lax.broadcasted_iota(I32, (rows, SD * cap), 0) + (first + 1)
    return jnp.where(seats == at, 1.0, 0.0).astype(BF)


def seat_part(meta, k, cap):
    hi = meta[k, 0:8, 0:cap].astype(F32)[0:1]
    lo = meta[k, 0:8, cap : 2 * cap].astype(F32)[0:1]
    at = (hi * CL + lo).astype(I32)
    seats = lax.broadcasted_iota(I32, (ROWS, cap), 0) + 1
    return jnp.where(seats == at, 1.0, 0.0).astype(BF)


def seat_rows(meta, blocks, cap, to):
    def body(t):
        r0 = pl.multiple_of(t * 256, 256)
        rows = blocks[...].reshape(SD * cap, D)
        to[pl.ds(r0, 256), :] = mm(seat_matrix(meta, r0, 256, cap), rows).astype(BF)

    loop(ROWS // 256, body)


def seat_kernel(cap, blocks, meta, to):
    seat_rows(meta, blocks, cap, to)


def gather_kernel(
    cap,
    count,
    tokens_h,
    cotangent_h,
    order,
    master_h,
    vector,
    owner_of,
    slots_h,
    x_c,
    cot_0,
    cot_1,
    cot_2,
    cot_3,
    recv_meta,
    vecs,
    b_u,
    occupancy,
    positions,
    tokens,
    cotangent,
    master,
    slots,
    own,
    send_x,
    send_c,
    meta,
    recv_x,
    got_meta,
    slot_of,
    digits,
    mine,
    by_z,
    by_tok,
    x_s,
    x_r,
    y_s,
    y_r,
    d_s,
    d_r,
    zx_s,
    zx_r,
    zd_s,
    zd_r,
    zy_s,
    zy_r,
    p_s,
    p_r,
    row_s,
    row_r,
    z_s,
    z_r,
    t_s,
    t_r,
    local_s,
    put_s,
):
    at = Place()
    me, z, side = at.me, at.z, at.side
    n_tok, n_rep = 8, 4
    peers = [((me + d) % n_tok, z) for d in range(1, n_tok)] + [(me, (z + d) % n_rep) for d in range(1, n_rep)]
    fetch = [
        pltpu.make_async_copy(src, dst, local_s.at[i])
        for i, (src, dst) in enumerate(((master_h, master), (tokens_h, tokens), (cotangent_h, cotangent)))
    ]
    for copy in fetch:
        copy.start()
    wait_peers = at.greet(peers)
    fetch[0].wait()

    last = count - 1

    def near(j):
        return side * last + (1 - 2 * side) * j

    def far(j):
        return (1 - side) * last - (1 - 2 * side) * j

    few_x, few_d, few_y = 11 * count // 26, 12 * count // 26, 8 * count // 26
    most_x, most_d, most_y = count - few_x, count - few_d, count - few_y

    def piece(owner, s):
        return slots.at[owner * count + s]

    def to_x(s):
        return remote(own.at[s], piece(me, s), x_s.at[s], x_r.at[s], at.xn, z)

    def to_y(s):
        return remote(own.at[s], piece(me, s), y_s.at[s], y_r.at[s], at.yn, z)

    def on_y(s):
        return remote(piece(at.xn, s), piece(at.xn, s), d_s.at[s], d_r.at[s], at.yn, z)

    def x_on_z(s):
        return remote(piece(at.xn, s), piece(at.xn, s), zx_s.at[s], zx_r.at[s], me, at.zp)

    def d_on_z(s):
        return remote(piece(at.dn, s), piece(at.dn, s), zd_s.at[s], zd_r.at[s], me, at.zp)

    def y_on_z(s):
        return remote(piece(at.yn, s), piece(at.yn, s), zy_s.at[s], zy_r.at[s], me, at.zp)

    def x_in(s):
        return remote(own.at[s], piece(at.xn, s), x_s.at[s], x_r.at[s], at.xn, z)

    def y_in(s):
        return remote(own.at[s], piece(at.yn, s), y_s.at[s], y_r.at[s], at.yn, z)

    def d_in(s):
        return remote(own.at[s], piece(at.dn, s), d_s.at[s], d_r.at[s], at.yn, z)

    owners = (me, at.xn, at.yn, at.dn)

    def near_run(q, j0, j1):
        return (q, (1 - side) * j0 + side * (count - j1), j1 - j0)

    def far_run(q, j0, j1):
        return (q, side * j0 + (1 - side) * (count - j1), j1 - j0)

    runs = (
        (0, 0, count),
        near_run(2, 0, few_y),
        near_run(1, 0, most_x),
        near_run(3, 0, most_d),
        far_run(1, 0, few_x),
        near_run(2, few_y, most_y),
        far_run(2, 0, few_y),
        far_run(3, 0, few_d // 2),
        far_run(3, few_d // 2, few_d - 2),
        far_run(3, few_d - 2, few_d),
    )

    def to_twin(i):
        q, s, n = runs[i]
        src = own if q == 0 else slots.at[pl.ds(owners[q] * count + s, n)]
        dst = slots.at[pl.ds(owners[q] * count + s, n)]
        return remote(src, dst, p_s.at[i], p_r.at[i], at.twin, z)

    def put_run(i, by_twin):
        q, s, n = runs[i]
        owner = at.twin_of(owners[q]) if by_twin else owners[q]
        part = pl.ds(owner * count + s, n)
        src = own if q == 0 and not by_twin else slots.at[part]
        return pltpu.make_async_copy(src, slots_h.at[part], put_s.at[int(by_twin), i])

    def pass_on(i):
        to_twin(i).start()
        put_run(i, False).start()

    def cast(j):
        own[near(j)] = master[near(j)].astype(BF)

    loop(most_x, cast)
    wait_peers()
    loop(most_x, lambda j: to_x(near(j)).start())
    loop(few_y, lambda j: to_y(near(j)).start())
    loop(count - most_x, lambda j: cast(most_x + j))
    pass_on(0)

    seat = me % SD
    seats = (me, at.twin, at.xn, at.twin_of(at.xn))
    rows_of = ((meta, got_meta), (send_x, recv_x))

    def row_copy(i, k):
        src, dst = rows_of[i]
        return remote(src.at[k], dst.at[k], row_s.at[i, k], row_r.at[i, k], seats[k], z)

    put_c = [
        pltpu.make_async_copy(send_c.at[k], to, local_s.at[4 + k])
        for k, to in enumerate((cot_0, cot_1, cot_2, cot_3))
    ]

    def route():
        fetch[1].wait()
        fetch[2].wait()
        slots_here, place = route_slots(order[...], seat, cap)
        slot_of[...] = slots_here
        digits[...] = (
            jnp.concatenate([place // CL, lax.rem(place, CL)] + [place * 0] * 6, axis=0).astype(F32).astype(BF)
        )

    def sort_tokens(k):
        picked = slot_matrix(slot_of[...], k, cap)
        send_x[k] = mm(picked, tokens[...]).astype(BF)
        coded = mm(digits[...], picked, NT)
        line = jnp.concatenate([coded[0:1], coded[1:2]], axis=1)
        meta[k] = jnp.broadcast_to(line, (META, D)).astype(BF)
        for i in range(2):
            if k:
                row_copy(i, k).start()
            else:
                src, dst = rows_of[i]
                dst[0] = src[0]

    def sort_cotangent(k):
        send_c[k] = mm(slot_matrix(slot_of[...], k, cap), cotangent[...]).astype(BF)
        put_c[k].start()

    def z_copy(d):
        return remote(by_z.at[0], by_z.at[d], z_s.at[d], z_r.at[d], me, (z + d) % n_rep)

    def t_copy(d):
        return remote(mine, by_tok.at[d], t_s.at[d], t_r.at[d], (me + d) % n_tok, z)

    def count_rows():
        residue = lax.rem(me // SD * CPS + order[...] // CL, n_tok)
        hit = lax.broadcasted_iota(I32, (128, ROWS), 0) == residue
        by_z[0] = mm(jnp.ones((8, ROWS), BF), jnp.where(hit, 1.0, 0.0).astype(BF), NT)
        for d in range(1, n_rep):
            z_copy(d).start()
        for i in range(9):
            mine[i : i + 1] = vector[i * 128 : (i + 1) * 128].reshape(1, 128).astype(BF).astype(F32)
        block_row = lax.broadcasted_iota(I32, (NBLK, NBLK), 0)
        block_col = lax.broadcasted_iota(I32, (NBLK, NBLK), 1)
        by_col = owner_of[...].astype(F32)
        by_row = lane_sum(jnp.where(block_row == block_col, by_col, 0.0))
        earlier = jnp.where((by_row == by_col) & (block_row < block_col), 1.0, 0.0)
        positions[...] = (by_col * (count * PART // BLK) + jnp.sum(earlier, axis=0, keepdims=True)).astype(I32)

    def share_vectors():
        for d in range(1, n_rep):
            z_copy(d).wait()
        mine[16:24] = by_z[0] + by_z[1] + by_z[2] + by_z[3]
        for d in range(1, n_tok):
            t_copy(d).start()

    def lay_out_vectors():
        by_tok[0] = mine[...]
        for d in range(1, n_tok):
            t_copy(d).wait()
        for owner in range(n_tok):
            share = by_tok[(me + n_tok - owner) % n_tok]
            occupancy[owner : owner + 1, :] = share[16:17, 0:n_tok].astype(I32)
            for i in range(9):
                chunk = owner * 9 + i
                row, lane = chunk // 6, chunk % 6 * 128
                if row < 8:
                    vecs[row : row + 1, lane : lane + 128] = share[i : i + 1]
                else:
                    lane += (row - 8) * D
                    b_u[:, lane : lane + 128] = share[i : i + 1]

    between = {
        1: lambda: (route(), sort_tokens(2)),
        3: lambda: sort_tokens(3),
        5: lambda: sort_tokens(1),
        7: lambda: (sort_tokens(0), count_rows()),
        9: lambda: sort_cotangent(1),
        11: lambda: sort_cotangent(2),
        13: lambda: sort_cotangent(3),
    }
    for j in range(most_x):
        x_in(near(j)).wait_recv()
        if j < most_d:
            on_y(near(j)).start()
        if j < few_x:
            x_on_z(near(j)).start()
        if j < few_y:
            y_in(near(j)).wait_recv()
            y_on_z(near(j)).start()
        if j == few_y:
            pass_on(1)
        if j in between:
            between[j]()
    pass_on(2)
    loop(most_y - few_y, lambda j: to_y(near(few_y + j)).start())
    share_vectors()
    sort_cotangent(0)

    def diagonal(j):
        d_in(near(j)).wait_recv()
        d_on_z(near(j)).start()

    loop(few_d, diagonal)
    loop(most_d - few_d, lambda j: d_in(near(few_d + j)).wait_recv())
    pass_on(3)
    loop(few_x, lambda j: x_on_z(far(j)).wait_recv())
    pass_on(4)
    lay_out_vectors()
    loop(most_y - few_y, lambda j: y_in(near(few_y + j)).wait_recv())
    pass_on(5)
    loop(few_y, lambda j: y_on_z(far(j)).wait_recv())
    pass_on(6)
    for i in (0, 1):
        for k in (2, 3, 1):
            row_copy(i, k).wait_recv()
    recv_meta[...] = got_meta[...]
    seat_rows(got_meta, recv_x, cap, x_c)
    done = 0
    for i, upto in ((7, few_d // 2), (8, few_d - 2), (9, few_d)):
        loop(upto - done, lambda j, done=done: d_on_z(far(done + j)).wait_recv())
        pass_on(i)
        done = upto

    for i in range(2):
        for k in (2, 3, 1):
            row_copy(i, k).wait_send()
    for i in range(len(runs)):
        to_twin(i).wait_recv()
        put_run(i, True).start()
    for copy in put_c:
        copy.wait()

    loop(most_x, lambda j: to_x(near(j)).wait_send())
    loop(most_y, lambda j: to_y(near(j)).wait_send())
    loop(most_d, lambda j: on_y(near(j)).wait_send())
    loop(few_x, lambda j: x_on_z(near(j)).wait_send())
    loop(few_d, lambda j: d_on_z(near(j)).wait_send())
    loop(few_y, lambda j: y_on_z(near(j)).wait_send())
    for i in range(len(runs)):
        to_twin(i).wait_send()
        put_run(i, False).wait()
        put_run(i, True).wait()


def gather_all(cap, tokens, cotangent, order, master, vector, block_owner):
    count = master.shape[0] * BLK // PART
    rows = jax.ShapeDtypeStruct((ROWS, D), BF)
    part = jax.ShapeDtypeStruct((cap, D), BF)
    dma = pltpu.SemaphoreType.DMA
    block = pltpu.VMEM((SD, cap, D), BF)
    meta = pltpu.VMEM((SD, META, D), BF)
    return pl.pallas_call(
        functools.partial(gather_kernel, cap, count),
        out_shape=(
            jax.ShapeDtypeStruct((8 * count, PART, D), BF),
            rows,
            part,
            part,
            part,
            part,
            jax.ShapeDtypeStruct((SD, META, D), BF),
            jax.ShapeDtypeStruct((8, D), F32),
            jax.ShapeDtypeStruct((1, FF), F32),
            jax.ShapeDtypeStruct((8, 8), I32),
            jax.ShapeDtypeStruct((1, NBLK), I32),
        ),
        in_specs=[ANY, ANY, VMEM, ANY, VMEM, VMEM],
        out_specs=(ANY, VMEM) + (ANY,) * SD + (VMEM,) * 5,
        scratch_shapes=[
            pltpu.VMEM((ROWS, D), BF),
            pltpu.VMEM((ROWS, D), BF),
            pltpu.VMEM((count, PART, D), F32),
            pltpu.VMEM((8 * count, PART, D), BF),
            pltpu.VMEM((count, PART, D), BF),
            block,
            block,
            meta,
            block,
            meta,
            pltpu.VMEM((1, ROWS), I32),
            pltpu.VMEM((8, ROWS), BF),
            pltpu.VMEM((24, 128), F32),
            pltpu.VMEM((4, 8, 128), F32),
            pltpu.VMEM((8, 24, 128), F32),
        ]
        + [dma((count,))] * 12
        + [dma((10,))] * 2
        + [dma((2, SD))] * 2
        + [dma((4,))] * 2
        + [dma((8,))] * 2
        + [dma((8,)), dma((2, 10))],
        compiler_params=pltpu.CompilerParams(collective_id=0, has_side_effects=True, vmem_limit_bytes=VMEM_LIMIT),
        cost_estimate=pl.CostEstimate(flops=8 * ROWS * ROWS * D, bytes_accessed=64 << 20, transcendentals=0),
        name="gather",
    )(tokens, cotangent, order, master.reshape(count, PART, D), vector, block_owner.reshape(1, NBLK))


def return_kernel(cap, order, *refs):
    outs, ings, (out, ing, entropy) = refs[:SD], refs[SD : 2 * SD], refs[2 * SD :]
    seat = lax.rem(lax.axis_index("tok"), SD)
    slots, _ = route_slots(order[...], seat, cap)
    picked = jnp.concatenate([slot_matrix(slots, at, cap) for at in range(SD)], axis=0)
    for to, blocks in ((out, outs), (ing, ings)):
        rows = jnp.concatenate([block[0:cap, :] for block in blocks], axis=0)
        to[...] = mm(picked, rows, TN).astype(BF)
    line = jnp.concatenate([block[cap : cap + 8, 0:cap] for block in outs], axis=1)
    entropy[...] = mm(line, picked)[0:1].astype(BF)


def swap_blocks(blocks):
    n = lax.axis_size("tok")
    parts = [blocks[0]]
    for k in range(1, SD):
        parts.append(lax.ppermute(blocks[k], "tok", [(i, i ^ k) for i in range(n)]))
    return parts


def reduce_kernel(
    cap,
    count,
    split,
    grads,
    vec,
    order,
    out_0,
    out_1,
    out_2,
    out_3,
    ing_0,
    ing_1,
    ing_2,
    ing_3,
    total,
    vec_out,
    output,
    input_grad,
    entropy,
    out_v,
    ing_v,
    slot_of,
    a,
    tw,
    rd,
    rx,
    ry,
    o,
    rz1,
    pz,
    rz2,
    fz,
    vt,
    va,
    vb,
    vc,
    a_l,
    keep_l,
    p_s,
    p_r,
    d_s,
    d_r,
    x_s,
    x_r,
    y_s,
    y_r,
    z1_s,
    z1_r,
    z2_s,
    z2_r,
    z3_s,
    z3_r,
    t_s,
    t_r,
    v_s,
    v_r,
    row_l,
):
    at = Place()
    me, z = at.me, at.z
    n_tok, n_rep = 8, 4
    peers = [((me + d) % n_tok, z) for d in range(1, n_tok)] + [(me, (z + d) % n_rep) for d in range(1, n_rep)]
    wait_peers = at.greet(peers)
    owners = (me, at.xn, at.yn, at.dn)

    def load(q):
        return pltpu.make_async_copy(grads.at[pl.ds(owners[q] * count, count)], a.at[q], a_l.at[q])

    for q in (3, 1, 2, 0):
        load(q).start()
    rows_in = [
        pltpu.make_async_copy(src, to.at[k], row_l.at[i, k])
        for i, (blocks, to) in enumerate((((out_0, out_1, out_2, out_3), out_v), ((ing_0, ing_1, ing_2, ing_3), ing_v)))
        for k, src in enumerate(blocks)
    ]
    for copy in rows_in:
        copy.start()
    wait_peers()

    groups = [(g, g * (count // 4), count // 4 if g < 3 else count - 3 * (count // 4)) for g in range(4)]

    def to_twin(q, group):
        g, s, n = group
        src = grads.at[pl.ds(at.twin_of(owners[q]) * count + s, n)]
        return remote(src, tw.at[q, pl.ds(s, n)], p_s.at[q, g], p_r.at[q, g], at.twin, z)

    def d_y(s):
        return remote(a.at[3, s], rd.at[s], d_s.at[s], d_r.at[s], at.yn, z)

    def d_x(s):
        return remote(a.at[3, s], rd.at[s], d_s.at[s], d_r.at[s], at.xn, z)

    def to_x(s):
        return remote(a.at[1, s], rx.at[s], x_s.at[s], x_r.at[s], at.xn, z)

    def to_y(s):
        return remote(a.at[2, s], ry.at[s], y_s.at[s], y_r.at[s], at.yn, z)

    def z_in(s):
        return remote(o.at[s], rz1.at[s], z1_s.at[s], z1_r.at[s], me, at.zp)

    def z_swap(s):
        return remote(pz.at[s], rz2.at[s], z2_s.at[s], z2_r.at[s], me, n_rep - 1 - z)

    def z_out(s):
        return remote(fz.at[s], fz.at[s], z3_s.at[s], z3_r.at[s], me, at.zp)

    def keep(s):
        return pltpu.make_async_copy(fz.at[s], total.at[s], keep_l.at[s])

    for group in groups:
        for q in (3, 1, 2, 0):
            to_twin(q, group).start()

    def v_tok(d):
        return remote(vec.at[(me + d) % n_tok], vt.at[d], t_s.at[d], t_r.at[d], (me + d) % n_tok, z)

    def v_rep(i, src):
        return remote(src, vb.at[i], v_s.at[i], v_r.at[i], me, at.zp if i == 0 else (z + 2) % n_rep)

    for d in range(1, n_tok):
        v_tok(d).start()

    def join(q, s):
        return a[q, s] + tw[q, s]

    def first(s, send):
        a[3, s] = join(3, s)
        send(s).start()

    def plain(q, s, send):
        a[q, s] = join(q, s)
        send(s).start()

    def joined(q, s, arrived, send):
        arrived(s).wait_recv()
        a[q, s] = join(q, s) + rd[s]
        send(s).start()

    inner = (z == 1) | (z == 2)
    outer = (z == 0) | (z == 3)

    def own(s):
        to_x(s).wait_recv()
        to_y(s).wait_recv()
        o[s] = join(0, s) + (rx[s] + ry[s])
        pl.when(outer)(lambda: z_in(s).start())

    def middle(s):
        @pl.when(inner)
        def _():
            z_in(s).wait_recv()
            pz[s] = o[s] + rz1[s]
            z_swap(s).start()

    def last(s):
        @pl.when(inner)
        def _():
            z_swap(s).wait_recv()
            fz[s] = pz[s] + rz2[s]
            z_out(s).start()
            keep(s).start()

    def taken(s):
        @pl.when(outer)
        def _():
            z_out(s).wait_recv()
            keep(s).start()

    def pick_rows(i):
        ts = pl.ds(pl.multiple_of(i * 256, 256), 256)
        hit = lax.broadcasted_iota(I32, (SD * cap, 256), 0) == slot_of[:, ts]
        picked = jnp.where(hit, 1.0, 0.0).astype(BF)
        outs = jnp.concatenate([out_v[k, 0:cap, :] for k in range(SD)], axis=0)
        ings = jnp.concatenate([ing_v[k] for k in range(SD)], axis=0)
        both = mm(picked, jnp.concatenate([outs, ings], axis=1), TN)
        output[ts, :] = both[:, 0:D].astype(BF)
        input_grad[ts, :] = both[:, D:].astype(BF)
        line = jnp.concatenate([out_v[k, cap : cap + 8, 0:cap] for k in range(SD)], axis=1)
        entropy[:, ts] = mm(line, picked)[0:1].astype(BF)

    for q in (3, 1, 2, 0):
        load(q).wait()

    def steps(i, lag, more):
        s = i - lag
        by_x = (s % 2 == 0) & (s < 2 * split)
        live = (s >= 0) & (s < count)
        pl.when(live & by_x)(lambda: more(s, True))
        pl.when(live & jnp.logical_not(by_x))(lambda: more(s, False))

    def steps_of(i, lag, more):
        pl.when((i >= lag) & (i < count + lag))(lambda: more(i - lag))

    def round_of(i):
        for group in groups:

            @pl.when(i == group[1])
            def _(group=group):
                to_twin(3, group).wait_recv()

            @pl.when(i == group[1] + 1)
            def _(group=group):
                to_twin(1, group).wait_recv()
                to_twin(2, group).wait_recv()

            @pl.when(i == group[1] + 6)
            def _(group=group):
                to_twin(0, group).wait_recv()

        steps(i, 0, lambda s, by_x: first(s, d_x if by_x else d_y))
        steps(i, 1, lambda s, by_x: plain(1, s, to_x) if by_x else plain(2, s, to_y))
        steps(i, 3, lambda s, by_x: joined(2, s, d_x, to_y) if by_x else joined(1, s, d_y, to_x))
        steps_of(i, 6, own)
        steps_of(i, 8, middle)
        steps_of(i, 10, last)
        steps_of(i, 12, taken)

    loop(3, round_of)
    for copy in rows_in:
        copy.wait()
    slots_here, _ = route_slots(order[...], me % SD, cap)
    slot_of[...] = slots_here

    v_sum = vec[me]
    for d in range(1, n_tok):
        v_tok(d).wait()
        v_sum = v_sum + vt[d]
    va[...] = v_sum
    v_rep(0, va).start()

    def four_rounds(i):
        loop(4, lambda j: round_of(3 + 4 * i + j))
        pick_rows(i)

    four_rounds(0)
    v_rep(0, va).wait()
    vc[...] = va[...] + vb[0]
    v_rep(1, vc).start()
    loop(3, lambda i: four_rounds(1 + i))
    loop(count + 12 - 19, lambda i: round_of(19 + i))
    v_rep(1, vc).wait()
    vec_out[...] = vc[...] + vb[1]

    for group in groups:
        for q in range(4):
            to_twin(q, group).wait_send()

    def sent(s):
        d_y(s).wait_send()
        to_x(s).wait_send()
        to_y(s).wait_send()
        keep(s).wait()

    loop(count, sent)

    @pl.when(outer)
    def _():
        loop(count, lambda s: z_in(s).wait_send())

    @pl.when(inner)
    def _():
        def back(s):
            z_swap(s).wait_send()
            z_out(s).wait_send()

        loop(count, back)


def reduce_all(cap, grads, shares, order, outs, ings, count):
    dma = pltpu.SemaphoreType.DMA
    count = count * BLK // PART
    part = pltpu.VMEM((count, PART, D), BF)
    whole = pltpu.VMEM((4, count, PART, D), BF)
    line = pltpu.VMEM((16, 128), F32)
    rows = jax.ShapeDtypeStruct((ROWS, D), BF)
    total, vec, output, input_grad, entropy = pl.pallas_call(
        functools.partial(reduce_kernel, cap, count, count // 2),
        out_shape=(
            jax.ShapeDtypeStruct((count, PART, D), BF),
            jax.ShapeDtypeStruct((16, 128), F32),
            rows,
            rows,
            jax.ShapeDtypeStruct((1, ROWS), BF),
        ),
        in_specs=[ANY, VMEM, VMEM] + [ANY] * (2 * SD),
        out_specs=(ANY,) + (VMEM,) * 4,
        scratch_shapes=[
            pltpu.VMEM((SD, cap + META, D), BF),
            pltpu.VMEM((SD, cap, D), BF),
            pltpu.VMEM((1, ROWS), I32),
            whole,
            whole,
        ]
        + [part] * 8
        + [pltpu.VMEM((8, 16, 128), F32), line, pltpu.VMEM((2, 16, 128), F32), line]
        + [dma((4,)), dma((count,))]
        + [dma((4, 4))] * 2
        + [dma((count,))] * 12
        + [dma((8,))] * 2
        + [dma((2,))] * 2
        + [dma((2, SD))],
        compiler_params=pltpu.CompilerParams(collective_id=1, has_side_effects=True, vmem_limit_bytes=VMEM_LIMIT),
        cost_estimate=pl.CostEstimate(flops=4 * ROWS * ROWS * D, bytes_accessed=64 << 20, transcendentals=0),
        name="reduce",
    )(grads.reshape(-1, PART, D), shares, order, *outs, *ings)
    return total.reshape(-1, BLK, D), vec, output, input_grad, entropy


V_BQ, V_BV, V_BO, V_BD, V_G1, V_C1, V_G2, V_C2 = range(8)


def inverse(x):
    r = pl.reciprocal(x, approx=True)
    return r * (2.0 - x * r)


def erf_parts(v):
    t = inverse(1.0 + (0.3275911 / math.sqrt(2.0)) * jnp.abs(v))
    e = jnp.exp2((v * v) * (-0.5 / math.log(2.0)))
    poly = 0.5 * 1.061405429
    for c in (-1.453152027, 1.421413741, -0.284496736, 0.254829592):
        poly = poly * t + 0.5 * c
    tail = poly * (t * e)
    return jnp.where(v >= 0.0, 1.0 - tail, tail), e


def lane_sum(x):
    return jnp.sum(x, axis=1, keepdims=True)


def gelu_parts(v):
    phi, e = erf_parts(v)
    return v * phi, phi + v * (e * (1.0 / math.sqrt(2.0 * math.pi)))


def weight_copies(pos, slots, w, sem, first):
    def copy(b):
        return pltpu.make_async_copy(slots.at[pos[first + b]], w.at[pl.ds(b * BLK, BLK)], sem)

    n = w.shape[0] // BLK
    return (lambda: loop(n, lambda b: copy(b).start())), (lambda: loop(n, lambda b: copy(b).wait()))


def halves_of_heads():
    lane = lax.broadcasted_iota(I32, (1, PW), 1)
    m0 = jnp.where(lane < HD, 1.0, 0.0).astype(BF)
    m1 = jnp.where(lane < HD, 0.0, 1.0).astype(BF)
    return lambda pair: jnp.concatenate([pair * m0, pair * m1], axis=0)


def tile_rows(t):
    return pl.ds(pl.multiple_of(t * TM, TM), TM)


def forward_kernel(
    cap,
    pos,
    slots,
    vecs,
    b_u,
    x_h,
    meta,
    back_0,
    back_1,
    back_2,
    back_3,
    heads_h,
    act_h,
    hid_h,
    q_h,
    k_h,
    v_h,
    p_h,
    slope_h,
    n1_h,
    n2_h,
    rs1_h,
    rs2_h,
    wqkv,
    wo,
    wu,
    wd,
    x_c,
    heads,
    act,
    hid,
    q,
    k,
    v,
    p_all,
    slope,
    n1,
    n2,
    rs1,
    rs2,
    out_c,
    ent,
    hid_t,
    w_sem,
    x_sem,
    o_sem,
):
    inv = 1.0 / math.sqrt(HD)
    get_x = pltpu.make_async_copy(x_h, x_c, x_sem)
    get_x.start()
    weights = [
        weight_copies(pos, slots, w, w_sem.at[i], first)
        for i, (w, first) in enumerate(((wqkv, 0), (wo, 24), (wu, 32), (wd, 64)))
    ]
    for start, _ in weights:
        start()
    get_x.wait()
    apart = halves_of_heads()

    def vec(i):
        return vecs[i : i + 1, :]

    saved = (
        (heads, heads_h),
        (act, act_h),
        (hid, hid_h),
        (q, q_h),
        (k, k_h),
        (v, v_h),
        (slope, slope_h),
        (n1, n1_h),
        (n2, n2_h),
        (rs1, rs1_h),
        (rs2, rs2_h),
    )

    def save(t, i):
        src, dst = saved[i]
        return pltpu.make_async_copy(src.at[tile_rows(t)], dst.at[tile_rows(t)], o_sem.at[i])

    def save_p(t):
        n = TM // CL
        cs = pl.ds(t * n, n)
        return pltpu.make_async_copy(p_all.at[cs], p_h.at[cs], o_sem.at[len(saved)])

    def normal(r, n, rs, rows):
        c = r - lane_sum(r) * (1.0 / D)
        scale = lax.rsqrt(lane_sum(c * c) * (1.0 / D) + norm_epsilon)
        rs[rows, :] = jnp.broadcast_to(scale, (TM, 128))
        n[rows, :] = c * scale

    def tile(t):
        rows = tile_rows(t)
        first = t == 0
        pl.when(first)(weights[0][1])
        x = x_c[rows, :]
        q[rows, :] = ((mm(x, wqkv[0:D, :]) + vec(V_BQ)).astype(BF).astype(F32) * inv).astype(BF)
        k[rows, :] = mm(x, wqkv[D : 2 * D, :]).astype(BF)
        v[rows, :] = (mm(x, wqkv[2 * D :, :]) + vec(V_BV)).astype(BF)

        def attend(c):
            groups = [pl.ds(pl.multiple_of(t * TM + (FWD_AT * c + i) * CL, CL), CL) for i in range(FWD_AT)]
            pairs = [(i, p, slice(p * PW, (p + 1) * PW)) for i in range(FWD_AT) for p in range(PAIRS)]
            scores = [mm(apart(k[groups[i], ps]), q[groups[i], ps], NT) for i, _, ps in pairs]
            total = [jnp.zeros((1, CL), F32)] * FWD_AT
            probs = []
            for (i, _, _), both in zip(pairs, scores):
                halves = []
                for h in range(2):
                    sh = both[h * CL : (h + 1) * CL]
                    sh = sh - jnp.max(sh, axis=0, keepdims=True)
                    e = jnp.exp(sh)
                    tot = jnp.sum(e, axis=0, keepdims=True)
                    r = 1.0 / tot
                    total[i] += jnp.log(tot) - jnp.sum(e * sh, axis=0, keepdims=True) * r
                    halves.append((e * r).astype(BF))
                probs.append(jnp.concatenate(halves, axis=0))
            mixed = [mm(w, apart(v[groups[i], ps]), TN).astype(BF) for (i, _, ps), w in zip(pairs, probs)]
            for (i, p, ps), w, o in zip(pairs, probs, mixed):
                p_all[t * (TM // CL) + FWD_AT * c + i, p] = w
                heads[groups[i], ps] = o
            for i in range(FWD_AT):
                ent[:, groups[i]] = jnp.broadcast_to(total[i] * (1.0 / HEADS), (8, CL))

        loop(TM // CL // FWD_AT, attend)
        for i in (0, 3, 4, 5):
            save(t, i).start()
        save_p(t).start()
        pl.when(first)(weights[1][1])
        normal(x_c[rows, :].astype(F32) + mm(heads[rows, :], wo[...]) + vec(V_BO), n1, rs1, rows)
        hidden = n1[rows, :] * vec(V_G1) + vec(V_C1)
        hid[rows, :] = hidden.astype(BF)
        hid_t[...] = hidden
        pl.when(first)(weights[2][1])

        def widen(f):
            parts = [pl.ds(pl.multiple_of((2 * f + i) * FC, FC), FC) for i in range(2)]
            ups = [mm(hid[rows, :], wu[fs, :], NT) for fs in parts]
            for fs, up in zip(parts, ups):
                g, g_slope = gelu_parts(up + b_u[:, fs])
                act[rows, fs] = g.astype(BF)
                slope[rows, fs] = g_slope.astype(BF)

        loop(FF // FC // 2, widen)
        for i in (1, 2, 6, 7, 9):
            save(t, i).start()
        pl.when(first)(weights[3][1])
        normal(hid_t[...] + mm(act[rows, :], wd[...]) + vec(V_BD), n2, rs2, rows)
        out_c[rows, :] = (n2[rows, :] * vec(V_G2) + vec(V_C2)).astype(BF)
        for i in (8, 10):
            save(t, i).start()

    loop(ROWS // TM, tile)

    for j, back in enumerate((back_0, back_1, back_2, back_3)):
        own = seat_part(meta, j, cap)
        back[0:cap, :] = mm(own, out_c[...], TN).astype(BF)
        line = mm(ent[...].astype(BF), own)
        back[cap:, :] = jnp.concatenate([line, line], axis=1)[0:1].astype(BF) * jnp.ones((META, 1), BF)

    def saved_all(t):
        for i in range(len(saved)):
            save(t, i).wait()
        save_p(t).wait()

    loop(ROWS // TM, saved_all)


def shape_of(kind, *shape):
    return jax.ShapeDtypeStruct(shape, kind)


def saved_shapes():
    rows, wide = ((ROWS, D), BF), ((ROWS, FF), BF)
    probs = ((ROWS // CL, PAIRS, 2 * CL, CL), BF)
    full, thin = ((ROWS, D), F32), ((ROWS, 128), F32)
    return rows, wide, probs, full, thin


def forward(cap, positions, slots, vecs, b_u, x_c, meta):
    rows, wide, probs, full, thin = saved_shapes()
    kept = (rows, wide, rows, rows, rows, rows, probs, wide, full, full, thin, thin)
    dma = pltpu.SemaphoreType.DMA
    return pl.pallas_call(
        functools.partial(forward_kernel, cap),
        out_shape=(shape_of(BF, cap + META, D),) * SD + tuple(shape_of(kind, *shape) for shape, kind in kept),
        in_specs=[SMEM, ANY, VMEM, VMEM, ANY, VMEM],
        out_specs=(VMEM,) * SD + (ANY,) * len(kept),
        scratch_shapes=[
            pltpu.VMEM((3 * D, D), BF),
            pltpu.VMEM((D, D), BF),
            pltpu.VMEM((FF, D), BF),
            pltpu.VMEM((FF, D), BF),
            pltpu.VMEM(*rows),
        ]
        + [pltpu.VMEM(*a) for a in kept]
        + [
            pltpu.VMEM(*rows),
            pltpu.VMEM((8, ROWS), F32),
            pltpu.VMEM((TM, D), F32),
            dma((4,)),
            dma,
            dma((12,)),
        ],
        compiler_params=pltpu.CompilerParams(vmem_limit_bytes=VMEM_LIMIT),
        cost_estimate=pl.CostEstimate(flops=2 * ROWS * WROWS * D, bytes_accessed=64 << 20, transcendentals=0),
        name="forward",
    )(positions, slots, vecs, b_u, x_c, meta)


def backward_kernel(
    cap,
    pos,
    slots,
    vecs,
    meta,
    cot_0,
    cot_1,
    cot_2,
    cot_3,
    q_h,
    k_h,
    v_h,
    p_h,
    slope_h,
    n1_h,
    n2_h,
    rs1_h,
    rs2_h,
    back_0,
    back_1,
    back_2,
    back_3,
    shares,
    d_up_h,
    d_q_h,
    d_k_h,
    d_v_h,
    d_proj_h,
    d_br_h,
    wqkv,
    wo,
    wu,
    wd,
    blocks,
    q,
    k,
    v,
    p_all,
    d_up,
    n1,
    n2,
    rs1,
    rs2,
    d_proj,
    d_br,
    ing_c,
    d_h_t,
    gvec,
    g_bu,
    w_sem,
    c_sem,
    i_sem,
    o_sem,
):
    inv = 1.0 / math.sqrt(HD)
    get_c = [
        pltpu.make_async_copy(cot, blocks.at[j], c_sem.at[j]) for j, cot in enumerate((cot_0, cot_1, cot_2, cot_3))
    ]
    for copy in get_c:
        copy.start()
    fetch = [
        pltpu.make_async_copy(src, dst, i_sem.at[i])
        for i, (src, dst) in enumerate(
            (
                (n2_h, n2),
                (rs2_h, rs2),
                (slope_h, d_up),
                (n1_h, n1),
                (rs1_h, rs1),
                (v_h, v),
                (p_h, p_all),
                (k_h, k),
                (q_h, q),
            )
        )
    ]
    weights = [
        weight_copies(pos, slots, w, w_sem.at[i], first)
        for i, (w, first) in enumerate(((wd, 64), (wu, 32), (wo, 24), (wqkv, 0)))
    ]
    fetch[0].start()
    fetch[1].start()
    weights[0][0]()
    fetch[2].start()
    weights[1][0]()
    fetch[3].start()
    fetch[4].start()
    weights[2][0]()
    for i in range(5, 9):
        fetch[i].start()
    weights[3][0]()
    gvec[...] = jnp.zeros_like(gvec)
    g_bu[...] = jnp.zeros_like(g_bu)
    shares[...] = jnp.zeros_like(shares)
    for copy in get_c:
        copy.wait()
    seat_rows(meta, blocks, cap, d_br)
    apart = halves_of_heads()

    def vec(i):
        return vecs[i : i + 1, :]

    def add_vec(i, value):
        gvec[i : i + 1, :] += jnp.sum(value, axis=0, keepdims=True)

    saved = ((d_up, d_up_h), (q, d_q_h), (k, d_k_h), (v, d_v_h), (d_proj, d_proj_h), (d_br, d_br_h))

    def save(t, i):
        src, dst = saved[i]
        return pltpu.make_async_copy(src.at[tile_rows(t)], dst.at[tile_rows(t)], o_sem.at[i])

    def norm_back(e, n, rs, gain, shift):
        add_vec(gain, e * n)
        add_vec(shift, e)
        eg = e * vec(gain)
        return rs * (eg - lane_sum(eg) * (1.0 / D) - n * (lane_sum(eg * n) * (1.0 / D)))

    def norm_two_back(t):
        rows = tile_rows(t)
        d_r2 = norm_back(d_br[rows, :].astype(F32), n2[rows, :], rs2[rows, 0:1], V_G2, V_C2)
        d_br[rows, :] = d_r2.astype(BF)
        add_vec(V_BD, d_br[rows, :].astype(F32))
        n2[rows, :] = d_r2

    def widen_back(t, columns):
        rows = tile_rows(t)
        parts = [pl.ds(pl.multiple_of(f * FC, FC), FC) for f in columns]
        ups = [mm(d_br[rows, :], wd[fs, :], NT) for fs in parts]

        def finish():
            for fs, up in zip(parts, ups):
                du = (up * d_up[rows, fs].astype(F32)).astype(BF)
                d_up[rows, fs] = du
                g_bu[:, fs] += jnp.sum(du.astype(F32), axis=0, keepdims=True)

        return finish

    def hidden_back(t):
        rows = tile_rows(t)
        return n2[rows, :] + mm(d_up[rows, :], wu[...])

    def norm_one_back(t, d_h):
        rows = tile_rows(t)
        d_r1 = norm_back(d_h, n1[rows, :], rs1[rows, 0:1], V_G1, V_C1)
        d_proj[rows, :] = d_r1.astype(BF)
        n2[rows, :] = d_r1
        add_vec(V_BO, d_proj[rows, :].astype(F32))

    def heads_back(t):
        rows = tile_rows(t)
        d_h_t[rows, :] = mm(d_proj[rows, :], wo[...], NT).astype(BF)

    def attend_back(clusters, meanwhile=lambda: None):
        pairs = [
            (c, p, pl.ds(pl.multiple_of(c * CL, CL), CL), slice(p * PW, (p + 1) * PW))
            for c in clusters
            for p in range(PAIRS)
        ]
        probs = [p_all[c, p] for c, p, _, _ in pairs]
        d_heads = [d_h_t[gr, ps] for _, _, gr, ps in pairs]
        d_probs = [mm(apart(v[gr, ps]), dh, NT) for (_, _, gr, ps), dh in zip(pairs, d_heads)]
        d_values = [
            mm(jnp.concatenate([w[0:CL], w[CL:]], axis=1), apart(dh)).astype(BF) for w, dh in zip(probs, d_heads)
        ]
        finish = meanwhile()
        d_scores = []
        for w, dw in zip(probs, d_probs):
            halves = []
            for h in range(2):
                wh = w[h * CL : (h + 1) * CL].astype(F32)
                dwh = dw[h * CL : (h + 1) * CL]
                halves.append((wh * (dwh - jnp.sum(dwh * wh, axis=0, keepdims=True))).astype(BF))
            d_scores.append(halves)
        d_keys = [
            mm(jnp.concatenate(ds, axis=1), apart(q[gr, ps])).astype(BF) for (_, _, gr, ps), ds in zip(pairs, d_scores)
        ]
        d_queries = [
            (mm(jnp.concatenate(ds, axis=0), apart(k[gr, ps]), TN) * inv).astype(BF)
            for (_, _, gr, ps), ds in zip(pairs, d_scores)
        ]
        if finish is not None:
            finish()
        for (_, _, gr, ps), dq, dk, dv in zip(pairs, d_queries, d_keys, d_values):
            q[gr, ps] = dq
            k[gr, ps] = dk
            v[gr, ps] = dv

    def rows_back(t):
        rows = tile_rows(t)
        return (
            mm(q[rows, :], wqkv[0:D, :], NT)
            + mm(k[rows, :], wqkv[D : 2 * D, :], NT)
            + mm(v[rows, :], wqkv[2 * D :, :], NT)
        )

    def rows_done(t, d_x):
        rows = tile_rows(t)
        add_vec(V_BQ, q[rows, :].astype(F32))
        add_vec(V_BV, v[rows, :].astype(F32))
        ing_c[rows, :] = (n2[rows, :] + d_x.astype(BF).astype(F32)).astype(BF)

    def save_all(t, which):
        for i in which:
            save(t, i).start()

    per = TM // CL
    fetch[0].wait()
    fetch[1].wait()
    norm_two_back(0)
    norm_two_back(1)
    weights[0][1]()
    fetch[2].wait()
    loop(FF // FC // 2, lambda f: widen_back(0, [2 * f, 2 * f + 1])())
    save_all(0, (0, 5))
    weights[1][1]()
    fetch[3].wait()
    fetch[4].wait()
    norm_one_back(0, hidden_back(0))
    weights[2][1]()
    for i in range(5, 9):
        fetch[i].wait()
    heads_back(0)
    save_all(0, (4,))
    loop(per, lambda c: attend_back([c], lambda: widen_back(1, [c])))
    save_all(0, (1, 2, 3))
    save_all(1, (0, 5))
    weights[3][1]()
    d_h = hidden_back(1)
    d_x = rows_back(0)
    norm_one_back(1, d_h)
    heads_back(1)
    rows_done(0, d_x)
    save_all(1, (4,))
    loop(per // BWD_AT, lambda c: attend_back([per + BWD_AT * c + i for i in range(BWD_AT)]))
    save_all(1, (1, 2, 3))
    rows_done(1, rows_back(1))

    for j, back in enumerate((back_0, back_1, back_2, back_3)):
        back[...] = mm(seat_part(meta, j, cap), ing_c[...], TN).astype(BF)

    for chunk in range(72):
        row, lane = chunk // 6, chunk % 6 * 128
        if row < 8:
            part = gvec[row : row + 1, lane : lane + 128]
        else:
            lane += (row - 8) * D
            part = g_bu[:, lane : lane + 128]
        shares[chunk // 9, chunk % 9 : chunk % 9 + 1, :] = part

    def saved_all(t):
        for i in range(len(saved)):
            save(t, i).wait()

    loop(ROWS // TM, saved_all)


def backward(cap, positions, slots, vecs, meta, cots, saved):
    rows, wide, probs, full, thin = saved_shapes()
    dma = pltpu.SemaphoreType.DMA
    grads = (wide, rows, rows, rows, rows, rows)
    return pl.pallas_call(
        functools.partial(backward_kernel, cap),
        out_shape=(shape_of(BF, cap, D),) * SD
        + (shape_of(F32, 8, 16, 128),)
        + tuple(shape_of(kind, *shape) for shape, kind in grads),
        in_specs=[SMEM, ANY, VMEM, VMEM] + [ANY] * (SD + 9),
        out_specs=(VMEM,) * (SD + 1) + (ANY,) * len(grads),
        scratch_shapes=[
            pltpu.VMEM((3 * D, D), BF),
            pltpu.VMEM((D, D), BF),
            pltpu.VMEM((FF, D), BF),
            pltpu.VMEM((FF, D), BF),
            pltpu.VMEM((SD, cap, D), BF),
        ]
        + [pltpu.VMEM(*a) for a in (rows, rows, rows, probs, wide, full, full, thin, thin, rows, rows, rows)]
        + [
            pltpu.VMEM(*rows),
            pltpu.VMEM((8, D), F32),
            pltpu.VMEM((1, FF), F32),
            dma((4,)),
            dma((4,)),
            dma((9,)),
            dma((6,)),
        ],
        compiler_params=pltpu.CompilerParams(vmem_limit_bytes=VMEM_LIMIT),
        cost_estimate=pl.CostEstimate(flops=2 * ROWS * WROWS * D, bytes_accessed=64 << 20, transcendentals=0),
        name="backward",
    )(positions, slots, vecs, meta, *cots, *saved)


WC = 8 * BLK


def weight_kernel(
    pos,
    x_h,
    heads_h,
    act_h,
    d_up_h,
    d_q_h,
    d_k_h,
    d_v_h,
    d_proj_h,
    hid_h,
    d_br_h,
    grads,
    x_c,
    heads,
    act,
    d_up,
    d_q,
    d_k,
    d_v,
    d_proj,
    hid,
    d_br,
    stage,
    i_sem,
    g_sem,
):
    refs = (
        (x_h, x_c),
        (d_q_h, d_q),
        (d_k_h, d_k),
        (d_v_h, d_v),
        (heads_h, heads),
        (d_proj_h, d_proj),
        (hid_h, hid),
        (d_up_h, d_up),
        (d_br_h, d_br),
        (act_h, act),
    )
    fetch = [pltpu.make_async_copy(src, dst, i_sem.at[i]) for i, (src, dst) in enumerate(refs)]
    for copy in fetch:
        copy.start()

    per = WC // BLK

    def g_copy(chunk, j, at):
        return pltpu.make_async_copy(
            stage.at[at, pl.ds(j * BLK, BLK)], grads.at[pos[chunk * per + j]], g_sem.at[at]
        )

    def put(chunk, left, right):
        at = lax.rem(chunk, 2)

        @pl.when(chunk >= 2)
        def _():
            for j in range(per):
                g_copy(chunk - 2, j, at).wait()

        stage[at] = mm(left, right, TN).astype(BF)
        for j in range(per):
            g_copy(chunk, j, at).start()

    first = 0
    for left, right, needs in (
        (x_c, d_q, (0, 1)),
        (x_c, d_k, (2,)),
        (x_c, d_v, (3,)),
        (heads, d_proj, (4, 5)),
        (d_up, hid, (6, 7)),
        (act, d_br, (8, 9)),
    ):
        for i in needs:
            fetch[i].wait()

        def body(j, left=left, right=right, first=first):
            put(first + j, left[:, pl.ds(pl.multiple_of(j * WC, WC), WC)], right[...])

        loop(left.shape[1] // WC, body)
        first += left.shape[1] // WC
    for chunk in (first - 2, first - 1):
        for j in range(per):
            g_copy(chunk, j, chunk % 2).wait()


def weight_grads_of(total_slots, positions, x_c, saved):
    r_v, w_v = pltpu.VMEM((ROWS, D), BF), pltpu.VMEM((ROWS, FF), BF)
    return pl.pallas_call(
        weight_kernel,
        out_shape=jax.ShapeDtypeStruct((total_slots, BLK, D), BF),
        in_specs=[SMEM] + [ANY] * 10,
        out_specs=ANY,
        scratch_shapes=[r_v, r_v, w_v, w_v]
        + [r_v] * 6
        + [
            pltpu.VMEM((2, WC, D), BF),
            pltpu.SemaphoreType.DMA((10,)),
            pltpu.SemaphoreType.DMA((2,)),
        ],
        compiler_params=pltpu.CompilerParams(vmem_limit_bytes=VMEM_LIMIT),
        cost_estimate=pl.CostEstimate(flops=2 * ROWS * WROWS * D, bytes_accessed=40 << 20, transcendentals=0),
        name="weight_grads",
    )(positions, x_c, *saved)


def finish_kernel(
    used,
    total,
    master,
    first,
    second,
    v_grad,
    v_master,
    v_first,
    v_second,
    line,
    counts,
    out_h,
    ing_h,
    grad_new,
    first_new,
    second_new,
    master_new,
    low_new,
    v_grad_new,
    v_first_new,
    v_second_new,
    v_master_new,
    v_low_new,
    entropy,
    occupancy,
    output,
    input_grad,
):
    i = pl.program_id(0)

    @pl.when(i == 0)
    def _():
        output[...] = out_h[...]
        input_grad[...] = ing_h[...]
        entropy[...] = line[...].reshape(ROWS)
        occupancy[...] = counts[...]
        length = v_master.shape[0]
        for n in range(-(-length // 128)):
            part = slice(n * 128, min((n + 1) * 128, length))
            g = v_grad[n : n + 1, 0 : part.stop - part.start].reshape(part.stop - part.start)
            m, v, w = adam_update(g, v_master[part], v_first[part], v_second[part], rate_vector)
            v_grad_new[part] = g
            v_first_new[part] = m
            v_second_new[part] = v
            v_master_new[part] = w
        v_low_new[...] = v_master_new[...].astype(BF)

    g = jnp.where(used[i] > 0, total[...].astype(F32), 0.0)
    m, v, w = adam_update(g, master[...], first[...], second[...], rate_matrix)
    grad_new[...] = g
    first_new[...] = m
    second_new[...] = v
    master_new[...] = w
    low_new[...] = w.astype(BF)


def finish(used, total, weights, v_grad, vectors, line, counts, out, ing):
    count = total.shape[0]
    slot = pl.BlockSpec((1, BLK, D), lambda i: (i, 0, 0))

    def whole(array):
        return pl.BlockSpec(array.shape, lambda i: (0,) * array.ndim)

    f32_slots, f32_vector = shape_of(F32, count, BLK, D), shape_of(F32, *vectors[0].shape)
    shapes = (
        (f32_slots,) * 4
        + (shape_of(BF, count, BLK, D),)
        + (f32_vector,) * 4
        + (shape_of(BF, *vectors[0].shape), shape_of(BF, ROWS), shape_of(I32, *counts.shape))
        + (shape_of(BF, ROWS, D),) * 2
    )
    return pl.pallas_call(
        finish_kernel,
        grid=(count,),
        out_shape=shapes,
        in_specs=[SMEM] + [slot] * 4 + [whole(a) for a in (v_grad, *vectors, line, counts, out, ing)],
        out_specs=(slot,) * 5 + tuple(whole(a) for a in shapes[5:]),
        compiler_params=pltpu.CompilerParams(vmem_limit_bytes=VMEM_LIMIT),
        name="finish",
    )(used, total, *weights, v_grad, *vectors, line, counts, out, ing)


def local(
    tokens,
    cotangent,
    cluster_order,
    block_owner,
    master_slots,
    moment_one,
    moment_two,
    vector_master,
    vector_moment_one,
    vector_moment_two,
):
    tok_count = lax.axis_size("tok")
    tok_index = lax.axis_index("tok")
    slot_count = master_slots.shape[0]
    cap = tok_count // SD * (max(1, CPS // tok_count) * 3 * CL // (2 * SD))
    total_slots = tok_count * slot_count
    order = cluster_order.reshape(1, ROWS)

    block = jax.ShapeDtypeStruct((SD, cap, D), BF)
    meta_shape = jax.ShapeDtypeStruct((SD, META, D), BF)
    row_block = jax.ShapeDtypeStruct((ROWS, D), BF)
    four_planes = tok_count == 8 and lax.axis_size("rep") == 4
    if four_planes:
        slots_low, x_c, *cots, recv_meta, vecs, b_u, occupancy, positions = gather_all(
            cap, tokens, cotangent, order, master_slots, vector_master, block_owner
        )
        positions = positions.reshape(NBLK)
        slots_low = slots_low.reshape(total_slots, BLK, D)
    else:
        positions = slot_positions(block_owner, slot_count)
        slots_low = lax.all_gather(master_slots.astype(BF), "tok", axis=0, tiled=True)
        vectors = lax.all_gather(vector_master.astype(BF), "tok", axis=0, tiled=True).astype(F32)
        vecs, b_u = vectors[: 8 * D].reshape(8, D), vectors[8 * D :].reshape(1, FF)
        cluster = tok_index // SD * CPS + cluster_order // CL
        target = cluster % tok_count
        chosen = target[None, :] == jnp.arange(tok_count, dtype=jnp.int32)[:, None]
        sent_counts = jnp.sum(chosen.astype(F32), axis=1)
        own_row = (jnp.arange(tok_count, dtype=jnp.int32) == tok_index).astype(F32)
        occupancy = lax.psum(own_row[:, None] * sent_counts[None, :], ("tok", "rep")).astype(jnp.int32)
        send_x, send_c, meta = pl.pallas_call(
            functools.partial(send_kernel, cap),
            out_shape=(block, block, meta_shape),
            in_specs=[VMEM] * 3,
            out_specs=(VMEM,) * 3,
            compiler_params=pltpu.CompilerParams(vmem_limit_bytes=VMEM_LIMIT),
            name="send_rows",
        )(tokens, cotangent, order)
        recv_x, recv_meta = (jnp.stack(swap_blocks(b)) for b in (send_x, meta))
        x_c = pl.pallas_call(
            functools.partial(seat_kernel, cap),
            out_shape=row_block,
            in_specs=[VMEM] * 2,
            out_specs=VMEM,
            compiler_params=pltpu.CompilerParams(vmem_limit_bytes=VMEM_LIMIT),
            name="seat_rows",
        )(recv_x, recv_meta)
        cots = [send_c[k] for k in range(SD)]

    cots = swap_blocks(cots)
    *out_blocks, heads, act, hid, q, k, v, p, slope, n1, n2, rs1, rs2 = forward(
        cap, positions, slots_low, vecs, b_u, x_c, recv_meta
    )
    out_blocks = swap_blocks(out_blocks)
    *ing_blocks, shares, d_up, d_q, d_k, d_v, d_proj, d_br = backward(
        cap, positions, slots_low, vecs, recv_meta, cots, (q, k, v, p, slope, n1, n2, rs1, rs2)
    )
    ing_blocks = swap_blocks(ing_blocks)
    grads = weight_grads_of(
        total_slots, positions, x_c, (heads, act, d_up, d_q, d_k, d_v, d_proj, hid, d_br)
    )
    if four_planes:
        total, vec_owned, output, input_grad, entropy = reduce_all(
            cap, grads, shares, order, out_blocks, ing_blocks, slot_count
        )
    else:
        total = lax.psum(lax.psum_scatter(grads, "tok", scatter_dimension=0, tiled=True), "rep")
        grad_vector = shares[:, 0:9].reshape(-1)
        vec_owned = lax.psum(lax.psum_scatter(grad_vector, "tok", scatter_dimension=0, tiled=True), "rep")
        vec_owned = jnp.pad(vec_owned, (0, -vec_owned.shape[0] % 128)).reshape(-1, 128)
        output, input_grad, entropy = pl.pallas_call(
            functools.partial(return_kernel, cap),
            out_shape=(row_block, row_block, jax.ShapeDtypeStruct((1, ROWS), BF)),
            in_specs=[VMEM] * (2 * SD + 1),
            out_specs=(VMEM,) * 3,
            compiler_params=pltpu.CompilerParams(vmem_limit_bytes=VMEM_LIMIT),
            name="return_rows",
        )(order, *out_blocks, *ing_blocks)

    used = jnp.any(
        positions[None, :] == (tok_index * slot_count + jnp.arange(slot_count, dtype=I32))[:, None], axis=1
    )
    (
        owned_grad,
        first_new,
        second_new,
        master_new,
        low_new,
        vec_owned,
        vec_first,
        vec_second,
        vec_new,
        vec_low_new,
        row_entropy,
        occupancy,
        output,
        input_grad,
    ) = finish(
        used.astype(I32),
        total,
        (master_slots, moment_one, moment_two),
        vec_owned,
        (vector_master, vector_moment_one, vector_moment_two),
        entropy,
        occupancy,
        output,
        input_grad,
    )
    return (
        output,
        input_grad,
        owned_grad,
        first_new,
        second_new,
        master_new,
        low_new,
        vec_owned,
        vec_first,
        vec_second,
        vec_new,
        vec_low_new,
        row_entropy,
        occupancy,
    )


def solution(mesh):
    placed = (
        P(("rep", "tok"), None),
        P(("rep", "tok"), None),
        P(("rep", "tok")),
        P(),
        P("tok", None, None),
        P("tok", None, None),
        P("tok", None, None),
        P("tok"),
        P("tok"),
        P("tok"),
    )
    return jax.shard_map(
        local,
        mesh=mesh,
        in_specs=placed,
        out_specs=(
            P(("rep", "tok"), None),
            P(("rep", "tok"), None),
            P("tok", None, None),
            P("tok", None, None),
            P("tok", None, None),
            P("tok", None, None),
            P("tok", None, None),
            P("tok"),
            P("tok"),
            P("tok"),
            P("tok"),
            P("tok"),
            P(("rep", "tok")),
            P(),
        ),
        check_vma=False,
    )
```

```python
import functools
import math

import jax
import jax.numpy as jnp
from jax import lax
from jax.experimental import pallas as pl
from jax.experimental.pallas import tpu as pltpu
from jax.sharding import PartitionSpec as P

D = 768
HEADS = 12
HD = 64
FF = 3072
SD = 4
CL = 128
NBLK = 96
STEP = 10
CPS = 32
WROWS = 9216
BLK = 96
ROWS = 1024
PAIRS = HEADS // 2
PW = 2 * HD
TM = 512
PART = 48
META = 16
VMEM_LIMIT = 63 << 20
FC = 768
FWD_AT = 4
BWD_AT = 2

norm_epsilon = 1e-06
beta_first = 0.9
beta_second = 0.999
adam_epsilon = 1e-08
weight_decay = 0.01
rate_matrix = 0.02
rate_vector = 0.2

BF = jnp.bfloat16
F32 = jnp.float32
I32 = jnp.int32

VMEM = pl.BlockSpec(memory_space=pltpu.VMEM)
SMEM = pl.BlockSpec(memory_space=pltpu.SMEM)
ANY = pl.BlockSpec(memory_space=pl.ANY)

NN = (((1,), (0,)), ((), ()))
NT = (((1,), (1,)), ((), ()))
TN = (((0,), (0,)), ((), ()))


def mm(a, b, dims=NN):
    return lax.dot_general(a, b, dims, preferred_element_type=F32)


def slot_positions(block_owner, slot_count):
    owners = block_owner[:, 0]
    blocks = owners.shape[0]
    shared = owners[:, None] == owners[None, :]
    before = (
        jnp.arange(blocks, dtype=jnp.int32)[None, :] < jnp.arange(blocks, dtype=jnp.int32)[:, None]
    )
    earlier = jnp.sum((shared & before).astype(jnp.int32), axis=1)
    return owners * slot_count + earlier


def adam_update(grad_now, weight_old, first_old, second_old, rate_step):
    first_new = beta_first * first_old + (1.0 - beta_first) * grad_now
    second_new = beta_second * second_old + (1.0 - beta_second) * grad_now * grad_now
    first_hat = first_new / (1.0 - beta_first**STEP)
    second_hat = second_new / (1.0 - beta_second**STEP)
    weight_new = weight_old - rate_step * (
        first_hat / (jnp.sqrt(second_hat) + adam_epsilon) + weight_decay * weight_old
    )
    return (first_new, second_new, weight_new)


def route_slots(order, seat, cap):
    cluster = order // CL
    rel = lax.rem(cluster, SD) ^ seat
    place = (cluster // SD) * CL + lax.rem(order, CL) + 1
    chosen = lax.broadcasted_iota(I32, (8, ROWS), 0) == rel
    chosen_low = jnp.where(chosen, 1.0, 0.0).astype(BF)
    before = lax.broadcasted_iota(I32, (ROWS, ROWS), 0) < lax.broadcasted_iota(I32, (ROWS, ROWS), 1)
    before_low = jnp.where(before, 1.0, 0.0).astype(BF)
    running = mm(chosen_low, before_low)
    rank = jnp.sum(jnp.where(chosen, running, 0.0), axis=0, keepdims=True).astype(I32)
    return rel * cap + rank, place


def slot_matrix(slots, at, cap):
    rows = lax.broadcasted_iota(I32, (cap, ROWS), 0) + at * cap
    return jnp.where(rows == slots, 1.0, 0.0).astype(BF)


def send_kernel(cap, tokens, cotangent, order, send_x, send_c, meta):
    seat = lax.rem(lax.axis_index("tok"), SD)
    slots, place = route_slots(order[...], seat, cap)
    digits = jnp.concatenate([place // CL, lax.rem(place, CL)] + [place * 0] * 6, axis=0).astype(F32).astype(BF)
    for at in range(SD):
        picked = slot_matrix(slots, at, cap)
        send_x[at] = mm(picked, tokens[...]).astype(BF)
        send_c[at] = mm(picked, cotangent[...]).astype(BF)
        coded = mm(digits, picked, NT)
        line = jnp.concatenate([coded[0:1], coded[1:2]], axis=1)
        meta[at] = jnp.broadcast_to(line, (META, D)).astype(BF)


def remote(src, dst, send_sem, recv_sem, tok, rep):
    return pltpu.make_async_remote_copy(
        src_ref=src,
        dst_ref=dst,
        send_sem=send_sem,
        recv_sem=recv_sem,
        device_id={"tok": tok, "rep": rep},
        device_id_type=pl.DeviceIdType.MESH,
    )


def loop(n, body):
    def run(i, c):
        body(i)
        return c

    lax.fori_loop(0, n, run, 0)


class Place:
    def __init__(self):
        self.me = me = lax.axis_index("tok")
        self.z = z = lax.axis_index("rep")
        core, x, y = me % 2, (me // 2) % 2, me // 4
        self.twin = me + 1 - 2 * core
        self.xn = me + 2 - 4 * x
        self.yn = me + 4 - 8 * y
        self.dn = self.xn + 4 - 8 * y
        self.side = z % 2
        self.zp = z + 1 - 2 * self.side

    def twin_of(self, tok):
        return tok + 1 - 2 * (tok % 2)

    def greet(self, peers):
        barrier = pltpu.get_barrier_semaphore()
        for tok, rep in peers:
            pl.semaphore_signal(
                barrier, inc=1, device_id={"tok": tok, "rep": rep}, device_id_type=pl.DeviceIdType.MESH
            )
        return lambda: pl.semaphore_wait(barrier, len(peers))


def seat_matrix(meta, first, rows, cap):
    hi = jnp.concatenate([meta[k, 0:8, 0:cap] for k in range(SD)], axis=1).astype(F32)[0:1]
    lo = jnp.concatenate([meta[k, 0:8, cap : 2 * cap] for k in range(SD)], axis=1).astype(F32)[0:1]
    at = (hi * CL + lo).astype(I32)
    seats = lax.broadcasted_iota(I32, (rows, SD * cap), 0) + (first + 1)
    return jnp.where(seats == at, 1.0, 0.0).astype(BF)


def seat_part(meta, k, cap):
    hi = meta[k, 0:8, 0:cap].astype(F32)[0:1]
    lo = meta[k, 0:8, cap : 2 * cap].astype(F32)[0:1]
    at = (hi * CL + lo).astype(I32)
    seats = lax.broadcasted_iota(I32, (ROWS, cap), 0) + 1
    return jnp.where(seats == at, 1.0, 0.0).astype(BF)


def seat_rows(meta, blocks, cap, to):
    def body(t):
        r0 = pl.multiple_of(t * 256, 256)
        rows = blocks[...].reshape(SD * cap, D)
        to[pl.ds(r0, 256), :] = mm(seat_matrix(meta, r0, 256, cap), rows).astype(BF)

    loop(ROWS // 256, body)


def seat_kernel(cap, blocks, meta, to):
    seat_rows(meta, blocks, cap, to)


def gather_kernel(
    cap,
    count,
    tokens_h,
    cotangent_h,
    order,
    master_h,
    vector,
    owner_of,
    slots,
    x_c,
    cot_0,
    cot_1,
    cot_2,
    cot_3,
    recv_meta,
    vecs,
    b_u,
    occupancy,
    positions,
    tokens,
    cotangent,
    master,
    own,
    send_x,
    send_c,
    meta,
    recv_x,
    got_meta,
    slot_of,
    digits,
    mine,
    by_z,
    by_tok,
    x_s,
    x_r,
    y_s,
    y_r,
    d_s,
    d_r,
    zx_s,
    zx_r,
    zd_s,
    zd_r,
    zy_s,
    zy_r,
    p_s,
    p_r,
    row_s,
    row_r,
    z_s,
    z_r,
    t_s,
    t_r,
    local_s,
):
    at = Place()
    me, z, side = at.me, at.z, at.side
    n_tok, n_rep = 8, 4
    peers = [((me + d) % n_tok, z) for d in range(1, n_tok)] + [(me, (z + d) % n_rep) for d in range(1, n_rep)]
    fetch = [
        pltpu.make_async_copy(src, dst, local_s.at[i])
        for i, (src, dst) in enumerate(((master_h, master), (tokens_h, tokens), (cotangent_h, cotangent)))
    ]
    for copy in fetch:
        copy.start()
    wait_peers = at.greet(peers)
    fetch[0].wait()

    last = count - 1

    def near(j):
        return side * last + (1 - 2 * side) * j

    def far(j):
        return (1 - side) * last - (1 - 2 * side) * j

    few_x, few_d, few_y = 12 * count // 26, 12 * count // 26, 8 * count // 26
    most_x, most_d, most_y = count - few_x, count - few_d, count - few_y

    def piece(owner, s):
        return slots.at[owner * count + s]

    def to_x(s):
        return remote(own.at[s], piece(me, s), x_s.at[s], x_r.at[s], at.xn, z)

    def to_y(s):
        return remote(own.at[s], piece(me, s), y_s.at[s], y_r.at[s], at.yn, z)

    def on_y(s):
        return remote(piece(at.xn, s), piece(at.xn, s), d_s.at[s], d_r.at[s], at.yn, z)

    def x_on_z(s):
        return remote(piece(at.xn, s), piece(at.xn, s), zx_s.at[s], zx_r.at[s], me, at.zp)

    def d_on_z(s):
        return remote(piece(at.dn, s), piece(at.dn, s), zd_s.at[s], zd_r.at[s], me, at.zp)

    def y_on_z(s):
        return remote(piece(at.yn, s), piece(at.yn, s), zy_s.at[s], zy_r.at[s], me, at.zp)

    def x_in(s):
        return remote(own.at[s], piece(at.xn, s), x_s.at[s], x_r.at[s], at.xn, z)

    def y_in(s):
        return remote(own.at[s], piece(at.yn, s), y_s.at[s], y_r.at[s], at.yn, z)

    def d_in(s):
        return remote(own.at[s], piece(at.dn, s), d_s.at[s], d_r.at[s], at.yn, z)

    owners = (me, at.xn, at.yn, at.dn)

    def near_run(q, j0, j1):
        return (q, (1 - side) * j0 + side * (count - j1), j1 - j0)

    def far_run(q, j0, j1):
        return (q, side * j0 + (1 - side) * (count - j1), j1 - j0)

    runs = (
        (0, 0, count),
        near_run(2, 0, few_y),
        near_run(1, 0, most_x),
        near_run(3, 0, most_d),
        far_run(1, 0, few_x),
        near_run(2, few_y, most_y),
        far_run(2, 0, few_y),
        far_run(3, 0, few_d // 2),
        far_run(3, few_d // 2, few_d - 2),
        far_run(3, few_d - 2, few_d),
    )

    def to_twin(i):
        q, s, n = runs[i]
        src = own if q == 0 else slots.at[pl.ds(owners[q] * count + s, n)]
        dst = slots.at[pl.ds(owners[q] * count + s, n)]
        return remote(src, dst, p_s.at[i], p_r.at[i], at.twin, z)

    def cast(j):
        own[near(j)] = master[near(j)].astype(BF)

    loop(most_x, cast)
    wait_peers()
    loop(most_x, lambda j: to_x(near(j)).start())
    loop(few_y, lambda j: to_y(near(j)).start())
    loop(count - most_x, lambda j: cast(most_x + j))
    to_twin(0).start()
    keep = pltpu.make_async_copy(own, slots.at[pl.ds(me * count, count)], local_s.at[3])
    keep.start()

    seat = me % SD
    seats = (me, at.twin, at.xn, at.twin_of(at.xn))
    rows_of = ((meta, got_meta), (send_x, recv_x))

    def row_copy(i, k):
        src, dst = rows_of[i]
        return remote(src.at[k], dst.at[k], row_s.at[i, k], row_r.at[i, k], seats[k], z)

    put_c = [
        pltpu.make_async_copy(send_c.at[k], to, local_s.at[4 + k])
        for k, to in enumerate((cot_0, cot_1, cot_2, cot_3))
    ]

    def route():
        fetch[1].wait()
        fetch[2].wait()
        slots_here, place = route_slots(order[...], seat, cap)
        slot_of[...] = slots_here
        digits[...] = (
            jnp.concatenate([place // CL, lax.rem(place, CL)] + [place * 0] * 6, axis=0).astype(F32).astype(BF)
        )

    def sort_tokens(k):
        picked = slot_matrix(slot_of[...], k, cap)
        send_x[k] = mm(picked, tokens[...]).astype(BF)
        coded = mm(digits[...], picked, NT)
        line = jnp.concatenate([coded[0:1], coded[1:2]], axis=1)
        meta[k] = jnp.broadcast_to(line, (META, D)).astype(BF)
        for i in range(2):
            if k:
                row_copy(i, k).start()
            else:
                src, dst = rows_of[i]
                dst[0] = src[0]

    def sort_cotangent(k):
        send_c[k] = mm(slot_matrix(slot_of[...], k, cap), cotangent[...]).astype(BF)
        put_c[k].start()

    def z_copy(d):
        return remote(by_z.at[0], by_z.at[d], z_s.at[d], z_r.at[d], me, (z + d) % n_rep)

    def t_copy(d):
        return remote(mine, by_tok.at[d], t_s.at[d], t_r.at[d], (me + d) % n_tok, z)

    def count_rows():
        residue = lax.rem(me // SD * CPS + order[...] // CL, n_tok)
        hit = lax.broadcasted_iota(I32, (128, ROWS), 0) == residue
        by_z[0] = mm(jnp.ones((8, ROWS), BF), jnp.where(hit, 1.0, 0.0).astype(BF), NT)
        for d in range(1, n_rep):
            z_copy(d).start()
        for i in range(9):
            mine[i : i + 1] = vector[i * 128 : (i + 1) * 128].reshape(1, 128).astype(BF).astype(F32)
        block_row = lax.broadcasted_iota(I32, (NBLK, NBLK), 0)
        block_col = lax.broadcasted_iota(I32, (NBLK, NBLK), 1)
        by_col = owner_of[...].astype(F32)
        by_row = lane_sum(jnp.where(block_row == block_col, by_col, 0.0))
        earlier = jnp.where((by_row == by_col) & (block_row < block_col), 1.0, 0.0)
        positions[...] = (by_col * (count * PART // BLK) + jnp.sum(earlier, axis=0, keepdims=True)).astype(I32)

    def share_vectors():
        for d in range(1, n_rep):
            z_copy(d).wait()
        mine[16:24] = by_z[0] + by_z[1] + by_z[2] + by_z[3]
        for d in range(1, n_tok):
            t_copy(d).start()

    def lay_out_vectors():
        by_tok[0] = mine[...]
        for d in range(1, n_tok):
            t_copy(d).wait()
        for owner in range(n_tok):
            share = by_tok[(me + n_tok - owner) % n_tok]
            occupancy[owner : owner + 1, :] = share[16:17, 0:n_tok].astype(I32)
            for i in range(9):
                chunk = owner * 9 + i
                row, lane = chunk // 6, chunk % 6 * 128
                if row < 8:
                    vecs[row : row + 1, lane : lane + 128] = share[i : i + 1]
                else:
                    lane += (row - 8) * D
                    b_u[:, lane : lane + 128] = share[i : i + 1]

    between = {
        1: lambda: (route(), sort_tokens(2)),
        3: lambda: sort_tokens(3),
        5: lambda: sort_tokens(1),
        7: lambda: (sort_tokens(0), count_rows()),
        9: lambda: sort_cotangent(1),
        11: lambda: sort_cotangent(2),
        13: lambda: sort_cotangent(3),
    }
    for j in range(most_x):
        x_in(near(j)).wait_recv()
        if j < most_d:
            on_y(near(j)).start()
        if j < few_x:
            x_on_z(near(j)).start()
        if j < few_y:
            y_in(near(j)).wait_recv()
            y_on_z(near(j)).start()
        if j == few_y:
            to_twin(1).start()
        if j in between:
            between[j]()
    to_twin(2).start()
    loop(most_y - few_y, lambda j: to_y(near(few_y + j)).start())
    share_vectors()
    sort_cotangent(0)

    def diagonal(j):
        d_in(near(j)).wait_recv()
        d_on_z(near(j)).start()

    loop(few_d, diagonal)
    loop(most_d - few_d, lambda j: d_in(near(few_d + j)).wait_recv())
    to_twin(3).start()
    loop(few_x, lambda j: x_on_z(far(j)).wait_recv())
    to_twin(4).start()
    lay_out_vectors()
    loop(most_y - few_y, lambda j: y_in(near(few_y + j)).wait_recv())
    to_twin(5).start()
    loop(few_y, lambda j: y_on_z(far(j)).wait_recv())
    to_twin(6).start()
    for i in (0, 1):
        for k in (2, 3, 1):
            row_copy(i, k).wait_recv()
    recv_meta[...] = got_meta[...]
    seat_rows(got_meta, recv_x, cap, x_c)
    done = 0
    for i, upto in ((7, few_d // 2), (8, few_d - 2), (9, few_d)):
        loop(upto - done, lambda j, done=done: d_on_z(far(done + j)).wait_recv())
        to_twin(i).start()
        done = upto

    for i in range(2):
        for k in (2, 3, 1):
            row_copy(i, k).wait_send()
    for copy in put_c:
        copy.wait()
    keep.wait()

    loop(most_x, lambda j: to_x(near(j)).wait_send())
    loop(most_y, lambda j: to_y(near(j)).wait_send())
    loop(most_d, lambda j: on_y(near(j)).wait_send())
    loop(few_x, lambda j: x_on_z(near(j)).wait_send())
    loop(few_d, lambda j: d_on_z(near(j)).wait_send())
    loop(few_y, lambda j: y_on_z(near(j)).wait_send())
    for i in range(len(runs)):
        to_twin(i).wait()


def gather_all(cap, tokens, cotangent, order, master, vector, block_owner):
    count = master.shape[0] * BLK // PART
    rows = jax.ShapeDtypeStruct((ROWS, D), BF)
    part = jax.ShapeDtypeStruct((cap, D), BF)
    dma = pltpu.SemaphoreType.DMA
    block = pltpu.VMEM((SD, cap, D), BF)
    meta = pltpu.VMEM((SD, META, D), BF)
    return pl.pallas_call(
        functools.partial(gather_kernel, cap, count),
        out_shape=(
            jax.ShapeDtypeStruct((8 * count, PART, D), BF),
            rows,
            part,
            part,
            part,
            part,
            jax.ShapeDtypeStruct((SD, META, D), BF),
            jax.ShapeDtypeStruct((8, D), F32),
            jax.ShapeDtypeStruct((1, FF), F32),
            jax.ShapeDtypeStruct((8, 8), I32),
            jax.ShapeDtypeStruct((1, NBLK), I32),
        ),
        in_specs=[ANY, ANY, VMEM, ANY, VMEM, VMEM],
        out_specs=(ANY, VMEM) + (ANY,) * SD + (VMEM,) * 5,
        scratch_shapes=[
            pltpu.VMEM((ROWS, D), BF),
            pltpu.VMEM((ROWS, D), BF),
            pltpu.VMEM((count, PART, D), F32),
            pltpu.VMEM((count, PART, D), BF),
            block,
            block,
            meta,
            block,
            meta,
            pltpu.VMEM((1, ROWS), I32),
            pltpu.VMEM((8, ROWS), BF),
            pltpu.VMEM((24, 128), F32),
            pltpu.VMEM((4, 8, 128), F32),
            pltpu.VMEM((8, 24, 128), F32),
        ]
        + [dma((count,))] * 12
        + [dma((10,))] * 2
        + [dma((2, SD))] * 2
        + [dma((4,))] * 2
        + [dma((8,))] * 2
        + [dma((8,))],
        compiler_params=pltpu.CompilerParams(collective_id=0, has_side_effects=True, vmem_limit_bytes=VMEM_LIMIT),
        cost_estimate=pl.CostEstimate(flops=8 * ROWS * ROWS * D, bytes_accessed=64 << 20, transcendentals=0),
        name="gather",
    )(tokens, cotangent, order, master.reshape(count, PART, D), vector, block_owner.reshape(1, NBLK))


def return_kernel(cap, order, *refs):
    outs, ings, (out, ing, entropy) = refs[:SD], refs[SD : 2 * SD], refs[2 * SD :]
    seat = lax.rem(lax.axis_index("tok"), SD)
    slots, _ = route_slots(order[...], seat, cap)
    picked = jnp.concatenate([slot_matrix(slots, at, cap) for at in range(SD)], axis=0)
    for to, blocks in ((out, outs), (ing, ings)):
        rows = jnp.concatenate([block[0:cap, :] for block in blocks], axis=0)
        to[...] = mm(picked, rows, TN).astype(BF)
    line = jnp.concatenate([block[cap : cap + 8, 0:cap] for block in outs], axis=1)
    entropy[...] = mm(line, picked)[0:1].astype(BF)


def swap_blocks(blocks):
    n = lax.axis_size("tok")
    parts = [blocks[0]]
    for k in range(1, SD):
        parts.append(lax.ppermute(blocks[k], "tok", [(i, i ^ k) for i in range(n)]))
    return parts


def reduce_kernel(
    cap,
    count,
    split,
    grads,
    vec,
    order,
    out_0,
    out_1,
    out_2,
    out_3,
    ing_0,
    ing_1,
    ing_2,
    ing_3,
    total,
    vec_out,
    output,
    input_grad,
    entropy,
    out_v,
    ing_v,
    slot_of,
    a,
    tw,
    rd,
    rx,
    ry,
    o,
    rz1,
    pz,
    rz2,
    fz,
    vt,
    va,
    vb,
    vc,
    a_l,
    keep_l,
    p_s,
    p_r,
    d_s,
    d_r,
    x_s,
    x_r,
    y_s,
    y_r,
    z1_s,
    z1_r,
    z2_s,
    z2_r,
    z3_s,
    z3_r,
    t_s,
    t_r,
    v_s,
    v_r,
    row_l,
):
    at = Place()
    me, z = at.me, at.z
    n_tok, n_rep = 8, 4
    peers = [((me + d) % n_tok, z) for d in range(1, n_tok)] + [(me, (z + d) % n_rep) for d in range(1, n_rep)]
    wait_peers = at.greet(peers)
    owners = (me, at.xn, at.yn, at.dn)

    def load(q):
        return pltpu.make_async_copy(grads.at[pl.ds(owners[q] * count, count)], a.at[q], a_l.at[q])

    for q in (3, 1, 2, 0):
        load(q).start()
    rows_in = [
        pltpu.make_async_copy(src, to.at[k], row_l.at[i, k])
        for i, (blocks, to) in enumerate((((out_0, out_1, out_2, out_3), out_v), ((ing_0, ing_1, ing_2, ing_3), ing_v)))
        for k, src in enumerate(blocks)
    ]
    for copy in rows_in:
        copy.start()
    wait_peers()

    groups = [(g, g * (count // 4), count // 4 if g < 3 else count - 3 * (count // 4)) for g in range(4)]

    def to_twin(q, group):
        g, s, n = group
        src = grads.at[pl.ds(at.twin_of(owners[q]) * count + s, n)]
        return remote(src, tw.at[q, pl.ds(s, n)], p_s.at[q, g], p_r.at[q, g], at.twin, z)

    def d_y(s):
        return remote(a.at[3, s], rd.at[s], d_s.at[s], d_r.at[s], at.yn, z)

    def d_x(s):
        return remote(a.at[3, s], rd.at[s], d_s.at[s], d_r.at[s], at.xn, z)

    def to_x(s):
        return remote(a.at[1, s], rx.at[s], x_s.at[s], x_r.at[s], at.xn, z)

    def to_y(s):
        return remote(a.at[2, s], ry.at[s], y_s.at[s], y_r.at[s], at.yn, z)

    def z_in(s):
        return remote(o.at[s], rz1.at[s], z1_s.at[s], z1_r.at[s], me, at.zp)

    def z_swap(s):
        return remote(pz.at[s], rz2.at[s], z2_s.at[s], z2_r.at[s], me, n_rep - 1 - z)

    def z_out(s):
        return remote(fz.at[s], fz.at[s], z3_s.at[s], z3_r.at[s], me, at.zp)

    def keep(s):
        return pltpu.make_async_copy(fz.at[s], total.at[s], keep_l.at[s])

    for group in groups:
        for q in (3, 1, 2, 0):
            to_twin(q, group).start()

    def v_tok(d):
        return remote(vec.at[(me + d) % n_tok], vt.at[d], t_s.at[d], t_r.at[d], (me + d) % n_tok, z)

    def v_rep(i, src):
        return remote(src, vb.at[i], v_s.at[i], v_r.at[i], me, at.zp if i == 0 else (z + 2) % n_rep)

    for d in range(1, n_tok):
        v_tok(d).start()

    def join(q, s):
        return a[q, s] + tw[q, s]

    def first(s, send):
        a[3, s] = join(3, s)
        send(s).start()

    def plain(q, s, send):
        a[q, s] = join(q, s)
        send(s).start()

    def joined(q, s, arrived, send):
        arrived(s).wait_recv()
        a[q, s] = join(q, s) + rd[s]
        send(s).start()

    inner = (z == 1) | (z == 2)
    outer = (z == 0) | (z == 3)

    def own(s):
        to_x(s).wait_recv()
        to_y(s).wait_recv()
        o[s] = join(0, s) + (rx[s] + ry[s])
        pl.when(outer)(lambda: z_in(s).start())

    def middle(s):
        @pl.when(inner)
        def _():
            z_in(s).wait_recv()
            pz[s] = o[s] + rz1[s]
            z_swap(s).start()

    def last(s):
        @pl.when(inner)
        def _():
            z_swap(s).wait_recv()
            fz[s] = pz[s] + rz2[s]
            z_out(s).start()
            keep(s).start()

    def taken(s):
        @pl.when(outer)
        def _():
            z_out(s).wait_recv()
            keep(s).start()

    def pick_rows(i):
        ts = pl.ds(pl.multiple_of(i * 256, 256), 256)
        hit = lax.broadcasted_iota(I32, (SD * cap, 256), 0) == slot_of[:, ts]
        picked = jnp.where(hit, 1.0, 0.0).astype(BF)
        outs = jnp.concatenate([out_v[k, 0:cap, :] for k in range(SD)], axis=0)
        ings = jnp.concatenate([ing_v[k] for k in range(SD)], axis=0)
        both = mm(picked, jnp.concatenate([outs, ings], axis=1), TN)
        output[ts, :] = both[:, 0:D].astype(BF)
        input_grad[ts, :] = both[:, D:].astype(BF)
        line = jnp.concatenate([out_v[k, cap : cap + 8, 0:cap] for k in range(SD)], axis=1)
        entropy[:, ts] = mm(line, picked)[0:1].astype(BF)

    for q in (3, 1, 2, 0):
        load(q).wait()

    def steps(i, lag, more):
        s = i - lag
        by_x = (s % 2 == 0) & (s < 2 * split)
        live = (s >= 0) & (s < count)
        pl.when(live & by_x)(lambda: more(s, True))
        pl.when(live & jnp.logical_not(by_x))(lambda: more(s, False))

    def steps_of(i, lag, more):
        pl.when((i >= lag) & (i < count + lag))(lambda: more(i - lag))

    def round_of(i):
        for group in groups:

            @pl.when(i == group[1])
            def _(group=group):
                to_twin(3, group).wait_recv()

            @pl.when(i == group[1] + 1)
            def _(group=group):
                to_twin(1, group).wait_recv()
                to_twin(2, group).wait_recv()

            @pl.when(i == group[1] + 6)
            def _(group=group):
                to_twin(0, group).wait_recv()

        steps(i, 0, lambda s, by_x: first(s, d_x if by_x else d_y))
        steps(i, 1, lambda s, by_x: plain(1, s, to_x) if by_x else plain(2, s, to_y))
        steps(i, 3, lambda s, by_x: joined(2, s, d_x, to_y) if by_x else joined(1, s, d_y, to_x))
        steps_of(i, 6, own)
        steps_of(i, 8, middle)
        steps_of(i, 10, last)
        steps_of(i, 12, taken)

    loop(3, round_of)
    for copy in rows_in:
        copy.wait()
    slots_here, _ = route_slots(order[...], me % SD, cap)
    slot_of[...] = slots_here

    v_sum = vec[me]
    for d in range(1, n_tok):
        v_tok(d).wait()
        v_sum = v_sum + vt[d]
    va[...] = v_sum
    v_rep(0, va).start()

    def four_rounds(i):
        loop(4, lambda j: round_of(3 + 4 * i + j))
        pick_rows(i)

    four_rounds(0)
    v_rep(0, va).wait()
    vc[...] = va[...] + vb[0]
    v_rep(1, vc).start()
    loop(3, lambda i: four_rounds(1 + i))
    loop(count + 12 - 19, lambda i: round_of(19 + i))
    v_rep(1, vc).wait()
    vec_out[...] = vc[...] + vb[1]

    for group in groups:
        for q in range(4):
            to_twin(q, group).wait_send()

    def sent(s):
        d_y(s).wait_send()
        to_x(s).wait_send()
        to_y(s).wait_send()
        keep(s).wait()

    loop(count, sent)

    @pl.when(outer)
    def _():
        loop(count, lambda s: z_in(s).wait_send())

    @pl.when(inner)
    def _():
        def back(s):
            z_swap(s).wait_send()
            z_out(s).wait_send()

        loop(count, back)


def reduce_all(cap, grads, shares, order, outs, ings, count):
    dma = pltpu.SemaphoreType.DMA
    count = count * BLK // PART
    part = pltpu.VMEM((count, PART, D), BF)
    whole = pltpu.VMEM((4, count, PART, D), BF)
    line = pltpu.VMEM((16, 128), F32)
    rows = jax.ShapeDtypeStruct((ROWS, D), BF)
    total, vec, output, input_grad, entropy = pl.pallas_call(
        functools.partial(reduce_kernel, cap, count, count // 2),
        out_shape=(
            jax.ShapeDtypeStruct((count, PART, D), BF),
            jax.ShapeDtypeStruct((16, 128), F32),
            rows,
            rows,
            jax.ShapeDtypeStruct((1, ROWS), BF),
        ),
        in_specs=[ANY, VMEM, VMEM] + [ANY] * (2 * SD),
        out_specs=(ANY,) + (VMEM,) * 4,
        scratch_shapes=[
            pltpu.VMEM((SD, cap + META, D), BF),
            pltpu.VMEM((SD, cap, D), BF),
            pltpu.VMEM((1, ROWS), I32),
            whole,
            whole,
        ]
        + [part] * 8
        + [pltpu.VMEM((8, 16, 128), F32), line, pltpu.VMEM((2, 16, 128), F32), line]
        + [dma((4,)), dma((count,))]
        + [dma((4, 4))] * 2
        + [dma((count,))] * 12
        + [dma((8,))] * 2
        + [dma((2,))] * 2
        + [dma((2, SD))],
        compiler_params=pltpu.CompilerParams(collective_id=1, has_side_effects=True, vmem_limit_bytes=VMEM_LIMIT),
        cost_estimate=pl.CostEstimate(flops=4 * ROWS * ROWS * D, bytes_accessed=64 << 20, transcendentals=0),
        name="reduce",
    )(grads.reshape(-1, PART, D), shares, order, *outs, *ings)
    return total.reshape(-1, BLK, D), vec, output, input_grad, entropy


V_BQ, V_BV, V_BO, V_BD, V_G1, V_C1, V_G2, V_C2 = range(8)


def inverse(x):
    r = pl.reciprocal(x, approx=True)
    return r * (2.0 - x * r)


def erf_parts(v):
    t = inverse(1.0 + (0.3275911 / math.sqrt(2.0)) * jnp.abs(v))
    e = jnp.exp2((v * v) * (-0.5 / math.log(2.0)))
    poly = 0.5 * 1.061405429
    for c in (-1.453152027, 1.421413741, -0.284496736, 0.254829592):
        poly = poly * t + 0.5 * c
    tail = poly * (t * e)
    return jnp.where(v >= 0.0, 1.0 - tail, tail), e


def lane_sum(x):
    return jnp.sum(x, axis=1, keepdims=True)


def gelu_parts(v):
    phi, e = erf_parts(v)
    return v * phi, phi + v * (e * (1.0 / math.sqrt(2.0 * math.pi)))


def weight_copies(pos, slots, w, sem, first):
    def copy(b):
        return pltpu.make_async_copy(slots.at[pos[first + b]], w.at[pl.ds(b * BLK, BLK)], sem)

    n = w.shape[0] // BLK
    return (lambda: loop(n, lambda b: copy(b).start())), (lambda: loop(n, lambda b: copy(b).wait()))


def halves_of_heads():
    lane = lax.broadcasted_iota(I32, (1, PW), 1)
    m0 = jnp.where(lane < HD, 1.0, 0.0).astype(BF)
    m1 = jnp.where(lane < HD, 0.0, 1.0).astype(BF)
    return lambda pair: jnp.concatenate([pair * m0, pair * m1], axis=0)


def tile_rows(t):
    return pl.ds(pl.multiple_of(t * TM, TM), TM)


def forward_kernel(
    cap,
    pos,
    slots,
    vecs,
    b_u,
    x_h,
    meta,
    back_0,
    back_1,
    back_2,
    back_3,
    heads_h,
    act_h,
    hid_h,
    q_h,
    k_h,
    v_h,
    p_h,
    slope_h,
    n1_h,
    n2_h,
    rs1_h,
    rs2_h,
    wqkv,
    wo,
    wu,
    wd,
    x_c,
    heads,
    act,
    hid,
    q,
    k,
    v,
    p_all,
    slope,
    n1,
    n2,
    rs1,
    rs2,
    out_c,
    ent,
    hid_t,
    w_sem,
    x_sem,
    o_sem,
):
    inv = 1.0 / math.sqrt(HD)
    get_x = pltpu.make_async_copy(x_h, x_c, x_sem)
    get_x.start()
    weights = [
        weight_copies(pos, slots, w, w_sem.at[i], first)
        for i, (w, first) in enumerate(((wqkv, 0), (wo, 24), (wu, 32), (wd, 64)))
    ]
    for start, _ in weights:
        start()
    get_x.wait()
    apart = halves_of_heads()

    def vec(i):
        return vecs[i : i + 1, :]

    saved = (
        (heads, heads_h),
        (act, act_h),
        (hid, hid_h),
        (q, q_h),
        (k, k_h),
        (v, v_h),
        (slope, slope_h),
        (n1, n1_h),
        (n2, n2_h),
        (rs1, rs1_h),
        (rs2, rs2_h),
    )

    def save(t, i):
        src, dst = saved[i]
        return pltpu.make_async_copy(src.at[tile_rows(t)], dst.at[tile_rows(t)], o_sem.at[i])

    def save_p(t):
        n = TM // CL
        cs = pl.ds(t * n, n)
        return pltpu.make_async_copy(p_all.at[cs], p_h.at[cs], o_sem.at[len(saved)])

    def normal(r, n, rs, rows):
        c = r - lane_sum(r) * (1.0 / D)
        scale = lax.rsqrt(lane_sum(c * c) * (1.0 / D) + norm_epsilon)
        rs[rows, :] = jnp.broadcast_to(scale, (TM, 128))
        n[rows, :] = c * scale

    def tile(t):
        rows = tile_rows(t)
        first = t == 0
        pl.when(first)(weights[0][1])
        x = x_c[rows, :]
        q[rows, :] = ((mm(x, wqkv[0:D, :]) + vec(V_BQ)).astype(BF).astype(F32) * inv).astype(BF)
        k[rows, :] = mm(x, wqkv[D : 2 * D, :]).astype(BF)
        v[rows, :] = (mm(x, wqkv[2 * D :, :]) + vec(V_BV)).astype(BF)

        def attend(c):
            groups = [pl.ds(pl.multiple_of(t * TM + (FWD_AT * c + i) * CL, CL), CL) for i in range(FWD_AT)]
            pairs = [(i, p, slice(p * PW, (p + 1) * PW)) for i in range(FWD_AT) for p in range(PAIRS)]
            scores = [mm(apart(k[groups[i], ps]), q[groups[i], ps], NT) for i, _, ps in pairs]
            total = [jnp.zeros((1, CL), F32)] * FWD_AT
            probs = []
            for (i, _, _), both in zip(pairs, scores):
                halves = []
                for h in range(2):
                    sh = both[h * CL : (h + 1) * CL]
                    sh = sh - jnp.max(sh, axis=0, keepdims=True)
                    e = jnp.exp(sh)
                    tot = jnp.sum(e, axis=0, keepdims=True)
                    r = 1.0 / tot
                    total[i] += jnp.log(tot) - jnp.sum(e * sh, axis=0, keepdims=True) * r
                    halves.append((e * r).astype(BF))
                probs.append(jnp.concatenate(halves, axis=0))
            mixed = [mm(w, apart(v[groups[i], ps]), TN).astype(BF) for (i, _, ps), w in zip(pairs, probs)]
            for (i, p, ps), w, o in zip(pairs, probs, mixed):
                p_all[t * (TM // CL) + FWD_AT * c + i, p] = w
                heads[groups[i], ps] = o
            for i in range(FWD_AT):
                ent[:, groups[i]] = jnp.broadcast_to(total[i] * (1.0 / HEADS), (8, CL))

        loop(TM // CL // FWD_AT, attend)
        for i in (0, 3, 4, 5):
            save(t, i).start()
        save_p(t).start()
        pl.when(first)(weights[1][1])
        normal(x_c[rows, :].astype(F32) + mm(heads[rows, :], wo[...]) + vec(V_BO), n1, rs1, rows)
        hidden = n1[rows, :] * vec(V_G1) + vec(V_C1)
        hid[rows, :] = hidden.astype(BF)
        hid_t[...] = hidden
        pl.when(first)(weights[2][1])

        def widen(f):
            parts = [pl.ds(pl.multiple_of((2 * f + i) * FC, FC), FC) for i in range(2)]
            ups = [mm(hid[rows, :], wu[fs, :], NT) for fs in parts]
            for fs, up in zip(parts, ups):
                g, g_slope = gelu_parts(up + b_u[:, fs])
                act[rows, fs] = g.astype(BF)
                slope[rows, fs] = g_slope.astype(BF)

        loop(FF // FC // 2, widen)
        for i in (1, 2, 6, 7, 9):
            save(t, i).start()
        pl.when(first)(weights[3][1])
        normal(hid_t[...] + mm(act[rows, :], wd[...]) + vec(V_BD), n2, rs2, rows)
        out_c[rows, :] = (n2[rows, :] * vec(V_G2) + vec(V_C2)).astype(BF)
        for i in (8, 10):
            save(t, i).start()

    loop(ROWS // TM, tile)

    for j, back in enumerate((back_0, back_1, back_2, back_3)):
        own = seat_part(meta, j, cap)
        back[0:cap, :] = mm(own, out_c[...], TN).astype(BF)
        line = mm(ent[...].astype(BF), own)
        back[cap:, :] = jnp.concatenate([line, line], axis=1)[0:1].astype(BF) * jnp.ones((META, 1), BF)

    def saved_all(t):
        for i in range(len(saved)):
            save(t, i).wait()
        save_p(t).wait()

    loop(ROWS // TM, saved_all)


def shape_of(kind, *shape):
    return jax.ShapeDtypeStruct(shape, kind)


def saved_shapes():
    rows, wide = ((ROWS, D), BF), ((ROWS, FF), BF)
    probs = ((ROWS // CL, PAIRS, 2 * CL, CL), BF)
    full, thin = ((ROWS, D), F32), ((ROWS, 128), F32)
    return rows, wide, probs, full, thin


def forward(cap, positions, slots, vecs, b_u, x_c, meta):
    rows, wide, probs, full, thin = saved_shapes()
    kept = (rows, wide, rows, rows, rows, rows, probs, wide, full, full, thin, thin)
    dma = pltpu.SemaphoreType.DMA
    return pl.pallas_call(
        functools.partial(forward_kernel, cap),
        out_shape=(shape_of(BF, cap + META, D),) * SD + tuple(shape_of(kind, *shape) for shape, kind in kept),
        in_specs=[SMEM, ANY, VMEM, VMEM, ANY, VMEM],
        out_specs=(VMEM,) * SD + (ANY,) * len(kept),
        scratch_shapes=[
            pltpu.VMEM((3 * D, D), BF),
            pltpu.VMEM((D, D), BF),
            pltpu.VMEM((FF, D), BF),
            pltpu.VMEM((FF, D), BF),
            pltpu.VMEM(*rows),
        ]
        + [pltpu.VMEM(*a) for a in kept]
        + [
            pltpu.VMEM(*rows),
            pltpu.VMEM((8, ROWS), F32),
            pltpu.VMEM((TM, D), F32),
            dma((4,)),
            dma,
            dma((12,)),
        ],
        compiler_params=pltpu.CompilerParams(vmem_limit_bytes=VMEM_LIMIT),
        cost_estimate=pl.CostEstimate(flops=2 * ROWS * WROWS * D, bytes_accessed=64 << 20, transcendentals=0),
        name="forward",
    )(positions, slots, vecs, b_u, x_c, meta)


def backward_kernel(
    cap,
    pos,
    slots,
    vecs,
    meta,
    cot_0,
    cot_1,
    cot_2,
    cot_3,
    q_h,
    k_h,
    v_h,
    p_h,
    slope_h,
    n1_h,
    n2_h,
    rs1_h,
    rs2_h,
    back_0,
    back_1,
    back_2,
    back_3,
    shares,
    d_up_h,
    d_q_h,
    d_k_h,
    d_v_h,
    d_proj_h,
    d_br_h,
    wqkv,
    wo,
    wu,
    wd,
    blocks,
    q,
    k,
    v,
    p_all,
    d_up,
    n1,
    n2,
    rs1,
    rs2,
    d_proj,
    d_br,
    ing_c,
    d_h_t,
    gvec,
    g_bu,
    w_sem,
    c_sem,
    i_sem,
    o_sem,
):
    inv = 1.0 / math.sqrt(HD)
    get_c = [
        pltpu.make_async_copy(cot, blocks.at[j], c_sem.at[j]) for j, cot in enumerate((cot_0, cot_1, cot_2, cot_3))
    ]
    for copy in get_c:
        copy.start()
    fetch = [
        pltpu.make_async_copy(src, dst, i_sem.at[i])
        for i, (src, dst) in enumerate(
            (
                (n2_h, n2),
                (rs2_h, rs2),
                (slope_h, d_up),
                (n1_h, n1),
                (rs1_h, rs1),
                (v_h, v),
                (p_h, p_all),
                (k_h, k),
                (q_h, q),
            )
        )
    ]
    weights = [
        weight_copies(pos, slots, w, w_sem.at[i], first)
        for i, (w, first) in enumerate(((wd, 64), (wu, 32), (wo, 24), (wqkv, 0)))
    ]
    fetch[0].start()
    fetch[1].start()
    weights[0][0]()
    fetch[2].start()
    weights[1][0]()
    fetch[3].start()
    fetch[4].start()
    weights[2][0]()
    for i in range(5, 9):
        fetch[i].start()
    weights[3][0]()
    gvec[...] = jnp.zeros_like(gvec)
    g_bu[...] = jnp.zeros_like(g_bu)
    shares[...] = jnp.zeros_like(shares)
    for copy in get_c:
        copy.wait()
    seat_rows(meta, blocks, cap, d_br)
    apart = halves_of_heads()

    def vec(i):
        return vecs[i : i + 1, :]

    def add_vec(i, value):
        gvec[i : i + 1, :] += jnp.sum(value, axis=0, keepdims=True)

    saved = ((d_up, d_up_h), (q, d_q_h), (k, d_k_h), (v, d_v_h), (d_proj, d_proj_h), (d_br, d_br_h))

    def save(t, i):
        src, dst = saved[i]
        return pltpu.make_async_copy(src.at[tile_rows(t)], dst.at[tile_rows(t)], o_sem.at[i])

    def norm_back(e, n, rs, gain, shift):
        add_vec(gain, e * n)
        add_vec(shift, e)
        eg = e * vec(gain)
        return rs * (eg - lane_sum(eg) * (1.0 / D) - n * (lane_sum(eg * n) * (1.0 / D)))

    def norm_two_back(t):
        rows = tile_rows(t)
        d_r2 = norm_back(d_br[rows, :].astype(F32), n2[rows, :], rs2[rows, 0:1], V_G2, V_C2)
        d_br[rows, :] = d_r2.astype(BF)
        add_vec(V_BD, d_br[rows, :].astype(F32))
        n2[rows, :] = d_r2

    def widen_back(t, columns):
        rows = tile_rows(t)
        parts = [pl.ds(pl.multiple_of(f * FC, FC), FC) for f in columns]
        ups = [mm(d_br[rows, :], wd[fs, :], NT) for fs in parts]

        def finish():
            for fs, up in zip(parts, ups):
                du = (up * d_up[rows, fs].astype(F32)).astype(BF)
                d_up[rows, fs] = du
                g_bu[:, fs] += jnp.sum(du.astype(F32), axis=0, keepdims=True)

        return finish

    def hidden_back(t):
        rows = tile_rows(t)
        return n2[rows, :] + mm(d_up[rows, :], wu[...])

    def norm_one_back(t, d_h):
        rows = tile_rows(t)
        d_r1 = norm_back(d_h, n1[rows, :], rs1[rows, 0:1], V_G1, V_C1)
        d_proj[rows, :] = d_r1.astype(BF)
        n2[rows, :] = d_r1
        add_vec(V_BO, d_proj[rows, :].astype(F32))

    def heads_back(t):
        rows = tile_rows(t)
        d_h_t[rows, :] = mm(d_proj[rows, :], wo[...], NT).astype(BF)

    def attend_back(clusters, meanwhile=lambda: None):
        pairs = [
            (c, p, pl.ds(pl.multiple_of(c * CL, CL), CL), slice(p * PW, (p + 1) * PW))
            for c in clusters
            for p in range(PAIRS)
        ]
        probs = [p_all[c, p] for c, p, _, _ in pairs]
        d_heads = [d_h_t[gr, ps] for _, _, gr, ps in pairs]
        d_probs = [mm(apart(v[gr, ps]), dh, NT) for (_, _, gr, ps), dh in zip(pairs, d_heads)]
        d_values = [
            mm(jnp.concatenate([w[0:CL], w[CL:]], axis=1), apart(dh)).astype(BF) for w, dh in zip(probs, d_heads)
        ]
        finish = meanwhile()
        d_scores = []
        for w, dw in zip(probs, d_probs):
            halves = []
            for h in range(2):
                wh = w[h * CL : (h + 1) * CL].astype(F32)
                dwh = dw[h * CL : (h + 1) * CL]
                halves.append((wh * (dwh - jnp.sum(dwh * wh, axis=0, keepdims=True))).astype(BF))
            d_scores.append(halves)
        d_keys = [
            mm(jnp.concatenate(ds, axis=1), apart(q[gr, ps])).astype(BF) for (_, _, gr, ps), ds in zip(pairs, d_scores)
        ]
        d_queries = [
            (mm(jnp.concatenate(ds, axis=0), apart(k[gr, ps]), TN) * inv).astype(BF)
            for (_, _, gr, ps), ds in zip(pairs, d_scores)
        ]
        if finish is not None:
            finish()
        for (_, _, gr, ps), dq, dk, dv in zip(pairs, d_queries, d_keys, d_values):
            q[gr, ps] = dq
            k[gr, ps] = dk
            v[gr, ps] = dv

    def rows_back(t):
        rows = tile_rows(t)
        return (
            mm(q[rows, :], wqkv[0:D, :], NT)
            + mm(k[rows, :], wqkv[D : 2 * D, :], NT)
            + mm(v[rows, :], wqkv[2 * D :, :], NT)
        )

    def rows_done(t, d_x):
        rows = tile_rows(t)
        add_vec(V_BQ, q[rows, :].astype(F32))
        add_vec(V_BV, v[rows, :].astype(F32))
        ing_c[rows, :] = (n2[rows, :] + d_x.astype(BF).astype(F32)).astype(BF)

    def save_all(t, which):
        for i in which:
            save(t, i).start()

    per = TM // CL
    fetch[0].wait()
    fetch[1].wait()
    norm_two_back(0)
    norm_two_back(1)
    weights[0][1]()
    fetch[2].wait()
    loop(FF // FC // 2, lambda f: widen_back(0, [2 * f, 2 * f + 1])())
    save_all(0, (0, 5))
    weights[1][1]()
    fetch[3].wait()
    fetch[4].wait()
    norm_one_back(0, hidden_back(0))
    weights[2][1]()
    for i in range(5, 9):
        fetch[i].wait()
    heads_back(0)
    save_all(0, (4,))
    loop(per, lambda c: attend_back([c], lambda: widen_back(1, [c])))
    save_all(0, (1, 2, 3))
    save_all(1, (0, 5))
    weights[3][1]()
    d_h = hidden_back(1)
    d_x = rows_back(0)
    norm_one_back(1, d_h)
    heads_back(1)
    rows_done(0, d_x)
    save_all(1, (4,))
    loop(per // BWD_AT, lambda c: attend_back([per + BWD_AT * c + i for i in range(BWD_AT)]))
    save_all(1, (1, 2, 3))
    rows_done(1, rows_back(1))

    for j, back in enumerate((back_0, back_1, back_2, back_3)):
        back[...] = mm(seat_part(meta, j, cap), ing_c[...], TN).astype(BF)

    for chunk in range(72):
        row, lane = chunk // 6, chunk % 6 * 128
        if row < 8:
            part = gvec[row : row + 1, lane : lane + 128]
        else:
            lane += (row - 8) * D
            part = g_bu[:, lane : lane + 128]
        shares[chunk // 9, chunk % 9 : chunk % 9 + 1, :] = part

    def saved_all(t):
        for i in range(len(saved)):
            save(t, i).wait()

    loop(ROWS // TM, saved_all)


def backward(cap, positions, slots, vecs, meta, cots, saved):
    rows, wide, probs, full, thin = saved_shapes()
    dma = pltpu.SemaphoreType.DMA
    grads = (wide, rows, rows, rows, rows, rows)
    return pl.pallas_call(
        functools.partial(backward_kernel, cap),
        out_shape=(shape_of(BF, cap, D),) * SD
        + (shape_of(F32, 8, 16, 128),)
        + tuple(shape_of(kind, *shape) for shape, kind in grads),
        in_specs=[SMEM, ANY, VMEM, VMEM] + [ANY] * (SD + 9),
        out_specs=(VMEM,) * (SD + 1) + (ANY,) * len(grads),
        scratch_shapes=[
            pltpu.VMEM((3 * D, D), BF),
            pltpu.VMEM((D, D), BF),
            pltpu.VMEM((FF, D), BF),
            pltpu.VMEM((FF, D), BF),
            pltpu.VMEM((SD, cap, D), BF),
        ]
        + [pltpu.VMEM(*a) for a in (rows, rows, rows, probs, wide, full, full, thin, thin, rows, rows, rows)]
        + [
            pltpu.VMEM(*rows),
            pltpu.VMEM((8, D), F32),
            pltpu.VMEM((1, FF), F32),
            dma((4,)),
            dma((4,)),
            dma((9,)),
            dma((6,)),
        ],
        compiler_params=pltpu.CompilerParams(vmem_limit_bytes=VMEM_LIMIT),
        cost_estimate=pl.CostEstimate(flops=2 * ROWS * WROWS * D, bytes_accessed=64 << 20, transcendentals=0),
        name="backward",
    )(positions, slots, vecs, meta, *cots, *saved)


WC = 8 * BLK


def weight_kernel(
    pos,
    x_h,
    heads_h,
    act_h,
    d_up_h,
    d_q_h,
    d_k_h,
    d_v_h,
    d_proj_h,
    hid_h,
    d_br_h,
    grads,
    x_c,
    heads,
    act,
    d_up,
    d_q,
    d_k,
    d_v,
    d_proj,
    hid,
    d_br,
    stage,
    i_sem,
    g_sem,
):
    refs = (
        (x_h, x_c),
        (d_q_h, d_q),
        (d_k_h, d_k),
        (d_v_h, d_v),
        (heads_h, heads),
        (d_proj_h, d_proj),
        (hid_h, hid),
        (d_up_h, d_up),
        (d_br_h, d_br),
        (act_h, act),
    )
    fetch = [pltpu.make_async_copy(src, dst, i_sem.at[i]) for i, (src, dst) in enumerate(refs)]
    for copy in fetch:
        copy.start()

    per = WC // BLK

    def g_copy(chunk, j, at):
        return pltpu.make_async_copy(
            stage.at[at, pl.ds(j * BLK, BLK)], grads.at[pos[chunk * per + j]], g_sem.at[at]
        )

    def put(chunk, left, right):
        at = lax.rem(chunk, 2)

        @pl.when(chunk >= 2)
        def _():
            for j in range(per):
                g_copy(chunk - 2, j, at).wait()

        stage[at] = mm(left, right, TN).astype(BF)
        for j in range(per):
            g_copy(chunk, j, at).start()

    first = 0
    for left, right, needs in (
        (x_c, d_q, (0, 1)),
        (x_c, d_k, (2,)),
        (x_c, d_v, (3,)),
        (heads, d_proj, (4, 5)),
        (d_up, hid, (6, 7)),
        (act, d_br, (8, 9)),
    ):
        for i in needs:
            fetch[i].wait()

        def body(j, left=left, right=right, first=first):
            put(first + j, left[:, pl.ds(pl.multiple_of(j * WC, WC), WC)], right[...])

        loop(left.shape[1] // WC, body)
        first += left.shape[1] // WC
    for chunk in (first - 2, first - 1):
        for j in range(per):
            g_copy(chunk, j, chunk % 2).wait()


def weight_grads_of(total_slots, positions, x_c, saved):
    r_v, w_v = pltpu.VMEM((ROWS, D), BF), pltpu.VMEM((ROWS, FF), BF)
    return pl.pallas_call(
        weight_kernel,
        out_shape=jax.ShapeDtypeStruct((total_slots, BLK, D), BF),
        in_specs=[SMEM] + [ANY] * 10,
        out_specs=ANY,
        scratch_shapes=[r_v, r_v, w_v, w_v]
        + [r_v] * 6
        + [
            pltpu.VMEM((2, WC, D), BF),
            pltpu.SemaphoreType.DMA((10,)),
            pltpu.SemaphoreType.DMA((2,)),
        ],
        compiler_params=pltpu.CompilerParams(vmem_limit_bytes=VMEM_LIMIT),
        cost_estimate=pl.CostEstimate(flops=2 * ROWS * WROWS * D, bytes_accessed=40 << 20, transcendentals=0),
        name="weight_grads",
    )(positions, x_c, *saved)


def adam_step(grad_now, weight_old, first_old, second_old, rate_step):
    first_new = beta_first * first_old + (1.0 - beta_first) * grad_now
    second_new = beta_second * second_old + (1.0 - beta_second) * grad_now * grad_now
    square = second_new * (1.0 / (1.0 - beta_second**STEP))
    root = jnp.where(square > 0.0, square * lax.rsqrt(square), 0.0)
    step = first_new * (1.0 / (1.0 - beta_first**STEP)) * inverse(root + adam_epsilon)
    return (first_new, second_new, weight_old - rate_step * (step + weight_decay * weight_old))


def finish_kernel(
    used,
    total,
    master,
    first,
    second,
    v_grad,
    v_master,
    v_first,
    v_second,
    line,
    counts,
    out_h,
    ing_h,
    grad_new,
    first_new,
    second_new,
    master_new,
    low_new,
    v_grad_new,
    v_first_new,
    v_second_new,
    v_master_new,
    v_low_new,
    entropy,
    occupancy,
    output,
    input_grad,
):
    i = pl.program_id(0)

    @pl.when(i == 0)
    def _():
        entropy[...] = line[...].reshape(ROWS)
        occupancy[...] = counts[...]
        length = v_master.shape[0]
        for n in range(-(-length // 128)):
            part = slice(n * 128, min((n + 1) * 128, length))
            g = v_grad[n : n + 1, 0 : part.stop - part.start].reshape(part.stop - part.start)
            m, v, w = adam_update(g, v_master[part], v_first[part], v_second[part], rate_vector)
            v_grad_new[part] = g
            v_first_new[part] = m
            v_second_new[part] = v
            v_master_new[part] = w
        v_low_new[...] = v_master_new[...].astype(BF)

    output[...] = out_h[...]
    input_grad[...] = ing_h[...]
    g = jnp.where(used[jnp.minimum(i, used.shape[0] - 1)] > 0, total[...].astype(F32), 0.0)
    m, v, w = adam_step(g, master[...], first[...], second[...], rate_matrix)
    grad_new[...] = g
    first_new[...] = m
    second_new[...] = v
    master_new[...] = w
    low_new[...] = w.astype(BF)


def finish(used, total, weights, v_grad, vectors, line, counts, out, ing):
    count = total.shape[0]
    slot = pl.BlockSpec((1, BLK, D), lambda i: (jnp.minimum(i, count - 1), 0, 0))
    rows = pl.BlockSpec((64, D), lambda i: (jnp.minimum(i, ROWS // 64 - 1), 0))

    def whole(array):
        return pl.BlockSpec(array.shape, lambda i: (0,) * array.ndim)

    f32_slots, f32_vector = shape_of(F32, count, BLK, D), shape_of(F32, *vectors[0].shape)
    shapes = (
        (f32_slots,) * 4
        + (shape_of(BF, count, BLK, D),)
        + (f32_vector,) * 4
        + (shape_of(BF, *vectors[0].shape), shape_of(BF, ROWS), shape_of(I32, *counts.shape))
        + (shape_of(BF, ROWS, D),) * 2
    )
    return pl.pallas_call(
        finish_kernel,
        grid=(max(count, ROWS // 64),),
        out_shape=shapes,
        in_specs=[SMEM] + [slot] * 4 + [whole(a) for a in (v_grad, *vectors, line, counts)] + [rows] * 2,
        out_specs=(slot,) * 5 + tuple(whole(a) for a in shapes[5:12]) + (rows,) * 2,
        compiler_params=pltpu.CompilerParams(vmem_limit_bytes=VMEM_LIMIT),
        name="finish",
    )(used, total, *weights, v_grad, *vectors, line, counts, out, ing)


def local(
    tokens,
    cotangent,
    cluster_order,
    block_owner,
    master_slots,
    moment_one,
    moment_two,
    vector_master,
    vector_moment_one,
    vector_moment_two,
):
    tok_count = lax.axis_size("tok")
    tok_index = lax.axis_index("tok")
    slot_count = master_slots.shape[0]
    cap = tok_count // SD * (max(1, CPS // tok_count) * 3 * CL // (2 * SD))
    total_slots = tok_count * slot_count
    order = cluster_order.reshape(1, ROWS)

    block = jax.ShapeDtypeStruct((SD, cap, D), BF)
    meta_shape = jax.ShapeDtypeStruct((SD, META, D), BF)
    row_block = jax.ShapeDtypeStruct((ROWS, D), BF)
    four_planes = tok_count == 8 and lax.axis_size("rep") == 4
    if four_planes:
        slots_low, x_c, *cots, recv_meta, vecs, b_u, occupancy, positions = gather_all(
            cap, tokens, cotangent, order, master_slots, vector_master, block_owner
        )
        positions = positions.reshape(NBLK)
        slots_low = slots_low.reshape(total_slots, BLK, D)
    else:
        positions = slot_positions(block_owner, slot_count)
        slots_low = lax.all_gather(master_slots.astype(BF), "tok", axis=0, tiled=True)
        vectors = lax.all_gather(vector_master.astype(BF), "tok", axis=0, tiled=True).astype(F32)
        vecs, b_u = vectors[: 8 * D].reshape(8, D), vectors[8 * D :].reshape(1, FF)
        cluster = tok_index // SD * CPS + cluster_order // CL
        target = cluster % tok_count
        chosen = target[None, :] == jnp.arange(tok_count, dtype=jnp.int32)[:, None]
        sent_counts = jnp.sum(chosen.astype(F32), axis=1)
        own_row = (jnp.arange(tok_count, dtype=jnp.int32) == tok_index).astype(F32)
        occupancy = lax.psum(own_row[:, None] * sent_counts[None, :], ("tok", "rep")).astype(jnp.int32)
        send_x, send_c, meta = pl.pallas_call(
            functools.partial(send_kernel, cap),
            out_shape=(block, block, meta_shape),
            in_specs=[VMEM] * 3,
            out_specs=(VMEM,) * 3,
            compiler_params=pltpu.CompilerParams(vmem_limit_bytes=VMEM_LIMIT),
            name="send_rows",
        )(tokens, cotangent, order)
        recv_x, recv_meta = (jnp.stack(swap_blocks(b)) for b in (send_x, meta))
        x_c = pl.pallas_call(
            functools.partial(seat_kernel, cap),
            out_shape=row_block,
            in_specs=[VMEM] * 2,
            out_specs=VMEM,
            compiler_params=pltpu.CompilerParams(vmem_limit_bytes=VMEM_LIMIT),
            name="seat_rows",
        )(recv_x, recv_meta)
        cots = [send_c[k] for k in range(SD)]

    cots = swap_blocks(cots)
    *out_blocks, heads, act, hid, q, k, v, p, slope, n1, n2, rs1, rs2 = forward(
        cap, positions, slots_low, vecs, b_u, x_c, recv_meta
    )
    out_blocks = swap_blocks(out_blocks)
    *ing_blocks, shares, d_up, d_q, d_k, d_v, d_proj, d_br = backward(
        cap, positions, slots_low, vecs, recv_meta, cots, (q, k, v, p, slope, n1, n2, rs1, rs2)
    )
    ing_blocks = swap_blocks(ing_blocks)
    grads = weight_grads_of(
        total_slots, positions, x_c, (heads, act, d_up, d_q, d_k, d_v, d_proj, hid, d_br)
    )
    if four_planes:
        total, vec_owned, output, input_grad, entropy = reduce_all(
            cap, grads, shares, order, out_blocks, ing_blocks, slot_count
        )
    else:
        total = lax.psum(lax.psum_scatter(grads, "tok", scatter_dimension=0, tiled=True), "rep")
        grad_vector = shares[:, 0:9].reshape(-1)
        vec_owned = lax.psum(lax.psum_scatter(grad_vector, "tok", scatter_dimension=0, tiled=True), "rep")
        vec_owned = jnp.pad(vec_owned, (0, -vec_owned.shape[0] % 128)).reshape(-1, 128)
        output, input_grad, entropy = pl.pallas_call(
            functools.partial(return_kernel, cap),
            out_shape=(row_block, row_block, jax.ShapeDtypeStruct((1, ROWS), BF)),
            in_specs=[VMEM] * (2 * SD + 1),
            out_specs=(VMEM,) * 3,
            compiler_params=pltpu.CompilerParams(vmem_limit_bytes=VMEM_LIMIT),
            name="return_rows",
        )(order, *out_blocks, *ing_blocks)

    used = jnp.any(
        positions[None, :] == (tok_index * slot_count + jnp.arange(slot_count, dtype=I32))[:, None], axis=1
    )
    (
        owned_grad,
        first_new,
        second_new,
        master_new,
        low_new,
        vec_owned,
        vec_first,
        vec_second,
        vec_new,
        vec_low_new,
        row_entropy,
        occupancy,
        output,
        input_grad,
    ) = finish(
        used.astype(I32),
        total,
        (master_slots, moment_one, moment_two),
        vec_owned,
        (vector_master, vector_moment_one, vector_moment_two),
        entropy,
        occupancy,
        output,
        input_grad,
    )
    return (
        output,
        input_grad,
        owned_grad,
        first_new,
        second_new,
        master_new,
        low_new,
        vec_owned,
        vec_first,
        vec_second,
        vec_new,
        vec_low_new,
        row_entropy,
        occupancy,
    )


def solution(mesh):
    placed = (
        P(("rep", "tok"), None),
        P(("rep", "tok"), None),
        P(("rep", "tok")),
        P(),
        P("tok", None, None),
        P("tok", None, None),
        P("tok", None, None),
        P("tok"),
        P("tok"),
        P("tok"),
    )
    return jax.shard_map(
        local,
        mesh=mesh,
        in_specs=placed,
        out_specs=(
            P(("rep", "tok"), None),
            P(("rep", "tok"), None),
            P("tok", None, None),
            P("tok", None, None),
            P("tok", None, None),
            P("tok", None, None),
            P("tok", None, None),
            P("tok"),
            P("tok"),
            P("tok"),
            P("tok"),
            P("tok"),
            P(("rep", "tok")),
            P(),
        ),
        check_vma=False,
    )
```

```python
import functools
import math

import jax
import jax.numpy as jnp
from jax import lax
from jax.experimental import pallas as pl
from jax.experimental.pallas import tpu as pltpu
from jax.sharding import PartitionSpec as P

D = 768
HEADS = 12
HD = 64
FF = 3072
SD = 4
CL = 128
NBLK = 96
STEP = 10
CPS = 32
WROWS = 9216
BLK = 96
ROWS = 1024
PAIRS = HEADS // 2
PW = 2 * HD
TM = 512
PART = 48
META = 16
VMEM_LIMIT = 63 << 20
FC = 768
FWD_AT = 4
BWD_AT = 2

norm_epsilon = 1e-06
beta_first = 0.9
beta_second = 0.999
adam_epsilon = 1e-08
weight_decay = 0.01
rate_matrix = 0.02
rate_vector = 0.2

BF = jnp.bfloat16
F32 = jnp.float32
I32 = jnp.int32

VMEM = pl.BlockSpec(memory_space=pltpu.VMEM)
SMEM = pl.BlockSpec(memory_space=pltpu.SMEM)
ANY = pl.BlockSpec(memory_space=pl.ANY)

NN = (((1,), (0,)), ((), ()))
NT = (((1,), (1,)), ((), ()))
TN = (((0,), (0,)), ((), ()))


def mm(a, b, dims=NN):
    return lax.dot_general(a, b, dims, preferred_element_type=F32)


def slot_positions(block_owner, slot_count):
    owners = block_owner[:, 0]
    blocks = owners.shape[0]
    shared = owners[:, None] == owners[None, :]
    before = (
        jnp.arange(blocks, dtype=jnp.int32)[None, :] < jnp.arange(blocks, dtype=jnp.int32)[:, None]
    )
    earlier = jnp.sum((shared & before).astype(jnp.int32), axis=1)
    return owners * slot_count + earlier


def adam_update(grad_now, weight_old, first_old, second_old, rate_step):
    first_new = beta_first * first_old + (1.0 - beta_first) * grad_now
    second_new = beta_second * second_old + (1.0 - beta_second) * grad_now * grad_now
    first_hat = first_new / (1.0 - beta_first**STEP)
    second_hat = second_new / (1.0 - beta_second**STEP)
    weight_new = weight_old - rate_step * (
        first_hat / (jnp.sqrt(second_hat) + adam_epsilon) + weight_decay * weight_old
    )
    return (first_new, second_new, weight_new)


def route_slots(order, seat, cap):
    cluster = order // CL
    rel = lax.rem(cluster, SD) ^ seat
    place = (cluster // SD) * CL + lax.rem(order, CL) + 1
    chosen = lax.broadcasted_iota(I32, (8, ROWS), 0) == rel
    chosen_low = jnp.where(chosen, 1.0, 0.0).astype(BF)
    before = lax.broadcasted_iota(I32, (ROWS, ROWS), 0) < lax.broadcasted_iota(I32, (ROWS, ROWS), 1)
    before_low = jnp.where(before, 1.0, 0.0).astype(BF)
    running = mm(chosen_low, before_low)
    rank = jnp.sum(jnp.where(chosen, running, 0.0), axis=0, keepdims=True).astype(I32)
    return rel * cap + rank, place


def slot_matrix(slots, at, cap):
    rows = lax.broadcasted_iota(I32, (cap, ROWS), 0) + at * cap
    return jnp.where(rows == slots, 1.0, 0.0).astype(BF)


def send_kernel(cap, tokens, cotangent, order, send_x, send_c, meta):
    seat = lax.rem(lax.axis_index("tok"), SD)
    slots, place = route_slots(order[...], seat, cap)
    digits = jnp.concatenate([place // CL, lax.rem(place, CL)] + [place * 0] * 6, axis=0).astype(F32).astype(BF)
    for at in range(SD):
        picked = slot_matrix(slots, at, cap)
        send_x[at] = mm(picked, tokens[...]).astype(BF)
        send_c[at] = mm(picked, cotangent[...]).astype(BF)
        coded = mm(digits, picked, NT)
        line = jnp.concatenate([coded[0:1], coded[1:2]], axis=1)
        meta[at] = jnp.broadcast_to(line, (META, D)).astype(BF)


def remote(src, dst, send_sem, recv_sem, tok, rep):
    return pltpu.make_async_remote_copy(
        src_ref=src,
        dst_ref=dst,
        send_sem=send_sem,
        recv_sem=recv_sem,
        device_id={"tok": tok, "rep": rep},
        device_id_type=pl.DeviceIdType.MESH,
    )


def loop(n, body):
    def run(i, c):
        body(i)
        return c

    lax.fori_loop(0, n, run, 0)


class Place:
    def __init__(self):
        self.me = me = lax.axis_index("tok")
        self.z = z = lax.axis_index("rep")
        core, x, y = me % 2, (me // 2) % 2, me // 4
        self.twin = me + 1 - 2 * core
        self.xn = me + 2 - 4 * x
        self.yn = me + 4 - 8 * y
        self.dn = self.xn + 4 - 8 * y
        self.side = z % 2
        self.zp = z + 1 - 2 * self.side

    def twin_of(self, tok):
        return tok + 1 - 2 * (tok % 2)

    def greet(self, peers):
        barrier = pltpu.get_barrier_semaphore()
        for tok, rep in peers:
            pl.semaphore_signal(
                barrier, inc=1, device_id={"tok": tok, "rep": rep}, device_id_type=pl.DeviceIdType.MESH
            )
        return lambda: pl.semaphore_wait(barrier, len(peers))


def seat_matrix(meta, first, rows, cap):
    hi = jnp.concatenate([meta[k, 0:8, 0:cap] for k in range(SD)], axis=1).astype(F32)[0:1]
    lo = jnp.concatenate([meta[k, 0:8, cap : 2 * cap] for k in range(SD)], axis=1).astype(F32)[0:1]
    at = (hi * CL + lo).astype(I32)
    seats = lax.broadcasted_iota(I32, (rows, SD * cap), 0) + (first + 1)
    return jnp.where(seats == at, 1.0, 0.0).astype(BF)


def seat_part(meta, k, cap):
    hi = meta[k, 0:8, 0:cap].astype(F32)[0:1]
    lo = meta[k, 0:8, cap : 2 * cap].astype(F32)[0:1]
    at = (hi * CL + lo).astype(I32)
    seats = lax.broadcasted_iota(I32, (ROWS, cap), 0) + 1
    return jnp.where(seats == at, 1.0, 0.0).astype(BF)


def seat_rows(meta, blocks, cap, to):
    def body(t):
        r0 = pl.multiple_of(t * 256, 256)
        rows = blocks[...].reshape(SD * cap, D)
        to[pl.ds(r0, 256), :] = mm(seat_matrix(meta, r0, 256, cap), rows).astype(BF)

    loop(ROWS // 256, body)


def seat_kernel(cap, blocks, meta, to):
    seat_rows(meta, blocks, cap, to)


def gather_kernel(
    cap,
    count,
    tokens_h,
    cotangent_h,
    order,
    master_h,
    vector,
    owner_of,
    slots,
    x_c,
    cot_0,
    cot_1,
    cot_2,
    cot_3,
    recv_meta,
    vecs,
    b_u,
    occupancy,
    positions,
    tokens,
    cotangent,
    master,
    own,
    send_x,
    send_c,
    meta,
    recv_x,
    got_meta,
    slot_of,
    digits,
    mine,
    by_z,
    by_tok,
    x_s,
    x_r,
    y_s,
    y_r,
    d_s,
    d_r,
    zx_s,
    zx_r,
    zd_s,
    zd_r,
    zy_s,
    zy_r,
    p_s,
    p_r,
    row_s,
    row_r,
    z_s,
    z_r,
    t_s,
    t_r,
    local_s,
):
    at = Place()
    me, z, side = at.me, at.z, at.side
    n_tok, n_rep = 8, 4
    peers = [((me + d) % n_tok, z) for d in range(1, n_tok)] + [(me, (z + d) % n_rep) for d in range(1, n_rep)]
    fetch = [
        pltpu.make_async_copy(src, dst, local_s.at[i])
        for i, (src, dst) in enumerate(((master_h, master), (tokens_h, tokens), (cotangent_h, cotangent)))
    ]
    for copy in fetch:
        copy.start()
    wait_peers = at.greet(peers)
    fetch[0].wait()

    last = count - 1

    def near(j):
        return side * last + (1 - 2 * side) * j

    def far(j):
        return (1 - side) * last - (1 - 2 * side) * j

    few_x, few_d, few_y = 11 * count // 26, 12 * count // 26, 8 * count // 26
    most_x, most_d, most_y = count - few_x, count - few_d, count - few_y

    def piece(owner, s):
        return slots.at[owner * count + s]

    def to_x(s):
        return remote(own.at[s], piece(me, s), x_s.at[s], x_r.at[s], at.xn, z)

    def to_y(s):
        return remote(own.at[s], piece(me, s), y_s.at[s], y_r.at[s], at.yn, z)

    def on_y(s):
        return remote(piece(at.xn, s), piece(at.xn, s), d_s.at[s], d_r.at[s], at.yn, z)

    def x_on_z(s):
        return remote(piece(at.xn, s), piece(at.xn, s), zx_s.at[s], zx_r.at[s], me, at.zp)

    def d_on_z(s):
        return remote(piece(at.dn, s), piece(at.dn, s), zd_s.at[s], zd_r.at[s], me, at.zp)

    def y_on_z(s):
        return remote(piece(at.yn, s), piece(at.yn, s), zy_s.at[s], zy_r.at[s], me, at.zp)

    def x_in(s):
        return remote(own.at[s], piece(at.xn, s), x_s.at[s], x_r.at[s], at.xn, z)

    def y_in(s):
        return remote(own.at[s], piece(at.yn, s), y_s.at[s], y_r.at[s], at.yn, z)

    def d_in(s):
        return remote(own.at[s], piece(at.dn, s), d_s.at[s], d_r.at[s], at.yn, z)

    owners = (me, at.xn, at.yn, at.dn)

    def near_run(q, j0, j1):
        return (q, (1 - side) * j0 + side * (count - j1), j1 - j0)

    def far_run(q, j0, j1):
        return (q, side * j0 + (1 - side) * (count - j1), j1 - j0)

    runs = (
        (0, 0, count),
        near_run(2, 0, few_y),
        near_run(1, 0, most_x),
        near_run(3, 0, most_d),
        far_run(1, 0, few_x),
        near_run(2, few_y, most_y),
        far_run(2, 0, few_y),
        far_run(3, 0, few_d // 2),
        far_run(3, few_d // 2, few_d - 2),
        far_run(3, few_d - 2, few_d),
    )

    def to_twin(i):
        q, s, n = runs[i]
        src = own if q == 0 else slots.at[pl.ds(owners[q] * count + s, n)]
        dst = slots.at[pl.ds(owners[q] * count + s, n)]
        return remote(src, dst, p_s.at[i], p_r.at[i], at.twin, z)

    def cast(j):
        own[near(j)] = master[near(j)].astype(BF)

    loop(most_x, cast)
    wait_peers()
    loop(most_x, lambda j: to_x(near(j)).start())
    loop(few_y, lambda j: to_y(near(j)).start())
    loop(count - most_x, lambda j: cast(most_x + j))
    to_twin(0).start()
    keep = pltpu.make_async_copy(own, slots.at[pl.ds(me * count, count)], local_s.at[3])
    keep.start()

    seat = me % SD
    seats = (me, at.twin, at.xn, at.twin_of(at.xn))
    rows_of = ((meta, got_meta), (send_x, recv_x))

    def row_copy(i, k):
        src, dst = rows_of[i]
        return remote(src.at[k], dst.at[k], row_s.at[i, k], row_r.at[i, k], seats[k], z)

    put_c = [
        pltpu.make_async_copy(send_c.at[k], to, local_s.at[4 + k])
        for k, to in enumerate((cot_0, cot_1, cot_2, cot_3))
    ]

    def route():
        fetch[1].wait()
        fetch[2].wait()
        slots_here, place = route_slots(order[...], seat, cap)
        slot_of[...] = slots_here
        digits[...] = (
            jnp.concatenate([place // CL, lax.rem(place, CL)] + [place * 0] * 6, axis=0).astype(F32).astype(BF)
        )

    def sort_tokens(k):
        picked = slot_matrix(slot_of[...], k, cap)
        send_x[k] = mm(picked, tokens[...]).astype(BF)
        coded = mm(digits[...], picked, NT)
        line = jnp.concatenate([coded[0:1], coded[1:2]], axis=1)
        meta[k] = jnp.broadcast_to(line, (META, D)).astype(BF)
        for i in range(2):
            if k:
                row_copy(i, k).start()
            else:
                src, dst = rows_of[i]
                dst[0] = src[0]

    def sort_cotangent(k):
        send_c[k] = mm(slot_matrix(slot_of[...], k, cap), cotangent[...]).astype(BF)
        put_c[k].start()

    def z_copy(d):
        return remote(by_z.at[0], by_z.at[d], z_s.at[d], z_r.at[d], me, (z + d) % n_rep)

    def t_copy(d):
        return remote(mine, by_tok.at[d], t_s.at[d], t_r.at[d], (me + d) % n_tok, z)

    def count_rows():
        residue = lax.rem(me // SD * CPS + order[...] // CL, n_tok)
        hit = lax.broadcasted_iota(I32, (128, ROWS), 0) == residue
        by_z[0] = mm(jnp.ones((8, ROWS), BF), jnp.where(hit, 1.0, 0.0).astype(BF), NT)
        for d in range(1, n_rep):
            z_copy(d).start()
        for i in range(9):
            mine[i : i + 1] = vector[i * 128 : (i + 1) * 128].reshape(1, 128).astype(BF).astype(F32)
        block_row = lax.broadcasted_iota(I32, (NBLK, NBLK), 0)
        block_col = lax.broadcasted_iota(I32, (NBLK, NBLK), 1)
        by_col = owner_of[...].astype(F32)
        by_row = lane_sum(jnp.where(block_row == block_col, by_col, 0.0))
        earlier = jnp.where((by_row == by_col) & (block_row < block_col), 1.0, 0.0)
        positions[...] = (by_col * (count * PART // BLK) + jnp.sum(earlier, axis=0, keepdims=True)).astype(I32)

    def share_vectors():
        for d in range(1, n_rep):
            z_copy(d).wait()
        mine[16:24] = by_z[0] + by_z[1] + by_z[2] + by_z[3]
        for d in range(1, n_tok):
            t_copy(d).start()

    def lay_out_vectors():
        by_tok[0] = mine[...]
        for d in range(1, n_tok):
            t_copy(d).wait()
        for owner in range(n_tok):
            share = by_tok[(me + n_tok - owner) % n_tok]
            occupancy[owner : owner + 1, :] = share[16:17, 0:n_tok].astype(I32)
            for i in range(9):
                chunk = owner * 9 + i
                row, lane = chunk // 6, chunk % 6 * 128
                if row < 8:
                    vecs[row : row + 1, lane : lane + 128] = share[i : i + 1]
                else:
                    lane += (row - 8) * D
                    b_u[:, lane : lane + 128] = share[i : i + 1]

    between = {
        1: lambda: (route(), sort_tokens(2)),
        3: lambda: sort_tokens(3),
        5: lambda: sort_tokens(1),
        7: lambda: (sort_tokens(0), count_rows()),
        9: lambda: sort_cotangent(1),
        11: lambda: sort_cotangent(2),
        13: lambda: sort_cotangent(3),
    }
    for j in range(most_x):
        x_in(near(j)).wait_recv()
        if j < most_d:
            on_y(near(j)).start()
        if j < few_x:
            x_on_z(near(j)).start()
        if j < few_y:
            y_in(near(j)).wait_recv()
            y_on_z(near(j)).start()
        if j == few_y:
            to_twin(1).start()
        if j in between:
            between[j]()
    to_twin(2).start()
    loop(most_y - few_y, lambda j: to_y(near(few_y + j)).start())
    share_vectors()
    sort_cotangent(0)

    def diagonal(j):
        d_in(near(j)).wait_recv()
        d_on_z(near(j)).start()

    loop(few_d, diagonal)
    loop(most_d - few_d, lambda j: d_in(near(few_d + j)).wait_recv())
    to_twin(3).start()
    loop(few_x, lambda j: x_on_z(far(j)).wait_recv())
    to_twin(4).start()
    lay_out_vectors()
    loop(most_y - few_y, lambda j: y_in(near(few_y + j)).wait_recv())
    to_twin(5).start()
    loop(few_y, lambda j: y_on_z(far(j)).wait_recv())
    to_twin(6).start()
    for i in (0, 1):
        for k in (2, 3, 1):
            row_copy(i, k).wait_recv()
    recv_meta[...] = got_meta[...]
    seat_rows(got_meta, recv_x, cap, x_c)
    done = 0
    for i, upto in ((7, few_d // 2), (8, few_d - 2), (9, few_d)):
        loop(upto - done, lambda j, done=done: d_on_z(far(done + j)).wait_recv())
        to_twin(i).start()
        done = upto

    for i in range(2):
        for k in (2, 3, 1):
            row_copy(i, k).wait_send()
    for copy in put_c:
        copy.wait()
    keep.wait()

    loop(most_x, lambda j: to_x(near(j)).wait_send())
    loop(most_y, lambda j: to_y(near(j)).wait_send())
    loop(most_d, lambda j: on_y(near(j)).wait_send())
    loop(few_x, lambda j: x_on_z(near(j)).wait_send())
    loop(few_d, lambda j: d_on_z(near(j)).wait_send())
    loop(few_y, lambda j: y_on_z(near(j)).wait_send())
    for i in range(len(runs)):
        to_twin(i).wait()


def gather_all(cap, tokens, cotangent, order, master, vector, block_owner):
    count = master.shape[0] * BLK // PART
    rows = jax.ShapeDtypeStruct((ROWS, D), BF)
    part = jax.ShapeDtypeStruct((cap, D), BF)
    dma = pltpu.SemaphoreType.DMA
    block = pltpu.VMEM((SD, cap, D), BF)
    meta = pltpu.VMEM((SD, META, D), BF)
    return pl.pallas_call(
        functools.partial(gather_kernel, cap, count),
        out_shape=(
            jax.ShapeDtypeStruct((8 * count, PART, D), BF),
            rows,
            part,
            part,
            part,
            part,
            jax.ShapeDtypeStruct((SD, META, D), BF),
            jax.ShapeDtypeStruct((8, D), F32),
            jax.ShapeDtypeStruct((1, FF), F32),
            jax.ShapeDtypeStruct((8, 8), I32),
            jax.ShapeDtypeStruct((1, NBLK), I32),
        ),
        in_specs=[ANY, ANY, VMEM, ANY, VMEM, VMEM],
        out_specs=(ANY, VMEM) + (ANY,) * SD + (VMEM,) * 5,
        scratch_shapes=[
            pltpu.VMEM((ROWS, D), BF),
            pltpu.VMEM((ROWS, D), BF),
            pltpu.VMEM((count, PART, D), F32),
            pltpu.VMEM((count, PART, D), BF),
            block,
            block,
            meta,
            block,
            meta,
            pltpu.VMEM((1, ROWS), I32),
            pltpu.VMEM((8, ROWS), BF),
            pltpu.VMEM((24, 128), F32),
            pltpu.VMEM((4, 8, 128), F32),
            pltpu.VMEM((8, 24, 128), F32),
        ]
        + [dma((count,))] * 12
        + [dma((10,))] * 2
        + [dma((2, SD))] * 2
        + [dma((4,))] * 2
        + [dma((8,))] * 2
        + [dma((8,))],
        compiler_params=pltpu.CompilerParams(collective_id=0, has_side_effects=True, vmem_limit_bytes=VMEM_LIMIT),
        cost_estimate=pl.CostEstimate(flops=8 * ROWS * ROWS * D, bytes_accessed=64 << 20, transcendentals=0),
        name="gather",
    )(tokens, cotangent, order, master.reshape(count, PART, D), vector, block_owner.reshape(1, NBLK))


def return_kernel(cap, order, *refs):
    outs, ings, (out, ing, entropy) = refs[:SD], refs[SD : 2 * SD], refs[2 * SD :]
    seat = lax.rem(lax.axis_index("tok"), SD)
    slots, _ = route_slots(order[...], seat, cap)
    picked = jnp.concatenate([slot_matrix(slots, at, cap) for at in range(SD)], axis=0)
    for to, blocks in ((out, outs), (ing, ings)):
        rows = jnp.concatenate([block[0:cap, :] for block in blocks], axis=0)
        to[...] = mm(picked, rows, TN).astype(BF)
    line = jnp.concatenate([block[cap : cap + 8, 0:cap] for block in outs], axis=1)
    entropy[...] = mm(line, picked)[0:1].astype(BF)


def swap_blocks(blocks):
    n = lax.axis_size("tok")
    parts = [blocks[0]]
    for k in range(1, SD):
        parts.append(lax.ppermute(blocks[k], "tok", [(i, i ^ k) for i in range(n)]))
    return parts


def reduce_kernel(
    cap,
    count,
    split,
    grads,
    vec,
    order,
    out_0,
    out_1,
    out_2,
    out_3,
    ing_0,
    ing_1,
    ing_2,
    ing_3,
    total,
    vec_out,
    output,
    input_grad,
    entropy,
    out_v,
    ing_v,
    slot_of,
    a,
    tw,
    rd,
    rx,
    ry,
    o,
    rz1,
    pz,
    rz2,
    fz,
    vt,
    va,
    vb,
    vc,
    a_l,
    keep_l,
    p_s,
    p_r,
    d_s,
    d_r,
    x_s,
    x_r,
    y_s,
    y_r,
    z1_s,
    z1_r,
    z2_s,
    z2_r,
    z3_s,
    z3_r,
    t_s,
    t_r,
    v_s,
    v_r,
    row_l,
):
    at = Place()
    me, z = at.me, at.z
    n_tok, n_rep = 8, 4
    peers = [((me + d) % n_tok, z) for d in range(1, n_tok)] + [(me, (z + d) % n_rep) for d in range(1, n_rep)]
    wait_peers = at.greet(peers)
    owners = (me, at.xn, at.yn, at.dn)

    def load(q):
        return pltpu.make_async_copy(grads.at[pl.ds(owners[q] * count, count)], a.at[q], a_l.at[q])

    for q in (3, 1, 2, 0):
        load(q).start()
    rows_in = [
        pltpu.make_async_copy(src, to.at[k], row_l.at[i, k])
        for i, (blocks, to) in enumerate((((out_0, out_1, out_2, out_3), out_v), ((ing_0, ing_1, ing_2, ing_3), ing_v)))
        for k, src in enumerate(blocks)
    ]
    for copy in rows_in:
        copy.start()
    wait_peers()

    def to_twin(q, g):
        src = grads.at[pl.ds(at.twin_of(owners[q]) * count + 2 * g, 2)]
        return remote(src, tw.at[q, pl.ds(2 * g, 2)], p_s.at[q, g], p_r.at[q, g], at.twin, z)

    def d_y(s):
        return remote(a.at[3, s], rd.at[s], d_s.at[s], d_r.at[s], at.yn, z)

    def d_x(s):
        return remote(a.at[3, s], rd.at[s], d_s.at[s], d_r.at[s], at.xn, z)

    def to_x(s):
        return remote(a.at[1, s], rx.at[s], x_s.at[s], x_r.at[s], at.xn, z)

    def to_y(s):
        return remote(a.at[2, s], ry.at[s], y_s.at[s], y_r.at[s], at.yn, z)

    def z_in(s):
        return remote(o.at[s], rz1.at[s], z1_s.at[s], z1_r.at[s], me, at.zp)

    def z_swap(s):
        return remote(pz.at[s], rz2.at[s], z2_s.at[s], z2_r.at[s], me, n_rep - 1 - z)

    def z_out(s):
        return remote(fz.at[s], fz.at[s], z3_s.at[s], z3_r.at[s], me, at.zp)

    def keep(s):
        return pltpu.make_async_copy(fz.at[s], total.at[s], keep_l.at[s])

    def twin_start(g):
        for q in (3, 1, 2, 0):
            to_twin(q, g).start()

    loop(count // 2, twin_start)

    def v_tok(d):
        return remote(vec.at[(me + d) % n_tok], vt.at[d], t_s.at[d], t_r.at[d], (me + d) % n_tok, z)

    def v_rep(i, src):
        return remote(src, vb.at[i], v_s.at[i], v_r.at[i], me, at.zp if i == 0 else (z + 2) % n_rep)

    for d in range(1, n_tok):
        v_tok(d).start()

    def join(q, s):
        return a[q, s] + tw[q, s]

    def first(s, send):
        a[3, s] = join(3, s)
        send(s).start()

    def plain(q, s, send):
        a[q, s] = join(q, s)
        send(s).start()

    def joined(q, s, arrived, send):
        arrived(s).wait_recv()
        a[q, s] = join(q, s) + rd[s]
        send(s).start()

    inner = (z == 1) | (z == 2)
    outer = (z == 0) | (z == 3)

    def own(s):
        to_x(s).wait_recv()
        to_y(s).wait_recv()
        o[s] = join(0, s) + (rx[s] + ry[s])
        pl.when(outer)(lambda: z_in(s).start())

    def middle(s):
        @pl.when(inner)
        def _():
            z_in(s).wait_recv()
            pz[s] = o[s] + rz1[s]
            z_swap(s).start()

    def last(s):
        @pl.when(inner)
        def _():
            z_swap(s).wait_recv()
            fz[s] = pz[s] + rz2[s]
            z_out(s).start()
            keep(s).start()

    def taken(s):
        @pl.when(outer)
        def _():
            z_out(s).wait_recv()
            keep(s).start()

    def pick_rows(i):
        ts = pl.ds(pl.multiple_of(i * 256, 256), 256)
        hit = lax.broadcasted_iota(I32, (SD * cap, 256), 0) == slot_of[:, ts]
        picked = jnp.where(hit, 1.0, 0.0).astype(BF)
        outs = jnp.concatenate([out_v[k, 0:cap, :] for k in range(SD)], axis=0)
        ings = jnp.concatenate([ing_v[k] for k in range(SD)], axis=0)
        both = mm(picked, jnp.concatenate([outs, ings], axis=1), TN)
        output[ts, :] = both[:, 0:D].astype(BF)
        input_grad[ts, :] = both[:, D:].astype(BF)
        line = jnp.concatenate([out_v[k, cap : cap + 8, 0:cap] for k in range(SD)], axis=1)
        entropy[:, ts] = mm(line, picked)[0:1].astype(BF)

    for q in (3, 1, 2, 0):
        load(q).wait()

    def steps(i, lag, more):
        s = i - lag
        by_x = (s % 2 == 0) & (s < 2 * split)
        live = (s >= 0) & (s < count)
        pl.when(live & by_x)(lambda: more(s, True))
        pl.when(live & jnp.logical_not(by_x))(lambda: more(s, False))

    def steps_of(i, lag, more):
        pl.when((i >= lag) & (i < count + lag))(lambda: more(i - lag))

    def round_of(i):
        for lag, which in ((0, (3,)), (1, (1, 2)), (6, (0,))):

            @pl.when((i >= lag) & ((i - lag) % 2 == 0) & (i < count + lag))
            def _(lag=lag, which=which):
                for q in which:
                    to_twin(q, (i - lag) // 2).wait_recv()

        steps(i, 0, lambda s, by_x: first(s, d_x if by_x else d_y))
        steps(i, 1, lambda s, by_x: plain(1, s, to_x) if by_x else plain(2, s, to_y))
        steps(i, 3, lambda s, by_x: joined(2, s, d_x, to_y) if by_x else joined(1, s, d_y, to_x))
        steps_of(i, 6, own)
        steps_of(i, 8, middle)
        steps_of(i, 10, last)
        steps_of(i, 12, taken)

    loop(3, round_of)
    for copy in rows_in:
        copy.wait()
    slots_here, _ = route_slots(order[...], me % SD, cap)
    slot_of[...] = slots_here

    v_sum = vec[me]
    for d in range(1, n_tok):
        v_tok(d).wait()
        v_sum = v_sum + vt[d]
    va[...] = v_sum
    v_rep(0, va).start()

    def four_rounds(i):
        loop(4, lambda j: round_of(3 + 4 * i + j))
        pick_rows(i)

    four_rounds(0)
    v_rep(0, va).wait()
    vc[...] = va[...] + vb[0]
    v_rep(1, vc).start()
    loop(3, lambda i: four_rounds(1 + i))
    loop(count + 12 - 19, lambda i: round_of(19 + i))
    v_rep(1, vc).wait()
    vec_out[...] = vc[...] + vb[1]

    def twin_sent(g):
        for q in range(4):
            to_twin(q, g).wait_send()

    loop(count // 2, twin_sent)

    def sent(s):
        d_y(s).wait_send()
        to_x(s).wait_send()
        to_y(s).wait_send()
        keep(s).wait()

    loop(count, sent)

    @pl.when(outer)
    def _():
        loop(count, lambda s: z_in(s).wait_send())

    @pl.when(inner)
    def _():
        def back(s):
            z_swap(s).wait_send()
            z_out(s).wait_send()

        loop(count, back)


def reduce_all(cap, grads, shares, order, outs, ings, count):
    dma = pltpu.SemaphoreType.DMA
    count = count * BLK // PART
    part = pltpu.VMEM((count, PART, D), BF)
    whole = pltpu.VMEM((4, count, PART, D), BF)
    line = pltpu.VMEM((16, 128), F32)
    rows = jax.ShapeDtypeStruct((ROWS, D), BF)
    total, vec, output, input_grad, entropy = pl.pallas_call(
        functools.partial(reduce_kernel, cap, count, count // 2),
        out_shape=(
            jax.ShapeDtypeStruct((count, PART, D), BF),
            jax.ShapeDtypeStruct((16, 128), F32),
            rows,
            rows,
            jax.ShapeDtypeStruct((1, ROWS), BF),
        ),
        in_specs=[ANY, VMEM, VMEM] + [ANY] * (2 * SD),
        out_specs=(ANY,) + (VMEM,) * 4,
        scratch_shapes=[
            pltpu.VMEM((SD, cap + META, D), BF),
            pltpu.VMEM((SD, cap, D), BF),
            pltpu.VMEM((1, ROWS), I32),
            whole,
            whole,
        ]
        + [part] * 8
        + [pltpu.VMEM((8, 16, 128), F32), line, pltpu.VMEM((2, 16, 128), F32), line]
        + [dma((4,)), dma((count,))]
        + [dma((4, count // 2))] * 2
        + [dma((count,))] * 12
        + [dma((8,))] * 2
        + [dma((2,))] * 2
        + [dma((2, SD))],
        compiler_params=pltpu.CompilerParams(collective_id=1, has_side_effects=True, vmem_limit_bytes=VMEM_LIMIT),
        cost_estimate=pl.CostEstimate(flops=4 * ROWS * ROWS * D, bytes_accessed=64 << 20, transcendentals=0),
        name="reduce",
    )(grads.reshape(-1, PART, D), shares, order, *outs, *ings)
    return total.reshape(-1, BLK, D), vec, output, input_grad, entropy


V_BQ, V_BV, V_BO, V_BD, V_G1, V_C1, V_G2, V_C2 = range(8)


def inverse(x):
    r = pl.reciprocal(x, approx=True)
    return r * (2.0 - x * r)


def erf_parts(v):
    t = inverse(1.0 + (0.3275911 / math.sqrt(2.0)) * jnp.abs(v))
    e = jnp.exp2((v * v) * (-0.5 / math.log(2.0)))
    poly = 0.5 * 1.061405429
    for c in (-1.453152027, 1.421413741, -0.284496736, 0.254829592):
        poly = poly * t + 0.5 * c
    tail = poly * (t * e)
    return jnp.where(v >= 0.0, 1.0 - tail, tail), e


def lane_sum(x):
    return jnp.sum(x, axis=1, keepdims=True)


def gelu_parts(v):
    phi, e = erf_parts(v)
    return v * phi, phi + v * (e * (1.0 / math.sqrt(2.0 * math.pi)))


def weight_copies(pos, slots, w, sem, first):
    def copy(b):
        return pltpu.make_async_copy(slots.at[pos[first + b]], w.at[pl.ds(b * BLK, BLK)], sem)

    n = w.shape[0] // BLK
    return (lambda: loop(n, lambda b: copy(b).start())), (lambda: loop(n, lambda b: copy(b).wait()))


def halves_of_heads():
    lane = lax.broadcasted_iota(I32, (1, PW), 1)
    m0 = jnp.where(lane < HD, 1.0, 0.0).astype(BF)
    m1 = jnp.where(lane < HD, 0.0, 1.0).astype(BF)
    return lambda pair: jnp.concatenate([pair * m0, pair * m1], axis=0)


def tile_rows(t):
    return pl.ds(pl.multiple_of(t * TM, TM), TM)


def forward_kernel(
    cap,
    pos,
    slots,
    vecs,
    b_u,
    x_h,
    meta,
    back_0,
    back_1,
    back_2,
    back_3,
    heads_h,
    act_h,
    hid_h,
    q_h,
    k_h,
    v_h,
    p_h,
    slope_h,
    n1_h,
    n2_h,
    rs1_h,
    rs2_h,
    wqkv,
    wo,
    wu,
    wd,
    x_c,
    heads,
    act,
    hid,
    q,
    k,
    v,
    p_all,
    slope,
    n1,
    n2,
    rs1,
    rs2,
    out_c,
    ent,
    hid_t,
    w_sem,
    x_sem,
    o_sem,
):
    inv = 1.0 / math.sqrt(HD)
    get_x = pltpu.make_async_copy(x_h, x_c, x_sem)
    get_x.start()
    weights = [
        weight_copies(pos, slots, w, w_sem.at[i], first)
        for i, (w, first) in enumerate(((wqkv, 0), (wo, 24), (wu, 32), (wd, 64)))
    ]
    for start, _ in weights:
        start()
    get_x.wait()
    apart = halves_of_heads()

    def vec(i):
        return vecs[i : i + 1, :]

    saved = (
        (heads, heads_h),
        (act, act_h),
        (hid, hid_h),
        (q, q_h),
        (k, k_h),
        (v, v_h),
        (slope, slope_h),
        (n1, n1_h),
        (n2, n2_h),
        (rs1, rs1_h),
        (rs2, rs2_h),
    )

    def save(t, i):
        src, dst = saved[i]
        return pltpu.make_async_copy(src.at[tile_rows(t)], dst.at[tile_rows(t)], o_sem.at[i])

    def save_p(t):
        n = TM // CL
        cs = pl.ds(t * n, n)
        return pltpu.make_async_copy(p_all.at[cs], p_h.at[cs], o_sem.at[len(saved)])

    def normal(r, n, rs, rows):
        c = r - lane_sum(r) * (1.0 / D)
        scale = lax.rsqrt(lane_sum(c * c) * (1.0 / D) + norm_epsilon)
        rs[rows, :] = jnp.broadcast_to(scale, (TM, 128))
        n[rows, :] = c * scale

    def tile(t):
        rows = tile_rows(t)
        first = t == 0
        pl.when(first)(weights[0][1])
        x = x_c[rows, :]
        q[rows, :] = ((mm(x, wqkv[0:D, :]) + vec(V_BQ)).astype(BF).astype(F32) * inv).astype(BF)
        k[rows, :] = mm(x, wqkv[D : 2 * D, :]).astype(BF)
        v[rows, :] = (mm(x, wqkv[2 * D :, :]) + vec(V_BV)).astype(BF)

        def attend(c):
            groups = [pl.ds(pl.multiple_of(t * TM + (FWD_AT * c + i) * CL, CL), CL) for i in range(FWD_AT)]
            pairs = [(i, p, slice(p * PW, (p + 1) * PW)) for i in range(FWD_AT) for p in range(PAIRS)]
            scores = [mm(apart(k[groups[i], ps]), q[groups[i], ps], NT) for i, _, ps in pairs]
            total = [jnp.zeros((1, CL), F32)] * FWD_AT
            probs = []
            for (i, _, _), both in zip(pairs, scores):
                halves = []
                for h in range(2):
                    sh = both[h * CL : (h + 1) * CL]
                    sh = sh - jnp.max(sh, axis=0, keepdims=True)
                    e = jnp.exp(sh)
                    tot = jnp.sum(e, axis=0, keepdims=True)
                    r = 1.0 / tot
                    total[i] += jnp.log(tot) - jnp.sum(e * sh, axis=0, keepdims=True) * r
                    halves.append((e * r).astype(BF))
                probs.append(jnp.concatenate(halves, axis=0))
            mixed = [mm(w, apart(v[groups[i], ps]), TN).astype(BF) for (i, _, ps), w in zip(pairs, probs)]
            for (i, p, ps), w, o in zip(pairs, probs, mixed):
                p_all[t * (TM // CL) + FWD_AT * c + i, p] = w
                heads[groups[i], ps] = o
            for i in range(FWD_AT):
                ent[:, groups[i]] = jnp.broadcast_to(total[i] * (1.0 / HEADS), (8, CL))

        loop(TM // CL // FWD_AT, attend)
        for i in (0, 3, 4, 5):
            save(t, i).start()
        save_p(t).start()
        pl.when(first)(weights[1][1])
        normal(x_c[rows, :].astype(F32) + mm(heads[rows, :], wo[...]) + vec(V_BO), n1, rs1, rows)
        hidden = n1[rows, :] * vec(V_G1) + vec(V_C1)
        hid[rows, :] = hidden.astype(BF)
        hid_t[...] = hidden
        pl.when(first)(weights[2][1])

        def widen(f):
            parts = [pl.ds(pl.multiple_of((2 * f + i) * FC, FC), FC) for i in range(2)]
            ups = [mm(hid[rows, :], wu[fs, :], NT) for fs in parts]
            for fs, up in zip(parts, ups):
                g, g_slope = gelu_parts(up + b_u[:, fs])
                act[rows, fs] = g.astype(BF)
                slope[rows, fs] = g_slope.astype(BF)

        loop(FF // FC // 2, widen)
        for i in (1, 2, 6, 7, 9):
            save(t, i).start()
        pl.when(first)(weights[3][1])
        normal(hid_t[...] + mm(act[rows, :], wd[...]) + vec(V_BD), n2, rs2, rows)
        out_c[rows, :] = (n2[rows, :] * vec(V_G2) + vec(V_C2)).astype(BF)
        for i in (8, 10):
            save(t, i).start()

    loop(ROWS // TM, tile)

    for j, back in enumerate((back_0, back_1, back_2, back_3)):
        own = seat_part(meta, j, cap)
        back[0:cap, :] = mm(own, out_c[...], TN).astype(BF)
        line = mm(ent[...].astype(BF), own)
        back[cap:, :] = jnp.concatenate([line, line], axis=1)[0:1].astype(BF) * jnp.ones((META, 1), BF)

    def saved_all(t):
        for i in range(len(saved)):
            save(t, i).wait()
        save_p(t).wait()

    loop(ROWS // TM, saved_all)


def shape_of(kind, *shape):
    return jax.ShapeDtypeStruct(shape, kind)


def saved_shapes():
    rows, wide = ((ROWS, D), BF), ((ROWS, FF), BF)
    probs = ((ROWS // CL, PAIRS, 2 * CL, CL), BF)
    full, thin = ((ROWS, D), F32), ((ROWS, 128), F32)
    return rows, wide, probs, full, thin


def forward(cap, positions, slots, vecs, b_u, x_c, meta):
    rows, wide, probs, full, thin = saved_shapes()
    kept = (rows, wide, rows, rows, rows, rows, probs, wide, full, full, thin, thin)
    dma = pltpu.SemaphoreType.DMA
    return pl.pallas_call(
        functools.partial(forward_kernel, cap),
        out_shape=(shape_of(BF, cap + META, D),) * SD + tuple(shape_of(kind, *shape) for shape, kind in kept),
        in_specs=[SMEM, ANY, VMEM, VMEM, ANY, VMEM],
        out_specs=(VMEM,) * SD + (ANY,) * len(kept),
        scratch_shapes=[
            pltpu.VMEM((3 * D, D), BF),
            pltpu.VMEM((D, D), BF),
            pltpu.VMEM((FF, D), BF),
            pltpu.VMEM((FF, D), BF),
            pltpu.VMEM(*rows),
        ]
        + [pltpu.VMEM(*a) for a in kept]
        + [
            pltpu.VMEM(*rows),
            pltpu.VMEM((8, ROWS), F32),
            pltpu.VMEM((TM, D), F32),
            dma((4,)),
            dma,
            dma((12,)),
        ],
        compiler_params=pltpu.CompilerParams(vmem_limit_bytes=VMEM_LIMIT),
        cost_estimate=pl.CostEstimate(flops=2 * ROWS * WROWS * D, bytes_accessed=64 << 20, transcendentals=0),
        name="forward",
    )(positions, slots, vecs, b_u, x_c, meta)


def backward_kernel(
    cap,
    pos,
    slots,
    vecs,
    meta,
    cot_0,
    cot_1,
    cot_2,
    cot_3,
    q_h,
    k_h,
    v_h,
    p_h,
    slope_h,
    n1_h,
    n2_h,
    rs1_h,
    rs2_h,
    back_0,
    back_1,
    back_2,
    back_3,
    shares,
    d_up_h,
    d_q_h,
    d_k_h,
    d_v_h,
    d_proj_h,
    d_br_h,
    wqkv,
    wo,
    wu,
    wd,
    blocks,
    q,
    k,
    v,
    p_all,
    d_up,
    n1,
    n2,
    rs1,
    rs2,
    d_proj,
    d_br,
    ing_c,
    d_h_t,
    gvec,
    g_bu,
    w_sem,
    c_sem,
    i_sem,
    o_sem,
):
    inv = 1.0 / math.sqrt(HD)
    get_c = [
        pltpu.make_async_copy(cot, blocks.at[j], c_sem.at[j]) for j, cot in enumerate((cot_0, cot_1, cot_2, cot_3))
    ]
    for copy in get_c:
        copy.start()
    fetch = [
        pltpu.make_async_copy(src, dst, i_sem.at[i])
        for i, (src, dst) in enumerate(
            (
                (n2_h, n2),
                (rs2_h, rs2),
                (slope_h, d_up),
                (n1_h, n1),
                (rs1_h, rs1),
                (v_h, v),
                (p_h, p_all),
                (k_h, k),
                (q_h, q),
            )
        )
    ]
    weights = [
        weight_copies(pos, slots, w, w_sem.at[i], first)
        for i, (w, first) in enumerate(((wd, 64), (wu, 32), (wo, 24), (wqkv, 0)))
    ]
    fetch[0].start()
    fetch[1].start()
    weights[0][0]()
    fetch[2].start()
    weights[1][0]()
    fetch[3].start()
    fetch[4].start()
    weights[2][0]()
    for i in range(5, 9):
        fetch[i].start()
    weights[3][0]()
    gvec[...] = jnp.zeros_like(gvec)
    g_bu[...] = jnp.zeros_like(g_bu)
    shares[...] = jnp.zeros_like(shares)
    for copy in get_c:
        copy.wait()
    seat_rows(meta, blocks, cap, d_br)
    apart = halves_of_heads()

    def vec(i):
        return vecs[i : i + 1, :]

    def add_vec(i, value):
        gvec[i : i + 1, :] += jnp.sum(value, axis=0, keepdims=True)

    saved = ((d_up, d_up_h), (q, d_q_h), (k, d_k_h), (v, d_v_h), (d_proj, d_proj_h), (d_br, d_br_h))

    def save(t, i):
        src, dst = saved[i]
        return pltpu.make_async_copy(src.at[tile_rows(t)], dst.at[tile_rows(t)], o_sem.at[i])

    def norm_back(e, n, rs, gain, shift):
        add_vec(gain, e * n)
        add_vec(shift, e)
        eg = e * vec(gain)
        return rs * (eg - lane_sum(eg) * (1.0 / D) - n * (lane_sum(eg * n) * (1.0 / D)))

    def norm_two_back(t):
        rows = tile_rows(t)
        d_r2 = norm_back(d_br[rows, :].astype(F32), n2[rows, :], rs2[rows, 0:1], V_G2, V_C2)
        d_br[rows, :] = d_r2.astype(BF)
        add_vec(V_BD, d_br[rows, :].astype(F32))
        n2[rows, :] = d_r2

    def widen_back(t, columns):
        rows = tile_rows(t)
        parts = [pl.ds(pl.multiple_of(f * FC, FC), FC) for f in columns]
        ups = [mm(d_br[rows, :], wd[fs, :], NT) for fs in parts]

        def finish():
            for fs, up in zip(parts, ups):
                du = (up * d_up[rows, fs].astype(F32)).astype(BF)
                d_up[rows, fs] = du
                g_bu[:, fs] += jnp.sum(du.astype(F32), axis=0, keepdims=True)

        return finish

    def hidden_back(t):
        rows = tile_rows(t)
        return n2[rows, :] + mm(d_up[rows, :], wu[...])

    def norm_one_back(t, d_h):
        rows = tile_rows(t)
        d_r1 = norm_back(d_h, n1[rows, :], rs1[rows, 0:1], V_G1, V_C1)
        d_proj[rows, :] = d_r1.astype(BF)
        n2[rows, :] = d_r1
        add_vec(V_BO, d_proj[rows, :].astype(F32))

    def heads_back(t):
        rows = tile_rows(t)
        d_h_t[rows, :] = mm(d_proj[rows, :], wo[...], NT).astype(BF)

    def attend_back(clusters, meanwhile=lambda: None):
        pairs = [
            (c, p, pl.ds(pl.multiple_of(c * CL, CL), CL), slice(p * PW, (p + 1) * PW))
            for c in clusters
            for p in range(PAIRS)
        ]
        probs = [p_all[c, p] for c, p, _, _ in pairs]
        d_heads = [d_h_t[gr, ps] for _, _, gr, ps in pairs]
        d_probs = [mm(apart(v[gr, ps]), dh, NT) for (_, _, gr, ps), dh in zip(pairs, d_heads)]
        d_values = [
            mm(jnp.concatenate([w[0:CL], w[CL:]], axis=1), apart(dh)).astype(BF) for w, dh in zip(probs, d_heads)
        ]
        finish = meanwhile()
        d_scores = []
        for w, dw in zip(probs, d_probs):
            halves = []
            for h in range(2):
                wh = w[h * CL : (h + 1) * CL].astype(F32)
                dwh = dw[h * CL : (h + 1) * CL]
                halves.append((wh * (dwh - jnp.sum(dwh * wh, axis=0, keepdims=True))).astype(BF))
            d_scores.append(halves)
        d_keys = [
            mm(jnp.concatenate(ds, axis=1), apart(q[gr, ps])).astype(BF) for (_, _, gr, ps), ds in zip(pairs, d_scores)
        ]
        d_queries = [
            (mm(jnp.concatenate(ds, axis=0), apart(k[gr, ps]), TN) * inv).astype(BF)
            for (_, _, gr, ps), ds in zip(pairs, d_scores)
        ]
        if finish is not None:
            finish()
        for (_, _, gr, ps), dq, dk, dv in zip(pairs, d_queries, d_keys, d_values):
            q[gr, ps] = dq
            k[gr, ps] = dk
            v[gr, ps] = dv

    def rows_back(t):
        rows = tile_rows(t)
        return (
            mm(q[rows, :], wqkv[0:D, :], NT)
            + mm(k[rows, :], wqkv[D : 2 * D, :], NT)
            + mm(v[rows, :], wqkv[2 * D :, :], NT)
        )

    def rows_done(t, d_x):
        rows = tile_rows(t)
        add_vec(V_BQ, q[rows, :].astype(F32))
        add_vec(V_BV, v[rows, :].astype(F32))
        ing_c[rows, :] = (n2[rows, :] + d_x.astype(BF).astype(F32)).astype(BF)

    def save_all(t, which):
        for i in which:
            save(t, i).start()

    per = TM // CL
    fetch[0].wait()
    fetch[1].wait()
    norm_two_back(0)
    norm_two_back(1)
    weights[0][1]()
    fetch[2].wait()
    loop(FF // FC // 2, lambda f: widen_back(0, [2 * f, 2 * f + 1])())
    save_all(0, (0, 5))
    weights[1][1]()
    fetch[3].wait()
    fetch[4].wait()
    norm_one_back(0, hidden_back(0))
    weights[2][1]()
    for i in range(5, 9):
        fetch[i].wait()
    heads_back(0)
    save_all(0, (4,))
    loop(per, lambda c: attend_back([c], lambda: widen_back(1, [c])))
    save_all(0, (1, 2, 3))
    save_all(1, (0, 5))
    weights[3][1]()
    d_h = hidden_back(1)
    d_x = rows_back(0)
    norm_one_back(1, d_h)
    heads_back(1)
    rows_done(0, d_x)
    save_all(1, (4,))
    loop(per // BWD_AT, lambda c: attend_back([per + BWD_AT * c + i for i in range(BWD_AT)]))
    save_all(1, (1, 2, 3))
    rows_done(1, rows_back(1))

    for j, back in enumerate((back_0, back_1, back_2, back_3)):
        back[...] = mm(seat_part(meta, j, cap), ing_c[...], TN).astype(BF)

    for chunk in range(72):
        row, lane = chunk // 6, chunk % 6 * 128
        if row < 8:
            part = gvec[row : row + 1, lane : lane + 128]
        else:
            lane += (row - 8) * D
            part = g_bu[:, lane : lane + 128]
        shares[chunk // 9, chunk % 9 : chunk % 9 + 1, :] = part

    def saved_all(t):
        for i in range(len(saved)):
            save(t, i).wait()

    loop(ROWS // TM, saved_all)


def backward(cap, positions, slots, vecs, meta, cots, saved):
    rows, wide, probs, full, thin = saved_shapes()
    dma = pltpu.SemaphoreType.DMA
    grads = (wide, rows, rows, rows, rows, rows)
    return pl.pallas_call(
        functools.partial(backward_kernel, cap),
        out_shape=(shape_of(BF, cap, D),) * SD
        + (shape_of(F32, 8, 16, 128),)
        + tuple(shape_of(kind, *shape) for shape, kind in grads),
        in_specs=[SMEM, ANY, VMEM, VMEM] + [ANY] * (SD + 9),
        out_specs=(VMEM,) * (SD + 1) + (ANY,) * len(grads),
        scratch_shapes=[
            pltpu.VMEM((3 * D, D), BF),
            pltpu.VMEM((D, D), BF),
            pltpu.VMEM((FF, D), BF),
            pltpu.VMEM((FF, D), BF),
            pltpu.VMEM((SD, cap, D), BF),
        ]
        + [pltpu.VMEM(*a) for a in (rows, rows, rows, probs, wide, full, full, thin, thin, rows, rows, rows)]
        + [
            pltpu.VMEM(*rows),
            pltpu.VMEM((8, D), F32),
            pltpu.VMEM((1, FF), F32),
            dma((4,)),
            dma((4,)),
            dma((9,)),
            dma((6,)),
        ],
        compiler_params=pltpu.CompilerParams(vmem_limit_bytes=VMEM_LIMIT),
        cost_estimate=pl.CostEstimate(flops=2 * ROWS * WROWS * D, bytes_accessed=64 << 20, transcendentals=0),
        name="backward",
    )(positions, slots, vecs, meta, *cots, *saved)


WC = 8 * BLK


def weight_kernel(
    pos,
    x_h,
    heads_h,
    act_h,
    d_up_h,
    d_q_h,
    d_k_h,
    d_v_h,
    d_proj_h,
    hid_h,
    d_br_h,
    grads,
    x_c,
    heads,
    act,
    d_up,
    d_q,
    d_k,
    d_v,
    d_proj,
    hid,
    d_br,
    stage,
    i_sem,
    g_sem,
):
    refs = (
        (x_h, x_c),
        (d_q_h, d_q),
        (d_k_h, d_k),
        (d_v_h, d_v),
        (heads_h, heads),
        (d_proj_h, d_proj),
        (hid_h, hid),
        (d_up_h, d_up),
        (d_br_h, d_br),
        (act_h, act),
    )
    fetch = [pltpu.make_async_copy(src, dst, i_sem.at[i]) for i, (src, dst) in enumerate(refs)]
    for copy in fetch:
        copy.start()

    per = WC // BLK

    def g_copy(chunk, j, at):
        return pltpu.make_async_copy(
            stage.at[at, pl.ds(j * BLK, BLK)], grads.at[pos[chunk * per + j]], g_sem.at[at]
        )

    def put(chunk, left, right):
        at = lax.rem(chunk, 2)

        @pl.when(chunk >= 2)
        def _():
            for j in range(per):
                g_copy(chunk - 2, j, at).wait()

        stage[at] = mm(left, right, TN).astype(BF)
        for j in range(per):
            g_copy(chunk, j, at).start()

    first = 0
    for left, right, needs in (
        (x_c, d_q, (0, 1)),
        (x_c, d_k, (2,)),
        (x_c, d_v, (3,)),
        (heads, d_proj, (4, 5)),
        (d_up, hid, (6, 7)),
        (act, d_br, (8, 9)),
    ):
        for i in needs:
            fetch[i].wait()

        def body(j, left=left, right=right, first=first):
            put(first + j, left[:, pl.ds(pl.multiple_of(j * WC, WC), WC)], right[...])

        loop(left.shape[1] // WC, body)
        first += left.shape[1] // WC
    for chunk in (first - 2, first - 1):
        for j in range(per):
            g_copy(chunk, j, chunk % 2).wait()


def weight_grads_of(total_slots, positions, x_c, saved):
    r_v, w_v = pltpu.VMEM((ROWS, D), BF), pltpu.VMEM((ROWS, FF), BF)
    return pl.pallas_call(
        weight_kernel,
        out_shape=jax.ShapeDtypeStruct((total_slots, BLK, D), BF),
        in_specs=[SMEM] + [ANY] * 10,
        out_specs=ANY,
        scratch_shapes=[r_v, r_v, w_v, w_v]
        + [r_v] * 6
        + [
            pltpu.VMEM((2, WC, D), BF),
            pltpu.SemaphoreType.DMA((10,)),
            pltpu.SemaphoreType.DMA((2,)),
        ],
        compiler_params=pltpu.CompilerParams(vmem_limit_bytes=VMEM_LIMIT),
        cost_estimate=pl.CostEstimate(flops=2 * ROWS * WROWS * D, bytes_accessed=40 << 20, transcendentals=0),
        name="weight_grads",
    )(positions, x_c, *saved)


def adam_step(grad_now, weight_old, first_old, second_old, rate_step):
    first_new = beta_first * first_old + (1.0 - beta_first) * grad_now
    second_new = beta_second * second_old + (1.0 - beta_second) * grad_now * grad_now
    square = second_new * (1.0 / (1.0 - beta_second**STEP))
    root = jnp.where(square > 0.0, square * lax.rsqrt(square), 0.0)
    step = first_new * (1.0 / (1.0 - beta_first**STEP)) * inverse(root + adam_epsilon)
    return (first_new, second_new, weight_old - rate_step * (step + weight_decay * weight_old))


def finish_kernel(
    used,
    total_h,
    master_h,
    first_h,
    second_h,
    v_grad,
    v_master,
    v_first,
    v_second,
    line,
    counts,
    out_h,
    ing_h,
    grad_new,
    first_new,
    second_new,
    master_new,
    low_new,
    v_grad_new,
    v_first_new,
    v_second_new,
    v_master_new,
    v_low_new,
    entropy,
    occupancy,
    output,
    input_grad,
    total,
    master,
    first,
    second,
    grad,
    out_v,
    ing_v,
    in_s,
    out_s,
    row_s,
):
    count = total.shape[0]
    ins = ((total_h, total), (master_h, master), (first_h, first), (second_h, second))
    outs = ((total, low_new), (master, master_new), (first, first_new), (second, second_new), (grad, grad_new))

    def fetch(i, s):
        src, dst = ins[i]
        return pltpu.make_async_copy(src.at[s], dst.at[s], in_s.at[i, s])

    def put(i, s):
        src, dst = outs[i]
        return pltpu.make_async_copy(src.at[s], dst.at[s], out_s.at[i, s])

    def each(n, copy, act):
        def body(s):
            for i in range(n):
                act(copy(i, s))

        loop(count, body)

    rows_in = [pltpu.make_async_copy(a, b, row_s.at[0, n]) for n, (a, b) in enumerate(((out_h, out_v), (ing_h, ing_v)))]
    rows_out = [pltpu.make_async_copy(a, b, row_s.at[1, n]) for n, (a, b) in enumerate(((out_v, output), (ing_v, input_grad)))]
    each(4, fetch, lambda copy: copy.start())
    for copy in rows_in:
        copy.start()
    entropy[...] = line[...].reshape(ROWS)
    occupancy[...] = counts[...]
    length = v_master.shape[0]
    for n in range(-(-length // 128)):
        part = slice(n * 128, min((n + 1) * 128, length))
        g = v_grad[n : n + 1, 0 : part.stop - part.start].reshape(part.stop - part.start)
        m, v, w = adam_update(g, v_master[part], v_first[part], v_second[part], rate_vector)
        v_grad_new[part] = g
        v_first_new[part] = m
        v_second_new[part] = v
        v_master_new[part] = w
    v_low_new[...] = v_master_new[...].astype(BF)

    def slot(s):
        for i in range(4):
            fetch(i, s).wait()
        g = jnp.where(used[s] > 0, total[s].astype(F32), 0.0)
        m, v, w = adam_step(g, master[s], first[s], second[s], rate_matrix)
        grad[s] = g
        first[s] = m
        second[s] = v
        master[s] = w
        total[s] = w.astype(BF)
        for i in range(5):
            put(i, s).start()

    loop(count, slot)
    for copy_in, copy_out in zip(rows_in, rows_out):
        copy_in.wait()
        copy_out.start()
    each(5, put, lambda copy: copy.wait())
    for copy in rows_out:
        copy.wait()


def finish(used, total, weights, v_grad, vectors, line, counts, out, ing):
    count = total.shape[0]
    low, full = pltpu.VMEM((count, BLK, D), BF), pltpu.VMEM((count, BLK, D), F32)
    f32_slots, f32_vector = shape_of(F32, count, BLK, D), shape_of(F32, *vectors[0].shape)
    dma = pltpu.SemaphoreType.DMA
    return pl.pallas_call(
        finish_kernel,
        out_shape=(f32_slots,) * 4
        + (shape_of(BF, count, BLK, D),)
        + (f32_vector,) * 4
        + (shape_of(BF, *vectors[0].shape), shape_of(BF, ROWS), shape_of(I32, *counts.shape))
        + (shape_of(BF, ROWS, D),) * 2,
        in_specs=[SMEM] + [ANY] * 4 + [VMEM] * 6 + [ANY] * 2,
        out_specs=(ANY,) * 5 + (VMEM,) * 7 + (ANY,) * 2,
        scratch_shapes=[low, full, full, full, full]
        + [pltpu.VMEM((ROWS, D), BF)] * 2
        + [dma((4, count)), dma((5, count)), dma((2, 2))],
        compiler_params=pltpu.CompilerParams(vmem_limit_bytes=VMEM_LIMIT),
        name="finish",
    )(used, total, *weights, v_grad, *vectors, line, counts, out, ing)


def local(
    tokens,
    cotangent,
    cluster_order,
    block_owner,
    master_slots,
    moment_one,
    moment_two,
    vector_master,
    vector_moment_one,
    vector_moment_two,
):
    tok_count = lax.axis_size("tok")
    tok_index = lax.axis_index("tok")
    slot_count = master_slots.shape[0]
    cap = tok_count // SD * (max(1, CPS // tok_count) * 3 * CL // (2 * SD))
    total_slots = tok_count * slot_count
    order = cluster_order.reshape(1, ROWS)

    block = jax.ShapeDtypeStruct((SD, cap, D), BF)
    meta_shape = jax.ShapeDtypeStruct((SD, META, D), BF)
    row_block = jax.ShapeDtypeStruct((ROWS, D), BF)
    four_planes = tok_count == 8 and lax.axis_size("rep") == 4
    if four_planes:
        slots_low, x_c, *cots, recv_meta, vecs, b_u, occupancy, positions = gather_all(
            cap, tokens, cotangent, order, master_slots, vector_master, block_owner
        )
        positions = positions.reshape(NBLK)
        slots_low = slots_low.reshape(total_slots, BLK, D)
    else:
        positions = slot_positions(block_owner, slot_count)
        slots_low = lax.all_gather(master_slots.astype(BF), "tok", axis=0, tiled=True)
        vectors = lax.all_gather(vector_master.astype(BF), "tok", axis=0, tiled=True).astype(F32)
        vecs, b_u = vectors[: 8 * D].reshape(8, D), vectors[8 * D :].reshape(1, FF)
        cluster = tok_index // SD * CPS + cluster_order // CL
        target = cluster % tok_count
        chosen = target[None, :] == jnp.arange(tok_count, dtype=jnp.int32)[:, None]
        sent_counts = jnp.sum(chosen.astype(F32), axis=1)
        own_row = (jnp.arange(tok_count, dtype=jnp.int32) == tok_index).astype(F32)
        occupancy = lax.psum(own_row[:, None] * sent_counts[None, :], ("tok", "rep")).astype(jnp.int32)
        send_x, send_c, meta = pl.pallas_call(
            functools.partial(send_kernel, cap),
            out_shape=(block, block, meta_shape),
            in_specs=[VMEM] * 3,
            out_specs=(VMEM,) * 3,
            compiler_params=pltpu.CompilerParams(vmem_limit_bytes=VMEM_LIMIT),
            name="send_rows",
        )(tokens, cotangent, order)
        recv_x, recv_meta = (jnp.stack(swap_blocks(b)) for b in (send_x, meta))
        x_c = pl.pallas_call(
            functools.partial(seat_kernel, cap),
            out_shape=row_block,
            in_specs=[VMEM] * 2,
            out_specs=VMEM,
            compiler_params=pltpu.CompilerParams(vmem_limit_bytes=VMEM_LIMIT),
            name="seat_rows",
        )(recv_x, recv_meta)
        cots = [send_c[k] for k in range(SD)]

    cots = swap_blocks(cots)
    *out_blocks, heads, act, hid, q, k, v, p, slope, n1, n2, rs1, rs2 = forward(
        cap, positions, slots_low, vecs, b_u, x_c, recv_meta
    )
    out_blocks = swap_blocks(out_blocks)
    *ing_blocks, shares, d_up, d_q, d_k, d_v, d_proj, d_br = backward(
        cap, positions, slots_low, vecs, recv_meta, cots, (q, k, v, p, slope, n1, n2, rs1, rs2)
    )
    ing_blocks = swap_blocks(ing_blocks)
    grads = weight_grads_of(
        total_slots, positions, x_c, (heads, act, d_up, d_q, d_k, d_v, d_proj, hid, d_br)
    )
    if four_planes:
        total, vec_owned, output, input_grad, entropy = reduce_all(
            cap, grads, shares, order, out_blocks, ing_blocks, slot_count
        )
    else:
        total = lax.psum(lax.psum_scatter(grads, "tok", scatter_dimension=0, tiled=True), "rep")
        grad_vector = shares[:, 0:9].reshape(-1)
        vec_owned = lax.psum(lax.psum_scatter(grad_vector, "tok", scatter_dimension=0, tiled=True), "rep")
        vec_owned = jnp.pad(vec_owned, (0, -vec_owned.shape[0] % 128)).reshape(-1, 128)
        output, input_grad, entropy = pl.pallas_call(
            functools.partial(return_kernel, cap),
            out_shape=(row_block, row_block, jax.ShapeDtypeStruct((1, ROWS), BF)),
            in_specs=[VMEM] * (2 * SD + 1),
            out_specs=(VMEM,) * 3,
            compiler_params=pltpu.CompilerParams(vmem_limit_bytes=VMEM_LIMIT),
            name="return_rows",
        )(order, *out_blocks, *ing_blocks)

    used = jnp.any(
        positions[None, :] == (tok_index * slot_count + jnp.arange(slot_count, dtype=I32))[:, None], axis=1
    )
    (
        owned_grad,
        first_new,
        second_new,
        master_new,
        low_new,
        vec_owned,
        vec_first,
        vec_second,
        vec_new,
        vec_low_new,
        row_entropy,
        occupancy,
        output,
        input_grad,
    ) = finish(
        used.astype(I32),
        total,
        (master_slots, moment_one, moment_two),
        vec_owned,
        (vector_master, vector_moment_one, vector_moment_two),
        entropy,
        occupancy,
        output,
        input_grad,
    )
    return (
        output,
        input_grad,
        owned_grad,
        first_new,
        second_new,
        master_new,
        low_new,
        vec_owned,
        vec_first,
        vec_second,
        vec_new,
        vec_low_new,
        row_entropy,
        occupancy,
    )


def solution(mesh):
    placed = (
        P(("rep", "tok"), None),
        P(("rep", "tok"), None),
        P(("rep", "tok")),
        P(),
        P("tok", None, None),
        P("tok", None, None),
        P("tok", None, None),
        P("tok"),
        P("tok"),
        P("tok"),
    )
    return jax.shard_map(
        local,
        mesh=mesh,
        in_specs=placed,
        out_specs=(
            P(("rep", "tok"), None),
            P(("rep", "tok"), None),
            P("tok", None, None),
            P("tok", None, None),
            P("tok", None, None),
            P("tok", None, None),
            P("tok", None, None),
            P("tok"),
            P("tok"),
            P("tok"),
            P("tok"),
            P("tok"),
            P(("rep", "tok")),
            P(),
        ),
        check_vma=False,
    )
```

```python
import functools
import math

import jax
import jax.numpy as jnp
from jax import lax
from jax.experimental import pallas as pl
from jax.experimental.pallas import tpu as pltpu
from jax.sharding import PartitionSpec as P

D = 768
HEADS = 12
HD = 64
FF = 3072
SD = 4
CL = 128
NBLK = 96
STEP = 10
CPS = 32
WROWS = 9216
BLK = 96
ROWS = 1024
PAIRS = HEADS // 2
PW = 2 * HD
TM = 512
PART = 48
META = 16
VMEM_LIMIT = 63 << 20
FC = 768
FWD_AT = 4

norm_epsilon = 1e-06
beta_first = 0.9
beta_second = 0.999
adam_epsilon = 1e-08
weight_decay = 0.01
rate_matrix = 0.02
rate_vector = 0.2

BF = jnp.bfloat16
F32 = jnp.float32
I32 = jnp.int32

VMEM = pl.BlockSpec(memory_space=pltpu.VMEM)
SMEM = pl.BlockSpec(memory_space=pltpu.SMEM)
ANY = pl.BlockSpec(memory_space=pl.ANY)

NN = (((1,), (0,)), ((), ()))
NT = (((1,), (1,)), ((), ()))
TN = (((0,), (0,)), ((), ()))


def mm(a, b, dims=NN):
    return lax.dot_general(a, b, dims, preferred_element_type=F32)


def slot_positions(block_owner, slot_count):
    owners = block_owner[:, 0]
    blocks = owners.shape[0]
    shared = owners[:, None] == owners[None, :]
    before = (
        jnp.arange(blocks, dtype=jnp.int32)[None, :] < jnp.arange(blocks, dtype=jnp.int32)[:, None]
    )
    earlier = jnp.sum((shared & before).astype(jnp.int32), axis=1)
    return owners * slot_count + earlier


def adam_update(grad_now, weight_old, first_old, second_old, rate_step):
    first_new = beta_first * first_old + (1.0 - beta_first) * grad_now
    second_new = beta_second * second_old + (1.0 - beta_second) * grad_now * grad_now
    first_hat = first_new / (1.0 - beta_first**STEP)
    second_hat = second_new / (1.0 - beta_second**STEP)
    weight_new = weight_old - rate_step * (
        first_hat / (jnp.sqrt(second_hat) + adam_epsilon) + weight_decay * weight_old
    )
    return (first_new, second_new, weight_new)


def route_slots(order, seat, cap):
    cluster = order // CL
    rel = lax.rem(cluster, SD) ^ seat
    place = (cluster // SD) * CL + lax.rem(order, CL) + 1
    chosen = lax.broadcasted_iota(I32, (8, ROWS), 0) == rel
    chosen_low = jnp.where(chosen, 1.0, 0.0).astype(BF)
    before = lax.broadcasted_iota(I32, (ROWS, ROWS), 0) < lax.broadcasted_iota(I32, (ROWS, ROWS), 1)
    before_low = jnp.where(before, 1.0, 0.0).astype(BF)
    running = mm(chosen_low, before_low)
    rank = jnp.sum(jnp.where(chosen, running, 0.0), axis=0, keepdims=True).astype(I32)
    return rel * cap + rank, place


def slot_matrix(slots, at, cap):
    rows = lax.broadcasted_iota(I32, (cap, ROWS), 0) + at * cap
    return jnp.where(rows == slots, 1.0, 0.0).astype(BF)


def send_kernel(cap, tokens, cotangent, order, send_x, send_c, meta):
    seat = lax.rem(lax.axis_index("tok"), SD)
    slots, place = route_slots(order[...], seat, cap)
    digits = jnp.concatenate([place // CL, lax.rem(place, CL)] + [place * 0] * 6, axis=0).astype(F32).astype(BF)
    for at in range(SD):
        picked = slot_matrix(slots, at, cap)
        send_x[at] = mm(picked, tokens[...]).astype(BF)
        send_c[at] = mm(picked, cotangent[...]).astype(BF)
        coded = mm(digits, picked, NT)
        line = jnp.concatenate([coded[0:1], coded[1:2]], axis=1)
        meta[at] = jnp.broadcast_to(line, (META, D)).astype(BF)


def remote(src, dst, send_sem, recv_sem, tok, rep):
    return pltpu.make_async_remote_copy(
        src_ref=src,
        dst_ref=dst,
        send_sem=send_sem,
        recv_sem=recv_sem,
        device_id={"tok": tok, "rep": rep},
        device_id_type=pl.DeviceIdType.MESH,
    )


def loop(n, body):
    def run(i, c):
        body(i)
        return c

    lax.fori_loop(0, n, run, 0)


class Place:
    def __init__(self):
        self.me = me = lax.axis_index("tok")
        self.z = z = lax.axis_index("rep")
        core, x, y = me % 2, (me // 2) % 2, me // 4
        self.twin = me + 1 - 2 * core
        self.xn = me + 2 - 4 * x
        self.yn = me + 4 - 8 * y
        self.dn = self.xn + 4 - 8 * y
        self.side = z % 2
        self.zp = z + 1 - 2 * self.side

    def twin_of(self, tok):
        return tok + 1 - 2 * (tok % 2)

    def greet(self, peers):
        barrier = pltpu.get_barrier_semaphore()
        for tok, rep in peers:
            pl.semaphore_signal(
                barrier, inc=1, device_id={"tok": tok, "rep": rep}, device_id_type=pl.DeviceIdType.MESH
            )
        return lambda: pl.semaphore_wait(barrier, len(peers))


def seat_matrix(meta, first, rows, cap):
    hi = jnp.concatenate([meta[k, 0:8, 0:cap] for k in range(SD)], axis=1).astype(F32)[0:1]
    lo = jnp.concatenate([meta[k, 0:8, cap : 2 * cap] for k in range(SD)], axis=1).astype(F32)[0:1]
    at = (hi * CL + lo).astype(I32)
    seats = lax.broadcasted_iota(I32, (rows, SD * cap), 0) + (first + 1)
    return jnp.where(seats == at, 1.0, 0.0).astype(BF)


def seat_part(meta, k, cap):
    hi = meta[k, 0:8, 0:cap].astype(F32)[0:1]
    lo = meta[k, 0:8, cap : 2 * cap].astype(F32)[0:1]
    at = (hi * CL + lo).astype(I32)
    seats = lax.broadcasted_iota(I32, (ROWS, cap), 0) + 1
    return jnp.where(seats == at, 1.0, 0.0).astype(BF)


def seat_rows(meta, blocks, cap, to):
    def body(t):
        r0 = pl.multiple_of(t * 256, 256)
        rows = blocks[...].reshape(SD * cap, D)
        to[pl.ds(r0, 256), :] = mm(seat_matrix(meta, r0, 256, cap), rows).astype(BF)

    loop(ROWS // 256, body)


def seat_kernel(cap, blocks, meta, to):
    seat_rows(meta, blocks, cap, to)


def gather_kernel(
    cap,
    count,
    tokens_h,
    cotangent_h,
    order,
    master_h,
    vector,
    owner_of,
    slots,
    x_c,
    cot_0,
    cot_1,
    cot_2,
    cot_3,
    recv_meta,
    vecs,
    b_u,
    occupancy,
    positions,
    tokens,
    cotangent,
    master,
    own,
    send_x,
    send_c,
    meta,
    recv_x,
    got_meta,
    slot_of,
    digits,
    mine,
    by_z,
    by_tok,
    x_s,
    x_r,
    y_s,
    y_r,
    d_s,
    d_r,
    zx_s,
    zx_r,
    zd_s,
    zd_r,
    zy_s,
    zy_r,
    p_s,
    p_r,
    row_s,
    row_r,
    z_s,
    z_r,
    t_s,
    t_r,
    local_s,
):
    at = Place()
    me, z, side = at.me, at.z, at.side
    n_tok, n_rep = 8, 4
    peers = [((me + d) % n_tok, z) for d in range(1, n_tok)] + [(me, (z + d) % n_rep) for d in range(1, n_rep)]
    fetch = [
        pltpu.make_async_copy(src, dst, local_s.at[i])
        for i, (src, dst) in enumerate(((master_h, master), (tokens_h, tokens), (cotangent_h, cotangent)))
    ]
    for copy in fetch:
        copy.start()
    wait_peers = at.greet(peers)
    fetch[0].wait()

    last = count - 1

    def near(j):
        return side * last + (1 - 2 * side) * j

    def far(j):
        return (1 - side) * last - (1 - 2 * side) * j

    few_x, few_d, few_y = 11 * count // 26, 12 * count // 26, 8 * count // 26
    most_x, most_d, most_y = count - few_x, count - few_d, count - few_y

    def piece(owner, s):
        return slots.at[owner * count + s]

    def to_x(s):
        return remote(own.at[s], piece(me, s), x_s.at[s], x_r.at[s], at.xn, z)

    def to_y(s):
        return remote(own.at[s], piece(me, s), y_s.at[s], y_r.at[s], at.yn, z)

    def on_y(s):
        return remote(piece(at.xn, s), piece(at.xn, s), d_s.at[s], d_r.at[s], at.yn, z)

    def x_on_z(s):
        return remote(piece(at.xn, s), piece(at.xn, s), zx_s.at[s], zx_r.at[s], me, at.zp)

    def d_on_z(s):
        return remote(piece(at.dn, s), piece(at.dn, s), zd_s.at[s], zd_r.at[s], me, at.zp)

    def y_on_z(s):
        return remote(piece(at.yn, s), piece(at.yn, s), zy_s.at[s], zy_r.at[s], me, at.zp)

    def x_in(s):
        return remote(own.at[s], piece(at.xn, s), x_s.at[s], x_r.at[s], at.xn, z)

    def y_in(s):
        return remote(own.at[s], piece(at.yn, s), y_s.at[s], y_r.at[s], at.yn, z)

    def d_in(s):
        return remote(own.at[s], piece(at.dn, s), d_s.at[s], d_r.at[s], at.yn, z)

    owners = (me, at.xn, at.yn, at.dn)

    def near_run(q, j0, j1):
        return (q, (1 - side) * j0 + side * (count - j1), j1 - j0)

    def far_run(q, j0, j1):
        return (q, side * j0 + (1 - side) * (count - j1), j1 - j0)

    runs = (
        (0, 0, count),
        near_run(2, 0, few_y),
        near_run(1, 0, most_x),
        near_run(3, 0, most_d),
        far_run(1, 0, few_x),
        near_run(2, few_y, most_y),
        far_run(2, 0, few_y),
        far_run(3, 0, few_d // 2),
        far_run(3, few_d // 2, few_d - 2),
        far_run(3, few_d - 2, few_d),
    )

    def to_twin(i):
        q, s, n = runs[i]
        src = own if q == 0 else slots.at[pl.ds(owners[q] * count + s, n)]
        dst = slots.at[pl.ds(owners[q] * count + s, n)]
        return remote(src, dst, p_s.at[i], p_r.at[i], at.twin, z)

    def cast(j):
        own[near(j)] = master[near(j)].astype(BF)

    loop(most_x, cast)
    wait_peers()
    loop(most_x, lambda j: to_x(near(j)).start())
    loop(few_y, lambda j: to_y(near(j)).start())
    loop(count - most_x, lambda j: cast(most_x + j))
    to_twin(0).start()
    keep = pltpu.make_async_copy(own, slots.at[pl.ds(me * count, count)], local_s.at[3])
    keep.start()

    seat = me % SD
    seats = (me, at.twin, at.xn, at.twin_of(at.xn))
    rows_of = ((meta, got_meta), (send_x, recv_x))

    def row_copy(i, k):
        src, dst = rows_of[i]
        return remote(src.at[k], dst.at[k], row_s.at[i, k], row_r.at[i, k], seats[k], z)

    put_c = [
        pltpu.make_async_copy(send_c.at[k], to, local_s.at[4 + k])
        for k, to in enumerate((cot_0, cot_1, cot_2, cot_3))
    ]

    def route():
        fetch[1].wait()
        fetch[2].wait()
        slots_here, place = route_slots(order[...], seat, cap)
        slot_of[...] = slots_here
        digits[...] = (
            jnp.concatenate([place // CL, lax.rem(place, CL)] + [place * 0] * 6, axis=0).astype(F32).astype(BF)
        )

    def sort_tokens(k):
        picked = slot_matrix(slot_of[...], k, cap)
        send_x[k] = mm(picked, tokens[...]).astype(BF)
        coded = mm(digits[...], picked, NT)
        line = jnp.concatenate([coded[0:1], coded[1:2]], axis=1)
        meta[k] = jnp.broadcast_to(line, (META, D)).astype(BF)
        for i in range(2):
            if k:
                row_copy(i, k).start()
            else:
                src, dst = rows_of[i]
                dst[0] = src[0]

    def sort_cotangent(k):
        send_c[k] = mm(slot_matrix(slot_of[...], k, cap), cotangent[...]).astype(BF)
        put_c[k].start()

    def z_copy(d):
        return remote(by_z.at[0], by_z.at[d], z_s.at[d], z_r.at[d], me, (z + d) % n_rep)

    def t_copy(d):
        return remote(mine, by_tok.at[d], t_s.at[d], t_r.at[d], (me + d) % n_tok, z)

    def count_rows():
        residue = lax.rem(me // SD * CPS + order[...] // CL, n_tok)
        hit = lax.broadcasted_iota(I32, (128, ROWS), 0) == residue
        by_z[0] = mm(jnp.ones((8, ROWS), BF), jnp.where(hit, 1.0, 0.0).astype(BF), NT)
        for d in range(1, n_rep):
            z_copy(d).start()
        for i in range(9):
            mine[i : i + 1] = vector[i * 128 : (i + 1) * 128].reshape(1, 128).astype(BF).astype(F32)
        block_row = lax.broadcasted_iota(I32, (NBLK, NBLK), 0)
        block_col = lax.broadcasted_iota(I32, (NBLK, NBLK), 1)
        by_col = owner_of[...].astype(F32)
        by_row = lane_sum(jnp.where(block_row == block_col, by_col, 0.0))
        earlier = jnp.where((by_row == by_col) & (block_row < block_col), 1.0, 0.0)
        positions[...] = (by_col * (count * PART // BLK) + jnp.sum(earlier, axis=0, keepdims=True)).astype(I32)

    def share_vectors():
        for d in range(1, n_rep):
            z_copy(d).wait()
        mine[16:24] = by_z[0] + by_z[1] + by_z[2] + by_z[3]
        for d in range(1, n_tok):
            t_copy(d).start()

    def lay_out_vectors():
        by_tok[0] = mine[...]
        for d in range(1, n_tok):
            t_copy(d).wait()
        for owner in range(n_tok):
            share = by_tok[(me + n_tok - owner) % n_tok]
            occupancy[owner : owner + 1, :] = share[16:17, 0:n_tok].astype(I32)
            for i in range(9):
                chunk = owner * 9 + i
                row, lane = chunk // 6, chunk % 6 * 128
                if row < 8:
                    vecs[row : row + 1, lane : lane + 128] = share[i : i + 1]
                else:
                    lane += (row - 8) * D
                    b_u[:, lane : lane + 128] = share[i : i + 1]

    between = {
        1: lambda: (route(), sort_tokens(2)),
        3: lambda: sort_tokens(3),
        5: lambda: sort_tokens(1),
        7: lambda: (sort_tokens(0), count_rows()),
        9: lambda: sort_cotangent(1),
        11: lambda: sort_cotangent(2),
        13: lambda: sort_cotangent(3),
    }
    for j in range(most_x):
        x_in(near(j)).wait_recv()
        if j < most_d:
            on_y(near(j)).start()
        if j < few_x:
            x_on_z(near(j)).start()
        if j < few_y:
            y_in(near(j)).wait_recv()
            y_on_z(near(j)).start()
        if j == few_y:
            to_twin(1).start()
        if j in between:
            between[j]()
    to_twin(2).start()
    loop(most_y - few_y, lambda j: to_y(near(few_y + j)).start())
    share_vectors()
    sort_cotangent(0)

    def diagonal(j):
        d_in(near(j)).wait_recv()
        d_on_z(near(j)).start()

    loop(few_d, diagonal)
    loop(most_d - few_d, lambda j: d_in(near(few_d + j)).wait_recv())
    to_twin(3).start()
    loop(few_x, lambda j: x_on_z(far(j)).wait_recv())
    to_twin(4).start()
    lay_out_vectors()
    loop(most_x, lambda j: to_x(near(j)).wait_send())
    loop(few_x, lambda j: x_on_z(near(j)).wait_send())
    loop(few_y, lambda j: y_on_z(near(j)).wait_send())
    loop(most_y - few_y, lambda j: y_in(near(few_y + j)).wait_recv())
    to_twin(5).start()
    loop(few_y, lambda j: y_on_z(far(j)).wait_recv())
    to_twin(6).start()
    for i in (0, 1):
        for k in (2, 3, 1):
            row_copy(i, k).wait_recv()
    recv_meta[...] = got_meta[...]
    seat_rows(got_meta, recv_x, cap, x_c)
    loop(most_y, lambda j: to_y(near(j)).wait_send())
    loop(most_d, lambda j: on_y(near(j)).wait_send())
    done = 0
    for i, upto in ((7, few_d // 2), (8, few_d - 2), (9, few_d)):
        loop(upto - done, lambda j, done=done: d_on_z(far(done + j)).wait_recv())
        to_twin(i).start()
        done = upto

    for i in range(2):
        for k in (2, 3, 1):
            row_copy(i, k).wait_send()
    for copy in put_c:
        copy.wait()
    keep.wait()

    loop(few_d, lambda j: d_on_z(near(j)).wait_send())
    for i in range(len(runs)):
        to_twin(i).wait()


def gather_all(cap, tokens, cotangent, order, master, vector, block_owner):
    count = master.shape[0] * BLK // PART
    rows = jax.ShapeDtypeStruct((ROWS, D), BF)
    part = jax.ShapeDtypeStruct((cap, D), BF)
    dma = pltpu.SemaphoreType.DMA
    block = pltpu.VMEM((SD, cap, D), BF)
    meta = pltpu.VMEM((SD, META, D), BF)
    return pl.pallas_call(
        functools.partial(gather_kernel, cap, count),
        out_shape=(
            jax.ShapeDtypeStruct((8 * count, PART, D), BF),
            rows,
            part,
            part,
            part,
            part,
            jax.ShapeDtypeStruct((SD, META, D), BF),
            jax.ShapeDtypeStruct((8, D), F32),
            jax.ShapeDtypeStruct((1, FF), F32),
            jax.ShapeDtypeStruct((8, 8), I32),
            jax.ShapeDtypeStruct((1, NBLK), I32),
        ),
        in_specs=[ANY, ANY, VMEM, ANY, VMEM, VMEM],
        out_specs=(ANY, VMEM) + (ANY,) * SD + (VMEM,) * 5,
        scratch_shapes=[
            pltpu.VMEM((ROWS, D), BF),
            pltpu.VMEM((ROWS, D), BF),
            pltpu.VMEM((count, PART, D), F32),
            pltpu.VMEM((count, PART, D), BF),
            block,
            block,
            meta,
            block,
            meta,
            pltpu.VMEM((1, ROWS), I32),
            pltpu.VMEM((8, ROWS), BF),
            pltpu.VMEM((24, 128), F32),
            pltpu.VMEM((4, 8, 128), F32),
            pltpu.VMEM((8, 24, 128), F32),
        ]
        + [dma((count,))] * 12
        + [dma((10,))] * 2
        + [dma((2, SD))] * 2
        + [dma((4,))] * 2
        + [dma((8,))] * 2
        + [dma((8,))],
        compiler_params=pltpu.CompilerParams(collective_id=0, has_side_effects=True, vmem_limit_bytes=VMEM_LIMIT),
        cost_estimate=pl.CostEstimate(flops=8 * ROWS * ROWS * D, bytes_accessed=64 << 20, transcendentals=0),
        name="gather",
    )(tokens, cotangent, order, master.reshape(count, PART, D), vector, block_owner.reshape(1, NBLK))


def return_kernel(cap, order, *refs):
    outs, ings, (out, ing, entropy) = refs[:SD], refs[SD : 2 * SD], refs[2 * SD :]
    seat = lax.rem(lax.axis_index("tok"), SD)
    slots, _ = route_slots(order[...], seat, cap)
    picked = jnp.concatenate([slot_matrix(slots, at, cap) for at in range(SD)], axis=0)
    for to, blocks in ((out, outs), (ing, ings)):
        rows = jnp.concatenate([block[0:cap, :] for block in blocks], axis=0)
        to[...] = mm(picked, rows, TN).astype(BF)
    line = jnp.concatenate([block[cap : cap + 8, 0:cap] for block in outs], axis=1)
    entropy[...] = mm(line, picked)[0:1].astype(BF)


def swap_blocks(blocks):
    n = lax.axis_size("tok")
    parts = [blocks[0]]
    for k in range(1, SD):
        parts.append(lax.ppermute(blocks[k], "tok", [(i, i ^ k) for i in range(n)]))
    return parts


def reduce_kernel(
    cap,
    count,
    split,
    grads,
    vec,
    order,
    out_0,
    out_1,
    out_2,
    out_3,
    ing_0,
    ing_1,
    ing_2,
    ing_3,
    total,
    vec_out,
    output,
    input_grad,
    entropy,
    out_v,
    ing_v,
    slot_of,
    a,
    tw,
    rd,
    rx,
    ry,
    o,
    rz1,
    pz,
    rz2,
    fz,
    vt,
    va,
    vb,
    vc,
    a_l,
    keep_l,
    p_s,
    p_r,
    d_s,
    d_r,
    x_s,
    x_r,
    y_s,
    y_r,
    z1_s,
    z1_r,
    z2_s,
    z2_r,
    z3_s,
    z3_r,
    t_s,
    t_r,
    v_s,
    v_r,
    row_l,
):
    at = Place()
    me, z = at.me, at.z
    n_tok, n_rep = 8, 4
    peers = [((me + d) % n_tok, z) for d in range(1, n_tok)] + [(me, (z + d) % n_rep) for d in range(1, n_rep)]
    wait_peers = at.greet(peers)
    owners = (me, at.xn, at.yn, at.dn)

    def load(q):
        return pltpu.make_async_copy(grads.at[pl.ds(owners[q] * count, count)], a.at[q], a_l.at[q])

    for q in (3, 1, 2, 0):
        load(q).start()
    rows_in = [
        pltpu.make_async_copy(src, to.at[k], row_l.at[i, k])
        for i, (blocks, to) in enumerate((((out_0, out_1, out_2, out_3), out_v), ((ing_0, ing_1, ing_2, ing_3), ing_v)))
        for k, src in enumerate(blocks)
    ]
    for copy in rows_in:
        copy.start()
    wait_peers()

    def to_twin(q, g):
        src = grads.at[pl.ds(at.twin_of(owners[q]) * count + 2 * g, 2)]
        return remote(src, tw.at[q, pl.ds(2 * g, 2)], p_s.at[q, g], p_r.at[q, g], at.twin, z)

    def d_y(s):
        return remote(a.at[3, s], rd.at[s], d_s.at[s], d_r.at[s], at.yn, z)

    def d_x(s):
        return remote(a.at[3, s], rd.at[s], d_s.at[s], d_r.at[s], at.xn, z)

    def to_x(s):
        return remote(a.at[1, s], rx.at[s], x_s.at[s], x_r.at[s], at.xn, z)

    def to_y(s):
        return remote(a.at[2, s], ry.at[s], y_s.at[s], y_r.at[s], at.yn, z)

    def z_in(s):
        return remote(o.at[s], rz1.at[s], z1_s.at[s], z1_r.at[s], me, at.zp)

    def z_swap(s):
        return remote(pz.at[s], rz2.at[s], z2_s.at[s], z2_r.at[s], me, n_rep - 1 - z)

    def z_out(s):
        return remote(fz.at[s], fz.at[s], z3_s.at[s], z3_r.at[s], me, at.zp)

    def keep(s):
        return pltpu.make_async_copy(fz.at[s], total.at[s], keep_l.at[s])

    def twin_start(g):
        for q in (3, 1, 2, 0):
            to_twin(q, g).start()

    loop(count // 2, twin_start)

    def v_tok(d):
        return remote(vec.at[(me + d) % n_tok], vt.at[d], t_s.at[d], t_r.at[d], (me + d) % n_tok, z)

    def v_rep(i, src):
        return remote(src, vb.at[i], v_s.at[i], v_r.at[i], me, at.zp if i == 0 else (z + 2) % n_rep)

    for d in range(1, n_tok):
        v_tok(d).start()

    def join(q, s):
        return a[q, s] + tw[q, s]

    def first(s, send):
        a[3, s] = join(3, s)
        send(s).start()

    def plain(q, s, send):
        a[q, s] = join(q, s)
        send(s).start()

    def joined(q, s, arrived, send):
        arrived(s).wait_recv()
        a[q, s] = join(q, s) + rd[s]
        send(s).start()

    inner = (z == 1) | (z == 2)
    outer = (z == 0) | (z == 3)

    def own(s):
        to_x(s).wait_recv()
        to_y(s).wait_recv()
        o[s] = join(0, s) + (rx[s] + ry[s])
        pl.when(outer)(lambda: z_in(s).start())

    def middle(s):
        @pl.when(inner)
        def _():
            z_in(s).wait_recv()
            pz[s] = o[s] + rz1[s]
            z_swap(s).start()

    def last(s):
        @pl.when(inner)
        def _():
            z_swap(s).wait_recv()
            fz[s] = pz[s] + rz2[s]
            z_out(s).start()
            keep(s).start()

    def taken(s):
        @pl.when(outer)
        def _():
            z_out(s).wait_recv()
            keep(s).start()

    def twin_sent(g):
        for q in range(4):
            to_twin(q, g).wait_send()

    def sent(s):
        d_y(s).wait_send()
        to_x(s).wait_send()
        to_y(s).wait_send()
        keep(s).wait()

        @pl.when(outer)
        def _():
            z_in(s).wait_send()

        @pl.when(inner)
        def _():
            z_swap(s).wait_send()
            z_out(s).wait_send()

    def pick_rows(i):
        ts = pl.ds(pl.multiple_of(i * 256, 256), 256)
        hit = lax.broadcasted_iota(I32, (SD * cap, 256), 0) == slot_of[:, ts]
        picked = jnp.where(hit, 1.0, 0.0).astype(BF)
        outs = jnp.concatenate([out_v[k, 0:cap, :] for k in range(SD)], axis=0)
        ings = jnp.concatenate([ing_v[k] for k in range(SD)], axis=0)
        both = mm(picked, jnp.concatenate([outs, ings], axis=1), TN)
        output[ts, :] = both[:, 0:D].astype(BF)
        input_grad[ts, :] = both[:, D:].astype(BF)
        line = jnp.concatenate([out_v[k, cap : cap + 8, 0:cap] for k in range(SD)], axis=1)
        entropy[:, ts] = mm(line, picked)[0:1].astype(BF)

    for q in (3, 1, 2, 0):
        load(q).wait()

    def steps(i, lag, more):
        s = i - lag
        by_x = (s % 2 == 0) & (s < 2 * split)
        live = (s >= 0) & (s < count)
        pl.when(live & by_x)(lambda: more(s, True))
        pl.when(live & jnp.logical_not(by_x))(lambda: more(s, False))

    def steps_of(i, lag, more):
        pl.when((i >= lag) & (i < count + lag))(lambda: more(i - lag))

    def round_of(i):
        for lag, which in ((0, (3,)), (1, (1, 2)), (6, (0,))):

            @pl.when((i >= lag) & ((i - lag) % 2 == 0) & (i < count + lag))
            def _(lag=lag, which=which):
                for q in which:
                    to_twin(q, (i - lag) // 2).wait_recv()

        steps(i, 0, lambda s, by_x: first(s, d_x if by_x else d_y))
        steps(i, 1, lambda s, by_x: plain(1, s, to_x) if by_x else plain(2, s, to_y))
        steps(i, 3, lambda s, by_x: joined(2, s, d_x, to_y) if by_x else joined(1, s, d_y, to_x))
        steps_of(i, 6, own)
        steps_of(i, 8, middle)
        steps_of(i, 10, last)
        steps_of(i, 12, taken)
        steps_of(i, 14, sent)
        pl.when((i >= 8) & (i % 2 == 0) & (i < count + 8))(lambda: twin_sent((i - 8) // 2))

    loop(3, round_of)
    for copy in rows_in:
        copy.wait()
    slots_here, _ = route_slots(order[...], me % SD, cap)
    slot_of[...] = slots_here

    v_sum = vec[me]
    for d in range(1, n_tok):
        v_tok(d).wait()
        v_sum = v_sum + vt[d]
    va[...] = v_sum
    v_rep(0, va).start()

    def four_rounds(i):
        loop(4, lambda j: round_of(3 + 4 * i + j))
        pick_rows(i)

    four_rounds(0)
    v_rep(0, va).wait()
    vc[...] = va[...] + vb[0]
    v_rep(1, vc).start()
    loop(3, lambda i: four_rounds(1 + i))
    loop(count + 12 - 19, lambda i: round_of(19 + i))
    v_rep(1, vc).wait()
    vec_out[...] = vc[...] + vb[1]

    loop(2, lambda j: sent(count - 2 + j))


def reduce_all(cap, grads, shares, order, outs, ings, count):
    dma = pltpu.SemaphoreType.DMA
    count = count * BLK // PART
    part = pltpu.VMEM((count, PART, D), BF)
    whole = pltpu.VMEM((4, count, PART, D), BF)
    line = pltpu.VMEM((16, 128), F32)
    rows = jax.ShapeDtypeStruct((ROWS, D), BF)
    total, vec, output, input_grad, entropy = pl.pallas_call(
        functools.partial(reduce_kernel, cap, count, count // 2),
        out_shape=(
            jax.ShapeDtypeStruct((count, PART, D), BF),
            jax.ShapeDtypeStruct((16, 128), F32),
            rows,
            rows,
            jax.ShapeDtypeStruct((1, ROWS), BF),
        ),
        in_specs=[ANY, VMEM, VMEM] + [ANY] * (2 * SD),
        out_specs=(ANY,) + (VMEM,) * 4,
        scratch_shapes=[
            pltpu.VMEM((SD, cap + META, D), BF),
            pltpu.VMEM((SD, cap, D), BF),
            pltpu.VMEM((1, ROWS), I32),
            whole,
            whole,
        ]
        + [part] * 8
        + [pltpu.VMEM((8, 16, 128), F32), line, pltpu.VMEM((2, 16, 128), F32), line]
        + [dma((4,)), dma((count,))]
        + [dma((4, count // 2))] * 2
        + [dma((count,))] * 12
        + [dma((8,))] * 2
        + [dma((2,))] * 2
        + [dma((2, SD))],
        compiler_params=pltpu.CompilerParams(collective_id=1, has_side_effects=True, vmem_limit_bytes=VMEM_LIMIT),
        cost_estimate=pl.CostEstimate(flops=4 * ROWS * ROWS * D, bytes_accessed=64 << 20, transcendentals=0),
        name="reduce",
    )(grads.reshape(-1, PART, D), shares, order, *outs, *ings)
    return total.reshape(-1, BLK, D), vec, output, input_grad, entropy


V_BQ, V_BV, V_BO, V_BD, V_G1, V_C1, V_G2, V_C2 = range(8)


def inverse(x):
    r = pl.reciprocal(x, approx=True)
    return r * (2.0 - x * r)


def erf_parts(v):
    t = inverse(1.0 + (0.3275911 / math.sqrt(2.0)) * jnp.abs(v))
    e = jnp.exp2((v * v) * (-0.5 / math.log(2.0)))
    poly = 0.5 * 1.061405429
    for c in (-1.453152027, 1.421413741, -0.284496736, 0.254829592):
        poly = poly * t + 0.5 * c
    tail = poly * (t * e)
    return jnp.where(v >= 0.0, 1.0 - tail, tail), e


def lane_sum(x):
    return jnp.sum(x, axis=1, keepdims=True)


def gelu_parts(v):
    phi, e = erf_parts(v)
    return v * phi, phi + v * (e * (1.0 / math.sqrt(2.0 * math.pi)))


def weight_copies(pos, slots, w, sem, first):
    def copy(b):
        return pltpu.make_async_copy(slots.at[pos[first + b]], w.at[pl.ds(b * BLK, BLK)], sem)

    n = w.shape[0] // BLK
    return (lambda: loop(n, lambda b: copy(b).start())), (lambda: loop(n, lambda b: copy(b).wait()))


def halves_of_heads():
    lane = lax.broadcasted_iota(I32, (1, PW), 1)
    m0 = jnp.where(lane < HD, 1.0, 0.0).astype(BF)
    m1 = jnp.where(lane < HD, 0.0, 1.0).astype(BF)
    return lambda pair: jnp.concatenate([pair * m0, pair * m1], axis=0)


def tile_rows(t):
    return pl.ds(pl.multiple_of(t * TM, TM), TM)


def forward_kernel(
    cap,
    pos,
    slots,
    vecs,
    b_u,
    x_h,
    meta,
    back_0,
    back_1,
    back_2,
    back_3,
    heads_h,
    act_h,
    hid_h,
    q_h,
    k_h,
    v_h,
    p_h,
    slope_h,
    n1_h,
    n2_h,
    rs1_h,
    rs2_h,
    wqkv,
    wo,
    wu,
    wd,
    x_c,
    heads,
    act,
    hid,
    q,
    k,
    v,
    p_all,
    slope,
    n1,
    n2,
    rs1,
    rs2,
    out_c,
    ent,
    hid_t,
    w_sem,
    x_sem,
    o_sem,
):
    inv = 1.0 / math.sqrt(HD)
    get_x = pltpu.make_async_copy(x_h, x_c, x_sem)
    get_x.start()
    weights = [
        weight_copies(pos, slots, w, w_sem.at[i], first)
        for i, (w, first) in enumerate(((wqkv, 0), (wo, 24), (wu, 32), (wd, 64)))
    ]
    for start, _ in weights:
        start()
    get_x.wait()
    apart = halves_of_heads()

    def vec(i):
        return vecs[i : i + 1, :]

    saved = (
        (heads, heads_h),
        (act, act_h),
        (hid, hid_h),
        (q, q_h),
        (k, k_h),
        (v, v_h),
        (slope, slope_h),
        (n1, n1_h),
        (n2, n2_h),
        (rs1, rs1_h),
        (rs2, rs2_h),
    )

    def save(t, i):
        src, dst = saved[i]
        return pltpu.make_async_copy(src.at[tile_rows(t)], dst.at[tile_rows(t)], o_sem.at[i])

    def save_p(t):
        n = TM // CL
        cs = pl.ds(t * n, n)
        return pltpu.make_async_copy(p_all.at[cs], p_h.at[cs], o_sem.at[len(saved)])

    def normal(r, n, rs, rows):
        c = r - lane_sum(r) * (1.0 / D)
        scale = lax.rsqrt(lane_sum(c * c) * (1.0 / D) + norm_epsilon)
        rs[rows, :] = jnp.broadcast_to(scale, (TM, 128))
        n[rows, :] = c * scale

    def tile(t):
        rows = tile_rows(t)
        first = t == 0
        pl.when(first)(weights[0][1])
        x = x_c[rows, :]
        q[rows, :] = ((mm(x, wqkv[0:D, :]) + vec(V_BQ)).astype(BF).astype(F32) * inv).astype(BF)
        k[rows, :] = mm(x, wqkv[D : 2 * D, :]).astype(BF)
        v[rows, :] = (mm(x, wqkv[2 * D :, :]) + vec(V_BV)).astype(BF)

        def attend(c):
            groups = [pl.ds(pl.multiple_of(t * TM + (FWD_AT * c + i) * CL, CL), CL) for i in range(FWD_AT)]
            pairs = [(i, p, slice(p * PW, (p + 1) * PW)) for i in range(FWD_AT) for p in range(PAIRS)]
            scores = [mm(apart(k[groups[i], ps]), q[groups[i], ps], NT) for i, _, ps in pairs]
            total = [jnp.zeros((1, CL), F32)] * FWD_AT
            probs = []
            for (i, _, _), both in zip(pairs, scores):
                halves = []
                for h in range(2):
                    sh = both[h * CL : (h + 1) * CL]
                    sh = sh - jnp.max(sh, axis=0, keepdims=True)
                    e = jnp.exp(sh)
                    tot = jnp.sum(e, axis=0, keepdims=True)
                    r = 1.0 / tot
                    total[i] += jnp.log(tot) - jnp.sum(e * sh, axis=0, keepdims=True) * r
                    halves.append((e * r).astype(BF))
                probs.append(jnp.concatenate(halves, axis=0))
            mixed = [mm(w, apart(v[groups[i], ps]), TN).astype(BF) for (i, _, ps), w in zip(pairs, probs)]
            for (i, p, ps), w, o in zip(pairs, probs, mixed):
                p_all[t * (TM // CL) + FWD_AT * c + i, p] = w
                heads[groups[i], ps] = o
            for i in range(FWD_AT):
                ent[:, groups[i]] = jnp.broadcast_to(total[i] * (1.0 / HEADS), (8, CL))

        loop(TM // CL // FWD_AT, attend)
        for i in (0, 3, 4, 5):
            save(t, i).start()
        save_p(t).start()
        pl.when(first)(weights[1][1])
        normal(x_c[rows, :].astype(F32) + mm(heads[rows, :], wo[...]) + vec(V_BO), n1, rs1, rows)
        hidden = n1[rows, :] * vec(V_G1) + vec(V_C1)
        hid[rows, :] = hidden.astype(BF)
        hid_t[...] = hidden
        pl.when(first)(weights[2][1])

        def widen(f):
            parts = [pl.ds(pl.multiple_of((2 * f + i) * FC, FC), FC) for i in range(2)]
            ups = [mm(hid[rows, :], wu[fs, :], NT) for fs in parts]
            for fs, up in zip(parts, ups):
                g, g_slope = gelu_parts(up + b_u[:, fs])
                act[rows, fs] = g.astype(BF)
                slope[rows, fs] = g_slope.astype(BF)

        loop(FF // FC // 2, widen)
        for i in (1, 2, 6, 7, 9):
            save(t, i).start()
        pl.when(first)(weights[3][1])
        normal(hid_t[...] + mm(act[rows, :], wd[...]) + vec(V_BD), n2, rs2, rows)
        out_c[rows, :] = (n2[rows, :] * vec(V_G2) + vec(V_C2)).astype(BF)
        for i in (8, 10):
            save(t, i).start()

    loop(ROWS // TM, tile)

    for j, back in enumerate((back_0, back_1, back_2, back_3)):
        own = seat_part(meta, j, cap)
        back[0:cap, :] = mm(own, out_c[...], TN).astype(BF)
        line = mm(ent[...].astype(BF), own)
        back[cap:, :] = jnp.concatenate([line, line], axis=1)[0:1].astype(BF) * jnp.ones((META, 1), BF)

    def saved_all(t):
        for i in range(len(saved)):
            save(t, i).wait()
        save_p(t).wait()

    loop(ROWS // TM, saved_all)


def shape_of(kind, *shape):
    return jax.ShapeDtypeStruct(shape, kind)


def saved_shapes():
    rows, wide = ((ROWS, D), BF), ((ROWS, FF), BF)
    probs = ((ROWS // CL, PAIRS, 2 * CL, CL), BF)
    full, thin = ((ROWS, D), F32), ((ROWS, 128), F32)
    return rows, wide, probs, full, thin


def forward(cap, positions, slots, vecs, b_u, x_c, meta):
    rows, wide, probs, full, thin = saved_shapes()
    kept = (rows, wide, rows, rows, rows, rows, probs, wide, full, full, thin, thin)
    dma = pltpu.SemaphoreType.DMA
    return pl.pallas_call(
        functools.partial(forward_kernel, cap),
        out_shape=(shape_of(BF, cap + META, D),) * SD + tuple(shape_of(kind, *shape) for shape, kind in kept),
        in_specs=[SMEM, ANY, VMEM, VMEM, ANY, VMEM],
        out_specs=(VMEM,) * SD + (ANY,) * len(kept),
        scratch_shapes=[
            pltpu.VMEM((3 * D, D), BF),
            pltpu.VMEM((D, D), BF),
            pltpu.VMEM((FF, D), BF),
            pltpu.VMEM((FF, D), BF),
            pltpu.VMEM(*rows),
        ]
        + [pltpu.VMEM(*a) for a in kept]
        + [
            pltpu.VMEM(*rows),
            pltpu.VMEM((8, ROWS), F32),
            pltpu.VMEM((TM, D), F32),
            dma((4,)),
            dma,
            dma((12,)),
        ],
        compiler_params=pltpu.CompilerParams(vmem_limit_bytes=VMEM_LIMIT),
        cost_estimate=pl.CostEstimate(flops=2 * ROWS * WROWS * D, bytes_accessed=64 << 20, transcendentals=0),
        name="forward",
    )(positions, slots, vecs, b_u, x_c, meta)


def backward_kernel(
    cap,
    pos,
    slots,
    vecs,
    meta,
    cot_0,
    cot_1,
    cot_2,
    cot_3,
    q_h,
    k_h,
    v_h,
    p_h,
    slope_h,
    n1_h,
    n2_h,
    rs1_h,
    rs2_h,
    back_0,
    back_1,
    back_2,
    back_3,
    shares,
    d_up_h,
    d_q_h,
    d_k_h,
    d_v_h,
    d_proj_h,
    d_br_h,
    wqkv,
    wo,
    wu,
    wd,
    blocks,
    q,
    k,
    v,
    p_all,
    d_up,
    n1,
    n2,
    rs1,
    rs2,
    d_proj,
    d_br,
    ing_c,
    d_h_t,
    gvec,
    g_bu,
    w_sem,
    c_sem,
    i_sem,
    o_sem,
):
    inv = 1.0 / math.sqrt(HD)
    get_c = [
        pltpu.make_async_copy(cot, blocks.at[j], c_sem.at[j]) for j, cot in enumerate((cot_0, cot_1, cot_2, cot_3))
    ]
    for copy in get_c:
        copy.start()
    fetch = [
        pltpu.make_async_copy(src, dst, i_sem.at[i])
        for i, (src, dst) in enumerate(
            (
                (n2_h, n2),
                (rs2_h, rs2),
                (slope_h, d_up),
                (n1_h, n1),
                (rs1_h, rs1),
                (v_h, v),
                (p_h, p_all),
                (k_h, k),
                (q_h, q),
            )
        )
    ]
    weights = [
        weight_copies(pos, slots, w, w_sem.at[i], first)
        for i, (w, first) in enumerate(((wd, 64), (wu, 32), (wo, 24), (wqkv, 0)))
    ]
    fetch[0].start()
    fetch[1].start()
    weights[0][0]()
    fetch[2].start()
    weights[1][0]()
    fetch[3].start()
    fetch[4].start()
    weights[2][0]()
    for i in range(5, 9):
        fetch[i].start()
    weights[3][0]()
    gvec[...] = jnp.zeros_like(gvec)
    g_bu[...] = jnp.zeros_like(g_bu)
    shares[...] = jnp.zeros_like(shares)
    for copy in get_c:
        copy.wait()
    seat_rows(meta, blocks, cap, d_br)
    apart = halves_of_heads()

    def vec(i):
        return vecs[i : i + 1, :]

    def add_vec(i, value):
        gvec[i : i + 1, :] += jnp.sum(value, axis=0, keepdims=True)

    saved = ((d_up, d_up_h), (q, d_q_h), (k, d_k_h), (v, d_v_h), (d_proj, d_proj_h), (d_br, d_br_h))

    def save(t, i):
        src, dst = saved[i]
        return pltpu.make_async_copy(src.at[tile_rows(t)], dst.at[tile_rows(t)], o_sem.at[i])

    def norm_back(e, n, rs, gain, shift):
        add_vec(gain, e * n)
        add_vec(shift, e)
        eg = e * vec(gain)
        return rs * (eg - lane_sum(eg) * (1.0 / D) - n * (lane_sum(eg * n) * (1.0 / D)))

    def norm_two_back(t):
        rows = tile_rows(t)
        d_r2 = norm_back(d_br[rows, :].astype(F32), n2[rows, :], rs2[rows, 0:1], V_G2, V_C2)
        d_br[rows, :] = d_r2.astype(BF)
        add_vec(V_BD, d_br[rows, :].astype(F32))
        n2[rows, :] = d_r2

    def widen_back(t, columns):
        rows = tile_rows(t)
        parts = [pl.ds(pl.multiple_of(f * FC, FC), FC) for f in columns]
        ups = [mm(d_br[rows, :], wd[fs, :], NT) for fs in parts]

        def finish():
            for fs, up in zip(parts, ups):
                du = (up * d_up[rows, fs].astype(F32)).astype(BF)
                d_up[rows, fs] = du
                g_bu[:, fs] += jnp.sum(du.astype(F32), axis=0, keepdims=True)

        return finish

    def hidden_back(t):
        rows = tile_rows(t)
        return n2[rows, :] + mm(d_up[rows, :], wu[...])

    def norm_one_back(t, d_h):
        rows = tile_rows(t)
        d_r1 = norm_back(d_h, n1[rows, :], rs1[rows, 0:1], V_G1, V_C1)
        d_proj[rows, :] = d_r1.astype(BF)
        n2[rows, :] = d_r1
        add_vec(V_BO, d_proj[rows, :].astype(F32))

    def heads_back(t):
        rows = tile_rows(t)
        d_h_t[rows, :] = mm(d_proj[rows, :], wo[...], NT).astype(BF)

    def attend_back(clusters, meanwhile=lambda: None):
        pairs = [
            (c, p, pl.ds(pl.multiple_of(c * CL, CL), CL), slice(p * PW, (p + 1) * PW))
            for c in clusters
            for p in range(PAIRS)
        ]
        probs = [p_all[c, p] for c, p, _, _ in pairs]
        d_heads = [d_h_t[gr, ps] for _, _, gr, ps in pairs]
        d_probs = [mm(apart(v[gr, ps]), dh, NT) for (_, _, gr, ps), dh in zip(pairs, d_heads)]
        d_values = [
            mm(jnp.concatenate([w[0:CL], w[CL:]], axis=1), apart(dh)).astype(BF) for w, dh in zip(probs, d_heads)
        ]
        finish = meanwhile()
        d_scores = []
        for w, dw in zip(probs, d_probs):
            halves = []
            for h in range(2):
                wh = w[h * CL : (h + 1) * CL].astype(F32)
                dwh = dw[h * CL : (h + 1) * CL]
                halves.append((wh * (dwh - jnp.sum(dwh * wh, axis=0, keepdims=True))).astype(BF))
            d_scores.append(halves)
        d_keys = [
            mm(jnp.concatenate(ds, axis=1), apart(q[gr, ps])).astype(BF) for (_, _, gr, ps), ds in zip(pairs, d_scores)
        ]
        d_queries = [
            (mm(jnp.concatenate(ds, axis=0), apart(k[gr, ps]), TN) * inv).astype(BF)
            for (_, _, gr, ps), ds in zip(pairs, d_scores)
        ]
        if finish is not None:
            finish()
        for (_, _, gr, ps), dq, dk, dv in zip(pairs, d_queries, d_keys, d_values):
            q[gr, ps] = dq
            k[gr, ps] = dk
            v[gr, ps] = dv

    def rows_back(t):
        rows = tile_rows(t)
        return (
            mm(q[rows, :], wqkv[0:D, :], NT)
            + mm(k[rows, :], wqkv[D : 2 * D, :], NT)
            + mm(v[rows, :], wqkv[2 * D :, :], NT)
        )

    def rows_done(t, d_x):
        rows = tile_rows(t)
        add_vec(V_BQ, q[rows, :].astype(F32))
        add_vec(V_BV, v[rows, :].astype(F32))
        ing_c[rows, :] = (n2[rows, :] + d_x.astype(BF).astype(F32)).astype(BF)

    def save_all(t, which):
        for i in which:
            save(t, i).start()

    per = TM // CL
    fetch[0].wait()
    fetch[1].wait()
    norm_two_back(0)
    norm_two_back(1)
    weights[0][1]()
    fetch[2].wait()
    loop(FF // FC // 2, lambda f: widen_back(0, [2 * f, 2 * f + 1])())
    save_all(0, (0, 5))
    weights[1][1]()
    fetch[3].wait()
    fetch[4].wait()
    norm_one_back(0, hidden_back(0))
    weights[2][1]()
    for i in range(5, 9):
        fetch[i].wait()
    heads_back(0)
    save_all(0, (4,))
    loop(FF // FC // 2, lambda f: widen_back(1, [2 * f, 2 * f + 1])())
    attend_back(range(per))
    save_all(0, (1, 2, 3))
    save_all(1, (0, 5))
    weights[3][1]()
    d_h = hidden_back(1)
    d_x = rows_back(0)
    norm_one_back(1, d_h)
    heads_back(1)
    rows_done(0, d_x)
    save_all(1, (4,))
    attend_back(range(per, 2 * per))
    save_all(1, (1, 2, 3))
    rows_done(1, rows_back(1))

    for j, back in enumerate((back_0, back_1, back_2, back_3)):
        back[...] = mm(seat_part(meta, j, cap), ing_c[...], TN).astype(BF)

    for chunk in range(72):
        row, lane = chunk // 6, chunk % 6 * 128
        if row < 8:
            part = gvec[row : row + 1, lane : lane + 128]
        else:
            lane += (row - 8) * D
            part = g_bu[:, lane : lane + 128]
        shares[chunk // 9, chunk % 9 : chunk % 9 + 1, :] = part

    def saved_all(t):
        for i in range(len(saved)):
            save(t, i).wait()

    loop(ROWS // TM, saved_all)


def backward(cap, positions, slots, vecs, meta, cots, saved):
    rows, wide, probs, full, thin = saved_shapes()
    dma = pltpu.SemaphoreType.DMA
    grads = (wide, rows, rows, rows, rows, rows)
    return pl.pallas_call(
        functools.partial(backward_kernel, cap),
        out_shape=(shape_of(BF, cap, D),) * SD
        + (shape_of(F32, 8, 16, 128),)
        + tuple(shape_of(kind, *shape) for shape, kind in grads),
        in_specs=[SMEM, ANY, VMEM, VMEM] + [ANY] * (SD + 9),
        out_specs=(VMEM,) * (SD + 1) + (ANY,) * len(grads),
        scratch_shapes=[
            pltpu.VMEM((3 * D, D), BF),
            pltpu.VMEM((D, D), BF),
            pltpu.VMEM((FF, D), BF),
            pltpu.VMEM((FF, D), BF),
            pltpu.VMEM((SD, cap, D), BF),
        ]
        + [pltpu.VMEM(*a) for a in (rows, rows, rows, probs, wide, full, full, thin, thin, rows, rows, rows)]
        + [
            pltpu.VMEM(*rows),
            pltpu.VMEM((8, D), F32),
            pltpu.VMEM((1, FF), F32),
            dma((4,)),
            dma((4,)),
            dma((9,)),
            dma((6,)),
        ],
        compiler_params=pltpu.CompilerParams(vmem_limit_bytes=VMEM_LIMIT),
        cost_estimate=pl.CostEstimate(flops=2 * ROWS * WROWS * D, bytes_accessed=64 << 20, transcendentals=0),
        name="backward",
    )(positions, slots, vecs, meta, *cots, *saved)


WC = 8 * BLK


def weight_kernel(
    pos,
    x_h,
    heads_h,
    act_h,
    d_up_h,
    d_q_h,
    d_k_h,
    d_v_h,
    d_proj_h,
    hid_h,
    d_br_h,
    grads,
    x_c,
    heads,
    act,
    d_up,
    d_q,
    d_k,
    d_v,
    d_proj,
    hid,
    d_br,
    stage,
    i_sem,
    g_sem,
):
    refs = (
        (x_h, x_c),
        (d_q_h, d_q),
        (d_k_h, d_k),
        (d_v_h, d_v),
        (heads_h, heads),
        (d_proj_h, d_proj),
        (hid_h, hid),
        (d_up_h, d_up),
        (d_br_h, d_br),
        (act_h, act),
    )
    fetch = [pltpu.make_async_copy(src, dst, i_sem.at[i]) for i, (src, dst) in enumerate(refs)]
    for copy in fetch:
        copy.start()

    per = WC // BLK

    def g_copy(chunk, j, at):
        return pltpu.make_async_copy(
            stage.at[at, pl.ds(j * BLK, BLK)], grads.at[pos[chunk * per + j]], g_sem.at[at]
        )

    def put(chunk, left, right):
        at = lax.rem(chunk, 2)

        @pl.when(chunk >= 2)
        def _():
            for j in range(per):
                g_copy(chunk - 2, j, at).wait()

        stage[at] = mm(left, right, TN).astype(BF)
        for j in range(per):
            g_copy(chunk, j, at).start()

    first = 0
    for left, right, needs in (
        (x_c, d_q, (0, 1)),
        (x_c, d_k, (2,)),
        (x_c, d_v, (3,)),
        (heads, d_proj, (4, 5)),
        (d_up, hid, (6, 7)),
        (act, d_br, (8, 9)),
    ):
        for i in needs:
            fetch[i].wait()

        def body(j, left=left, right=right, first=first):
            put(first + j, left[:, pl.ds(pl.multiple_of(j * WC, WC), WC)], right[...])

        loop(left.shape[1] // WC, body)
        first += left.shape[1] // WC
    for chunk in (first - 2, first - 1):
        for j in range(per):
            g_copy(chunk, j, chunk % 2).wait()


def weight_grads_of(total_slots, positions, x_c, saved):
    r_v, w_v = pltpu.VMEM((ROWS, D), BF), pltpu.VMEM((ROWS, FF), BF)
    return pl.pallas_call(
        weight_kernel,
        out_shape=jax.ShapeDtypeStruct((total_slots, BLK, D), BF),
        in_specs=[SMEM] + [ANY] * 10,
        out_specs=ANY,
        scratch_shapes=[r_v, r_v, w_v, w_v]
        + [r_v] * 6
        + [
            pltpu.VMEM((2, WC, D), BF),
            pltpu.SemaphoreType.DMA((10,)),
            pltpu.SemaphoreType.DMA((2,)),
        ],
        compiler_params=pltpu.CompilerParams(vmem_limit_bytes=VMEM_LIMIT),
        cost_estimate=pl.CostEstimate(flops=2 * ROWS * WROWS * D, bytes_accessed=40 << 20, transcendentals=0),
        name="weight_grads",
    )(positions, x_c, *saved)


def adam_step(grad_now, weight_old, first_old, second_old, rate_step):
    first_new = beta_first * first_old + (1.0 - beta_first) * grad_now
    second_new = beta_second * second_old + (1.0 - beta_second) * grad_now * grad_now
    square = second_new * (1.0 / (1.0 - beta_second**STEP))
    root = jnp.where(square > 0.0, square * lax.rsqrt(square), 0.0)
    step = first_new * (1.0 / (1.0 - beta_first**STEP)) * inverse(root + adam_epsilon)
    return (first_new, second_new, weight_old - rate_step * (step + weight_decay * weight_old))


def finish_kernel(
    used,
    total_h,
    master_h,
    first_h,
    second_h,
    v_grad,
    v_master,
    v_first,
    v_second,
    line,
    counts,
    out_h,
    ing_h,
    grad_new,
    first_new,
    second_new,
    master_new,
    low_new,
    v_grad_new,
    v_first_new,
    v_second_new,
    v_master_new,
    v_low_new,
    entropy,
    occupancy,
    output,
    input_grad,
    total,
    master,
    first,
    second,
    grad,
    out_v,
    ing_v,
    in_s,
    out_s,
    row_s,
):
    count = total.shape[0]
    ins = ((total_h, total), (master_h, master), (first_h, first), (second_h, second))
    outs = ((total, low_new), (master, master_new), (first, first_new), (second, second_new), (grad, grad_new))

    groups = [(first, min(max(first, 1), 4, count - first)) for first in (0, 1, 2, 4, 8, 12) if first < count]

    def fetch(i, n):
        src, dst = ins[i]
        part = pl.ds(*groups[n])
        return pltpu.make_async_copy(src.at[part], dst.at[part], in_s.at[i, n])

    def put(i, n):
        src, dst = outs[i]
        part = pl.ds(*groups[n])
        return pltpu.make_async_copy(src.at[part], dst.at[part], out_s.at[i, n])

    rows_in = [pltpu.make_async_copy(a, b, row_s.at[0, n]) for n, (a, b) in enumerate(((out_h, out_v), (ing_h, ing_v)))]
    rows_out = [pltpu.make_async_copy(a, b, row_s.at[1, n]) for n, (a, b) in enumerate(((out_v, output), (ing_v, input_grad)))]
    for n in range(len(groups)):
        for i in range(4):
            fetch(i, n).start()
    for copy in rows_in:
        copy.start()
    entropy[...] = line[...].reshape(ROWS)
    occupancy[...] = counts[...]
    length = v_master.shape[0]
    for n in range(-(-length // 128)):
        part = slice(n * 128, min((n + 1) * 128, length))
        g = v_grad[n : n + 1, 0 : part.stop - part.start].reshape(part.stop - part.start)
        m, v, w = adam_update(g, v_master[part], v_first[part], v_second[part], rate_vector)
        v_grad_new[part] = g
        v_first_new[part] = m
        v_second_new[part] = v
        v_master_new[part] = w
    v_low_new[...] = v_master_new[...].astype(BF)

    def slot(s):
        g = jnp.where(used[s] > 0, total[s].astype(F32), 0.0)
        m, v, w = adam_step(g, master[s], first[s], second[s], rate_matrix)
        grad[s] = g
        first[s] = m
        second[s] = v
        master[s] = w
        total[s] = w.astype(BF)

    for n, (start, size) in enumerate(groups):
        for i in range(4):
            fetch(i, n).wait()
        loop(size, lambda j, start=start: slot(start + j))
        for i in range(5):
            put(i, n).start()
    for copy_in, copy_out in zip(rows_in, rows_out):
        copy_in.wait()
        copy_out.start()
    for n in range(len(groups)):
        for i in range(5):
            put(i, n).wait()
    for copy in rows_out:
        copy.wait()


def finish(used, total, weights, v_grad, vectors, line, counts, out, ing):
    count = total.shape[0]
    low, full = pltpu.VMEM((count, BLK, D), BF), pltpu.VMEM((count, BLK, D), F32)
    f32_slots, f32_vector = shape_of(F32, count, BLK, D), shape_of(F32, *vectors[0].shape)
    dma = pltpu.SemaphoreType.DMA
    return pl.pallas_call(
        finish_kernel,
        out_shape=(f32_slots,) * 4
        + (shape_of(BF, count, BLK, D),)
        + (f32_vector,) * 4
        + (shape_of(BF, *vectors[0].shape), shape_of(BF, ROWS), shape_of(I32, *counts.shape))
        + (shape_of(BF, ROWS, D),) * 2,
        in_specs=[SMEM] + [ANY] * 4 + [VMEM] * 6 + [ANY] * 2,
        out_specs=(ANY,) * 5 + (VMEM,) * 7 + (ANY,) * 2,
        scratch_shapes=[low, full, full, full, full]
        + [pltpu.VMEM((ROWS, D), BF)] * 2
        + [dma((4, 6)), dma((5, 6)), dma((2, 2))],
        compiler_params=pltpu.CompilerParams(vmem_limit_bytes=VMEM_LIMIT),
        name="finish",
    )(used, total, *weights, v_grad, *vectors, line, counts, out, ing)


def local(
    tokens,
    cotangent,
    cluster_order,
    block_owner,
    master_slots,
    moment_one,
    moment_two,
    vector_master,
    vector_moment_one,
    vector_moment_two,
):
    tok_count = lax.axis_size("tok")
    tok_index = lax.axis_index("tok")
    slot_count = master_slots.shape[0]
    cap = tok_count // SD * (max(1, CPS // tok_count) * 3 * CL // (2 * SD))
    total_slots = tok_count * slot_count
    order = cluster_order.reshape(1, ROWS)

    block = jax.ShapeDtypeStruct((SD, cap, D), BF)
    meta_shape = jax.ShapeDtypeStruct((SD, META, D), BF)
    row_block = jax.ShapeDtypeStruct((ROWS, D), BF)
    four_planes = tok_count == 8 and lax.axis_size("rep") == 4
    if four_planes:
        slots_low, x_c, *cots, recv_meta, vecs, b_u, occupancy, positions = gather_all(
            cap, tokens, cotangent, order, master_slots, vector_master, block_owner
        )
        positions = positions.reshape(NBLK)
        slots_low = slots_low.reshape(total_slots, BLK, D)
    else:
        positions = slot_positions(block_owner, slot_count)
        slots_low = lax.all_gather(master_slots.astype(BF), "tok", axis=0, tiled=True)
        vectors = lax.all_gather(vector_master.astype(BF), "tok", axis=0, tiled=True).astype(F32)
        vecs, b_u = vectors[: 8 * D].reshape(8, D), vectors[8 * D :].reshape(1, FF)
        cluster = tok_index // SD * CPS + cluster_order // CL
        target = cluster % tok_count
        chosen = target[None, :] == jnp.arange(tok_count, dtype=jnp.int32)[:, None]
        sent_counts = jnp.sum(chosen.astype(F32), axis=1)
        own_row = (jnp.arange(tok_count, dtype=jnp.int32) == tok_index).astype(F32)
        occupancy = lax.psum(own_row[:, None] * sent_counts[None, :], ("tok", "rep")).astype(jnp.int32)
        send_x, send_c, meta = pl.pallas_call(
            functools.partial(send_kernel, cap),
            out_shape=(block, block, meta_shape),
            in_specs=[VMEM] * 3,
            out_specs=(VMEM,) * 3,
            compiler_params=pltpu.CompilerParams(vmem_limit_bytes=VMEM_LIMIT),
            name="send_rows",
        )(tokens, cotangent, order)
        recv_x, recv_meta = (jnp.stack(swap_blocks(b)) for b in (send_x, meta))
        x_c = pl.pallas_call(
            functools.partial(seat_kernel, cap),
            out_shape=row_block,
            in_specs=[VMEM] * 2,
            out_specs=VMEM,
            compiler_params=pltpu.CompilerParams(vmem_limit_bytes=VMEM_LIMIT),
            name="seat_rows",
        )(recv_x, recv_meta)
        cots = [send_c[k] for k in range(SD)]

    cots = swap_blocks(cots)
    *out_blocks, heads, act, hid, q, k, v, p, slope, n1, n2, rs1, rs2 = forward(
        cap, positions, slots_low, vecs, b_u, x_c, recv_meta
    )
    out_blocks = swap_blocks(out_blocks)
    *ing_blocks, shares, d_up, d_q, d_k, d_v, d_proj, d_br = backward(
        cap, positions, slots_low, vecs, recv_meta, cots, (q, k, v, p, slope, n1, n2, rs1, rs2)
    )
    ing_blocks = swap_blocks(ing_blocks)
    grads = weight_grads_of(
        total_slots, positions, x_c, (heads, act, d_up, d_q, d_k, d_v, d_proj, hid, d_br)
    )
    if four_planes:
        total, vec_owned, output, input_grad, entropy = reduce_all(
            cap, grads, shares, order, out_blocks, ing_blocks, slot_count
        )
    else:
        total = lax.psum(lax.psum_scatter(grads, "tok", scatter_dimension=0, tiled=True), "rep")
        grad_vector = shares[:, 0:9].reshape(-1)
        vec_owned = lax.psum(lax.psum_scatter(grad_vector, "tok", scatter_dimension=0, tiled=True), "rep")
        vec_owned = jnp.pad(vec_owned, (0, -vec_owned.shape[0] % 128)).reshape(-1, 128)
        output, input_grad, entropy = pl.pallas_call(
            functools.partial(return_kernel, cap),
            out_shape=(row_block, row_block, jax.ShapeDtypeStruct((1, ROWS), BF)),
            in_specs=[VMEM] * (2 * SD + 1),
            out_specs=(VMEM,) * 3,
            compiler_params=pltpu.CompilerParams(vmem_limit_bytes=VMEM_LIMIT),
            name="return_rows",
        )(order, *out_blocks, *ing_blocks)

    used = jnp.any(
        positions[None, :] == (tok_index * slot_count + jnp.arange(slot_count, dtype=I32))[:, None], axis=1
    )
    (
        owned_grad,
        first_new,
        second_new,
        master_new,
        low_new,
        vec_owned,
        vec_first,
        vec_second,
        vec_new,
        vec_low_new,
        row_entropy,
        occupancy,
        output,
        input_grad,
    ) = finish(
        used.astype(I32),
        total,
        (master_slots, moment_one, moment_two),
        vec_owned,
        (vector_master, vector_moment_one, vector_moment_two),
        entropy,
        occupancy,
        output,
        input_grad,
    )
    return (
        output,
        input_grad,
        owned_grad,
        first_new,
        second_new,
        master_new,
        low_new,
        vec_owned,
        vec_first,
        vec_second,
        vec_new,
        vec_low_new,
        row_entropy,
        occupancy,
    )


def solution(mesh):
    placed = (
        P(("rep", "tok"), None),
        P(("rep", "tok"), None),
        P(("rep", "tok")),
        P(),
        P("tok", None, None),
        P("tok", None, None),
        P("tok", None, None),
        P("tok"),
        P("tok"),
        P("tok"),
    )
    return jax.shard_map(
        local,
        mesh=mesh,
        in_specs=placed,
        out_specs=(
            P(("rep", "tok"), None),
            P(("rep", "tok"), None),
            P("tok", None, None),
            P("tok", None, None),
            P("tok", None, None),
            P("tok", None, None),
            P("tok", None, None),
            P("tok"),
            P("tok"),
            P("tok"),
            P("tok"),
            P("tok"),
            P(("rep", "tok")),
            P(),
        ),
        check_vma=False,
    )
```

```python
import functools
import math

import jax
import jax.numpy as jnp
from jax import lax
from jax.experimental import pallas as pl
from jax.experimental.pallas import tpu as pltpu
from jax.sharding import PartitionSpec as P

D = 768
HEADS = 12
HD = 64
FF = 3072
SD = 4
CL = 128
NBLK = 96
STEP = 10
CPS = 32
WROWS = 9216
BLK = 96
ROWS = 1024
PAIRS = HEADS // 2
PW = 2 * HD
TM = 512
PART = 48
META = 16
VMEM_LIMIT = 63 << 20
FC = 768

norm_epsilon = 1e-06
beta_first = 0.9
beta_second = 0.999
adam_epsilon = 1e-08
weight_decay = 0.01
rate_matrix = 0.02
rate_vector = 0.2

BF = jnp.bfloat16
F32 = jnp.float32
I32 = jnp.int32

VMEM = pl.BlockSpec(memory_space=pltpu.VMEM)
SMEM = pl.BlockSpec(memory_space=pltpu.SMEM)
ANY = pl.BlockSpec(memory_space=pl.ANY)

NN = (((1,), (0,)), ((), ()))
NT = (((1,), (1,)), ((), ()))
TN = (((0,), (0,)), ((), ()))


def mm(a, b, dims=NN):
    return lax.dot_general(a, b, dims, preferred_element_type=F32)


def slot_positions(block_owner, slot_count):
    owners = block_owner[:, 0]
    blocks = owners.shape[0]
    shared = owners[:, None] == owners[None, :]
    before = (
        jnp.arange(blocks, dtype=jnp.int32)[None, :] < jnp.arange(blocks, dtype=jnp.int32)[:, None]
    )
    earlier = jnp.sum((shared & before).astype(jnp.int32), axis=1)
    return owners * slot_count + earlier


def adam_update(grad_now, weight_old, first_old, second_old, rate_step):
    first_new = beta_first * first_old + (1.0 - beta_first) * grad_now
    second_new = beta_second * second_old + (1.0 - beta_second) * grad_now * grad_now
    first_hat = first_new / (1.0 - beta_first**STEP)
    second_hat = second_new / (1.0 - beta_second**STEP)
    weight_new = weight_old - rate_step * (
        first_hat / (jnp.sqrt(second_hat) + adam_epsilon) + weight_decay * weight_old
    )
    return (first_new, second_new, weight_new)


def route_slots(order, seat, cap):
    cluster = order // CL
    rel = lax.rem(cluster, SD) ^ seat
    place = (cluster // SD) * CL + lax.rem(order, CL) + 1
    chosen = lax.broadcasted_iota(I32, (8, ROWS), 0) == rel
    chosen_low = jnp.where(chosen, 1.0, 0.0).astype(BF)
    before = lax.broadcasted_iota(I32, (ROWS, ROWS), 0) < lax.broadcasted_iota(I32, (ROWS, ROWS), 1)
    before_low = jnp.where(before, 1.0, 0.0).astype(BF)
    running = mm(chosen_low, before_low)
    rank = jnp.sum(jnp.where(chosen, running, 0.0), axis=0, keepdims=True).astype(I32)
    return rel * cap + rank, place


def slot_matrix(slots, at, cap):
    rows = lax.broadcasted_iota(I32, (cap, ROWS), 0) + at * cap
    return jnp.where(rows == slots, 1.0, 0.0).astype(BF)


def send_kernel(cap, tokens, cotangent, order, send_x, send_c, meta):
    seat = lax.rem(lax.axis_index("tok"), SD)
    slots, place = route_slots(order[...], seat, cap)
    digits = jnp.concatenate([place // CL, lax.rem(place, CL)] + [place * 0] * 6, axis=0).astype(F32).astype(BF)
    for at in range(SD):
        picked = slot_matrix(slots, at, cap)
        send_x[at] = mm(picked, tokens[...]).astype(BF)
        send_c[at] = mm(picked, cotangent[...]).astype(BF)
        coded = mm(digits, picked, NT)
        line = jnp.concatenate([coded[0:1], coded[1:2]], axis=1)
        meta[at] = jnp.broadcast_to(line, (META, D)).astype(BF)


def remote(src, dst, send_sem, recv_sem, tok, rep):
    return pltpu.make_async_remote_copy(
        src_ref=src,
        dst_ref=dst,
        send_sem=send_sem,
        recv_sem=recv_sem,
        device_id={"tok": tok, "rep": rep},
        device_id_type=pl.DeviceIdType.MESH,
    )


def loop(n, body):
    def run(i, c):
        body(i)
        return c

    lax.fori_loop(0, n, run, 0)


class Place:
    def __init__(self):
        self.me = me = lax.axis_index("tok")
        self.z = z = lax.axis_index("rep")
        core, x, y = me % 2, (me // 2) % 2, me // 4
        self.twin = me + 1 - 2 * core
        self.xn = me + 2 - 4 * x
        self.yn = me + 4 - 8 * y
        self.dn = self.xn + 4 - 8 * y
        self.side = z % 2
        self.zp = z + 1 - 2 * self.side

    def twin_of(self, tok):
        return tok + 1 - 2 * (tok % 2)

    def greet(self, peers):
        barrier = pltpu.get_barrier_semaphore()
        for tok, rep in peers:
            pl.semaphore_signal(
                barrier, inc=1, device_id={"tok": tok, "rep": rep}, device_id_type=pl.DeviceIdType.MESH
            )
        return lambda: pl.semaphore_wait(barrier, len(peers))


def seat_matrix(meta, first, rows, cap):
    hi = jnp.concatenate([meta[k, 0:8, 0:cap] for k in range(SD)], axis=1).astype(F32)[0:1]
    lo = jnp.concatenate([meta[k, 0:8, cap : 2 * cap] for k in range(SD)], axis=1).astype(F32)[0:1]
    at = (hi * CL + lo).astype(I32)
    seats = lax.broadcasted_iota(I32, (rows, SD * cap), 0) + (first + 1)
    return jnp.where(seats == at, 1.0, 0.0).astype(BF)


def seat_part(meta, k, cap):
    hi = meta[k, 0:8, 0:cap].astype(F32)[0:1]
    lo = meta[k, 0:8, cap : 2 * cap].astype(F32)[0:1]
    at = (hi * CL + lo).astype(I32)
    seats = lax.broadcasted_iota(I32, (ROWS, cap), 0) + 1
    return jnp.where(seats == at, 1.0, 0.0).astype(BF)


def seat_rows(meta, blocks, cap, to):
    def body(t):
        r0 = pl.multiple_of(t * 256, 256)
        rows = blocks[...].reshape(SD * cap, D)
        to[pl.ds(r0, 256), :] = mm(seat_matrix(meta, r0, 256, cap), rows).astype(BF)

    loop(ROWS // 256, body)


def seat_kernel(cap, blocks, meta, to):
    seat_rows(meta, blocks, cap, to)


def gather_kernel(
    cap,
    count,
    tokens_h,
    cotangent_h,
    order,
    master_h,
    vector,
    owner_of,
    slots,
    x_c,
    cot_0,
    cot_1,
    cot_2,
    cot_3,
    recv_meta,
    vecs,
    b_u,
    occupancy,
    positions,
    tokens,
    cotangent,
    master,
    own,
    send_x,
    send_c,
    meta,
    recv_x,
    got_meta,
    slot_of,
    digits,
    mine,
    by_z,
    by_tok,
    x_s,
    x_r,
    y_s,
    y_r,
    d_s,
    d_r,
    zx_s,
    zx_r,
    zd_s,
    zd_r,
    zy_s,
    zy_r,
    p_s,
    p_r,
    row_s,
    row_r,
    z_s,
    z_r,
    t_s,
    t_r,
    local_s,
):
    at = Place()
    me, z, side = at.me, at.z, at.side
    n_tok, n_rep = 8, 4
    peers = [((me + d) % n_tok, z) for d in range(1, n_tok)] + [(me, (z + d) % n_rep) for d in range(1, n_rep)]
    fetch = [
        pltpu.make_async_copy(src, dst, local_s.at[i])
        for i, (src, dst) in enumerate(((master_h, master), (tokens_h, tokens), (cotangent_h, cotangent)))
    ]
    for copy in fetch:
        copy.start()
    wait_peers = at.greet(peers)
    fetch[0].wait()

    last = count - 1

    def near(j):
        return side * last + (1 - 2 * side) * j

    def far(j):
        return (1 - side) * last - (1 - 2 * side) * j

    few_x, few_d, few_y = 11 * count // 26, 12 * count // 26, 8 * count // 26
    most_x, most_d, most_y = count - few_x, count - few_d, count - few_y

    def piece(owner, s):
        return slots.at[owner * count + s]

    def to_x(s):
        return remote(own.at[s], piece(me, s), x_s.at[s], x_r.at[s], at.xn, z)

    def to_y(s):
        return remote(own.at[s], piece(me, s), y_s.at[s], y_r.at[s], at.yn, z)

    def on_y(s):
        return remote(piece(at.xn, s), piece(at.xn, s), d_s.at[s], d_r.at[s], at.yn, z)

    def x_on_z(s):
        return remote(piece(at.xn, s), piece(at.xn, s), zx_s.at[s], zx_r.at[s], me, at.zp)

    def d_on_z(s):
        return remote(piece(at.dn, s), piece(at.dn, s), zd_s.at[s], zd_r.at[s], me, at.zp)

    def y_on_z(s):
        return remote(piece(at.yn, s), piece(at.yn, s), zy_s.at[s], zy_r.at[s], me, at.zp)

    def x_in(s):
        return remote(own.at[s], piece(at.xn, s), x_s.at[s], x_r.at[s], at.xn, z)

    def y_in(s):
        return remote(own.at[s], piece(at.yn, s), y_s.at[s], y_r.at[s], at.yn, z)

    def d_in(s):
        return remote(own.at[s], piece(at.dn, s), d_s.at[s], d_r.at[s], at.yn, z)

    owners = (me, at.xn, at.yn, at.dn)

    def near_run(q, j0, j1):
        return (q, (1 - side) * j0 + side * (count - j1), j1 - j0)

    def far_run(q, j0, j1):
        return (q, side * j0 + (1 - side) * (count - j1), j1 - j0)

    runs = (
        (0, 0, count),
        near_run(2, 0, few_y),
        near_run(1, 0, most_x),
        near_run(3, 0, most_d),
        far_run(1, 0, few_x),
        near_run(2, few_y, most_y),
        far_run(2, 0, few_y),
        far_run(3, 0, few_d // 2),
        far_run(3, few_d // 2, few_d - 2),
        far_run(3, few_d - 2, few_d),
    )

    def to_twin(i):
        q, s, n = runs[i]
        src = own if q == 0 else slots.at[pl.ds(owners[q] * count + s, n)]
        dst = slots.at[pl.ds(owners[q] * count + s, n)]
        return remote(src, dst, p_s.at[i], p_r.at[i], at.twin, z)

    def cast(j):
        own[near(j)] = master[near(j)].astype(BF)

    loop(most_x, cast)
    wait_peers()
    loop(most_x, lambda j: to_x(near(j)).start())
    loop(few_y, lambda j: to_y(near(j)).start())
    loop(count - most_x, lambda j: cast(most_x + j))
    to_twin(0).start()
    keep = pltpu.make_async_copy(own, slots.at[pl.ds(me * count, count)], local_s.at[3])
    keep.start()

    seat = me % SD
    seats = (me, at.twin, at.xn, at.twin_of(at.xn))
    rows_of = ((meta, got_meta), (send_x, recv_x))

    def row_copy(i, k):
        src, dst = rows_of[i]
        return remote(src.at[k], dst.at[k], row_s.at[i, k], row_r.at[i, k], seats[k], z)

    put_c = [
        pltpu.make_async_copy(send_c.at[k], to, local_s.at[4 + k])
        for k, to in enumerate((cot_0, cot_1, cot_2, cot_3))
    ]

    def route():
        fetch[1].wait()
        fetch[2].wait()
        slots_here, place = route_slots(order[...], seat, cap)
        slot_of[...] = slots_here
        digits[...] = (
            jnp.concatenate([place // CL, lax.rem(place, CL)] + [place * 0] * 6, axis=0).astype(F32).astype(BF)
        )

    def sort_tokens(k):
        picked = slot_matrix(slot_of[...], k, cap)
        send_x[k] = mm(picked, tokens[...]).astype(BF)
        coded = mm(digits[...], picked, NT)
        line = jnp.concatenate([coded[0:1], coded[1:2]], axis=1)
        meta[k] = jnp.broadcast_to(line, (META, D)).astype(BF)
        for i in range(2):
            if k:
                row_copy(i, k).start()
            else:
                src, dst = rows_of[i]
                dst[0] = src[0]

    def sort_cotangent(k):
        send_c[k] = mm(slot_matrix(slot_of[...], k, cap), cotangent[...]).astype(BF)
        put_c[k].start()

    def z_copy(d):
        return remote(by_z.at[0], by_z.at[d], z_s.at[d], z_r.at[d], me, (z + d) % n_rep)

    def t_copy(d):
        return remote(mine, by_tok.at[d], t_s.at[d], t_r.at[d], (me + d) % n_tok, z)

    def count_rows():
        residue = lax.rem(me // SD * CPS + order[...] // CL, n_tok)
        hit = lax.broadcasted_iota(I32, (128, ROWS), 0) == residue
        by_z[0] = mm(jnp.ones((8, ROWS), BF), jnp.where(hit, 1.0, 0.0).astype(BF), NT)
        for d in range(1, n_rep):
            z_copy(d).start()
        for i in range(9):
            mine[i : i + 1] = vector[i * 128 : (i + 1) * 128].reshape(1, 128).astype(BF).astype(F32)
        block_row = lax.broadcasted_iota(I32, (NBLK, NBLK), 0)
        block_col = lax.broadcasted_iota(I32, (NBLK, NBLK), 1)
        by_col = owner_of[...].astype(F32)
        by_row = lane_sum(jnp.where(block_row == block_col, by_col, 0.0))
        earlier = jnp.where((by_row == by_col) & (block_row < block_col), 1.0, 0.0)
        seats_of = (by_col * (count * PART // BLK) + jnp.sum(earlier, axis=0, keepdims=True)).astype(I32)
        mine_all = lane_sum(jnp.where(owner_of[...] == me, 1.0, 0.0)).astype(I32)
        positions[...] = jnp.concatenate([seats_of, jnp.broadcast_to(mine_all, (1, 128 - NBLK))], axis=1)

    def share_vectors():
        for d in range(1, n_rep):
            z_copy(d).wait()
        mine[16:24] = by_z[0] + by_z[1] + by_z[2] + by_z[3]
        for d in range(1, n_tok):
            t_copy(d).start()

    def lay_out_vectors():
        by_tok[0] = mine[...]
        for d in range(1, n_tok):
            t_copy(d).wait()
        for owner in range(n_tok):
            share = by_tok[(me + n_tok - owner) % n_tok]
            occupancy[owner : owner + 1, :] = share[16:17, 0:n_tok].astype(I32)
            for i in range(9):
                chunk = owner * 9 + i
                row, lane = chunk // 6, chunk % 6 * 128
                if row < 8:
                    vecs[row : row + 1, lane : lane + 128] = share[i : i + 1]
                else:
                    lane += (row - 8) * D
                    b_u[:, lane : lane + 128] = share[i : i + 1]

    between = {
        1: lambda: (route(), sort_tokens(2)),
        3: lambda: sort_tokens(3),
        5: lambda: sort_tokens(1),
        7: lambda: (sort_tokens(0), count_rows()),
        9: lambda: sort_cotangent(1),
        11: lambda: sort_cotangent(2),
        13: lambda: sort_cotangent(3),
    }
    for j in range(most_x):
        x_in(near(j)).wait_recv()
        if j < most_d:
            on_y(near(j)).start()
        if j < few_x:
            x_on_z(near(j)).start()
        if j < few_y:
            y_in(near(j)).wait_recv()
            y_on_z(near(j)).start()
        if j == few_y:
            to_twin(1).start()
        if j in between:
            between[j]()
    to_twin(2).start()
    loop(most_y - few_y, lambda j: to_y(near(few_y + j)).start())
    share_vectors()
    sort_cotangent(0)

    def diagonal(j):
        d_in(near(j)).wait_recv()
        d_on_z(near(j)).start()

    loop(few_d, diagonal)
    loop(most_d - few_d, lambda j: d_in(near(few_d + j)).wait_recv())
    to_twin(3).start()
    loop(few_x, lambda j: x_on_z(far(j)).wait_recv())
    to_twin(4).start()
    lay_out_vectors()
    loop(most_x, lambda j: to_x(near(j)).wait_send())
    loop(few_x, lambda j: x_on_z(near(j)).wait_send())
    loop(few_y, lambda j: y_on_z(near(j)).wait_send())
    loop(most_y - few_y, lambda j: y_in(near(few_y + j)).wait_recv())
    to_twin(5).start()
    loop(few_y, lambda j: y_on_z(far(j)).wait_recv())
    to_twin(6).start()
    for i in (0, 1):
        for k in (2, 3, 1):
            row_copy(i, k).wait_recv()
    recv_meta[...] = got_meta[...]
    seat_rows(got_meta, recv_x, cap, x_c)
    loop(most_y, lambda j: to_y(near(j)).wait_send())
    loop(most_d, lambda j: on_y(near(j)).wait_send())
    done = 0
    for i, upto in ((7, few_d // 2), (8, few_d - 2), (9, few_d)):
        loop(upto - done, lambda j, done=done: d_on_z(far(done + j)).wait_recv())
        to_twin(i).start()
        done = upto

    for i in range(2):
        for k in (2, 3, 1):
            row_copy(i, k).wait_send()
    for copy in put_c:
        copy.wait()
    keep.wait()

    loop(few_d, lambda j: d_on_z(near(j)).wait_send())
    for i in range(len(runs)):
        to_twin(i).wait()


def gather_all(cap, tokens, cotangent, order, master, vector, block_owner):
    count = master.shape[0] * BLK // PART
    rows = jax.ShapeDtypeStruct((ROWS, D), BF)
    part = jax.ShapeDtypeStruct((cap, D), BF)
    dma = pltpu.SemaphoreType.DMA
    block = pltpu.VMEM((SD, cap, D), BF)
    meta = pltpu.VMEM((SD, META, D), BF)
    return pl.pallas_call(
        functools.partial(gather_kernel, cap, count),
        out_shape=(
            jax.ShapeDtypeStruct((8 * count, PART, D), BF),
            rows,
            part,
            part,
            part,
            part,
            jax.ShapeDtypeStruct((SD, META, D), BF),
            jax.ShapeDtypeStruct((8, D), F32),
            jax.ShapeDtypeStruct((1, FF), F32),
            jax.ShapeDtypeStruct((8, 8), I32),
            jax.ShapeDtypeStruct((1, 128), I32),
        ),
        in_specs=[ANY, ANY, VMEM, ANY, VMEM, VMEM],
        out_specs=(ANY, VMEM) + (ANY,) * SD + (VMEM,) * 5,
        scratch_shapes=[
            pltpu.VMEM((ROWS, D), BF),
            pltpu.VMEM((ROWS, D), BF),
            pltpu.VMEM((count, PART, D), F32),
            pltpu.VMEM((count, PART, D), BF),
            block,
            block,
            meta,
            block,
            meta,
            pltpu.VMEM((1, ROWS), I32),
            pltpu.VMEM((8, ROWS), BF),
            pltpu.VMEM((24, 128), F32),
            pltpu.VMEM((4, 8, 128), F32),
            pltpu.VMEM((8, 24, 128), F32),
        ]
        + [dma((count,))] * 12
        + [dma((10,))] * 2
        + [dma((2, SD))] * 2
        + [dma((4,))] * 2
        + [dma((8,))] * 2
        + [dma((8,))],
        compiler_params=pltpu.CompilerParams(collective_id=0, has_side_effects=True, vmem_limit_bytes=VMEM_LIMIT),
        cost_estimate=pl.CostEstimate(flops=8 * ROWS * ROWS * D, bytes_accessed=64 << 20, transcendentals=0),
        name="gather",
    )(tokens, cotangent, order, master.reshape(count, PART, D), vector, block_owner.reshape(1, NBLK))


def return_kernel(cap, order, *refs):
    outs, ings, (out, ing, entropy) = refs[:SD], refs[SD : 2 * SD], refs[2 * SD :]
    seat = lax.rem(lax.axis_index("tok"), SD)
    slots, _ = route_slots(order[...], seat, cap)
    picked = jnp.concatenate([slot_matrix(slots, at, cap) for at in range(SD)], axis=0)
    for to, blocks in ((out, outs), (ing, ings)):
        rows = jnp.concatenate([block[0:cap, :] for block in blocks], axis=0)
        to[...] = mm(picked, rows, TN).astype(BF)
    line = jnp.concatenate([block[cap : cap + 8, 0:cap] for block in outs], axis=1)
    entropy[...] = mm(line, picked)[0:1].astype(BF)


def swap_blocks(blocks):
    n = lax.axis_size("tok")
    parts = [blocks[0]]
    for k in range(1, SD):
        parts.append(lax.ppermute(blocks[k], "tok", [(i, i ^ k) for i in range(n)]))
    return parts


def reduce_kernel(
    cap,
    count,
    split,
    grads,
    vec,
    order,
    out_0,
    out_1,
    out_2,
    out_3,
    ing_0,
    ing_1,
    ing_2,
    ing_3,
    total,
    vec_out,
    output,
    input_grad,
    entropy,
    out_v,
    ing_v,
    slot_of,
    a,
    tw,
    rd,
    rx,
    ry,
    o,
    rz1,
    pz,
    rz2,
    fz,
    vt,
    va,
    vb,
    vc,
    a_l,
    keep_l,
    p_s,
    p_r,
    d_s,
    d_r,
    x_s,
    x_r,
    y_s,
    y_r,
    z1_s,
    z1_r,
    z2_s,
    z2_r,
    z3_s,
    z3_r,
    t_s,
    t_r,
    v_s,
    v_r,
    row_l,
):
    at = Place()
    me, z = at.me, at.z
    n_tok, n_rep = 8, 4
    peers = [((me + d) % n_tok, z) for d in range(1, n_tok)] + [(me, (z + d) % n_rep) for d in range(1, n_rep)]
    wait_peers = at.greet(peers)
    owners = (me, at.xn, at.yn, at.dn)

    def load(q):
        return pltpu.make_async_copy(grads.at[pl.ds(owners[q] * count, count)], a.at[q], a_l.at[q])

    for q in (3, 1, 2, 0):
        load(q).start()
    rows_in = [
        pltpu.make_async_copy(src, to.at[k], row_l.at[i, k])
        for i, (blocks, to) in enumerate((((out_0, out_1, out_2, out_3), out_v), ((ing_0, ing_1, ing_2, ing_3), ing_v)))
        for k, src in enumerate(blocks)
    ]
    for copy in rows_in:
        copy.start()
    wait_peers()

    def to_twin(q, g):
        src = grads.at[pl.ds(at.twin_of(owners[q]) * count + 2 * g, 2)]
        return remote(src, tw.at[q, pl.ds(2 * g, 2)], p_s.at[q, g], p_r.at[q, g], at.twin, z)

    def d_y(s):
        return remote(a.at[3, s], rd.at[s], d_s.at[s], d_r.at[s], at.yn, z)

    def d_x(s):
        return remote(a.at[3, s], rd.at[s], d_s.at[s], d_r.at[s], at.xn, z)

    def to_x(s):
        return remote(a.at[1, s], rx.at[s], x_s.at[s], x_r.at[s], at.xn, z)

    def to_y(s):
        return remote(a.at[2, s], ry.at[s], y_s.at[s], y_r.at[s], at.yn, z)

    def z_in(s):
        return remote(o.at[s], rz1.at[s], z1_s.at[s], z1_r.at[s], me, at.zp)

    def z_swap(s):
        return remote(pz.at[s], rz2.at[s], z2_s.at[s], z2_r.at[s], me, n_rep - 1 - z)

    def z_out(s):
        return remote(fz.at[s], fz.at[s], z3_s.at[s], z3_r.at[s], me, at.zp)

    def keep(s):
        return pltpu.make_async_copy(fz.at[s], total.at[s], keep_l.at[s])

    def twin_start(g):
        for q in (3, 1, 2, 0):
            to_twin(q, g).start()

    loop(count // 2, twin_start)

    def v_tok(d):
        return remote(vec.at[(me + d) % n_tok], vt.at[d], t_s.at[d], t_r.at[d], (me + d) % n_tok, z)

    def v_rep(i, src):
        return remote(src, vb.at[i], v_s.at[i], v_r.at[i], me, at.zp if i == 0 else (z + 2) % n_rep)

    for d in range(1, n_tok):
        v_tok(d).start()

    def join(q, s):
        return a[q, s] + tw[q, s]

    def first(s, send):
        a[3, s] = join(3, s)
        send(s).start()

    def plain(q, s, send):
        a[q, s] = join(q, s)
        send(s).start()

    def joined(q, s, arrived, send):
        arrived(s).wait_recv()
        a[q, s] = join(q, s) + rd[s]
        send(s).start()

    inner = (z == 1) | (z == 2)
    outer = (z == 0) | (z == 3)

    def own(s):
        to_x(s).wait_recv()
        to_y(s).wait_recv()
        o[s] = join(0, s) + (rx[s] + ry[s])
        pl.when(outer)(lambda: z_in(s).start())

    def middle(s):
        @pl.when(inner)
        def _():
            z_in(s).wait_recv()
            pz[s] = o[s] + rz1[s]
            z_swap(s).start()

    def last(s):
        @pl.when(inner)
        def _():
            z_swap(s).wait_recv()
            fz[s] = pz[s] + rz2[s]
            z_out(s).start()
            keep(s).start()

    def taken(s):
        @pl.when(outer)
        def _():
            z_out(s).wait_recv()
            keep(s).start()

    def twin_sent(g):
        for q in range(4):
            to_twin(q, g).wait_send()

    def sent(s):
        d_y(s).wait_send()
        to_x(s).wait_send()
        to_y(s).wait_send()
        keep(s).wait()

        @pl.when(outer)
        def _():
            z_in(s).wait_send()

        @pl.when(inner)
        def _():
            z_swap(s).wait_send()
            z_out(s).wait_send()

    def pick_rows(i):
        ts = pl.ds(pl.multiple_of(i * 256, 256), 256)
        hit = lax.broadcasted_iota(I32, (SD * cap, 256), 0) == slot_of[:, ts]
        picked = jnp.where(hit, 1.0, 0.0).astype(BF)
        outs = jnp.concatenate([out_v[k, 0:cap, :] for k in range(SD)], axis=0)
        ings = jnp.concatenate([ing_v[k] for k in range(SD)], axis=0)
        both = mm(picked, jnp.concatenate([outs, ings], axis=1), TN)
        output[ts, :] = both[:, 0:D].astype(BF)
        input_grad[ts, :] = both[:, D:].astype(BF)
        line = jnp.concatenate([out_v[k, cap : cap + 8, 0:cap] for k in range(SD)], axis=1)
        entropy[:, ts] = mm(line, picked)[0:1].astype(BF)

    for q in (3, 1, 2, 0):
        load(q).wait()

    def steps(i, lag, more):
        s = i - lag
        by_x = (s % 2 == 0) & (s < 2 * split)
        live = (s >= 0) & (s < count)
        pl.when(live & by_x)(lambda: more(s, True))
        pl.when(live & jnp.logical_not(by_x))(lambda: more(s, False))

    def steps_of(i, lag, more):
        pl.when((i >= lag) & (i < count + lag))(lambda: more(i - lag))

    def round_of(i):
        for lag, which in ((0, (3,)), (1, (1, 2)), (6, (0,))):

            @pl.when((i >= lag) & ((i - lag) % 2 == 0) & (i < count + lag))
            def _(lag=lag, which=which):
                for q in which:
                    to_twin(q, (i - lag) // 2).wait_recv()

        steps(i, 0, lambda s, by_x: first(s, d_x if by_x else d_y))
        steps(i, 1, lambda s, by_x: plain(1, s, to_x) if by_x else plain(2, s, to_y))
        steps(i, 3, lambda s, by_x: joined(2, s, d_x, to_y) if by_x else joined(1, s, d_y, to_x))
        steps_of(i, 6, own)
        steps_of(i, 8, middle)
        steps_of(i, 10, last)
        steps_of(i, 12, taken)
        steps_of(i, 14, sent)
        pl.when((i >= 8) & (i % 2 == 0) & (i < count + 8))(lambda: twin_sent((i - 8) // 2))

    loop(3, round_of)
    for copy in rows_in:
        copy.wait()
    slots_here, _ = route_slots(order[...], me % SD, cap)
    slot_of[...] = slots_here

    v_sum = vec[me]
    for d in range(1, n_tok):
        v_tok(d).wait()
        v_sum = v_sum + vt[d]
    va[...] = v_sum
    v_rep(0, va).start()

    def four_rounds(i):
        loop(4, lambda j: round_of(3 + 4 * i + j))
        pick_rows(i)

    four_rounds(0)
    v_rep(0, va).wait()
    vc[...] = va[...] + vb[0]
    v_rep(1, vc).start()
    loop(3, lambda i: four_rounds(1 + i))
    loop(count + 12 - 19, lambda i: round_of(19 + i))
    v_rep(1, vc).wait()
    vec_out[...] = vc[...] + vb[1]

    loop(2, lambda j: sent(count - 2 + j))


def reduce_all(cap, grads, shares, order, outs, ings, count):
    dma = pltpu.SemaphoreType.DMA
    count = count * BLK // PART
    part = pltpu.VMEM((count, PART, D), BF)
    whole = pltpu.VMEM((4, count, PART, D), BF)
    line = pltpu.VMEM((16, 128), F32)
    rows = jax.ShapeDtypeStruct((ROWS, D), BF)
    total, vec, output, input_grad, entropy = pl.pallas_call(
        functools.partial(reduce_kernel, cap, count, count // 2),
        out_shape=(
            jax.ShapeDtypeStruct((count, PART, D), BF),
            jax.ShapeDtypeStruct((16, 128), F32),
            rows,
            rows,
            jax.ShapeDtypeStruct((1, ROWS), BF),
        ),
        in_specs=[ANY, VMEM, VMEM] + [ANY] * (2 * SD),
        out_specs=(ANY,) + (VMEM,) * 4,
        scratch_shapes=[
            pltpu.VMEM((SD, cap + META, D), BF),
            pltpu.VMEM((SD, cap, D), BF),
            pltpu.VMEM((1, ROWS), I32),
            whole,
            whole,
        ]
        + [part] * 8
        + [pltpu.VMEM((8, 16, 128), F32), line, pltpu.VMEM((2, 16, 128), F32), line]
        + [dma((4,)), dma((count,))]
        + [dma((4, count // 2))] * 2
        + [dma((count,))] * 12
        + [dma((8,))] * 2
        + [dma((2,))] * 2
        + [dma((2, SD))],
        compiler_params=pltpu.CompilerParams(collective_id=1, has_side_effects=True, vmem_limit_bytes=VMEM_LIMIT),
        cost_estimate=pl.CostEstimate(flops=4 * ROWS * ROWS * D, bytes_accessed=64 << 20, transcendentals=0),
        name="reduce",
    )(grads.reshape(-1, PART, D), shares, order, *outs, *ings)
    return total.reshape(-1, BLK, D), vec, output, input_grad, entropy


V_BQ, V_BV, V_BO, V_BD, V_G1, V_C1, V_G2, V_C2 = range(8)


def inverse(x):
    r = pl.reciprocal(x, approx=True)
    return r * (2.0 - x * r)


def erf_parts(v):
    t = inverse(1.0 + (0.3275911 / math.sqrt(2.0)) * jnp.abs(v))
    e = jnp.exp2((v * v) * (-0.5 / math.log(2.0)))
    poly = 0.5 * 1.061405429
    for c in (-1.453152027, 1.421413741, -0.284496736, 0.254829592):
        poly = poly * t + 0.5 * c
    tail = poly * (t * e)
    return jnp.where(v >= 0.0, 1.0 - tail, tail), e


def lane_sum(x):
    return jnp.sum(x, axis=1, keepdims=True)


def gelu_parts(v):
    phi, e = erf_parts(v)
    return v * phi, phi + v * (e * (1.0 / math.sqrt(2.0 * math.pi)))


def weight_copies(pos, slots, w, sem, first):
    def copy(b):
        return pltpu.make_async_copy(slots.at[pos[first + b]], w.at[pl.ds(b * BLK, BLK)], sem)

    n = w.shape[0] // BLK
    return (lambda: loop(n, lambda b: copy(b).start())), (lambda: loop(n, lambda b: copy(b).wait()))


def halves_of_heads():
    lane = lax.broadcasted_iota(I32, (1, PW), 1)
    m0 = jnp.where(lane < HD, 1.0, 0.0).astype(BF)
    m1 = jnp.where(lane < HD, 0.0, 1.0).astype(BF)
    return lambda pair: jnp.concatenate([pair * m0, pair * m1], axis=0)


def tile_rows(t):
    return pl.ds(pl.multiple_of(t * TM, TM), TM)


def forward_kernel(
    cap,
    pos,
    slots,
    vecs,
    b_u,
    x_h,
    meta,
    back_0,
    back_1,
    back_2,
    back_3,
    heads_h,
    act_h,
    hid_h,
    q_h,
    k_h,
    v_h,
    p_h,
    slope_h,
    n1_h,
    n2_h,
    rs1_h,
    rs2_h,
    wqkv,
    wo,
    wu,
    wd,
    x_c,
    heads,
    act,
    hid,
    q,
    k,
    v,
    p_all,
    slope,
    n1,
    n2,
    rs1,
    rs2,
    out_c,
    ent,
    w_sem,
    x_sem,
    o_sem,
):
    inv = 1.0 / math.sqrt(HD)
    get_x = pltpu.make_async_copy(x_h, x_c, x_sem)
    get_x.start()
    weights = [
        weight_copies(pos, slots, w, w_sem.at[i], first)
        for i, (w, first) in enumerate(((wqkv, 0), (wo, 24), (wu, 32), (wd, 64)))
    ]
    for start, _ in weights:
        start()
    get_x.wait()
    apart = halves_of_heads()

    def vec(i):
        return vecs[i : i + 1, :]

    saved = (
        (heads, heads_h),
        (act, act_h),
        (hid, hid_h),
        (q, q_h),
        (k, k_h),
        (v, v_h),
        (slope, slope_h),
        (n1, n1_h),
        (n2, n2_h),
        (rs1, rs1_h),
        (rs2, rs2_h),
    )

    def save(t, i):
        src, dst = saved[i]
        return pltpu.make_async_copy(src.at[tile_rows(t)], dst.at[tile_rows(t)], o_sem.at[i])

    def save_p(t):
        n = TM // CL
        cs = pl.ds(t * n, n)
        return pltpu.make_async_copy(p_all.at[cs], p_h.at[cs], o_sem.at[len(saved)])

    def normal(r, n, rs, rows):
        c = r - lane_sum(r) * (1.0 / D)
        scale = lax.rsqrt(lane_sum(c * c) * (1.0 / D) + norm_epsilon)
        rs[rows, :] = jnp.broadcast_to(scale, (TM, 128))
        n[rows, :] = c * scale

    def project(t):
        rows = tile_rows(t)
        x = x_c[rows, :]
        q[rows, :] = ((mm(x, wqkv[0:D, :]) + vec(V_BQ)).astype(BF).astype(F32) * inv).astype(BF)
        k[rows, :] = mm(x, wqkv[D : 2 * D, :]).astype(BF)
        v[rows, :] = (mm(x, wqkv[2 * D :, :]) + vec(V_BV)).astype(BF)

    def attend(clusters):
        groups = [pl.ds(pl.multiple_of(c * CL, CL), CL) for c in clusters]
        pairs = [(i, p, slice(p * PW, (p + 1) * PW)) for i in range(len(groups)) for p in range(PAIRS)]
        scores = [mm(apart(k[groups[i], ps]), q[groups[i], ps], NT) for i, _, ps in pairs]
        total = [jnp.zeros((1, CL), F32)] * len(groups)
        probs = []
        for (i, _, _), both in zip(pairs, scores):
            halves = []
            for h in range(2):
                sh = both[h * CL : (h + 1) * CL]
                sh = sh - jnp.max(sh, axis=0, keepdims=True)
                e = jnp.exp(sh)
                tot = jnp.sum(e, axis=0, keepdims=True)
                r = 1.0 / tot
                total[i] += jnp.log(tot) - jnp.sum(e * sh, axis=0, keepdims=True) * r
                halves.append((e * r).astype(BF))
            probs.append(jnp.concatenate(halves, axis=0))
        mixed = [mm(w, apart(v[groups[i], ps]), TN).astype(BF) for (i, _, ps), w in zip(pairs, probs)]
        for (i, p, ps), w, o in zip(pairs, probs, mixed):
            p_all[clusters[i], p] = w
            heads[groups[i], ps] = o
        for i, group in enumerate(groups):
            ent[:, group] = jnp.broadcast_to(total[i] * (1.0 / HEADS), (8, CL))

    def resid_one(t):
        rows = tile_rows(t)
        return x_c[rows, :].astype(F32) + mm(heads[rows, :], wo[...]) + vec(V_BO)

    def norm_one(t, r1):
        rows = tile_rows(t)
        normal(r1, n1, rs1, rows)
        hidden = n1[rows, :] * vec(V_G1) + vec(V_C1)
        hid[rows, :] = hidden.astype(BF)
        n2[rows, :] = hidden

    def widen(t, columns):
        rows = tile_rows(t)
        parts = [pl.ds(pl.multiple_of(f * FC, FC), FC) for f in columns]
        ups = [mm(hid[rows, :], wu[fs, :], NT) for fs in parts]

        def finish():
            for fs, up in zip(parts, ups):
                g, g_slope = gelu_parts(up + b_u[:, fs])
                act[rows, fs] = g.astype(BF)
                slope[rows, fs] = g_slope.astype(BF)

        return finish

    def resid_two(t):
        rows = tile_rows(t)
        return n2[rows, :] + mm(act[rows, :], wd[...]) + vec(V_BD)

    def norm_two(t, r2):
        rows = tile_rows(t)
        normal(r2, n2, rs2, rows)
        out_c[rows, :] = (n2[rows, :] * vec(V_G2) + vec(V_C2)).astype(BF)

    def save_all(t, which):
        for i in which:
            save(t, i).start()

    per = TM // CL
    weights[0][1]()
    project(0)
    project(1)
    for t in range(2):
        attend(range(t * per, (t + 1) * per))
        save_all(t, (0, 3, 4, 5))
        save_p(t).start()
    weights[1][1]()
    r1 = [resid_one(t) for t in range(2)]
    for t in range(2):
        norm_one(t, r1[t])
    weights[2][1]()
    for t in range(2):
        loop(FF // FC // 2, lambda f, t=t: widen(t, [2 * f, 2 * f + 1])())
        save_all(t, (1, 2, 6, 7, 9))
    weights[3][1]()
    r2 = [resid_two(t) for t in range(2)]
    for t in range(2):
        norm_two(t, r2[t])
        save_all(t, (8, 10))

    for j, back in enumerate((back_0, back_1, back_2, back_3)):
        own = seat_part(meta, j, cap)
        back[0:cap, :] = mm(own, out_c[...], TN).astype(BF)
        line = mm(ent[...].astype(BF), own)
        back[cap:, :] = jnp.concatenate([line, line], axis=1)[0:1].astype(BF) * jnp.ones((META, 1), BF)

    def saved_all(t):
        for i in range(len(saved)):
            save(t, i).wait()
        save_p(t).wait()

    loop(ROWS // TM, saved_all)


def shape_of(kind, *shape):
    return jax.ShapeDtypeStruct(shape, kind)


def saved_shapes():
    rows, wide = ((ROWS, D), BF), ((ROWS, FF), BF)
    probs = ((ROWS // CL, PAIRS, 2 * CL, CL), BF)
    full, thin = ((ROWS, D), F32), ((ROWS, 128), F32)
    return rows, wide, probs, full, thin


def forward(cap, positions, slots, vecs, b_u, x_c, meta):
    rows, wide, probs, full, thin = saved_shapes()
    kept = (rows, wide, rows, rows, rows, rows, probs, wide, full, full, thin, thin)
    dma = pltpu.SemaphoreType.DMA
    return pl.pallas_call(
        functools.partial(forward_kernel, cap),
        out_shape=(shape_of(BF, cap + META, D),) * SD + tuple(shape_of(kind, *shape) for shape, kind in kept),
        in_specs=[SMEM, ANY, VMEM, VMEM, ANY, VMEM],
        out_specs=(VMEM,) * SD + (ANY,) * len(kept),
        scratch_shapes=[
            pltpu.VMEM((3 * D, D), BF),
            pltpu.VMEM((D, D), BF),
            pltpu.VMEM((FF, D), BF),
            pltpu.VMEM((FF, D), BF),
            pltpu.VMEM(*rows),
        ]
        + [pltpu.VMEM(*a) for a in kept]
        + [
            pltpu.VMEM(*rows),
            pltpu.VMEM((8, ROWS), F32),
            dma((4,)),
            dma,
            dma((12,)),
        ],
        compiler_params=pltpu.CompilerParams(vmem_limit_bytes=VMEM_LIMIT),
        cost_estimate=pl.CostEstimate(flops=2 * ROWS * WROWS * D, bytes_accessed=64 << 20, transcendentals=0),
        name="forward",
    )(positions, slots, vecs, b_u, x_c, meta)


def backward_kernel(
    cap,
    pos,
    slots,
    vecs,
    meta,
    cot_0,
    cot_1,
    cot_2,
    cot_3,
    q_h,
    k_h,
    v_h,
    p_h,
    slope_h,
    n1_h,
    n2_h,
    rs1_h,
    rs2_h,
    back_0,
    back_1,
    back_2,
    back_3,
    shares,
    d_up_h,
    d_q_h,
    d_k_h,
    d_v_h,
    d_proj_h,
    d_br_h,
    wqkv,
    wo,
    wu,
    wd,
    blocks,
    q,
    k,
    v,
    p_all,
    d_up,
    n1,
    n2,
    rs1,
    rs2,
    d_proj,
    d_br,
    ing_c,
    d_h_t,
    gvec,
    g_bu,
    w_sem,
    c_sem,
    i_sem,
    o_sem,
):
    inv = 1.0 / math.sqrt(HD)
    get_c = [
        pltpu.make_async_copy(cot, blocks.at[j], c_sem.at[j]) for j, cot in enumerate((cot_0, cot_1, cot_2, cot_3))
    ]
    for copy in get_c:
        copy.start()
    fetch = [
        pltpu.make_async_copy(src, dst, i_sem.at[i])
        for i, (src, dst) in enumerate(
            (
                (n2_h, n2),
                (rs2_h, rs2),
                (slope_h, d_up),
                (n1_h, n1),
                (rs1_h, rs1),
                (v_h, v),
                (p_h, p_all),
                (k_h, k),
                (q_h, q),
            )
        )
    ]
    weights = [
        weight_copies(pos, slots, w, w_sem.at[i], first)
        for i, (w, first) in enumerate(((wd, 64), (wu, 32), (wo, 24), (wqkv, 0)))
    ]
    fetch[0].start()
    fetch[1].start()
    weights[0][0]()
    fetch[2].start()
    weights[1][0]()
    fetch[3].start()
    fetch[4].start()
    weights[2][0]()
    for i in range(5, 9):
        fetch[i].start()
    weights[3][0]()
    gvec[...] = jnp.zeros_like(gvec)
    g_bu[...] = jnp.zeros_like(g_bu)
    shares[...] = jnp.zeros_like(shares)
    for copy in get_c:
        copy.wait()
    seat_rows(meta, blocks, cap, d_br)
    apart = halves_of_heads()

    def vec(i):
        return vecs[i : i + 1, :]

    def add_vec(i, value):
        gvec[i : i + 1, :] += jnp.sum(value, axis=0, keepdims=True)

    saved = ((d_up, d_up_h), (q, d_q_h), (k, d_k_h), (v, d_v_h), (d_proj, d_proj_h), (d_br, d_br_h))

    def save(t, i):
        src, dst = saved[i]
        return pltpu.make_async_copy(src.at[tile_rows(t)], dst.at[tile_rows(t)], o_sem.at[i])

    def norm_back(e, n, rs, gain, shift):
        add_vec(gain, e * n)
        add_vec(shift, e)
        eg = e * vec(gain)
        return rs * (eg - lane_sum(eg) * (1.0 / D) - n * (lane_sum(eg * n) * (1.0 / D)))

    def norm_two_back(t):
        rows = tile_rows(t)
        d_r2 = norm_back(d_br[rows, :].astype(F32), n2[rows, :], rs2[rows, 0:1], V_G2, V_C2)
        d_br[rows, :] = d_r2.astype(BF)
        add_vec(V_BD, d_br[rows, :].astype(F32))
        n2[rows, :] = d_r2

    def widen_back(t, columns):
        rows = tile_rows(t)
        parts = [pl.ds(pl.multiple_of(f * FC, FC), FC) for f in columns]
        ups = [mm(d_br[rows, :], wd[fs, :], NT) for fs in parts]

        def finish():
            for fs, up in zip(parts, ups):
                du = (up * d_up[rows, fs].astype(F32)).astype(BF)
                d_up[rows, fs] = du
                g_bu[:, fs] += jnp.sum(du.astype(F32), axis=0, keepdims=True)

        return finish

    def hidden_back(t):
        rows = tile_rows(t)
        return n2[rows, :] + mm(d_up[rows, :], wu[...])

    def norm_one_back(t, d_h):
        rows = tile_rows(t)
        d_r1 = norm_back(d_h, n1[rows, :], rs1[rows, 0:1], V_G1, V_C1)
        d_proj[rows, :] = d_r1.astype(BF)
        n2[rows, :] = d_r1
        add_vec(V_BO, d_proj[rows, :].astype(F32))

    def heads_back(t):
        rows = tile_rows(t)
        d_h_t[rows, :] = mm(d_proj[rows, :], wo[...], NT).astype(BF)

    def attend_back(clusters):
        pairs = [
            (c, p, pl.ds(pl.multiple_of(c * CL, CL), CL), slice(p * PW, (p + 1) * PW))
            for c in clusters
            for p in range(PAIRS)
        ]
        probs = [p_all[c, p] for c, p, _, _ in pairs]
        d_heads = [d_h_t[gr, ps] for _, _, gr, ps in pairs]
        d_probs = [mm(apart(v[gr, ps]), dh, NT) for (_, _, gr, ps), dh in zip(pairs, d_heads)]
        d_values = [
            mm(jnp.concatenate([w[0:CL], w[CL:]], axis=1), apart(dh)).astype(BF) for w, dh in zip(probs, d_heads)
        ]
        d_scores = []
        for w, dw in zip(probs, d_probs):
            halves = []
            for h in range(2):
                wh = w[h * CL : (h + 1) * CL].astype(F32)
                dwh = dw[h * CL : (h + 1) * CL]
                halves.append((wh * (dwh - jnp.sum(dwh * wh, axis=0, keepdims=True))).astype(BF))
            d_scores.append(halves)
        d_keys = [
            mm(jnp.concatenate(ds, axis=1), apart(q[gr, ps])).astype(BF) for (_, _, gr, ps), ds in zip(pairs, d_scores)
        ]
        d_queries = [
            (mm(jnp.concatenate(ds, axis=0), apart(k[gr, ps]), TN) * inv).astype(BF)
            for (_, _, gr, ps), ds in zip(pairs, d_scores)
        ]
        for (_, _, gr, ps), dq, dk, dv in zip(pairs, d_queries, d_keys, d_values):
            q[gr, ps] = dq
            k[gr, ps] = dk
            v[gr, ps] = dv

    def rows_back(t):
        rows = tile_rows(t)
        return (
            mm(q[rows, :], wqkv[0:D, :], NT)
            + mm(k[rows, :], wqkv[D : 2 * D, :], NT)
            + mm(v[rows, :], wqkv[2 * D :, :], NT)
        )

    def rows_done(t, d_x):
        rows = tile_rows(t)
        add_vec(V_BQ, q[rows, :].astype(F32))
        add_vec(V_BV, v[rows, :].astype(F32))
        ing_c[rows, :] = (n2[rows, :] + d_x.astype(BF).astype(F32)).astype(BF)

    def save_all(t, which):
        for i in which:
            save(t, i).start()

    per = TM // CL
    fetch[0].wait()
    fetch[1].wait()
    norm_two_back(0)
    norm_two_back(1)
    weights[0][1]()
    fetch[2].wait()
    loop(FF // FC // 2, lambda f: widen_back(0, [2 * f, 2 * f + 1])())
    save_all(0, (0, 5))
    weights[1][1]()
    fetch[3].wait()
    fetch[4].wait()
    norm_one_back(0, hidden_back(0))
    weights[2][1]()
    for i in range(5, 9):
        fetch[i].wait()
    heads_back(0)
    save_all(0, (4,))
    loop(FF // FC // 2, lambda f: widen_back(1, [2 * f, 2 * f + 1])())
    attend_back(range(per))
    save_all(0, (1, 2, 3))
    save_all(1, (0, 5))
    weights[3][1]()
    d_h = hidden_back(1)
    d_x = rows_back(0)
    norm_one_back(1, d_h)
    heads_back(1)
    rows_done(0, d_x)
    save_all(1, (4,))
    attend_back(range(per, 2 * per))
    save_all(1, (1, 2, 3))
    rows_done(1, rows_back(1))

    for j, back in enumerate((back_0, back_1, back_2, back_3)):
        back[...] = mm(seat_part(meta, j, cap), ing_c[...], TN).astype(BF)

    for chunk in range(72):
        row, lane = chunk // 6, chunk % 6 * 128
        if row < 8:
            part = gvec[row : row + 1, lane : lane + 128]
        else:
            lane += (row - 8) * D
            part = g_bu[:, lane : lane + 128]
        shares[chunk // 9, chunk % 9 : chunk % 9 + 1, :] = part

    def saved_all(t):
        for i in range(len(saved)):
            save(t, i).wait()

    loop(ROWS // TM, saved_all)


def backward(cap, positions, slots, vecs, meta, cots, saved):
    rows, wide, probs, full, thin = saved_shapes()
    dma = pltpu.SemaphoreType.DMA
    grads = (wide, rows, rows, rows, rows, rows)
    return pl.pallas_call(
        functools.partial(backward_kernel, cap),
        out_shape=(shape_of(BF, cap, D),) * SD
        + (shape_of(F32, 8, 16, 128),)
        + tuple(shape_of(kind, *shape) for shape, kind in grads),
        in_specs=[SMEM, ANY, VMEM, VMEM] + [ANY] * (SD + 9),
        out_specs=(VMEM,) * (SD + 1) + (ANY,) * len(grads),
        scratch_shapes=[
            pltpu.VMEM((3 * D, D), BF),
            pltpu.VMEM((D, D), BF),
            pltpu.VMEM((FF, D), BF),
            pltpu.VMEM((FF, D), BF),
            pltpu.VMEM((SD, cap, D), BF),
        ]
        + [pltpu.VMEM(*a) for a in (rows, rows, rows, probs, wide, full, full, thin, thin, rows, rows, rows)]
        + [
            pltpu.VMEM(*rows),
            pltpu.VMEM((8, D), F32),
            pltpu.VMEM((1, FF), F32),
            dma((4,)),
            dma((4,)),
            dma((9,)),
            dma((6,)),
        ],
        compiler_params=pltpu.CompilerParams(vmem_limit_bytes=VMEM_LIMIT),
        cost_estimate=pl.CostEstimate(flops=2 * ROWS * WROWS * D, bytes_accessed=64 << 20, transcendentals=0),
        name="backward",
    )(positions, slots, vecs, meta, *cots, *saved)


WC = 8 * BLK


def weight_kernel(
    pos,
    x_h,
    heads_h,
    act_h,
    d_up_h,
    d_q_h,
    d_k_h,
    d_v_h,
    d_proj_h,
    hid_h,
    d_br_h,
    grads,
    x_c,
    heads,
    act,
    d_up,
    d_q,
    d_k,
    d_v,
    d_proj,
    hid,
    d_br,
    stage,
    i_sem,
    g_sem,
):
    refs = (
        (x_h, x_c),
        (d_q_h, d_q),
        (d_k_h, d_k),
        (d_v_h, d_v),
        (heads_h, heads),
        (d_proj_h, d_proj),
        (hid_h, hid),
        (d_up_h, d_up),
        (d_br_h, d_br),
        (act_h, act),
    )
    fetch = [pltpu.make_async_copy(src, dst, i_sem.at[i]) for i, (src, dst) in enumerate(refs)]
    for copy in fetch:
        copy.start()

    per = WC // BLK

    def g_copy(chunk, j, at):
        return pltpu.make_async_copy(
            stage.at[at, pl.ds(j * BLK, BLK)], grads.at[pos[chunk * per + j]], g_sem.at[at]
        )

    def put(chunk, left, right):
        at = lax.rem(chunk, 2)

        @pl.when(chunk >= 2)
        def _():
            for j in range(per):
                g_copy(chunk - 2, j, at).wait()

        stage[at] = mm(left, right, TN).astype(BF)
        for j in range(per):
            g_copy(chunk, j, at).start()

    first = 0
    for left, right, needs in (
        (x_c, d_q, (0, 1)),
        (x_c, d_k, (2,)),
        (x_c, d_v, (3,)),
        (heads, d_proj, (4, 5)),
        (d_up, hid, (6, 7)),
        (act, d_br, (8, 9)),
    ):
        for i in needs:
            fetch[i].wait()

        def body(j, left=left, right=right, first=first):
            put(first + j, left[:, pl.ds(pl.multiple_of(j * WC, WC), WC)], right[...])

        loop(left.shape[1] // WC, body)
        first += left.shape[1] // WC
    for chunk in (first - 2, first - 1):
        for j in range(per):
            g_copy(chunk, j, chunk % 2).wait()


def weight_grads_of(total_slots, positions, x_c, saved):
    r_v, w_v = pltpu.VMEM((ROWS, D), BF), pltpu.VMEM((ROWS, FF), BF)
    return pl.pallas_call(
        weight_kernel,
        out_shape=jax.ShapeDtypeStruct((total_slots, BLK, D), BF),
        in_specs=[SMEM] + [ANY] * 10,
        out_specs=ANY,
        scratch_shapes=[r_v, r_v, w_v, w_v]
        + [r_v] * 6
        + [
            pltpu.VMEM((2, WC, D), BF),
            pltpu.SemaphoreType.DMA((10,)),
            pltpu.SemaphoreType.DMA((2,)),
        ],
        compiler_params=pltpu.CompilerParams(vmem_limit_bytes=VMEM_LIMIT),
        cost_estimate=pl.CostEstimate(flops=2 * ROWS * WROWS * D, bytes_accessed=40 << 20, transcendentals=0),
        name="weight_grads",
    )(positions, x_c, *saved)


def adam_step(grad_now, weight_old, first_old, second_old, rate_step):
    first_new = beta_first * first_old + (1.0 - beta_first) * grad_now
    second_new = beta_second * second_old + (1.0 - beta_second) * grad_now * grad_now
    square = second_new * (1.0 / (1.0 - beta_second**STEP))
    root = jnp.where(square > 0.0, square * lax.rsqrt(square), 0.0)
    step = first_new * (1.0 / (1.0 - beta_first**STEP)) * inverse(root + adam_epsilon)
    return (first_new, second_new, weight_old - rate_step * (step + weight_decay * weight_old))


def finish_kernel(
    pos,
    total_h,
    master_h,
    first_h,
    second_h,
    v_grad,
    v_master,
    v_first,
    v_second,
    line,
    counts,
    out_h,
    ing_h,
    grad_new,
    first_new,
    second_new,
    master_new,
    low_new,
    v_grad_new,
    v_first_new,
    v_second_new,
    v_master_new,
    v_low_new,
    entropy,
    occupancy,
    output,
    input_grad,
    total,
    master,
    first,
    second,
    grad,
    out_v,
    ing_v,
    in_s,
    out_s,
    row_s,
):
    count = total.shape[0]
    ins = ((total_h, total), (master_h, master), (first_h, first), (second_h, second))
    outs = ((total, low_new), (master, master_new), (first, first_new), (second, second_new), (grad, grad_new))

    groups = [(first, min(max(first, 1), 4, count - first)) for first in (0, 1, 2, 4, 8, 12) if first < count]

    def fetch(i, n):
        src, dst = ins[i]
        part = pl.ds(*groups[n])
        return pltpu.make_async_copy(src.at[part], dst.at[part], in_s.at[i, n])

    def put(i, n):
        src, dst = outs[i]
        part = pl.ds(*groups[n])
        return pltpu.make_async_copy(src.at[part], dst.at[part], out_s.at[i, n])

    rows_in = [pltpu.make_async_copy(a, b, row_s.at[0, n]) for n, (a, b) in enumerate(((out_h, out_v), (ing_h, ing_v)))]
    rows_out = [pltpu.make_async_copy(a, b, row_s.at[1, n]) for n, (a, b) in enumerate(((out_v, output), (ing_v, input_grad)))]
    for n in range(len(groups)):
        for i in range(4):
            fetch(i, n).start()
    for copy in rows_in:
        copy.start()
    entropy[...] = line[...].reshape(ROWS)
    occupancy[...] = counts[...]
    length = v_master.shape[0]
    for n in range(-(-length // 128)):
        part = slice(n * 128, min((n + 1) * 128, length))
        g = v_grad[n : n + 1, 0 : part.stop - part.start].reshape(part.stop - part.start)
        m, v, w = adam_update(g, v_master[part], v_first[part], v_second[part], rate_vector)
        v_grad_new[part] = g
        v_first_new[part] = m
        v_second_new[part] = v
        v_master_new[part] = w
    v_low_new[...] = v_master_new[...].astype(BF)

    def slot(s):
        g = jnp.where(s < pos[NBLK], total[s].astype(F32), 0.0)
        m, v, w = adam_step(g, master[s], first[s], second[s], rate_matrix)
        grad[s] = g
        first[s] = m
        second[s] = v
        master[s] = w
        total[s] = w.astype(BF)

    for n, (start, size) in enumerate(groups):
        for i in range(4):
            fetch(i, n).wait()
        loop(size, lambda j, start=start: slot(start + j))
        for i in range(5):
            put(i, n).start()
    for copy_in, copy_out in zip(rows_in, rows_out):
        copy_in.wait()
        copy_out.start()
    for n in range(len(groups)):
        for i in range(5):
            put(i, n).wait()
    for copy in rows_out:
        copy.wait()


def finish(positions, total, weights, v_grad, vectors, line, counts, out, ing):
    count = total.shape[0]
    low, full = pltpu.VMEM((count, BLK, D), BF), pltpu.VMEM((count, BLK, D), F32)
    f32_slots, f32_vector = shape_of(F32, count, BLK, D), shape_of(F32, *vectors[0].shape)
    dma = pltpu.SemaphoreType.DMA
    return pl.pallas_call(
        finish_kernel,
        out_shape=(f32_slots,) * 4
        + (shape_of(BF, count, BLK, D),)
        + (f32_vector,) * 4
        + (shape_of(BF, *vectors[0].shape), shape_of(BF, ROWS), shape_of(I32, *counts.shape))
        + (shape_of(BF, ROWS, D),) * 2,
        in_specs=[SMEM] + [ANY] * 4 + [VMEM] * 6 + [ANY] * 2,
        out_specs=(ANY,) * 5 + (VMEM,) * 7 + (ANY,) * 2,
        scratch_shapes=[low, full, full, full, full]
        + [pltpu.VMEM((ROWS, D), BF)] * 2
        + [dma((4, 6)), dma((5, 6)), dma((2, 2))],
        compiler_params=pltpu.CompilerParams(vmem_limit_bytes=VMEM_LIMIT),
        name="finish",
    )(positions, total, *weights, v_grad, *vectors, line, counts, out, ing)


def local(
    tokens,
    cotangent,
    cluster_order,
    block_owner,
    master_slots,
    moment_one,
    moment_two,
    vector_master,
    vector_moment_one,
    vector_moment_two,
):
    tok_count = lax.axis_size("tok")
    tok_index = lax.axis_index("tok")
    slot_count = master_slots.shape[0]
    cap = tok_count // SD * (max(1, CPS // tok_count) * 3 * CL // (2 * SD))
    total_slots = tok_count * slot_count
    order = cluster_order.reshape(1, ROWS)

    block = jax.ShapeDtypeStruct((SD, cap, D), BF)
    meta_shape = jax.ShapeDtypeStruct((SD, META, D), BF)
    row_block = jax.ShapeDtypeStruct((ROWS, D), BF)
    four_planes = tok_count == 8 and lax.axis_size("rep") == 4
    if four_planes:
        slots_low, x_c, *cots, recv_meta, vecs, b_u, occupancy, positions = gather_all(
            cap, tokens, cotangent, order, master_slots, vector_master, block_owner
        )
        positions = positions.reshape(128)
        slots_low = slots_low.reshape(total_slots, BLK, D)
    else:
        positions = slot_positions(block_owner, slot_count)
        owned = jnp.sum((block_owner == tok_index).astype(I32)).reshape(1)
        positions = jnp.concatenate([positions, owned])
        slots_low = lax.all_gather(master_slots.astype(BF), "tok", axis=0, tiled=True)
        vectors = lax.all_gather(vector_master.astype(BF), "tok", axis=0, tiled=True).astype(F32)
        vecs, b_u = vectors[: 8 * D].reshape(8, D), vectors[8 * D :].reshape(1, FF)
        cluster = tok_index // SD * CPS + cluster_order // CL
        target = cluster % tok_count
        chosen = target[None, :] == jnp.arange(tok_count, dtype=jnp.int32)[:, None]
        sent_counts = jnp.sum(chosen.astype(F32), axis=1)
        own_row = (jnp.arange(tok_count, dtype=jnp.int32) == tok_index).astype(F32)
        occupancy = lax.psum(own_row[:, None] * sent_counts[None, :], ("tok", "rep")).astype(jnp.int32)
        send_x, send_c, meta = pl.pallas_call(
            functools.partial(send_kernel, cap),
            out_shape=(block, block, meta_shape),
            in_specs=[VMEM] * 3,
            out_specs=(VMEM,) * 3,
            compiler_params=pltpu.CompilerParams(vmem_limit_bytes=VMEM_LIMIT),
            name="send_rows",
        )(tokens, cotangent, order)
        recv_x, recv_meta = (jnp.stack(swap_blocks(b)) for b in (send_x, meta))
        x_c = pl.pallas_call(
            functools.partial(seat_kernel, cap),
            out_shape=row_block,
            in_specs=[VMEM] * 2,
            out_specs=VMEM,
            compiler_params=pltpu.CompilerParams(vmem_limit_bytes=VMEM_LIMIT),
            name="seat_rows",
        )(recv_x, recv_meta)
        cots = [send_c[k] for k in range(SD)]

    cots = swap_blocks(cots)
    *out_blocks, heads, act, hid, q, k, v, p, slope, n1, n2, rs1, rs2 = forward(
        cap, positions, slots_low, vecs, b_u, x_c, recv_meta
    )
    out_blocks = swap_blocks(out_blocks)
    *ing_blocks, shares, d_up, d_q, d_k, d_v, d_proj, d_br = backward(
        cap, positions, slots_low, vecs, recv_meta, cots, (q, k, v, p, slope, n1, n2, rs1, rs2)
    )
    ing_blocks = swap_blocks(ing_blocks)
    grads = weight_grads_of(
        total_slots, positions, x_c, (heads, act, d_up, d_q, d_k, d_v, d_proj, hid, d_br)
    )
    if four_planes:
        total, vec_owned, output, input_grad, entropy = reduce_all(
            cap, grads, shares, order, out_blocks, ing_blocks, slot_count
        )
    else:
        total = lax.psum(lax.psum_scatter(grads, "tok", scatter_dimension=0, tiled=True), "rep")
        grad_vector = shares[:, 0:9].reshape(-1)
        vec_owned = lax.psum(lax.psum_scatter(grad_vector, "tok", scatter_dimension=0, tiled=True), "rep")
        vec_owned = jnp.pad(vec_owned, (0, -vec_owned.shape[0] % 128)).reshape(-1, 128)
        output, input_grad, entropy = pl.pallas_call(
            functools.partial(return_kernel, cap),
            out_shape=(row_block, row_block, jax.ShapeDtypeStruct((1, ROWS), BF)),
            in_specs=[VMEM] * (2 * SD + 1),
            out_specs=(VMEM,) * 3,
            compiler_params=pltpu.CompilerParams(vmem_limit_bytes=VMEM_LIMIT),
            name="return_rows",
        )(order, *out_blocks, *ing_blocks)

    (
        owned_grad,
        first_new,
        second_new,
        master_new,
        low_new,
        vec_owned,
        vec_first,
        vec_second,
        vec_new,
        vec_low_new,
        row_entropy,
        occupancy,
        output,
        input_grad,
    ) = finish(
        positions,
        total,
        (master_slots, moment_one, moment_two),
        vec_owned,
        (vector_master, vector_moment_one, vector_moment_two),
        entropy,
        occupancy,
        output,
        input_grad,
    )
    return (
        output,
        input_grad,
        owned_grad,
        first_new,
        second_new,
        master_new,
        low_new,
        vec_owned,
        vec_first,
        vec_second,
        vec_new,
        vec_low_new,
        row_entropy,
        occupancy,
    )


def solution(mesh):
    placed = (
        P(("rep", "tok"), None),
        P(("rep", "tok"), None),
        P(("rep", "tok")),
        P(),
        P("tok", None, None),
        P("tok", None, None),
        P("tok", None, None),
        P("tok"),
        P("tok"),
        P("tok"),
    )
    return jax.shard_map(
        local,
        mesh=mesh,
        in_specs=placed,
        out_specs=(
            P(("rep", "tok"), None),
            P(("rep", "tok"), None),
            P("tok", None, None),
            P("tok", None, None),
            P("tok", None, None),
            P("tok", None, None),
            P("tok", None, None),
            P("tok"),
            P("tok"),
            P("tok"),
            P("tok"),
            P("tok"),
            P(("rep", "tok")),
            P(),
        ),
        check_vma=False,
    )
```

```python
import functools
import math

import jax
import jax.numpy as jnp
from jax import lax
from jax.experimental import pallas as pl
from jax.experimental.pallas import tpu as pltpu
from jax.sharding import PartitionSpec as P

D = 768
HEADS = 12
HD = 64
FF = 3072
SD = 4
CL = 128
NBLK = 96
STEP = 10
CPS = 32
WROWS = 9216
BLK = 96
ROWS = 1024
PAIRS = HEADS // 2
PW = 2 * HD
TM = 512
PART = 48
META = 16
VMEM_LIMIT = 63 << 20
FC = 768

norm_epsilon = 1e-06
beta_first = 0.9
beta_second = 0.999
adam_epsilon = 1e-08
weight_decay = 0.01
rate_matrix = 0.02
rate_vector = 0.2

BF = jnp.bfloat16
F32 = jnp.float32
I32 = jnp.int32

VMEM = pl.BlockSpec(memory_space=pltpu.VMEM)
SMEM = pl.BlockSpec(memory_space=pltpu.SMEM)
ANY = pl.BlockSpec(memory_space=pl.ANY)

NN = (((1,), (0,)), ((), ()))
NT = (((1,), (1,)), ((), ()))
TN = (((0,), (0,)), ((), ()))


def mm(a, b, dims=NN):
    return lax.dot_general(a, b, dims, preferred_element_type=F32)


def slot_positions(block_owner, slot_count):
    owners = block_owner[:, 0]
    blocks = owners.shape[0]
    shared = owners[:, None] == owners[None, :]
    before = (
        jnp.arange(blocks, dtype=jnp.int32)[None, :] < jnp.arange(blocks, dtype=jnp.int32)[:, None]
    )
    earlier = jnp.sum((shared & before).astype(jnp.int32), axis=1)
    return owners * slot_count + earlier


def adam_update(grad_now, weight_old, first_old, second_old, rate_step):
    first_new = beta_first * first_old + (1.0 - beta_first) * grad_now
    second_new = beta_second * second_old + (1.0 - beta_second) * grad_now * grad_now
    first_hat = first_new / (1.0 - beta_first**STEP)
    second_hat = second_new / (1.0 - beta_second**STEP)
    weight_new = weight_old - rate_step * (
        first_hat / (jnp.sqrt(second_hat) + adam_epsilon) + weight_decay * weight_old
    )
    return (first_new, second_new, weight_new)


def route_slots(order, seat, cap):
    cluster = order // CL
    rel = lax.rem(cluster, SD) ^ seat
    place = (cluster // SD) * CL + lax.rem(order, CL) + 1
    chosen = lax.broadcasted_iota(I32, (8, ROWS), 0) == rel
    chosen_low = jnp.where(chosen, 1.0, 0.0).astype(BF)
    before = lax.broadcasted_iota(I32, (ROWS, ROWS), 0) < lax.broadcasted_iota(I32, (ROWS, ROWS), 1)
    before_low = jnp.where(before, 1.0, 0.0).astype(BF)
    running = mm(chosen_low, before_low)
    rank = jnp.sum(jnp.where(chosen, running, 0.0), axis=0, keepdims=True).astype(I32)
    return rel * cap + rank, place


def slot_matrix(slots, at, cap):
    rows = lax.broadcasted_iota(I32, (cap, ROWS), 0) + at * cap
    return jnp.where(rows == slots, 1.0, 0.0).astype(BF)


def send_kernel(cap, tokens, cotangent, order, send_x, send_c, meta):
    seat = lax.rem(lax.axis_index("tok"), SD)
    slots, place = route_slots(order[...], seat, cap)
    digits = jnp.concatenate([place // CL, lax.rem(place, CL)] + [place * 0] * 6, axis=0).astype(F32).astype(BF)
    for at in range(SD):
        picked = slot_matrix(slots, at, cap)
        send_x[at] = mm(picked, tokens[...]).astype(BF)
        send_c[at] = mm(picked, cotangent[...]).astype(BF)
        coded = mm(digits, picked, NT)
        line = jnp.concatenate([coded[0:1], coded[1:2]], axis=1)
        meta[at] = jnp.broadcast_to(line, (META, D)).astype(BF)


def remote(src, dst, send_sem, recv_sem, tok, rep):
    return pltpu.make_async_remote_copy(
        src_ref=src,
        dst_ref=dst,
        send_sem=send_sem,
        recv_sem=recv_sem,
        device_id={"tok": tok, "rep": rep},
        device_id_type=pl.DeviceIdType.MESH,
    )


def loop(n, body):
    def run(i, c):
        body(i)
        return c

    lax.fori_loop(0, n, run, 0)


class Place:
    def __init__(self):
        self.me = me = lax.axis_index("tok")
        self.z = z = lax.axis_index("rep")
        core, x, y = me % 2, (me // 2) % 2, me // 4
        self.twin = me + 1 - 2 * core
        self.xn = me + 2 - 4 * x
        self.yn = me + 4 - 8 * y
        self.dn = self.xn + 4 - 8 * y
        self.side = z % 2
        self.zp = z + 1 - 2 * self.side

    def twin_of(self, tok):
        return tok + 1 - 2 * (tok % 2)

    def greet(self, peers):
        barrier = pltpu.get_barrier_semaphore()
        for tok, rep in peers:
            pl.semaphore_signal(
                barrier, inc=1, device_id={"tok": tok, "rep": rep}, device_id_type=pl.DeviceIdType.MESH
            )
        return lambda: pl.semaphore_wait(barrier, len(peers))


def seat_matrix(meta, first, rows, cap):
    hi = jnp.concatenate([meta[k, 0:8, 0:cap] for k in range(SD)], axis=1).astype(F32)[0:1]
    lo = jnp.concatenate([meta[k, 0:8, cap : 2 * cap] for k in range(SD)], axis=1).astype(F32)[0:1]
    at = (hi * CL + lo).astype(I32)
    seats = lax.broadcasted_iota(I32, (rows, SD * cap), 0) + (first + 1)
    return jnp.where(seats == at, 1.0, 0.0).astype(BF)


def seat_part(meta, k, cap):
    hi = meta[k, 0:8, 0:cap].astype(F32)[0:1]
    lo = meta[k, 0:8, cap : 2 * cap].astype(F32)[0:1]
    at = (hi * CL + lo).astype(I32)
    seats = lax.broadcasted_iota(I32, (ROWS, cap), 0) + 1
    return jnp.where(seats == at, 1.0, 0.0).astype(BF)


def seat_rows(meta, blocks, cap, to):
    def body(t):
        r0 = pl.multiple_of(t * 256, 256)
        rows = blocks[...].reshape(SD * cap, D)
        to[pl.ds(r0, 256), :] = mm(seat_matrix(meta, r0, 256, cap), rows).astype(BF)

    loop(ROWS // 256, body)


def seat_kernel(cap, blocks, meta, to):
    seat_rows(meta, blocks, cap, to)


def gather_kernel(
    cap,
    count,
    tokens_h,
    cotangent_h,
    order,
    master_h,
    vector,
    owner_of,
    slots,
    x_c,
    cot_0,
    cot_1,
    cot_2,
    cot_3,
    recv_meta,
    vecs,
    b_u,
    occupancy,
    positions,
    tokens,
    cotangent,
    master,
    own,
    send_x,
    send_c,
    meta,
    recv_x,
    got_meta,
    slot_of,
    digits,
    mine,
    by_z,
    by_tok,
    x_s,
    x_r,
    y_s,
    y_r,
    d_s,
    d_r,
    zx_s,
    zx_r,
    zd_s,
    zd_r,
    zy_s,
    zy_r,
    p_s,
    p_r,
    row_s,
    row_r,
    z_s,
    z_r,
    t_s,
    t_r,
    local_s,
):
    at = Place()
    me, z, side = at.me, at.z, at.side
    n_tok, n_rep = 8, 4
    peers = [((me + d) % n_tok, z) for d in range(1, n_tok)] + [(me, (z + d) % n_rep) for d in range(1, n_rep)]
    fetch = [
        pltpu.make_async_copy(src, dst, local_s.at[i])
        for i, (src, dst) in enumerate(((master_h, master), (tokens_h, tokens), (cotangent_h, cotangent)))
    ]
    for copy in fetch:
        copy.start()
    wait_peers = at.greet(peers)
    fetch[0].wait()

    last = count - 1

    def near(j):
        return side * last + (1 - 2 * side) * j

    def far(j):
        return (1 - side) * last - (1 - 2 * side) * j

    few_x, few_d, few_y = 11 * count // 26, 12 * count // 26, 8 * count // 26
    most_x, most_d, most_y = count - few_x, count - few_d, count - few_y

    def piece(owner, s):
        return slots.at[owner * count + s]

    def to_x(s):
        return remote(own.at[s], piece(me, s), x_s.at[s], x_r.at[s], at.xn, z)

    def to_y(s):
        return remote(own.at[s], piece(me, s), y_s.at[s], y_r.at[s], at.yn, z)

    def on_y(s):
        return remote(piece(at.xn, s), piece(at.xn, s), d_s.at[s], d_r.at[s], at.yn, z)

    def x_on_z(s):
        return remote(piece(at.xn, s), piece(at.xn, s), zx_s.at[s], zx_r.at[s], me, at.zp)

    def d_on_z(s):
        return remote(piece(at.dn, s), piece(at.dn, s), zd_s.at[s], zd_r.at[s], me, at.zp)

    def y_on_z(s):
        return remote(piece(at.yn, s), piece(at.yn, s), zy_s.at[s], zy_r.at[s], me, at.zp)

    def x_in(s):
        return remote(own.at[s], piece(at.xn, s), x_s.at[s], x_r.at[s], at.xn, z)

    def y_in(s):
        return remote(own.at[s], piece(at.yn, s), y_s.at[s], y_r.at[s], at.yn, z)

    def d_in(s):
        return remote(own.at[s], piece(at.dn, s), d_s.at[s], d_r.at[s], at.yn, z)

    owners = (me, at.xn, at.yn, at.dn)

    def near_run(q, j0, j1):
        return (q, (1 - side) * j0 + side * (count - j1), j1 - j0)

    def far_run(q, j0, j1):
        return (q, side * j0 + (1 - side) * (count - j1), j1 - j0)

    runs = (
        (0, 0, count),
        near_run(2, 0, few_y),
        near_run(1, 0, most_x),
        near_run(3, 0, most_d),
        far_run(1, 0, few_x),
        near_run(2, few_y, most_y),
        far_run(2, 0, few_y),
        far_run(3, 0, few_d // 2),
        far_run(3, few_d // 2, few_d - 2),
        far_run(3, few_d - 2, few_d),
    )

    def to_twin(i):
        q, s, n = runs[i]
        src = own if q == 0 else slots.at[pl.ds(owners[q] * count + s, n)]
        dst = slots.at[pl.ds(owners[q] * count + s, n)]
        return remote(src, dst, p_s.at[i], p_r.at[i], at.twin, z)

    def cast(j):
        own[near(j)] = master[near(j)].astype(BF)

    loop(most_x, cast)
    wait_peers()
    loop(most_x, lambda j: to_x(near(j)).start())
    loop(few_y, lambda j: to_y(near(j)).start())
    loop(count - most_x, lambda j: cast(most_x + j))
    to_twin(0).start()
    keep = pltpu.make_async_copy(own, slots.at[pl.ds(me * count, count)], local_s.at[3])
    keep.start()

    seat = me % SD
    seats = (me, at.twin, at.xn, at.twin_of(at.xn))
    rows_of = ((meta, got_meta), (send_x, recv_x))

    def row_copy(i, k):
        src, dst = rows_of[i]
        return remote(src.at[k], dst.at[k], row_s.at[i, k], row_r.at[i, k], seats[k], z)

    put_c = [
        pltpu.make_async_copy(send_c.at[k], to, local_s.at[4 + k])
        for k, to in enumerate((cot_0, cot_1, cot_2, cot_3))
    ]

    def route():
        fetch[1].wait()
        fetch[2].wait()
        slots_here, place = route_slots(order[...], seat, cap)
        slot_of[...] = slots_here
        digits[...] = (
            jnp.concatenate([place // CL, lax.rem(place, CL)] + [place * 0] * 6, axis=0).astype(F32).astype(BF)
        )

    def sort_tokens(k):
        picked = slot_matrix(slot_of[...], k, cap)
        send_x[k] = mm(picked, tokens[...]).astype(BF)
        coded = mm(digits[...], picked, NT)
        line = jnp.concatenate([coded[0:1], coded[1:2]], axis=1)
        meta[k] = jnp.broadcast_to(line, (META, D)).astype(BF)
        for i in range(2):
            if k:
                row_copy(i, k).start()
            else:
                src, dst = rows_of[i]
                dst[0] = src[0]

    def sort_cotangent(k):
        send_c[k] = mm(slot_matrix(slot_of[...], k, cap), cotangent[...]).astype(BF)
        put_c[k].start()

    def z_copy(d):
        return remote(by_z.at[0], by_z.at[d], z_s.at[d], z_r.at[d], me, (z + d) % n_rep)

    def t_copy(d):
        return remote(mine, by_tok.at[d], t_s.at[d], t_r.at[d], (me + d) % n_tok, z)

    def count_rows():
        residue = lax.rem(me // SD * CPS + order[...] // CL, n_tok)
        hit = lax.broadcasted_iota(I32, (128, ROWS), 0) == residue
        by_z[0] = mm(jnp.ones((8, ROWS), BF), jnp.where(hit, 1.0, 0.0).astype(BF), NT)
        for d in range(1, n_rep):
            z_copy(d).start()
        for i in range(9):
            mine[i : i + 1] = vector[i * 128 : (i + 1) * 128].reshape(1, 128).astype(BF).astype(F32)
        block_row = lax.broadcasted_iota(I32, (NBLK, NBLK), 0)
        block_col = lax.broadcasted_iota(I32, (NBLK, NBLK), 1)
        by_col = owner_of[...].astype(F32)
        by_row = lane_sum(jnp.where(block_row == block_col, by_col, 0.0))
        earlier = jnp.where((by_row == by_col) & (block_row < block_col), 1.0, 0.0)
        seats_of = (by_col * (count * PART // BLK) + jnp.sum(earlier, axis=0, keepdims=True)).astype(I32)
        mine_all = lane_sum(jnp.where(owner_of[...] == me, 1.0, 0.0)).astype(I32)
        positions[...] = jnp.concatenate([seats_of, jnp.broadcast_to(mine_all, (1, 128 - NBLK))], axis=1)

    def share_vectors():
        for d in range(1, n_rep):
            z_copy(d).wait()
        mine[16:24] = by_z[0] + by_z[1] + by_z[2] + by_z[3]
        for d in range(1, n_tok):
            t_copy(d).start()

    def lay_out_vectors():
        by_tok[0] = mine[...]
        for d in range(1, n_tok):
            t_copy(d).wait()
        for owner in range(n_tok):
            share = by_tok[(me + n_tok - owner) % n_tok]
            occupancy[owner : owner + 1, :] = share[16:17, 0:n_tok].astype(I32)
            for i in range(9):
                chunk = owner * 9 + i
                row, lane = chunk // 6, chunk % 6 * 128
                if row < 8:
                    vecs[row : row + 1, lane : lane + 128] = share[i : i + 1]
                else:
                    lane += (row - 8) * D
                    b_u[:, lane : lane + 128] = share[i : i + 1]

    between = {
        1: lambda: (route(), sort_tokens(2)),
        3: lambda: sort_tokens(3),
        5: lambda: sort_tokens(1),
        7: lambda: (sort_tokens(0), count_rows()),
        9: lambda: sort_cotangent(1),
        11: lambda: sort_cotangent(2),
        13: lambda: sort_cotangent(3),
    }
    for j in range(most_x):
        x_in(near(j)).wait_recv()
        if j < most_d:
            on_y(near(j)).start()
        if j < few_x:
            x_on_z(near(j)).start()
        if j < few_y:
            y_in(near(j)).wait_recv()
            y_on_z(near(j)).start()
        if j == few_y:
            to_twin(1).start()
        if j in between:
            between[j]()
    to_twin(2).start()
    loop(most_y - few_y, lambda j: to_y(near(few_y + j)).start())
    share_vectors()
    sort_cotangent(0)

    def diagonal(j):
        d_in(near(j)).wait_recv()
        d_on_z(near(j)).start()

    loop(few_d, diagonal)
    loop(most_d - few_d, lambda j: d_in(near(few_d + j)).wait_recv())
    to_twin(3).start()
    loop(few_x, lambda j: x_on_z(far(j)).wait_recv())
    to_twin(4).start()
    lay_out_vectors()
    loop(most_x, lambda j: to_x(near(j)).wait_send())
    loop(few_x, lambda j: x_on_z(near(j)).wait_send())
    loop(few_y, lambda j: y_on_z(near(j)).wait_send())
    loop(most_y - few_y, lambda j: y_in(near(few_y + j)).wait_recv())
    to_twin(5).start()
    loop(few_y, lambda j: y_on_z(far(j)).wait_recv())
    to_twin(6).start()
    for i in (0, 1):
        for k in (2, 3, 1):
            row_copy(i, k).wait_recv()
    recv_meta[...] = got_meta[...]
    seat_rows(got_meta, recv_x, cap, x_c)
    loop(most_y, lambda j: to_y(near(j)).wait_send())
    loop(most_d, lambda j: on_y(near(j)).wait_send())
    done = 0
    for i, upto in ((7, few_d // 2), (8, few_d - 2), (9, few_d)):
        loop(upto - done, lambda j, done=done: d_on_z(far(done + j)).wait_recv())
        to_twin(i).start()
        done = upto

    for i in range(2):
        for k in (2, 3, 1):
            row_copy(i, k).wait_send()
    for copy in put_c:
        copy.wait()
    keep.wait()

    loop(few_d, lambda j: d_on_z(near(j)).wait_send())
    for i in range(len(runs)):
        to_twin(i).wait()


def gather_all(cap, tokens, cotangent, order, master, vector, block_owner):
    count = master.shape[0] * BLK // PART
    rows = jax.ShapeDtypeStruct((ROWS, D), BF)
    part = jax.ShapeDtypeStruct((cap, D), BF)
    dma = pltpu.SemaphoreType.DMA
    block = pltpu.VMEM((SD, cap, D), BF)
    meta = pltpu.VMEM((SD, META, D), BF)
    return pl.pallas_call(
        functools.partial(gather_kernel, cap, count),
        out_shape=(
            jax.ShapeDtypeStruct((8 * count, PART, D), BF),
            rows,
            part,
            part,
            part,
            part,
            jax.ShapeDtypeStruct((SD, META, D), BF),
            jax.ShapeDtypeStruct((8, D), F32),
            jax.ShapeDtypeStruct((1, FF), F32),
            jax.ShapeDtypeStruct((8, 8), I32),
            jax.ShapeDtypeStruct((1, 128), I32),
        ),
        in_specs=[ANY, ANY, VMEM, ANY, VMEM, VMEM],
        out_specs=(ANY, VMEM) + (ANY,) * SD + (VMEM,) * 5,
        scratch_shapes=[
            pltpu.VMEM((ROWS, D), BF),
            pltpu.VMEM((ROWS, D), BF),
            pltpu.VMEM((count, PART, D), F32),
            pltpu.VMEM((count, PART, D), BF),
            block,
            block,
            meta,
            block,
            meta,
            pltpu.VMEM((1, ROWS), I32),
            pltpu.VMEM((8, ROWS), BF),
            pltpu.VMEM((24, 128), F32),
            pltpu.VMEM((4, 8, 128), F32),
            pltpu.VMEM((8, 24, 128), F32),
        ]
        + [dma((count,))] * 12
        + [dma((10,))] * 2
        + [dma((2, SD))] * 2
        + [dma((4,))] * 2
        + [dma((8,))] * 2
        + [dma((8,))],
        compiler_params=pltpu.CompilerParams(collective_id=0, has_side_effects=True, vmem_limit_bytes=VMEM_LIMIT),
        cost_estimate=pl.CostEstimate(flops=8 * ROWS * ROWS * D, bytes_accessed=64 << 20, transcendentals=0),
        name="gather",
    )(tokens, cotangent, order, master.reshape(count, PART, D), vector, block_owner.reshape(1, NBLK))


def return_kernel(cap, order, *refs):
    outs, ings, (out, ing, entropy) = refs[:SD], refs[SD : 2 * SD], refs[2 * SD :]
    seat = lax.rem(lax.axis_index("tok"), SD)
    slots, _ = route_slots(order[...], seat, cap)
    picked = jnp.concatenate([slot_matrix(slots, at, cap) for at in range(SD)], axis=0)
    for to, blocks in ((out, outs), (ing, ings)):
        rows = jnp.concatenate([block[0:cap, :] for block in blocks], axis=0)
        to[...] = mm(picked, rows, TN).astype(BF)
    line = jnp.concatenate([block[cap : cap + 8, 0:cap] for block in outs], axis=1)
    entropy[...] = mm(line, picked)[0:1].astype(BF)


def swap_blocks(blocks):
    n = lax.axis_size("tok")
    parts = [blocks[0]]
    for k in range(1, SD):
        parts.append(lax.ppermute(blocks[k], "tok", [(i, i ^ k) for i in range(n)]))
    return parts


def reduce_kernel(
    cap,
    count,
    split,
    grads,
    vec,
    order,
    out_0,
    out_1,
    out_2,
    out_3,
    ing_0,
    ing_1,
    ing_2,
    ing_3,
    total,
    vec_out,
    output,
    input_grad,
    entropy,
    out_v,
    ing_v,
    slot_of,
    a,
    tw,
    rd,
    rx,
    ry,
    o,
    rz1,
    pz,
    rz2,
    fz,
    vt,
    va,
    vb,
    vc,
    a_l,
    keep_l,
    p_s,
    p_r,
    d_s,
    d_r,
    x_s,
    x_r,
    y_s,
    y_r,
    z1_s,
    z1_r,
    z2_s,
    z2_r,
    z3_s,
    z3_r,
    t_s,
    t_r,
    v_s,
    v_r,
    row_l,
):
    at = Place()
    me, z = at.me, at.z
    n_tok, n_rep = 8, 4
    peers = [((me + d) % n_tok, z) for d in range(1, n_tok)] + [(me, (z + d) % n_rep) for d in range(1, n_rep)]
    wait_peers = at.greet(peers)
    owners = (me, at.xn, at.yn, at.dn)

    def load(q):
        return pltpu.make_async_copy(grads.at[pl.ds(owners[q] * count, count)], a.at[q], a_l.at[q])

    for q in (3, 1, 2, 0):
        load(q).start()
    rows_in = [
        pltpu.make_async_copy(src, to.at[k], row_l.at[i, k])
        for i, (blocks, to) in enumerate((((out_0, out_1, out_2, out_3), out_v), ((ing_0, ing_1, ing_2, ing_3), ing_v)))
        for k, src in enumerate(blocks)
    ]
    for copy in rows_in:
        copy.start()
    wait_peers()

    def to_twin(q, g):
        src = grads.at[pl.ds(at.twin_of(owners[q]) * count + 2 * g, 2)]
        return remote(src, tw.at[q, pl.ds(2 * g, 2)], p_s.at[q, g], p_r.at[q, g], at.twin, z)

    def d_y(s):
        return remote(a.at[3, s], rd.at[s], d_s.at[s], d_r.at[s], at.yn, z)

    def d_x(s):
        return remote(a.at[3, s], rd.at[s], d_s.at[s], d_r.at[s], at.xn, z)

    def to_x(s):
        return remote(a.at[1, s], rx.at[s], x_s.at[s], x_r.at[s], at.xn, z)

    def to_y(s):
        return remote(a.at[2, s], ry.at[s], y_s.at[s], y_r.at[s], at.yn, z)

    def z_in(s):
        return remote(o.at[s], rz1.at[s], z1_s.at[s], z1_r.at[s], me, at.zp)

    def z_swap(s):
        return remote(pz.at[s], rz2.at[s], z2_s.at[s], z2_r.at[s], me, n_rep - 1 - z)

    def z_out(s):
        return remote(fz.at[s], fz.at[s], z3_s.at[s], z3_r.at[s], me, at.zp)

    def keep(s):
        return pltpu.make_async_copy(fz.at[s], total.at[s], keep_l.at[s])

    def twin_start(g):
        for q in (3, 1, 2, 0):
            to_twin(q, g).start()

    loop(count // 2, twin_start)

    def v_tok(d):
        return remote(vec.at[(me + d) % n_tok], vt.at[d], t_s.at[d], t_r.at[d], (me + d) % n_tok, z)

    def v_rep(i, src):
        return remote(src, vb.at[i], v_s.at[i], v_r.at[i], me, at.zp if i == 0 else (z + 2) % n_rep)

    for d in range(1, n_tok):
        v_tok(d).start()

    def join(q, s):
        return a[q, s] + tw[q, s]

    def first(s, send):
        a[3, s] = join(3, s)
        send(s).start()

    def plain(q, s, send):
        a[q, s] = join(q, s)
        send(s).start()

    def joined(q, s, arrived, send):
        arrived(s).wait_recv()
        a[q, s] = join(q, s) + rd[s]
        send(s).start()

    inner = (z == 1) | (z == 2)
    outer = (z == 0) | (z == 3)

    def own(s):
        to_x(s).wait_recv()
        to_y(s).wait_recv()
        o[s] = join(0, s) + (rx[s] + ry[s])
        pl.when(outer)(lambda: z_in(s).start())

    def middle(s):
        @pl.when(inner)
        def _():
            z_in(s).wait_recv()
            pz[s] = o[s] + rz1[s]
            z_swap(s).start()

    def last(s):
        @pl.when(inner)
        def _():
            z_swap(s).wait_recv()
            fz[s] = pz[s] + rz2[s]
            z_out(s).start()
            keep(s).start()

    def taken(s):
        @pl.when(outer)
        def _():
            z_out(s).wait_recv()
            keep(s).start()

    def twin_sent(g):
        for q in range(4):
            to_twin(q, g).wait_send()

    def sent(s):
        d_y(s).wait_send()
        to_x(s).wait_send()
        to_y(s).wait_send()
        keep(s).wait()

        @pl.when(outer)
        def _():
            z_in(s).wait_send()

        @pl.when(inner)
        def _():
            z_swap(s).wait_send()
            z_out(s).wait_send()

    def pick_rows(i):
        ts = pl.ds(pl.multiple_of(i * 256, 256), 256)
        hit = lax.broadcasted_iota(I32, (SD * cap, 256), 0) == slot_of[:, ts]
        picked = jnp.where(hit, 1.0, 0.0).astype(BF)
        outs = jnp.concatenate([out_v[k, 0:cap, :] for k in range(SD)], axis=0)
        ings = jnp.concatenate([ing_v[k] for k in range(SD)], axis=0)
        both = mm(picked, jnp.concatenate([outs, ings], axis=1), TN)
        output[ts, :] = both[:, 0:D].astype(BF)
        input_grad[ts, :] = both[:, D:].astype(BF)
        line = jnp.concatenate([out_v[k, cap : cap + 8, 0:cap] for k in range(SD)], axis=1)
        entropy[:, ts] = mm(line, picked)[0:1].astype(BF)

    for q in (3, 1, 2, 0):
        load(q).wait()

    def steps(i, lag, more):
        s = i - lag
        by_x = (s % 2 == 0) & (s < 2 * split)
        live = (s >= 0) & (s < count)
        pl.when(live & by_x)(lambda: more(s, True))
        pl.when(live & jnp.logical_not(by_x))(lambda: more(s, False))

    def steps_of(i, lag, more):
        pl.when((i >= lag) & (i < count + lag))(lambda: more(i - lag))

    def round_of(i):
        for lag, which in ((0, (3,)), (1, (1, 2)), (6, (0,))):

            @pl.when((i >= lag) & ((i - lag) % 2 == 0) & (i < count + lag))
            def _(lag=lag, which=which):
                for q in which:
                    to_twin(q, (i - lag) // 2).wait_recv()

        steps(i, 0, lambda s, by_x: first(s, d_x if by_x else d_y))
        steps(i, 1, lambda s, by_x: plain(1, s, to_x) if by_x else plain(2, s, to_y))
        steps(i, 3, lambda s, by_x: joined(2, s, d_x, to_y) if by_x else joined(1, s, d_y, to_x))
        steps_of(i, 6, own)
        steps_of(i, 8, middle)
        steps_of(i, 10, last)
        steps_of(i, 12, taken)
        steps_of(i, 14, sent)
        pl.when((i >= 8) & (i % 2 == 0) & (i < count + 8))(lambda: twin_sent((i - 8) // 2))

    loop(3, round_of)
    for copy in rows_in:
        copy.wait()
    slots_here, _ = route_slots(order[...], me % SD, cap)
    slot_of[...] = slots_here

    v_sum = vec[me]
    for d in range(1, n_tok):
        v_tok(d).wait()
        v_sum = v_sum + vt[d]
    va[...] = v_sum
    v_rep(0, va).start()

    def four_rounds(i):
        loop(4, lambda j: round_of(3 + 4 * i + j))
        pick_rows(i)

    four_rounds(0)
    v_rep(0, va).wait()
    vc[...] = va[...] + vb[0]
    v_rep(1, vc).start()
    loop(3, lambda i: four_rounds(1 + i))
    loop(count + 12 - 19, lambda i: round_of(19 + i))
    v_rep(1, vc).wait()
    vec_out[...] = vc[...] + vb[1]

    loop(2, lambda j: sent(count - 2 + j))


def reduce_all(cap, grads, shares, order, outs, ings, count):
    dma = pltpu.SemaphoreType.DMA
    count = count * BLK // PART
    part = pltpu.VMEM((count, PART, D), BF)
    whole = pltpu.VMEM((4, count, PART, D), BF)
    line = pltpu.VMEM((16, 128), F32)
    rows = jax.ShapeDtypeStruct((ROWS, D), BF)
    total, vec, output, input_grad, entropy = pl.pallas_call(
        functools.partial(reduce_kernel, cap, count, count // 2),
        out_shape=(
            jax.ShapeDtypeStruct((count, PART, D), BF),
            jax.ShapeDtypeStruct((16, 128), F32),
            rows,
            rows,
            jax.ShapeDtypeStruct((1, ROWS), BF),
        ),
        in_specs=[ANY, VMEM, VMEM] + [ANY] * (2 * SD),
        out_specs=(ANY,) + (VMEM,) * 4,
        scratch_shapes=[
            pltpu.VMEM((SD, cap + META, D), BF),
            pltpu.VMEM((SD, cap, D), BF),
            pltpu.VMEM((1, ROWS), I32),
            whole,
            whole,
        ]
        + [part] * 8
        + [pltpu.VMEM((8, 16, 128), F32), line, pltpu.VMEM((2, 16, 128), F32), line]
        + [dma((4,)), dma((count,))]
        + [dma((4, count // 2))] * 2
        + [dma((count,))] * 12
        + [dma((8,))] * 2
        + [dma((2,))] * 2
        + [dma((2, SD))],
        compiler_params=pltpu.CompilerParams(collective_id=1, has_side_effects=True, vmem_limit_bytes=VMEM_LIMIT),
        cost_estimate=pl.CostEstimate(flops=4 * ROWS * ROWS * D, bytes_accessed=64 << 20, transcendentals=0),
        name="reduce",
    )(grads.reshape(-1, PART, D), shares, order, *outs, *ings)
    return total.reshape(-1, BLK, D), vec, output, input_grad, entropy


V_BQ, V_BV, V_BO, V_BD, V_G1, V_C1, V_G2, V_C2 = range(8)


def inverse(x):
    r = pl.reciprocal(x, approx=True)
    return r * (2.0 - x * r)


def erf_parts(v):
    t = inverse(1.0 + (0.3275911 / math.sqrt(2.0)) * jnp.abs(v))
    e = jnp.exp2((v * v) * (-0.5 / math.log(2.0)))
    poly = 0.5 * 1.061405429
    for c in (-1.453152027, 1.421413741, -0.284496736, 0.254829592):
        poly = poly * t + 0.5 * c
    tail = poly * (t * e)
    return jnp.where(v >= 0.0, 1.0 - tail, tail), e


def lane_sum(x):
    return jnp.sum(x, axis=1, keepdims=True)


def gelu_parts(v):
    phi, e = erf_parts(v)
    return v * phi, phi + v * (e * (1.0 / math.sqrt(2.0 * math.pi)))


def weight_copies(pos, slots, w, sem, first):
    def copy(b):
        return pltpu.make_async_copy(slots.at[pos[first + b]], w.at[pl.ds(b * BLK, BLK)], sem)

    n = w.shape[0] // BLK
    return (lambda: loop(n, lambda b: copy(b).start())), (lambda: loop(n, lambda b: copy(b).wait()))


def halves_of_heads():
    lane = lax.broadcasted_iota(I32, (1, PW), 1)
    m0 = jnp.where(lane < HD, 1.0, 0.0).astype(BF)
    m1 = jnp.where(lane < HD, 0.0, 1.0).astype(BF)
    return lambda pair: jnp.concatenate([pair * m0, pair * m1], axis=0)


def tile_rows(t):
    return pl.ds(pl.multiple_of(t * TM, TM), TM)


def forward_kernel(
    cap,
    pos,
    slots,
    vecs,
    b_u,
    x_h,
    meta,
    back_0,
    back_1,
    back_2,
    back_3,
    heads_h,
    act_h,
    hid_h,
    q_h,
    k_h,
    v_h,
    p_h,
    slope_h,
    n1_h,
    n2_h,
    rs1_h,
    rs2_h,
    wqkv,
    wo,
    wu,
    wd,
    x_c,
    heads,
    act,
    hid,
    q,
    k,
    v,
    p_all,
    slope,
    n1,
    n2,
    rs1,
    rs2,
    out_c,
    ent,
    w_sem,
    x_sem,
    o_sem,
):
    inv = 1.0 / math.sqrt(HD)
    get_x = pltpu.make_async_copy(x_h, x_c, x_sem)
    get_x.start()
    weights = [
        weight_copies(pos, slots, w, w_sem.at[i], first)
        for i, (w, first) in enumerate(((wqkv, 0), (wo, 24), (wu, 32), (wd, 64)))
    ]
    for start, _ in weights:
        start()
    get_x.wait()
    apart = halves_of_heads()

    def vec(i):
        return vecs[i : i + 1, :]

    saved = (
        (heads, heads_h),
        (act, act_h),
        (hid, hid_h),
        (q, q_h),
        (k, k_h),
        (v, v_h),
        (slope, slope_h),
        (n1, n1_h),
        (n2, n2_h),
        (rs1, rs1_h),
        (rs2, rs2_h),
    )

    def save(t, i):
        src, dst = saved[i]
        return pltpu.make_async_copy(src.at[tile_rows(t)], dst.at[tile_rows(t)], o_sem.at[i])

    def save_p(t):
        n = TM // CL
        cs = pl.ds(t * n, n)
        return pltpu.make_async_copy(p_all.at[cs], p_h.at[cs], o_sem.at[len(saved)])

    def normal(r, n, rs, rows):
        c = r - lane_sum(r) * (1.0 / D)
        scale = lax.rsqrt(lane_sum(c * c) * (1.0 / D) + norm_epsilon)
        rs[rows, :] = jnp.broadcast_to(scale, (TM, 128))
        n[rows, :] = c * scale

    def project(t):
        rows = tile_rows(t)
        x = x_c[rows, :]
        q[rows, :] = ((mm(x, wqkv[0:D, :]) + vec(V_BQ)).astype(BF).astype(F32) * inv).astype(BF)
        k[rows, :] = mm(x, wqkv[D : 2 * D, :]).astype(BF)
        v[rows, :] = (mm(x, wqkv[2 * D :, :]) + vec(V_BV)).astype(BF)

    def attend(clusters):
        groups = [pl.ds(pl.multiple_of(c * CL, CL), CL) for c in clusters]
        pairs = [(i, p, slice(p * PW, (p + 1) * PW)) for i in range(len(groups)) for p in range(PAIRS)]
        scores = [mm(apart(k[groups[i], ps]), q[groups[i], ps], NT) for i, _, ps in pairs]
        total = [jnp.zeros((1, CL), F32)] * len(groups)
        probs = []
        for (i, _, _), both in zip(pairs, scores):
            halves = []
            for h in range(2):
                sh = both[h * CL : (h + 1) * CL]
                sh = sh - jnp.max(sh, axis=0, keepdims=True)
                e = jnp.exp(sh)
                tot = jnp.sum(e, axis=0, keepdims=True)
                r = 1.0 / tot
                total[i] += jnp.log(tot) - jnp.sum(e * sh, axis=0, keepdims=True) * r
                halves.append((e * r).astype(BF))
            probs.append(jnp.concatenate(halves, axis=0))
        mixed = [mm(w, apart(v[groups[i], ps]), TN).astype(BF) for (i, _, ps), w in zip(pairs, probs)]
        for (i, p, ps), w, o in zip(pairs, probs, mixed):
            p_all[clusters[i], p] = w
            heads[groups[i], ps] = o
        for i, group in enumerate(groups):
            ent[:, group] = jnp.broadcast_to(total[i] * (1.0 / HEADS), (8, CL))

    def resid_one(t):
        rows = tile_rows(t)
        return x_c[rows, :].astype(F32) + mm(heads[rows, :], wo[...]) + vec(V_BO)

    def norm_one(t, r1):
        rows = tile_rows(t)
        normal(r1, n1, rs1, rows)
        hidden = n1[rows, :] * vec(V_G1) + vec(V_C1)
        hid[rows, :] = hidden.astype(BF)
        n2[rows, :] = hidden

    def widen(t, columns):
        rows = tile_rows(t)
        parts = [pl.ds(pl.multiple_of(f * FC, FC), FC) for f in columns]
        ups = [mm(hid[rows, :], wu[fs, :], NT) for fs in parts]

        def finish():
            for fs, up in zip(parts, ups):
                g, g_slope = gelu_parts(up + b_u[:, fs])
                act[rows, fs] = g.astype(BF)
                slope[rows, fs] = g_slope.astype(BF)

        return finish

    def resid_two(t):
        rows = tile_rows(t)
        return n2[rows, :] + mm(act[rows, :], wd[...]) + vec(V_BD)

    def norm_two(t, r2):
        rows = tile_rows(t)
        normal(r2, n2, rs2, rows)
        out_c[rows, :] = (n2[rows, :] * vec(V_G2) + vec(V_C2)).astype(BF)

    def save_all(t, which):
        for i in which:
            save(t, i).start()

    per = TM // CL
    weights[0][1]()
    project(0)
    project(1)
    for t in range(2):
        attend(range(t * per, (t + 1) * per))
        save_all(t, (0, 3, 4, 5))
        save_p(t).start()
    weights[1][1]()
    r1 = [resid_one(t) for t in range(2)]
    for t in range(2):
        norm_one(t, r1[t])
    weights[2][1]()
    for t in range(2):
        loop(FF // FC // 2, lambda f, t=t: widen(t, [2 * f, 2 * f + 1])())
        save_all(t, (1, 2, 6, 7, 9))
    weights[3][1]()
    r2 = [resid_two(t) for t in range(2)]
    for t in range(2):
        norm_two(t, r2[t])
        save_all(t, (8, 10))

    for j, back in enumerate((back_0, back_1, back_2, back_3)):
        own = seat_part(meta, j, cap)
        back[0:cap, :] = mm(own, out_c[...], TN).astype(BF)
        line = mm(ent[...].astype(BF), own)
        back[cap:, :] = jnp.concatenate([line, line], axis=1)[0:1].astype(BF) * jnp.ones((META, 1), BF)

    def saved_all(t):
        for i in range(len(saved)):
            save(t, i).wait()
        save_p(t).wait()

    loop(ROWS // TM, saved_all)


def shape_of(kind, *shape):
    return jax.ShapeDtypeStruct(shape, kind)


def saved_shapes():
    rows, wide = ((ROWS, D), BF), ((ROWS, FF), BF)
    probs = ((ROWS // CL, PAIRS, 2 * CL, CL), BF)
    full, thin = ((ROWS, D), F32), ((ROWS, 128), F32)
    return rows, wide, probs, full, thin


def forward(cap, positions, slots, vecs, b_u, x_c, meta):
    rows, wide, probs, full, thin = saved_shapes()
    kept = (rows, wide, rows, rows, rows, rows, probs, wide, full, full, thin, thin)
    dma = pltpu.SemaphoreType.DMA
    return pl.pallas_call(
        functools.partial(forward_kernel, cap),
        out_shape=(shape_of(BF, cap + META, D),) * SD + tuple(shape_of(kind, *shape) for shape, kind in kept),
        in_specs=[SMEM, ANY, VMEM, VMEM, ANY, VMEM],
        out_specs=(VMEM,) * SD + (ANY,) * len(kept),
        scratch_shapes=[
            pltpu.VMEM((3 * D, D), BF),
            pltpu.VMEM((D, D), BF),
            pltpu.VMEM((FF, D), BF),
            pltpu.VMEM((FF, D), BF),
            pltpu.VMEM(*rows),
        ]
        + [pltpu.VMEM(*a) for a in kept]
        + [
            pltpu.VMEM(*rows),
            pltpu.VMEM((8, ROWS), F32),
            dma((4,)),
            dma,
            dma((12,)),
        ],
        compiler_params=pltpu.CompilerParams(vmem_limit_bytes=VMEM_LIMIT),
        cost_estimate=pl.CostEstimate(flops=2 * ROWS * WROWS * D, bytes_accessed=64 << 20, transcendentals=0),
        name="forward",
    )(positions, slots, vecs, b_u, x_c, meta)


def backward_kernel(
    cap,
    pos,
    slots,
    vecs,
    meta,
    cot_0,
    cot_1,
    cot_2,
    cot_3,
    q_h,
    k_h,
    v_h,
    p_h,
    slope_h,
    n1_h,
    n2_h,
    rs1_h,
    rs2_h,
    back_0,
    back_1,
    back_2,
    back_3,
    shares,
    d_up_h,
    d_q_h,
    d_k_h,
    d_v_h,
    d_proj_h,
    d_br_h,
    wqkv,
    wo,
    wu,
    wd,
    blocks,
    q,
    k,
    v,
    p_all,
    d_up,
    n1,
    n2,
    rs1,
    rs2,
    d_proj,
    d_br,
    ing_c,
    d_h_t,
    gvec,
    g_bu,
    w_sem,
    c_sem,
    i_sem,
    o_sem,
):
    inv = 1.0 / math.sqrt(HD)
    get_c = [
        pltpu.make_async_copy(cot, blocks.at[j], c_sem.at[j]) for j, cot in enumerate((cot_0, cot_1, cot_2, cot_3))
    ]
    for copy in get_c:
        copy.start()
    fetch = [
        pltpu.make_async_copy(src, dst, i_sem.at[i])
        for i, (src, dst) in enumerate(
            (
                (n2_h, n2),
                (rs2_h, rs2),
                (slope_h, d_up),
                (n1_h, n1),
                (rs1_h, rs1),
                (v_h, v),
                (p_h, p_all),
                (k_h, k),
                (q_h, q),
            )
        )
    ]
    weights = [
        weight_copies(pos, slots, w, w_sem.at[i], first)
        for i, (w, first) in enumerate(((wd, 64), (wu, 32), (wo, 24), (wqkv, 0)))
    ]
    fetch[0].start()
    fetch[1].start()
    weights[0][0]()
    fetch[2].start()
    weights[1][0]()
    fetch[3].start()
    fetch[4].start()
    weights[2][0]()
    for i in range(5, 9):
        fetch[i].start()
    weights[3][0]()
    gvec[...] = jnp.zeros_like(gvec)
    g_bu[...] = jnp.zeros_like(g_bu)
    shares[...] = jnp.zeros_like(shares)
    for copy in get_c:
        copy.wait()
    seat_rows(meta, blocks, cap, d_br)
    apart = halves_of_heads()

    def vec(i):
        return vecs[i : i + 1, :]

    def add_vec(i, value):
        gvec[i : i + 1, :] += jnp.sum(value, axis=0, keepdims=True)

    saved = ((d_up, d_up_h), (q, d_q_h), (k, d_k_h), (v, d_v_h), (d_proj, d_proj_h), (d_br, d_br_h))

    def save(t, i):
        src, dst = saved[i]
        return pltpu.make_async_copy(src.at[tile_rows(t)], dst.at[tile_rows(t)], o_sem.at[i])

    def norm_back(e, n, rs, gain, shift):
        add_vec(gain, e * n)
        add_vec(shift, e)
        eg = e * vec(gain)
        return rs * (eg - lane_sum(eg) * (1.0 / D) - n * (lane_sum(eg * n) * (1.0 / D)))

    def norm_two_back(t):
        rows = tile_rows(t)
        d_r2 = norm_back(d_br[rows, :].astype(F32), n2[rows, :], rs2[rows, 0:1], V_G2, V_C2)
        d_br[rows, :] = d_r2.astype(BF)
        add_vec(V_BD, d_br[rows, :].astype(F32))
        n2[rows, :] = d_r2

    def widen_back(t, columns):
        rows = tile_rows(t)
        parts = [pl.ds(pl.multiple_of(f * FC, FC), FC) for f in columns]
        ups = [mm(d_br[rows, :], wd[fs, :], NT) for fs in parts]

        def finish():
            for fs, up in zip(parts, ups):
                du = (up * d_up[rows, fs].astype(F32)).astype(BF)
                d_up[rows, fs] = du
                g_bu[:, fs] += jnp.sum(du.astype(F32), axis=0, keepdims=True)

        return finish

    def hidden_back(t):
        rows = tile_rows(t)
        return n2[rows, :] + mm(d_up[rows, :], wu[...])

    def norm_one_back(t, d_h):
        rows = tile_rows(t)
        d_r1 = norm_back(d_h, n1[rows, :], rs1[rows, 0:1], V_G1, V_C1)
        d_proj[rows, :] = d_r1.astype(BF)
        n2[rows, :] = d_r1
        add_vec(V_BO, d_proj[rows, :].astype(F32))

    def heads_back(t):
        rows = tile_rows(t)
        d_h_t[rows, :] = mm(d_proj[rows, :], wo[...], NT).astype(BF)

    def attend_back(clusters):
        pairs = [
            (c, p, pl.ds(pl.multiple_of(c * CL, CL), CL), slice(p * PW, (p + 1) * PW))
            for c in clusters
            for p in range(PAIRS)
        ]
        probs = [p_all[c, p] for c, p, _, _ in pairs]
        d_heads = [d_h_t[gr, ps] for _, _, gr, ps in pairs]
        d_probs = [mm(apart(v[gr, ps]), dh, NT) for (_, _, gr, ps), dh in zip(pairs, d_heads)]
        d_values = [
            mm(jnp.concatenate([w[0:CL], w[CL:]], axis=1), apart(dh)).astype(BF) for w, dh in zip(probs, d_heads)
        ]
        d_scores = []
        for w, dw in zip(probs, d_probs):
            halves = []
            for h in range(2):
                wh = w[h * CL : (h + 1) * CL].astype(F32)
                dwh = dw[h * CL : (h + 1) * CL]
                halves.append((wh * (dwh - jnp.sum(dwh * wh, axis=0, keepdims=True))).astype(BF))
            d_scores.append(halves)
        d_keys = [
            mm(jnp.concatenate(ds, axis=1), apart(q[gr, ps])).astype(BF) for (_, _, gr, ps), ds in zip(pairs, d_scores)
        ]
        d_queries = [
            (mm(jnp.concatenate(ds, axis=0), apart(k[gr, ps]), TN) * inv).astype(BF)
            for (_, _, gr, ps), ds in zip(pairs, d_scores)
        ]
        for (_, _, gr, ps), dq, dk, dv in zip(pairs, d_queries, d_keys, d_values):
            q[gr, ps] = dq
            k[gr, ps] = dk
            v[gr, ps] = dv

    def rows_back(t):
        rows = tile_rows(t)
        return (
            mm(q[rows, :], wqkv[0:D, :], NT)
            + mm(k[rows, :], wqkv[D : 2 * D, :], NT)
            + mm(v[rows, :], wqkv[2 * D :, :], NT)
        )

    def rows_done(t, d_x):
        rows = tile_rows(t)
        add_vec(V_BQ, q[rows, :].astype(F32))
        add_vec(V_BV, v[rows, :].astype(F32))
        ing_c[rows, :] = (n2[rows, :] + d_x.astype(BF).astype(F32)).astype(BF)

    def save_all(t, which):
        for i in which:
            save(t, i).start()

    per = TM // CL
    fetch[0].wait()
    fetch[1].wait()
    norm_two_back(0)
    norm_two_back(1)
    weights[0][1]()
    fetch[2].wait()
    for t in range(2):
        loop(FF // FC // 2, lambda f, t=t: widen_back(t, [2 * f, 2 * f + 1])())
        save_all(t, (0, 5))
    weights[1][1]()
    fetch[3].wait()
    fetch[4].wait()
    d_h = [hidden_back(t) for t in range(2)]
    for t in range(2):
        norm_one_back(t, d_h[t])
    weights[2][1]()
    for i in range(5, 9):
        fetch[i].wait()
    for t in range(2):
        heads_back(t)
        save_all(t, (4,))
    for t in range(2):
        attend_back(range(t * per, (t + 1) * per))
        save_all(t, (1, 2, 3))
    weights[3][1]()
    d_x = [rows_back(t) for t in range(2)]
    for t in range(2):
        rows_done(t, d_x[t])

    for j, back in enumerate((back_0, back_1, back_2, back_3)):
        back[...] = mm(seat_part(meta, j, cap), ing_c[...], TN).astype(BF)

    for chunk in range(72):
        row, lane = chunk // 6, chunk % 6 * 128
        if row < 8:
            part = gvec[row : row + 1, lane : lane + 128]
        else:
            lane += (row - 8) * D
            part = g_bu[:, lane : lane + 128]
        shares[chunk // 9, chunk % 9 : chunk % 9 + 1, :] = part

    def saved_all(t):
        for i in range(len(saved)):
            save(t, i).wait()

    loop(ROWS // TM, saved_all)


def backward(cap, positions, slots, vecs, meta, cots, saved):
    rows, wide, probs, full, thin = saved_shapes()
    dma = pltpu.SemaphoreType.DMA
    grads = (wide, rows, rows, rows, rows, rows)
    return pl.pallas_call(
        functools.partial(backward_kernel, cap),
        out_shape=(shape_of(BF, cap, D),) * SD
        + (shape_of(F32, 8, 16, 128),)
        + tuple(shape_of(kind, *shape) for shape, kind in grads),
        in_specs=[SMEM, ANY, VMEM, VMEM] + [ANY] * (SD + 9),
        out_specs=(VMEM,) * (SD + 1) + (ANY,) * len(grads),
        scratch_shapes=[
            pltpu.VMEM((3 * D, D), BF),
            pltpu.VMEM((D, D), BF),
            pltpu.VMEM((FF, D), BF),
            pltpu.VMEM((FF, D), BF),
            pltpu.VMEM((SD, cap, D), BF),
        ]
        + [pltpu.VMEM(*a) for a in (rows, rows, rows, probs, wide, full, full, thin, thin, rows, rows, rows)]
        + [
            pltpu.VMEM(*rows),
            pltpu.VMEM((8, D), F32),
            pltpu.VMEM((1, FF), F32),
            dma((4,)),
            dma((4,)),
            dma((9,)),
            dma((6,)),
        ],
        compiler_params=pltpu.CompilerParams(vmem_limit_bytes=VMEM_LIMIT),
        cost_estimate=pl.CostEstimate(flops=2 * ROWS * WROWS * D, bytes_accessed=64 << 20, transcendentals=0),
        name="backward",
    )(positions, slots, vecs, meta, *cots, *saved)


WC = 8 * BLK


def weight_kernel(
    pos,
    x_h,
    heads_h,
    act_h,
    d_up_h,
    d_q_h,
    d_k_h,
    d_v_h,
    d_proj_h,
    hid_h,
    d_br_h,
    grads,
    x_c,
    heads,
    act,
    d_up,
    d_q,
    d_k,
    d_v,
    d_proj,
    hid,
    d_br,
    stage,
    i_sem,
    g_sem,
):
    refs = (
        (x_h, x_c),
        (d_q_h, d_q),
        (d_k_h, d_k),
        (d_v_h, d_v),
        (heads_h, heads),
        (d_proj_h, d_proj),
        (hid_h, hid),
        (d_up_h, d_up),
        (d_br_h, d_br),
        (act_h, act),
    )
    fetch = [pltpu.make_async_copy(src, dst, i_sem.at[i]) for i, (src, dst) in enumerate(refs)]
    for copy in fetch:
        copy.start()

    per = WC // BLK

    def g_copy(chunk, j, at):
        return pltpu.make_async_copy(
            stage.at[at, pl.ds(j * BLK, BLK)], grads.at[pos[chunk * per + j]], g_sem.at[at]
        )

    def put(chunk, left, right):
        at = lax.rem(chunk, 2)

        @pl.when(chunk >= 2)
        def _():
            for j in range(per):
                g_copy(chunk - 2, j, at).wait()

        stage[at] = mm(left, right, TN).astype(BF)
        for j in range(per):
            g_copy(chunk, j, at).start()

    first = 0
    for left, right, needs in (
        (x_c, d_q, (0, 1)),
        (x_c, d_k, (2,)),
        (x_c, d_v, (3,)),
        (heads, d_proj, (4, 5)),
        (d_up, hid, (6, 7)),
        (act, d_br, (8, 9)),
    ):
        for i in needs:
            fetch[i].wait()

        def body(j, left=left, right=right, first=first):
            put(first + j, left[:, pl.ds(pl.multiple_of(j * WC, WC), WC)], right[...])

        loop(left.shape[1] // WC, body)
        first += left.shape[1] // WC
    for chunk in (first - 2, first - 1):
        for j in range(per):
            g_copy(chunk, j, chunk % 2).wait()


def weight_grads_of(total_slots, positions, x_c, saved):
    r_v, w_v = pltpu.VMEM((ROWS, D), BF), pltpu.VMEM((ROWS, FF), BF)
    return pl.pallas_call(
        weight_kernel,
        out_shape=jax.ShapeDtypeStruct((total_slots, BLK, D), BF),
        in_specs=[SMEM] + [ANY] * 10,
        out_specs=ANY,
        scratch_shapes=[r_v, r_v, w_v, w_v]
        + [r_v] * 6
        + [
            pltpu.VMEM((2, WC, D), BF),
            pltpu.SemaphoreType.DMA((10,)),
            pltpu.SemaphoreType.DMA((2,)),
        ],
        compiler_params=pltpu.CompilerParams(vmem_limit_bytes=VMEM_LIMIT),
        cost_estimate=pl.CostEstimate(flops=2 * ROWS * WROWS * D, bytes_accessed=40 << 20, transcendentals=0),
        name="weight_grads",
    )(positions, x_c, *saved)


def adam_step(grad_now, weight_old, first_old, second_old, rate_step):
    first_new = beta_first * first_old + (1.0 - beta_first) * grad_now
    second_new = beta_second * second_old + (1.0 - beta_second) * grad_now * grad_now
    square = second_new * (1.0 / (1.0 - beta_second**STEP))
    root = jnp.where(square > 0.0, square * lax.rsqrt(square), 0.0)
    step = first_new * (1.0 / (1.0 - beta_first**STEP)) * inverse(root + adam_epsilon)
    return (first_new, second_new, weight_old - rate_step * (step + weight_decay * weight_old))


def finish_kernel(
    pos,
    total_h,
    master_h,
    first_h,
    second_h,
    v_grad,
    v_master,
    v_first,
    v_second,
    line,
    counts,
    out_h,
    ing_h,
    grad_new,
    first_new,
    second_new,
    master_new,
    low_new,
    v_grad_new,
    v_first_new,
    v_second_new,
    v_master_new,
    v_low_new,
    entropy,
    occupancy,
    output,
    input_grad,
    total,
    master,
    first,
    second,
    grad,
    out_v,
    ing_v,
    in_s,
    out_s,
    row_s,
):
    count = total.shape[0]
    ins = ((total_h, total), (master_h, master), (first_h, first), (second_h, second))
    outs = ((total, low_new), (master, master_new), (first, first_new), (second, second_new), (grad, grad_new))

    groups = [(first, min(max(first, 1), 4, count - first)) for first in (0, 1, 2, 4, 8, 12) if first < count]

    def fetch(i, n):
        src, dst = ins[i]
        part = pl.ds(*groups[n])
        return pltpu.make_async_copy(src.at[part], dst.at[part], in_s.at[i, n])

    def put(i, n):
        src, dst = outs[i]
        part = pl.ds(*groups[n])
        return pltpu.make_async_copy(src.at[part], dst.at[part], out_s.at[i, n])

    rows_in = [pltpu.make_async_copy(a, b, row_s.at[0, n]) for n, (a, b) in enumerate(((out_h, out_v), (ing_h, ing_v)))]
    rows_out = [pltpu.make_async_copy(a, b, row_s.at[1, n]) for n, (a, b) in enumerate(((out_v, output), (ing_v, input_grad)))]
    for n in range(len(groups)):
        for i in range(4):
            fetch(i, n).start()
    for copy in rows_in:
        copy.start()
    entropy[...] = line[...].reshape(ROWS)
    occupancy[...] = counts[...]
    length = v_master.shape[0]
    for n in range(-(-length // 128)):
        part = slice(n * 128, min((n + 1) * 128, length))
        g = v_grad[n : n + 1, 0 : part.stop - part.start].reshape(part.stop - part.start)
        m, v, w = adam_update(g, v_master[part], v_first[part], v_second[part], rate_vector)
        v_grad_new[part] = g
        v_first_new[part] = m
        v_second_new[part] = v
        v_master_new[part] = w
    v_low_new[...] = v_master_new[...].astype(BF)

    def slot(s):
        g = jnp.where(s < pos[NBLK], total[s].astype(F32), 0.0)
        m, v, w = adam_step(g, master[s], first[s], second[s], rate_matrix)
        grad[s] = g
        first[s] = m
        second[s] = v
        master[s] = w
        total[s] = w.astype(BF)

    for n, (start, size) in enumerate(groups):
        for i in range(4):
            fetch(i, n).wait()
        loop(size, lambda j, start=start: slot(start + j))
        for i in range(5):
            put(i, n).start()
    for copy_in, copy_out in zip(rows_in, rows_out):
        copy_in.wait()
        copy_out.start()
    for n in range(len(groups)):
        for i in range(5):
            put(i, n).wait()
    for copy in rows_out:
        copy.wait()


def finish(positions, total, weights, v_grad, vectors, line, counts, out, ing):
    count = total.shape[0]
    low, full = pltpu.VMEM((count, BLK, D), BF), pltpu.VMEM((count, BLK, D), F32)
    f32_slots, f32_vector = shape_of(F32, count, BLK, D), shape_of(F32, *vectors[0].shape)
    dma = pltpu.SemaphoreType.DMA
    return pl.pallas_call(
        finish_kernel,
        out_shape=(f32_slots,) * 4
        + (shape_of(BF, count, BLK, D),)
        + (f32_vector,) * 4
        + (shape_of(BF, *vectors[0].shape), shape_of(BF, ROWS), shape_of(I32, *counts.shape))
        + (shape_of(BF, ROWS, D),) * 2,
        in_specs=[SMEM] + [ANY] * 4 + [VMEM] * 6 + [ANY] * 2,
        out_specs=(ANY,) * 5 + (VMEM,) * 7 + (ANY,) * 2,
        scratch_shapes=[low, full, full, full, full]
        + [pltpu.VMEM((ROWS, D), BF)] * 2
        + [dma((4, 6)), dma((5, 6)), dma((2, 2))],
        compiler_params=pltpu.CompilerParams(vmem_limit_bytes=VMEM_LIMIT),
        name="finish",
    )(positions, total, *weights, v_grad, *vectors, line, counts, out, ing)


def local(
    tokens,
    cotangent,
    cluster_order,
    block_owner,
    master_slots,
    moment_one,
    moment_two,
    vector_master,
    vector_moment_one,
    vector_moment_two,
):
    tok_count = lax.axis_size("tok")
    tok_index = lax.axis_index("tok")
    slot_count = master_slots.shape[0]
    cap = tok_count // SD * (max(1, CPS // tok_count) * 3 * CL // (2 * SD))
    total_slots = tok_count * slot_count
    order = cluster_order.reshape(1, ROWS)

    block = jax.ShapeDtypeStruct((SD, cap, D), BF)
    meta_shape = jax.ShapeDtypeStruct((SD, META, D), BF)
    row_block = jax.ShapeDtypeStruct((ROWS, D), BF)
    four_planes = tok_count == 8 and lax.axis_size("rep") == 4
    if four_planes:
        slots_low, x_c, *cots, recv_meta, vecs, b_u, occupancy, positions = gather_all(
            cap, tokens, cotangent, order, master_slots, vector_master, block_owner
        )
        positions = positions.reshape(128)
        slots_low = slots_low.reshape(total_slots, BLK, D)
    else:
        positions = slot_positions(block_owner, slot_count)
        owned = jnp.sum((block_owner == tok_index).astype(I32)).reshape(1)
        positions = jnp.concatenate([positions, owned])
        slots_low = lax.all_gather(master_slots.astype(BF), "tok", axis=0, tiled=True)
        vectors = lax.all_gather(vector_master.astype(BF), "tok", axis=0, tiled=True).astype(F32)
        vecs, b_u = vectors[: 8 * D].reshape(8, D), vectors[8 * D :].reshape(1, FF)
        cluster = tok_index // SD * CPS + cluster_order // CL
        target = cluster % tok_count
        chosen = target[None, :] == jnp.arange(tok_count, dtype=jnp.int32)[:, None]
        sent_counts = jnp.sum(chosen.astype(F32), axis=1)
        own_row = (jnp.arange(tok_count, dtype=jnp.int32) == tok_index).astype(F32)
        occupancy = lax.psum(own_row[:, None] * sent_counts[None, :], ("tok", "rep")).astype(jnp.int32)
        send_x, send_c, meta = pl.pallas_call(
            functools.partial(send_kernel, cap),
            out_shape=(block, block, meta_shape),
            in_specs=[VMEM] * 3,
            out_specs=(VMEM,) * 3,
            compiler_params=pltpu.CompilerParams(vmem_limit_bytes=VMEM_LIMIT),
            name="send_rows",
        )(tokens, cotangent, order)
        recv_x, recv_meta = (jnp.stack(swap_blocks(b)) for b in (send_x, meta))
        x_c = pl.pallas_call(
            functools.partial(seat_kernel, cap),
            out_shape=row_block,
            in_specs=[VMEM] * 2,
            out_specs=VMEM,
            compiler_params=pltpu.CompilerParams(vmem_limit_bytes=VMEM_LIMIT),
            name="seat_rows",
        )(recv_x, recv_meta)
        cots = [send_c[k] for k in range(SD)]

    cots = swap_blocks(cots)
    *out_blocks, heads, act, hid, q, k, v, p, slope, n1, n2, rs1, rs2 = forward(
        cap, positions, slots_low, vecs, b_u, x_c, recv_meta
    )
    out_blocks = swap_blocks(out_blocks)
    *ing_blocks, shares, d_up, d_q, d_k, d_v, d_proj, d_br = backward(
        cap, positions, slots_low, vecs, recv_meta, cots, (q, k, v, p, slope, n1, n2, rs1, rs2)
    )
    ing_blocks = swap_blocks(ing_blocks)
    grads = weight_grads_of(
        total_slots, positions, x_c, (heads, act, d_up, d_q, d_k, d_v, d_proj, hid, d_br)
    )
    if four_planes:
        total, vec_owned, output, input_grad, entropy = reduce_all(
            cap, grads, shares, order, out_blocks, ing_blocks, slot_count
        )
    else:
        total = lax.psum(lax.psum_scatter(grads, "tok", scatter_dimension=0, tiled=True), "rep")
        grad_vector = shares[:, 0:9].reshape(-1)
        vec_owned = lax.psum(lax.psum_scatter(grad_vector, "tok", scatter_dimension=0, tiled=True), "rep")
        vec_owned = jnp.pad(vec_owned, (0, -vec_owned.shape[0] % 128)).reshape(-1, 128)
        output, input_grad, entropy = pl.pallas_call(
            functools.partial(return_kernel, cap),
            out_shape=(row_block, row_block, jax.ShapeDtypeStruct((1, ROWS), BF)),
            in_specs=[VMEM] * (2 * SD + 1),
            out_specs=(VMEM,) * 3,
            compiler_params=pltpu.CompilerParams(vmem_limit_bytes=VMEM_LIMIT),
            name="return_rows",
        )(order, *out_blocks, *ing_blocks)

    (
        owned_grad,
        first_new,
        second_new,
        master_new,
        low_new,
        vec_owned,
        vec_first,
        vec_second,
        vec_new,
        vec_low_new,
        row_entropy,
        occupancy,
        output,
        input_grad,
    ) = finish(
        positions,
        total,
        (master_slots, moment_one, moment_two),
        vec_owned,
        (vector_master, vector_moment_one, vector_moment_two),
        entropy,
        occupancy,
        output,
        input_grad,
    )
    return (
        output,
        input_grad,
        owned_grad,
        first_new,
        second_new,
        master_new,
        low_new,
        vec_owned,
        vec_first,
        vec_second,
        vec_new,
        vec_low_new,
        row_entropy,
        occupancy,
    )


def solution(mesh):
    placed = (
        P(("rep", "tok"), None),
        P(("rep", "tok"), None),
        P(("rep", "tok")),
        P(),
        P("tok", None, None),
        P("tok", None, None),
        P("tok", None, None),
        P("tok"),
        P("tok"),
        P("tok"),
    )
    return jax.shard_map(
        local,
        mesh=mesh,
        in_specs=placed,
        out_specs=(
            P(("rep", "tok"), None),
            P(("rep", "tok"), None),
            P("tok", None, None),
            P("tok", None, None),
            P("tok", None, None),
            P("tok", None, None),
            P("tok", None, None),
            P("tok"),
            P("tok"),
            P("tok"),
            P("tok"),
            P("tok"),
            P(("rep", "tok")),
            P(),
        ),
        check_vma=False,
    )
```
